128 devices in a mesh: dp: 32 (over x, z_hi, y), tensor: 4 (over z_lo, core).
Axes of the slice: x: 4, y: 4, z: 4 (z_hi: 2, z_lo: 2; z = z_hi * 2 + z_lo), core: 2. Of those that a mesh axis runs over, the one named last changes fastest.
Arguments:
- block_in: bfloat16 [16384, 1536], P(('dp', 'tensor')), may hold values from -6 to 6
- out_grad: bfloat16 [16384, 1536], P(('dp', 'tensor')), may hold values from -6 to 6
- condition: bfloat16 [96, 1024], P('dp'), may hold values from -6 to 6
- captions: bfloat16 [96, 256, 4096], P('dp'), may hold values from -6 to 6
- caption_len: int32 [96], P('dp'), may hold values from 64 to 256
- segment_ids: int32 [16384], P('dp'), may hold values from 0 to 2, as said below
- ada_weight: bfloat16 [1024, 6144], P(None, 'tensor'), may hold values from -0.1875 to 0.1875
- norm_gains: float32 [4, 1536], replicated, may hold values from 0.25 to 1.75
- query_weight: bfloat16 [1536, 1536], P(None, 'tensor'), may hold values from -0.15625 to 0.15625
- key_weight: bfloat16 [1536, 1536], P(None, 'tensor'), may hold values from -0.15625 to 0.15625
- value_weight: bfloat16 [1536, 1536], P(None, 'tensor'), may hold values from -0.15625 to 0.15625
- head_gains: float32 [3, 64], replicated, may hold values from 0.25 to 1.75
- textkey_weight: bfloat16 [4096, 1536], P(None, 'tensor'), may hold values from -0.09375 to 0.09375
- textvalue_weight: bfloat16 [4096, 1536], P(None, 'tensor'), may hold values from -0.09375 to 0.09375
- cross_gate: float32 [24], P('tensor'), may hold values from 0.3 to 1.5
- out_weight: bfloat16 [1536, 1536], P('tensor'), may hold values from -0.15625 to 0.15625
- gate_weight: bfloat16 [1536, 4096], P(None, 'tensor'), may hold values from -0.15625 to 0.15625
- up_weight: bfloat16 [1536, 4096], P(None, 'tensor'), may hold values from -0.15625 to 0.15625
- down_weight: bfloat16 [4096, 1536], P('tensor'), may hold values from -0.09375 to 0.09375
Outputs:
- block_out: bfloat16 [16384, 1536], P(('dp', 'tensor'))
- in_grad: bfloat16 [16384, 1536], P(('dp', 'tensor'))
- ada_grad: float32 [1024, 6144], P('dp', 'tensor')
- norm_grads: float32 [4, 1536], replicated
- query_grad: float32 [1536, 1536], P('dp', 'tensor')
- key_grad: float32 [1536, 1536], P('dp', 'tensor')
- value_grad: float32 [1536, 1536], P('dp', 'tensor')
- head_grads: float32 [3, 64], replicated
- textkey_grad: float32 [4096, 1536], P('dp', 'tensor')
- textvalue_grad: float32 [4096, 1536], P('dp', 'tensor')
- crossgate_grad: float32 [24], replicated
- outw_grad: float32 [1536, 1536], P('tensor', 'dp')
- gate_grad: float32 [1536, 4096], P('dp', 'tensor')
- up_grad: float32 [1536, 4096], P('dp', 'tensor')
- down_grad: float32 [4096, 1536], P('tensor', 'dp')
The draws below stay inside these ranges and needn't reach their ends.
Inputs may be any that keep to these rules, and one draw needn't show every extreme that they name: `segment_ids`: within each sequence the ids never fall, every one of 0 to 2 holds one run of rows, and one segment is longer than 384.
All inputs are finite; a program needn't handle non-finite values.
Results may differ from the reference program's by a relative error of at most 0.025.
Values may be sent and summed in bfloat16 or wider, within the bound.
No kernel may reach another device: no remote copies, remote signals or barrier semaphores. Data moves between devices by JAX's collectives and lax.ppermute only.
A program may use at most 192 MiB of HBM per device.

```python
import math
import jax
import jax.numpy as jnp
from jax import lax

D = 1536
HEADS = 24
HEAD = 64
FF = 4096
TEXT_D = 4096
COND_D = 1024
TXT = 256
SEGS = 3
TOK_DEV = 128
LENGTH = 512
TOKENS = 16384
N_DP = 32


def draw_segment_ids(key, part):
    key = jax.random.fold_in(key, 7)
    key_big, key_small = jax.random.split(key, 2)
    groups = TOKENS // LENGTH
    biggest = jax.random.randint(key_big, (groups,), 0, SEGS)
    most_small = (TOK_DEV - 1) // (SEGS - 1)
    small = jax.random.randint(key_small, (groups, SEGS), 1, most_small + 1)
    labels = jnp.arange(SEGS, dtype=jnp.int32)
    chosen = labels[None, :] == biggest[:, None]
    small = jnp.where(chosen, 0, small)
    big_len = LENGTH - jnp.sum(small, axis=1)
    lengths = jnp.where(chosen, big_len[:, None], small)
    starts = jnp.cumsum(lengths, axis=1) - lengths
    places = jnp.arange(LENGTH, dtype=jnp.int32)
    ids = jnp.sum((places[None, :, None] >= starts[:, None, 1:]).astype(jnp.int32), axis=-1)
    return ids.reshape(-1).astype(jnp.int32)


def touch_ends(array, own_key, least, top_value):
    place = [jax.random.randint(jax.random.fold_in(own_key, axis), (), 0, length) for axis, length in enumerate(array.shape)]
    widest = array.shape.index(max(array.shape))
    neighbour = place[:widest] + [(place[widest] + 1) % array.shape[widest]] + place[widest + 1:]
    return array.at[tuple(place)].set(least).at[tuple(neighbour)].set(top_value)


def levels(own_key, dims, shards, least, top_value):
    level, own = 1.0, jax.random.fold_in(own_key, 6)
    for position, parts in shards:
        steps = jnp.exp(jax.random.uniform(jax.random.fold_in(own, position), (parts,), jnp.float32, least / len(shards), top_value / len(shards)))
        level = level * jnp.repeat(steps, dims[position] // parts).reshape([-1 if axis == position else 1 for axis in range(len(dims))])
    return level


def centred(key, shape, spread, bound, pieces=(), kind=jnp.bfloat16):
    values = spread * jax.random.normal(key, shape, jnp.float32)
    if pieces:
        values = values * levels(key, shape, pieces, -0.22, 0.18)
    return jnp.clip(values, -bound, bound).astype(kind)


def setup_inputs(seed: int = 0) -> dict:
    key_list = jax.random.split(jax.random.key(seed), 20)
    block_in = centred(key_list[0], (TOKENS, D), 1.0, 6.0, ((0, 128),))
    out_grad = centred(key_list[1], (TOKENS, D), 1.0, 6.0, ((0, 128),))
    condition = centred(key_list[2], (N_DP * SEGS, COND_D), 1.0, 6.0, ((0, 32),))
    captions = centred(key_list[3], (N_DP * SEGS, TXT, TEXT_D), 1.0, 6.0, ((0, 32),))
    caption_len = touch_ends(jax.random.randint(key_list[4], (N_DP * SEGS,), TXT // 4, TXT + 1), jax.random.fold_in(key_list[4], 1), TXT // 4, TXT).astype(jnp.int32)
    segment_ids = draw_segment_ids(jax.random.fold_in(key_list[19], 71), 0)
    ada_weight = centred(key_list[6], (COND_D, 4 * D), COND_D ** -0.5, 0.1875, ((1, 4),))
    norm_gains = jnp.clip(1.0 + 0.15 * jax.random.normal(key_list[7], (4, D), jnp.float32), 0.25, 1.75)
    query_weight = centred(key_list[8], (D, D), D ** -0.5, 0.15625, ((1, 4),))
    key_weight = centred(key_list[9], (D, D), D ** -0.5, 0.15625, ((1, 4),))
    value_weight = centred(key_list[10], (D, D), D ** -0.5, 0.15625, ((1, 4),))
    head_gains = jnp.clip(1.0 + 0.15 * jax.random.normal(key_list[11], (3, HEAD), jnp.float32), 0.25, 1.75)
    textkey_weight = centred(key_list[12], (TEXT_D, D), TEXT_D ** -0.5, 0.09375, ((1, 4),))
    textvalue_weight = centred(key_list[13], (TEXT_D, D), TEXT_D ** -0.5, 0.09375, ((1, 4),))
    cross_gate = jnp.clip(0.3 + 1.2 * jax.random.uniform(key_list[14], (HEADS,), jnp.float32) ** levels(key_list[14], (HEADS,), ((0, 4),), -0.2, 0.2), 0.3, 1.5)
    out_weight = centred(key_list[15], (D, D), D ** -0.5, 0.15625, ((0, 4),))
    gate_weight = centred(key_list[16], (D, FF), D ** -0.5, 0.15625, ((1, 4),))
    up_weight = centred(key_list[17], (D, FF), D ** -0.5, 0.15625, ((1, 4),))
    down_weight = centred(key_list[18], (FF, D), FF ** -0.5, 0.09375, ((0, 4),))
    return dict(block_in=block_in, out_grad=out_grad, condition=condition, captions=captions, caption_len=caption_len, segment_ids=segment_ids, ada_weight=ada_weight, norm_gains=norm_gains, query_weight=query_weight, key_weight=key_weight, value_weight=value_weight, head_gains=head_gains, textkey_weight=textkey_weight, textvalue_weight=textvalue_weight, cross_gate=cross_gate, out_weight=out_weight, gate_weight=gate_weight, up_weight=up_weight, down_weight=down_weight)


EPS = 1e-06
PRECISION = lax.Precision.HIGHEST

@jax.custom_vjp
def low(v):
    return lax.optimization_barrier(v.astype(jnp.bfloat16)).astype(jnp.float32)

@jax.custom_vjp
def low_back(v):
    return v

def low_keep(v):
    return (low(v), None)

def low_pass(kept, grad):
    return (grad,)

def back_keep(v):
    return (v, None)

def back_low(kept, grad):
    return (low(grad),)
low.defvjp(low_keep, low_pass)
low_back.defvjp(back_keep, back_low)

def matmul(left, right):
    return jnp.dot(left, right, precision=PRECISION)

def rms(values):
    return values * lax.rsqrt(lax.optimization_barrier(jnp.mean(values * values, axis=-1, keepdims=True)) + EPS)

def head_norm(values, gain):
    return rms(values.reshape(values.shape[0], -1, HEAD)) * gain

def rotate(values, cosine, sine):
    half = HEAD // 2
    first = values[..., :half]
    second = values[..., half:]
    cosine = cosine[:, None, :]
    sine = sine[:, None, :]
    return jnp.concatenate([first * cosine - second * sine, first * sine + second * cosine], axis=-1)

def rope_tables(segments):
    labels = jnp.arange(SEGS, dtype=jnp.int32)
    starts = lax.optimization_barrier(jnp.sum((segments[None, :] < labels[:, None]).astype(jnp.int32), axis=1))
    member = (segments[:, None] == labels[None, :]).astype(jnp.int32)
    places = jnp.arange(segments.shape[0], dtype=jnp.int32) - lax.optimization_barrier(jnp.sum(member * starts[None, :], axis=1))
    freqs = jnp.exp(jnp.arange(HEAD // 2, dtype=jnp.float32) * (-2.0 * math.log(10000.0) / HEAD))
    angles = places.astype(jnp.float32)[:, None] * freqs[None, :]
    return (jnp.cos(angles), jnp.sin(angles))

def attend(queries, keys, values, mask):
    scores = low_back(jnp.einsum('qhd,khd->hqk', queries, keys, precision=PRECISION) * HEAD ** (-0.5))
    scores = jnp.where(mask[None], scores, -1e+30)
    probs = low(jax.nn.softmax(scores, axis=-1))
    return jnp.einsum('hqk,khd->qhd', probs, values, precision=PRECISION)

def group_forward(weights, block, cond, text, caption_len, segments):
    ada_weight, norm_gains, query_weight, key_weight, value_weight, head_gains, textkey_weight, textvalue_weight, cross_gate, out_weight, gate_weight, up_weight, down_weight = weights
    width = block.shape[1]
    length = block.shape[0]
    cond_act = low(jax.nn.silu(cond))
    modulation = matmul(cond_act, ada_weight)
    member = (segments[:, None] == jnp.arange(SEGS, dtype=jnp.int32)[None, :]).astype(jnp.float32)
    mod_rows = matmul(member, modulation)
    scale_attn = mod_rows[:, :width]
    gate_attn = mod_rows[:, width:2 * width]
    scale_ffn = mod_rows[:, 2 * width:3 * width]
    gate_ffn = mod_rows[:, 3 * width:]
    cosine, sine = rope_tables(segments)
    attn_in = low(rms(block) * norm_gains[0] * (1.0 + scale_attn))
    raw_query = low_back(matmul(attn_in, query_weight))
    raw_key = low_back(matmul(attn_in, key_weight))
    values = low_back(low(matmul(attn_in, value_weight))).reshape(length, -1, HEAD)
    queries = low_back(low(rotate(head_norm(raw_query, head_gains[0]), cosine, sine)))
    keys = low_back(low(rotate(head_norm(raw_key, head_gains[1]), cosine, sine)))
    raw_text = low_back(matmul(text, textkey_weight))
    text_keys = low_back(low(head_norm(raw_text, head_gains[2])))
    text_values = low_back(low(matmul(text, textvalue_weight))).reshape(text.shape[0], -1, HEAD)
    self_mask = segments[:, None] == segments[None, :]
    key_segment = jnp.arange(SEGS * TXT, dtype=jnp.int32) // TXT
    key_place = jnp.arange(SEGS * TXT, dtype=jnp.int32) % TXT
    valid = key_place < caption_len[key_segment]
    cross_mask = (segments[:, None] == key_segment[None, :]) & valid[None, :]
    self_out = attend(queries, keys, values, self_mask)
    cross_out = attend(queries, text_keys, text_values, cross_mask)
    mixed = self_out + jnp.tanh(cross_gate)[None, :, None] * cross_out
    mixed = low_back(low(mixed.reshape(length, width)))
    attn_sum = low_back(matmul(mixed, out_weight))
    middle = block + jnp.tanh(gate_attn) * rms(attn_sum) * norm_gains[1]
    ffn_in = low(rms(middle) * norm_gains[2] * (1.0 + scale_ffn))
    gate_pre = low_back(matmul(ffn_in, gate_weight))
    up_pre = low_back(matmul(ffn_in, up_weight))
    hidden = low(jax.nn.silu(gate_pre) * up_pre)
    ffn_sum = low_back(matmul(hidden, down_weight))
    return middle + jnp.tanh(gate_ffn) * rms(ffn_sum) * norm_gains[3]

def reference(block_in, out_grad, condition, captions, caption_len, segment_ids, ada_weight, norm_gains, query_weight, key_weight, value_weight, head_gains, textkey_weight, textvalue_weight, cross_gate, out_weight, gate_weight, up_weight, down_weight):
    groups = TOKENS // LENGTH
    weights = tuple((item.astype(jnp.float32) for item in (ada_weight, norm_gains, query_weight, key_weight, value_weight, head_gains, textkey_weight, textvalue_weight, cross_gate, out_weight, gate_weight, up_weight, down_weight)))
    blocks = block_in.astype(jnp.float32).reshape(groups, LENGTH, D)
    conds = condition.astype(jnp.float32).reshape(groups, SEGS, COND_D)
    texts = captions.astype(jnp.float32).reshape(groups, SEGS * TXT, TEXT_D)
    lengths = caption_len.reshape(groups, SEGS)
    segments = segment_ids.reshape(groups, LENGTH)
    checked = jax.checkpoint(group_forward)

    def whole(block_all, *weight_list):

        def one_group(item):
            return checked(weight_list, item[0], item[1], item[2], item[3], item[4])
        return lax.map(one_group, (block_all, conds, texts, lengths, segments))
    result, pull = jax.vjp(whole, blocks, *weights)
    grads = pull(out_grad.astype(jnp.float32).reshape(groups, LENGTH, D))
    block_out = result.reshape(TOKENS, D).astype(jnp.bfloat16)
    in_grad = grads[0].reshape(TOKENS, D).astype(jnp.bfloat16)
    return (block_out, in_grad, grads[1], grads[2], grads[3], grads[4], grads[5], grads[6], grads[7], grads[8], grads[9], grads[10], grads[11], grads[12], grads[13])
```

```python
import math

import jax
import jax.numpy as jnp
from jax import lax
from jax.sharding import PartitionSpec as P

HEAD = 64
HEADS = 24
TXT = 256
SEGS = 3
EPS = 1e-06
PRECISION = lax.Precision.HIGHEST

RING = 4
PAIR = 2
CORE_SWAP = [(0, 1), (1, 0), (2, 3), (3, 2)]
CHIP_SWAP = [(0, 2), (2, 0), (1, 3), (3, 1)]


def dp_index(x, z, y):
    return (x * PAIR + z) * RING + y


def dp_perm(axis, step):
    pairs = []
    for x in range(RING):
        for z in range(PAIR):
            for y in range(RING):
                target = {
                    "x": ((x + step) % RING, z, y),
                    "y": (x, z, (y + step) % RING),
                    "z": (x, (z + step) % PAIR, y),
                }[axis]
                pairs.append((dp_index(x, z, y), dp_index(*target)))
    return pairs


def dp_place():
    index = lax.axis_index("dp")
    return {"x": index // (RING * PAIR), "z": index // RING % PAIR, "y": index % RING}


def swap_core(values):
    return lax.ppermute(values, "tensor", CORE_SWAP)


def swap_chip(values):
    return lax.ppermute(values, "tensor", CHIP_SWAP)


def contract_rows(left, right):
    return lax.dot_general(
        left, right, (((0,), (0,)), ((), ())), preferred_element_type=jnp.float32
    )


def times_transpose(left, right):
    return lax.dot_general(
        left, right, (((1,), (1,)), ((), ())), preferred_element_type=jnp.float32
    )


def gather_tensor(block):
    far = swap_chip(block)
    near = swap_core(block)
    return [block, near, far, swap_core(far)]


def scatter_tensor(blocks):
    near = swap_core(jnp.concatenate([blocks[1], blocks[3]], axis=0))
    rows = blocks[0].shape[0]
    far = (blocks[2].astype(jnp.float32) + near[rows:].astype(jnp.float32)).astype(near.dtype)
    return (
        blocks[0].astype(jnp.float32)
        + near[:rows].astype(jnp.float32)
        + swap_chip(far).astype(jnp.float32)
    )


def pick(stacked, index):
    return lax.dynamic_index_in_dim(stacked, index, 0, keepdims=False)


def gather_dp(block):
    block = block[None]
    for axis, size in (("z", PAIR), ("y", RING), ("x", RING)):
        block = jnp.concatenate(
            [block] + [lax.ppermute(block, "dp", dp_perm(axis, step)) for step in range(1, size)],
            axis=0,
        )
    return block


def scatter_stage(chunk_of, axis, place, size):
    total = chunk_of(place).astype(jnp.float32)
    for step in range(1, size):
        sent = chunk_of((place + step) % size)
        total = total + lax.ppermute(sent, "dp", dp_perm(axis, step)).astype(jnp.float32)
    return total


def scatter_dp(first_parts, second_parts, place):
    def whole(parts):
        return [
            part.reshape(RING, PAIR, RING, part.shape[0] // (RING * PAIR * RING), part.shape[1])
            for part in parts
        ]

    def along(parts, axis):
        def chunk_of(index):
            return jnp.concatenate(
                [
                    lax.dynamic_index_in_dim(part, index, axis, keepdims=False)
                    for part in parts
                ],
                axis=-1,
            )

        return chunk_of

    by_x = scatter_stage(along(whole(first_parts), 0), "x", place["x"], RING)
    by_y = scatter_stage(along(whole(second_parts), 2), "y", place["y"], RING)
    by_x = by_x.astype(jnp.bfloat16)
    by_y = by_y.astype(jnp.bfloat16)
    by_x = scatter_stage(along([by_x], 1), "y", place["y"], RING)
    by_y = scatter_stage(along([by_y], 0), "x", place["x"], RING)
    both = jnp.concatenate([by_x, by_y], axis=-1).astype(jnp.bfloat16)
    return scatter_stage(along([both], 0), "z", place["z"], PAIR)


def inverse_rms(values):
    return lax.rsqrt(jnp.mean(values * values, axis=-1, keepdims=True) + EPS)


def head_norm(values, gain):
    values = values.reshape(values.shape[0], -1, HEAD)
    return values * inverse_rms(values) * gain


def rotate(values, cosine, sine):
    half = HEAD // 2
    first = values[..., :half]
    second = values[..., half:]
    cosine = cosine[:, None, :]
    sine = sine[:, None, :]
    return jnp.concatenate(
        [first * cosine - second * sine, first * sine + second * cosine], axis=-1
    )


def rope_tables(segments, tokens, whole_segments):
    labels = jnp.arange(SEGS, dtype=jnp.int32)
    starts = jnp.sum((whole_segments[None, :] < labels[:, None]).astype(jnp.int32), axis=1)
    member = (segments[:, None] == labels[None, :]).astype(jnp.int32)
    places = tokens - jnp.sum(member * starts[None, :], axis=1)
    freqs = jnp.exp(jnp.arange(HEAD // 2, dtype=jnp.float32) * (-2.0 * math.log(10000.0) / HEAD))
    angles = places.astype(jnp.float32)[:, None] * freqs[None, :]
    return (jnp.cos(angles), jnp.sin(angles))


def masked_scores(queries, keys, mask):
    scores = jnp.einsum(
        "qhd,khd->hqk", queries, keys, preferred_element_type=jnp.float32
    ) * HEAD ** (-0.5)
    return jnp.where(mask[None], scores, -1e30)


def attend_forward(queries, keys, values, mask):
    scores = masked_scores(queries, keys, mask)
    top = jnp.max(scores, axis=-1, keepdims=True)
    expo = jnp.exp(scores - top)
    total = jnp.sum(expo, axis=-1, keepdims=True)
    probs = (expo / total).astype(jnp.bfloat16)
    output = jnp.einsum("hqk,khd->qhd", probs, values, preferred_element_type=jnp.float32)
    return (output, top + jnp.log(total))


def attend_backward(queries, keys, values, mask, log_total, grad_out, head_scale):
    probs = jnp.exp(masked_scores(queries, keys, mask) - log_total)
    grad_probs = jnp.einsum("qhd,khd->hqk", grad_out, values, preferred_element_type=jnp.float32)
    grad_probs = grad_probs * head_scale[:, None, None]
    grad_values = (
        jnp.einsum(
            "hqk,qhd->khd", probs.astype(jnp.bfloat16), grad_out, preferred_element_type=jnp.float32
        )
        * head_scale[None, :, None]
    )
    delta = jnp.sum(grad_probs * probs, axis=-1, keepdims=True)
    grad_scores = (probs * (grad_probs - delta)).astype(jnp.bfloat16)
    grad_queries = jnp.einsum(
        "hqk,khd->qhd", grad_scores, keys, preferred_element_type=jnp.float32
    ) * HEAD ** (-0.5)
    grad_keys = jnp.einsum(
        "hqk,qhd->khd", grad_scores, queries, preferred_element_type=jnp.float32
    ) * HEAD ** (-0.5)
    return (grad_queries, grad_keys, grad_values)


def narrow(values):
    return lax.optimization_barrier(values.astype(jnp.bfloat16)).astype(jnp.float32)


def shards(
    block_in,
    out_grad,
    condition,
    captions,
    caption_len,
    segment_ids,
    ada_weight,
    norm_gains,
    query_weight,
    key_weight,
    value_weight,
    head_gains,
    textkey_weight,
    textvalue_weight,
    cross_gate,
    out_weight,
    gate_weight,
    up_weight,
    down_weight,
):
    rows, width = block_in.shape
    length = segment_ids.shape[0]
    parts = length // rows
    local_heads = cross_gate.shape[0]
    position = lax.axis_index("tensor")
    place = dp_place()

    all_rows = jnp.concatenate(gather_tensor(block_in), axis=0)
    own_act = jax.nn.silu(condition.astype(jnp.float32)).astype(jnp.bfloat16)
    own_part = jnp.dot(own_act, ada_weight, preferred_element_type=jnp.float32)
    near_first = jnp.stack(gather_tensor(own_part))
    scale_attn, gate_attn, scale_ffn, gate_ffn = [
        pick(near_first, jnp.bitwise_xor(position, block)) for block in range(parts)
    ]
    order = [jnp.bitwise_xor(position, block) for block in range(parts)]
    segments = jnp.concatenate(
        [lax.dynamic_slice_in_dim(segment_ids, block * rows, rows) for block in order]
    )
    tokens = jnp.concatenate([block * rows + jnp.arange(rows, dtype=jnp.int32) for block in order])
    own_segments = segments[:rows]
    own_member = (own_segments[:, None] == jnp.arange(SEGS, dtype=jnp.int32)[None, :]).astype(
        jnp.float32
    )

    def per_row(table, ids):
        ids = ids[:, None]
        return jnp.where(ids == 0, table[0], jnp.where(ids == 1, table[1], table[2]))

    def segment_sum(values):
        return lax.dot_general(
            own_member, values, (((0,), (0,)), ((), ())), precision=PRECISION
        )

    cosine, sine = rope_tables(segments, tokens, segment_ids)
    self_mask = segments[:, None] == segments[None, :]
    key_segment = jnp.arange(SEGS * TXT, dtype=jnp.int32) // TXT
    key_place = jnp.arange(SEGS * TXT, dtype=jnp.int32) % TXT
    valid = key_place < jnp.repeat(caption_len, TXT)
    cross_mask = (segments[:, None] == key_segment[None, :]) & valid[None, :]

    all_f = all_rows.astype(jnp.float32)
    attn_rows = (
        all_f * inverse_rms(all_f) * norm_gains[0] * (1.0 + per_row(scale_attn, segments))
    ).astype(jnp.bfloat16)
    raw_query = jnp.dot(attn_rows, query_weight, preferred_element_type=jnp.float32)
    raw_key = jnp.dot(attn_rows, key_weight, preferred_element_type=jnp.float32)
    values_b = jnp.dot(attn_rows, value_weight, preferred_element_type=jnp.float32).astype(
        jnp.bfloat16
    )
    values_b = values_b.reshape(length, local_heads, HEAD)

    def prepare(query_part, key_part, gain_query, gain_key):
        return (
            rotate(head_norm(query_part, gain_query), cosine, sine),
            rotate(head_norm(key_part, gain_key), cosine, sine),
        )

    (query_f, key_f), prep_pull = jax.vjp(prepare, raw_query, raw_key, head_gains[0], head_gains[1])
    queries_b = query_f.astype(jnp.bfloat16)
    keys_b = key_f.astype(jnp.bfloat16)
    caption_flat = captions.reshape(-1, captions.shape[-1])
    text_raw = jnp.dot(caption_flat, textkey_weight, preferred_element_type=jnp.float32)
    text_key_f, text_pull = jax.vjp(head_norm, text_raw, head_gains[2])
    text_keys_b = text_key_f.astype(jnp.bfloat16)
    text_values_b = jnp.dot(caption_flat, textvalue_weight, preferred_element_type=jnp.float32)
    text_values_b = text_values_b.astype(jnp.bfloat16).reshape(
        caption_flat.shape[0], local_heads, HEAD
    )
    self_out, self_log = attend_forward(queries_b, keys_b, values_b, self_mask)
    cross_out, cross_log = attend_forward(queries_b, text_keys_b, text_values_b, cross_mask)
    tanh_gate = jnp.tanh(cross_gate)
    mixed = (
        (self_out + tanh_gate[None, :, None] * cross_out).reshape(length, -1).astype(jnp.bfloat16)
    )

    def row_blocks(values):
        values = values.astype(jnp.bfloat16)
        return [values[block * rows : (block + 1) * rows] for block in range(parts)]

    def all_of(block):
        return jnp.concatenate(gather_tensor(block.astype(jnp.bfloat16)), axis=0)

    attn_sum = scatter_tensor(
        row_blocks(jnp.dot(mixed, out_weight, preferred_element_type=jnp.float32))
    )
    block_f = block_in.astype(jnp.float32)
    attn_inv = inverse_rms(attn_sum)
    attn_unit = attn_sum * attn_inv
    attn_factor = jnp.tanh(per_row(gate_attn, own_segments)) * norm_gains[1]
    middle = block_f + attn_factor * attn_unit
    mid_inv = inverse_rms(middle)
    mid_unit = middle * mid_inv
    mid_factor = norm_gains[2] * (1.0 + per_row(scale_ffn, own_segments))
    ffn_rows = all_of(mid_unit * mid_factor)
    gate_pre = jnp.dot(ffn_rows, gate_weight, preferred_element_type=jnp.float32)
    up_pre = jnp.dot(ffn_rows, up_weight, preferred_element_type=jnp.float32)
    sigmoid_gate = jax.nn.sigmoid(gate_pre)
    silu_gate = gate_pre * sigmoid_gate
    hidden = (silu_gate * up_pre).astype(jnp.bfloat16)
    ffn_sum = scatter_tensor(
        row_blocks(jnp.dot(hidden, down_weight, preferred_element_type=jnp.float32))
    )
    ffn_inv = inverse_rms(ffn_sum)
    ffn_unit = ffn_sum * ffn_inv
    ffn_factor = jnp.tanh(per_row(gate_ffn, own_segments)) * norm_gains[3]
    block_out = (middle + ffn_factor * ffn_unit).astype(jnp.bfloat16)

    def norm_back(weighted, unit, inverse):
        return inverse * (weighted - unit * jnp.mean(weighted * unit, axis=-1, keepdims=True))

    grad_out = out_grad.astype(jnp.float32)
    sum_gate_ffn = segment_sum(grad_out * ffn_unit)
    grad_ffn = all_of(norm_back(grad_out * ffn_factor, ffn_unit, ffn_inv))
    grad_hidden = times_transpose(grad_ffn, down_weight)
    down_grad = contract_rows(grad_ffn, hidden).astype(jnp.bfloat16)
    grad_gate_b = (
        grad_hidden * up_pre * sigmoid_gate * (1.0 + gate_pre * (1.0 - sigmoid_gate))
    ).astype(jnp.bfloat16)
    grad_up_b = (grad_hidden * silu_gate).astype(jnp.bfloat16)
    grad_ffn_in = scatter_tensor(
        row_blocks(
            times_transpose(grad_gate_b, gate_weight) + times_transpose(grad_up_b, up_weight)
        )
    )
    gate_grad = contract_rows(ffn_rows, grad_gate_b).astype(jnp.bfloat16)
    up_grad = contract_rows(ffn_rows, grad_up_b).astype(jnp.bfloat16)
    sum_scale_ffn = segment_sum(grad_ffn_in * mid_unit)
    grad_middle = grad_out + norm_back(grad_ffn_in * mid_factor, mid_unit, mid_inv)
    sum_gate_attn = segment_sum(grad_middle * attn_unit)
    grad_attn = all_of(norm_back(grad_middle * attn_factor, attn_unit, attn_inv))
    grad_mixed_b = times_transpose(grad_attn, out_weight).astype(jnp.bfloat16)
    outw_grad = contract_rows(grad_attn, mixed).astype(jnp.bfloat16)
    grad_mixed_b = grad_mixed_b.reshape(length, local_heads, HEAD)
    gate_term = jnp.sum(grad_mixed_b.astype(jnp.float32) * cross_out, axis=(0, 2)) * (
        1.0 - tanh_gate * tanh_gate
    )
    unit_scale = jnp.ones((local_heads,), jnp.float32)
    query_cross, text_key_back, text_value_back = attend_backward(
        queries_b, text_keys_b, text_values_b, cross_mask, cross_log, grad_mixed_b, tanh_gate
    )
    query_self, key_self, value_self = attend_backward(
        queries_b, keys_b, values_b, self_mask, self_log, grad_mixed_b, unit_scale
    )
    grad_text_raw, grad_gain_text = text_pull(narrow(text_key_back))
    textkey_grad = contract_rows(caption_flat, grad_text_raw.astype(jnp.bfloat16))
    textvalue_grad = contract_rows(
        caption_flat, text_value_back.reshape(caption_flat.shape[0], -1).astype(jnp.bfloat16)
    )
    grad_raw_query, grad_raw_key, grad_gain_query, grad_gain_key = prep_pull(
        (narrow(query_self + query_cross), narrow(key_self))
    )
    grad_query_b = grad_raw_query.astype(jnp.bfloat16)
    grad_key_b = grad_raw_key.astype(jnp.bfloat16)
    grad_value_b = value_self.reshape(length, -1).astype(jnp.bfloat16)
    grad_attn_in = scatter_tensor(
        row_blocks(
            times_transpose(grad_query_b, query_weight)
            + times_transpose(grad_key_b, key_weight)
            + times_transpose(grad_value_b, value_weight)
        )
    )
    query_grad = contract_rows(attn_rows, grad_query_b).astype(jnp.bfloat16)
    key_grad = contract_rows(attn_rows, grad_key_b).astype(jnp.bfloat16)
    value_grad = contract_rows(attn_rows, grad_value_b).astype(jnp.bfloat16)
    block_inv = inverse_rms(block_f)
    block_unit = block_f * block_inv
    block_factor = norm_gains[0] * (1.0 + per_row(scale_attn, own_segments))
    sum_scale_attn = segment_sum(grad_attn_in * block_unit)
    in_grad = (
        grad_middle + norm_back(grad_attn_in * block_factor, block_unit, block_inv)
    ).astype(jnp.bfloat16)

    half = down_grad.shape[1] // 2
    ffn_group = scatter_dp(
        [gate_grad, down_grad[:, :half]], [up_grad, down_grad[:, half:]], place
    )
    text_group = scatter_dp(
        [textkey_grad.astype(jnp.bfloat16)], [textvalue_grad.astype(jnp.bfloat16)], place
    )
    attn_group = scatter_dp([query_grad, key_grad], [value_grad, outw_grad], place)
    hidden_cols = gate_grad.shape[1]
    gate_sum = ffn_group[:, :hidden_cols]
    up_sum = ffn_group[:, hidden_cols + half : 2 * hidden_cols + half]
    down_sum = jnp.concatenate(
        [ffn_group[:, hidden_cols : hidden_cols + half], ffn_group[:, 2 * hidden_cols + half :]],
        axis=1,
    ).T
    head_cols = query_grad.shape[1]
    query_sum, key_sum, value_sum, outw_sum = [
        attn_group[:, block * head_cols : (block + 1) * head_cols] for block in range(4)
    ]
    textkey_sum = text_group[:, :head_cols]
    textvalue_sum = text_group[:, head_cols:]

    sums = jnp.stack([sum_scale_attn, sum_gate_attn, sum_scale_ffn, sum_gate_ffn])
    own_sum = scatter_tensor([pick(sums, block) for block in order])
    gate_full = lax.dynamic_update_slice_in_dim(
        jnp.zeros((HEADS,), jnp.float32), gate_term, position * local_heads, 0
    )
    extras = jnp.concatenate([grad_gain_query, grad_gain_key, grad_gain_text, gate_full])
    extras = jnp.pad(extras, (0, width - extras.shape[0]))
    gathered = gather_dp(jnp.concatenate([own_sum, extras[None]], axis=0))
    conditions = gather_dp(condition).reshape(-1, condition.shape[1])
    acts = jax.nn.silu(conditions.astype(jnp.float32)).astype(jnp.bfloat16)
    parts_all = jnp.dot(acts, ada_weight, preferred_element_type=jnp.float32)
    all_sums = gathered[:, :SEGS].reshape(-1, width)
    is_gate = position % 2 == 1
    tanh_all = jnp.tanh(parts_all)
    factor = jnp.where(is_gate, tanh_all, 1.0 + parts_all)
    slope = jnp.where(is_gate, 1.0 - tanh_all * tanh_all, 1.0)
    grad_mod = all_sums * slope * pick(norm_gains, position)
    ada_rows = acts.shape[1] // (RING * PAIR * RING)
    own_cols = lax.dynamic_slice_in_dim(
        acts.astype(jnp.float32), lax.axis_index("dp") * ada_rows, ada_rows, 1
    )
    ada_grad = lax.dot_general(own_cols, grad_mod, (((0,), (0,)), ((), ())), precision=PRECISION)
    own_gain = jnp.sum(all_sums * factor, axis=0)
    own_extras = jnp.sum(gathered[:, SEGS], axis=0)
    last = jnp.stack(gather_tensor(jnp.stack([own_gain, own_extras])))
    norm_grads = jnp.stack([pick(last[:, 0], block) for block in order])
    extras_sum = jnp.sum(last[:, 1], axis=0)
    head_grads = extras_sum[: 3 * HEAD].reshape(3, HEAD)
    crossgate_grad = extras_sum[3 * HEAD : 3 * HEAD + HEADS]
    return (
        block_out,
        in_grad,
        ada_grad,
        norm_grads,
        query_sum,
        key_sum,
        value_sum,
        head_grads,
        textkey_sum,
        textvalue_sum,
        crossgate_grad,
        outw_sum.T,
        gate_sum,
        up_sum,
        down_sum,
    )


def solution(mesh):
    return jax.shard_map(
        shards,
        mesh=mesh,
        in_specs=(
            P(("dp", "tensor"), None),
            P(("dp", "tensor"), None),
            P("dp", None),
            P("dp", None, None),
            P("dp"),
            P("dp"),
            P(None, "tensor"),
            P(),
            P(None, "tensor"),
            P(None, "tensor"),
            P(None, "tensor"),
            P(),
            P(None, "tensor"),
            P(None, "tensor"),
            P("tensor"),
            P("tensor", None),
            P(None, "tensor"),
            P(None, "tensor"),
            P("tensor", None),
        ),
        out_specs=(
            P(("dp", "tensor"), None),
            P(("dp", "tensor"), None),
            P("dp", "tensor"),
            P(),
            P("dp", "tensor"),
            P("dp", "tensor"),
            P("dp", "tensor"),
            P(),
            P("dp", "tensor"),
            P("dp", "tensor"),
            P(),
            P("tensor", "dp"),
            P("dp", "tensor"),
            P("dp", "tensor"),
            P("tensor", "dp"),
        ),
        check_vma=False,
    )
```

```python
import functools
import math

import jax
import jax.numpy as jnp
from jax import lax
from jax.experimental import pallas as pl
from jax.experimental.pallas import tpu as pltpu
from jax.sharding import PartitionSpec as P

HEAD = 64
HEADS = 24
TXT = 256
SEGS = 3
EPS = 1e-06
PRECISION = lax.Precision.HIGHEST

RING = 4
PAIR = 2
CORE_SWAP = [(0, 1), (1, 0), (2, 3), (3, 2)]
CHIP_SWAP = [(0, 2), (2, 0), (1, 3), (3, 1)]


def dp_index(x, z, y):
    return (x * PAIR + z) * RING + y


def dp_perm(axis, step):
    pairs = []
    for x in range(RING):
        for z in range(PAIR):
            for y in range(RING):
                target = {
                    "x": ((x + step) % RING, z, y),
                    "y": (x, z, (y + step) % RING),
                    "z": (x, (z + step) % PAIR, y),
                }[axis]
                pairs.append((dp_index(x, z, y), dp_index(*target)))
    return pairs


def dp_place():
    index = lax.axis_index("dp")
    return {"x": index // (RING * PAIR), "z": index // RING % PAIR, "y": index % RING}


def swap_core(values):
    return lax.ppermute(values, "tensor", CORE_SWAP)


def swap_chip(values):
    return lax.ppermute(values, "tensor", CHIP_SWAP)


def contract_rows(left, right):
    return lax.dot_general(
        left, right, (((0,), (0,)), ((), ())), preferred_element_type=jnp.float32
    )


def times_transpose(left, right):
    return lax.dot_general(
        left, right, (((1,), (1,)), ((), ())), preferred_element_type=jnp.float32
    )


def gather_tensor(block):
    far = swap_chip(block)
    near = swap_core(block)
    return [block, near, far, swap_core(far)]


def scatter_tensor(blocks, with_sent=False):
    near = swap_core(jnp.concatenate([blocks[1], blocks[3]], axis=0))
    rows = blocks[0].shape[0]
    far = (blocks[2].astype(jnp.float32) + near[rows:].astype(jnp.float32)).astype(near.dtype)
    total = (
        blocks[0].astype(jnp.float32)
        + near[:rows].astype(jnp.float32)
        + swap_chip(far).astype(jnp.float32)
    )
    return (total, far) if with_sent else total


def pick(stacked, index):
    return lax.dynamic_index_in_dim(stacked, index, 0, keepdims=False)


def gather_dp(block):
    block = block[None]
    for axis, size in (("z", PAIR), ("y", RING), ("x", RING)):
        block = jnp.concatenate(
            [block] + [lax.ppermute(block, "dp", dp_perm(axis, step)) for step in range(1, size)],
            axis=0,
        )
    return block


BLOCKS = RING * PAIR * RING
SLOTS = BLOCKS // RING
SEND_ORDER = (2, 1, 3, 0)
VMEM_LIMIT = 50 * 2**20


def turn_kernel(source, target):
    target[...] = source[...].T


def turned(values, ties=()):
    tile = 512 if values.shape[1] % 512 == 0 else values.shape[1]
    return pl.pallas_call(
        lambda source, *rest: turn_kernel(source, rest[-1]),
        grid=(values.shape[1] // tile,),
        in_specs=[pl.BlockSpec((values.shape[0], tile), lambda step: (0, step))]
        + [pl.BlockSpec(memory_space=pl.ANY)] * len(ties),
        out_specs=pl.BlockSpec((tile, values.shape[0]), lambda step: (step, 0)),
        out_shape=jax.ShapeDtypeStruct(values.shape[::-1], values.dtype),
        compiler_params=pltpu.CompilerParams(vmem_limit_bytes=VMEM_LIMIT),
        cost_estimate=pl.CostEstimate(
            flops=0, bytes_accessed=4 * values.size, transcendentals=0
        ),
    )(values, *ties)


def send_chunk(step, make, outs, held, sems):
    def copy(place):
        return pltpu.make_async_copy(
            held.at[place % 2], outs[SEND_ORDER[place]], sems.at[place % 2]
        )

    for place in range(RING):

        @pl.when(step == place)
        def _(place=place):
            if place >= 2:
                copy(place - 2).wait()
            make(held.at[place % 2])
            copy(place).start()
            if place == RING - 1:
                copy(place - 1).wait()
                copy(place).wait()


def chunk_of_step(step, here):
    offset = jnp.where(step == 0, 2, jnp.where(step == 1, 1, jnp.where(step == 2, 3, 0)))
    return (here[0] + offset) % RING


def row_chunk_kernel(pairs, here, *refs):
    lefts, rights = refs[:pairs], refs[pairs : 2 * pairs]
    outs, held, sems = refs[-RING - 2 : -2], refs[-2], refs[-1]

    def make(slot):
        column = 0
        for left, right in zip(lefts, rights):
            rows = left[...].reshape(-1, left.shape[-1])
            product = jnp.dot(rows, right[...], preferred_element_type=jnp.float32)
            slot[:, column : column + right.shape[1]] = product.astype(jnp.bfloat16)
            column += right.shape[1]

    send_chunk(pl.program_id(0), make, outs, held, sems)


def row_chunks(pairs, axis, place, ties=()):
    lefts = [
        left.reshape(RING, PAIR, RING, left.shape[0] // BLOCKS, left.shape[1])
        for left, _ in pairs
    ]
    rights = [right for _, right in pairs]
    rows = lefts[0].shape[3]
    total = sum(right.shape[1] for right in rights)

    def spec(left):
        if axis == "x":
            return pl.BlockSpec(
                (1, PAIR, RING, rows, left.shape[-1]),
                lambda step, here: (chunk_of_step(step, here), 0, 0, 0, 0),
            )
        return pl.BlockSpec(
            (RING, PAIR, 1, rows, left.shape[-1]),
            lambda step, here: (0, 0, chunk_of_step(step, here), 0, 0),
        )

    return pl.pallas_call(
        functools.partial(row_chunk_kernel, len(pairs)),
        grid_spec=pltpu.PrefetchScalarGridSpec(
            num_scalar_prefetch=1,
            grid=(RING,),
            in_specs=[spec(left) for left in lefts]
            + [pl.BlockSpec(right.shape, lambda step, here: (0, 0)) for right in rights]
            + [pl.BlockSpec(memory_space=pl.ANY)] * len(ties),
            out_specs=[pl.BlockSpec(memory_space=pl.ANY)] * RING,
            scratch_shapes=[
                pltpu.VMEM((2, SLOTS * rows, total), jnp.bfloat16),
                pltpu.SemaphoreType.DMA((2,)),
            ],
        ),
        out_shape=[jax.ShapeDtypeStruct((SLOTS * rows, total), jnp.bfloat16)] * RING,
        compiler_params=pltpu.CompilerParams(vmem_limit_bytes=VMEM_LIMIT),
        cost_estimate=pl.CostEstimate(
            flops=sum(2 * left.size * right.shape[1] for left, right in zip(lefts, rights)),
            bytes_accessed=2 * sum(part.size for part in lefts + rights)
            + 2 * BLOCKS * rows * total,
            transcendentals=0,
        ),
    )(place[axis].reshape(1), *lefts, *rights, *ties)


def column_chunk_kernel(pieces, here, left, *refs):
    rights = refs[:pieces]
    outs, held, sems = refs[-RING - 2 : -2], refs[-2], refs[-1]

    def make(slot):
        lanes = rights[0].shape[1]
        for piece, right in enumerate(rights):
            product = jnp.dot(left[...], right[...], preferred_element_type=jnp.float32)
            slot[:, piece * lanes : (piece + 1) * lanes] = product.astype(jnp.bfloat16)

    send_chunk(pl.program_id(0), make, outs, held, sems)


def column_chunks(left, right, axis, place, ties=()):
    rows, depth = left.shape
    columns = right.shape[1]
    if axis == "x":
        specs = [
            pl.BlockSpec(
                (depth, columns // RING), lambda step, here: (0, chunk_of_step(step, here))
            )
        ]
    else:
        specs = [
            pl.BlockSpec(
                (depth, columns // BLOCKS),
                lambda step, here, slot=slot: (0, slot * RING + chunk_of_step(step, here)),
            )
            for slot in range(SLOTS)
        ]
    return pl.pallas_call(
        functools.partial(column_chunk_kernel, len(specs)),
        grid_spec=pltpu.PrefetchScalarGridSpec(
            num_scalar_prefetch=1,
            grid=(RING,),
            in_specs=[pl.BlockSpec((rows, depth), lambda step, here: (0, 0))]
            + specs
            + [pl.BlockSpec(memory_space=pl.ANY)] * len(ties),
            out_specs=[pl.BlockSpec(memory_space=pl.ANY)] * RING,
            scratch_shapes=[
                pltpu.VMEM((2, rows, columns // RING), jnp.bfloat16),
                pltpu.SemaphoreType.DMA((2,)),
            ],
        ),
        out_shape=[jax.ShapeDtypeStruct((rows, columns // RING), jnp.bfloat16)] * RING,
        compiler_params=pltpu.CompilerParams(vmem_limit_bytes=VMEM_LIMIT),
        cost_estimate=pl.CostEstimate(
            flops=2 * rows * depth * columns,
            bytes_accessed=2 * (rows * depth + depth * columns + rows * columns),
            transcendentals=0,
        ),
    )(place[axis].reshape(1), left, *([right] * len(specs)), *ties)


def add_up(refs, index):
    total = refs[0][index].astype(jnp.float32)
    for ref in refs[1:]:
        total = total + ref[index].astype(jnp.float32)
    return total


def second_stage_kernel(by_rows, here, *refs):
    by_x, by_y = refs[:RING], refs[RING : 2 * RING]
    outs_x, outs_y = refs[-2 * RING : -RING], refs[-RING:]
    lanes = outs_x[0].shape[1] // PAIR
    for offset in range(RING):
        next_x = (here[0] + offset) % RING
        next_y = (here[2] + offset) % RING
        for z in range(PAIR):
            for parts, outs, slot in (
                (by_x, outs_x, z * RING + next_y),
                (by_y, outs_y, next_x * PAIR + z),
            ):
                if by_rows:
                    outs[offset][z] = add_up(parts, slot).astype(jnp.bfloat16)
                else:
                    index = (slice(None), pl.ds(pl.multiple_of(slot * lanes, lanes), lanes))
                    outs[offset][:, z * lanes : (z + 1) * lanes] = add_up(parts, index).astype(
                        jnp.bfloat16
                    )


def third_stage_kernel(by_rows, here, *refs):
    by_x, by_y = refs[:RING], refs[RING : 2 * RING]
    kept, sent = refs[-2], refs[-1]
    for out, z in ((kept, here[1]), (sent, (here[1] + 1) % PAIR)):
        if by_rows:
            width = by_x[0].shape[-1]
            out[:, :width] = add_up(by_x, z).astype(jnp.bfloat16)
            out[:, width:] = add_up(by_y, z).astype(jnp.bfloat16)
        else:
            rows, lanes = by_x[0].shape[0], out.shape[1]
            index = (slice(None), pl.ds(pl.multiple_of(z * lanes, lanes), lanes))
            out[:rows, :] = add_up(by_x, index).astype(jnp.bfloat16)
            out[rows:, :] = add_up(by_y, index).astype(jnp.bfloat16)


def stage_call(kernel, here, operands, outs, ties):
    whole = pl.BlockSpec(memory_space=pltpu.VMEM)
    return pl.pallas_call(
        kernel,
        in_specs=[pl.BlockSpec(memory_space=pltpu.SMEM)]
        + [whole] * len(operands)
        + [pl.BlockSpec(memory_space=pl.ANY)] * len(ties),
        out_specs=[whole] * len(outs),
        out_shape=[jax.ShapeDtypeStruct(shape, jnp.bfloat16) for shape in outs],
        compiler_params=pltpu.CompilerParams(vmem_limit_bytes=VMEM_LIMIT),
        cost_estimate=pl.CostEstimate(
            flops=0,
            bytes_accessed=2 * sum(part.size for part in operands)
            + 2 * sum(math.prod(shape) for shape in outs),
            transcendentals=0,
        ),
    )(here, *operands, *ties)


def exchange(chunks, axis):
    return [chunks[0]] + [
        lax.ppermute(chunks[step], "dp", dp_perm(axis, step)) for step in range(1, len(chunks))
    ]


def finish_sum(by_x, by_y, by_rows, place, ties):
    here = jnp.stack([place["x"], place["z"], place["y"]])
    got = exchange(by_x, "x") + exchange(by_y, "y")
    if by_rows:
        got = [part.reshape(SLOTS, part.shape[0] // SLOTS, part.shape[1]) for part in got]
        shapes = [(PAIR,) + got[0].shape[1:], (PAIR,) + got[RING].shape[1:]]
        last = (got[0].shape[1], got[0].shape[2] + got[RING].shape[2])
    else:
        shapes = [
            (got[0].shape[0], PAIR * got[0].shape[1] // SLOTS),
            (got[RING].shape[0], PAIR * got[RING].shape[1] // SLOTS),
        ]
        last = (got[0].shape[0] + got[RING].shape[0], got[0].shape[1] // SLOTS)
    parts = stage_call(
        functools.partial(second_stage_kernel, by_rows),
        here,
        got,
        [shapes[0]] * RING + [shapes[1]] * RING,
        ties[0],
    )
    got = exchange(parts[:RING], "y") + exchange(parts[RING:], "x")
    kept, sent = stage_call(
        functools.partial(third_stage_kernel, by_rows), here, got, [last, last], ties[1]
    )
    return kept.astype(jnp.float32) + exchange([kept, sent], "z")[1].astype(jnp.float32)


def inverse_rms(values):
    return lax.rsqrt(jnp.mean(values * values, axis=-1, keepdims=True) + EPS)


def head_norm(values, gain):
    values = values.reshape(values.shape[0], -1, HEAD)
    return values * inverse_rms(values) * gain


def rotate(values, cosine, sine):
    half = HEAD // 2
    first = values[..., :half]
    second = values[..., half:]
    cosine = cosine[:, None, :]
    sine = sine[:, None, :]
    return jnp.concatenate(
        [first * cosine - second * sine, first * sine + second * cosine], axis=-1
    )


def rope_tables(segments, tokens, whole_segments):
    labels = jnp.arange(SEGS, dtype=jnp.int32)
    starts = jnp.sum((whole_segments[None, :] < labels[:, None]).astype(jnp.int32), axis=1)
    member = (segments[:, None] == labels[None, :]).astype(jnp.int32)
    places = tokens - jnp.sum(member * starts[None, :], axis=1)
    freqs = jnp.exp(jnp.arange(HEAD // 2, dtype=jnp.float32) * (-2.0 * math.log(10000.0) / HEAD))
    angles = places.astype(jnp.float32)[:, None] * freqs[None, :]
    return (jnp.cos(angles), jnp.sin(angles))


def masked_scores(queries, keys, mask):
    scores = jnp.einsum(
        "qhd,khd->hqk", queries, keys, preferred_element_type=jnp.float32
    ) * HEAD ** (-0.5)
    return jnp.where(mask[None], scores, -1e30)


def attend_forward(queries, keys, values, mask):
    scores = masked_scores(queries, keys, mask)
    top = jnp.max(scores, axis=-1, keepdims=True)
    expo = jnp.exp(scores - top)
    total = jnp.sum(expo, axis=-1, keepdims=True)
    probs = (expo / total).astype(jnp.bfloat16)
    output = jnp.einsum("hqk,khd->qhd", probs, values, preferred_element_type=jnp.float32)
    return (output, top + jnp.log(total))


def attend_backward(queries, keys, values, mask, log_total, grad_out, head_scale):
    probs = jnp.exp(masked_scores(queries, keys, mask) - log_total)
    grad_probs = jnp.einsum("qhd,khd->hqk", grad_out, values, preferred_element_type=jnp.float32)
    grad_probs = grad_probs * head_scale[:, None, None]
    grad_values = (
        jnp.einsum(
            "hqk,qhd->khd", probs.astype(jnp.bfloat16), grad_out, preferred_element_type=jnp.float32
        )
        * head_scale[None, :, None]
    )
    delta = jnp.sum(grad_probs * probs, axis=-1, keepdims=True)
    grad_scores = (probs * (grad_probs - delta)).astype(jnp.bfloat16)
    grad_queries = jnp.einsum(
        "hqk,khd->qhd", grad_scores, keys, preferred_element_type=jnp.float32
    ) * HEAD ** (-0.5)
    grad_keys = jnp.einsum(
        "hqk,qhd->khd", grad_scores, queries, preferred_element_type=jnp.float32
    ) * HEAD ** (-0.5)
    return (grad_queries, grad_keys, grad_values)


def narrow(values):
    return lax.optimization_barrier(values.astype(jnp.bfloat16)).astype(jnp.float32)


def shards(
    block_in,
    out_grad,
    condition,
    captions,
    caption_len,
    segment_ids,
    ada_weight,
    norm_gains,
    query_weight,
    key_weight,
    value_weight,
    head_gains,
    textkey_weight,
    textvalue_weight,
    cross_gate,
    out_weight,
    gate_weight,
    up_weight,
    down_weight,
):
    rows, width = block_in.shape
    length = segment_ids.shape[0]
    parts = length // rows
    local_heads = cross_gate.shape[0]
    position = lax.axis_index("tensor")
    place = dp_place()

    all_rows = jnp.concatenate(gather_tensor(block_in), axis=0)
    own_act = jax.nn.silu(condition.astype(jnp.float32)).astype(jnp.bfloat16)
    own_part = jnp.dot(own_act, ada_weight, preferred_element_type=jnp.float32)
    near_first = jnp.stack(gather_tensor(own_part))
    scale_attn, gate_attn, scale_ffn, gate_ffn = [
        pick(near_first, jnp.bitwise_xor(position, block)) for block in range(parts)
    ]
    order = [jnp.bitwise_xor(position, block) for block in range(parts)]
    segments = jnp.concatenate(
        [lax.dynamic_slice_in_dim(segment_ids, block * rows, rows) for block in order]
    )
    tokens = jnp.concatenate([block * rows + jnp.arange(rows, dtype=jnp.int32) for block in order])
    own_segments = segments[:rows]
    own_member = (own_segments[:, None] == jnp.arange(SEGS, dtype=jnp.int32)[None, :]).astype(
        jnp.float32
    )

    def per_row(table, ids):
        ids = ids[:, None]
        return jnp.where(ids == 0, table[0], jnp.where(ids == 1, table[1], table[2]))

    def segment_sum(values):
        return lax.dot_general(
            own_member, values, (((0,), (0,)), ((), ())), precision=PRECISION
        )

    cosine, sine = rope_tables(segments, tokens, segment_ids)
    self_mask = segments[:, None] == segments[None, :]
    key_segment = jnp.arange(SEGS * TXT, dtype=jnp.int32) // TXT
    key_place = jnp.arange(SEGS * TXT, dtype=jnp.int32) % TXT
    valid = key_place < jnp.repeat(caption_len, TXT)
    cross_mask = (segments[:, None] == key_segment[None, :]) & valid[None, :]

    all_f = all_rows.astype(jnp.float32)
    attn_rows = (
        all_f * inverse_rms(all_f) * norm_gains[0] * (1.0 + per_row(scale_attn, segments))
    ).astype(jnp.bfloat16)
    raw_query = jnp.dot(attn_rows, query_weight, preferred_element_type=jnp.float32)
    raw_key = jnp.dot(attn_rows, key_weight, preferred_element_type=jnp.float32)
    values_b = jnp.dot(attn_rows, value_weight, preferred_element_type=jnp.float32).astype(
        jnp.bfloat16
    )
    values_b = values_b.reshape(length, local_heads, HEAD)

    def prepare(query_part, key_part, gain_query, gain_key):
        return (
            rotate(head_norm(query_part, gain_query), cosine, sine),
            rotate(head_norm(key_part, gain_key), cosine, sine),
        )

    (query_f, key_f), prep_pull = jax.vjp(prepare, raw_query, raw_key, head_gains[0], head_gains[1])
    queries_b = query_f.astype(jnp.bfloat16)
    keys_b = key_f.astype(jnp.bfloat16)
    caption_flat = captions.reshape(-1, captions.shape[-1])
    text_raw = jnp.dot(caption_flat, textkey_weight, preferred_element_type=jnp.float32)
    text_key_f, text_pull = jax.vjp(head_norm, text_raw, head_gains[2])
    text_keys_b = text_key_f.astype(jnp.bfloat16)
    text_values_b = jnp.dot(caption_flat, textvalue_weight, preferred_element_type=jnp.float32)
    text_values_b = text_values_b.astype(jnp.bfloat16).reshape(
        caption_flat.shape[0], local_heads, HEAD
    )
    self_out, self_log = attend_forward(queries_b, keys_b, values_b, self_mask)
    cross_out, cross_log = attend_forward(queries_b, text_keys_b, text_values_b, cross_mask)
    tanh_gate = jnp.tanh(cross_gate)
    mixed = (
        (self_out + tanh_gate[None, :, None] * cross_out).reshape(length, -1).astype(jnp.bfloat16)
    )

    def row_blocks(values):
        values = values.astype(jnp.bfloat16)
        return [values[block * rows : (block + 1) * rows] for block in range(parts)]

    def all_of(block):
        return jnp.concatenate(gather_tensor(block.astype(jnp.bfloat16)), axis=0)

    attn_sum = scatter_tensor(
        row_blocks(jnp.dot(mixed, out_weight, preferred_element_type=jnp.float32))
    )
    block_f = block_in.astype(jnp.float32)
    attn_inv = inverse_rms(attn_sum)
    attn_unit = attn_sum * attn_inv
    attn_factor = jnp.tanh(per_row(gate_attn, own_segments)) * norm_gains[1]
    middle = block_f + attn_factor * attn_unit
    mid_inv = inverse_rms(middle)
    mid_unit = middle * mid_inv
    mid_factor = norm_gains[2] * (1.0 + per_row(scale_ffn, own_segments))
    ffn_rows = all_of(mid_unit * mid_factor)
    ffn_rows_t = turned(ffn_rows)
    gate_pre = jnp.dot(ffn_rows, gate_weight, preferred_element_type=jnp.float32)
    up_pre = jnp.dot(ffn_rows, up_weight, preferred_element_type=jnp.float32)
    sigmoid_gate = jax.nn.sigmoid(gate_pre)
    silu_gate = gate_pre * sigmoid_gate
    hidden = (silu_gate * up_pre).astype(jnp.bfloat16)
    ffn_sum = scatter_tensor(
        row_blocks(jnp.dot(hidden, down_weight, preferred_element_type=jnp.float32))
    )
    ffn_inv = inverse_rms(ffn_sum)
    ffn_unit = ffn_sum * ffn_inv
    ffn_factor = jnp.tanh(per_row(gate_ffn, own_segments)) * norm_gains[3]
    block_out = (middle + ffn_factor * ffn_unit).astype(jnp.bfloat16)

    def norm_back(weighted, unit, inverse):
        return inverse * (weighted - unit * jnp.mean(weighted * unit, axis=-1, keepdims=True))

    grad_out = out_grad.astype(jnp.float32)
    sum_gate_ffn = segment_sum(grad_out * ffn_unit)
    grad_ffn = all_of(norm_back(grad_out * ffn_factor, ffn_unit, ffn_inv))
    grad_hidden = times_transpose(grad_ffn, down_weight)
    grad_gate_b = (
        grad_hidden * up_pre * sigmoid_gate * (1.0 + gate_pre * (1.0 - sigmoid_gate))
    ).astype(jnp.bfloat16)
    grad_up_b = (grad_hidden * silu_gate).astype(jnp.bfloat16)
    grad_ffn_in, sent_ffn = scatter_tensor(
        row_blocks(
            times_transpose(grad_gate_b, gate_weight) + times_transpose(grad_up_b, up_weight)
        ),
        with_sent=True,
    )
    half = hidden.shape[1] // 2
    grad_ffn_t = turned(grad_ffn)
    ffn_by_x = row_chunks(
        [(ffn_rows_t, grad_gate_b), (grad_ffn_t, hidden[:, :half])], "x", place, (sent_ffn,)
    )
    ffn_by_y = row_chunks(
        [(ffn_rows_t, grad_up_b), (grad_ffn_t, hidden[:, half:])], "y", place, (sent_ffn,)
    )
    sum_scale_ffn = segment_sum(grad_ffn_in * mid_unit)
    grad_middle = grad_out + norm_back(grad_ffn_in * mid_factor, mid_unit, mid_inv)
    sum_gate_attn = segment_sum(grad_middle * attn_unit)
    grad_attn = all_of(norm_back(grad_middle * attn_factor, attn_unit, attn_inv))
    grad_mixed_b = times_transpose(grad_attn, out_weight).astype(jnp.bfloat16)
    grad_mixed_b = grad_mixed_b.reshape(length, local_heads, HEAD)
    gate_term = jnp.sum(grad_mixed_b.astype(jnp.float32) * cross_out, axis=(0, 2)) * (
        1.0 - tanh_gate * tanh_gate
    )
    unit_scale = jnp.ones((local_heads,), jnp.float32)
    query_cross, text_key_back, text_value_back = attend_backward(
        queries_b, text_keys_b, text_values_b, cross_mask, cross_log, grad_mixed_b, tanh_gate
    )
    query_self, key_self, value_self = attend_backward(
        queries_b, keys_b, values_b, self_mask, self_log, grad_mixed_b, unit_scale
    )
    grad_text_raw, grad_gain_text = text_pull(narrow(text_key_back))
    text_by_x = column_chunks(
        turned(grad_text_raw.astype(jnp.bfloat16)), caption_flat, "x", place
    )
    text_by_y = column_chunks(
        turned(text_value_back.reshape(caption_flat.shape[0], -1).astype(jnp.bfloat16)),
        caption_flat,
        "y",
        place,
    )
    grad_raw_query, grad_raw_key, grad_gain_query, grad_gain_key = prep_pull(
        (narrow(query_self + query_cross), narrow(key_self))
    )
    grad_query_b = grad_raw_query.astype(jnp.bfloat16)
    grad_key_b = grad_raw_key.astype(jnp.bfloat16)
    grad_value_b = value_self.reshape(length, -1).astype(jnp.bfloat16)
    grad_attn_in, sent_attn = scatter_tensor(
        row_blocks(
            times_transpose(grad_query_b, query_weight)
            + times_transpose(grad_key_b, key_weight)
            + times_transpose(grad_value_b, value_weight)
        ),
        with_sent=True,
    )
    attn_rows_t = turned(attn_rows)
    attn_by_x = row_chunks(
        [(attn_rows_t, grad_query_b), (attn_rows_t, grad_key_b)], "x", place, (sent_attn,)
    )
    attn_by_y = row_chunks(
        [(attn_rows_t, grad_value_b), (turned(grad_attn), mixed)], "y", place, (sent_attn,)
    )
    block_inv = inverse_rms(block_f)
    block_unit = block_f * block_inv
    block_factor = norm_gains[0] * (1.0 + per_row(scale_attn, own_segments))
    sum_scale_attn = segment_sum(grad_attn_in * block_unit)
    in_grad = (
        grad_middle + norm_back(grad_attn_in * block_factor, block_unit, block_inv)
    ).astype(jnp.bfloat16)

    ffn_group = finish_sum(ffn_by_x, ffn_by_y, True, place, ((text_value_back,), (query_self,)))
    text_group = finish_sum(text_by_x, text_by_y, False, place, ((attn_by_x[0],), (attn_by_y[0],)))
    attn_group = finish_sum(attn_by_x, attn_by_y, True, place, ((), ()))
    hidden_cols = grad_gate_b.shape[1]
    gate_sum = ffn_group[:, :hidden_cols]
    up_sum = ffn_group[:, hidden_cols + half : 2 * hidden_cols + half]
    down_sum = jnp.concatenate(
        [ffn_group[:, hidden_cols : hidden_cols + half], ffn_group[:, 2 * hidden_cols + half :]],
        axis=1,
    ).T
    head_cols = grad_query_b.shape[1]
    query_sum, key_sum, value_sum, outw_sum = [
        attn_group[:, block * head_cols : (block + 1) * head_cols] for block in range(4)
    ]
    textkey_sum = text_group[:head_cols].T
    textvalue_sum = text_group[head_cols:].T

    sums = jnp.stack([sum_scale_attn, sum_gate_attn, sum_scale_ffn, sum_gate_ffn])
    own_sum = scatter_tensor([pick(sums, block) for block in order])
    gate_full = lax.dynamic_update_slice_in_dim(
        jnp.zeros((HEADS,), jnp.float32), gate_term, position * local_heads, 0
    )
    extras = jnp.concatenate([grad_gain_query, grad_gain_key, grad_gain_text, gate_full])
    extras = jnp.pad(extras, (0, width - extras.shape[0]))
    gathered = gather_dp(jnp.concatenate([own_sum, extras[None]], axis=0))
    conditions = gather_dp(condition).reshape(-1, condition.shape[1])
    acts = jax.nn.silu(conditions.astype(jnp.float32)).astype(jnp.bfloat16)
    parts_all = jnp.dot(acts, ada_weight, preferred_element_type=jnp.float32)
    all_sums = gathered[:, :SEGS].reshape(-1, width)
    is_gate = position % 2 == 1
    tanh_all = jnp.tanh(parts_all)
    factor = jnp.where(is_gate, tanh_all, 1.0 + parts_all)
    slope = jnp.where(is_gate, 1.0 - tanh_all * tanh_all, 1.0)
    grad_mod = all_sums * slope * pick(norm_gains, position)
    ada_rows = acts.shape[1] // BLOCKS
    own_cols = lax.dynamic_slice_in_dim(
        acts.astype(jnp.float32), lax.axis_index("dp") * ada_rows, ada_rows, 1
    )
    ada_grad = lax.dot_general(own_cols, grad_mod, (((0,), (0,)), ((), ())), precision=PRECISION)
    own_gain = jnp.sum(all_sums * factor, axis=0)
    own_extras = jnp.sum(gathered[:, SEGS], axis=0)
    last = jnp.stack(gather_tensor(jnp.stack([own_gain, own_extras])))
    norm_grads = jnp.stack([pick(last[:, 0], block) for block in order])
    extras_sum = jnp.sum(last[:, 1], axis=0)
    head_grads = extras_sum[: 3 * HEAD].reshape(3, HEAD)
    crossgate_grad = extras_sum[3 * HEAD : 3 * HEAD + HEADS]
    return (
        block_out,
        in_grad,
        ada_grad,
        norm_grads,
        query_sum,
        key_sum,
        value_sum,
        head_grads,
        textkey_sum,
        textvalue_sum,
        crossgate_grad,
        outw_sum.T,
        gate_sum,
        up_sum,
        down_sum,
    )


def solution(mesh):
    return jax.shard_map(
        shards,
        mesh=mesh,
        in_specs=(
            P(("dp", "tensor"), None),
            P(("dp", "tensor"), None),
            P("dp", None),
            P("dp", None, None),
            P("dp"),
            P("dp"),
            P(None, "tensor"),
            P(),
            P(None, "tensor"),
            P(None, "tensor"),
            P(None, "tensor"),
            P(),
            P(None, "tensor"),
            P(None, "tensor"),
            P("tensor"),
            P("tensor", None),
            P(None, "tensor"),
            P(None, "tensor"),
            P("tensor", None),
        ),
        out_specs=(
            P(("dp", "tensor"), None),
            P(("dp", "tensor"), None),
            P("dp", "tensor"),
            P(),
            P("dp", "tensor"),
            P("dp", "tensor"),
            P("dp", "tensor"),
            P(),
            P("dp", "tensor"),
            P("dp", "tensor"),
            P(),
            P("tensor", "dp"),
            P("dp", "tensor"),
            P("dp", "tensor"),
            P("tensor", "dp"),
        ),
        check_vma=False,
    )
```

```python
import functools
import math

import jax
import jax.numpy as jnp
from jax import lax
from jax.experimental import pallas as pl
from jax.experimental.pallas import tpu as pltpu
from jax.sharding import PartitionSpec as P

HEAD = 64
HEADS = 24
TXT = 256
SEGS = 3
EPS = 1e-06
LANES = 2 * HEAD
SHUT = 256.0
ROOT = HEAD ** (-0.5)
VMEM_LIMIT = 50 * 2**20

RING = 4
PAIR = 2
BLOCKS = RING * PAIR * RING
SLOTS = BLOCKS // RING
SEND_ORDER = (2, 1, 3, 0)
CORE_SWAP = [(0, 1), (1, 0), (2, 3), (3, 2)]
CHIP_SWAP = [(0, 2), (2, 0), (1, 3), (3, 1)]
ROW_ORDER = (0, 2, 1, 3)

def dp_index(x, z, y):
    return (x * PAIR + z) * RING + y


def dp_perm(axis, step):
    pairs = []
    for x in range(RING):
        for z in range(PAIR):
            for y in range(RING):
                target = {
                    "x": ((x + step) % RING, z, y),
                    "y": (x, z, (y + step) % RING),
                    "z": (x, (z + step) % PAIR, y),
                }[axis]
                pairs.append((dp_index(x, z, y), dp_index(*target)))
    return pairs


def dp_place():
    index = lax.axis_index("dp")
    return {"x": index // (RING * PAIR), "z": index // RING % PAIR, "y": index % RING}


def swap_core(values):
    return lax.ppermute(values, "tensor", CORE_SWAP)


def swap_chip(values):
    return lax.ppermute(values, "tensor", CHIP_SWAP)


def times_transpose(left, right):
    return lax.dot_general(
        left, right, (((1,), (1,)), ((), ())), preferred_element_type=jnp.float32
    )


def gather_tensor(block):
    far = swap_chip(block)
    near = swap_core(block)
    return [block, far, near, swap_core(far)]


def scatter_tensor(upper, lower):
    near = swap_core(lower)
    rows = upper.shape[0] // 2
    far = (upper[rows:].astype(jnp.float32) + near[rows:].astype(jnp.float32)).astype(near.dtype)
    return [upper, near, swap_chip(far)], far


def gather_dp(block):
    block = block[None]
    for axis, size in (("z", PAIR), ("y", RING), ("x", RING)):
        block = jnp.concatenate(
            [block] + [lax.ppermute(block, "dp", dp_perm(axis, step)) for step in range(1, size)],
            axis=0,
        )
    return block


def turn_kernel(source, target):
    target[...] = source[...].T


def turned(values, ties=()):
    tile = 512 if values.shape[1] % 512 == 0 else values.shape[1]
    return pl.pallas_call(
        lambda source, *rest: turn_kernel(source, rest[-1]),
        grid=(values.shape[1] // tile,),
        in_specs=[pl.BlockSpec((values.shape[0], tile), lambda step: (0, step))]
        + [pl.BlockSpec(memory_space=pl.ANY)] * len(ties),
        out_specs=pl.BlockSpec((tile, values.shape[0]), lambda step: (step, 0)),
        out_shape=jax.ShapeDtypeStruct(values.shape[::-1], values.dtype),
        compiler_params=pltpu.CompilerParams(vmem_limit_bytes=VMEM_LIMIT),
        cost_estimate=pl.CostEstimate(
            flops=0, bytes_accessed=4 * values.size, transcendentals=0
        ),
    )(values, *ties)


def send_chunk(step, make, outs, held, sems):
    def copy(place):
        return pltpu.make_async_copy(
            held.at[place % 2], outs[SEND_ORDER[place]], sems.at[place % 2]
        )

    for place in range(RING):

        @pl.when(step == place)
        def _(place=place):
            if place >= 2:
                copy(place - 2).wait()
            make(held.at[place % 2])
            copy(place).start()
            if place == RING - 1:
                copy(place - 1).wait()
                copy(place).wait()


def chunk_of_step(step, here):
    offset = jnp.where(step == 0, 2, jnp.where(step == 1, 1, jnp.where(step == 2, 3, 0)))
    return (here[0] + offset) % RING


def row_chunk_kernel(pairs, here, *refs):
    lefts, rights = refs[:pairs], refs[pairs : 2 * pairs]
    outs, held, sems = refs[-RING - 2 : -2], refs[-2], refs[-1]

    def make(slot):
        column = 0
        for left, right in zip(lefts, rights):
            rows = left[...].reshape(-1, left.shape[-1])
            product = jnp.dot(rows, right[...], preferred_element_type=jnp.float32)
            slot[:, column : column + right.shape[1]] = product.astype(jnp.bfloat16)
            column += right.shape[1]

    send_chunk(pl.program_id(0), make, outs, held, sems)


def row_chunks(pairs, axis, place, ties=()):
    lefts = [
        left.reshape(RING, PAIR, RING, left.shape[0] // BLOCKS, left.shape[1])
        for left, _ in pairs
    ]
    rights = [right for _, right in pairs]
    rows = lefts[0].shape[3]
    total = sum(right.shape[1] for right in rights)

    def spec(left):
        if axis == "x":
            return pl.BlockSpec(
                (1, PAIR, RING, rows, left.shape[-1]),
                lambda step, here: (chunk_of_step(step, here), 0, 0, 0, 0),
            )
        return pl.BlockSpec(
            (RING, PAIR, 1, rows, left.shape[-1]),
            lambda step, here: (0, 0, chunk_of_step(step, here), 0, 0),
        )

    return pl.pallas_call(
        functools.partial(row_chunk_kernel, len(pairs)),
        grid_spec=pltpu.PrefetchScalarGridSpec(
            num_scalar_prefetch=1,
            grid=(RING,),
            in_specs=[spec(left) for left in lefts]
            + [pl.BlockSpec(right.shape, lambda step, here: (0, 0)) for right in rights]
            + [pl.BlockSpec(memory_space=pl.ANY)] * len(ties),
            out_specs=[pl.BlockSpec(memory_space=pl.ANY)] * RING,
            scratch_shapes=[
                pltpu.VMEM((2, SLOTS * rows, total), jnp.bfloat16),
                pltpu.SemaphoreType.DMA((2,)),
            ],
        ),
        out_shape=[jax.ShapeDtypeStruct((SLOTS * rows, total), jnp.bfloat16)] * RING,
        compiler_params=pltpu.CompilerParams(vmem_limit_bytes=VMEM_LIMIT),
        cost_estimate=pl.CostEstimate(
            flops=sum(2 * left.size * right.shape[1] for left, right in zip(lefts, rights)),
            bytes_accessed=2 * sum(part.size for part in lefts + rights)
            + 2 * BLOCKS * rows * total,
            transcendentals=0,
        ),
    )(place[axis].reshape(1), *lefts, *rights, *ties)


def column_chunk_kernel(pieces, here, left, *refs):
    rights = refs[:pieces]
    outs, held, sems = refs[-RING - 2 : -2], refs[-2], refs[-1]

    def make(slot):
        lanes = rights[0].shape[1]
        for piece, right in enumerate(rights):
            product = jnp.dot(left[...], right[...], preferred_element_type=jnp.float32)
            slot[:, piece * lanes : (piece + 1) * lanes] = product.astype(jnp.bfloat16)

    send_chunk(pl.program_id(0), make, outs, held, sems)


def column_chunks(left, right, axis, place, ties=()):
    rows, depth = left.shape
    columns = right.shape[1]
    if axis == "x":
        specs = [
            pl.BlockSpec(
                (depth, columns // RING), lambda step, here: (0, chunk_of_step(step, here))
            )
        ]
    else:
        specs = [
            pl.BlockSpec(
                (depth, columns // BLOCKS),
                lambda step, here, slot=slot: (0, slot * RING + chunk_of_step(step, here)),
            )
            for slot in range(SLOTS)
        ]
    return pl.pallas_call(
        functools.partial(column_chunk_kernel, len(specs)),
        grid_spec=pltpu.PrefetchScalarGridSpec(
            num_scalar_prefetch=1,
            grid=(RING,),
            in_specs=[pl.BlockSpec((rows, depth), lambda step, here: (0, 0))]
            + specs
            + [pl.BlockSpec(memory_space=pl.ANY)] * len(ties),
            out_specs=[pl.BlockSpec(memory_space=pl.ANY)] * RING,
            scratch_shapes=[
                pltpu.VMEM((2, rows, columns // RING), jnp.bfloat16),
                pltpu.SemaphoreType.DMA((2,)),
            ],
        ),
        out_shape=[jax.ShapeDtypeStruct((rows, columns // RING), jnp.bfloat16)] * RING,
        compiler_params=pltpu.CompilerParams(vmem_limit_bytes=VMEM_LIMIT),
        cost_estimate=pl.CostEstimate(
            flops=2 * rows * depth * columns,
            bytes_accessed=2 * (rows * depth + depth * columns + rows * columns),
            transcendentals=0,
        ),
    )(place[axis].reshape(1), left, *([right] * len(specs)), *ties)


def add_up(refs, index):
    total = refs[0][index].astype(jnp.float32)
    for ref in refs[1:]:
        total = total + ref[index].astype(jnp.float32)
    return total


def lane_slice(start, size):
    return (slice(None), pl.ds(pl.multiple_of(start * size, size), size))


def next_slots(here, offset, z):
    next_x = (here[0] + offset) % RING
    next_y = (here[2] + offset) % RING
    return z * RING + next_y, next_x * PAIR + z


def ffn_second_kernel(here, *refs):
    by_x, by_y, outs = refs[:RING], refs[RING : 2 * RING], refs[2 * RING :]
    for offset in range(RING):
        for z in range(PAIR):
            slot_x, slot_y = next_slots(here, offset, z)
            outs[offset][z] = add_up(by_x, slot_x).astype(jnp.bfloat16)
            outs[RING + offset][z] = add_up(by_y, slot_y).astype(jnp.bfloat16)


def ffn_third_kernel(here, *refs):
    by_x, by_y = refs[:RING], refs[RING : 2 * RING]
    width = by_x[0].shape[-1]
    for out, z in ((refs[-2], here[1]), (refs[-1], (here[1] + 1) % PAIR)):
        out[:, :width] = add_up(by_x, z).astype(jnp.bfloat16)
        out[:, width:] = add_up(by_y, z).astype(jnp.bfloat16)


def ffn_last_kernel(kept, got, gate_out, up_out, down_out):
    total = kept[...].astype(jnp.float32) + got[...].astype(jnp.float32)
    hidden = gate_out.shape[1]
    half = hidden // 2
    gate_out[...] = total[:, :hidden]
    up_out[...] = total[:, hidden + half : 2 * hidden + half]
    down_out[:half, :] = total[:, hidden : hidden + half].T
    down_out[half:, :] = total[:, 2 * hidden + half :].T


def mixed_second_kernel(here, *refs):
    text_x, text_y, attn_x, attn_y = [refs[RING * i : RING * (i + 1)] for i in range(4)]
    outs = refs[4 * RING :]
    columns = text_x[0].shape[0]
    lanes = text_x[0].shape[1] // SLOTS
    rows = attn_x[0].shape[1]
    for offset in range(RING):
        for z in range(PAIR):
            slots = next_slots(here, offset, z)
            for text, attn, slot, out in (
                (text_x, attn_x, slots[0], outs[offset]),
                (text_y, attn_y, slots[1], outs[RING + offset]),
            ):
                out[:columns, z * lanes : (z + 1) * lanes] = add_up(
                    text, lane_slice(slot, lanes)
                ).astype(jnp.bfloat16)
                block = add_up(attn, slot).astype(jnp.bfloat16)
                wide = PAIR * lanes
                for piece in range(block.shape[1] // wide):
                    start = columns + (piece * PAIR + z) * rows
                    out[start : start + rows, :] = block[:, piece * wide : (piece + 1) * wide]


def mixed_third_kernel(columns, rows, here, *refs):
    by_x, by_y = refs[:RING], refs[RING : 2 * RING]
    lanes = refs[-1].shape[1]
    for out, z in ((refs[-2], here[1]), (refs[-1], (here[1] + 1) % PAIR)):
        place = PAIR * columns
        for way, parts in enumerate((by_x, by_y)):
            index = (slice(0, columns), pl.ds(pl.multiple_of(z * lanes, lanes), lanes))
            out[way * columns : (way + 1) * columns, :] = add_up(parts, index).astype(jnp.bfloat16)
            pieces = (parts[0].shape[0] - columns) // (PAIR * rows)
            for piece in range(pieces):
                start = pl.multiple_of(columns + (piece * PAIR + z) * rows, 16)
                block = add_up(parts, (pl.ds(start, rows), slice(None))).astype(jnp.bfloat16)
                for side in range(PAIR):
                    out[place : place + rows, :] = block[:, side * lanes : (side + 1) * lanes]
                    place += rows


def mixed_last_kernel(columns, kept, got, textkey, textvalue, query, key, value, outw):
    total = kept[...].astype(jnp.float32) + got[...].astype(jnp.float32)
    textkey[...] = total[:columns].T
    textvalue[...] = total[columns : 2 * columns].T
    rows = query.shape[0]
    lanes = total.shape[1]
    place = 2 * columns
    for out in (query, key, value, None):
        blocks = []
        for piece in range(columns // lanes):
            blocks.append(total[place : place + rows])
            place += rows
        whole = jnp.concatenate(blocks, axis=1)
        if out is None:
            outw[...] = whole.T
        else:
            out[...] = whole


def whole_call(kernel, scalars, operands, outs, name, ties=(), flops=0):
    whole = pl.BlockSpec(memory_space=pltpu.VMEM)
    count = len(scalars) + len(operands)
    return pl.pallas_call(
        lambda *refs: kernel(*refs[:count], *refs[count + len(ties) :]),
        in_specs=[pl.BlockSpec(memory_space=pltpu.SMEM)] * len(scalars)
        + [whole] * len(operands)
        + [pl.BlockSpec(memory_space=pl.ANY)] * len(ties),
        out_specs=[whole] * len(outs),
        out_shape=[jax.ShapeDtypeStruct(shape, kind) for shape, kind in outs],
        compiler_params=pltpu.CompilerParams(vmem_limit_bytes=VMEM_LIMIT),
        cost_estimate=pl.CostEstimate(
            flops=flops,
            bytes_accessed=sum(part.size * part.dtype.itemsize for part in operands)
            + sum(math.prod(shape) * jnp.dtype(kind).itemsize for shape, kind in outs),
            transcendentals=0,
        ),
        name=name,
    )(*scalars, *operands, *ties)


def exchange(chunks, axis):
    return [chunks[0]] + [
        lax.ppermute(chunks[step], "dp", dp_perm(axis, step)) for step in range(1, len(chunks))
    ]


def by_slots(chunk):
    return chunk.reshape(SLOTS, chunk.shape[0] // SLOTS, chunk.shape[1])


def lane_index(shape):
    return lax.broadcasted_iota(jnp.int32, shape, 1)


def head_lanes(shape, head):
    lane = lane_index(shape)
    return (lane < HEAD) if head == 0 else (lane >= HEAD)


def per_head(values, reduce):
    first = head_lanes(values.shape, 0)
    left = jnp.sum(jnp.where(first, values, 0.0), axis=1, keepdims=True)
    right = jnp.sum(jnp.where(first, 0.0, values), axis=1, keepdims=True)
    return jnp.where(first, left, right)


def head_units(raw):
    inverse = lax.rsqrt(per_head(raw * raw, None) * (1.0 / HEAD) + EPS)
    return raw * inverse, inverse


def partner(values):
    lane = lane_index(values.shape)
    return jnp.where(
        lane % HEAD < HEAD // 2,
        pltpu.roll(values, LANES - HEAD // 2, 1),
        pltpu.roll(values, HEAD // 2, 1),
    )


def dot(left, right):
    return jnp.dot(left, right, preferred_element_type=jnp.float32)


def dot_t(left, right):
    return lax.dot_general(left, right, (((1,), (1,)), ((), ())), preferred_element_type=jnp.float32)


def attend_kernel(
    raw_q, raw_k, value, raw_t, text_value, cosine, sine, gains, gate, gate_swapped, mark_q, mark_k, mark_t,
    query_out, key_out, text_out, mixed_out, self_out, cross_out, self_log, cross_log,
):
    cos, sin = cosine[...], sine[...]
    unit = head_units(raw_q[...])[0] * gains[0:1, :]
    query = ((unit * cos + partner(unit) * sin).astype(jnp.bfloat16) * ROOT).astype(jnp.bfloat16)
    unit = head_units(raw_k[...])[0] * gains[1:2, :]
    key = (unit * cos + partner(unit) * sin).astype(jnp.bfloat16)
    text = (head_units(raw_t[...])[0] * gains[2:3, :]).astype(jnp.bfloat16)
    query_out[...] = query
    key_out[...] = key
    text_out[...] = text

    def attention(keys, marks, values):
        outs, sums = [], []
        for head in range(2):
            own = head_lanes(query.shape, head)
            own_keys = head_lanes(keys.shape, head)
            probe = jnp.where(own, query, mark_q[...])
            scores = dot_t(probe, jnp.where(own_keys, keys, marks))
            weights = jnp.exp(scores).astype(jnp.bfloat16)
            both = dot(weights, jnp.where(own_keys, values, jnp.ones_like(values)))
            outs.append(both)
        first = head_lanes(outs[0].shape, 0)
        product = jnp.where(first, outs[0], outs[1])
        total = jnp.where(first, outs[1], outs[0])
        return product / pltpu.roll(total, HEAD, 1), jnp.log(total)

    out, log = attention(key, mark_k[...], value[...])
    self_out[...] = out
    self_log[...] = log
    cross, log = attention(text, mark_t[...], text_value[...])
    cross_out[...] = cross
    cross_log[...] = log - jnp.log(gate_swapped[...])
    mixed_out[...] = (out + gate[...] * cross).astype(jnp.bfloat16)


def attention_grads(query, keys, marks, values, grad, out, log, mark_q):
    rows = grad.astype(jnp.float32)
    delta = per_head(rows * out, None)
    delta = pltpu.roll(delta, HEAD, 1)
    lane = lane_index(query.shape) % HEAD
    log_high = log.astype(jnp.bfloat16)
    log_low = (log - log_high.astype(jnp.float32)).astype(jnp.bfloat16)
    delta_high = delta.astype(jnp.bfloat16)
    delta_low = (delta - delta_high.astype(jnp.float32)).astype(jnp.bfloat16)
    zero = jnp.zeros_like(query)
    code = jnp.where(lane == 4, -log_high, jnp.where(lane == 5, -log_low, mark_q))
    shift = jnp.where(lane == 4, -delta_high, jnp.where(lane == 5, -delta_low, zero))
    key_grads, value_grads, query_grads = [], [], []
    for head in range(2):
        own = head_lanes(query.shape, head)
        own_keys = head_lanes(keys.shape, head)
        probe = jnp.where(own, query, code)
        probs = jnp.exp(dot_t(jnp.where(own_keys, keys, marks), probe))
        slope = dot_t(jnp.where(own_keys, values, marks), jnp.where(own, grad, shift))
        score_grad = (probs * slope).astype(jnp.bfloat16)
        value_grads.append(dot(probs.astype(jnp.bfloat16), grad))
        key_grads.append(dot(score_grad, query))
        turned = keys[:, head * HEAD : (head + 1) * HEAD].T
        query_grads.append(dot(turned, score_grad))
    first = head_lanes(keys.shape, 0)
    return (
        jnp.concatenate(query_grads, axis=0),
        jnp.where(first, key_grads[0], key_grads[1]),
        jnp.where(first, value_grads[0], value_grads[1]),
    )


def norm_back(weighted, unit, inverse):
    return inverse * (weighted - unit * (per_head(weighted * unit, None) * (1.0 / HEAD)))


def cross_back_kernel(
    query, text, text_value, raw_t, grad, out, log, gains, mark_q, mark_t,
    query_grad, raw_grad, value_grad, gain_sum, gate_sum,
):
    grad_q, grad_t, grad_v = attention_grads(
        query[...], text[...], mark_t[...], text_value[...], grad[...], out[...], log[...], mark_q[...]
    )
    query_grad[...] = grad_q.T
    value_grad[...] = grad_v.astype(jnp.bfloat16).T
    grad_t = grad_t.astype(jnp.bfloat16).astype(jnp.float32)
    unit, inverse = head_units(raw_t[...])
    gain_sum[...] = jnp.sum(grad_t * unit, axis=0, keepdims=True)
    raw_grad[...] = norm_back(grad_t * gains[2:3, :], unit, inverse).astype(jnp.bfloat16).T
    gate_sum[...] = jnp.sum(grad[...].astype(jnp.float32) * out[...], axis=0, keepdims=True)


def self_back_kernel(
    query, key, value, raw_q, raw_k, grad, out, log, cross_grad, cosine, sine, gains, mark_q, mark_k,
    query_grad, key_grad, value_grad, gain_sum,
):
    grad_q, grad_k, grad_v = attention_grads(
        query[...], key[...], mark_k[...], value[...], grad[...], out[...], log[...], mark_q[...]
    )
    value_grad[...] = grad_v.astype(jnp.bfloat16)
    cos, sin = cosine[...], sine[...]
    grad_q = (grad_q.T + cross_grad[...]) * ROOT
    for turn, raw, row, target in ((grad_q, raw_q, 0, query_grad), (grad_k, raw_k, 1, key_grad)):
        turn = turn.astype(jnp.bfloat16).astype(jnp.float32)
        turn = turn * cos - partner(turn) * sin
        unit, inverse = head_units(raw[...])
        gain_sum[row : row + 1, :] = jnp.sum(turn * unit, axis=0, keepdims=True)
        target[...] = norm_back(turn * gains[row : row + 1, :], unit, inverse).astype(jnp.bfloat16)


def pair_call(kernel, operands, outs, flops, transcendentals, name, ties=()):
    def spec(shape, cut):
        if cut is None:
            return pl.BlockSpec(shape, lambda pair: (0, 0))
        if cut == 1:
            return pl.BlockSpec((shape[0], LANES), lambda pair: (0, pair))
        return pl.BlockSpec((LANES, shape[1]), lambda pair: (pair, 0))

    width = outs[0][0][0] if outs[0][2] == 0 else outs[0][0][1]
    return pl.pallas_call(
        lambda *refs: kernel(*refs[: len(operands)], *refs[len(operands) + len(ties) :]),
        grid=(width // LANES,),
        in_specs=[spec(part.shape, cut) for part, cut in operands]
        + [pl.BlockSpec(memory_space=pl.ANY)] * len(ties),
        out_specs=[spec(shape, cut) for shape, _, cut in outs],
        out_shape=[jax.ShapeDtypeStruct(shape, kind) for shape, kind, _ in outs],
        compiler_params=pltpu.CompilerParams(vmem_limit_bytes=VMEM_LIMIT),
        cost_estimate=pl.CostEstimate(
            flops=flops,
            bytes_accessed=sum(part.size * part.dtype.itemsize for part, _ in operands),
            transcendentals=transcendentals,
        ),
        name=name,
    )(*[part for part, _ in operands], *ties)
def inverse_rms(values):
    return lax.rsqrt(jnp.mean(values * values, axis=-1, keepdims=True) + EPS)


def row_norm_back(weighted, unit, inverse):
    return inverse * (weighted - unit * jnp.mean(weighted * unit, axis=-1, keepdims=True))


def per_row(table, segment):
    return jnp.where(segment == 0.0, table[0:1], jnp.where(segment == 1.0, table[1:2], table[2:3]))


def total_of(parts):
    upper, near, far = parts
    rows = far.shape[0]
    return (
        upper[:rows].astype(jnp.float32) + near[:rows].astype(jnp.float32) + far[...].astype(jnp.float32)
    )


def segment_sums(member, values):
    high = values.astype(jnp.bfloat16)
    low = (values - high.astype(jnp.float32)).astype(jnp.bfloat16)
    return dot(member, high) + dot(member, low)


def tables_kernel(here, lens, segments, cosine, sine, mark_q, mark_k, mark_t, segment, member):
    rows = segments.shape[1]
    ids = segments[...]
    first = jnp.sum((ids < 1).astype(jnp.float32))
    second = jnp.sum((ids < 2).astype(jnp.float32))
    lane = lane_index((rows, LANES))
    half = HEAD // 2
    rate = jnp.exp((lane % half).astype(jnp.float32) * (-2.0 * math.log(10000.0) / HEAD))
    within = lane % HEAD
    for block, code in enumerate(ROW_ORDER):
        source = here[0] ^ code
        line = segments[pl.ds(source, 1), :].astype(jnp.float32)
        label = jnp.broadcast_to(line, (rows, rows)).T
        start = jnp.where(label == 0.0, 0.0, jnp.where(label == 1.0, first, second))
        token = (lax.broadcasted_iota(jnp.int32, (rows, LANES), 0) + source * rows).astype(jnp.float32)
        angle = (token - start) * rate
        index = slice(block * rows, (block + 1) * rows)
        cosine[index, :] = jnp.cos(angle)
        sine[index, :] = jnp.where(within < half, -1.0, 1.0) * jnp.sin(angle)
        same = ((label == within.astype(jnp.float32)) & (within < SEGS)).astype(jnp.float32)
        shut = (within == SEGS).astype(jnp.float32)
        ones = ((within >= SEGS) & (within < SEGS + 3)).astype(jnp.float32)
        mark_q[index, :] = (SHUT * same - SHUT * shut).astype(jnp.bfloat16)
        mark_k[index, :] = (same + ones).astype(jnp.bfloat16)
        if block == 0:
            segment[...] = label
            member[...] = (
                lax.broadcasted_iota(jnp.int32, (8, rows), 0).astype(jnp.float32) == line
            ).astype(jnp.bfloat16)
    for group in range(SEGS):
        lane = lane_index((TXT, LANES)) % HEAD
        row = lax.broadcasted_iota(jnp.int32, (TXT, LANES), 0)
        inside = ((lane == group) & (row < lens[group])).astype(jnp.float32)
        ones = ((lane >= SEGS) & (lane < SEGS + 3)).astype(jnp.float32)
        mark_t[group * TXT : (group + 1) * TXT, :] = (inside + ones).astype(jnp.bfloat16)


def text_kernel(captions, key_weight, value_weight, raw_out, value_out, raw_sum, value_sum):
    step = pl.program_id(0)

    @pl.when(step == 0)
    def _():
        raw_sum[...] = dot(captions[...], key_weight[...])
        value_sum[...] = dot(captions[...], value_weight[...])

    @pl.when(step > 0)
    def _():
        raw_sum[...] += dot(captions[...], key_weight[...])
        value_sum[...] += dot(captions[...], value_weight[...])

    @pl.when(step == pl.num_programs(0) - 1)
    def _():
        raw_out[...] = raw_sum[...]
        value_out[...] = value_sum[...].astype(jnp.bfloat16)


def text_call(captions, key_weight, value_weight):
    rows, depth = captions.shape
    columns = key_weight.shape[1]
    tile = depth // 4
    return pl.pallas_call(
        text_kernel,
        grid=(depth // tile,),
        in_specs=[
            pl.BlockSpec((rows, tile), lambda step: (0, step)),
            pl.BlockSpec((tile, columns), lambda step: (step, 0)),
            pl.BlockSpec((tile, columns), lambda step: (step, 0)),
        ],
        out_specs=[pl.BlockSpec((rows, columns), lambda step: (0, 0))] * 2,
        out_shape=[
            jax.ShapeDtypeStruct((rows, columns), jnp.float32),
            jax.ShapeDtypeStruct((rows, columns), jnp.bfloat16),
        ],
        scratch_shapes=[pltpu.VMEM((rows, columns), jnp.float32)] * 2,
        compiler_params=pltpu.CompilerParams(vmem_limit_bytes=VMEM_LIMIT),
        cost_estimate=pl.CostEstimate(
            flops=4 * rows * depth * columns,
            bytes_accessed=2 * depth * (rows + 2 * columns),
            transcendentals=0,
        ),
        name="text",
    )(captions, key_weight, value_weight)


def project_kernel(here, own, far, near, last, mods, gains, segment_q, query_w, key_w, value_w,
                   rows_out, raw_q, raw_k, value):
    table = mods[here[0]]
    rows = own.shape[0]
    for block, part in enumerate((own, far, near, last)):
        index = slice(block * rows, (block + 1) * rows)
        values = part[...].astype(jnp.float32)
        marks = segment_q[index, :].astype(jnp.float32)
        scale = jnp.where(
            marks[:, 0:1] > 0.0, table[0:1], jnp.where(marks[:, 1:2] > 0.0, table[1:2], table[2:3])
        )
        rows_out[index, :] = (
            values * inverse_rms(values) * gains[0:1] * (1.0 + scale)
        ).astype(jnp.bfloat16)
    raw_q[...] = dot(rows_out[...], query_w[...])
    raw_k[...] = dot(rows_out[...], key_w[...])
    value[...] = dot(rows_out[...], value_w[...]).astype(jnp.bfloat16)


def middle_kernel(here, block, upper, near, far, mods, gains, segment, attn_out, middle_out, rows_out):
    attn_sum = total_of((upper, near, far))
    label = segment[:, 0:1]
    factor = jnp.tanh(per_row(mods[here[0] ^ 1], label)) * gains[1:2]
    middle = block[...].astype(jnp.float32) + factor * (attn_sum * inverse_rms(attn_sum))
    attn_out[...] = attn_sum
    middle_out[...] = middle
    scale = per_row(mods[here[0] ^ 2], label)
    rows_out[...] = (middle * inverse_rms(middle) * gains[2:3] * (1.0 + scale)).astype(jnp.bfloat16)


def block_out_kernel(here, middle, upper, near, far, grad, mods, gains, segment, member,
                     block_out, grad_out, sums):
    ffn_sum = total_of((upper, near, far))
    inverse = inverse_rms(ffn_sum)
    unit = ffn_sum * inverse
    factor = jnp.tanh(per_row(mods[here[0] ^ 3], segment[:, 0:1])) * gains[3:4]
    block_out[...] = (middle[...] + factor * unit).astype(jnp.bfloat16)
    incoming = grad[...].astype(jnp.float32)
    grad_out[...] = row_norm_back(incoming * factor, unit, inverse).astype(jnp.bfloat16)
    sums[...] = segment_sums(member[...], incoming * unit)


def middle_back_kernel(here, middle, attn, upper, near, far, grad, mods, gains, segment, member,
                       middle_grad, attn_grad, ffn_sums, attn_sums):
    grad_in = total_of((upper, near, far))
    label = segment[:, 0:1]
    inverse = inverse_rms(middle[...])
    unit = middle[...] * inverse
    factor = gains[2:3] * (1.0 + per_row(mods[here[0] ^ 2], label))
    ffn_sums[...] = segment_sums(member[...], grad_in * unit)
    grad_middle = grad[...].astype(jnp.float32) + row_norm_back(grad_in * factor, unit, inverse)
    middle_grad[...] = grad_middle
    inverse = inverse_rms(attn[...])
    unit = attn[...] * inverse
    factor = jnp.tanh(per_row(mods[here[0] ^ 1], label)) * gains[1:2]
    attn_grad[...] = row_norm_back(grad_middle * factor, unit, inverse).astype(jnp.bfloat16)
    attn_sums[...] = segment_sums(member[...], grad_middle * unit)


def block_in_kernel(here, block, middle_grad, upper, near, far, mods, gains, segment, member,
                    in_grad, sums):
    grad_in = total_of((upper, near, far))
    values = block[...].astype(jnp.float32)
    inverse = inverse_rms(values)
    unit = values * inverse
    factor = gains[0:1] * (1.0 + per_row(mods[here[0]], segment[:, 0:1]))
    in_grad[...] = (
        middle_grad[...] + row_norm_back(grad_in * factor, unit, inverse)
    ).astype(jnp.bfloat16)
    sums[...] = segment_sums(member[...], grad_in * unit)


def shards(
    block_in,
    out_grad,
    condition,
    captions,
    caption_len,
    segment_ids,
    ada_weight,
    norm_gains,
    query_weight,
    key_weight,
    value_weight,
    head_gains,
    textkey_weight,
    textvalue_weight,
    cross_gate,
    out_weight,
    gate_weight,
    up_weight,
    down_weight,
):
    rows, width = block_in.shape
    length = segment_ids.shape[0]
    heads = cross_gate.shape[0]
    inner = heads * HEAD
    half_rows = length // 2
    position = lax.axis_index("tensor")
    place = dp_place()
    here = position.reshape(1)
    b16, f32 = jnp.bfloat16, jnp.float32

    blocks = gather_tensor(block_in)
    own_act = jax.nn.silu(condition.astype(f32)).astype(b16)
    own_part = jnp.dot(own_act, ada_weight, preferred_element_type=f32)
    parts = gather_tensor(own_part)
    mods = jnp.stack([parts[ROW_ORDER.index(code)] for code in range(4)])

    cosine, sine, mark_q, mark_k, mark_t, segment, member = whole_call(
        tables_kernel,
        (here, caption_len),
        [segment_ids.reshape(length // rows, rows)],
        [((length, LANES), f32)] * 2
        + [((length, LANES), b16)] * 2
        + [((SEGS * TXT, LANES), b16), ((rows, LANES), f32), ((8, rows), b16)],
        "tables",
    )
    caption_flat = captions.reshape(-1, captions.shape[-1])
    texts = caption_flat.shape[0]
    raw_t, text_value = text_call(caption_flat, textkey_weight, textvalue_weight)
    attn_rows, raw_q, raw_k, value = whole_call(
        project_kernel,
        (here,),
        blocks + [mods, norm_gains, mark_q, query_weight, key_weight, value_weight],
        [((length, width), b16), ((length, inner), f32), ((length, inner), f32), ((length, inner), b16)],
        "project",
        flops=6 * length * width * inner,
    )
    tanh_gate = jnp.tanh(cross_gate)
    gate_lanes = jnp.repeat(tanh_gate, HEAD)[None]
    gate_swapped = jnp.repeat(tanh_gate.reshape(-1, 2)[:, ::-1].reshape(-1), HEAD)[None]
    gains = jnp.tile(head_gains, (1, heads))
    query, key, text, mixed, self_out, cross_out, self_log, cross_log = pair_call(
        attend_kernel,
        [(raw_q, 1), (raw_k, 1), (value, 1), (raw_t, 1), (text_value, 1), (cosine, None), (sine, None)]
        + [(gains, 1), (gate_lanes, 1), (gate_swapped, 1), (mark_q, None), (mark_k, None), (mark_t, None)],
        [((length, inner), b16, 1)] * 2
        + [((texts, inner), b16, 1), ((length, inner), b16, 1)]
        + [((length, inner), f32, 1)] * 4,
        4 * length * (length + texts) * inner,
        length * (length + texts) * heads,
        "attend",
    )

    def halves(product):
        return product(slice(0, half_rows)).astype(b16), product(slice(half_rows, None)).astype(b16)

    def all_of(block):
        return jnp.concatenate(gather_tensor(block), axis=0)

    upper, lower = halves(lambda part: jnp.dot(mixed[part], out_weight, preferred_element_type=f32))
    sums, sent = scatter_tensor(upper, lower)
    attn_rows_t = turned(attn_rows, (sent,))
    wide = ((rows, width), f32)
    narrow = ((rows, width), b16)
    totals = ((8, width), f32)
    attn_sum, middle, ffn_own = whole_call(
        middle_kernel,
        (here,),
        [block_in] + sums + [mods, norm_gains, segment],
        [wide, wide, narrow],
        "middle",
    )
    ffn_rows = all_of(ffn_own)
    gate_pre = jnp.dot(ffn_rows, gate_weight, preferred_element_type=f32)
    up_pre = jnp.dot(ffn_rows, up_weight, preferred_element_type=f32)
    sigmoid_gate = jax.nn.sigmoid(gate_pre)
    silu_gate = gate_pre * sigmoid_gate
    hidden = (silu_gate * up_pre).astype(b16)
    upper, lower = halves(lambda part: jnp.dot(hidden[part], down_weight, preferred_element_type=f32))
    sums, sent = scatter_tensor(upper, lower)
    ffn_rows_t = turned(ffn_rows, (sent,))
    block_out, grad_own, sum_gate_ffn = whole_call(
        block_out_kernel,
        (here,),
        [middle] + sums + [out_grad, mods, norm_gains, segment, member],
        [narrow, narrow, totals],
        "block_out",
    )

    grad_ffn = all_of(grad_own)
    grad_hidden = times_transpose(grad_ffn, down_weight)
    grad_gate = (
        grad_hidden * up_pre * sigmoid_gate * (1.0 + gate_pre * (1.0 - sigmoid_gate))
    ).astype(b16)
    grad_up = (grad_hidden * silu_gate).astype(b16)
    upper, lower = halves(
        lambda part: times_transpose(grad_gate[part], gate_weight)
        + times_transpose(grad_up[part], up_weight)
    )
    sums, sent = scatter_tensor(upper, lower)
    half = hidden.shape[1] // 2
    grad_ffn_t = turned(grad_ffn, (sent,))
    ffn_by_x = row_chunks(
        [(ffn_rows_t, grad_gate), (grad_ffn_t, hidden[:, :half])], "x", place, (sent,)
    )
    ffn_by_y = row_chunks(
        [(ffn_rows_t, grad_up), (grad_ffn_t, hidden[:, half:])], "y", place, (sent,)
    )
    grad_middle, grad_own, sum_scale_ffn, sum_gate_attn = whole_call(
        middle_back_kernel,
        (here,),
        [middle, attn_sum] + sums + [out_grad, mods, norm_gains, segment, member],
        [wide, narrow, totals, totals],
        "middle_back",
    )

    grad_attn = all_of(grad_own)
    grad_mixed = times_transpose(grad_attn, out_weight).astype(b16)
    cross_grad, text_grad, text_value_grad, text_gain, gate_sum = pair_call(
        cross_back_kernel,
        [(query, 1), (text, 1), (text_value, 1), (raw_t, 1), (grad_mixed, 1), (cross_out, 1)]
        + [(cross_log, 1), (gains, 1), (mark_q, None), (mark_t, None)],
        [((length, inner), f32, 1), ((inner, texts), b16, 0), ((inner, texts), b16, 0)]
        + [((1, inner), f32, 1)] * 2,
        10 * length * texts * inner,
        length * texts * heads,
        "cross_back",
    )
    text_by_x = column_chunks(text_grad, caption_flat, "x", place)
    text_by_y = column_chunks(text_value_grad, caption_flat, "y", place)
    query_grad, key_grad, value_grad, head_gain = pair_call(
        self_back_kernel,
        [(query, 1), (key, 1), (value, 1), (raw_q, 1), (raw_k, 1), (grad_mixed, 1), (self_out, 1)]
        + [(self_log, 1), (cross_grad, 1), (cosine, None), (sine, None), (gains, 1)]
        + [(mark_q, None), (mark_k, None)],
        [((length, inner), b16, 1)] * 3 + [((2, inner), f32, 1)],
        10 * length * length * inner,
        length * length * heads,
        "self_back",
        (text_by_x[0], text_by_y[0]),
    )
    upper, lower = halves(
        lambda part: times_transpose(query_grad[part], query_weight)
        + times_transpose(key_grad[part], key_weight)
        + times_transpose(value_grad[part], value_weight)
    )
    sums, sent = scatter_tensor(upper, lower)
    attn_by_x = row_chunks(
        [(attn_rows_t, query_grad), (attn_rows_t, key_grad)], "x", place, (sent,)
    )
    attn_by_y = row_chunks(
        [(attn_rows_t, value_grad), (turned(grad_attn, (sent,)), mixed)], "y", place, (sent,)
    )
    in_grad, sum_scale_attn = whole_call(
        block_in_kernel,
        (here,),
        [block_in, grad_middle] + sums + [mods, norm_gains, segment, member],
        [narrow, totals],
        "block_in",
    )

    spot = jnp.stack([place["x"], place["z"], place["y"]])
    hidden_cols = hidden.shape[1]
    block_rows = width // BLOCKS
    got = [by_slots(part) for part in exchange(ffn_by_x, "x") + exchange(ffn_by_y, "y")]
    shape = ((PAIR, block_rows, hidden_cols + half), b16)
    stage = whole_call(
        ffn_second_kernel, (spot,), got, [shape] * (2 * RING), "ffn_second", (text_grad,)
    )
    got = exchange(stage[:RING], "y") + exchange(stage[RING:], "x")
    shape = ((block_rows, 3 * hidden_cols), b16)
    kept, sent = whole_call(
        ffn_third_kernel, (spot,), got, [shape] * 2, "ffn_third", (query_grad,)
    )
    gate_sum_out, up_sum_out, down_sum_out = whole_call(
        ffn_last_kernel,
        (),
        exchange([kept, sent], "z"),
        [((block_rows, hidden_cols), f32)] * 2 + [((hidden_cols, block_rows), f32)],
        "ffn_last",
        (attn_by_y[0],),
    )

    text_rows = caption_flat.shape[1] // BLOCKS
    got = (
        exchange(text_by_x, "x")
        + exchange(text_by_y, "y")
        + [by_slots(part) for part in exchange(attn_by_x, "x") + exchange(attn_by_y, "y")]
    )
    attn_pieces = 2 * inner // (PAIR * text_rows)
    shape = ((inner + attn_pieces * PAIR * block_rows, PAIR * text_rows), b16)
    stage = whole_call(mixed_second_kernel, (spot,), got, [shape] * (2 * RING), "mixed_second")
    got = exchange(stage[:RING], "y") + exchange(stage[RING:], "x")
    shape = ((2 * inner + 4 * inner // text_rows * block_rows, text_rows), b16)
    kept, sent = whole_call(
        functools.partial(mixed_third_kernel, inner, block_rows),
        (spot,),
        got,
        [shape] * 2,
        "mixed_third",
    )
    textkey_sum, textvalue_sum, query_sum, key_sum, value_sum, outw_sum = whole_call(
        functools.partial(mixed_last_kernel, inner),
        (),
        exchange([kept, sent], "z"),
        [((text_rows, inner), f32)] * 2
        + [((block_rows, inner), f32)] * 3
        + [((inner, block_rows), f32)],
        "mixed_last",
    )

    by_name = jnp.stack([sum_scale_attn, sum_gate_attn, sum_scale_ffn, sum_gate_ffn])
    by_code = [
        lax.dynamic_index_in_dim(by_name, position ^ code, 0, keepdims=False)[:SEGS]
        for code in range(4)
    ]
    near = swap_core(jnp.stack([by_code[1], by_code[3]]))
    own_sum = by_code[0] + near[0] + swap_chip(by_code[2] + near[1])
    is_gate = position % 2 == 1
    tanh_part = jnp.tanh(own_part)
    factor = jnp.where(is_gate, tanh_part, 1.0 + own_part)
    slope = jnp.where(is_gate, 1.0 - tanh_part * tanh_part, 1.0)
    own_gain = lax.dynamic_index_in_dim(norm_gains, position, 0)
    grad_mod = own_sum * slope * own_gain

    def split(values):
        high = values.astype(b16)
        return high, (values - high.astype(f32)).astype(b16)

    gain_high, gain_low = split(jnp.sum(own_sum * factor, axis=0, keepdims=True))
    gate_term = jnp.sum(gate_sum.reshape(heads, HEAD), axis=1) * (1.0 - tanh_gate * tanh_gate)
    gate_full = lax.dynamic_update_slice_in_dim(
        jnp.zeros((HEADS,), f32), gate_term, position * heads, 0
    )
    head_sums = jnp.concatenate([head_gain, text_gain]).reshape(3, heads, HEAD).sum(axis=1)
    extras = jnp.concatenate([head_sums.reshape(-1), gate_full])
    extra_size = extras.shape[0]
    extras = jnp.pad(jnp.concatenate(split(extras)), (0, width - 2 * extra_size))[None]
    packed = jnp.concatenate(
        [grad_mod.astype(b16), condition.reshape(-1, width), gain_high, gain_low, extras]
    )
    gathered = gather_dp(packed)
    acts = gathered[:, SEGS : SEGS + 2].reshape(BLOCKS * SEGS, condition.shape[1])
    ada_rows = acts.shape[1] // BLOCKS
    acts = lax.dynamic_slice_in_dim(acts, lax.axis_index("dp") * ada_rows, ada_rows, 1)
    acts = jax.nn.silu(acts.astype(f32)).astype(b16)
    ada_grad = lax.dot_general(
        acts,
        gathered[:, :SEGS].reshape(-1, width),
        (((0,), (0,)), ((), ())),
        preferred_element_type=f32,
    )
    rest = jnp.sum(gathered[:, SEGS + 2 :].astype(f32), axis=0)
    rest = jnp.stack([rest[0] + rest[1], rest[2]])
    last = gather_tensor(rest)
    last = [last[ROW_ORDER.index(code)] for code in range(4)]
    extras_sum = last[0][1] + last[1][1] + last[2][1] + last[3][1]
    extras_sum = extras_sum[:extra_size] + extras_sum[extra_size : 2 * extra_size]
    gain_rows = jnp.stack([part[0] for part in last])
    norm_grads = jnp.stack(
        [lax.dynamic_index_in_dim(gain_rows, position ^ name, 0, keepdims=False) for name in range(4)]
    )
    head_grads = extras_sum[: 3 * HEAD].reshape(3, HEAD)
    crossgate_grad = extras_sum[3 * HEAD : 3 * HEAD + HEADS]
    return (
        block_out,
        in_grad,
        ada_grad,
        norm_grads,
        query_sum,
        key_sum,
        value_sum,
        head_grads,
        textkey_sum,
        textvalue_sum,
        crossgate_grad,
        outw_sum,
        gate_sum_out,
        up_sum_out,
        down_sum_out,
    )


def solution(mesh):
    return jax.shard_map(
        shards,
        mesh=mesh,
        in_specs=(
            P(("dp", "tensor"), None),
            P(("dp", "tensor"), None),
            P("dp", None),
            P("dp", None, None),
            P("dp"),
            P("dp"),
            P(None, "tensor"),
            P(),
            P(None, "tensor"),
            P(None, "tensor"),
            P(None, "tensor"),
            P(),
            P(None, "tensor"),
            P(None, "tensor"),
            P("tensor"),
            P("tensor", None),
            P(None, "tensor"),
            P(None, "tensor"),
            P("tensor", None),
        ),
        out_specs=(
            P(("dp", "tensor"), None),
            P(("dp", "tensor"), None),
            P("dp", "tensor"),
            P(),
            P("dp", "tensor"),
            P("dp", "tensor"),
            P("dp", "tensor"),
            P(),
            P("dp", "tensor"),
            P("dp", "tensor"),
            P(),
            P("tensor", "dp"),
            P("dp", "tensor"),
            P("dp", "tensor"),
            P("tensor", "dp"),
        ),
        check_vma=False,
    )
```

```python
import functools
import math

import jax
import jax.numpy as jnp
from jax import lax
from jax.experimental import pallas as pl
from jax.experimental.pallas import tpu as pltpu
from jax.sharding import PartitionSpec as P

HEAD = 64
HEADS = 24
TXT = 256
SEGS = 3
EPS = 1e-06
LANES = 2 * HEAD
SHUT = 256.0
ROOT = HEAD ** (-0.5)
VMEM_LIMIT = 50 * 2**20
NO_COST = pl.CostEstimate(flops=0, bytes_accessed=0, transcendentals=0)


def cost_of(micros):
    return pl.CostEstimate(flops=int(micros * 1e9), bytes_accessed=0, transcendentals=0)


CROSS_MICROS = 10
BLOCK_IN_MICROS = 10

RING = 4
PAIR = 2
BLOCKS = RING * PAIR * RING
SLOTS = BLOCKS // RING
SEND_ORDER = (2, 1, 3, 0)
CORE_SWAP = [(0, 1), (1, 0), (2, 3), (3, 2)]
CHIP_SWAP = [(0, 2), (2, 0), (1, 3), (3, 1)]
ROW_ORDER = (0, 2, 1, 3)

def dp_index(x, z, y):
    return (x * PAIR + z) * RING + y


def dp_perm(axis, step):
    pairs = []
    for x in range(RING):
        for z in range(PAIR):
            for y in range(RING):
                for tensor in range(2 * PAIR):
                    way = axis
                    if axis in ("first", "second"):
                        way = "x" if (tensor % 2 == 0) == (axis == "first") else "y"
                    target = {
                        "x": ((x + step) % RING, z, y),
                        "y": (x, z, (y + step) % RING),
                        "z": (x, (z + step) % PAIR, y),
                    }[way]
                    pairs.append(
                        (
                            dp_index(x, z, y) * 2 * PAIR + tensor,
                            dp_index(*target) * 2 * PAIR + tensor,
                        )
                    )
    return pairs


def dp_permute(values, axis, step):
    return lax.ppermute(values, ("dp", "tensor"), dp_perm(axis, step))


def dp_spot(position):
    index = lax.axis_index("dp")
    x, z, y = index // (RING * PAIR), index // RING % PAIR, index % RING
    core = position % 2
    return jnp.stack([jnp.where(core == 0, x, y), z, jnp.where(core == 0, y, x), core])


def swap_core(values):
    return lax.ppermute(values, "tensor", CORE_SWAP)


def swap_chip(values):
    return lax.ppermute(values, "tensor", CHIP_SWAP)


def times_transpose(left, right):
    return lax.dot_general(
        left, right, (((1,), (1,)), ((), ())), preferred_element_type=jnp.float32
    )


def gather_tensor(block):
    far = swap_chip(block)
    near = swap_core(block)
    return [block, far, near, swap_core(far)]


def scatter_tensor(upper, lower):
    near = swap_core(lower)
    rows = upper.shape[0] // 2
    far = (upper[rows:].astype(jnp.float32) + near[rows:].astype(jnp.float32)).astype(near.dtype)
    return [upper, near, swap_chip(far)], far


def gather_dp(block):
    block = block[None]
    for axis, step in (("x", 1), ("x", 2), ("y", 1), ("y", 2), ("z", 1)):
        block = jnp.concatenate([block, dp_permute(block, axis, step)], axis=0)
    return block


def turn_kernel(source, target):
    target[...] = source[...].T


def turned(values, ties=()):
    tile = 512 if values.shape[1] % 512 == 0 else values.shape[1]
    return pl.pallas_call(
        lambda source, *rest: turn_kernel(source, rest[-1]),
        grid=(values.shape[1] // tile,),
        in_specs=[pl.BlockSpec((values.shape[0], tile), lambda step: (0, step))]
        + [pl.BlockSpec(memory_space=pl.ANY)] * len(ties),
        out_specs=pl.BlockSpec((tile, values.shape[0]), lambda step: (step, 0)),
        out_shape=jax.ShapeDtypeStruct(values.shape[::-1], values.dtype),
        compiler_params=pltpu.CompilerParams(vmem_limit_bytes=VMEM_LIMIT),
        cost_estimate=NO_COST,
    )(values, *ties)


def send_chunk(step, make, outs, held, sems):
    count = len(outs)

    def copy(place):
        return pltpu.make_async_copy(held.at[place % 2], outs[place], sems.at[place % 2])

    for place in range(count):

        @pl.when(step == place)
        def _(place=place):
            if place >= 2:
                copy(place - 2).wait()
            make(held.at[place % 2])
            copy(place).start()
            if place == count - 1:
                if place >= 1:
                    copy(place - 1).wait()
                copy(place).wait()


def chunk_block(order, slot, step, spot):
    offset = order[-1]
    for place in range(len(order) - 1):
        offset = jnp.where(step == place, order[place], offset)
    first = (spot[0] + offset) % RING
    z, second = slot // RING, slot % RING
    x = jnp.where(spot[3] == 0, first, second)
    y = jnp.where(spot[3] == 0, second, first)
    return dp_index(x, z, y)


def row_chunk_kernel(groups, spot, *refs):
    lefts = refs[: SLOTS * len(groups)]
    rights = refs[SLOTS * len(groups) : SLOTS * len(groups) + sum(groups)]
    outs, held, sems = refs[-RING - 2 : -2], refs[-2], refs[-1]

    def make(slot):
        column = place = 0
        for group, count in enumerate(groups):
            rows = jnp.concatenate(
                [left[0] for left in lefts[SLOTS * group : SLOTS * (group + 1)]], axis=0
            )
            for right in rights[place : place + count]:
                slot[:, column : column + right.shape[1]] = dot(rows, right[...]).astype(
                    jnp.bfloat16
                )
                column += right.shape[1]
            place += count

    send_chunk(pl.program_id(0), make, outs, held, sems)


def row_chunks(pairs, spot, ties=(), micros=0):
    lefts = [left.reshape(BLOCKS, left.shape[0] // BLOCKS, left.shape[1]) for left, _ in pairs]
    rights = [right for _, group in pairs for right in group]
    rows = lefts[0].shape[1]
    total = sum(right.shape[1] for right in rights)
    in_specs, operands = [], []
    for left in lefts:
        for slot in range(SLOTS):
            in_specs.append(
                pl.BlockSpec(
                    (1,) + left.shape[1:],
                    lambda step, spot, slot=slot: (
                        chunk_block(SEND_ORDER, slot, step, spot),
                        0,
                        0,
                    ),
                )
            )
            operands.append(left)
    parts = pl.pallas_call(
        functools.partial(row_chunk_kernel, [len(group) for _, group in pairs]),
        grid_spec=pltpu.PrefetchScalarGridSpec(
            num_scalar_prefetch=1,
            grid=(RING,),
            in_specs=in_specs
            + [pl.BlockSpec(right.shape, lambda step, spot: (0, 0)) for right in rights]
            + [pl.BlockSpec(memory_space=pl.ANY)] * len(ties),
            out_specs=[pl.BlockSpec(memory_space=pl.ANY)] * RING,
            scratch_shapes=[
                pltpu.VMEM((2, SLOTS * rows, total), jnp.bfloat16),
                pltpu.SemaphoreType.DMA((2,)),
            ],
        ),
        out_shape=[jax.ShapeDtypeStruct((SLOTS * rows, total), jnp.bfloat16)] * RING,
        compiler_params=pltpu.CompilerParams(vmem_limit_bytes=VMEM_LIMIT),
        cost_estimate=cost_of(micros),
        name="row_chunks",
    )(spot, *operands, *rights, *ties)
    return [parts[SEND_ORDER.index(offset)] for offset in range(RING)]


def column_chunk_kernel(lefts, count, spot, *refs):
    rights = refs[lefts : lefts + SLOTS]
    outs, held, sems = refs[-count - 2 : -2], refs[-2], refs[-1]

    def make(slot):
        whole = jnp.concatenate([right[...] for right in rights], axis=1)
        row = 0
        for left in refs[:lefts]:
            slot[row : row + left.shape[0], :] = dot(left[...], whole).astype(jnp.bfloat16)
            row += left.shape[0]

    send_chunk(pl.program_id(0), make, outs, held, sems)


def column_chunks(lefts, right, order, spot, ties=()):
    rows = sum(left.shape[0] for left in lefts)
    depth, columns = right.shape
    return pl.pallas_call(
        functools.partial(column_chunk_kernel, len(lefts), len(order)),
        grid_spec=pltpu.PrefetchScalarGridSpec(
            num_scalar_prefetch=1,
            grid=(len(order),),
            in_specs=[pl.BlockSpec(left.shape, lambda step, spot: (0, 0)) for left in lefts]
            + [
                pl.BlockSpec(
                    (depth, columns // BLOCKS),
                    lambda step, spot, slot=slot: (0, chunk_block(order, slot, step, spot)),
                )
                for slot in range(SLOTS)
            ]
            + [pl.BlockSpec(memory_space=pl.ANY)] * len(ties),
            out_specs=[pl.BlockSpec(memory_space=pl.ANY)] * len(order),
            scratch_shapes=[
                pltpu.VMEM((2, rows, columns // RING), jnp.bfloat16),
                pltpu.SemaphoreType.DMA((2,)),
            ],
        ),
        out_shape=[jax.ShapeDtypeStruct((rows, columns // RING), jnp.bfloat16)] * len(order),
        compiler_params=pltpu.CompilerParams(vmem_limit_bytes=VMEM_LIMIT),
        cost_estimate=NO_COST,
        name="column_chunks",
    )(spot, *lefts, *([right] * SLOTS), *ties)


def add_up(refs, index):
    total = refs[0][index].astype(jnp.float32)
    for ref in refs[1:]:
        total = total + ref[index].astype(jnp.float32)
    return total


def lane_slice(start, size):
    return (slice(None), pl.ds(pl.multiple_of(start * size, size), size))


def ffn_second_kernel(spot, *refs):
    parts, outs = refs[:RING], refs[RING:]
    for offset in range(RING):
        for z in range(PAIR):
            slot = z * RING + (spot[2] + offset) % RING
            outs[offset][z] = add_up(parts, slot).astype(jnp.bfloat16)


def ffn_third_kernel(spot, *refs):
    for out, z in ((refs[-2], spot[1]), (refs[-1], (spot[1] + 1) % PAIR)):
        out[...] = add_up(refs[:RING], z).astype(jnp.bfloat16)


def ffn_last_kernel(kept, got, gate_out, up_out, down_out):
    total = kept[...].astype(jnp.float32) + got[...].astype(jnp.float32)
    hidden = gate_out.shape[1]
    gate_out[...] = total[:, :hidden]
    up_out[...] = total[:, hidden : 2 * hidden]
    down_out[...] = total[:, 2 * hidden :].T


def text_second_kernel(spot, *refs):
    parts, outs = refs[:RING], refs[RING:]
    lanes = parts[0].shape[1] // SLOTS
    for offset in range(RING):
        for z in range(PAIR):
            slot = z * RING + (spot[2] + offset) % RING
            outs[offset][:, z * lanes : (z + 1) * lanes] = add_up(
                parts, lane_slice(slot, lanes)
            ).astype(jnp.bfloat16)


def mixed_second_kernel(spot, *refs):
    text, attn, outs = refs[:RING], refs[RING : 2 * RING], refs[2 * RING :]
    columns, wide = text[0].shape
    rows = attn[0].shape[1]
    for offset in range(RING):
        out = outs[offset]
        out[:columns, :] = text[offset][...]
        for z in range(PAIR):
            slot = z * RING + (spot[2] + offset) % RING
            block = add_up(attn, slot).astype(jnp.bfloat16)
            for piece in range(block.shape[1] // wide):
                start = columns + (piece * PAIR + z) * rows
                out[start : start + rows, :] = block[:, piece * wide : (piece + 1) * wide]


def mixed_third_kernel(columns, rows, spot, *refs):
    parts = refs[:RING]
    lanes = refs[-1].shape[1]
    for out, z in ((refs[-2], spot[1]), (refs[-1], (spot[1] + 1) % PAIR)):
        index = (slice(0, columns), pl.ds(pl.multiple_of(z * lanes, lanes), lanes))
        out[:columns, :] = add_up(parts, index).astype(jnp.bfloat16)
        place = columns
        for piece in range((parts[0].shape[0] - columns) // (PAIR * rows)):
            start = pl.multiple_of(columns + (piece * PAIR + z) * rows, 16)
            block = add_up(parts, (pl.ds(start, rows), slice(None))).astype(jnp.bfloat16)
            for side in range(PAIR):
                out[place : place + rows, :] = block[:, side * lanes : (side + 1) * lanes]
                place += rows


def mixed_last_kernel(kept, got, textkey, textvalue, query, key, value, outw):
    total = kept[...].astype(jnp.float32) + got[...].astype(jnp.float32)
    columns = query.shape[1]
    textkey[...] = total[:columns].T
    textvalue[...] = total[columns : 2 * columns].T
    rows = query.shape[0]
    lanes = total.shape[1]
    place = 2 * columns
    for out in (query, key, value, None):
        blocks = []
        for piece in range(columns // lanes):
            blocks.append(total[place : place + rows])
            place += rows
        whole = jnp.concatenate(blocks, axis=1)
        if out is None:
            outw[...] = whole.T
        else:
            out[...] = whole


def whole_call(kernel, scalars, operands, outs, name, ties=(), scratch=(), micros=0):
    whole = pl.BlockSpec(memory_space=pltpu.VMEM)
    count = len(scalars) + len(operands)
    return pl.pallas_call(
        lambda *refs: kernel(*refs[:count], *refs[count + len(ties) :]),
        in_specs=[pl.BlockSpec(memory_space=pltpu.SMEM)] * len(scalars)
        + [whole] * len(operands)
        + [pl.BlockSpec(memory_space=pl.ANY)] * len(ties),
        out_specs=[whole] * len(outs),
        out_shape=[jax.ShapeDtypeStruct(shape, kind) for shape, kind in outs],
        scratch_shapes=list(scratch),
        compiler_params=pltpu.CompilerParams(vmem_limit_bytes=VMEM_LIMIT),
        cost_estimate=cost_of(micros),
        name=name,
    )(*scalars, *operands, *ties)


def exchange(chunks, axis):
    return [chunks[0]] + [
        dp_permute(chunks[step], axis, step) for step in range(1, len(chunks))
    ]


def by_slots(chunk):
    return chunk.reshape(SLOTS, chunk.shape[0] // SLOTS, chunk.shape[1])


def lane_index(shape):
    return lax.broadcasted_iota(jnp.int32, shape, 1)


def head_lanes(shape, head):
    lane = lane_index(shape)
    return (lane < HEAD) if head == 0 else (lane >= HEAD)


def per_head(values, reduce):
    first = head_lanes(values.shape, 0)
    left = jnp.sum(jnp.where(first, values, 0.0), axis=1, keepdims=True)
    right = jnp.sum(jnp.where(first, 0.0, values), axis=1, keepdims=True)
    return jnp.where(first, left, right)


def head_units(raw):
    inverse = lax.rsqrt(per_head(raw * raw, None) * (1.0 / HEAD) + EPS)
    return raw * inverse, inverse


def partner(values):
    lane = lane_index(values.shape)
    return jnp.where(
        lane % HEAD < HEAD // 2,
        pltpu.roll(values, LANES - HEAD // 2, 1),
        pltpu.roll(values, HEAD // 2, 1),
    )


def dot(left, right):
    return jnp.dot(left, right, preferred_element_type=jnp.float32)


def dot_t(left, right):
    return lax.dot_general(left, right, (((1,), (1,)), ((), ())), preferred_element_type=jnp.float32)


def attend_kernel(
    raw_q, raw_k, value, raw_t, text_value, cosine, sine, gains, gate, gate_swapped, mark_q, mark_k, mark_t,
    query_out, key_out, text_out, mixed_out, self_out, cross_out, self_log, cross_log,
):
    cos, sin = cosine[...], sine[...]
    unit = head_units(raw_q[...])[0] * gains[0:1, :]
    query = ((unit * cos + partner(unit) * sin).astype(jnp.bfloat16) * ROOT).astype(jnp.bfloat16)
    unit = head_units(raw_k[...])[0] * gains[1:2, :]
    key = (unit * cos + partner(unit) * sin).astype(jnp.bfloat16)
    text = (head_units(raw_t[...])[0] * gains[2:3, :]).astype(jnp.bfloat16)
    query_out[...] = query
    key_out[...] = key
    text_out[...] = text

    def attention(keys, marks, values):
        outs, sums = [], []
        for head in range(2):
            own = head_lanes(query.shape, head)
            own_keys = head_lanes(keys.shape, head)
            probe = jnp.where(own, query, mark_q[...])
            scores = dot_t(probe, jnp.where(own_keys, keys, marks))
            weights = jnp.exp(scores).astype(jnp.bfloat16)
            both = dot(weights, jnp.where(own_keys, values, jnp.ones_like(values)))
            outs.append(both)
        first = head_lanes(outs[0].shape, 0)
        product = jnp.where(first, outs[0], outs[1])
        total = jnp.where(first, outs[1], outs[0])
        return product / pltpu.roll(total, HEAD, 1), jnp.log(total)

    out, log = attention(key, mark_k[...], value[...])
    self_out[...] = out
    self_log[...] = log
    cross, log = attention(text, mark_t[...], text_value[...])
    cross_out[...] = cross
    cross_log[...] = log - jnp.log(gate_swapped[...])
    mixed_out[...] = (out + gate[...] * cross).astype(jnp.bfloat16)


def attention_grads(query, keys, marks, values, grad, out, log, mark_q):
    rows = grad.astype(jnp.float32)
    delta = per_head(rows * out, None)
    delta = pltpu.roll(delta, HEAD, 1)
    lane = lane_index(query.shape) % HEAD
    log_high = log.astype(jnp.bfloat16)
    log_low = (log - log_high.astype(jnp.float32)).astype(jnp.bfloat16)
    delta_high = delta.astype(jnp.bfloat16)
    delta_low = (delta - delta_high.astype(jnp.float32)).astype(jnp.bfloat16)
    zero = jnp.zeros_like(query)
    code = jnp.where(lane == 4, -log_high, jnp.where(lane == 5, -log_low, mark_q))
    shift = jnp.where(lane == 4, -delta_high, jnp.where(lane == 5, -delta_low, zero))
    key_grads, value_grads, query_grads = [], [], []
    for head in range(2):
        own = head_lanes(query.shape, head)
        own_keys = head_lanes(keys.shape, head)
        probe = jnp.where(own, query, code)
        probs = jnp.exp(dot_t(jnp.where(own_keys, keys, marks), probe))
        slope = dot_t(jnp.where(own_keys, values, marks), jnp.where(own, grad, shift))
        score_grad = (probs * slope).astype(jnp.bfloat16)
        value_grads.append(dot(probs.astype(jnp.bfloat16), grad))
        key_grads.append(dot(score_grad, query))
        turned = keys[:, head * HEAD : (head + 1) * HEAD].T
        query_grads.append(dot(turned, score_grad))
    first = head_lanes(keys.shape, 0)
    return (
        jnp.concatenate(query_grads, axis=0),
        jnp.where(first, key_grads[0], key_grads[1]),
        jnp.where(first, value_grads[0], value_grads[1]),
    )


def norm_back(weighted, unit, inverse):
    return inverse * (weighted - unit * (per_head(weighted * unit, None) * (1.0 / HEAD)))


def cross_back_kernel(
    query, text, text_value, raw_t, grad, out, log, gains, mark_q, mark_t,
    query_grad, raw_grad, value_grad, gain_sum, gate_sum,
):
    grad_q, grad_t, grad_v = attention_grads(
        query[...], text[...], mark_t[...], text_value[...], grad[...], out[...], log[...], mark_q[...]
    )
    query_grad[...] = grad_q.T
    value_grad[...] = grad_v.astype(jnp.bfloat16).T
    grad_t = grad_t.astype(jnp.bfloat16).astype(jnp.float32)
    unit, inverse = head_units(raw_t[...])
    gain_sum[...] = jnp.sum(grad_t * unit, axis=0, keepdims=True)
    raw_grad[...] = norm_back(grad_t * gains[2:3, :], unit, inverse).astype(jnp.bfloat16).T
    gate_sum[...] = jnp.sum(grad[...].astype(jnp.float32) * out[...], axis=0, keepdims=True)


def self_back_kernel(
    query, key, value, raw_q, raw_k, grad, out, log, cross_grad, cosine, sine, gains, mark_q, mark_k,
    query_grad, key_grad, value_grad, gain_sum,
):
    grad_q, grad_k, grad_v = attention_grads(
        query[...], key[...], mark_k[...], value[...], grad[...], out[...], log[...], mark_q[...]
    )
    value_grad[...] = grad_v.astype(jnp.bfloat16)
    cos, sin = cosine[...], sine[...]
    grad_q = (grad_q.T + cross_grad[...]) * ROOT
    for turn, raw, row, target in ((grad_q, raw_q, 0, query_grad), (grad_k, raw_k, 1, key_grad)):
        turn = turn.astype(jnp.bfloat16).astype(jnp.float32)
        turn = turn * cos - partner(turn) * sin
        unit, inverse = head_units(raw[...])
        gain_sum[row : row + 1, :] = jnp.sum(turn * unit, axis=0, keepdims=True)
        target[...] = norm_back(turn * gains[row : row + 1, :], unit, inverse).astype(jnp.bfloat16)


def pair_call(kernel, operands, outs, name, ties=(), micros=0):
    def spec(shape, cut):
        if cut is None:
            return pl.BlockSpec(shape, lambda pair: (0, 0))
        if cut == 1:
            return pl.BlockSpec((shape[0], LANES), lambda pair: (0, pair))
        return pl.BlockSpec((LANES, shape[1]), lambda pair: (pair, 0))

    width = outs[0][0][0] if outs[0][2] == 0 else outs[0][0][1]
    return pl.pallas_call(
        lambda *refs: kernel(*refs[: len(operands)], *refs[len(operands) + len(ties) :]),
        grid=(width // LANES,),
        in_specs=[spec(part.shape, cut) for part, cut in operands]
        + [pl.BlockSpec(memory_space=pl.ANY)] * len(ties),
        out_specs=[spec(shape, cut) for shape, _, cut in outs],
        out_shape=[jax.ShapeDtypeStruct(shape, kind) for shape, kind, _ in outs],
        compiler_params=pltpu.CompilerParams(vmem_limit_bytes=VMEM_LIMIT),
        cost_estimate=cost_of(micros),
        name=name,
    )(*[part for part, _ in operands], *ties)
def inverse_rms(values):
    return lax.rsqrt(jnp.mean(values * values, axis=-1, keepdims=True) + EPS)


def row_norm_back(weighted, unit, inverse):
    return inverse * (weighted - unit * jnp.mean(weighted * unit, axis=-1, keepdims=True))


def per_row(table, segment):
    return jnp.where(segment == 0.0, table[0:1], jnp.where(segment == 1.0, table[1:2], table[2:3]))


def total_of(parts):
    upper, near, far = parts
    rows = far.shape[0]
    return (
        upper[:rows].astype(jnp.float32) + near[:rows].astype(jnp.float32) + far[...].astype(jnp.float32)
    )


def segment_sums(member, values):
    high = values.astype(jnp.bfloat16)
    low = (values - high.astype(jnp.float32)).astype(jnp.bfloat16)
    return dot(member, high) + dot(member, low)


def tables_kernel(here, lens, segments, cosine, sine, mark_q, mark_k, mark_t, segment, member):
    rows = segments.shape[1]
    ids = segments[...]
    first = jnp.sum((ids < 1).astype(jnp.float32))
    second = jnp.sum((ids < 2).astype(jnp.float32))
    lane = lane_index((rows, LANES))
    half = HEAD // 2
    rate = jnp.exp((lane % half).astype(jnp.float32) * (-2.0 * math.log(10000.0) / HEAD))
    within = lane % HEAD
    for block, code in enumerate(ROW_ORDER):
        source = here[0] ^ code
        line = segments[pl.ds(source, 1), :].astype(jnp.float32)
        label = jnp.broadcast_to(line, (rows, rows)).T
        start = jnp.where(label == 0.0, 0.0, jnp.where(label == 1.0, first, second))
        token = (lax.broadcasted_iota(jnp.int32, (rows, LANES), 0) + source * rows).astype(jnp.float32)
        angle = (token - start) * rate
        index = slice(block * rows, (block + 1) * rows)
        cosine[index, :] = jnp.cos(angle)
        sine[index, :] = jnp.where(within < half, -1.0, 1.0) * jnp.sin(angle)
        same = ((label == within.astype(jnp.float32)) & (within < SEGS)).astype(jnp.float32)
        shut = (within == SEGS).astype(jnp.float32)
        ones = ((within >= SEGS) & (within < SEGS + 3)).astype(jnp.float32)
        mark_q[index, :] = (SHUT * same - SHUT * shut).astype(jnp.bfloat16)
        mark_k[index, :] = (same + ones).astype(jnp.bfloat16)
        if block == 0:
            segment[...] = label
            member[...] = (
                lax.broadcasted_iota(jnp.int32, (8, rows), 0).astype(jnp.float32) == line
            ).astype(jnp.bfloat16)
    for group in range(SEGS):
        lane = lane_index((TXT, LANES)) % HEAD
        row = lax.broadcasted_iota(jnp.int32, (TXT, LANES), 0)
        inside = ((lane == group) & (row < lens[group])).astype(jnp.float32)
        ones = ((lane >= SEGS) & (lane < SEGS + 3)).astype(jnp.float32)
        mark_t[group * TXT : (group + 1) * TXT, :] = (inside + ones).astype(jnp.bfloat16)


def text_kernel(captions, key_weight, value_weight, raw_out, value_out, raw_sum, value_sum):
    step = pl.program_id(0)

    @pl.when(step == 0)
    def _():
        raw_sum[...] = dot(captions[...], key_weight[...])
        value_sum[...] = dot(captions[...], value_weight[...])

    @pl.when(step > 0)
    def _():
        raw_sum[...] += dot(captions[...], key_weight[...])
        value_sum[...] += dot(captions[...], value_weight[...])

    @pl.when(step == pl.num_programs(0) - 1)
    def _():
        raw_out[...] = raw_sum[...]
        value_out[...] = value_sum[...].astype(jnp.bfloat16)


def text_call(captions, key_weight, value_weight):
    rows, depth = captions.shape
    columns = key_weight.shape[1]
    tile = depth // 4
    return pl.pallas_call(
        text_kernel,
        grid=(depth // tile,),
        in_specs=[
            pl.BlockSpec((rows, tile), lambda step: (0, step)),
            pl.BlockSpec((tile, columns), lambda step: (step, 0)),
            pl.BlockSpec((tile, columns), lambda step: (step, 0)),
        ],
        out_specs=[pl.BlockSpec((rows, columns), lambda step: (0, 0))] * 2,
        out_shape=[
            jax.ShapeDtypeStruct((rows, columns), jnp.float32),
            jax.ShapeDtypeStruct((rows, columns), jnp.bfloat16),
        ],
        scratch_shapes=[pltpu.VMEM((rows, columns), jnp.float32)] * 2,
        compiler_params=pltpu.CompilerParams(vmem_limit_bytes=VMEM_LIMIT),
        cost_estimate=NO_COST,
        name="text",
    )(captions, key_weight, value_weight)


def project_kernel(here, own, far, near, last, mods, gains, segment_q, query_w, key_w, value_w,
                   rows_out, raw_q, raw_k, value):
    table = mods[here[0]]
    rows = own.shape[0]
    for block, part in enumerate((own, far, near, last)):
        index = slice(block * rows, (block + 1) * rows)
        values = part[...].astype(jnp.float32)
        marks = segment_q[index, :].astype(jnp.float32)
        scale = jnp.where(
            marks[:, 0:1] > 0.0, table[0:1], jnp.where(marks[:, 1:2] > 0.0, table[1:2], table[2:3])
        )
        rows_out[index, :] = (
            values * inverse_rms(values) * gains[0:1] * (1.0 + scale)
        ).astype(jnp.bfloat16)
    raw_q[...] = dot(rows_out[...], query_w[...])
    raw_k[...] = dot(rows_out[...], key_w[...])
    value[...] = dot(rows_out[...], value_w[...]).astype(jnp.bfloat16)


def middle_kernel(here, block, upper, near, far, mods, gains, segment, attn_out, middle_out, rows_out):
    attn_sum = total_of((upper, near, far))
    label = segment[:, 0:1]
    factor = jnp.tanh(per_row(mods[here[0] ^ 1], label)) * gains[1:2]
    middle = block[...].astype(jnp.float32) + factor * (attn_sum * inverse_rms(attn_sum))
    attn_out[...] = attn_sum
    middle_out[...] = middle
    scale = per_row(mods[here[0] ^ 2], label)
    rows_out[...] = (middle * inverse_rms(middle) * gains[2:3] * (1.0 + scale)).astype(jnp.bfloat16)


def block_out_kernel(here, middle, upper, near, far, grad, mods, gains, segment, member,
                     block_out, grad_out, sums):
    ffn_sum = total_of((upper, near, far))
    inverse = inverse_rms(ffn_sum)
    unit = ffn_sum * inverse
    factor = jnp.tanh(per_row(mods[here[0] ^ 3], segment[:, 0:1])) * gains[3:4]
    block_out[...] = (middle[...] + factor * unit).astype(jnp.bfloat16)
    incoming = grad[...].astype(jnp.float32)
    grad_out[...] = row_norm_back(incoming * factor, unit, inverse).astype(jnp.bfloat16)
    sums[...] = segment_sums(member[...], incoming * unit)


def middle_back_kernel(here, middle, attn, upper, near, far, grad, mods, gains, segment, member,
                       middle_grad, attn_grad, ffn_sums, attn_sums):
    grad_in = total_of((upper, near, far))
    label = segment[:, 0:1]
    inverse = inverse_rms(middle[...])
    unit = middle[...] * inverse
    factor = gains[2:3] * (1.0 + per_row(mods[here[0] ^ 2], label))
    ffn_sums[...] = segment_sums(member[...], grad_in * unit)
    grad_middle = grad[...].astype(jnp.float32) + row_norm_back(grad_in * factor, unit, inverse)
    middle_grad[...] = grad_middle
    inverse = inverse_rms(attn[...])
    unit = attn[...] * inverse
    factor = jnp.tanh(per_row(mods[here[0] ^ 1], label)) * gains[1:2]
    attn_grad[...] = row_norm_back(grad_middle * factor, unit, inverse).astype(jnp.bfloat16)
    attn_sums[...] = segment_sums(member[...], grad_middle * unit)


def block_in_kernel(here, block, middle_grad, upper, near, far, mods, gains, segment, member,
                    in_grad, sums):
    grad_in = total_of((upper, near, far))
    values = block[...].astype(jnp.float32)
    inverse = inverse_rms(values)
    unit = values * inverse
    factor = gains[0:1] * (1.0 + per_row(mods[here[0]], segment[:, 0:1]))
    in_grad[...] = (
        middle_grad[...] + row_norm_back(grad_in * factor, unit, inverse)
    ).astype(jnp.bfloat16)
    sums[...] = segment_sums(member[...], grad_in * unit)


def sort_sums_kernel(here, *refs):
    names, kept, sent, held = refs[:4], refs[4], refs[5], refs[6]
    for name, part in enumerate(names):
        held[name] = part[...]
    for out, codes in ((kept, (0, 2)), (sent, (1, 3))):
        for half, code in enumerate(codes):
            out[half] = held[here[0] ^ code]


def pack_kernel(here, kept, near, far, part, gains, cond, head_gain, text_gain, gate_sum, gate, packed):
    total = (kept[0] + near[0] + far[...])[:SEGS]
    is_gate = (jnp.zeros(total.shape, jnp.int32) + here[0] % 2) == 1
    mod = part[...]
    bent = jnp.tanh(mod)
    factor = jnp.where(is_gate, bent, 1.0 + mod)
    slope = jnp.where(is_gate, 1.0 - bent * bent, 1.0)
    grad = total * slope * gains[pl.ds(here[0], 1), :]
    gain = jnp.sum(total * factor, axis=0, keepdims=True)
    high = gain.astype(jnp.bfloat16).astype(jnp.float32)
    gate_slope = 1.0 - gate[...] * gate[...]
    extras = jnp.concatenate(
        [head_gain[0:1], head_gain[1:2], text_gain[...], gate_sum[...] * gate_slope], axis=1
    )
    rows = [grad, cond[...].astype(jnp.float32), high, gain - high, extras]
    packed[...] = jnp.concatenate(rows, axis=0).astype(jnp.bfloat16)


def gains_kernel(heads, here, own, far, near, last, norm_out, head_out, gate_out):
    inner = heads * HEAD
    lane = lane_index((1, LANES))
    total = jnp.zeros((1, 3 * inner), jnp.float32)
    for code, part in zip(ROW_ORDER, (own, far, near, last)):
        source = here[0] ^ code
        norm_out[pl.ds(source, 1), :] = part[0:1, :]
        total = total + part[1:2, : 3 * inner]
        line = jnp.zeros((1, LANES), jnp.float32)
        for head in range(heads):
            start = 3 * inner + head * HEAD
            value = jnp.sum(part[1:2, start : start + HEAD], axis=1, keepdims=True)
            line = jnp.where(lane == head, value, line)
        gate_out[pl.ds(source, 1), :] = line
    for row in range(3):
        line = jnp.zeros((1, HEAD), jnp.float32)
        for head in range(heads):
            start = row * inner + head * HEAD
            line = line + total[:, start : start + HEAD]
        head_out[row : row + 1, :] = line


def shards(
    block_in,
    out_grad,
    condition,
    captions,
    caption_len,
    segment_ids,
    ada_weight,
    norm_gains,
    query_weight,
    key_weight,
    value_weight,
    head_gains,
    textkey_weight,
    textvalue_weight,
    cross_gate,
    out_weight,
    gate_weight,
    up_weight,
    down_weight,
):
    rows, width = block_in.shape
    length = segment_ids.shape[0]
    heads = cross_gate.shape[0]
    inner = heads * HEAD
    half_rows = length // 2
    position = lax.axis_index("tensor")
    spot = dp_spot(position)
    here = position.reshape(1)
    b16, f32 = jnp.bfloat16, jnp.float32

    blocks = gather_tensor(block_in)
    own_act = jax.nn.silu(condition.astype(f32)).astype(b16)
    own_part = jnp.dot(own_act, ada_weight, preferred_element_type=f32)
    parts = gather_tensor(own_part)
    mods = jnp.stack([parts[ROW_ORDER.index(code)] for code in range(4)])

    cosine, sine, mark_q, mark_k, mark_t, segment, member = whole_call(
        tables_kernel,
        (here, caption_len),
        [segment_ids.reshape(length // rows, rows)],
        [((length, LANES), f32)] * 2
        + [((length, LANES), b16)] * 2
        + [((SEGS * TXT, LANES), b16), ((rows, LANES), f32), ((8, rows), b16)],
        "tables",
    )
    caption_flat = captions.reshape(-1, captions.shape[-1])
    texts = caption_flat.shape[0]
    raw_t, text_value = text_call(caption_flat, textkey_weight, textvalue_weight)
    attn_rows, raw_q, raw_k, value = whole_call(
        project_kernel,
        (here,),
        blocks + [mods, norm_gains, mark_q, query_weight, key_weight, value_weight],
        [((length, width), b16), ((length, inner), f32), ((length, inner), f32), ((length, inner), b16)],
        "project",
    )
    tanh_gate = jnp.tanh(cross_gate)
    gate_lanes = jnp.repeat(tanh_gate, HEAD)[None]
    gate_swapped = jnp.repeat(tanh_gate.reshape(-1, 2)[:, ::-1].reshape(-1), HEAD)[None]
    gains = jnp.tile(head_gains, (1, heads))
    query, key, text, mixed, self_out, cross_out, self_log, cross_log = pair_call(
        attend_kernel,
        [(raw_q, 1), (raw_k, 1), (value, 1), (raw_t, 1), (text_value, 1), (cosine, None), (sine, None)]
        + [(gains, 1), (gate_lanes, 1), (gate_swapped, 1), (mark_q, None), (mark_k, None), (mark_t, None)],
        [((length, inner), b16, 1)] * 2
        + [((texts, inner), b16, 1), ((length, inner), b16, 1)]
        + [((length, inner), f32, 1)] * 4,
        "attend",
    )

    def halves(product):
        return product(slice(0, half_rows)).astype(b16), product(slice(half_rows, None)).astype(b16)

    def all_of(block):
        return jnp.concatenate(gather_tensor(block), axis=0)

    upper, lower = halves(lambda part: jnp.dot(mixed[part], out_weight, preferred_element_type=f32))
    sums, sent = scatter_tensor(upper, lower)
    attn_rows_t = turned(attn_rows, (sent,))
    wide = ((rows, width), f32)
    narrow = ((rows, width), b16)
    totals = ((8, width), f32)
    attn_sum, middle, ffn_own = whole_call(
        middle_kernel,
        (here,),
        [block_in] + sums + [mods, norm_gains, segment],
        [wide, wide, narrow],
        "middle",
    )
    ffn_rows = all_of(ffn_own)
    gate_pre = jnp.dot(ffn_rows, gate_weight, preferred_element_type=f32)
    up_pre = jnp.dot(ffn_rows, up_weight, preferred_element_type=f32)
    sigmoid_gate = jax.nn.sigmoid(gate_pre)
    silu_gate = gate_pre * sigmoid_gate
    hidden = (silu_gate * up_pre).astype(b16)
    upper, lower = halves(lambda part: jnp.dot(hidden[part], down_weight, preferred_element_type=f32))
    sums, sent = scatter_tensor(upper, lower)
    ffn_rows_t = turned(ffn_rows, (sent,))
    block_out, grad_own, sum_gate_ffn = whole_call(
        block_out_kernel,
        (here,),
        [middle] + sums + [out_grad, mods, norm_gains, segment, member],
        [narrow, narrow, totals],
        "block_out",
    )

    grad_ffn = all_of(grad_own)
    grad_hidden = times_transpose(grad_ffn, down_weight)
    grad_gate = (
        grad_hidden * up_pre * sigmoid_gate * (1.0 + gate_pre * (1.0 - sigmoid_gate))
    ).astype(b16)
    grad_up = (grad_hidden * silu_gate).astype(b16)
    upper, lower = halves(
        lambda part: times_transpose(grad_gate[part], gate_weight)
        + times_transpose(grad_up[part], up_weight)
    )
    sums, sent = scatter_tensor(upper, lower)
    grad_ffn_t = turned(grad_ffn, (sent,))
    ffn_parts = row_chunks(
        [(ffn_rows_t, [grad_gate, grad_up]), (grad_ffn_t, [hidden])], spot, (sent,)
    )
    grad_middle, grad_own, sum_scale_ffn, sum_gate_attn = whole_call(
        middle_back_kernel,
        (here,),
        [middle, attn_sum] + sums + [out_grad, mods, norm_gains, segment, member],
        [wide, narrow, totals, totals],
        "middle_back",
    )

    grad_attn = all_of(grad_own)
    grad_mixed = times_transpose(grad_attn, out_weight).astype(b16)
    cross_grad, text_grad, text_value_grad, text_gain, gate_sum = pair_call(
        cross_back_kernel,
        [(query, 1), (text, 1), (text_value, 1), (raw_t, 1), (grad_mixed, 1), (cross_out, 1)]
        + [(cross_log, 1), (gains, 1), (mark_q, None), (mark_t, None)],
        [((length, inner), f32, 1), ((inner, texts), b16, 0), ((inner, texts), b16, 0)]
        + [((1, inner), f32, 1)] * 2,
        "cross_back",
        micros=CROSS_MICROS,
    )
    hidden_cols = hidden.shape[1]
    block_rows = width // BLOCKS
    got = [by_slots(part) for part in exchange(ffn_parts, "first")]
    shape = (PAIR, block_rows, 3 * hidden_cols)
    stage = whole_call(
        ffn_second_kernel, (spot,), got, [(shape, b16)] * RING, "ffn_second", (text_grad,)
    )
    text_lefts = [text_grad, text_value_grad]
    text_parts = [None] * RING
    text_parts[2], text_parts[1] = column_chunks(
        text_lefts, caption_flat, (2, 1), spot, (stage[0],)
    )
    text_parts[3], text_parts[0] = column_chunks(
        text_lefts, caption_flat, (3, 0), spot, (text_parts[2],)
    )
    kept, sent = whole_call(
        ffn_third_kernel,
        (spot,),
        exchange(stage, "second"),
        [(shape[1:], b16)] * 2,
        "ffn_third",
        (text_parts[0],),
    )
    query_grad, key_grad, value_grad, head_gain = pair_call(
        self_back_kernel,
        [(query, 1), (key, 1), (value, 1), (raw_q, 1), (raw_k, 1), (grad_mixed, 1), (self_out, 1)]
        + [(self_log, 1), (cross_grad, 1), (cosine, None), (sine, None), (gains, 1)]
        + [(mark_q, None), (mark_k, None)],
        [((length, inner), b16, 1)] * 3 + [((2, inner), f32, 1)],
        "self_back",
        (kept,),
    )
    gate_sum_out, up_sum_out, down_sum_out = whole_call(
        ffn_last_kernel,
        (),
        exchange([kept, sent], "z"),
        [((block_rows, hidden_cols), f32)] * 2 + [((hidden_cols, block_rows), f32)],
        "ffn_last",
    )
    upper, lower = halves(
        lambda part: times_transpose(query_grad[part], query_weight)
        + times_transpose(key_grad[part], key_weight)
        + times_transpose(value_grad[part], value_weight)
    )
    sums, sent = scatter_tensor(upper, lower)
    text_rows = caption_flat.shape[1] // BLOCKS
    stacked = 2 * inner + 4 * inner // text_rows * block_rows
    text_stage = whole_call(
        text_second_kernel,
        (spot,),
        exchange(text_parts, "first"),
        [((2 * inner, PAIR * text_rows), b16)] * RING,
        "text_second",
        (gate_sum_out,),
    )
    attn_parts = row_chunks(
        [
            (attn_rows_t, [query_grad, key_grad, value_grad]),
            (turned(grad_attn, (text_parts[0],)), [mixed]),
        ],
        spot,
        (sent, text_stage[0]),
    )
    in_grad, sum_scale_attn = whole_call(
        block_in_kernel,
        (here,),
        [block_in, grad_middle] + sums + [mods, norm_gains, segment, member],
        [narrow, totals],
        "block_in",
        micros=BLOCK_IN_MICROS,
    )

    stage = whole_call(
        mixed_second_kernel,
        (spot,),
        list(text_stage) + [by_slots(part) for part in exchange(attn_parts, "first")],
        [((stacked, PAIR * text_rows), b16)] * RING,
        "mixed_second",
    )
    kept, sent = whole_call(
        functools.partial(mixed_third_kernel, 2 * inner, block_rows),
        (spot,),
        exchange(stage, "second"),
        [((stacked, text_rows), b16)] * 2,
        "mixed_third",
    )
    textkey_sum, textvalue_sum, query_sum, key_sum, value_sum, outw_sum = whole_call(
        mixed_last_kernel,
        (),
        exchange([kept, sent], "z"),
        [((text_rows, inner), f32)] * 2
        + [((block_rows, inner), f32)] * 3
        + [((inner, block_rows), f32)],
        "mixed_last",
    )

    kept, sent = whole_call(
        sort_sums_kernel,
        (here,),
        [sum_scale_attn, sum_gate_attn, sum_scale_ffn, sum_gate_ffn],
        [((2, 8, width), f32)] * 2,
        "sort_sums",
        scratch=[pltpu.VMEM((4, 8, width), f32)],
    )
    near = swap_core(sent)
    far = swap_chip(kept[1] + near[1])
    (packed,) = whole_call(
        pack_kernel,
        (here,),
        [kept, near, far, own_part, norm_gains, condition.reshape(-1, width)]
        + [head_gain, text_gain, gate_sum, gate_lanes],
        [((8, width), b16)],
        "pack",
        (stage[0],),
    )
    gathered = gather_dp(packed)
    acts = gathered[:, SEGS : SEGS + 2].reshape(BLOCKS * SEGS, condition.shape[1])
    ada_rows = acts.shape[1] // BLOCKS
    acts = lax.dynamic_slice_in_dim(acts, lax.axis_index("dp") * ada_rows, ada_rows, 1)
    acts = jax.nn.silu(acts.astype(f32)).astype(b16)
    ada_grad = lax.dot_general(
        acts,
        gathered[:, :SEGS].reshape(-1, width),
        (((0,), (0,)), ((), ())),
        preferred_element_type=f32,
    )
    rest = jnp.sum(gathered[:, SEGS + 2 :].astype(f32), axis=0)
    rest = jnp.stack([rest[0] + rest[1], rest[2]])
    norm_grads, head_grads, crossgate = whole_call(
        functools.partial(gains_kernel, heads),
        (here,),
        gather_tensor(rest),
        [((4, width), f32), ((3, HEAD), f32), ((4, LANES), f32)],
        "gains",
    )
    crossgate_grad = crossgate[:, :heads].reshape(-1)
    return (
        block_out,
        in_grad,
        ada_grad,
        norm_grads,
        query_sum,
        key_sum,
        value_sum,
        head_grads,
        textkey_sum,
        textvalue_sum,
        crossgate_grad,
        outw_sum,
        gate_sum_out,
        up_sum_out,
        down_sum_out,
    )


def solution(mesh):
    return jax.shard_map(
        shards,
        mesh=mesh,
        in_specs=(
            P(("dp", "tensor"), None),
            P(("dp", "tensor"), None),
            P("dp", None),
            P("dp", None, None),
            P("dp"),
            P("dp"),
            P(None, "tensor"),
            P(),
            P(None, "tensor"),
            P(None, "tensor"),
            P(None, "tensor"),
            P(),
            P(None, "tensor"),
            P(None, "tensor"),
            P("tensor"),
            P("tensor", None),
            P(None, "tensor"),
            P(None, "tensor"),
            P("tensor", None),
        ),
        out_specs=(
            P(("dp", "tensor"), None),
            P(("dp", "tensor"), None),
            P("dp", "tensor"),
            P(),
            P("dp", "tensor"),
            P("dp", "tensor"),
            P("dp", "tensor"),
            P(),
            P("dp", "tensor"),
            P("dp", "tensor"),
            P(),
            P("tensor", "dp"),
            P("dp", "tensor"),
            P("dp", "tensor"),
            P("tensor", "dp"),
        ),
        check_vma=False,
    )
```

```python
import functools
import math

import jax
import jax.numpy as jnp
from jax import lax
from jax.experimental import pallas as pl
from jax.experimental.pallas import tpu as pltpu
from jax.sharding import PartitionSpec as P

HEAD = 64
HEADS = 24
TXT = 256
SEGS = 3
EPS = 1e-06
LANES = 2 * HEAD
SHUT = 256.0
ROOT = HEAD ** (-0.5)
VMEM_LIMIT = 50 * 2**20
NO_COST = pl.CostEstimate(flops=0, bytes_accessed=0, transcendentals=0)


def cost_of(micros):
    return pl.CostEstimate(flops=int(micros * 1e9), bytes_accessed=0, transcendentals=0)


CROSS_MICROS = 10
BLOCK_IN_MICROS = 10
FFN_MICROS = 3
FFN_NEXT_MICROS = 8
MIDDLE_MICROS = 10
SELF_MICROS = 0

RING = 4
PAIR = 2
BLOCKS = RING * PAIR * RING
SLOTS = BLOCKS // RING
SEND_ORDER = (2, 1, 3, 0)
CORE_SWAP = [(0, 1), (1, 0), (2, 3), (3, 2)]
CHIP_SWAP = [(0, 2), (2, 0), (1, 3), (3, 1)]
ROW_ORDER = (0, 2, 1, 3)

def dp_index(x, z, y):
    return (x * PAIR + z) * RING + y


def dp_perm(axis, step):
    pairs = []
    for x in range(RING):
        for z in range(PAIR):
            for y in range(RING):
                for tensor in range(2 * PAIR):
                    way = axis
                    if axis in ("first", "second"):
                        way = "x" if (tensor % 2 == 0) == (axis == "first") else "y"
                    target = {
                        "x": ((x + step) % RING, z, y),
                        "y": (x, z, (y + step) % RING),
                        "z": (x, (z + step) % PAIR, y),
                    }[way]
                    pairs.append(
                        (
                            dp_index(x, z, y) * 2 * PAIR + tensor,
                            dp_index(*target) * 2 * PAIR + tensor,
                        )
                    )
    return pairs


def dp_permute(values, axis, step):
    return lax.ppermute(values, ("dp", "tensor"), dp_perm(axis, step))


def dp_spot(position):
    index = lax.axis_index("dp")
    x, z, y = index // (RING * PAIR), index // RING % PAIR, index % RING
    core = position % 2
    return jnp.stack([jnp.where(core == 0, x, y), z, jnp.where(core == 0, y, x), core])


def swap_core(values):
    return lax.ppermute(values, "tensor", CORE_SWAP)


def swap_chip(values):
    return lax.ppermute(values, "tensor", CHIP_SWAP)


def times_transpose(left, right):
    return lax.dot_general(
        left, right, (((1,), (1,)), ((), ())), preferred_element_type=jnp.float32
    )


def gather_tensor(block):
    far = swap_chip(block)
    near = swap_core(block)
    return [block, far, near, swap_core(far)]


def join_kernel(own, far, both, far_out):
    rows = own.shape[0]
    both[:rows, :] = own[...]
    both[rows:, :] = far[...]
    far_out[...] = far[...]


def gather_rows(block, ties=()):
    rows, width = block.shape
    near = swap_core(block)
    upper, far = whole_call(
        join_kernel,
        (),
        [block, swap_chip(block)],
        [((2 * rows, width), block.dtype), ((rows, width), block.dtype)],
        "join",
        ties,
    )
    return jnp.concatenate([upper, near, swap_core(far)], axis=0)


def scatter_tensor(upper, lower):
    near = swap_core(lower)
    rows = upper.shape[0] // 2
    far = (upper[rows:].astype(jnp.float32) + near[rows:].astype(jnp.float32)).astype(near.dtype)
    return [upper, near, swap_chip(far)], far


def turn_kernel(source, target):
    target[...] = source[...].T


def turned(values, ties=()):
    tile = 512 if values.shape[1] % 512 == 0 else values.shape[1]
    return pl.pallas_call(
        lambda source, *rest: turn_kernel(source, rest[-1]),
        grid=(values.shape[1] // tile,),
        in_specs=[pl.BlockSpec((values.shape[0], tile), lambda step: (0, step))]
        + [pl.BlockSpec(memory_space=pl.ANY)] * len(ties),
        out_specs=pl.BlockSpec((tile, values.shape[0]), lambda step: (step, 0)),
        out_shape=jax.ShapeDtypeStruct(values.shape[::-1], values.dtype),
        compiler_params=pltpu.CompilerParams(vmem_limit_bytes=VMEM_LIMIT),
        cost_estimate=NO_COST,
    )(values, *ties)


def chunk_block(offset, slot, spot):
    first = (spot[0] + offset) % RING
    z, second = slot // RING, slot % RING
    x = jnp.where(spot[3] == 0, first, second)
    y = jnp.where(spot[3] == 0, second, first)
    return dp_index(x, z, y)


def offset_of_step(offsets, step):
    offset = offsets[-1]
    for place in range(len(offsets) - 1):
        offset = jnp.where(step == place, offsets[place], offset)
    return offset


def chunk_kernel(make, offsets, halves, extra, outs, held, sems):
    step = pl.program_id(0)
    first, second = halves

    def copies(place):
        slot = held.at[place % 2]
        if offsets[place] != 2:
            return [pltpu.make_async_copy(slot, outs[place], sems.at[place % 2, 0])]
        return [
            pltpu.make_async_copy(slot.at[half], out, sems.at[place % 2, way])
            for way, (half, out) in enumerate(zip((first, second), outs[place]))
        ]

    for place, offset in enumerate(offsets):

        @pl.when(step == place)
        def _(place=place, offset=offset):
            if place >= 2:
                for copy in copies(place - 2):
                    copy.wait()
            added = {1: (first, extra[0]), 3: (second, extra[1])}.get(offset) if extra else None
            make(held.at[place % 2], added)
            for copy in copies(place):
                copy.start()
            if place == len(offsets) - 1:
                for last in range(max(place - 1, 0), place + 1):
                    for copy in copies(last):
                        copy.wait()


def chunk_call(make, operands, specs, offsets, halves, shape, spot, extra, ties, name, micros):
    count = len(operands)
    pieces = []
    for offset in offsets:
        if offset == 2:
            pieces += [tuple(len(range(*s.indices(d))) for s, d in zip(h, shape)) for h in halves]
        else:
            pieces.append(shape)

    def kernel(spot_ref, *refs):
        inputs, extras = refs[:count], refs[count : count + len(extra)]
        outs = list(refs[-len(pieces) - 2 : -2])
        grouped = []
        for offset in offsets:
            grouped.append((outs.pop(0), outs.pop(0)) if offset == 2 else outs.pop(0))
        chunk_kernel(
            functools.partial(make, inputs), offsets, halves, extras, grouped, refs[-2], refs[-1]
        )

    found = pl.pallas_call(
        kernel,
        grid_spec=pltpu.PrefetchScalarGridSpec(
            num_scalar_prefetch=1,
            grid=(len(offsets),),
            in_specs=list(specs)
            + [pl.BlockSpec(part.shape, lambda step, spot: (0, 0)) for part in extra]
            + [pl.BlockSpec(memory_space=pl.ANY)] * len(ties),
            out_specs=[pl.BlockSpec(memory_space=pl.ANY)] * len(pieces),
            scratch_shapes=[
                pltpu.VMEM((2,) + shape, jnp.bfloat16),
                pltpu.SemaphoreType.DMA((2, 2)),
            ],
        ),
        out_shape=[jax.ShapeDtypeStruct(piece, jnp.bfloat16) for piece in pieces],
        compiler_params=pltpu.CompilerParams(vmem_limit_bytes=VMEM_LIMIT),
        cost_estimate=cost_of(micros),
        name=name,
    )(spot, *operands, *extra, *ties)
    found = list(found)
    return [
        (found.pop(0), found.pop(0)) if offset == 2 else found.pop(0) for offset in offsets
    ]


def make_rows(groups, inputs, slot, added):
    lefts, rights = inputs[: SLOTS * len(groups)], inputs[SLOTS * len(groups) :]
    column = place = 0
    for group, count in enumerate(groups):
        rows = jnp.concatenate(
            [left[0] for left in lefts[SLOTS * group : SLOTS * (group + 1)]], axis=0
        )
        for right in rights[place : place + count]:
            wide = right.shape[1]
            product = dot(rows, right[...])
            low, high = column, column
            if added is not None:
                low = min(max(column, added[0][1].start), column + wide)
                high = min(max(column, added[0][1].stop), column + wide)
            for start, stop in ((column, low), (low, high), (high, column + wide)):
                if start < stop:
                    part = product[:, start - column : stop - column]
                    if (start, stop) == (low, high):
                        base = added[0][1].start
                        part = part + added[1][:, start - base : stop - base].astype(jnp.float32)
                    slot[:, start:stop] = part.astype(jnp.bfloat16)
            column += wide
        place += count


def row_chunks(pairs, offsets, spot, extra=(), ties=(), micros=0):
    lefts = [left.reshape(BLOCKS, left.shape[0] // BLOCKS, left.shape[1]) for left, _ in pairs]
    rights = [right for _, group in pairs for right in group]
    total = sum(right.shape[1] for right in rights)
    specs, operands = [], []
    for left in lefts:
        for slot in range(SLOTS):
            specs.append(
                pl.BlockSpec(
                    (1,) + left.shape[1:],
                    lambda step, spot, slot=slot: (
                        chunk_block(offset_of_step(offsets, step), slot, spot),
                        0,
                        0,
                    ),
                )
            )
            operands.append(left)
    specs += [pl.BlockSpec(right.shape, lambda step, spot: (0, 0)) for right in rights]
    rows = SLOTS * lefts[0].shape[1]
    halves = [(slice(0, rows), slice(0, total // 2)), (slice(0, rows), slice(total // 2, total))]
    return chunk_call(
        functools.partial(make_rows, [len(group) for _, group in pairs]),
        operands + rights,
        specs,
        offsets,
        halves,
        (rows, total),
        spot,
        extra,
        ties,
        "row_chunks",
        micros,
    )


def make_columns(lefts, inputs, slot, added):
    whole = jnp.concatenate([right[...] for right in inputs[lefts:]], axis=1)
    row = 0
    for left in inputs[:lefts]:
        product = dot(left[...], whole)
        if added is not None and added[0][0].start == row:
            product = product + added[1][...].astype(jnp.float32)
        slot[row : row + left.shape[0], :] = product.astype(jnp.bfloat16)
        row += left.shape[0]


def column_chunks(lefts, right, offsets, spot, extra=(), ties=(), micros=0):
    rows = lefts[0].shape[0]
    depth, columns = right.shape
    specs = [pl.BlockSpec(left.shape, lambda step, spot: (0, 0)) for left in lefts]
    for slot in range(SLOTS):
        specs.append(
            pl.BlockSpec(
                (depth, columns // BLOCKS),
                lambda step, spot, slot=slot: (
                    0,
                    chunk_block(offset_of_step(offsets, step), slot, spot),
                ),
            )
        )
    lanes = columns // RING
    halves = [(slice(0, rows), slice(0, lanes)), (slice(rows, 2 * rows), slice(0, lanes))]
    return chunk_call(
        functools.partial(make_columns, len(lefts)),
        list(lefts) + [right] * SLOTS,
        specs,
        offsets,
        halves,
        (2 * rows, lanes),
        spot,
        extra,
        ties,
        "column_chunks",
        micros,
    )


def add_up(refs, index):
    total = refs[0][index].astype(jnp.float32)
    for ref in refs[1:]:
        total = total + ref[index].astype(jnp.float32)
    return total


def lane_slice(start, size):
    return (slice(None), pl.ds(pl.multiple_of(start * size, size), size))


def ffn_second_kernel(spot, *refs):
    parts, outs = refs[:-RING], refs[-RING:]
    for offset in range(RING):
        for z in range(PAIR):
            slot = z * RING + (spot[2] + offset) % RING
            outs[offset][z] = add_up(parts, slot).astype(jnp.bfloat16)


def ffn_third_kernel(spot, *refs):
    for out, z in ((refs[-2], spot[1]), (refs[-1], (spot[1] + 1) % PAIR)):
        out[...] = add_up(refs[:RING], z).astype(jnp.bfloat16)


def ffn_last_kernel(kept, got, gate_out, up_out, down_out):
    total = kept[...].astype(jnp.float32) + got[...].astype(jnp.float32)
    hidden = gate_out.shape[1]
    gate_out[...] = total[:, :hidden]
    up_out[...] = total[:, hidden : 2 * hidden]
    down_out[...] = total[:, 2 * hidden :].T


def text_second_kernel(spot, *refs):
    parts, outs = refs[:-RING], refs[-RING:]
    lanes = parts[0].shape[1] // SLOTS
    for offset in range(RING):
        for z in range(PAIR):
            slot = z * RING + (spot[2] + offset) % RING
            outs[offset][:, z * lanes : (z + 1) * lanes] = add_up(
                parts, lane_slice(slot, lanes)
            ).astype(jnp.bfloat16)


def mixed_second_kernel(spot, *refs):
    text, attn, outs = refs[:RING], refs[RING:-RING], refs[-RING:]
    columns, wide = text[0].shape
    rows = attn[0].shape[1]
    for offset in range(RING):
        out = outs[offset]
        out[:columns, :] = text[offset][...]
        for z in range(PAIR):
            slot = z * RING + (spot[2] + offset) % RING
            block = add_up(attn, slot).astype(jnp.bfloat16)
            for piece in range(block.shape[1] // wide):
                start = columns + (piece * PAIR + z) * rows
                out[start : start + rows, :] = block[:, piece * wide : (piece + 1) * wide]


def mixed_third_kernel(columns, rows, spot, *refs):
    parts = refs[:RING]
    lanes = refs[-1].shape[1]
    for out, z in ((refs[-2], spot[1]), (refs[-1], (spot[1] + 1) % PAIR)):
        index = (slice(0, columns), pl.ds(pl.multiple_of(z * lanes, lanes), lanes))
        out[:columns, :] = add_up(parts, index).astype(jnp.bfloat16)
        place = columns
        for piece in range((parts[0].shape[0] - columns) // (PAIR * rows)):
            start = pl.multiple_of(columns + (piece * PAIR + z) * rows, 16)
            block = add_up(parts, (pl.ds(start, rows), slice(None))).astype(jnp.bfloat16)
            for side in range(PAIR):
                out[place : place + rows, :] = block[:, side * lanes : (side + 1) * lanes]
                place += rows


def mixed_last_kernel(kept, got, textkey, textvalue, query, key, value, outw):
    total = kept[...].astype(jnp.float32) + got[...].astype(jnp.float32)
    columns = query.shape[1]
    textkey[...] = total[:columns].T
    textvalue[...] = total[columns : 2 * columns].T
    rows = query.shape[0]
    lanes = total.shape[1]
    place = 2 * columns
    for out in (query, key, value, None):
        blocks = []
        for piece in range(columns // lanes):
            blocks.append(total[place : place + rows])
            place += rows
        whole = jnp.concatenate(blocks, axis=1)
        if out is None:
            outw[...] = whole.T
        else:
            out[...] = whole


def whole_call(kernel, scalars, operands, outs, name, ties=(), scratch=(), micros=0):
    whole = pl.BlockSpec(memory_space=pltpu.VMEM)
    count = len(scalars) + len(operands)
    return pl.pallas_call(
        lambda *refs: kernel(*refs[:count], *refs[count + len(ties) :]),
        in_specs=[pl.BlockSpec(memory_space=pltpu.SMEM)] * len(scalars)
        + [whole] * len(operands)
        + [pl.BlockSpec(memory_space=pl.ANY)] * len(ties),
        out_specs=[whole] * len(outs),
        out_shape=[jax.ShapeDtypeStruct(shape, kind) for shape, kind in outs],
        scratch_shapes=list(scratch),
        compiler_params=pltpu.CompilerParams(vmem_limit_bytes=VMEM_LIMIT),
        cost_estimate=cost_of(micros),
        name=name,
    )(*scalars, *operands, *ties)


def exchange(chunks, axis):
    return [chunks[0]] + [
        dp_permute(chunks[step], axis, step) for step in range(1, len(chunks))
    ]


def one_on(halves):
    return dp_permute(halves[0], "first", 1), dp_permute(halves[1], "first", RING - 1)


def to_neighbours(own, ahead, behind):
    return [own, dp_permute(ahead, "first", 1), dp_permute(behind, "first", RING - 1)]


def by_slots(chunk):
    return chunk.reshape(SLOTS, chunk.shape[0] // SLOTS, chunk.shape[1])


def lane_index(shape):
    return lax.broadcasted_iota(jnp.int32, shape, 1)


def head_lanes(shape, head):
    lane = lane_index(shape)
    return (lane < HEAD) if head == 0 else (lane >= HEAD)


def per_head(values, reduce):
    first = head_lanes(values.shape, 0)
    left = jnp.sum(jnp.where(first, values, 0.0), axis=1, keepdims=True)
    right = jnp.sum(jnp.where(first, 0.0, values), axis=1, keepdims=True)
    return jnp.where(first, left, right)


def head_units(raw):
    inverse = lax.rsqrt(per_head(raw * raw, None) * (1.0 / HEAD) + EPS)
    return raw * inverse, inverse


def partner(values):
    lane = lane_index(values.shape)
    return jnp.where(
        lane % HEAD < HEAD // 2,
        pltpu.roll(values, LANES - HEAD // 2, 1),
        pltpu.roll(values, HEAD // 2, 1),
    )


def dot(left, right):
    return jnp.dot(left, right, preferred_element_type=jnp.float32)


def dot_t(left, right):
    return lax.dot_general(left, right, (((1,), (1,)), ((), ())), preferred_element_type=jnp.float32)


def attend_kernel(
    raw_q, raw_k, value, raw_t, text_value, cosine, sine, gains, gate, gate_swapped, mark_q, mark_k, mark_t,
    query_out, key_out, text_out, mixed_out, self_out, cross_out, self_log, cross_log,
):
    cos, sin = cosine[...], sine[...]
    unit = head_units(raw_q[...])[0] * gains[0:1, :]
    query = ((unit * cos + partner(unit) * sin).astype(jnp.bfloat16) * ROOT).astype(jnp.bfloat16)
    unit = head_units(raw_k[...])[0] * gains[1:2, :]
    key = (unit * cos + partner(unit) * sin).astype(jnp.bfloat16)
    text = (head_units(raw_t[...])[0] * gains[2:3, :]).astype(jnp.bfloat16)
    query_out[...] = query
    key_out[...] = key
    text_out[...] = text

    def attention(keys, marks, values):
        outs, sums = [], []
        for head in range(2):
            own = head_lanes(query.shape, head)
            own_keys = head_lanes(keys.shape, head)
            probe = jnp.where(own, query, mark_q[...])
            scores = dot_t(probe, jnp.where(own_keys, keys, marks))
            weights = jnp.exp(scores).astype(jnp.bfloat16)
            both = dot(weights, jnp.where(own_keys, values, jnp.ones_like(values)))
            outs.append(both)
        first = head_lanes(outs[0].shape, 0)
        product = jnp.where(first, outs[0], outs[1])
        total = jnp.where(first, outs[1], outs[0])
        return product / pltpu.roll(total, HEAD, 1), jnp.log(total)

    out, log = attention(key, mark_k[...], value[...])
    self_out[...] = out
    self_log[...] = log
    cross, log = attention(text, mark_t[...], text_value[...])
    cross_out[...] = cross
    cross_log[...] = log - jnp.log(gate_swapped[...])
    mixed_out[...] = (out + gate[...] * cross).astype(jnp.bfloat16)


def attention_grads(query, keys, marks, values, grad, out, log, mark_q):
    rows = grad.astype(jnp.float32)
    delta = per_head(rows * out, None)
    delta = pltpu.roll(delta, HEAD, 1)
    lane = lane_index(query.shape) % HEAD
    log_high = log.astype(jnp.bfloat16)
    log_low = (log - log_high.astype(jnp.float32)).astype(jnp.bfloat16)
    delta_high = delta.astype(jnp.bfloat16)
    delta_low = (delta - delta_high.astype(jnp.float32)).astype(jnp.bfloat16)
    zero = jnp.zeros_like(query)
    code = jnp.where(lane == 4, -log_high, jnp.where(lane == 5, -log_low, mark_q))
    shift = jnp.where(lane == 4, -delta_high, jnp.where(lane == 5, -delta_low, zero))
    key_grads, value_grads, query_grads = [], [], []
    for head in range(2):
        own = head_lanes(query.shape, head)
        own_keys = head_lanes(keys.shape, head)
        probe = jnp.where(own, query, code)
        probs = jnp.exp(dot_t(jnp.where(own_keys, keys, marks), probe))
        slope = dot_t(jnp.where(own_keys, values, marks), jnp.where(own, grad, shift))
        score_grad = (probs * slope).astype(jnp.bfloat16)
        value_grads.append(dot(probs.astype(jnp.bfloat16), grad))
        key_grads.append(dot(score_grad, query))
        turned = keys[:, head * HEAD : (head + 1) * HEAD].T
        query_grads.append(dot(turned, score_grad))
    first = head_lanes(keys.shape, 0)
    return (
        jnp.concatenate(query_grads, axis=0),
        jnp.where(first, key_grads[0], key_grads[1]),
        jnp.where(first, value_grads[0], value_grads[1]),
    )


def norm_back(weighted, unit, inverse):
    return inverse * (weighted - unit * (per_head(weighted * unit, None) * (1.0 / HEAD)))


def cross_back_kernel(
    query, text, text_value, raw_t, grad, out, log, gains, mark_q, mark_t,
    query_grad, raw_grad, value_grad, gain_sum, gate_sum,
):
    grad_q, grad_t, grad_v = attention_grads(
        query[...], text[...], mark_t[...], text_value[...], grad[...], out[...], log[...], mark_q[...]
    )
    query_grad[...] = grad_q.T
    value_grad[...] = grad_v.astype(jnp.bfloat16).T
    grad_t = grad_t.astype(jnp.bfloat16).astype(jnp.float32)
    unit, inverse = head_units(raw_t[...])
    gain_sum[...] = jnp.sum(grad_t * unit, axis=0, keepdims=True)
    raw_grad[...] = norm_back(grad_t * gains[2:3, :], unit, inverse).astype(jnp.bfloat16).T
    gate_sum[...] = jnp.sum(grad[...].astype(jnp.float32) * out[...], axis=0, keepdims=True)


def self_back_kernel(
    query, key, value, raw_q, raw_k, grad, out, log, cross_grad, cosine, sine, gains, mark_q, mark_k,
    query_grad, key_grad, value_grad, gain_sum,
):
    grad_q, grad_k, grad_v = attention_grads(
        query[...], key[...], mark_k[...], value[...], grad[...], out[...], log[...], mark_q[...]
    )
    value_grad[...] = grad_v.astype(jnp.bfloat16)
    cos, sin = cosine[...], sine[...]
    grad_q = (grad_q.T + cross_grad[...]) * ROOT
    for turn, raw, row, target in ((grad_q, raw_q, 0, query_grad), (grad_k, raw_k, 1, key_grad)):
        turn = turn.astype(jnp.bfloat16).astype(jnp.float32)
        turn = turn * cos - partner(turn) * sin
        unit, inverse = head_units(raw[...])
        gain_sum[row : row + 1, :] = jnp.sum(turn * unit, axis=0, keepdims=True)
        target[...] = norm_back(turn * gains[row : row + 1, :], unit, inverse).astype(jnp.bfloat16)


def pair_call(kernel, operands, outs, name, ties=(), micros=0):
    def spec(shape, cut):
        if cut is None:
            return pl.BlockSpec(shape, lambda pair: (0, 0))
        if cut == 1:
            return pl.BlockSpec((shape[0], LANES), lambda pair: (0, pair))
        return pl.BlockSpec((LANES, shape[1]), lambda pair: (pair, 0))

    width = outs[0][0][0] if outs[0][2] == 0 else outs[0][0][1]
    return pl.pallas_call(
        lambda *refs: kernel(*refs[: len(operands)], *refs[len(operands) + len(ties) :]),
        grid=(width // LANES,),
        in_specs=[spec(part.shape, cut) for part, cut in operands]
        + [pl.BlockSpec(memory_space=pl.ANY)] * len(ties),
        out_specs=[spec(shape, cut) for shape, _, cut in outs],
        out_shape=[jax.ShapeDtypeStruct(shape, kind) for shape, kind, _ in outs],
        compiler_params=pltpu.CompilerParams(vmem_limit_bytes=VMEM_LIMIT),
        cost_estimate=cost_of(micros),
        name=name,
    )(*[part for part, _ in operands], *ties)
def inverse_rms(values):
    return lax.rsqrt(jnp.mean(values * values, axis=-1, keepdims=True) + EPS)


def row_norm_back(weighted, unit, inverse):
    return inverse * (weighted - unit * jnp.mean(weighted * unit, axis=-1, keepdims=True))


def per_row(table, segment):
    return jnp.where(segment == 0.0, table[0:1], jnp.where(segment == 1.0, table[1:2], table[2:3]))


def total_of(parts):
    upper, near, far = parts
    rows = far.shape[0]
    return (
        upper[:rows].astype(jnp.float32) + near[:rows].astype(jnp.float32) + far[...].astype(jnp.float32)
    )


def segment_sums(member, values):
    high = values.astype(jnp.bfloat16)
    low = (values - high.astype(jnp.float32)).astype(jnp.bfloat16)
    return dot(member, high) + dot(member, low)


def tables_kernel(here, lens, segments, cosine, sine, mark_q, mark_k, mark_t, segment, member):
    rows = segments.shape[1]
    ids = segments[...]
    first = jnp.sum((ids < 1).astype(jnp.float32))
    second = jnp.sum((ids < 2).astype(jnp.float32))
    lane = lane_index((rows, LANES))
    half = HEAD // 2
    rate = jnp.exp((lane % half).astype(jnp.float32) * (-2.0 * math.log(10000.0) / HEAD))
    within = lane % HEAD
    for block, code in enumerate(ROW_ORDER):
        source = here[0] ^ code
        line = segments[pl.ds(source, 1), :].astype(jnp.float32)
        label = jnp.broadcast_to(line, (rows, rows)).T
        start = jnp.where(label == 0.0, 0.0, jnp.where(label == 1.0, first, second))
        token = (lax.broadcasted_iota(jnp.int32, (rows, LANES), 0) + source * rows).astype(jnp.float32)
        angle = (token - start) * rate
        index = slice(block * rows, (block + 1) * rows)
        cosine[index, :] = jnp.cos(angle)
        sine[index, :] = jnp.where(within < half, -1.0, 1.0) * jnp.sin(angle)
        same = ((label == within.astype(jnp.float32)) & (within < SEGS)).astype(jnp.float32)
        shut = (within == SEGS).astype(jnp.float32)
        ones = ((within >= SEGS) & (within < SEGS + 3)).astype(jnp.float32)
        mark_q[index, :] = (SHUT * same - SHUT * shut).astype(jnp.bfloat16)
        mark_k[index, :] = (same + ones).astype(jnp.bfloat16)
        if block == 0:
            segment[...] = label
            member[...] = (
                lax.broadcasted_iota(jnp.int32, (8, rows), 0).astype(jnp.float32) == line
            ).astype(jnp.bfloat16)
    for group in range(SEGS):
        lane = lane_index((TXT, LANES)) % HEAD
        row = lax.broadcasted_iota(jnp.int32, (TXT, LANES), 0)
        inside = ((lane == group) & (row < lens[group])).astype(jnp.float32)
        ones = ((lane >= SEGS) & (lane < SEGS + 3)).astype(jnp.float32)
        mark_t[group * TXT : (group + 1) * TXT, :] = (inside + ones).astype(jnp.bfloat16)


def text_kernel(captions, key_weight, value_weight, raw_out, value_out, raw_sum, value_sum):
    step = pl.program_id(0)

    @pl.when(step == 0)
    def _():
        raw_sum[...] = dot(captions[...], key_weight[...])
        value_sum[...] = dot(captions[...], value_weight[...])

    @pl.when(step > 0)
    def _():
        raw_sum[...] += dot(captions[...], key_weight[...])
        value_sum[...] += dot(captions[...], value_weight[...])

    @pl.when(step == pl.num_programs(0) - 1)
    def _():
        raw_out[...] = raw_sum[...]
        value_out[...] = value_sum[...].astype(jnp.bfloat16)


def text_call(captions, key_weight, value_weight):
    rows, depth = captions.shape
    columns = key_weight.shape[1]
    tile = depth // 4
    return pl.pallas_call(
        text_kernel,
        grid=(depth // tile,),
        in_specs=[
            pl.BlockSpec((rows, tile), lambda step: (0, step)),
            pl.BlockSpec((tile, columns), lambda step: (step, 0)),
            pl.BlockSpec((tile, columns), lambda step: (step, 0)),
        ],
        out_specs=[pl.BlockSpec((rows, columns), lambda step: (0, 0))] * 2,
        out_shape=[
            jax.ShapeDtypeStruct((rows, columns), jnp.float32),
            jax.ShapeDtypeStruct((rows, columns), jnp.bfloat16),
        ],
        scratch_shapes=[pltpu.VMEM((rows, columns), jnp.float32)] * 2,
        compiler_params=pltpu.CompilerParams(vmem_limit_bytes=VMEM_LIMIT),
        cost_estimate=NO_COST,
        name="text",
    )(captions, key_weight, value_weight)


def project_kernel(here, own, far, near, last, mods, gains, segment_q, query_w, key_w, value_w,
                   rows_out, raw_q, raw_k, value):
    table = mods[here[0]]
    rows = own.shape[0]
    for block, part in enumerate((own, far, near, last)):
        index = slice(block * rows, (block + 1) * rows)
        values = part[...].astype(jnp.float32)
        marks = segment_q[index, :].astype(jnp.float32)
        scale = jnp.where(
            marks[:, 0:1] > 0.0, table[0:1], jnp.where(marks[:, 1:2] > 0.0, table[1:2], table[2:3])
        )
        rows_out[index, :] = (
            values * inverse_rms(values) * gains[0:1] * (1.0 + scale)
        ).astype(jnp.bfloat16)
    raw_q[...] = dot(rows_out[...], query_w[...])
    raw_k[...] = dot(rows_out[...], key_w[...])
    value[...] = dot(rows_out[...], value_w[...]).astype(jnp.bfloat16)


def middle_kernel(here, block, upper, near, far, mods, gains, segment, attn_out, middle_out, rows_out):
    attn_sum = total_of((upper, near, far))
    label = segment[:, 0:1]
    factor = jnp.tanh(per_row(mods[here[0] ^ 1], label)) * gains[1:2]
    middle = block[...].astype(jnp.float32) + factor * (attn_sum * inverse_rms(attn_sum))
    attn_out[...] = attn_sum
    middle_out[...] = middle
    scale = per_row(mods[here[0] ^ 2], label)
    rows_out[...] = (middle * inverse_rms(middle) * gains[2:3] * (1.0 + scale)).astype(jnp.bfloat16)


def block_out_kernel(here, middle, upper, near, far, grad, mods, gains, segment, member,
                     block_out, grad_out, sums):
    ffn_sum = total_of((upper, near, far))
    inverse = inverse_rms(ffn_sum)
    unit = ffn_sum * inverse
    factor = jnp.tanh(per_row(mods[here[0] ^ 3], segment[:, 0:1])) * gains[3:4]
    block_out[...] = (middle[...] + factor * unit).astype(jnp.bfloat16)
    incoming = grad[...].astype(jnp.float32)
    grad_out[...] = row_norm_back(incoming * factor, unit, inverse).astype(jnp.bfloat16)
    sums[...] = segment_sums(member[...], incoming * unit)


def middle_back_kernel(here, middle, attn, upper, near, far, grad, mods, gains, segment, member,
                       middle_grad, attn_grad, ffn_sums, attn_sums):
    grad_in = total_of((upper, near, far))
    label = segment[:, 0:1]
    inverse = inverse_rms(middle[...])
    unit = middle[...] * inverse
    factor = gains[2:3] * (1.0 + per_row(mods[here[0] ^ 2], label))
    ffn_sums[...] = segment_sums(member[...], grad_in * unit)
    grad_middle = grad[...].astype(jnp.float32) + row_norm_back(grad_in * factor, unit, inverse)
    middle_grad[...] = grad_middle
    inverse = inverse_rms(attn[...])
    unit = attn[...] * inverse
    factor = jnp.tanh(per_row(mods[here[0] ^ 1], label)) * gains[1:2]
    attn_grad[...] = row_norm_back(grad_middle * factor, unit, inverse).astype(jnp.bfloat16)
    attn_sums[...] = segment_sums(member[...], grad_middle * unit)


def block_in_kernel(here, block, middle_grad, upper, near, far, mods, gains, segment, member,
                    in_grad, sums):
    grad_in = total_of((upper, near, far))
    values = block[...].astype(jnp.float32)
    inverse = inverse_rms(values)
    unit = values * inverse
    factor = gains[0:1] * (1.0 + per_row(mods[here[0]], segment[:, 0:1]))
    in_grad[...] = (
        middle_grad[...] + row_norm_back(grad_in * factor, unit, inverse)
    ).astype(jnp.bfloat16)
    sums[...] = segment_sums(member[...], grad_in * unit)


def sort_sums_kernel(here, *refs):
    names, kept, sent, held = refs[:4], refs[4], refs[5], refs[6]
    for name, part in enumerate(names):
        held[name] = part[...]
    for out, codes in ((kept, (0, 2)), (sent, (1, 3))):
        for half, code in enumerate(codes):
            out[half] = held[here[0] ^ code]


def pack_kernel(here, kept, near, far, part, gains, cond, head_gain, text_gain, gate_sum, gate, packed):
    total = (kept[0] + near[0] + far[...])[:SEGS]
    is_gate = (jnp.zeros(total.shape, jnp.int32) + here[0] % 2) == 1
    mod = part[...]
    bent = jnp.tanh(mod)
    factor = jnp.where(is_gate, bent, 1.0 + mod)
    slope = jnp.where(is_gate, 1.0 - bent * bent, 1.0)
    grad = total * slope * gains[pl.ds(here[0], 1), :]
    gain = jnp.sum(total * factor, axis=0, keepdims=True)
    gate_slope = 1.0 - gate[...] * gate[...]
    extras = jnp.concatenate(
        [head_gain[0:1], head_gain[1:2], text_gain[...], gate_sum[...] * gate_slope], axis=1
    )
    rows = [grad, cond[...].astype(jnp.float32), gain, extras]
    packed[...] = jnp.concatenate(rows, axis=0).astype(jnp.bfloat16)


def ada_kernel(dp, ours, theirs, ada_out, sums_out):
    grads = jnp.concatenate([ours[...], theirs[...]], axis=0)
    rows, width = grads.shape
    columns = ada_out.shape[0]
    share = LANES // columns
    start = pl.multiple_of(dp[0] // share * LANES, LANES)
    index = (slice(None), pl.ds(start, LANES))
    conds = jnp.concatenate([ours[index], theirs[index]], axis=0).astype(jnp.float32)
    conds = pltpu.roll(conds, (LANES - dp[0] % share * columns) % LANES, 1)
    conds = pltpu.roll(conds, rows - SEGS, 0)
    acts = conds / (1.0 + jnp.exp(-conds))
    row = lax.broadcasted_iota(jnp.int32, acts.shape, 0) % 8
    acts = jnp.where(row < SEGS, acts, 0.0).astype(jnp.bfloat16)
    ada_out[...] = dot(acts.astype(jnp.float32).T.astype(jnp.bfloat16), grads)[:columns]
    kind = lax.broadcasted_iota(jnp.int32, (8, rows), 0)
    member = lax.broadcasted_iota(jnp.int32, (8, rows), 1) % 8 == kind + 2 * SEGS
    sums_out[...] = dot(member.astype(jnp.float32).astype(jnp.bfloat16), grads)


def gains_kernel(heads, here, own, far, near, last, norm_out, head_out, gate_out):
    inner = heads * HEAD
    lane = lane_index((1, LANES))
    total = jnp.zeros((1, 3 * inner), jnp.float32)
    for code, part in zip(ROW_ORDER, (own, far, near, last)):
        source = here[0] ^ code
        norm_out[pl.ds(source, 1), :] = part[0:1, :]
        total = total + part[1:2, : 3 * inner]
        line = jnp.zeros((1, LANES), jnp.float32)
        for head in range(heads):
            start = 3 * inner + head * HEAD
            value = jnp.sum(part[1:2, start : start + HEAD], axis=1, keepdims=True)
            line = jnp.where(lane == head, value, line)
        gate_out[pl.ds(source, 1), :] = line
    for row in range(3):
        line = jnp.zeros((1, HEAD), jnp.float32)
        for head in range(heads):
            start = row * inner + head * HEAD
            line = line + total[:, start : start + HEAD]
        head_out[row : row + 1, :] = line


def shards(
    block_in,
    out_grad,
    condition,
    captions,
    caption_len,
    segment_ids,
    ada_weight,
    norm_gains,
    query_weight,
    key_weight,
    value_weight,
    head_gains,
    textkey_weight,
    textvalue_weight,
    cross_gate,
    out_weight,
    gate_weight,
    up_weight,
    down_weight,
):
    rows, width = block_in.shape
    length = segment_ids.shape[0]
    heads = cross_gate.shape[0]
    inner = heads * HEAD
    half_rows = length // 2
    position = lax.axis_index("tensor")
    spot = dp_spot(position)
    here = position.reshape(1)
    b16, f32 = jnp.bfloat16, jnp.float32

    blocks = gather_tensor(block_in)
    cond_rows = jnp.pad(condition, ((0, 0), (0, width - condition.shape[1])))
    own_act = jax.nn.silu(condition.astype(f32)).astype(b16)
    own_part = jnp.dot(own_act, ada_weight, preferred_element_type=f32)
    parts = gather_tensor(own_part)
    mods = jnp.stack([parts[ROW_ORDER.index(code)] for code in range(4)])

    cosine, sine, mark_q, mark_k, mark_t, segment, member = whole_call(
        tables_kernel,
        (here, caption_len),
        [segment_ids.reshape(length // rows, rows)],
        [((length, LANES), f32)] * 2
        + [((length, LANES), b16)] * 2
        + [((SEGS * TXT, LANES), b16), ((rows, LANES), f32), ((8, rows), b16)],
        "tables",
    )
    caption_flat = captions.reshape(-1, captions.shape[-1])
    texts = caption_flat.shape[0]
    raw_t, text_value = text_call(caption_flat, textkey_weight, textvalue_weight)
    attn_rows, raw_q, raw_k, value = whole_call(
        project_kernel,
        (here,),
        blocks + [mods, norm_gains, mark_q, query_weight, key_weight, value_weight],
        [((length, width), b16), ((length, inner), f32), ((length, inner), f32), ((length, inner), b16)],
        "project",
    )
    tanh_gate = jnp.tanh(cross_gate)
    gate_lanes = jnp.repeat(tanh_gate, HEAD)[None]
    gate_swapped = jnp.repeat(tanh_gate.reshape(-1, 2)[:, ::-1].reshape(-1), HEAD)[None]
    gains = jnp.tile(head_gains, (1, heads))
    query, key, text, mixed, self_out, cross_out, self_log, cross_log = pair_call(
        attend_kernel,
        [(raw_q, 1), (raw_k, 1), (value, 1), (raw_t, 1), (text_value, 1), (cosine, None), (sine, None)]
        + [(gains, 1), (gate_lanes, 1), (gate_swapped, 1), (mark_q, None), (mark_k, None), (mark_t, None)],
        [((length, inner), b16, 1)] * 2
        + [((texts, inner), b16, 1), ((length, inner), b16, 1)]
        + [((length, inner), f32, 1)] * 4,
        "attend",
    )

    def halves(product):
        return product(slice(0, half_rows)).astype(b16), product(slice(half_rows, None)).astype(b16)

    def all_of(block):
        return jnp.concatenate(gather_tensor(block), axis=0)

    upper, lower = halves(lambda part: jnp.dot(mixed[part], out_weight, preferred_element_type=f32))
    sums, sent = scatter_tensor(upper, lower)
    attn_rows_t = turned(attn_rows, (sent,))
    wide = ((rows, width), f32)
    narrow = ((rows, width), b16)
    totals = ((8, width), f32)
    attn_sum, middle, ffn_own = whole_call(
        middle_kernel,
        (here,),
        [block_in] + sums + [mods, norm_gains, segment],
        [wide, wide, narrow],
        "middle",
    )
    ffn_rows = all_of(ffn_own)
    gate_pre = jnp.dot(ffn_rows, gate_weight, preferred_element_type=f32)
    up_pre = jnp.dot(ffn_rows, up_weight, preferred_element_type=f32)
    sigmoid_gate = jax.nn.sigmoid(gate_pre)
    silu_gate = gate_pre * sigmoid_gate
    hidden = (silu_gate * up_pre).astype(b16)
    upper, lower = halves(lambda part: jnp.dot(hidden[part], down_weight, preferred_element_type=f32))
    sums, sent = scatter_tensor(upper, lower)
    ffn_rows_t = turned(ffn_rows, (sent,))
    block_out, grad_own, sum_gate_ffn = whole_call(
        block_out_kernel,
        (here,),
        [middle] + sums + [out_grad, mods, norm_gains, segment, member],
        [narrow, narrow, totals],
        "block_out",
    )

    grad_ffn = all_of(grad_own)
    grad_hidden = times_transpose(grad_ffn, down_weight)
    grad_gate = (
        grad_hidden * up_pre * sigmoid_gate * (1.0 + gate_pre * (1.0 - sigmoid_gate))
    ).astype(b16)
    grad_up = (grad_hidden * silu_gate).astype(b16)
    upper, lower = halves(
        lambda part: times_transpose(grad_gate[part], gate_weight)
        + times_transpose(grad_up[part], up_weight)
    )
    sums, sent = scatter_tensor(upper, lower)
    grad_ffn_t = turned(grad_ffn, (sent,))
    ffn_pairs = [(ffn_rows_t, [grad_gate, grad_up]), (grad_ffn_t, [hidden])]
    (halves_two,) = row_chunks(ffn_pairs, (2,), spot, ties=(sent,), micros=FFN_MICROS)
    ffn_passed = one_on(halves_two)
    grad_middle, grad_own, sum_scale_ffn, sum_gate_attn = whole_call(
        middle_back_kernel,
        (here,),
        [middle, attn_sum] + sums + [out_grad, mods, norm_gains, segment, member],
        [wide, narrow, totals, totals],
        "middle_back",
        micros=MIDDLE_MICROS,
    )

    ffn_one, ffn_three, ffn_kept = row_chunks(
        ffn_pairs, (1, 3, 0), spot, extra=ffn_passed, ties=(grad_own,), micros=FFN_NEXT_MICROS
    )
    grad_attn = gather_rows(grad_own, (ffn_kept,))
    grad_mixed = times_transpose(grad_attn, out_weight).astype(b16)
    cross_grad, text_grad, text_value_grad, text_gain, gate_sum = pair_call(
        cross_back_kernel,
        [(query, 1), (text, 1), (text_value, 1), (raw_t, 1), (grad_mixed, 1), (cross_out, 1)]
        + [(cross_log, 1), (gains, 1), (mark_q, None), (mark_t, None)],
        [((length, inner), f32, 1), ((inner, texts), b16, 0), ((inner, texts), b16, 0)]
        + [((1, inner), f32, 1)] * 2,
        "cross_back",
        micros=CROSS_MICROS,
    )
    text_lefts = [text_grad, text_value_grad]
    (halves_two,) = column_chunks(text_lefts, caption_flat, (2,), spot)
    text_passed = one_on(halves_two)
    query_grad, key_grad, value_grad, head_gain = pair_call(
        self_back_kernel,
        [(query, 1), (key, 1), (value, 1), (raw_q, 1), (raw_k, 1), (grad_mixed, 1), (self_out, 1)]
        + [(self_log, 1), (cross_grad, 1), (cosine, None), (sine, None), (gains, 1)]
        + [(mark_q, None), (mark_k, None)],
        [((length, inner), b16, 1)] * 3 + [((2, inner), f32, 1)],
        "self_back",
        (halves_two[0],),
        micros=SELF_MICROS,
    )

    hidden_cols = hidden.shape[1]
    block_rows = width // BLOCKS
    got = [by_slots(part) for part in to_neighbours(ffn_kept, ffn_one, ffn_three)]
    shape = (PAIR, block_rows, 3 * hidden_cols)
    ffn_stage = whole_call(
        ffn_second_kernel, (spot,), got, [(shape, b16)] * RING, "ffn_second", (query_grad,)
    )
    upper, lower = halves(
        lambda part: times_transpose(query_grad[part], query_weight)
        + times_transpose(key_grad[part], key_weight)
        + times_transpose(value_grad[part], value_weight)
    )
    sums, sent = scatter_tensor(upper, lower)
    text_one, text_three, text_kept = column_chunks(
        text_lefts, caption_flat, (1, 3, 0), spot, extra=text_passed, ties=(sent, ffn_stage[0])
    )
    in_grad, sum_scale_attn = whole_call(
        block_in_kernel,
        (here,),
        [block_in, grad_middle] + sums + [mods, norm_gains, segment, member],
        [narrow, totals],
        "block_in",
        (text_kept,),
        micros=BLOCK_IN_MICROS,
    )
    attn_pairs = [
        (attn_rows_t, [query_grad, key_grad, value_grad]),
        (turned(grad_attn, (sent,)), [mixed]),
    ]
    kept, sent = whole_call(
        ffn_third_kernel,
        (spot,),
        exchange(ffn_stage, "second"),
        [(shape[1:], b16)] * 2,
        "ffn_third",
        (text_kept,),
    )
    (halves_two,) = row_chunks(attn_pairs, (2,), spot, ties=(kept, in_grad))
    attn_passed = one_on(halves_two)
    attn_one, attn_three, attn_kept = row_chunks(
        attn_pairs, (1, 3, 0), spot, extra=attn_passed
    )
    gate_sum_out, up_sum_out, down_sum_out = whole_call(
        ffn_last_kernel,
        (),
        exchange([kept, sent], "z"),
        [((block_rows, hidden_cols), f32)] * 2 + [((hidden_cols, block_rows), f32)],
        "ffn_last",
    )
    text_rows = caption_flat.shape[1] // BLOCKS
    stacked = 2 * inner + 4 * inner // text_rows * block_rows
    text_stage = whole_call(
        text_second_kernel,
        (spot,),
        to_neighbours(text_kept, text_one, text_three),
        [((2 * inner, PAIR * text_rows), b16)] * RING,
        "text_second",
        (attn_kept,),
    )
    stage = whole_call(
        mixed_second_kernel,
        (spot,),
        list(text_stage)
        + [by_slots(part) for part in to_neighbours(attn_kept, attn_one, attn_three)],
        [((stacked, PAIR * text_rows), b16)] * RING,
        "mixed_second",
    )
    kept, sent = whole_call(
        functools.partial(mixed_third_kernel, 2 * inner, block_rows),
        (spot,),
        exchange(stage, "second"),
        [((stacked, text_rows), b16)] * 2,
        "mixed_third",
    )
    textkey_sum, textvalue_sum, query_sum, key_sum, value_sum, outw_sum = whole_call(
        mixed_last_kernel,
        (),
        exchange([kept, sent], "z"),
        [((text_rows, inner), f32)] * 2
        + [((block_rows, inner), f32)] * 3
        + [((inner, block_rows), f32)],
        "mixed_last",
    )

    kept, sent = whole_call(
        sort_sums_kernel,
        (here,),
        [sum_scale_attn, sum_gate_attn, sum_scale_ffn, sum_gate_ffn],
        [((2, 8, width), f32)] * 2,
        "sort_sums",
        scratch=[pltpu.VMEM((4, 8, width), f32)],
    )
    near = swap_core(sent)
    far = swap_chip(kept[1] + near[1])
    (packed,) = whole_call(
        pack_kernel,
        (here,),
        [kept, near, far, own_part, norm_gains, cond_rows]
        + [head_gain, text_gain, gate_sum, gate_lanes],
        [((8, width), b16)],
        "pack",
    )
    gathered = packed
    for axis, step in (("x", 1), ("x", 2), ("y", 1), ("y", 2)):
        gathered = jnp.concatenate([gathered, dp_permute(gathered, axis, step)], axis=0)
    ada_grad, rest = whole_call(
        ada_kernel,
        (lax.axis_index("dp").reshape(1),),
        exchange([gathered, gathered], "z"),
        [((condition.shape[1] // BLOCKS, width), f32), ((8, width), f32)],
        "ada",
    )
    rest = rest[:2]
    norm_grads, head_grads, crossgate = whole_call(
        functools.partial(gains_kernel, heads),
        (here,),
        gather_tensor(rest),
        [((4, width), f32), ((3, HEAD), f32), ((4, LANES), f32)],
        "gains",
    )
    crossgate_grad = crossgate[:, :heads].reshape(-1)
    return (
        block_out,
        in_grad,
        ada_grad,
        norm_grads,
        query_sum,
        key_sum,
        value_sum,
        head_grads,
        textkey_sum,
        textvalue_sum,
        crossgate_grad,
        outw_sum,
        gate_sum_out,
        up_sum_out,
        down_sum_out,
    )


def solution(mesh):
    return jax.shard_map(
        shards,
        mesh=mesh,
        in_specs=(
            P(("dp", "tensor"), None),
            P(("dp", "tensor"), None),
            P("dp", None),
            P("dp", None, None),
            P("dp"),
            P("dp"),
            P(None, "tensor"),
            P(),
            P(None, "tensor"),
            P(None, "tensor"),
            P(None, "tensor"),
            P(),
            P(None, "tensor"),
            P(None, "tensor"),
            P("tensor"),
            P("tensor", None),
            P(None, "tensor"),
            P(None, "tensor"),
            P("tensor", None),
        ),
        out_specs=(
            P(("dp", "tensor"), None),
            P(("dp", "tensor"), None),
            P("dp", "tensor"),
            P(),
            P("dp", "tensor"),
            P("dp", "tensor"),
            P("dp", "tensor"),
            P(),
            P("dp", "tensor"),
            P("dp", "tensor"),
            P(),
            P("tensor", "dp"),
            P("dp", "tensor"),
            P("dp", "tensor"),
            P("tensor", "dp"),
        ),
        check_vma=False,
    )
```

```python
import functools
import math

import jax
import jax.numpy as jnp
from jax import lax
from jax.experimental import pallas as pl
from jax.experimental.pallas import tpu as pltpu
from jax.sharding import PartitionSpec as P

HEAD = 64
HEADS = 24
TXT = 256
SEGS = 3
EPS = 1e-06
LANES = 2 * HEAD
SHUT = 256.0
ROOT = HEAD ** (-0.5)
VMEM_LIMIT = 50 * 2**20
NO_COST = pl.CostEstimate(flops=0, bytes_accessed=0, transcendentals=0)


def cost_of(micros):
    return pl.CostEstimate(flops=int(micros * 1e9), bytes_accessed=0, transcendentals=0)


SUM_ROWS = 6
CROSS_MICROS = 10
BLOCK_IN_MICROS = 10
FFN_MICROS = 3
FFN_NEXT_MICROS = 8
MIDDLE_MICROS = 10
SELF_MICROS = 0

RING = 4
PAIR = 2
BLOCKS = RING * PAIR * RING
SLOTS = BLOCKS // RING
SEND_ORDER = (2, 1, 3, 0)
CORE_SWAP = [(0, 1), (1, 0), (2, 3), (3, 2)]
CHIP_SWAP = [(0, 2), (2, 0), (1, 3), (3, 1)]
ROW_ORDER = (0, 2, 1, 3)

def dp_index(x, z, y):
    return (x * PAIR + z) * RING + y


def dp_perm(axis, step):
    pairs = []
    for x in range(RING):
        for z in range(PAIR):
            for y in range(RING):
                for tensor in range(2 * PAIR):
                    way = axis
                    if axis in ("first", "second"):
                        way = "x" if (tensor % 2 == 0) == (axis == "first") else "y"
                    target = {
                        "x": ((x + step) % RING, z, y),
                        "y": (x, z, (y + step) % RING),
                        "z": (x, (z + step) % PAIR, y),
                    }[way]
                    pairs.append(
                        (
                            dp_index(x, z, y) * 2 * PAIR + tensor,
                            dp_index(*target) * 2 * PAIR + tensor,
                        )
                    )
    return pairs


def dp_permute(values, axis, step):
    return lax.ppermute(values, ("dp", "tensor"), dp_perm(axis, step))


def dp_spot(position):
    index = lax.axis_index("dp")
    x, z, y = index // (RING * PAIR), index // RING % PAIR, index % RING
    core = position % 2
    return jnp.stack([jnp.where(core == 0, x, y), z, jnp.where(core == 0, y, x), core])


def swap_core(values):
    return lax.ppermute(values, "tensor", CORE_SWAP)


def swap_chip(values):
    return lax.ppermute(values, "tensor", CHIP_SWAP)


def times_transpose(left, right):
    return lax.dot_general(
        left, right, (((1,), (1,)), ((), ())), preferred_element_type=jnp.float32
    )


def gather_tensor(block):
    far = swap_chip(block)
    near = swap_core(block)
    return [block, far, near, swap_core(far)]


def join_kernel(own, far, both, far_out):
    rows = own.shape[0]
    both[:rows, :] = own[...]
    both[rows:, :] = far[...]
    far_out[...] = far[...]


def gather_rows(block, ties=()):
    rows, width = block.shape
    near = swap_core(block)
    upper, far = whole_call(
        join_kernel,
        (),
        [block, swap_chip(block)],
        [((2 * rows, width), block.dtype), ((rows, width), block.dtype)],
        "join",
        ties,
    )
    return jnp.concatenate([upper, near, swap_core(far)], axis=0)


def scatter_tensor(upper, lower):
    near = swap_core(lower)
    rows = upper.shape[0] // 2
    far = (upper[rows:].astype(jnp.float32) + near[rows:].astype(jnp.float32)).astype(near.dtype)
    return [upper, near, swap_chip(far)], far


def turn_kernel(source, target):
    target[...] = source[...].T


def turned(values, ties=()):
    tile = 512 if values.shape[1] % 512 == 0 else values.shape[1]
    return pl.pallas_call(
        lambda source, *rest: turn_kernel(source, rest[-1]),
        grid=(values.shape[1] // tile,),
        in_specs=[pl.BlockSpec((values.shape[0], tile), lambda step: (0, step))]
        + [pl.BlockSpec(memory_space=pl.ANY)] * len(ties),
        out_specs=pl.BlockSpec((tile, values.shape[0]), lambda step: (step, 0)),
        out_shape=jax.ShapeDtypeStruct(values.shape[::-1], values.dtype),
        compiler_params=pltpu.CompilerParams(vmem_limit_bytes=VMEM_LIMIT),
        cost_estimate=NO_COST,
    )(values, *ties)


def chunk_block(offset, slot, spot):
    first = (spot[0] + offset) % RING
    z, second = slot // RING, slot % RING
    x = jnp.where(spot[3] == 0, first, second)
    y = jnp.where(spot[3] == 0, second, first)
    return dp_index(x, z, y)


def offset_of_step(offsets, step):
    offset = offsets[-1]
    for place in range(len(offsets) - 1):
        offset = jnp.where(step == place, offsets[place], offset)
    return offset


def chunk_kernel(make, offsets, halves, extra, outs, held, sems):
    step = pl.program_id(0)
    first, second = halves

    def copies(place):
        slot = held.at[place % 2]
        if offsets[place] != 2:
            return [pltpu.make_async_copy(slot, outs[place], sems.at[place % 2, 0])]
        return [
            pltpu.make_async_copy(slot.at[half], out, sems.at[place % 2, way])
            for way, (half, out) in enumerate(zip((first, second), outs[place]))
        ]

    for place, offset in enumerate(offsets):

        @pl.when(step == place)
        def _(place=place, offset=offset):
            if place >= 2:
                for copy in copies(place - 2):
                    copy.wait()
            added = {1: (first, extra[0]), 3: (second, extra[1])}.get(offset) if extra else None
            make(held.at[place % 2], added)
            for copy in copies(place):
                copy.start()
            if place == len(offsets) - 1:
                for last in range(max(place - 1, 0), place + 1):
                    for copy in copies(last):
                        copy.wait()


def chunk_call(make, operands, specs, offsets, halves, shape, spot, extra, ties, name, micros):
    count = len(operands)
    pieces = []
    for offset in offsets:
        if offset == 2:
            pieces += [tuple(len(range(*s.indices(d))) for s, d in zip(h, shape)) for h in halves]
        else:
            pieces.append(shape)

    def kernel(spot_ref, *refs):
        inputs, extras = refs[:count], refs[count : count + len(extra)]
        outs = list(refs[-len(pieces) - 2 : -2])
        grouped = []
        for offset in offsets:
            grouped.append((outs.pop(0), outs.pop(0)) if offset == 2 else outs.pop(0))
        chunk_kernel(
            functools.partial(make, inputs), offsets, halves, extras, grouped, refs[-2], refs[-1]
        )

    found = pl.pallas_call(
        kernel,
        grid_spec=pltpu.PrefetchScalarGridSpec(
            num_scalar_prefetch=1,
            grid=(len(offsets),),
            in_specs=list(specs)
            + [pl.BlockSpec(part.shape, lambda step, spot: (0, 0)) for part in extra]
            + [pl.BlockSpec(memory_space=pl.ANY)] * len(ties),
            out_specs=[pl.BlockSpec(memory_space=pl.ANY)] * len(pieces),
            scratch_shapes=[
                pltpu.VMEM((2,) + shape, jnp.bfloat16),
                pltpu.SemaphoreType.DMA((2, 2)),
            ],
        ),
        out_shape=[jax.ShapeDtypeStruct(piece, jnp.bfloat16) for piece in pieces],
        compiler_params=pltpu.CompilerParams(vmem_limit_bytes=VMEM_LIMIT),
        cost_estimate=cost_of(micros),
        name=name,
    )(spot, *operands, *extra, *ties)
    found = list(found)
    return [
        (found.pop(0), found.pop(0)) if offset == 2 else found.pop(0) for offset in offsets
    ]


def make_rows(groups, inputs, slot, added):
    lefts, rights = inputs[: SLOTS * len(groups)], inputs[SLOTS * len(groups) :]
    column = place = 0
    for group, count in enumerate(groups):
        rows = jnp.concatenate(
            [left[0] for left in lefts[SLOTS * group : SLOTS * (group + 1)]], axis=0
        )
        for right in rights[place : place + count]:
            wide = right.shape[1]
            product = dot(rows, right[...])
            low, high = column, column
            if added is not None:
                low = min(max(column, added[0][1].start), column + wide)
                high = min(max(column, added[0][1].stop), column + wide)
            for start, stop in ((column, low), (low, high), (high, column + wide)):
                if start < stop:
                    part = product[:, start - column : stop - column]
                    if (start, stop) == (low, high):
                        base = added[0][1].start
                        part = part + added[1][:, start - base : stop - base].astype(jnp.float32)
                    slot[:, start:stop] = part.astype(jnp.bfloat16)
            column += wide
        place += count


def row_chunks(pairs, offsets, spot, extra=(), ties=(), micros=0):
    lefts = [left.reshape(BLOCKS, left.shape[0] // BLOCKS, left.shape[1]) for left, _ in pairs]
    rights = [right for _, group in pairs for right in group]
    total = sum(right.shape[1] for right in rights)
    specs, operands = [], []
    for left in lefts:
        for slot in range(SLOTS):
            specs.append(
                pl.BlockSpec(
                    (1,) + left.shape[1:],
                    lambda step, spot, slot=slot: (
                        chunk_block(offset_of_step(offsets, step), slot, spot),
                        0,
                        0,
                    ),
                )
            )
            operands.append(left)
    specs += [pl.BlockSpec(right.shape, lambda step, spot: (0, 0)) for right in rights]
    rows = SLOTS * lefts[0].shape[1]
    halves = [(slice(0, rows), slice(0, total // 2)), (slice(0, rows), slice(total // 2, total))]
    return chunk_call(
        functools.partial(make_rows, [len(group) for _, group in pairs]),
        operands + rights,
        specs,
        offsets,
        halves,
        (rows, total),
        spot,
        extra,
        ties,
        "row_chunks",
        micros,
    )


def make_columns(lefts, inputs, slot, added):
    whole = jnp.concatenate([right[...] for right in inputs[lefts:]], axis=1)
    row = 0
    for left in inputs[:lefts]:
        product = dot(left[...], whole)
        if added is not None and added[0][0].start == row:
            product = product + added[1][...].astype(jnp.float32)
        slot[row : row + left.shape[0], :] = product.astype(jnp.bfloat16)
        row += left.shape[0]


def column_chunks(lefts, right, offsets, spot, extra=(), ties=(), micros=0):
    rows = lefts[0].shape[0]
    depth, columns = right.shape
    specs = [pl.BlockSpec(left.shape, lambda step, spot: (0, 0)) for left in lefts]
    for slot in range(SLOTS):
        specs.append(
            pl.BlockSpec(
                (depth, columns // BLOCKS),
                lambda step, spot, slot=slot: (
                    0,
                    chunk_block(offset_of_step(offsets, step), slot, spot),
                ),
            )
        )
    lanes = columns // RING
    halves = [(slice(0, rows), slice(0, lanes)), (slice(rows, 2 * rows), slice(0, lanes))]
    return chunk_call(
        functools.partial(make_columns, len(lefts)),
        list(lefts) + [right] * SLOTS,
        specs,
        offsets,
        halves,
        (2 * rows, lanes),
        spot,
        extra,
        ties,
        "column_chunks",
        micros,
    )


def add_up(refs, index):
    total = refs[0][index].astype(jnp.float32)
    for ref in refs[1:]:
        total = total + ref[index].astype(jnp.float32)
    return total


def lane_slice(start, size):
    return (slice(None), pl.ds(pl.multiple_of(start * size, size), size))


def ffn_second_kernel(spot, *refs):
    parts, outs = refs[:-RING], refs[-RING:]
    for offset in range(RING):
        for z in range(PAIR):
            slot = z * RING + (spot[2] + offset) % RING
            outs[offset][z] = add_up(parts, slot).astype(jnp.bfloat16)


def ffn_third_kernel(spot, *refs):
    for out, z in ((refs[-2], spot[1]), (refs[-1], (spot[1] + 1) % PAIR)):
        out[...] = add_up(refs[:RING], z).astype(jnp.bfloat16)


def ffn_last_kernel(kept, got, gate_out, up_out, down_out):
    total = kept[...].astype(jnp.float32) + got[...].astype(jnp.float32)
    hidden = gate_out.shape[1]
    gate_out[...] = total[:, :hidden]
    up_out[...] = total[:, hidden : 2 * hidden]
    down_out[...] = total[:, 2 * hidden :].T


def text_second_kernel(spot, *refs):
    parts, outs = refs[:-RING], refs[-RING:]
    lanes = parts[0].shape[1] // SLOTS
    for offset in range(RING):
        for z in range(PAIR):
            slot = z * RING + (spot[2] + offset) % RING
            outs[offset][:, z * lanes : (z + 1) * lanes] = add_up(
                parts, lane_slice(slot, lanes)
            ).astype(jnp.bfloat16)


def text_third_kernel(spot, *refs):
    lanes = refs[-1].shape[1]
    for out, z in ((refs[-2], spot[1]), (refs[-1], (spot[1] + 1) % PAIR)):
        out[...] = add_up(refs[:RING], lane_slice(z, lanes)).astype(jnp.bfloat16)


def text_last_kernel(kept, got, textkey, textvalue):
    total = kept[...].astype(jnp.float32) + got[...].astype(jnp.float32)
    columns = textkey.shape[1]
    textkey[...] = total[:columns].T
    textvalue[...] = total[columns:].T


def attn_second_kernel(spot, *refs):
    parts, riders, outs = refs[: -RING - 1], refs[-RING - 1], refs[-RING:]
    rows = parts[0].shape[1]
    for offset in range(RING):
        for z in range(PAIR):
            slot = z * RING + (spot[2] + offset) % RING
            outs[offset][z * rows : (z + 1) * rows, :] = add_up(parts, slot).astype(jnp.bfloat16)
        outs[offset][PAIR * rows :, :] = riders[...]


def attn_third_kernel(spot, *refs):
    rows = refs[-1].shape[0]
    for out, z in ((refs[-2], spot[1]), (refs[-1], (spot[1] + 1) % PAIR)):
        index = (pl.ds(pl.multiple_of(z * rows, 16), rows), slice(None))
        out[...] = add_up(refs[:RING], index).astype(jnp.bfloat16)


def attn_last_kernel(kept, got, query, key, value, outw):
    total = kept[...].astype(jnp.float32) + got[...].astype(jnp.float32)
    columns = query.shape[1]
    for place, out in enumerate((query, key, value)):
        out[...] = total[:, place * columns : (place + 1) * columns]
    outw[...] = total[:, 3 * columns :].T


def whole_call(kernel, scalars, operands, outs, name, ties=(), scratch=(), micros=0):
    whole = pl.BlockSpec(memory_space=pltpu.VMEM)
    count = len(scalars) + len(operands)
    return pl.pallas_call(
        lambda *refs: kernel(*refs[:count], *refs[count + len(ties) :]),
        in_specs=[pl.BlockSpec(memory_space=pltpu.SMEM)] * len(scalars)
        + [whole] * len(operands)
        + [pl.BlockSpec(memory_space=pl.ANY)] * len(ties),
        out_specs=[whole] * len(outs),
        out_shape=[jax.ShapeDtypeStruct(shape, kind) for shape, kind in outs],
        scratch_shapes=list(scratch),
        compiler_params=pltpu.CompilerParams(vmem_limit_bytes=VMEM_LIMIT),
        cost_estimate=cost_of(micros),
        name=name,
    )(*scalars, *operands, *ties)


def exchange(chunks, axis):
    return [chunks[0]] + [
        dp_permute(chunks[step], axis, step) for step in range(1, len(chunks))
    ]


def one_on(halves):
    return dp_permute(halves[0], "first", 1), dp_permute(halves[1], "first", RING - 1)


def to_neighbours(own, ahead, behind):
    return [own, dp_permute(ahead, "first", 1), dp_permute(behind, "first", RING - 1)]


def by_slots(chunk):
    return chunk.reshape(SLOTS, chunk.shape[0] // SLOTS, chunk.shape[1])


def lane_index(shape):
    return lax.broadcasted_iota(jnp.int32, shape, 1)


def head_lanes(shape, head):
    lane = lane_index(shape)
    return (lane < HEAD) if head == 0 else (lane >= HEAD)


def per_head(values, reduce):
    first = head_lanes(values.shape, 0)
    left = jnp.sum(jnp.where(first, values, 0.0), axis=1, keepdims=True)
    right = jnp.sum(jnp.where(first, 0.0, values), axis=1, keepdims=True)
    return jnp.where(first, left, right)


def head_units(raw):
    inverse = lax.rsqrt(per_head(raw * raw, None) * (1.0 / HEAD) + EPS)
    return raw * inverse, inverse


def partner(values):
    lane = lane_index(values.shape)
    return jnp.where(
        lane % HEAD < HEAD // 2,
        pltpu.roll(values, LANES - HEAD // 2, 1),
        pltpu.roll(values, HEAD // 2, 1),
    )


def dot(left, right):
    return jnp.dot(left, right, preferred_element_type=jnp.float32)


def dot_t(left, right):
    return lax.dot_general(left, right, (((1,), (1,)), ((), ())), preferred_element_type=jnp.float32)


def attend_kernel(
    raw_q, raw_k, value, raw_t, text_value, cosine, sine, gains, gate, gate_swapped, mark_q, mark_k, mark_t,
    query_out, key_out, text_out, mixed_out, self_out, cross_out, self_log, cross_log,
):
    cos, sin = cosine[...], sine[...]
    unit = head_units(raw_q[...])[0] * gains[0:1, :]
    query = ((unit * cos + partner(unit) * sin).astype(jnp.bfloat16) * ROOT).astype(jnp.bfloat16)
    unit = head_units(raw_k[...])[0] * gains[1:2, :]
    key = (unit * cos + partner(unit) * sin).astype(jnp.bfloat16)
    text = (head_units(raw_t[...])[0] * gains[2:3, :]).astype(jnp.bfloat16)
    query_out[...] = query
    key_out[...] = key
    text_out[...] = text

    def attention(keys, marks, values):
        outs, sums = [], []
        for head in range(2):
            own = head_lanes(query.shape, head)
            own_keys = head_lanes(keys.shape, head)
            probe = jnp.where(own, query, mark_q[...])
            scores = dot_t(probe, jnp.where(own_keys, keys, marks))
            weights = jnp.exp(scores).astype(jnp.bfloat16)
            both = dot(weights, jnp.where(own_keys, values, jnp.ones_like(values)))
            outs.append(both)
        first = head_lanes(outs[0].shape, 0)
        product = jnp.where(first, outs[0], outs[1])
        total = jnp.where(first, outs[1], outs[0])
        return product / pltpu.roll(total, HEAD, 1), jnp.log(total)

    out, log = attention(key, mark_k[...], value[...])
    self_out[...] = out
    self_log[...] = log
    cross, log = attention(text, mark_t[...], text_value[...])
    cross_out[...] = cross
    cross_log[...] = log - jnp.log(gate_swapped[...])
    mixed_out[...] = (out + gate[...] * cross).astype(jnp.bfloat16)


def attention_grads(query, keys, marks, values, grad, out, log, mark_q):
    rows = grad.astype(jnp.float32)
    delta = per_head(rows * out, None)
    delta = pltpu.roll(delta, HEAD, 1)
    lane = lane_index(query.shape) % HEAD
    log_high = log.astype(jnp.bfloat16)
    log_low = (log - log_high.astype(jnp.float32)).astype(jnp.bfloat16)
    delta_high = delta.astype(jnp.bfloat16)
    delta_low = (delta - delta_high.astype(jnp.float32)).astype(jnp.bfloat16)
    zero = jnp.zeros_like(query)
    code = jnp.where(lane == 4, -log_high, jnp.where(lane == 5, -log_low, mark_q))
    shift = jnp.where(lane == 4, -delta_high, jnp.where(lane == 5, -delta_low, zero))
    key_grads, value_grads, query_grads = [], [], []
    for head in range(2):
        own = head_lanes(query.shape, head)
        own_keys = head_lanes(keys.shape, head)
        probe = jnp.where(own, query, code)
        probs = jnp.exp(dot_t(jnp.where(own_keys, keys, marks), probe))
        slope = dot_t(jnp.where(own_keys, values, marks), jnp.where(own, grad, shift))
        score_grad = (probs * slope).astype(jnp.bfloat16)
        value_grads.append(dot(probs.astype(jnp.bfloat16), grad))
        key_grads.append(dot(score_grad, query))
        turned = keys[:, head * HEAD : (head + 1) * HEAD].T
        query_grads.append(dot(turned, score_grad))
    first = head_lanes(keys.shape, 0)
    return (
        jnp.concatenate(query_grads, axis=0),
        jnp.where(first, key_grads[0], key_grads[1]),
        jnp.where(first, value_grads[0], value_grads[1]),
    )


def norm_back(weighted, unit, inverse):
    return inverse * (weighted - unit * (per_head(weighted * unit, None) * (1.0 / HEAD)))


def cross_back_kernel(
    query, text, text_value, raw_t, grad, out, log, gains, mark_q, mark_t,
    query_grad, raw_grad, value_grad, gain_sum, gate_sum,
):
    grad_q, grad_t, grad_v = attention_grads(
        query[...], text[...], mark_t[...], text_value[...], grad[...], out[...], log[...], mark_q[...]
    )
    query_grad[...] = grad_q.T
    value_grad[...] = grad_v.astype(jnp.bfloat16).T
    grad_t = grad_t.astype(jnp.bfloat16).astype(jnp.float32)
    unit, inverse = head_units(raw_t[...])
    gain_sum[...] = jnp.sum(grad_t * unit, axis=0, keepdims=True)
    raw_grad[...] = norm_back(grad_t * gains[2:3, :], unit, inverse).astype(jnp.bfloat16).T
    gate_sum[...] = jnp.sum(grad[...].astype(jnp.float32) * out[...], axis=0, keepdims=True)


def self_back_kernel(
    query, key, value, raw_q, raw_k, grad, out, log, cross_grad, cosine, sine, gains, mark_q, mark_k,
    query_grad, key_grad, value_grad, gain_sum,
):
    grad_q, grad_k, grad_v = attention_grads(
        query[...], key[...], mark_k[...], value[...], grad[...], out[...], log[...], mark_q[...]
    )
    value_grad[...] = grad_v.astype(jnp.bfloat16)
    cos, sin = cosine[...], sine[...]
    grad_q = (grad_q.T + cross_grad[...]) * ROOT
    for turn, raw, row, target in ((grad_q, raw_q, 0, query_grad), (grad_k, raw_k, 1, key_grad)):
        turn = turn.astype(jnp.bfloat16).astype(jnp.float32)
        turn = turn * cos - partner(turn) * sin
        unit, inverse = head_units(raw[...])
        gain_sum[row : row + 1, :] = jnp.sum(turn * unit, axis=0, keepdims=True)
        target[...] = norm_back(turn * gains[row : row + 1, :], unit, inverse).astype(jnp.bfloat16)


def pair_call(kernel, operands, outs, name, ties=(), micros=0):
    def spec(shape, cut):
        if cut is None:
            return pl.BlockSpec(shape, lambda pair: (0, 0))
        if cut == 1:
            return pl.BlockSpec((shape[0], LANES), lambda pair: (0, pair))
        return pl.BlockSpec((LANES, shape[1]), lambda pair: (pair, 0))

    width = outs[0][0][0] if outs[0][2] == 0 else outs[0][0][1]
    return pl.pallas_call(
        lambda *refs: kernel(*refs[: len(operands)], *refs[len(operands) + len(ties) :]),
        grid=(width // LANES,),
        in_specs=[spec(part.shape, cut) for part, cut in operands]
        + [pl.BlockSpec(memory_space=pl.ANY)] * len(ties),
        out_specs=[spec(shape, cut) for shape, _, cut in outs],
        out_shape=[jax.ShapeDtypeStruct(shape, kind) for shape, kind, _ in outs],
        compiler_params=pltpu.CompilerParams(vmem_limit_bytes=VMEM_LIMIT),
        cost_estimate=cost_of(micros),
        name=name,
    )(*[part for part, _ in operands], *ties)
def inverse_rms(values):
    return lax.rsqrt(jnp.mean(values * values, axis=-1, keepdims=True) + EPS)


def row_norm_back(weighted, unit, inverse):
    return inverse * (weighted - unit * jnp.mean(weighted * unit, axis=-1, keepdims=True))


def per_row(table, segment):
    return jnp.where(segment == 0.0, table[0:1], jnp.where(segment == 1.0, table[1:2], table[2:3]))


def total_of(parts):
    upper, near, far = parts
    rows = far.shape[0]
    return (
        upper[:rows].astype(jnp.float32) + near[:rows].astype(jnp.float32) + far[...].astype(jnp.float32)
    )


def segment_sums(member, values):
    high = values.astype(jnp.bfloat16)
    low = (values - high.astype(jnp.float32)).astype(jnp.bfloat16)
    return dot(member, high) + dot(member, low)


def tables_kernel(here, lens, segments, cosine, sine, mark_q, mark_k, mark_t, segment, member):
    rows = segments.shape[1]
    ids = segments[...]
    first = jnp.sum((ids < 1).astype(jnp.float32))
    second = jnp.sum((ids < 2).astype(jnp.float32))
    lane = lane_index((rows, LANES))
    half = HEAD // 2
    rate = jnp.exp((lane % half).astype(jnp.float32) * (-2.0 * math.log(10000.0) / HEAD))
    within = lane % HEAD
    for block, code in enumerate(ROW_ORDER):
        source = here[0] ^ code
        line = segments[pl.ds(source, 1), :].astype(jnp.float32)
        label = jnp.broadcast_to(line, (rows, rows)).T
        start = jnp.where(label == 0.0, 0.0, jnp.where(label == 1.0, first, second))
        token = (lax.broadcasted_iota(jnp.int32, (rows, LANES), 0) + source * rows).astype(jnp.float32)
        angle = (token - start) * rate
        index = slice(block * rows, (block + 1) * rows)
        cosine[index, :] = jnp.cos(angle)
        sine[index, :] = jnp.where(within < half, -1.0, 1.0) * jnp.sin(angle)
        same = ((label == within.astype(jnp.float32)) & (within < SEGS)).astype(jnp.float32)
        shut = (within == SEGS).astype(jnp.float32)
        ones = ((within >= SEGS) & (within < SEGS + 3)).astype(jnp.float32)
        mark_q[index, :] = (SHUT * same - SHUT * shut).astype(jnp.bfloat16)
        mark_k[index, :] = (same + ones).astype(jnp.bfloat16)
        if block == 0:
            segment[...] = label
            member[...] = (
                lax.broadcasted_iota(jnp.int32, (8, rows), 0).astype(jnp.float32) == line
            ).astype(jnp.bfloat16)
    for group in range(SEGS):
        lane = lane_index((TXT, LANES)) % HEAD
        row = lax.broadcasted_iota(jnp.int32, (TXT, LANES), 0)
        inside = ((lane == group) & (row < lens[group])).astype(jnp.float32)
        ones = ((lane >= SEGS) & (lane < SEGS + 3)).astype(jnp.float32)
        mark_t[group * TXT : (group + 1) * TXT, :] = (inside + ones).astype(jnp.bfloat16)


def text_kernel(captions, key_weight, value_weight, raw_out, value_out, raw_sum, value_sum):
    step = pl.program_id(0)

    @pl.when(step == 0)
    def _():
        raw_sum[...] = dot(captions[...], key_weight[...])
        value_sum[...] = dot(captions[...], value_weight[...])

    @pl.when(step > 0)
    def _():
        raw_sum[...] += dot(captions[...], key_weight[...])
        value_sum[...] += dot(captions[...], value_weight[...])

    @pl.when(step == pl.num_programs(0) - 1)
    def _():
        raw_out[...] = raw_sum[...]
        value_out[...] = value_sum[...].astype(jnp.bfloat16)


def text_call(captions, key_weight, value_weight):
    rows, depth = captions.shape
    columns = key_weight.shape[1]
    tile = depth // 4
    return pl.pallas_call(
        text_kernel,
        grid=(depth // tile,),
        in_specs=[
            pl.BlockSpec((rows, tile), lambda step: (0, step)),
            pl.BlockSpec((tile, columns), lambda step: (step, 0)),
            pl.BlockSpec((tile, columns), lambda step: (step, 0)),
        ],
        out_specs=[pl.BlockSpec((rows, columns), lambda step: (0, 0))] * 2,
        out_shape=[
            jax.ShapeDtypeStruct((rows, columns), jnp.float32),
            jax.ShapeDtypeStruct((rows, columns), jnp.bfloat16),
        ],
        scratch_shapes=[pltpu.VMEM((rows, columns), jnp.float32)] * 2,
        compiler_params=pltpu.CompilerParams(vmem_limit_bytes=VMEM_LIMIT),
        cost_estimate=cost_of(9),
        name="text",
    )(captions, key_weight, value_weight)


def project_kernel(here, own, far, near, last, mods, gains, segment_q, query_w, key_w, value_w,
                   rows_out, raw_q, raw_k, value):
    table = mods[here[0]]
    rows = own.shape[0]
    for block, part in enumerate((own, far, near, last)):
        index = slice(block * rows, (block + 1) * rows)
        values = part[...].astype(jnp.float32)
        marks = segment_q[index, :].astype(jnp.float32)
        scale = jnp.where(
            marks[:, 0:1] > 0.0, table[0:1], jnp.where(marks[:, 1:2] > 0.0, table[1:2], table[2:3])
        )
        rows_out[index, :] = (
            values * inverse_rms(values) * gains[0:1] * (1.0 + scale)
        ).astype(jnp.bfloat16)
    raw_q[...] = dot(rows_out[...], query_w[...])
    raw_k[...] = dot(rows_out[...], key_w[...])
    value[...] = dot(rows_out[...], value_w[...]).astype(jnp.bfloat16)


def middle_kernel(here, block, upper, near, far, mods, gains, segment, attn_out, middle_out, rows_out):
    attn_sum = total_of((upper, near, far))
    label = segment[:, 0:1]
    factor = jnp.tanh(per_row(mods[here[0] ^ 1], label)) * gains[1:2]
    middle = block[...].astype(jnp.float32) + factor * (attn_sum * inverse_rms(attn_sum))
    attn_out[...] = attn_sum
    middle_out[...] = middle
    scale = per_row(mods[here[0] ^ 2], label)
    rows_out[...] = (middle * inverse_rms(middle) * gains[2:3] * (1.0 + scale)).astype(jnp.bfloat16)


def block_out_kernel(here, middle, upper, near, far, grad, mods, gains, segment, member,
                     block_out, grad_out, sums):
    ffn_sum = total_of((upper, near, far))
    inverse = inverse_rms(ffn_sum)
    unit = ffn_sum * inverse
    factor = jnp.tanh(per_row(mods[here[0] ^ 3], segment[:, 0:1])) * gains[3:4]
    block_out[...] = (middle[...] + factor * unit).astype(jnp.bfloat16)
    incoming = grad[...].astype(jnp.float32)
    grad_out[...] = row_norm_back(incoming * factor, unit, inverse).astype(jnp.bfloat16)
    sums[...] = segment_sums(member[...], incoming * unit)


def middle_back_kernel(here, middle, attn, upper, near, far, grad, mods, gains, segment, member,
                       middle_grad, attn_grad, ffn_sums, attn_sums):
    grad_in = total_of((upper, near, far))
    label = segment[:, 0:1]
    inverse = inverse_rms(middle[...])
    unit = middle[...] * inverse
    factor = gains[2:3] * (1.0 + per_row(mods[here[0] ^ 2], label))
    ffn_sums[...] = segment_sums(member[...], grad_in * unit)
    grad_middle = grad[...].astype(jnp.float32) + row_norm_back(grad_in * factor, unit, inverse)
    middle_grad[...] = grad_middle
    inverse = inverse_rms(attn[...])
    unit = attn[...] * inverse
    factor = jnp.tanh(per_row(mods[here[0] ^ 1], label)) * gains[1:2]
    attn_grad[...] = row_norm_back(grad_middle * factor, unit, inverse).astype(jnp.bfloat16)
    attn_sums[...] = segment_sums(member[...], grad_middle * unit)


def block_in_kernel(here, block, middle_grad, upper, near, far, mods, gains, segment, member,
                    in_grad, sums):
    grad_in = total_of((upper, near, far))
    values = block[...].astype(jnp.float32)
    inverse = inverse_rms(values)
    unit = values * inverse
    factor = gains[0:1] * (1.0 + per_row(mods[here[0]], segment[:, 0:1]))
    in_grad[...] = (
        middle_grad[...] + row_norm_back(grad_in * factor, unit, inverse)
    ).astype(jnp.bfloat16)
    sums[...] = segment_sums(member[...], grad_in * unit)


def stack_sums_kernel(here, first, second, third, fourth, head_gain, text_gain, gate_sum, gate, out):
    width = out.shape[1]
    heads = jnp.concatenate([head_gain[0:1], head_gain[1:2], text_gain[...]], axis=1)
    inner = heads.shape[1] // 3
    gates = gate_sum[...] * (1.0 - gate[...] * gate[...])
    gates = jnp.concatenate([gates, jnp.zeros((1, width - inner), jnp.float32)], axis=1)
    lane = lane_index(gates.shape)
    moved = jnp.zeros_like(gates)
    for position in range(4):
        turn = pltpu.roll(gates, position * inner, 1) if position else gates
        moved = jnp.where((lane // inner == position) & (here[0] == position), turn, moved)
    out[...] = jnp.concatenate(
        [part[0:SEGS] for part in (first, second, third, fourth)]
        + [
            jnp.concatenate([heads, jnp.zeros((1, width - 3 * inner), jnp.float32)], axis=1),
            moved,
            jnp.zeros((2, width), jnp.float32),
        ],
        axis=0,
    )


def pack_kernel(here, own, far, near, last, mods, gains, cond, packed):
    total = own[...] + far[...] + near[...] + last[...]
    grad = jnp.zeros((SEGS, total.shape[1]), jnp.float32)
    rows = []
    for name in range(4):
        part = total[name * SEGS : (name + 1) * SEGS]
        mod = mods[here[0] ^ name]
        gain = gains[name : name + 1]
        if name % 2 == 1:
            factor = jnp.tanh(mod)
            slope = 1.0 - factor * factor
        else:
            factor = 1.0 + mod
            slope = jnp.ones_like(mod)
        rows.append(jnp.sum(part * factor, axis=0, keepdims=True))
        mine = (jnp.zeros(part.shape, jnp.int32) + here[0]) == name
        grad = jnp.where(mine, part * slope * gain, grad)
    rows.append(total[4 * SEGS : 4 * SEGS + 2])
    rows = jnp.concatenate(rows, axis=0)
    high = rows.astype(jnp.bfloat16).astype(jnp.float32)
    pad = jnp.zeros((packed.shape[0] - 2 * SEGS - 2 * SUM_ROWS, total.shape[1]), jnp.float32)
    packed[...] = jnp.concatenate(
        [grad, cond[...].astype(jnp.float32), high, rows - high, pad], axis=0
    ).astype(jnp.bfloat16)


def rider_rows(count):
    return -(-(2 * SEGS * count + 2 * SUM_ROWS) // 16) * 16


def merge_kernel(count, ours, theirs, out):
    first, second = ours[...].astype(jnp.float32), theirs[...].astype(jnp.float32)
    wide = SEGS * count
    start = 2 * wide
    sums = (
        first[start : start + SUM_ROWS]
        + first[start + SUM_ROWS : start + 2 * SUM_ROWS]
        + second[start : start + SUM_ROWS]
        + second[start + SUM_ROWS : start + 2 * SUM_ROWS]
    )
    high = sums.astype(jnp.bfloat16).astype(jnp.float32)
    pieces = [first[:wide], second[:wide], first[wide:start], second[wide:start], high, sums - high]
    rest = out.shape[0] - 4 * wide - 2 * SUM_ROWS
    if rest:
        pieces.append(jnp.zeros((rest, first.shape[1]), jnp.float32))
    out[...] = jnp.concatenate(pieces, axis=0).astype(jnp.bfloat16)


def ada_kernel(count, heads, dp, own, *refs):
    parts = (own,) + refs[:3]
    ada_out, norm_out, head_out, gate_out = refs[3:]
    wide = SEGS * count
    base = own.shape[0] - rider_rows(count)
    columns = ada_out.shape[0]
    share = LANES // columns
    start = pl.multiple_of(dp[0] // share * LANES, LANES)
    grads, conds = [], []
    sums = jnp.zeros((SUM_ROWS, own.shape[1]), jnp.float32)
    for part in parts:
        rows = part[base:, :].astype(jnp.float32)
        grads.append(rows[:wide])
        conds.append(part[base:, pl.ds(start, LANES)].astype(jnp.float32)[wide : 2 * wide])
        for half in range(2):
            place = 2 * wide + half * SUM_ROWS
            sums = sums + rows[place : place + SUM_ROWS]
    conds = jnp.concatenate(conds, axis=0)
    conds = pltpu.roll(conds, (LANES - dp[0] % share * columns) % LANES, 1)
    acts = conds / (1.0 + jnp.exp(-conds))
    ada_out[...] = dot(
        acts.astype(jnp.bfloat16).astype(jnp.float32).T.astype(jnp.bfloat16),
        jnp.concatenate(grads, axis=0).astype(jnp.bfloat16),
    )[:columns]
    norm_out[...] = sums[:4]
    inner = heads * HEAD
    for row in range(3):
        line = jnp.zeros((1, HEAD), jnp.float32)
        for head in range(heads):
            place = row * inner + head * HEAD
            line = line + sums[4:5, place : place + HEAD]
        head_out[row : row + 1, :] = line
    lane = lane_index((1, LANES))
    line = jnp.zeros((1, LANES), jnp.float32)
    for head in range(HEADS):
        value = jnp.sum(sums[5:6, head * HEAD : (head + 1) * HEAD], axis=1, keepdims=True)
        line = jnp.where(lane == head, value, line)
    gate_out[...] = line


def shards(
    block_in,
    out_grad,
    condition,
    captions,
    caption_len,
    segment_ids,
    ada_weight,
    norm_gains,
    query_weight,
    key_weight,
    value_weight,
    head_gains,
    textkey_weight,
    textvalue_weight,
    cross_gate,
    out_weight,
    gate_weight,
    up_weight,
    down_weight,
):
    rows, width = block_in.shape
    length = segment_ids.shape[0]
    heads = cross_gate.shape[0]
    inner = heads * HEAD
    half_rows = length // 2
    position = lax.axis_index("tensor")
    spot = dp_spot(position)
    here = position.reshape(1)
    b16, f32 = jnp.bfloat16, jnp.float32

    blocks = gather_tensor(block_in)
    cond_rows = jnp.pad(condition, ((0, 0), (0, width - condition.shape[1])))
    own_act = jax.nn.silu(condition.astype(f32)).astype(b16)
    own_part = jnp.dot(own_act, ada_weight, preferred_element_type=f32)
    parts = gather_tensor(own_part)
    mods = jnp.stack([parts[ROW_ORDER.index(code)] for code in range(4)])

    cosine, sine, mark_q, mark_k, mark_t, segment, member = whole_call(
        tables_kernel,
        (here, caption_len),
        [segment_ids.reshape(length // rows, rows)],
        [((length, LANES), f32)] * 2
        + [((length, LANES), b16)] * 2
        + [((SEGS * TXT, LANES), b16), ((rows, LANES), f32), ((8, rows), b16)],
        "tables",
        micros=2,
    )
    caption_flat = captions.reshape(-1, captions.shape[-1])
    texts = caption_flat.shape[0]
    raw_t, text_value = text_call(caption_flat, textkey_weight, textvalue_weight)
    attn_rows, raw_q, raw_k, value = whole_call(
        project_kernel,
        (here,),
        blocks + [mods, norm_gains, mark_q, query_weight, key_weight, value_weight],
        [((length, width), b16), ((length, inner), f32), ((length, inner), f32), ((length, inner), b16)],
        "project",
        micros=6,
    )
    tanh_gate = jnp.tanh(cross_gate)
    gate_lanes = jnp.repeat(tanh_gate, HEAD)[None]
    gate_swapped = jnp.repeat(tanh_gate.reshape(-1, 2)[:, ::-1].reshape(-1), HEAD)[None]
    gains = jnp.tile(head_gains, (1, heads))
    query, key, text, mixed, self_out, cross_out, self_log, cross_log = pair_call(
        attend_kernel,
        [(raw_q, 1), (raw_k, 1), (value, 1), (raw_t, 1), (text_value, 1), (cosine, None), (sine, None)]
        + [(gains, 1), (gate_lanes, 1), (gate_swapped, 1), (mark_q, None), (mark_k, None), (mark_t, None)],
        [((length, inner), b16, 1)] * 2
        + [((texts, inner), b16, 1), ((length, inner), b16, 1)]
        + [((length, inner), f32, 1)] * 4,
        "attend",
        micros=11,
    )

    def halves(product):
        return product(slice(0, half_rows)).astype(b16), product(slice(half_rows, None)).astype(b16)

    def all_of(block):
        return jnp.concatenate(gather_tensor(block), axis=0)

    upper, lower = halves(lambda part: jnp.dot(mixed[part], out_weight, preferred_element_type=f32))
    sums, sent = scatter_tensor(upper, lower)
    attn_rows_t = turned(attn_rows, (sent,))
    wide = ((rows, width), f32)
    narrow = ((rows, width), b16)
    totals = ((8, width), f32)
    attn_sum, middle, ffn_own = whole_call(
        middle_kernel,
        (here,),
        [block_in] + sums + [mods, norm_gains, segment],
        [wide, wide, narrow],
        "middle",
    )
    ffn_rows = all_of(ffn_own)
    gate_pre = jnp.dot(ffn_rows, gate_weight, preferred_element_type=f32)
    up_pre = jnp.dot(ffn_rows, up_weight, preferred_element_type=f32)
    sigmoid_gate = jax.nn.sigmoid(gate_pre)
    silu_gate = gate_pre * sigmoid_gate
    hidden = (silu_gate * up_pre).astype(b16)
    upper, lower = halves(lambda part: jnp.dot(hidden[part], down_weight, preferred_element_type=f32))
    sums, sent = scatter_tensor(upper, lower)
    ffn_rows_t = turned(ffn_rows, (sent,))
    block_out, grad_own, sum_gate_ffn = whole_call(
        block_out_kernel,
        (here,),
        [middle] + sums + [out_grad, mods, norm_gains, segment, member],
        [narrow, narrow, totals],
        "block_out",
    )

    grad_ffn = all_of(grad_own)
    grad_hidden = times_transpose(grad_ffn, down_weight)
    grad_gate = (
        grad_hidden * up_pre * sigmoid_gate * (1.0 + gate_pre * (1.0 - sigmoid_gate))
    ).astype(b16)
    grad_up = (grad_hidden * silu_gate).astype(b16)
    upper, lower = halves(
        lambda part: times_transpose(grad_gate[part], gate_weight)
        + times_transpose(grad_up[part], up_weight)
    )
    sums, sent = scatter_tensor(upper, lower)
    grad_ffn_t = turned(grad_ffn, (sent,))
    ffn_pairs = [(ffn_rows_t, [grad_gate, grad_up]), (grad_ffn_t, [hidden])]
    (halves_two,) = row_chunks(ffn_pairs, (2,), spot, ties=(sent,), micros=FFN_MICROS)
    ffn_passed = one_on(halves_two)
    grad_middle, grad_own, sum_scale_ffn, sum_gate_attn = whole_call(
        middle_back_kernel,
        (here,),
        [middle, attn_sum] + sums + [out_grad, mods, norm_gains, segment, member],
        [wide, narrow, totals, totals],
        "middle_back",
        micros=MIDDLE_MICROS,
    )

    ffn_one, ffn_three, ffn_kept = row_chunks(
        ffn_pairs, (1, 3, 0), spot, extra=ffn_passed, ties=(grad_own,), micros=FFN_NEXT_MICROS
    )
    grad_attn = gather_rows(grad_own, (ffn_kept,))
    grad_mixed = times_transpose(grad_attn, out_weight).astype(b16)
    cross_grad, text_grad, text_value_grad, text_gain, gate_sum = pair_call(
        cross_back_kernel,
        [(query, 1), (text, 1), (text_value, 1), (raw_t, 1), (grad_mixed, 1), (cross_out, 1)]
        + [(cross_log, 1), (gains, 1), (mark_q, None), (mark_t, None)],
        [((length, inner), f32, 1), ((inner, texts), b16, 0), ((inner, texts), b16, 0)]
        + [((1, inner), f32, 1)] * 2,
        "cross_back",
        micros=CROSS_MICROS,
    )
    text_lefts = [text_grad, text_value_grad]
    (halves_two,) = column_chunks(text_lefts, caption_flat, (2,), spot)
    text_passed = one_on(halves_two)
    query_grad, key_grad, value_grad, head_gain = pair_call(
        self_back_kernel,
        [(query, 1), (key, 1), (value, 1), (raw_q, 1), (raw_k, 1), (grad_mixed, 1), (self_out, 1)]
        + [(self_log, 1), (cross_grad, 1), (cosine, None), (sine, None), (gains, 1)]
        + [(mark_q, None), (mark_k, None)],
        [((length, inner), b16, 1)] * 3 + [((2, inner), f32, 1)],
        "self_back",
        (halves_two[0],),
        micros=SELF_MICROS,
    )

    hidden_cols = hidden.shape[1]
    block_rows = width // BLOCKS
    got = [by_slots(part) for part in to_neighbours(ffn_kept, ffn_one, ffn_three)]
    shape = (PAIR, block_rows, 3 * hidden_cols)
    ffn_stage = whole_call(
        ffn_second_kernel, (spot,), got, [(shape, b16)] * RING, "ffn_second", (query_grad,)
    )
    upper, lower = halves(
        lambda part: times_transpose(query_grad[part], query_weight)
        + times_transpose(key_grad[part], key_weight)
        + times_transpose(value_grad[part], value_weight)
    )
    sums, sent = scatter_tensor(upper, lower)
    text_one, text_three, text_kept = column_chunks(
        text_lefts, caption_flat, (1, 3, 0), spot, extra=text_passed, ties=(sent, ffn_stage[0])
    )
    in_grad, sum_scale_attn = whole_call(
        block_in_kernel,
        (here,),
        [block_in, grad_middle] + sums + [mods, norm_gains, segment, member],
        [narrow, totals],
        "block_in",
        (text_kept,),
        micros=BLOCK_IN_MICROS,
    )
    attn_pairs = [
        (attn_rows_t, [query_grad, key_grad, value_grad]),
        (turned(grad_attn, (sent,)), [mixed]),
    ]
    kept, sent = whole_call(
        ffn_third_kernel,
        (spot,),
        exchange(ffn_stage, "second"),
        [(shape[1:], b16)] * 2,
        "ffn_third",
        (text_kept,),
    )
    gate_sum_out, up_sum_out, down_sum_out = whole_call(
        ffn_last_kernel,
        (),
        exchange([kept, sent], "z"),
        [((block_rows, hidden_cols), f32)] * 2 + [((hidden_cols, block_rows), f32)],
        "ffn_last",
    )
    (halves_two,) = row_chunks(attn_pairs, (2,), spot, ties=(kept, text_kept))
    attn_passed = one_on(halves_two)
    (stacked,) = whole_call(
        stack_sums_kernel,
        (here,),
        [sum_scale_attn, sum_gate_attn, sum_scale_ffn, sum_gate_ffn]
        + [head_gain, text_gain, gate_sum, gate_lanes],
        [((16, width), f32)],
        "stack_sums",
    )
    (riders,) = whole_call(
        pack_kernel,
        (here,),
        gather_tensor(stacked) + [mods, norm_gains, cond_rows],
        [((rider_rows(1), width), b16)],
        "pack",
    )
    count = 1
    held = []
    for axis, step in (("z", 1), ("first", 1), ("first", 2)):
        (riders,) = whole_call(
            functools.partial(merge_kernel, count),
            (),
            [riders, dp_permute(riders, axis, step)],
            [((rider_rows(2 * count), width), b16)],
            "merge",
        )
        held.append(riders)
        count *= 2
    attn_one, attn_three, attn_kept = row_chunks(
        attn_pairs, (1, 3, 0), spot, extra=attn_passed, ties=(held[0],), micros=7
    )


    text_rows = caption_flat.shape[1] // BLOCKS
    stage = whole_call(
        text_second_kernel,
        (spot,),
        to_neighbours(text_kept, text_one, text_three),
        [((2 * inner, PAIR * text_rows), b16)] * RING,
        "text_second",
        (attn_kept, gate_sum_out, held[1]),
    )
    kept, sent = whole_call(
        text_third_kernel,
        (spot,),
        exchange(stage, "second"),
        [((2 * inner, text_rows), b16)] * 2,
        "text_third",
    )
    textkey_sum, textvalue_sum = whole_call(
        text_last_kernel,
        (),
        exchange([kept, sent], "z"),
        [((text_rows, inner), f32)] * 2,
        "text_last",
    )
    stage = whole_call(
        attn_second_kernel,
        (spot,),
        [by_slots(part) for part in to_neighbours(attn_kept, attn_one, attn_three)] + [riders],
        [((PAIR * block_rows + riders.shape[0], width), b16)] * RING,
        "attn_second",
    )
    got = exchange(stage, "second")
    kept, sent = whole_call(
        attn_third_kernel, (spot,), got, [((block_rows, width), b16)] * 2, "attn_third"
    )
    ada_grad, norm_grads, head_grads, crossgate = whole_call(
        functools.partial(ada_kernel, count, heads),
        (lax.axis_index("dp").reshape(1),),
        got,
        [((condition.shape[1] // BLOCKS, width), f32), ((4, width), f32), ((3, HEAD), f32)]
        + [((1, LANES), f32)],
        "ada",
        (kept,),
    )
    crossgate_grad = crossgate[0, :HEADS]
    query_sum, key_sum, value_sum, outw_sum = whole_call(
        attn_last_kernel,
        (),
        exchange([kept, sent], "z"),
        [((block_rows, inner), f32)] * 3 + [((inner, block_rows), f32)],
        "attn_last",
    )
    return (
        block_out,
        in_grad,
        ada_grad,
        norm_grads,
        query_sum,
        key_sum,
        value_sum,
        head_grads,
        textkey_sum,
        textvalue_sum,
        crossgate_grad,
        outw_sum,
        gate_sum_out,
        up_sum_out,
        down_sum_out,
    )


def solution(mesh):
    return jax.shard_map(
        shards,
        mesh=mesh,
        in_specs=(
            P(("dp", "tensor"), None),
            P(("dp", "tensor"), None),
            P("dp", None),
            P("dp", None, None),
            P("dp"),
            P("dp"),
            P(None, "tensor"),
            P(),
            P(None, "tensor"),
            P(None, "tensor"),
            P(None, "tensor"),
            P(),
            P(None, "tensor"),
            P(None, "tensor"),
            P("tensor"),
            P("tensor", None),
            P(None, "tensor"),
            P(None, "tensor"),
            P("tensor", None),
        ),
        out_specs=(
            P(("dp", "tensor"), None),
            P(("dp", "tensor"), None),
            P("dp", "tensor"),
            P(),
            P("dp", "tensor"),
            P("dp", "tensor"),
            P("dp", "tensor"),
            P(),
            P("dp", "tensor"),
            P("dp", "tensor"),
            P(),
            P("tensor", "dp"),
            P("dp", "tensor"),
            P("dp", "tensor"),
            P("tensor", "dp"),
        ),
        check_vma=False,
    )
```

```python
import functools
import math

import jax
import jax.numpy as jnp
from jax import lax
from jax.experimental import pallas as pl
from jax.experimental.pallas import tpu as pltpu
from jax.sharding import PartitionSpec as P

HEAD = 64
HEADS = 24
TXT = 256
SEGS = 3
EPS = 1e-06
LANES = 2 * HEAD
SHUT = 256.0
ROOT = HEAD ** (-0.5)
VMEM_LIMIT = 50 * 2**20
NO_COST = pl.CostEstimate(flops=0, bytes_accessed=0, transcendentals=0)


def cost_of(micros):
    return pl.CostEstimate(flops=int(micros * 1e9), bytes_accessed=0, transcendentals=0)


SUM_ROWS = 6
CROSS_MICROS = 10
BLOCK_IN_MICROS = 0
FFN_MICROS = 3
FFN_NEXT_MICROS = 8
MIDDLE_MICROS = 10
SELF_MICROS = 0
ATTN_MICROS = 7
ATTN_FIRST_MICROS = 0

RING = 4
PAIR = 2
BLOCKS = RING * PAIR * RING
SLOTS = BLOCKS // RING
SEND_ORDER = (2, 1, 3, 0)
CORE_SWAP = [(0, 1), (1, 0), (2, 3), (3, 2)]
CHIP_SWAP = [(0, 2), (2, 0), (1, 3), (3, 1)]
ROW_ORDER = (0, 2, 1, 3)

def dp_index(x, z, y):
    return (x * PAIR + z) * RING + y


def dp_perm(axis, step):
    pairs = []
    for x in range(RING):
        for z in range(PAIR):
            for y in range(RING):
                for tensor in range(2 * PAIR):
                    way = axis
                    if axis in ("first", "second"):
                        way = "x" if (tensor % 2 == 0) == (axis == "first") else "y"
                    target = {
                        "x": ((x + step) % RING, z, y),
                        "y": (x, z, (y + step) % RING),
                        "z": (x, (z + step) % PAIR, y),
                    }[way]
                    pairs.append(
                        (
                            dp_index(x, z, y) * 2 * PAIR + tensor,
                            dp_index(*target) * 2 * PAIR + tensor,
                        )
                    )
    return pairs


def dp_permute(values, axis, step):
    return lax.ppermute(values, ("dp", "tensor"), dp_perm(axis, step))


def dp_spot(position):
    index = lax.axis_index("dp")
    x, z, y = index // (RING * PAIR), index // RING % PAIR, index % RING
    core = position % 2
    return jnp.stack([jnp.where(core == 0, x, y), z, jnp.where(core == 0, y, x), core])


def swap_core(values):
    return lax.ppermute(values, "tensor", CORE_SWAP)


def swap_chip(values):
    return lax.ppermute(values, "tensor", CHIP_SWAP)


def times_transpose(left, right):
    return lax.dot_general(
        left, right, (((1,), (1,)), ((), ())), preferred_element_type=jnp.float32
    )


def gather_tensor(block):
    far = swap_chip(block)
    near = swap_core(block)
    return [block, far, near, swap_core(far)]


def join_kernel(own, far, both, far_out):
    rows = own.shape[0]
    both[:rows, :] = own[...]
    both[rows:, :] = far[...]
    far_out[...] = far[...]


def gather_rows(block, ties=()):
    rows, width = block.shape
    near = swap_core(block)
    upper, far = whole_call(
        join_kernel,
        (),
        [block, swap_chip(block)],
        [((2 * rows, width), block.dtype), ((rows, width), block.dtype)],
        "join",
        ties,
    )
    return jnp.concatenate([upper, near, swap_core(far)], axis=0)


def scatter_tensor(upper, lower):
    near = swap_core(lower)
    rows = upper.shape[0] // 2
    far = (upper[rows:].astype(jnp.float32) + near[rows:].astype(jnp.float32)).astype(near.dtype)
    return [upper, near, swap_chip(far)], far


def turn_kernel(source, target):
    target[...] = source[...].T


def turned(values, ties=()):
    tile = 512 if values.shape[1] % 512 == 0 else values.shape[1]
    return pl.pallas_call(
        lambda source, *rest: turn_kernel(source, rest[-1]),
        grid=(values.shape[1] // tile,),
        in_specs=[pl.BlockSpec((values.shape[0], tile), lambda step: (0, step))]
        + [pl.BlockSpec(memory_space=pl.ANY)] * len(ties),
        out_specs=pl.BlockSpec((tile, values.shape[0]), lambda step: (step, 0)),
        out_shape=jax.ShapeDtypeStruct(values.shape[::-1], values.dtype),
        compiler_params=pltpu.CompilerParams(vmem_limit_bytes=VMEM_LIMIT),
        cost_estimate=NO_COST,
    )(values, *ties)


def chunk_block(offset, slot, spot):
    first = (spot[0] + offset) % RING
    z, second = slot // RING, slot % RING
    x = jnp.where(spot[3] == 0, first, second)
    y = jnp.where(spot[3] == 0, second, first)
    return dp_index(x, z, y)


def offset_of_step(offsets, step):
    offset = offsets[-1]
    for place in range(len(offsets) - 1):
        offset = jnp.where(step == place, offsets[place], offset)
    return offset


def chunk_kernel(make, offsets, halves, extra, outs, held, sems):
    step = pl.program_id(0)
    first, second = halves

    def copies(place):
        slot = held.at[place % 2]
        if offsets[place] != 2:
            return [pltpu.make_async_copy(slot, outs[place], sems.at[place % 2, 0])]
        return [
            pltpu.make_async_copy(slot.at[half], out, sems.at[place % 2, way])
            for way, (half, out) in enumerate(zip((first, second), outs[place]))
        ]

    for place, offset in enumerate(offsets):

        @pl.when(step == place)
        def _(place=place, offset=offset):
            if place >= 2:
                for copy in copies(place - 2):
                    copy.wait()
            added = {1: (first, extra[0]), 3: (second, extra[1])}.get(offset) if extra else None
            make(held.at[place % 2], added, offset)
            for copy in copies(place):
                copy.start()
            if place == len(offsets) - 1:
                for last in range(max(place - 1, 0), place + 1):
                    for copy in copies(last):
                        copy.wait()


def chunk_call(make, operands, specs, offsets, halves, shape, spot, extra, ties, name, micros):
    count = len(operands)
    pieces = []
    for offset in offsets:
        if offset == 2:
            pieces += [tuple(len(range(*s.indices(d))) for s, d in zip(h, shape)) for h in halves]
        else:
            pieces.append(shape)

    def kernel(spot_ref, *refs):
        inputs, extras = refs[:count], refs[count : count + len(extra)]
        outs = list(refs[-len(pieces) - 2 : -2])
        grouped = []
        for offset in offsets:
            grouped.append((outs.pop(0), outs.pop(0)) if offset == 2 else outs.pop(0))
        chunk_kernel(
            functools.partial(make, inputs), offsets, halves, extras, grouped, refs[-2], refs[-1]
        )

    found = pl.pallas_call(
        kernel,
        grid_spec=pltpu.PrefetchScalarGridSpec(
            num_scalar_prefetch=1,
            grid=(len(offsets),),
            in_specs=list(specs)
            + [pl.BlockSpec(part.shape, lambda step, spot: (0, 0)) for part in extra]
            + [pl.BlockSpec(memory_space=pl.ANY)] * len(ties),
            out_specs=[pl.BlockSpec(memory_space=pl.ANY)] * len(pieces),
            scratch_shapes=[
                pltpu.VMEM((2,) + shape, jnp.bfloat16),
                pltpu.SemaphoreType.DMA((2, 2)),
            ],
        ),
        out_shape=[jax.ShapeDtypeStruct(piece, jnp.bfloat16) for piece in pieces],
        compiler_params=pltpu.CompilerParams(vmem_limit_bytes=VMEM_LIMIT),
        cost_estimate=cost_of(micros),
        name=name,
    )(spot, *operands, *extra, *ties)
    found = list(found)
    return [
        (found.pop(0), found.pop(0)) if offset == 2 else found.pop(0) for offset in offsets
    ]


def make_rows(groups, inputs, slot, added, offset):
    lefts, rights = inputs[: SLOTS * len(groups)], inputs[SLOTS * len(groups) :]
    size = SLOTS * lefts[0].shape[1]
    if len(rights) > sum(groups):
        riders = rights[-1][...]
        count, half = riders.shape[0], riders.shape[1] // 2
        first, second = slice(size, size + count), slice(size + count, size + 2 * count)
        if offset == 2:
            for side in (slice(0, half), slice(half, 2 * half)):
                slot[first, side] = riders[:, :half]
                slot[second, side] = riders[:, half:]
        else:
            slot[first, :] = riders
            if offset == 1:
                slot[second, :half] = added[1][first, :]
                slot[second, half:] = added[1][second, :]
            else:
                slot[second, :] = riders
    column = place = 0
    for group, count in enumerate(groups):
        rows = jnp.concatenate(
            [left[0] for left in lefts[SLOTS * group : SLOTS * (group + 1)]], axis=0
        )
        for right in rights[place : place + count]:
            wide = right.shape[1]
            product = dot(rows, right[...])
            low, high = column, column
            if added is not None:
                low = min(max(column, added[0][1].start), column + wide)
                high = min(max(column, added[0][1].stop), column + wide)
            for start, stop in ((column, low), (low, high), (high, column + wide)):
                if start < stop:
                    part = product[:, start - column : stop - column]
                    if (start, stop) == (low, high):
                        base = added[0][1].start
                        part = part + added[1][:size, start - base : stop - base].astype(jnp.float32)
                    slot[:size, start:stop] = part.astype(jnp.bfloat16)
            column += wide
        place += count


def row_chunks(pairs, offsets, spot, extra=(), ties=(), micros=0, riders=()):
    lefts = [left.reshape(BLOCKS, left.shape[0] // BLOCKS, left.shape[1]) for left, _ in pairs]
    rights = [right for _, group in pairs for right in group]
    total = sum(right.shape[1] for right in rights)
    specs, operands = [], []
    for left in lefts:
        for slot in range(SLOTS):
            specs.append(
                pl.BlockSpec(
                    (1,) + left.shape[1:],
                    lambda step, spot, slot=slot: (
                        chunk_block(offset_of_step(offsets, step), slot, spot),
                        0,
                        0,
                    ),
                )
            )
            operands.append(left)
    specs += [pl.BlockSpec(right.shape, lambda step, spot: (0, 0)) for right in rights]
    specs += [pl.BlockSpec(part.shape, lambda step, spot: (0, 0)) for part in riders]
    rows = SLOTS * lefts[0].shape[1] + sum(2 * part.shape[0] for part in riders)
    halves = [(slice(0, rows), slice(0, total // 2)), (slice(0, rows), slice(total // 2, total))]
    return chunk_call(
        functools.partial(make_rows, [len(group) for _, group in pairs]),
        operands + rights + list(riders),
        specs,
        offsets,
        halves,
        (rows, total),
        spot,
        extra,
        ties,
        "row_chunks",
        micros,
    )


def make_columns(lefts, inputs, slot, added, offset):
    whole = jnp.concatenate([right[...] for right in inputs[lefts:]], axis=1)
    row = 0
    for left in inputs[:lefts]:
        product = dot(left[...], whole)
        if added is not None and added[0][0].start == row:
            product = product + added[1][...].astype(jnp.float32)
        slot[row : row + left.shape[0], :] = product.astype(jnp.bfloat16)
        row += left.shape[0]


def column_chunks(lefts, right, offsets, spot, extra=(), ties=(), micros=0):
    rows = lefts[0].shape[0]
    depth, columns = right.shape
    specs = [pl.BlockSpec(left.shape, lambda step, spot: (0, 0)) for left in lefts]
    for slot in range(SLOTS):
        specs.append(
            pl.BlockSpec(
                (depth, columns // BLOCKS),
                lambda step, spot, slot=slot: (
                    0,
                    chunk_block(offset_of_step(offsets, step), slot, spot),
                ),
            )
        )
    lanes = columns // RING
    halves = [(slice(0, rows), slice(0, lanes)), (slice(rows, 2 * rows), slice(0, lanes))]
    return chunk_call(
        functools.partial(make_columns, len(lefts)),
        list(lefts) + [right] * SLOTS,
        specs,
        offsets,
        halves,
        (2 * rows, lanes),
        spot,
        extra,
        ties,
        "column_chunks",
        micros,
    )


def add_up(refs, index):
    total = refs[0][index].astype(jnp.float32)
    for ref in refs[1:]:
        total = total + ref[index].astype(jnp.float32)
    return total


def lane_slice(start, size):
    return (slice(None), pl.ds(pl.multiple_of(start * size, size), size))


def ffn_second_kernel(spot, *refs):
    parts, outs = refs[:-RING], refs[-RING:]
    for offset in range(RING):
        for z in range(PAIR):
            slot = z * RING + (spot[2] + offset) % RING
            outs[offset][z] = add_up(parts, slot).astype(jnp.bfloat16)


def ffn_third_kernel(spot, *refs):
    for out, z in ((refs[-2], spot[1]), (refs[-1], (spot[1] + 1) % PAIR)):
        out[...] = add_up(refs[:RING], z).astype(jnp.bfloat16)


def ffn_last_kernel(kept, got, gate_out, up_out, down_out):
    total = kept[...].astype(jnp.float32) + got[...].astype(jnp.float32)
    hidden = gate_out.shape[1]
    gate_out[...] = total[:, :hidden]
    up_out[...] = total[:, hidden : 2 * hidden]
    down_out[...] = total[:, 2 * hidden :].T


def text_second_kernel(spot, *refs):
    parts, outs = refs[:-RING], refs[-RING:]
    lanes = parts[0].shape[1] // SLOTS
    for offset in range(RING):
        for z in range(PAIR):
            slot = z * RING + (spot[2] + offset) % RING
            outs[offset][:, z * lanes : (z + 1) * lanes] = add_up(
                parts, lane_slice(slot, lanes)
            ).astype(jnp.bfloat16)


def text_third_kernel(spot, *refs):
    lanes = refs[-1].shape[1]
    for out, z in ((refs[-2], spot[1]), (refs[-1], (spot[1] + 1) % PAIR)):
        out[...] = add_up(refs[:RING], lane_slice(z, lanes)).astype(jnp.bfloat16)


def text_last_kernel(kept, got, textkey, textvalue):
    total = kept[...].astype(jnp.float32) + got[...].astype(jnp.float32)
    columns = textkey.shape[1]
    textkey[...] = total[:columns].T
    textvalue[...] = total[columns:].T


def attn_second_kernel(rows, spot, riders, *refs):
    parts, outs = refs[:-RING], refs[-RING:]
    size, count = SLOTS * rows, riders.shape[0]
    for offset in range(RING):
        for z in range(PAIR):
            slot = z * RING + (spot[2] + offset) % RING
            index = (pl.ds(pl.multiple_of(slot * rows, 16), rows), slice(None))
            outs[offset][z * rows : (z + 1) * rows, :] = add_up(parts, index).astype(jnp.bfloat16)
    ahead, behind = parts[1], parts[2]
    pairs = (
        (riders[...], ahead[size : size + count, :]),
        (behind[size : size + count, :], ahead[size + count : size + 2 * count, :]),
    )
    joined = [merge_rows(PAIR, first, second, rider_rows(2 * PAIR)) for first, second in pairs]
    joined = merge_rows(2 * PAIR, joined[0], joined[1], rider_rows(4 * PAIR))
    for out in outs:
        out[PAIR * rows :, :] = joined


def attn_third_kernel(spot, *refs):
    rows = refs[-1].shape[0]
    for out, z in ((refs[-2], spot[1]), (refs[-1], (spot[1] + 1) % PAIR)):
        index = (pl.ds(pl.multiple_of(z * rows, 16), rows), slice(None))
        out[...] = add_up(refs[:RING], index).astype(jnp.bfloat16)


def attn_last_kernel(kept, got, query, key, value, outw):
    total = kept[...].astype(jnp.float32) + got[...].astype(jnp.float32)
    columns = query.shape[1]
    for place, out in enumerate((query, key, value)):
        out[...] = total[:, place * columns : (place + 1) * columns]
    outw[...] = total[:, 3 * columns :].T


def whole_call(kernel, scalars, operands, outs, name, ties=(), scratch=(), micros=0):
    whole = pl.BlockSpec(memory_space=pltpu.VMEM)
    count = len(scalars) + len(operands)
    return pl.pallas_call(
        lambda *refs: kernel(*refs[:count], *refs[count + len(ties) :]),
        in_specs=[pl.BlockSpec(memory_space=pltpu.SMEM)] * len(scalars)
        + [whole] * len(operands)
        + [pl.BlockSpec(memory_space=pl.ANY)] * len(ties),
        out_specs=[whole] * len(outs),
        out_shape=[jax.ShapeDtypeStruct(shape, kind) for shape, kind in outs],
        scratch_shapes=list(scratch),
        compiler_params=pltpu.CompilerParams(vmem_limit_bytes=VMEM_LIMIT),
        cost_estimate=cost_of(micros),
        name=name,
    )(*scalars, *operands, *ties)


def exchange(chunks, axis):
    return [chunks[0]] + [
        dp_permute(chunks[step], axis, step) for step in range(1, len(chunks))
    ]


def one_on(halves):
    return dp_permute(halves[0], "first", 1), dp_permute(halves[1], "first", RING - 1)


def to_neighbours(own, ahead, behind):
    return [own, dp_permute(ahead, "first", 1), dp_permute(behind, "first", RING - 1)]


def by_slots(chunk):
    return chunk.reshape(SLOTS, chunk.shape[0] // SLOTS, chunk.shape[1])


def lane_index(shape):
    return lax.broadcasted_iota(jnp.int32, shape, 1)


def head_lanes(shape, head):
    lane = lane_index(shape)
    return (lane < HEAD) if head == 0 else (lane >= HEAD)


def per_head(values, reduce):
    first = head_lanes(values.shape, 0)
    left = jnp.sum(jnp.where(first, values, 0.0), axis=1, keepdims=True)
    right = jnp.sum(jnp.where(first, 0.0, values), axis=1, keepdims=True)
    return jnp.where(first, left, right)


def head_units(raw):
    inverse = lax.rsqrt(per_head(raw * raw, None) * (1.0 / HEAD) + EPS)
    return raw * inverse, inverse


def partner(values):
    lane = lane_index(values.shape)
    return jnp.where(
        lane % HEAD < HEAD // 2,
        pltpu.roll(values, LANES - HEAD // 2, 1),
        pltpu.roll(values, HEAD // 2, 1),
    )


def dot(left, right):
    return jnp.dot(left, right, preferred_element_type=jnp.float32)


def dot_t(left, right):
    return lax.dot_general(left, right, (((1,), (1,)), ((), ())), preferred_element_type=jnp.float32)


def attend_kernel(
    raw_q, raw_k, value, raw_t, text_value, cosine, sine, gains, gate, gate_swapped, mark_q, mark_k, mark_t,
    query_out, key_out, text_out, mixed_out, self_out, cross_out, self_log, cross_log,
):
    cos, sin = cosine[...], sine[...]
    unit = head_units(raw_q[...])[0] * gains[0:1, :]
    query = ((unit * cos + partner(unit) * sin).astype(jnp.bfloat16) * ROOT).astype(jnp.bfloat16)
    unit = head_units(raw_k[...])[0] * gains[1:2, :]
    key = (unit * cos + partner(unit) * sin).astype(jnp.bfloat16)
    text = (head_units(raw_t[...])[0] * gains[2:3, :]).astype(jnp.bfloat16)
    query_out[...] = query
    key_out[...] = key
    text_out[...] = text

    def attention(keys, marks, values):
        outs, sums = [], []
        for head in range(2):
            own = head_lanes(query.shape, head)
            own_keys = head_lanes(keys.shape, head)
            probe = jnp.where(own, query, mark_q[...])
            scores = dot_t(probe, jnp.where(own_keys, keys, marks))
            weights = jnp.exp(scores).astype(jnp.bfloat16)
            both = dot(weights, jnp.where(own_keys, values, jnp.ones_like(values)))
            outs.append(both)
        first = head_lanes(outs[0].shape, 0)
        product = jnp.where(first, outs[0], outs[1])
        total = jnp.where(first, outs[1], outs[0])
        return product / pltpu.roll(total, HEAD, 1), jnp.log(total)

    out, log = attention(key, mark_k[...], value[...])
    self_out[...] = out
    self_log[...] = log
    cross, log = attention(text, mark_t[...], text_value[...])
    cross_out[...] = cross
    cross_log[...] = log - jnp.log(gate_swapped[...])
    mixed_out[...] = (out + gate[...] * cross).astype(jnp.bfloat16)


def attention_grads(query, keys, marks, values, grad, out, log, mark_q):
    rows = grad.astype(jnp.float32)
    delta = per_head(rows * out, None)
    delta = pltpu.roll(delta, HEAD, 1)
    lane = lane_index(query.shape) % HEAD
    log_high = log.astype(jnp.bfloat16)
    log_low = (log - log_high.astype(jnp.float32)).astype(jnp.bfloat16)
    delta_high = delta.astype(jnp.bfloat16)
    delta_low = (delta - delta_high.astype(jnp.float32)).astype(jnp.bfloat16)
    zero = jnp.zeros_like(query)
    code = jnp.where(lane == 4, -log_high, jnp.where(lane == 5, -log_low, mark_q))
    shift = jnp.where(lane == 4, -delta_high, jnp.where(lane == 5, -delta_low, zero))
    key_grads, value_grads, query_grads = [], [], []
    for head in range(2):
        own = head_lanes(query.shape, head)
        own_keys = head_lanes(keys.shape, head)
        probe = jnp.where(own, query, code)
        probs = jnp.exp(dot_t(jnp.where(own_keys, keys, marks), probe))
        slope = dot_t(jnp.where(own_keys, values, marks), jnp.where(own, grad, shift))
        score_grad = (probs * slope).astype(jnp.bfloat16)
        value_grads.append(dot(probs.astype(jnp.bfloat16), grad))
        key_grads.append(dot(score_grad, query))
        turned = keys[:, head * HEAD : (head + 1) * HEAD].T
        query_grads.append(dot(turned, score_grad))
    first = head_lanes(keys.shape, 0)
    return (
        jnp.concatenate(query_grads, axis=0),
        jnp.where(first, key_grads[0], key_grads[1]),
        jnp.where(first, value_grads[0], value_grads[1]),
    )


def norm_back(weighted, unit, inverse):
    return inverse * (weighted - unit * (per_head(weighted * unit, None) * (1.0 / HEAD)))


def cross_back_kernel(
    query, text, text_value, raw_t, grad, out, log, gains, mark_q, mark_t,
    query_grad, raw_grad, value_grad, gain_sum, gate_sum,
):
    grad_q, grad_t, grad_v = attention_grads(
        query[...], text[...], mark_t[...], text_value[...], grad[...], out[...], log[...], mark_q[...]
    )
    query_grad[...] = grad_q.T
    value_grad[...] = grad_v.astype(jnp.bfloat16).T
    grad_t = grad_t.astype(jnp.bfloat16).astype(jnp.float32)
    unit, inverse = head_units(raw_t[...])
    gain_sum[...] = jnp.sum(grad_t * unit, axis=0, keepdims=True)
    raw_grad[...] = norm_back(grad_t * gains[2:3, :], unit, inverse).astype(jnp.bfloat16).T
    gate_sum[...] = jnp.sum(grad[...].astype(jnp.float32) * out[...], axis=0, keepdims=True)


def self_back_kernel(
    query, key, value, raw_q, raw_k, grad, out, log, cross_grad, cosine, sine, gains, mark_q, mark_k,
    query_grad, key_grad, value_grad, gain_sum,
):
    grad_q, grad_k, grad_v = attention_grads(
        query[...], key[...], mark_k[...], value[...], grad[...], out[...], log[...], mark_q[...]
    )
    value_grad[...] = grad_v.astype(jnp.bfloat16)
    cos, sin = cosine[...], sine[...]
    grad_q = (grad_q.T + cross_grad[...]) * ROOT
    for turn, raw, row, target in ((grad_q, raw_q, 0, query_grad), (grad_k, raw_k, 1, key_grad)):
        turn = turn.astype(jnp.bfloat16).astype(jnp.float32)
        turn = turn * cos - partner(turn) * sin
        unit, inverse = head_units(raw[...])
        gain_sum[row : row + 1, :] = jnp.sum(turn * unit, axis=0, keepdims=True)
        target[...] = norm_back(turn * gains[row : row + 1, :], unit, inverse).astype(jnp.bfloat16)


def pair_call(kernel, operands, outs, name, ties=(), micros=0):
    def spec(shape, cut):
        if cut is None:
            return pl.BlockSpec(shape, lambda pair: (0, 0))
        if cut == 1:
            return pl.BlockSpec((shape[0], LANES), lambda pair: (0, pair))
        return pl.BlockSpec((LANES, shape[1]), lambda pair: (pair, 0))

    width = outs[0][0][0] if outs[0][2] == 0 else outs[0][0][1]
    return pl.pallas_call(
        lambda *refs: kernel(*refs[: len(operands)], *refs[len(operands) + len(ties) :]),
        grid=(width // LANES,),
        in_specs=[spec(part.shape, cut) for part, cut in operands]
        + [pl.BlockSpec(memory_space=pl.ANY)] * len(ties),
        out_specs=[spec(shape, cut) for shape, _, cut in outs],
        out_shape=[jax.ShapeDtypeStruct(shape, kind) for shape, kind, _ in outs],
        compiler_params=pltpu.CompilerParams(vmem_limit_bytes=VMEM_LIMIT),
        cost_estimate=cost_of(micros),
        name=name,
    )(*[part for part, _ in operands], *ties)
def inverse_rms(values):
    return lax.rsqrt(jnp.mean(values * values, axis=-1, keepdims=True) + EPS)


def row_norm_back(weighted, unit, inverse):
    return inverse * (weighted - unit * jnp.mean(weighted * unit, axis=-1, keepdims=True))


def per_row(table, segment):
    return jnp.where(segment == 0.0, table[0:1], jnp.where(segment == 1.0, table[1:2], table[2:3]))


def total_of(parts):
    upper, near, far = parts
    rows = far.shape[0]
    return (
        upper[:rows].astype(jnp.float32) + near[:rows].astype(jnp.float32) + far[...].astype(jnp.float32)
    )


def segment_sums(member, values):
    high = values.astype(jnp.bfloat16)
    low = (values - high.astype(jnp.float32)).astype(jnp.bfloat16)
    return dot(member, high) + dot(member, low)


def tables_kernel(here, lens, gate, segments, head_gains, cosine, sine, mark_q, mark_k, mark_t,
                  segment, member, gate_lanes, gate_swapped, gains):
    heads = gains.shape[1] // HEAD
    lane = lane_index(gate_lanes.shape) // HEAD
    line = jnp.zeros(gate_lanes.shape, jnp.float32)
    swapped = line
    for head in range(heads):
        line = jnp.where(lane == head, gate[head], line)
        swapped = jnp.where(lane == head ^ 1, gate[head], swapped)
    gate_lanes[...] = jnp.tanh(line)
    gate_swapped[...] = jnp.tanh(swapped)
    gains[...] = jnp.concatenate([head_gains[...]] * heads, axis=1)
    rows = segments.shape[1]
    ids = segments[...]
    first = jnp.sum((ids < 1).astype(jnp.float32))
    second = jnp.sum((ids < 2).astype(jnp.float32))
    lane = lane_index((rows, LANES))
    half = HEAD // 2
    rate = jnp.exp((lane % half).astype(jnp.float32) * (-2.0 * math.log(10000.0) / HEAD))
    within = lane % HEAD
    for block, code in enumerate(ROW_ORDER):
        source = here[0] ^ code
        line = segments[pl.ds(source, 1), :].astype(jnp.float32)
        label = jnp.broadcast_to(line, (rows, rows)).T
        start = jnp.where(label == 0.0, 0.0, jnp.where(label == 1.0, first, second))
        token = (lax.broadcasted_iota(jnp.int32, (rows, LANES), 0) + source * rows).astype(jnp.float32)
        angle = (token - start) * rate
        index = slice(block * rows, (block + 1) * rows)
        cosine[index, :] = jnp.cos(angle)
        sine[index, :] = jnp.where(within < half, -1.0, 1.0) * jnp.sin(angle)
        same = ((label == within.astype(jnp.float32)) & (within < SEGS)).astype(jnp.float32)
        shut = (within == SEGS).astype(jnp.float32)
        ones = ((within >= SEGS) & (within < SEGS + 3)).astype(jnp.float32)
        mark_q[index, :] = (SHUT * same - SHUT * shut).astype(jnp.bfloat16)
        mark_k[index, :] = (same + ones).astype(jnp.bfloat16)
        if block == 0:
            segment[...] = label
            member[...] = (
                lax.broadcasted_iota(jnp.int32, (8, rows), 0).astype(jnp.float32) == line
            ).astype(jnp.bfloat16)
    for group in range(SEGS):
        lane = lane_index((TXT, LANES)) % HEAD
        row = lax.broadcasted_iota(jnp.int32, (TXT, LANES), 0)
        inside = ((lane == group) & (row < lens[group])).astype(jnp.float32)
        ones = ((lane >= SEGS) & (lane < SEGS + 3)).astype(jnp.float32)
        mark_t[group * TXT : (group + 1) * TXT, :] = (inside + ones).astype(jnp.bfloat16)


def text_kernel(captions, key_weight, value_weight, raw_out, value_out, raw_sum, value_sum):
    step = pl.program_id(0)

    @pl.when(step == 0)
    def _():
        raw_sum[...] = dot(captions[...], key_weight[...])
        value_sum[...] = dot(captions[...], value_weight[...])

    @pl.when(step > 0)
    def _():
        raw_sum[...] += dot(captions[...], key_weight[...])
        value_sum[...] += dot(captions[...], value_weight[...])

    @pl.when(step == pl.num_programs(0) - 1)
    def _():
        raw_out[...] = raw_sum[...]
        value_out[...] = value_sum[...].astype(jnp.bfloat16)


def text_call(captions, key_weight, value_weight):
    rows, depth = captions.shape
    columns = key_weight.shape[1]
    tile = depth // 4
    return pl.pallas_call(
        text_kernel,
        grid=(depth // tile,),
        in_specs=[
            pl.BlockSpec((rows, tile), lambda step: (0, step)),
            pl.BlockSpec((tile, columns), lambda step: (step, 0)),
            pl.BlockSpec((tile, columns), lambda step: (step, 0)),
        ],
        out_specs=[pl.BlockSpec((rows, columns), lambda step: (0, 0))] * 2,
        out_shape=[
            jax.ShapeDtypeStruct((rows, columns), jnp.float32),
            jax.ShapeDtypeStruct((rows, columns), jnp.bfloat16),
        ],
        scratch_shapes=[pltpu.VMEM((rows, columns), jnp.float32)] * 2,
        compiler_params=pltpu.CompilerParams(vmem_limit_bytes=VMEM_LIMIT),
        cost_estimate=cost_of(9),
        name="text",
    )(captions, key_weight, value_weight)


def project_kernel(here, own, far, near, last, mods, gains, segment_q, query_w, key_w, value_w,
                   rows_out, raw_q, raw_k, value):
    table = mods[here[0]]
    rows = own.shape[0]
    for block, part in enumerate((own, far, near, last)):
        index = slice(block * rows, (block + 1) * rows)
        values = part[...].astype(jnp.float32)
        marks = segment_q[index, :].astype(jnp.float32)
        scale = jnp.where(
            marks[:, 0:1] > 0.0, table[0:1], jnp.where(marks[:, 1:2] > 0.0, table[1:2], table[2:3])
        )
        rows_out[index, :] = (
            values * inverse_rms(values) * gains[0:1] * (1.0 + scale)
        ).astype(jnp.bfloat16)
    raw_q[...] = dot(rows_out[...], query_w[...])
    raw_k[...] = dot(rows_out[...], key_w[...])
    value[...] = dot(rows_out[...], value_w[...]).astype(jnp.bfloat16)


def middle_kernel(here, block, upper, near, far, mods, gains, segment, attn_out, middle_out, rows_out):
    attn_sum = total_of((upper, near, far))
    label = segment[:, 0:1]
    factor = jnp.tanh(per_row(mods[here[0] ^ 1], label)) * gains[1:2]
    middle = block[...].astype(jnp.float32) + factor * (attn_sum * inverse_rms(attn_sum))
    attn_out[...] = attn_sum
    middle_out[...] = middle
    scale = per_row(mods[here[0] ^ 2], label)
    rows_out[...] = (middle * inverse_rms(middle) * gains[2:3] * (1.0 + scale)).astype(jnp.bfloat16)


def block_out_kernel(here, middle, upper, near, far, grad, mods, gains, segment, member,
                     block_out, grad_out, sums):
    ffn_sum = total_of((upper, near, far))
    inverse = inverse_rms(ffn_sum)
    unit = ffn_sum * inverse
    factor = jnp.tanh(per_row(mods[here[0] ^ 3], segment[:, 0:1])) * gains[3:4]
    block_out[...] = (middle[...] + factor * unit).astype(jnp.bfloat16)
    incoming = grad[...].astype(jnp.float32)
    grad_out[...] = row_norm_back(incoming * factor, unit, inverse).astype(jnp.bfloat16)
    sums[...] = segment_sums(member[...], incoming * unit)


def middle_back_kernel(here, middle, attn, upper, near, far, grad, mods, gains, segment, member,
                       middle_grad, attn_grad, ffn_sums, attn_sums):
    grad_in = total_of((upper, near, far))
    label = segment[:, 0:1]
    inverse = inverse_rms(middle[...])
    unit = middle[...] * inverse
    factor = gains[2:3] * (1.0 + per_row(mods[here[0] ^ 2], label))
    ffn_sums[...] = segment_sums(member[...], grad_in * unit)
    grad_middle = grad[...].astype(jnp.float32) + row_norm_back(grad_in * factor, unit, inverse)
    middle_grad[...] = grad_middle
    inverse = inverse_rms(attn[...])
    unit = attn[...] * inverse
    factor = jnp.tanh(per_row(mods[here[0] ^ 1], label)) * gains[1:2]
    attn_grad[...] = row_norm_back(grad_middle * factor, unit, inverse).astype(jnp.bfloat16)
    attn_sums[...] = segment_sums(member[...], grad_middle * unit)


def block_in_kernel(here, block, middle_grad, upper, near, far, mods, gains, segment, member,
                    in_grad, sums):
    grad_in = total_of((upper, near, far))
    values = block[...].astype(jnp.float32)
    inverse = inverse_rms(values)
    unit = values * inverse
    factor = gains[0:1] * (1.0 + per_row(mods[here[0]], segment[:, 0:1]))
    in_grad[...] = (
        middle_grad[...] + row_norm_back(grad_in * factor, unit, inverse)
    ).astype(jnp.bfloat16)
    sums[...] = segment_sums(member[...], grad_in * unit)


def stack_sums_kernel(here, first, second, third, fourth, head_gain, text_gain, gate_sum, gate, out):
    width = out.shape[1]
    heads = jnp.concatenate([head_gain[0:1], head_gain[1:2], text_gain[...]], axis=1)
    inner = heads.shape[1] // 3
    gates = gate_sum[...] * (1.0 - gate[...] * gate[...])
    gates = jnp.concatenate([gates, jnp.zeros((1, width - inner), jnp.float32)], axis=1)
    lane = lane_index(gates.shape)
    moved = jnp.zeros_like(gates)
    for position in range(4):
        turn = pltpu.roll(gates, position * inner, 1) if position else gates
        moved = jnp.where((lane // inner == position) & (here[0] == position), turn, moved)
    out[...] = jnp.concatenate(
        [part[0:SEGS] for part in (first, second, third, fourth)]
        + [
            jnp.concatenate([heads, jnp.zeros((1, width - 3 * inner), jnp.float32)], axis=1),
            moved,
            jnp.zeros((2, width), jnp.float32),
        ],
        axis=0,
    )


def pack_kernel(here, own, far, near, last, mods, gains, cond, packed):
    total = own[...] + far[...] + near[...] + last[...]
    grad = jnp.zeros((SEGS, total.shape[1]), jnp.float32)
    rows = []
    for name in range(4):
        part = total[name * SEGS : (name + 1) * SEGS]
        mod = mods[here[0] ^ name]
        gain = gains[name : name + 1]
        if name % 2 == 1:
            factor = jnp.tanh(mod)
            slope = 1.0 - factor * factor
        else:
            factor = 1.0 + mod
            slope = jnp.ones_like(mod)
        rows.append(jnp.sum(part * factor, axis=0, keepdims=True))
        mine = (jnp.zeros(part.shape, jnp.int32) + here[0]) == name
        grad = jnp.where(mine, part * slope * gain, grad)
    rows.append(total[4 * SEGS : 4 * SEGS + 2])
    rows = jnp.concatenate(rows, axis=0)
    high = rows.astype(jnp.bfloat16).astype(jnp.float32)
    pad = jnp.zeros((packed.shape[0] - 2 * SEGS - 2 * SUM_ROWS, total.shape[1]), jnp.float32)
    packed[...] = jnp.concatenate(
        [grad, cond[...].astype(jnp.float32), high, rows - high, pad], axis=0
    ).astype(jnp.bfloat16)


def rider_rows(count):
    return -(-(2 * SEGS * count + 2 * SUM_ROWS) // 16) * 16


def merge_rows(count, first, second, size):
    first, second = first.astype(jnp.float32), second.astype(jnp.float32)
    wide = SEGS * count
    start = 2 * wide
    sums = (
        first[start : start + SUM_ROWS]
        + first[start + SUM_ROWS : start + 2 * SUM_ROWS]
        + second[start : start + SUM_ROWS]
        + second[start + SUM_ROWS : start + 2 * SUM_ROWS]
    )
    high = sums.astype(jnp.bfloat16).astype(jnp.float32)
    pieces = [first[:wide], second[:wide], first[wide:start], second[wide:start], high, sums - high]
    rest = size - 4 * wide - 2 * SUM_ROWS
    if rest:
        pieces.append(jnp.zeros((rest, first.shape[1]), jnp.float32))
    return jnp.concatenate(pieces, axis=0).astype(jnp.bfloat16)


def merge_kernel(ours, theirs, out):
    out[...] = merge_rows(1, ours[...], theirs[...], out.shape[0])


def ada_kernel(count, heads, dp, own, *refs):
    parts = (own,) + refs[:3]
    ada_out, norm_out, head_out, gate_out = refs[3:]
    wide = SEGS * count
    base = own.shape[0] - rider_rows(count)
    columns = ada_out.shape[0]
    share = LANES // columns
    start = pl.multiple_of(dp[0] // share * LANES, LANES)
    grads, conds = [], []
    sums = jnp.zeros((SUM_ROWS, own.shape[1]), jnp.float32)
    for part in parts:
        rows = part[base:, :].astype(jnp.float32)
        grads.append(rows[:wide])
        conds.append(part[base:, pl.ds(start, LANES)].astype(jnp.float32)[wide : 2 * wide])
        for half in range(2):
            place = 2 * wide + half * SUM_ROWS
            sums = sums + rows[place : place + SUM_ROWS]
    conds = jnp.concatenate(conds, axis=0)
    conds = pltpu.roll(conds, (LANES - dp[0] % share * columns) % LANES, 1)
    acts = conds / (1.0 + jnp.exp(-conds))
    ada_out[...] = dot(
        acts.astype(jnp.bfloat16).astype(jnp.float32).T.astype(jnp.bfloat16),
        jnp.concatenate(grads, axis=0).astype(jnp.bfloat16),
    )[:columns]
    norm_out[...] = sums[:4]
    inner = heads * HEAD
    for row in range(3):
        line = jnp.zeros((1, HEAD), jnp.float32)
        for head in range(heads):
            place = row * inner + head * HEAD
            line = line + sums[4:5, place : place + HEAD]
        head_out[row : row + 1, :] = line
    lane = lane_index((1, LANES))
    line = jnp.zeros((1, LANES), jnp.float32)
    for head in range(HEADS):
        value = jnp.sum(sums[5:6, head * HEAD : (head + 1) * HEAD], axis=1, keepdims=True)
        line = jnp.where(lane == head, value, line)
    gate_out[...] = line


def shards(
    block_in,
    out_grad,
    condition,
    captions,
    caption_len,
    segment_ids,
    ada_weight,
    norm_gains,
    query_weight,
    key_weight,
    value_weight,
    head_gains,
    textkey_weight,
    textvalue_weight,
    cross_gate,
    out_weight,
    gate_weight,
    up_weight,
    down_weight,
):
    rows, width = block_in.shape
    length = segment_ids.shape[0]
    heads = cross_gate.shape[0]
    inner = heads * HEAD
    half_rows = length // 2
    position = lax.axis_index("tensor")
    spot = dp_spot(position)
    here = position.reshape(1)
    b16, f32 = jnp.bfloat16, jnp.float32

    blocks = gather_tensor(block_in)
    cond_rows = jnp.pad(condition, ((0, 0), (0, width - condition.shape[1])))
    own_act = jax.nn.silu(condition.astype(f32)).astype(b16)
    own_part = jnp.dot(own_act, ada_weight, preferred_element_type=f32)
    parts = gather_tensor(own_part)
    mods = jnp.stack([parts[ROW_ORDER.index(code)] for code in range(4)])

    cosine, sine, mark_q, mark_k, mark_t, segment, member, gate_lanes, gate_swapped, gains = whole_call(
        tables_kernel,
        (here, caption_len, cross_gate),
        [segment_ids.reshape(length // rows, rows), head_gains],
        [((length, LANES), f32)] * 2
        + [((length, LANES), b16)] * 2
        + [((SEGS * TXT, LANES), b16), ((rows, LANES), f32), ((8, rows), b16)]
        + [((1, inner), f32)] * 2
        + [((3, inner), f32)],
        "tables",
        micros=2,
    )
    caption_flat = captions.reshape(-1, captions.shape[-1])
    texts = caption_flat.shape[0]
    raw_t, text_value = text_call(caption_flat, textkey_weight, textvalue_weight)
    attn_rows, raw_q, raw_k, value = whole_call(
        project_kernel,
        (here,),
        blocks + [mods, norm_gains, mark_q, query_weight, key_weight, value_weight],
        [((length, width), b16), ((length, inner), f32), ((length, inner), f32), ((length, inner), b16)],
        "project",
        micros=6,
    )
    query, key, text, mixed, self_out, cross_out, self_log, cross_log = pair_call(
        attend_kernel,
        [(raw_q, 1), (raw_k, 1), (value, 1), (raw_t, 1), (text_value, 1), (cosine, None), (sine, None)]
        + [(gains, 1), (gate_lanes, 1), (gate_swapped, 1), (mark_q, None), (mark_k, None), (mark_t, None)],
        [((length, inner), b16, 1)] * 2
        + [((texts, inner), b16, 1), ((length, inner), b16, 1)]
        + [((length, inner), f32, 1)] * 4,
        "attend",
        micros=11,
    )

    def halves(product):
        return product(slice(0, half_rows)).astype(b16), product(slice(half_rows, None)).astype(b16)

    def all_of(block):
        return jnp.concatenate(gather_tensor(block), axis=0)

    upper, lower = halves(lambda part: jnp.dot(mixed[part], out_weight, preferred_element_type=f32))
    sums, sent = scatter_tensor(upper, lower)
    attn_rows_t = turned(attn_rows, (sent,))
    wide = ((rows, width), f32)
    narrow = ((rows, width), b16)
    totals = ((8, width), f32)
    attn_sum, middle, ffn_own = whole_call(
        middle_kernel,
        (here,),
        [block_in] + sums + [mods, norm_gains, segment],
        [wide, wide, narrow],
        "middle",
    )
    ffn_rows = all_of(ffn_own)
    gate_pre = jnp.dot(ffn_rows, gate_weight, preferred_element_type=f32)
    up_pre = jnp.dot(ffn_rows, up_weight, preferred_element_type=f32)
    sigmoid_gate = jax.nn.sigmoid(gate_pre)
    silu_gate = gate_pre * sigmoid_gate
    hidden = (silu_gate * up_pre).astype(b16)
    upper, lower = halves(lambda part: jnp.dot(hidden[part], down_weight, preferred_element_type=f32))
    sums, sent = scatter_tensor(upper, lower)
    ffn_rows_t = turned(ffn_rows, (sent,))
    block_out, grad_own, sum_gate_ffn = whole_call(
        block_out_kernel,
        (here,),
        [middle] + sums + [out_grad, mods, norm_gains, segment, member],
        [narrow, narrow, totals],
        "block_out",
    )

    grad_ffn = all_of(grad_own)
    grad_hidden = times_transpose(grad_ffn, down_weight)
    grad_gate = (
        grad_hidden * up_pre * sigmoid_gate * (1.0 + gate_pre * (1.0 - sigmoid_gate))
    ).astype(b16)
    grad_up = (grad_hidden * silu_gate).astype(b16)
    upper, lower = halves(
        lambda part: times_transpose(grad_gate[part], gate_weight)
        + times_transpose(grad_up[part], up_weight)
    )
    sums, sent = scatter_tensor(upper, lower)
    grad_ffn_t = turned(grad_ffn, (sent,))
    ffn_pairs = [(ffn_rows_t, [grad_gate, grad_up]), (grad_ffn_t, [hidden])]
    (halves_two,) = row_chunks(ffn_pairs, (2,), spot, ties=(sent,), micros=FFN_MICROS)
    ffn_passed = one_on(halves_two)
    grad_middle, grad_own, sum_scale_ffn, sum_gate_attn = whole_call(
        middle_back_kernel,
        (here,),
        [middle, attn_sum] + sums + [out_grad, mods, norm_gains, segment, member],
        [wide, narrow, totals, totals],
        "middle_back",
        micros=MIDDLE_MICROS,
    )

    ffn_one, ffn_three, ffn_kept = row_chunks(
        ffn_pairs, (1, 3, 0), spot, extra=ffn_passed, ties=(grad_own,), micros=FFN_NEXT_MICROS
    )
    grad_attn = gather_rows(grad_own, (ffn_kept,))
    grad_mixed = times_transpose(grad_attn, out_weight).astype(b16)
    cross_grad, text_grad, text_value_grad, text_gain, gate_sum = pair_call(
        cross_back_kernel,
        [(query, 1), (text, 1), (text_value, 1), (raw_t, 1), (grad_mixed, 1), (cross_out, 1)]
        + [(cross_log, 1), (gains, 1), (mark_q, None), (mark_t, None)],
        [((length, inner), f32, 1), ((inner, texts), b16, 0), ((inner, texts), b16, 0)]
        + [((1, inner), f32, 1)] * 2,
        "cross_back",
        micros=CROSS_MICROS,
    )
    text_lefts = [text_grad, text_value_grad]
    (halves_two,) = column_chunks(text_lefts, caption_flat, (2,), spot)
    text_passed = one_on(halves_two)
    query_grad, key_grad, value_grad, head_gain = pair_call(
        self_back_kernel,
        [(query, 1), (key, 1), (value, 1), (raw_q, 1), (raw_k, 1), (grad_mixed, 1), (self_out, 1)]
        + [(self_log, 1), (cross_grad, 1), (cosine, None), (sine, None), (gains, 1)]
        + [(mark_q, None), (mark_k, None)],
        [((length, inner), b16, 1)] * 3 + [((2, inner), f32, 1)],
        "self_back",
        (halves_two[0],),
        micros=SELF_MICROS,
    )

    hidden_cols = hidden.shape[1]
    block_rows = width // BLOCKS
    got = [by_slots(part) for part in to_neighbours(ffn_kept, ffn_one, ffn_three)]
    shape = (PAIR, block_rows, 3 * hidden_cols)
    ffn_stage = whole_call(
        ffn_second_kernel, (spot,), got, [(shape, b16)] * RING, "ffn_second", (query_grad,)
    )
    upper, lower = halves(
        lambda part: times_transpose(query_grad[part], query_weight)
        + times_transpose(key_grad[part], key_weight)
        + times_transpose(value_grad[part], value_weight)
    )
    sums, sent = scatter_tensor(upper, lower)
    in_grad, sum_scale_attn = whole_call(
        block_in_kernel,
        (here,),
        [block_in, grad_middle] + sums + [mods, norm_gains, segment, member],
        [narrow, totals],
        "block_in",
        (ffn_stage[0],),
        micros=BLOCK_IN_MICROS,
    )
    (stacked,) = whole_call(
        stack_sums_kernel,
        (here,),
        [sum_scale_attn, sum_gate_attn, sum_scale_ffn, sum_gate_ffn]
        + [head_gain, text_gain, gate_sum, gate_lanes],
        [((16, width), f32)],
        "stack_sums",
    )
    stacked = gather_tensor(stacked)
    (riders,) = whole_call(
        pack_kernel,
        (here,),
        stacked + [mods, norm_gains, cond_rows],
        [((rider_rows(1), width), b16)],
        "pack",
    )
    theirs = dp_permute(riders, "z", 1)
    (riders,) = whole_call(
        merge_kernel, (), [riders, theirs], [((rider_rows(PAIR), width), b16)], "merge"
    )
    attn_pairs = [
        (attn_rows_t, [query_grad, key_grad, value_grad]),
        (turned(grad_attn, (halves_two[0],)), [mixed]),
    ]
    (halves_two,) = row_chunks(attn_pairs, (2,), spot, riders=(riders,), micros=ATTN_FIRST_MICROS)
    attn_passed = one_on(halves_two)
    text_one, text_three, text_kept = column_chunks(
        text_lefts, caption_flat, (1, 3, 0), spot, extra=text_passed, ties=(halves_two[0],), micros=8
    )
    kept, sent = whole_call(
        ffn_third_kernel,
        (spot,),
        exchange(ffn_stage, "second"),
        [(shape[1:], b16)] * 2,
        "ffn_third",
        (text_kept,),
    )
    gate_sum_out, up_sum_out, down_sum_out = whole_call(
        ffn_last_kernel,
        (),
        exchange([kept, sent], "z"),
        [((block_rows, hidden_cols), f32)] * 2 + [((hidden_cols, block_rows), f32)],
        "ffn_last",
    )
    text_rows = caption_flat.shape[1] // BLOCKS
    attn_one, attn_three, attn_kept = row_chunks(
        attn_pairs, (1, 3, 0), spot, extra=attn_passed, ties=(kept,), riders=(riders,), micros=ATTN_MICROS
    )
    stage = whole_call(
        text_second_kernel,
        (spot,),
        to_neighbours(text_kept, text_one, text_three),
        [((2 * inner, PAIR * text_rows), b16)] * RING,
        "text_second",
        (attn_kept,),
    )
    kept, sent = whole_call(
        text_third_kernel,
        (spot,),
        exchange(stage, "second"),
        [((2 * inner, text_rows), b16)] * 2,
        "text_third",
        (gate_sum_out,),
    )
    textkey_sum, textvalue_sum = whole_call(
        text_last_kernel,
        (),
        exchange([kept, sent], "z"),
        [((text_rows, inner), f32)] * 2,
        "text_last",
    )
    stage = whole_call(
        functools.partial(attn_second_kernel, block_rows),
        (spot,),
        [riders] + to_neighbours(attn_kept, attn_one, attn_three),
        [((PAIR * block_rows + rider_rows(4 * PAIR), width), b16)] * RING,
        "attn_second",
        (kept,),
    )
    got = exchange(stage, "second")
    kept, sent = whole_call(
        attn_third_kernel, (spot,), got, [((block_rows, width), b16)] * 2, "attn_third"
    )
    ada_grad, norm_grads, head_grads, crossgate = whole_call(
        functools.partial(ada_kernel, 4 * PAIR, heads),
        (lax.axis_index("dp").reshape(1),),
        got,
        [((condition.shape[1] // BLOCKS, width), f32), ((4, width), f32), ((3, HEAD), f32)]
        + [((1, LANES), f32)],
        "ada",
        (kept,),
    )
    crossgate_grad = crossgate[0, :HEADS]
    query_sum, key_sum, value_sum, outw_sum = whole_call(
        attn_last_kernel,
        (),
        exchange([kept, sent], "z"),
        [((block_rows, inner), f32)] * 3 + [((inner, block_rows), f32)],
        "attn_last",
    )
    return (
        block_out,
        in_grad,
        ada_grad,
        norm_grads,
        query_sum,
        key_sum,
        value_sum,
        head_grads,
        textkey_sum,
        textvalue_sum,
        crossgate_grad,
        outw_sum,
        gate_sum_out,
        up_sum_out,
        down_sum_out,
    )


def solution(mesh):
    return jax.shard_map(
        shards,
        mesh=mesh,
        in_specs=(
            P(("dp", "tensor"), None),
            P(("dp", "tensor"), None),
            P("dp", None),
            P("dp", None, None),
            P("dp"),
            P("dp"),
            P(None, "tensor"),
            P(),
            P(None, "tensor"),
            P(None, "tensor"),
            P(None, "tensor"),
            P(),
            P(None, "tensor"),
            P(None, "tensor"),
            P("tensor"),
            P("tensor", None),
            P(None, "tensor"),
            P(None, "tensor"),
            P("tensor", None),
        ),
        out_specs=(
            P(("dp", "tensor"), None),
            P(("dp", "tensor"), None),
            P("dp", "tensor"),
            P(),
            P("dp", "tensor"),
            P("dp", "tensor"),
            P("dp", "tensor"),
            P(),
            P("dp", "tensor"),
            P("dp", "tensor"),
            P(),
            P("tensor", "dp"),
            P("dp", "tensor"),
            P("dp", "tensor"),
            P("tensor", "dp"),
        ),
        check_vma=False,
    )
```

```python
import functools
import math

import jax
import jax.numpy as jnp
from jax import lax
from jax.experimental import pallas as pl
from jax.experimental.pallas import tpu as pltpu
from jax.sharding import PartitionSpec as P

HEAD = 64
HEADS = 24
TXT = 256
SEGS = 3
EPS = 1e-06
LANES = 2 * HEAD
SHUT = 256.0
ROOT = HEAD ** (-0.5)
VMEM_LIMIT = 50 * 2**20
NO_COST = pl.CostEstimate(flops=0, bytes_accessed=0, transcendentals=0)


def cost_of(micros):
    return pl.CostEstimate(flops=int(micros * 1e9), bytes_accessed=0, transcendentals=0)


WIDE = 2 * LANES
TILES = 4
SUM_ROWS = 6
CROSS_MICROS = 10
BLOCK_IN_MICROS = 0
FFN_MICROS = 3
FFN_NEXT_MICROS = 8
MIDDLE_MICROS = 10
SELF_MICROS = 0
ATTN_MICROS = 0
STACK_MICROS = 20
TEXT_MICROS = 0
ATTN_FIRST_MICROS = 0

RING = 4
PAIR = 2
BLOCKS = RING * PAIR * RING
SLOTS = BLOCKS // RING
SEND_ORDER = (2, 1, 3, 0)
CORE_SWAP = [(0, 1), (1, 0), (2, 3), (3, 2)]
CHIP_SWAP = [(0, 2), (2, 0), (1, 3), (3, 1)]
ROW_ORDER = (0, 2, 1, 3)

def dp_index(x, z, y):
    return (x * PAIR + z) * RING + y


def dp_perm(axis, step):
    pairs = []
    for x in range(RING):
        for z in range(PAIR):
            for y in range(RING):
                for tensor in range(2 * PAIR):
                    way = axis
                    if axis in ("first", "second"):
                        way = "x" if (tensor % 2 == 0) == (axis == "first") else "y"
                    target = {
                        "x": ((x + step) % RING, z, y),
                        "y": (x, z, (y + step) % RING),
                        "z": (x, (z + step) % PAIR, y),
                    }[way]
                    pairs.append(
                        (
                            dp_index(x, z, y) * 2 * PAIR + tensor,
                            dp_index(*target) * 2 * PAIR + tensor,
                        )
                    )
    return pairs


def dp_permute(values, axis, step):
    return lax.ppermute(values, ("dp", "tensor"), dp_perm(axis, step))


def dp_spot(position):
    index = lax.axis_index("dp")
    x, z, y = index // (RING * PAIR), index // RING % PAIR, index % RING
    core = position % 2
    return jnp.stack([jnp.where(core == 0, x, y), z, jnp.where(core == 0, y, x), core])


def swap_core(values):
    return lax.ppermute(values, "tensor", CORE_SWAP)


def swap_chip(values):
    return lax.ppermute(values, "tensor", CHIP_SWAP)


def times_transpose(left, right):
    return lax.dot_general(
        left, right, (((1,), (1,)), ((), ())), preferred_element_type=jnp.float32
    )


def gather_tensor(block):
    far = swap_chip(block)
    near = swap_core(block)
    return [block, far, near, swap_core(far)]


def join_kernel(own, far, both, far_out):
    rows = own.shape[0]
    both[:rows, :] = own[...]
    both[rows:, :] = far[...]
    far_out[...] = far[...]


def gather_rows(block, ties=()):
    rows, width = block.shape
    near = swap_core(block)
    upper, far = whole_call(
        join_kernel,
        (),
        [block, swap_chip(block)],
        [((2 * rows, width), block.dtype), ((rows, width), block.dtype)],
        "join",
        ties,
    )
    return jnp.concatenate([upper, near, swap_core(far)], axis=0)


def scatter_tensor(upper, lower):
    near = swap_core(lower)
    rows = upper.shape[0] // 2
    far = (upper[rows:].astype(jnp.float32) + near[rows:].astype(jnp.float32)).astype(near.dtype)
    return [upper, near, swap_chip(far)], far


def turn_kernel(source, target):
    target[...] = source[...].T


def turned(values, ties=()):
    tile = 512 if values.shape[1] % 512 == 0 else values.shape[1]
    return pl.pallas_call(
        lambda source, *rest: turn_kernel(source, rest[-1]),
        grid=(values.shape[1] // tile,),
        in_specs=[pl.BlockSpec((values.shape[0], tile), lambda step: (0, step))]
        + [pl.BlockSpec(memory_space=pl.ANY)] * len(ties),
        out_specs=pl.BlockSpec((tile, values.shape[0]), lambda step: (step, 0)),
        out_shape=jax.ShapeDtypeStruct(values.shape[::-1], values.dtype),
        compiler_params=pltpu.CompilerParams(vmem_limit_bytes=VMEM_LIMIT),
        cost_estimate=NO_COST,
    )(values, *ties)


def chunk_block(offset, slot, spot):
    first = (spot[0] + offset) % RING
    z, second = slot // RING, slot % RING
    x = jnp.where(spot[3] == 0, first, second)
    y = jnp.where(spot[3] == 0, second, first)
    return dp_index(x, z, y)


def offset_of_step(offsets, step):
    offset = offsets[-1]
    for place in range(len(offsets) - 1):
        offset = jnp.where(step == place, offsets[place], offset)
    return offset


def chunk_kernel(make, offsets, halves, extra, outs, held, sems):
    step = pl.program_id(0)
    first, second = halves

    def copies(place):
        slot = held.at[place % 2]
        if offsets[place] != 2:
            return [pltpu.make_async_copy(slot, outs[place], sems.at[place % 2, 0])]
        return [
            pltpu.make_async_copy(slot.at[half], out, sems.at[place % 2, way])
            for way, (half, out) in enumerate(zip((first, second), outs[place]))
        ]

    for place, offset in enumerate(offsets):

        @pl.when(step == place)
        def _(place=place, offset=offset):
            if place >= 2:
                for copy in copies(place - 2):
                    copy.wait()
            added = {1: (first, extra[0]), 3: (second, extra[1])}.get(offset) if extra else None
            make(held.at[place % 2], added, offset)
            for copy in copies(place):
                copy.start()
            if place == len(offsets) - 1:
                for last in range(max(place - 1, 0), place + 1):
                    for copy in copies(last):
                        copy.wait()


def chunk_call(make, operands, specs, offsets, halves, shape, spot, extra, ties, name, micros):
    count = len(operands)
    pieces = []
    for offset in offsets:
        if offset == 2:
            pieces += [tuple(len(range(*s.indices(d))) for s, d in zip(h, shape)) for h in halves]
        else:
            pieces.append(shape)

    def kernel(spot_ref, *refs):
        inputs, extras = refs[:count], refs[count : count + len(extra)]
        outs = list(refs[-len(pieces) - 2 : -2])
        grouped = []
        for offset in offsets:
            grouped.append((outs.pop(0), outs.pop(0)) if offset == 2 else outs.pop(0))
        chunk_kernel(
            functools.partial(make, inputs), offsets, halves, extras, grouped, refs[-2], refs[-1]
        )

    found = pl.pallas_call(
        kernel,
        grid_spec=pltpu.PrefetchScalarGridSpec(
            num_scalar_prefetch=1,
            grid=(len(offsets),),
            in_specs=list(specs)
            + [pl.BlockSpec(part.shape, lambda step, spot: (0, 0)) for part in extra]
            + [pl.BlockSpec(memory_space=pl.ANY)] * len(ties),
            out_specs=[pl.BlockSpec(memory_space=pl.ANY)] * len(pieces),
            scratch_shapes=[
                pltpu.VMEM((2,) + shape, jnp.bfloat16),
                pltpu.SemaphoreType.DMA((2, 2)),
            ],
        ),
        out_shape=[jax.ShapeDtypeStruct(piece, jnp.bfloat16) for piece in pieces],
        compiler_params=pltpu.CompilerParams(vmem_limit_bytes=VMEM_LIMIT),
        cost_estimate=cost_of(micros),
        name=name,
    )(spot, *operands, *extra, *ties)
    found = list(found)
    return [
        (found.pop(0), found.pop(0)) if offset == 2 else found.pop(0) for offset in offsets
    ]


def make_rows(groups, inputs, slot, added, offset):
    lefts, rights = inputs[: SLOTS * len(groups)], inputs[SLOTS * len(groups) :]
    size = SLOTS * lefts[0].shape[1]
    if len(rights) > sum(groups):
        riders = rights[-1][...]
        count, half = riders.shape[0], riders.shape[1] // 2
        first, second = slice(size, size + count), slice(size + count, size + 2 * count)
        if offset == 2:
            for side in (slice(0, half), slice(half, 2 * half)):
                slot[first, side] = riders[:, :half]
                slot[second, side] = riders[:, half:]
        else:
            slot[first, :] = riders
            if offset == 1:
                slot[second, :half] = added[1][first, :]
                slot[second, half:] = added[1][second, :]
            else:
                slot[second, :] = riders
    column = place = 0
    for group, count in enumerate(groups):
        rows = jnp.concatenate(
            [left[0] for left in lefts[SLOTS * group : SLOTS * (group + 1)]], axis=0
        )
        for right in rights[place : place + count]:
            wide = right.shape[1]
            product = dot(rows, right[...])
            low, high = column, column
            if added is not None:
                low = min(max(column, added[0][1].start), column + wide)
                high = min(max(column, added[0][1].stop), column + wide)
            for start, stop in ((column, low), (low, high), (high, column + wide)):
                if start < stop:
                    part = product[:, start - column : stop - column]
                    if (start, stop) == (low, high):
                        base = added[0][1].start
                        part = part + added[1][:size, start - base : stop - base].astype(jnp.float32)
                    slot[:size, start:stop] = part.astype(jnp.bfloat16)
            column += wide
        place += count


def row_chunks(pairs, offsets, spot, extra=(), ties=(), micros=0, riders=()):
    lefts = [left.reshape(BLOCKS, left.shape[0] // BLOCKS, left.shape[1]) for left, _ in pairs]
    rights = [right for _, group in pairs for right in group]
    total = sum(right.shape[1] for right in rights)
    specs, operands = [], []
    for left in lefts:
        for slot in range(SLOTS):
            specs.append(
                pl.BlockSpec(
                    (1,) + left.shape[1:],
                    lambda step, spot, slot=slot: (
                        chunk_block(offset_of_step(offsets, step), slot, spot),
                        0,
                        0,
                    ),
                )
            )
            operands.append(left)
    specs += [pl.BlockSpec(right.shape, lambda step, spot: (0, 0)) for right in rights]
    specs += [pl.BlockSpec(part.shape, lambda step, spot: (0, 0)) for part in riders]
    rows = SLOTS * lefts[0].shape[1] + sum(2 * part.shape[0] for part in riders)
    halves = [(slice(0, rows), slice(0, total // 2)), (slice(0, rows), slice(total // 2, total))]
    return chunk_call(
        functools.partial(make_rows, [len(group) for _, group in pairs]),
        operands + rights + list(riders),
        specs,
        offsets,
        halves,
        (rows, total),
        spot,
        extra,
        ties,
        "row_chunks",
        micros,
    )


def make_columns(lefts, inputs, slot, added, offset):
    whole = jnp.concatenate([right[...] for right in inputs[lefts:]], axis=1)
    row = 0
    for left in inputs[:lefts]:
        product = dot(left[...], whole)
        if added is not None and added[0][0].start == row:
            product = product + added[1][...].astype(jnp.float32)
        slot[row : row + left.shape[0], :] = product.astype(jnp.bfloat16)
        row += left.shape[0]


def column_chunks(lefts, right, offsets, spot, extra=(), ties=(), micros=0):
    rows = lefts[0].shape[0]
    depth, columns = right.shape
    specs = [pl.BlockSpec(left.shape, lambda step, spot: (0, 0)) for left in lefts]
    for slot in range(SLOTS):
        specs.append(
            pl.BlockSpec(
                (depth, columns // BLOCKS),
                lambda step, spot, slot=slot: (
                    0,
                    chunk_block(offset_of_step(offsets, step), slot, spot),
                ),
            )
        )
    lanes = columns // RING
    halves = [(slice(0, rows), slice(0, lanes)), (slice(rows, 2 * rows), slice(0, lanes))]
    return chunk_call(
        functools.partial(make_columns, len(lefts)),
        list(lefts) + [right] * SLOTS,
        specs,
        offsets,
        halves,
        (2 * rows, lanes),
        spot,
        extra,
        ties,
        "column_chunks",
        micros,
    )


def add_up(refs, index):
    total = refs[0][index].astype(jnp.float32)
    for ref in refs[1:]:
        total = total + ref[index].astype(jnp.float32)
    return total


def lane_slice(start, size):
    return (slice(None), pl.ds(pl.multiple_of(start * size, size), size))


def both_second_kernel(spot, *refs):
    ffn, text, outs = refs[:3], refs[3:6], refs[6:]
    rows, lanes = ffn[0].shape[1], text[0].shape[1] // SLOTS
    for offset in range(RING):
        out = outs[offset]
        for z in range(PAIR):
            slot = z * RING + (spot[2] + offset) % RING
            block = add_up(ffn, slot).astype(jnp.bfloat16)
            pieces = block.shape[1] // WIDE
            for piece in range(pieces):
                start = (piece * PAIR + z) * rows
                out[start : start + rows, :] = block[:, piece * WIDE : (piece + 1) * WIDE]
            out[pieces * PAIR * rows :, z * lanes : (z + 1) * lanes] = add_up(
                text, lane_slice(slot, lanes)
            ).astype(jnp.bfloat16)


def both_third_kernel(rows, pieces, spot, *refs):
    parts = refs[:RING]
    lanes = WIDE // PAIR
    base = pieces * PAIR * rows
    for out, z in ((refs[-2], spot[1]), (refs[-1], (spot[1] + 1) % PAIR)):
        for piece in range(pieces):
            start = pl.multiple_of((piece * PAIR + z) * rows, 16)
            out[piece * rows : (piece + 1) * rows, :] = add_up(
                parts, (pl.ds(start, rows), slice(None))
            ).astype(jnp.bfloat16)
        index = (slice(base, None), pl.ds(pl.multiple_of(z * lanes, lanes), lanes))
        text = add_up(parts, index).astype(jnp.bfloat16)
        half = text.shape[0] // PAIR
        for side in range(PAIR):
            out[pieces * rows :, side * lanes : (side + 1) * lanes] = text[
                side * half : (side + 1) * half
            ]


def both_last_kernel(pieces, kept, got, gate, up, down, textkey, textvalue):
    total = kept[...].astype(jnp.float32) + got[...].astype(jnp.float32)
    rows, hidden = gate.shape
    lanes = WIDE // PAIR
    tile = total.shape[0] // TILES
    text = []
    for step in range(TILES):
        part = total[step * tile : (step + 1) * tile]
        for piece in range(pieces):
            column = (step * pieces + piece) * WIDE
            block = part[piece * rows : (piece + 1) * rows]
            place, start = column // hidden, column % hidden
            if place == 2:
                down[start : start + WIDE, :] = block.T
            else:
                (gate, up)[place][:, start : start + WIDE] = block
        rest = part[pieces * rows :]
        text += [rest[:, :lanes], rest[:, lanes:]]
    text = jnp.concatenate(text, axis=0)
    columns = textkey.shape[1]
    textkey[...] = text[:columns].T
    textvalue[...] = text[columns:].T


def attn_second_kernel(rows, spot, riders, *refs):
    parts, outs = refs[:-RING], refs[-RING:]
    size, count = SLOTS * rows, riders.shape[0]
    for offset in range(RING):
        for z in range(PAIR):
            slot = z * RING + (spot[2] + offset) % RING
            index = (pl.ds(pl.multiple_of(slot * rows, 16), rows), slice(None))
            outs[offset][z * rows : (z + 1) * rows, :] = add_up(parts, index).astype(jnp.bfloat16)
    ahead, behind = parts[1], parts[2]
    pairs = (
        (riders[...], ahead[size : size + count, :]),
        (behind[size : size + count, :], ahead[size + count : size + 2 * count, :]),
    )
    joined = [merge_rows(PAIR, first, second, rider_rows(2 * PAIR)) for first, second in pairs]
    joined = merge_rows(2 * PAIR, joined[0], joined[1], rider_rows(4 * PAIR))
    for out in outs:
        out[PAIR * rows :, :] = joined


def attn_third_kernel(spot, *refs):
    rows = refs[-1].shape[0]
    for out, z in ((refs[-2], spot[1]), (refs[-1], (spot[1] + 1) % PAIR)):
        index = (pl.ds(pl.multiple_of(z * rows, 16), rows), slice(None))
        out[...] = add_up(refs[:RING], index).astype(jnp.bfloat16)


def attn_last_kernel(kept, got, query, key, value, outw):
    total = kept[...].astype(jnp.float32) + got[...].astype(jnp.float32)
    columns = query.shape[1]
    for place, out in enumerate((query, key, value)):
        out[...] = total[:, place * columns : (place + 1) * columns]
    outw[...] = total[:, 3 * columns :].T


def whole_call(kernel, scalars, operands, outs, name, ties=(), scratch=(), micros=0):
    whole = pl.BlockSpec(memory_space=pltpu.VMEM)
    count = len(scalars) + len(operands)
    return pl.pallas_call(
        lambda *refs: kernel(*refs[:count], *refs[count + len(ties) :]),
        in_specs=[pl.BlockSpec(memory_space=pltpu.SMEM)] * len(scalars)
        + [whole] * len(operands)
        + [pl.BlockSpec(memory_space=pl.ANY)] * len(ties),
        out_specs=[whole] * len(outs),
        out_shape=[jax.ShapeDtypeStruct(shape, kind) for shape, kind in outs],
        scratch_shapes=list(scratch),
        compiler_params=pltpu.CompilerParams(vmem_limit_bytes=VMEM_LIMIT),
        cost_estimate=cost_of(micros),
        name=name,
    )(*scalars, *operands, *ties)


def tiled_call(kernel, scalars, operands, outs, name, axis, tiles, ties=(), micros=0, axes=None):
    def spec(shape, axis):
        block = list(shape)
        block[axis] //= tiles
        if axis == 0:
            return pl.BlockSpec(tuple(block), lambda step: (step,) + (0,) * (len(shape) - 1))
        return pl.BlockSpec(tuple(block), lambda step: (0,) * (len(shape) - 1) + (step,))

    count = len(scalars) + len(operands)
    return pl.pallas_call(
        lambda *refs: kernel(*refs[:count], *refs[count + len(ties) :]),
        grid=(tiles,),
        in_specs=[pl.BlockSpec(memory_space=pltpu.SMEM)] * len(scalars)
        + [spec(part.shape, way) for part, way in zip(operands, axes or [axis] * len(operands))]
        + [pl.BlockSpec(memory_space=pl.ANY)] * len(ties),
        out_specs=[spec(shape, axis) for shape, _ in outs],
        out_shape=[jax.ShapeDtypeStruct(shape, kind) for shape, kind in outs],
        compiler_params=pltpu.CompilerParams(vmem_limit_bytes=VMEM_LIMIT),
        cost_estimate=cost_of(micros),
        name=name,
    )(*scalars, *operands, *ties)


def exchange(chunks, axis):
    return [chunks[0]] + [
        dp_permute(chunks[step], axis, step) for step in range(1, len(chunks))
    ]


def one_on(halves):
    return dp_permute(halves[0], "first", 1), dp_permute(halves[1], "first", RING - 1)


def to_neighbours(own, ahead, behind):
    return [own, dp_permute(ahead, "first", 1), dp_permute(behind, "first", RING - 1)]


def by_slots(chunk):
    return chunk.reshape(SLOTS, chunk.shape[0] // SLOTS, chunk.shape[1])


def lane_index(shape):
    return lax.broadcasted_iota(jnp.int32, shape, 1)


def head_lanes(shape, head):
    lane = lane_index(shape)
    return (lane < HEAD) if head == 0 else (lane >= HEAD)


def per_head(values, reduce):
    first = head_lanes(values.shape, 0)
    left = jnp.sum(jnp.where(first, values, 0.0), axis=1, keepdims=True)
    right = jnp.sum(jnp.where(first, 0.0, values), axis=1, keepdims=True)
    return jnp.where(first, left, right)


def head_units(raw):
    inverse = lax.rsqrt(per_head(raw * raw, None) * (1.0 / HEAD) + EPS)
    return raw * inverse, inverse


def partner(values):
    lane = lane_index(values.shape)
    return jnp.where(
        lane % HEAD < HEAD // 2,
        pltpu.roll(values, LANES - HEAD // 2, 1),
        pltpu.roll(values, HEAD // 2, 1),
    )


def dot(left, right):
    return jnp.dot(left, right, preferred_element_type=jnp.float32)


def dot_t(left, right):
    return lax.dot_general(left, right, (((1,), (1,)), ((), ())), preferred_element_type=jnp.float32)


def attend_kernel(
    raw_q, raw_k, value, raw_t, text_value, cosine, sine, gains, gate, gate_swapped, mark_q, mark_k, mark_t,
    query_out, key_out, text_out, mixed_out, self_out, cross_out, self_log, cross_log,
):
    cos, sin = cosine[...], sine[...]
    unit = head_units(raw_q[...])[0] * gains[0:1, :]
    query = ((unit * cos + partner(unit) * sin).astype(jnp.bfloat16) * ROOT).astype(jnp.bfloat16)
    unit = head_units(raw_k[...])[0] * gains[1:2, :]
    key = (unit * cos + partner(unit) * sin).astype(jnp.bfloat16)
    text = (head_units(raw_t[...])[0] * gains[2:3, :]).astype(jnp.bfloat16)
    query_out[...] = query
    key_out[...] = key
    text_out[...] = text

    def attention(keys, marks, values):
        outs, sums = [], []
        for head in range(2):
            own = head_lanes(query.shape, head)
            own_keys = head_lanes(keys.shape, head)
            probe = jnp.where(own, query, mark_q[...])
            scores = dot_t(probe, jnp.where(own_keys, keys, marks))
            weights = jnp.exp(scores).astype(jnp.bfloat16)
            both = dot(weights, jnp.where(own_keys, values, jnp.ones_like(values)))
            outs.append(both)
        first = head_lanes(outs[0].shape, 0)
        product = jnp.where(first, outs[0], outs[1])
        total = jnp.where(first, outs[1], outs[0])
        return product / pltpu.roll(total, HEAD, 1), jnp.log(total)

    out, log = attention(key, mark_k[...], value[...])
    self_out[...] = out
    self_log[...] = log
    cross, log = attention(text, mark_t[...], text_value[...])
    cross_out[...] = cross
    cross_log[...] = log - jnp.log(gate_swapped[...])
    mixed_out[...] = (out + gate[...] * cross).astype(jnp.bfloat16)


def attention_grads(query, keys, marks, values, grad, out, log, mark_q):
    rows = grad.astype(jnp.float32)
    delta = per_head(rows * out, None)
    delta = pltpu.roll(delta, HEAD, 1)
    lane = lane_index(query.shape) % HEAD
    log_high = log.astype(jnp.bfloat16)
    log_low = (log - log_high.astype(jnp.float32)).astype(jnp.bfloat16)
    delta_high = delta.astype(jnp.bfloat16)
    delta_low = (delta - delta_high.astype(jnp.float32)).astype(jnp.bfloat16)
    zero = jnp.zeros_like(query)
    code = jnp.where(lane == 4, -log_high, jnp.where(lane == 5, -log_low, mark_q))
    shift = jnp.where(lane == 4, -delta_high, jnp.where(lane == 5, -delta_low, zero))
    key_grads, value_grads, query_grads = [], [], []
    for head in range(2):
        own = head_lanes(query.shape, head)
        own_keys = head_lanes(keys.shape, head)
        probe = jnp.where(own, query, code)
        probs = jnp.exp(dot_t(jnp.where(own_keys, keys, marks), probe))
        slope = dot_t(jnp.where(own_keys, values, marks), jnp.where(own, grad, shift))
        score_grad = (probs * slope).astype(jnp.bfloat16)
        value_grads.append(dot(probs.astype(jnp.bfloat16), grad))
        key_grads.append(dot(score_grad, query))
        turned = keys[:, head * HEAD : (head + 1) * HEAD].T
        query_grads.append(dot(turned, score_grad))
    first = head_lanes(keys.shape, 0)
    return (
        jnp.concatenate(query_grads, axis=0),
        jnp.where(first, key_grads[0], key_grads[1]),
        jnp.where(first, value_grads[0], value_grads[1]),
    )


def norm_back(weighted, unit, inverse):
    return inverse * (weighted - unit * (per_head(weighted * unit, None) * (1.0 / HEAD)))


def cross_back_kernel(
    query, text, text_value, raw_t, grad, out, log, gains, mark_q, mark_t,
    query_grad, raw_grad, value_grad, gain_sum, gate_sum,
):
    grad_q, grad_t, grad_v = attention_grads(
        query[...], text[...], mark_t[...], text_value[...], grad[...], out[...], log[...], mark_q[...]
    )
    query_grad[...] = grad_q.T
    value_grad[...] = grad_v.astype(jnp.bfloat16).T
    grad_t = grad_t.astype(jnp.bfloat16).astype(jnp.float32)
    unit, inverse = head_units(raw_t[...])
    gain_sum[...] = jnp.sum(grad_t * unit, axis=0, keepdims=True)
    raw_grad[...] = norm_back(grad_t * gains[2:3, :], unit, inverse).astype(jnp.bfloat16).T
    gate_sum[...] = jnp.sum(grad[...].astype(jnp.float32) * out[...], axis=0, keepdims=True)


def self_back_kernel(
    query, key, value, raw_q, raw_k, grad, out, log, cross_grad, cosine, sine, gains, mark_q, mark_k,
    query_grad, key_grad, value_grad, gain_sum,
):
    grad_q, grad_k, grad_v = attention_grads(
        query[...], key[...], mark_k[...], value[...], grad[...], out[...], log[...], mark_q[...]
    )
    value_grad[...] = grad_v.astype(jnp.bfloat16)
    cos, sin = cosine[...], sine[...]
    grad_q = (grad_q.T + cross_grad[...]) * ROOT
    for turn, raw, row, target in ((grad_q, raw_q, 0, query_grad), (grad_k, raw_k, 1, key_grad)):
        turn = turn.astype(jnp.bfloat16).astype(jnp.float32)
        turn = turn * cos - partner(turn) * sin
        unit, inverse = head_units(raw[...])
        gain_sum[row : row + 1, :] = jnp.sum(turn * unit, axis=0, keepdims=True)
        target[...] = norm_back(turn * gains[row : row + 1, :], unit, inverse).astype(jnp.bfloat16)


def pair_call(kernel, operands, outs, name, ties=(), micros=0):
    def spec(shape, cut):
        if cut is None:
            return pl.BlockSpec(shape, lambda pair: (0, 0))
        if cut == 1:
            return pl.BlockSpec((shape[0], LANES), lambda pair: (0, pair))
        return pl.BlockSpec((LANES, shape[1]), lambda pair: (pair, 0))

    width = outs[0][0][0] if outs[0][2] == 0 else outs[0][0][1]
    return pl.pallas_call(
        lambda *refs: kernel(*refs[: len(operands)], *refs[len(operands) + len(ties) :]),
        grid=(width // LANES,),
        in_specs=[spec(part.shape, cut) for part, cut in operands]
        + [pl.BlockSpec(memory_space=pl.ANY)] * len(ties),
        out_specs=[spec(shape, cut) for shape, _, cut in outs],
        out_shape=[jax.ShapeDtypeStruct(shape, kind) for shape, kind, _ in outs],
        compiler_params=pltpu.CompilerParams(vmem_limit_bytes=VMEM_LIMIT),
        cost_estimate=cost_of(micros),
        name=name,
    )(*[part for part, _ in operands], *ties)
def inverse_rms(values):
    return lax.rsqrt(jnp.mean(values * values, axis=-1, keepdims=True) + EPS)


def row_norm_back(weighted, unit, inverse):
    return inverse * (weighted - unit * jnp.mean(weighted * unit, axis=-1, keepdims=True))


def per_row(table, segment):
    return jnp.where(segment == 0.0, table[0:1], jnp.where(segment == 1.0, table[1:2], table[2:3]))


def total_of(parts):
    upper, near, far = parts
    rows = far.shape[0]
    return (
        upper[:rows].astype(jnp.float32) + near[:rows].astype(jnp.float32) + far[...].astype(jnp.float32)
    )


def segment_sums(member, values):
    high = values.astype(jnp.bfloat16)
    low = (values - high.astype(jnp.float32)).astype(jnp.bfloat16)
    return dot(member, high) + dot(member, low)


def tables_kernel(here, lens, gate, segments, head_gains, cosine, sine, mark_q, mark_k, mark_t,
                  segment, member, gate_lanes, gate_swapped, gains):
    heads = gains.shape[1] // HEAD
    lane = lane_index(gate_lanes.shape) // HEAD
    line = jnp.zeros(gate_lanes.shape, jnp.float32)
    swapped = line
    for head in range(heads):
        line = jnp.where(lane == head, gate[head], line)
        swapped = jnp.where(lane == head ^ 1, gate[head], swapped)
    gate_lanes[...] = jnp.tanh(line)
    gate_swapped[...] = jnp.tanh(swapped)
    gains[...] = jnp.concatenate([head_gains[...]] * heads, axis=1)
    rows = segments.shape[1]
    ids = segments[...]
    first = jnp.sum((ids < 1).astype(jnp.float32))
    second = jnp.sum((ids < 2).astype(jnp.float32))
    lane = lane_index((rows, LANES))
    half = HEAD // 2
    rate = jnp.exp((lane % half).astype(jnp.float32) * (-2.0 * math.log(10000.0) / HEAD))
    within = lane % HEAD
    for block, code in enumerate(ROW_ORDER):
        source = here[0] ^ code
        line = segments[pl.ds(source, 1), :].astype(jnp.float32)
        label = jnp.broadcast_to(line, (rows, rows)).T
        start = jnp.where(label == 0.0, 0.0, jnp.where(label == 1.0, first, second))
        token = (lax.broadcasted_iota(jnp.int32, (rows, LANES), 0) + source * rows).astype(jnp.float32)
        angle = (token - start) * rate
        index = slice(block * rows, (block + 1) * rows)
        cosine[index, :] = jnp.cos(angle)
        sine[index, :] = jnp.where(within < half, -1.0, 1.0) * jnp.sin(angle)
        same = ((label == within.astype(jnp.float32)) & (within < SEGS)).astype(jnp.float32)
        shut = (within == SEGS).astype(jnp.float32)
        ones = ((within >= SEGS) & (within < SEGS + 3)).astype(jnp.float32)
        mark_q[index, :] = (SHUT * same - SHUT * shut).astype(jnp.bfloat16)
        mark_k[index, :] = (same + ones).astype(jnp.bfloat16)
        if block == 0:
            segment[...] = label
            member[...] = (
                lax.broadcasted_iota(jnp.int32, (8, rows), 0).astype(jnp.float32) == line
            ).astype(jnp.bfloat16)
    for group in range(SEGS):
        lane = lane_index((TXT, LANES)) % HEAD
        row = lax.broadcasted_iota(jnp.int32, (TXT, LANES), 0)
        inside = ((lane == group) & (row < lens[group])).astype(jnp.float32)
        ones = ((lane >= SEGS) & (lane < SEGS + 3)).astype(jnp.float32)
        mark_t[group * TXT : (group + 1) * TXT, :] = (inside + ones).astype(jnp.bfloat16)


def text_kernel(captions, key_weight, value_weight, raw_out, value_out, raw_sum, value_sum):
    step = pl.program_id(0)

    @pl.when(step == 0)
    def _():
        raw_sum[...] = dot(captions[...], key_weight[...])
        value_sum[...] = dot(captions[...], value_weight[...])

    @pl.when(step > 0)
    def _():
        raw_sum[...] += dot(captions[...], key_weight[...])
        value_sum[...] += dot(captions[...], value_weight[...])

    @pl.when(step == pl.num_programs(0) - 1)
    def _():
        raw_out[...] = raw_sum[...]
        value_out[...] = value_sum[...].astype(jnp.bfloat16)


def text_call(captions, key_weight, value_weight):
    rows, depth = captions.shape
    columns = key_weight.shape[1]
    tile = depth // 4
    return pl.pallas_call(
        text_kernel,
        grid=(depth // tile,),
        in_specs=[
            pl.BlockSpec((rows, tile), lambda step: (0, step)),
            pl.BlockSpec((tile, columns), lambda step: (step, 0)),
            pl.BlockSpec((tile, columns), lambda step: (step, 0)),
        ],
        out_specs=[pl.BlockSpec((rows, columns), lambda step: (0, 0))] * 2,
        out_shape=[
            jax.ShapeDtypeStruct((rows, columns), jnp.float32),
            jax.ShapeDtypeStruct((rows, columns), jnp.bfloat16),
        ],
        scratch_shapes=[pltpu.VMEM((rows, columns), jnp.float32)] * 2,
        compiler_params=pltpu.CompilerParams(vmem_limit_bytes=VMEM_LIMIT),
        cost_estimate=cost_of(9),
        name="text",
    )(captions, key_weight, value_weight)


def project_kernel(here, own, far, near, last, mods, gains, segment_q, query_w, key_w, value_w,
                   rows_out, raw_q, raw_k, value):
    table = mods[here[0]]
    rows = own.shape[0]
    for block, part in enumerate((own, far, near, last)):
        index = slice(block * rows, (block + 1) * rows)
        values = part[...].astype(jnp.float32)
        marks = segment_q[index, :].astype(jnp.float32)
        scale = jnp.where(
            marks[:, 0:1] > 0.0, table[0:1], jnp.where(marks[:, 1:2] > 0.0, table[1:2], table[2:3])
        )
        rows_out[index, :] = (
            values * inverse_rms(values) * gains[0:1] * (1.0 + scale)
        ).astype(jnp.bfloat16)
    raw_q[...] = dot(rows_out[...], query_w[...])
    raw_k[...] = dot(rows_out[...], key_w[...])
    value[...] = dot(rows_out[...], value_w[...]).astype(jnp.bfloat16)


def middle_kernel(here, block, upper, near, far, mods, gains, segment, attn_out, middle_out, rows_out):
    attn_sum = total_of((upper, near, far))
    label = segment[:, 0:1]
    factor = jnp.tanh(per_row(mods[here[0] ^ 1], label)) * gains[1:2]
    middle = block[...].astype(jnp.float32) + factor * (attn_sum * inverse_rms(attn_sum))
    attn_out[...] = attn_sum
    middle_out[...] = middle
    scale = per_row(mods[here[0] ^ 2], label)
    rows_out[...] = (middle * inverse_rms(middle) * gains[2:3] * (1.0 + scale)).astype(jnp.bfloat16)


def block_out_kernel(here, middle, upper, near, far, grad, mods, gains, segment, member,
                     block_out, grad_out, sums):
    ffn_sum = total_of((upper, near, far))
    inverse = inverse_rms(ffn_sum)
    unit = ffn_sum * inverse
    factor = jnp.tanh(per_row(mods[here[0] ^ 3], segment[:, 0:1])) * gains[3:4]
    block_out[...] = (middle[...] + factor * unit).astype(jnp.bfloat16)
    incoming = grad[...].astype(jnp.float32)
    grad_out[...] = row_norm_back(incoming * factor, unit, inverse).astype(jnp.bfloat16)
    sums[...] = segment_sums(member[...], incoming * unit)


def middle_back_kernel(here, middle, attn, upper, near, far, grad, mods, gains, segment, member,
                       middle_grad, attn_grad, ffn_sums, attn_sums):
    grad_in = total_of((upper, near, far))
    label = segment[:, 0:1]
    inverse = inverse_rms(middle[...])
    unit = middle[...] * inverse
    factor = gains[2:3] * (1.0 + per_row(mods[here[0] ^ 2], label))
    ffn_sums[...] = segment_sums(member[...], grad_in * unit)
    grad_middle = grad[...].astype(jnp.float32) + row_norm_back(grad_in * factor, unit, inverse)
    middle_grad[...] = grad_middle
    inverse = inverse_rms(attn[...])
    unit = attn[...] * inverse
    factor = jnp.tanh(per_row(mods[here[0] ^ 1], label)) * gains[1:2]
    attn_grad[...] = row_norm_back(grad_middle * factor, unit, inverse).astype(jnp.bfloat16)
    attn_sums[...] = segment_sums(member[...], grad_middle * unit)


def block_in_kernel(here, block, middle_grad, upper, near, far, mods, gains, segment, member,
                    in_grad, sums):
    grad_in = total_of((upper, near, far))
    values = block[...].astype(jnp.float32)
    inverse = inverse_rms(values)
    unit = values * inverse
    factor = gains[0:1] * (1.0 + per_row(mods[here[0]], segment[:, 0:1]))
    in_grad[...] = (
        middle_grad[...] + row_norm_back(grad_in * factor, unit, inverse)
    ).astype(jnp.bfloat16)
    sums[...] = segment_sums(member[...], grad_in * unit)


def stack_sums_kernel(here, first, second, third, fourth, head_gain, text_gain, gate_sum, gate, out):
    width = out.shape[1]
    heads = jnp.concatenate([head_gain[0:1], head_gain[1:2], text_gain[...]], axis=1)
    inner = heads.shape[1] // 3
    gates = gate_sum[...] * (1.0 - gate[...] * gate[...])
    gates = jnp.concatenate([gates, jnp.zeros((1, width - inner), jnp.float32)], axis=1)
    lane = lane_index(gates.shape)
    moved = jnp.zeros_like(gates)
    for position in range(4):
        turn = pltpu.roll(gates, position * inner, 1) if position else gates
        moved = jnp.where((lane // inner == position) & (here[0] == position), turn, moved)
    out[...] = jnp.concatenate(
        [part[0:SEGS] for part in (first, second, third, fourth)]
        + [
            jnp.concatenate([heads, jnp.zeros((1, width - 3 * inner), jnp.float32)], axis=1),
            moved,
            jnp.zeros((2, width), jnp.float32),
        ],
        axis=0,
    )


def pack_kernel(here, own, far, near, last, mods, gains, cond, packed):
    total = own[...] + far[...] + near[...] + last[...]
    grad = jnp.zeros((SEGS, total.shape[1]), jnp.float32)
    rows = []
    for name in range(4):
        part = total[name * SEGS : (name + 1) * SEGS]
        mod = mods[here[0] ^ name]
        gain = gains[name : name + 1]
        if name % 2 == 1:
            factor = jnp.tanh(mod)
            slope = 1.0 - factor * factor
        else:
            factor = 1.0 + mod
            slope = jnp.ones_like(mod)
        rows.append(jnp.sum(part * factor, axis=0, keepdims=True))
        mine = (jnp.zeros(part.shape, jnp.int32) + here[0]) == name
        grad = jnp.where(mine, part * slope * gain, grad)
    rows.append(total[4 * SEGS : 4 * SEGS + 2])
    rows = jnp.concatenate(rows, axis=0)
    high = rows.astype(jnp.bfloat16).astype(jnp.float32)
    pad = jnp.zeros((packed.shape[0] - 2 * SEGS - 2 * SUM_ROWS, total.shape[1]), jnp.float32)
    packed[...] = jnp.concatenate(
        [grad, cond[...].astype(jnp.float32), high, rows - high, pad], axis=0
    ).astype(jnp.bfloat16)


def rider_rows(count):
    return -(-(2 * SEGS * count + 2 * SUM_ROWS) // 16) * 16


def merge_rows(count, first, second, size):
    first, second = first.astype(jnp.float32), second.astype(jnp.float32)
    wide = SEGS * count
    start = 2 * wide
    sums = (
        first[start : start + SUM_ROWS]
        + first[start + SUM_ROWS : start + 2 * SUM_ROWS]
        + second[start : start + SUM_ROWS]
        + second[start + SUM_ROWS : start + 2 * SUM_ROWS]
    )
    high = sums.astype(jnp.bfloat16).astype(jnp.float32)
    pieces = [first[:wide], second[:wide], first[wide:start], second[wide:start], high, sums - high]
    rest = size - 4 * wide - 2 * SUM_ROWS
    if rest:
        pieces.append(jnp.zeros((rest, first.shape[1]), jnp.float32))
    return jnp.concatenate(pieces, axis=0).astype(jnp.bfloat16)


def merge_kernel(ours, theirs, out):
    out[...] = merge_rows(1, ours[...], theirs[...], out.shape[0])


def ada_kernel(count, heads, dp, own, *refs):
    parts = (own,) + refs[:3]
    ada_out, norm_out, head_out, gate_out = refs[3:]
    wide = SEGS * count
    base = own.shape[0] - rider_rows(count)
    columns = ada_out.shape[0]
    share = LANES // columns
    start = pl.multiple_of(dp[0] // share * LANES, LANES)
    grads, conds = [], []
    sums = jnp.zeros((SUM_ROWS, own.shape[1]), jnp.float32)
    for part in parts:
        rows = part[base:, :].astype(jnp.float32)
        grads.append(rows[:wide])
        conds.append(part[base:, pl.ds(start, LANES)].astype(jnp.float32)[wide : 2 * wide])
        for half in range(2):
            place = 2 * wide + half * SUM_ROWS
            sums = sums + rows[place : place + SUM_ROWS]
    conds = jnp.concatenate(conds, axis=0)
    conds = pltpu.roll(conds, (LANES - dp[0] % share * columns) % LANES, 1)
    acts = conds / (1.0 + jnp.exp(-conds))
    ada_out[...] = dot(
        acts.astype(jnp.bfloat16).astype(jnp.float32).T.astype(jnp.bfloat16),
        jnp.concatenate(grads, axis=0).astype(jnp.bfloat16),
    )[:columns]
    norm_out[...] = sums[:4]
    inner = heads * HEAD
    for row in range(3):
        line = jnp.zeros((1, HEAD), jnp.float32)
        for head in range(heads):
            place = row * inner + head * HEAD
            line = line + sums[4:5, place : place + HEAD]
        head_out[row : row + 1, :] = line
    lane = lane_index((1, LANES))
    line = jnp.zeros((1, LANES), jnp.float32)
    for head in range(HEADS):
        value = jnp.sum(sums[5:6, head * HEAD : (head + 1) * HEAD], axis=1, keepdims=True)
        line = jnp.where(lane == head, value, line)
    gate_out[...] = line


def shards(
    block_in,
    out_grad,
    condition,
    captions,
    caption_len,
    segment_ids,
    ada_weight,
    norm_gains,
    query_weight,
    key_weight,
    value_weight,
    head_gains,
    textkey_weight,
    textvalue_weight,
    cross_gate,
    out_weight,
    gate_weight,
    up_weight,
    down_weight,
):
    rows, width = block_in.shape
    length = segment_ids.shape[0]
    heads = cross_gate.shape[0]
    inner = heads * HEAD
    half_rows = length // 2
    position = lax.axis_index("tensor")
    spot = dp_spot(position)
    here = position.reshape(1)
    b16, f32 = jnp.bfloat16, jnp.float32

    blocks = gather_tensor(block_in)
    cond_rows = jnp.pad(condition, ((0, 0), (0, width - condition.shape[1])))
    own_act = jax.nn.silu(condition.astype(f32)).astype(b16)
    own_part = jnp.dot(own_act, ada_weight, preferred_element_type=f32)
    parts = gather_tensor(own_part)
    mods = jnp.stack([parts[ROW_ORDER.index(code)] for code in range(4)])

    cosine, sine, mark_q, mark_k, mark_t, segment, member, gate_lanes, gate_swapped, gains = whole_call(
        tables_kernel,
        (here, caption_len, cross_gate),
        [segment_ids.reshape(length // rows, rows), head_gains],
        [((length, LANES), f32)] * 2
        + [((length, LANES), b16)] * 2
        + [((SEGS * TXT, LANES), b16), ((rows, LANES), f32), ((8, rows), b16)]
        + [((1, inner), f32)] * 2
        + [((3, inner), f32)],
        "tables",
        micros=2,
    )
    caption_flat = captions.reshape(-1, captions.shape[-1])
    texts = caption_flat.shape[0]
    raw_t, text_value = text_call(caption_flat, textkey_weight, textvalue_weight)
    attn_rows, raw_q, raw_k, value = whole_call(
        project_kernel,
        (here,),
        blocks + [mods, norm_gains, mark_q, query_weight, key_weight, value_weight],
        [((length, width), b16), ((length, inner), f32), ((length, inner), f32), ((length, inner), b16)],
        "project",
        micros=6,
    )
    query, key, text, mixed, self_out, cross_out, self_log, cross_log = pair_call(
        attend_kernel,
        [(raw_q, 1), (raw_k, 1), (value, 1), (raw_t, 1), (text_value, 1), (cosine, None), (sine, None)]
        + [(gains, 1), (gate_lanes, 1), (gate_swapped, 1), (mark_q, None), (mark_k, None), (mark_t, None)],
        [((length, inner), b16, 1)] * 2
        + [((texts, inner), b16, 1), ((length, inner), b16, 1)]
        + [((length, inner), f32, 1)] * 4,
        "attend",
        micros=11,
    )

    def halves(product):
        return product(slice(0, half_rows)).astype(b16), product(slice(half_rows, None)).astype(b16)

    def all_of(block):
        return jnp.concatenate(gather_tensor(block), axis=0)

    upper, lower = halves(lambda part: jnp.dot(mixed[part], out_weight, preferred_element_type=f32))
    sums, sent = scatter_tensor(upper, lower)
    attn_rows_t = turned(attn_rows, (sent,))
    wide = ((rows, width), f32)
    narrow = ((rows, width), b16)
    totals = ((8, width), f32)
    attn_sum, middle, ffn_own = whole_call(
        middle_kernel,
        (here,),
        [block_in] + sums + [mods, norm_gains, segment],
        [wide, wide, narrow],
        "middle",
    )
    ffn_rows = all_of(ffn_own)
    gate_pre = jnp.dot(ffn_rows, gate_weight, preferred_element_type=f32)
    up_pre = jnp.dot(ffn_rows, up_weight, preferred_element_type=f32)
    sigmoid_gate = jax.nn.sigmoid(gate_pre)
    silu_gate = gate_pre * sigmoid_gate
    hidden = (silu_gate * up_pre).astype(b16)
    upper, lower = halves(lambda part: jnp.dot(hidden[part], down_weight, preferred_element_type=f32))
    sums, sent = scatter_tensor(upper, lower)
    ffn_rows_t = turned(ffn_rows, (sent,))
    block_out, grad_own, sum_gate_ffn = whole_call(
        block_out_kernel,
        (here,),
        [middle] + sums + [out_grad, mods, norm_gains, segment, member],
        [narrow, narrow, totals],
        "block_out",
    )

    grad_ffn = all_of(grad_own)
    grad_hidden = times_transpose(grad_ffn, down_weight)
    grad_gate = (
        grad_hidden * up_pre * sigmoid_gate * (1.0 + gate_pre * (1.0 - sigmoid_gate))
    ).astype(b16)
    grad_up = (grad_hidden * silu_gate).astype(b16)
    upper, lower = halves(
        lambda part: times_transpose(grad_gate[part], gate_weight)
        + times_transpose(grad_up[part], up_weight)
    )
    sums, sent = scatter_tensor(upper, lower)
    grad_ffn_t = turned(grad_ffn, (sent,))
    ffn_pairs = [(ffn_rows_t, [grad_gate, grad_up]), (grad_ffn_t, [hidden])]
    (halves_two,) = row_chunks(ffn_pairs, (2,), spot, ties=(sent,), micros=FFN_MICROS)
    ffn_passed = one_on(halves_two)
    grad_middle, grad_own, sum_scale_ffn, sum_gate_attn = whole_call(
        middle_back_kernel,
        (here,),
        [middle, attn_sum] + sums + [out_grad, mods, norm_gains, segment, member],
        [wide, narrow, totals, totals],
        "middle_back",
        micros=MIDDLE_MICROS,
    )

    grad_attn = all_of(grad_own)
    grad_mixed = times_transpose(grad_attn, out_weight).astype(b16)
    cross_grad, text_grad, text_value_grad, text_gain, gate_sum = pair_call(
        cross_back_kernel,
        [(query, 1), (text, 1), (text_value, 1), (raw_t, 1), (grad_mixed, 1), (cross_out, 1)]
        + [(cross_log, 1), (gains, 1), (mark_q, None), (mark_t, None)],
        [((length, inner), f32, 1), ((inner, texts), b16, 0), ((inner, texts), b16, 0)]
        + [((1, inner), f32, 1)] * 2,
        "cross_back",
        micros=CROSS_MICROS,
    )
    text_lefts = [text_grad, text_value_grad]
    (halves_two,) = column_chunks(text_lefts, caption_flat, (2,), spot)
    text_passed = one_on(halves_two)
    query_grad, key_grad, value_grad, head_gain = pair_call(
        self_back_kernel,
        [(query, 1), (key, 1), (value, 1), (raw_q, 1), (raw_k, 1), (grad_mixed, 1), (self_out, 1)]
        + [(self_log, 1), (cross_grad, 1), (cosine, None), (sine, None), (gains, 1)]
        + [(mark_q, None), (mark_k, None)],
        [((length, inner), b16, 1)] * 3 + [((2, inner), f32, 1)],
        "self_back",
        (halves_two[0],),
        micros=SELF_MICROS,
    )

    hidden_cols = hidden.shape[1]
    block_rows = width // BLOCKS
    upper, lower = halves(
        lambda part: times_transpose(query_grad[part], query_weight)
        + times_transpose(key_grad[part], key_weight)
        + times_transpose(value_grad[part], value_weight)
    )
    sums, sent = scatter_tensor(upper, lower)
    ffn_one, ffn_three, ffn_kept = row_chunks(
        ffn_pairs, (1, 3, 0), spot, extra=ffn_passed, ties=(sent,), micros=FFN_NEXT_MICROS
    )
    in_grad, sum_scale_attn = whole_call(
        block_in_kernel,
        (here,),
        [block_in, grad_middle] + sums + [mods, norm_gains, segment, member],
        [narrow, totals],
        "block_in",
        (ffn_kept,),
        micros=BLOCK_IN_MICROS,
    )
    (stacked,) = whole_call(
        stack_sums_kernel,
        (here,),
        [sum_scale_attn, sum_gate_attn, sum_scale_ffn, sum_gate_ffn]
        + [head_gain, text_gain, gate_sum, gate_lanes],
        [((16, width), f32)],
        "stack_sums",
        micros=STACK_MICROS,
    )
    stacked = gather_tensor(stacked)
    (riders,) = whole_call(
        pack_kernel,
        (here,),
        stacked + [mods, norm_gains, cond_rows],
        [((rider_rows(1), width), b16)],
        "pack",
    )
    theirs = dp_permute(riders, "z", 1)
    (riders,) = whole_call(
        merge_kernel, (), [riders, theirs], [((rider_rows(PAIR), width), b16)], "merge"
    )
    attn_pairs = [
        (attn_rows_t, [query_grad, key_grad, value_grad]),
        (turned(grad_attn, (halves_two[0],)), [mixed]),
    ]
    (halves_two,) = row_chunks(attn_pairs, (2,), spot, riders=(riders,), micros=ATTN_FIRST_MICROS)
    attn_passed = one_on(halves_two)
    text_one, text_three, text_kept = column_chunks(
        text_lefts, caption_flat, (1, 3, 0), spot, extra=text_passed, ties=(halves_two[0],), micros=TEXT_MICROS
    )
    text_rows = caption_flat.shape[1] // BLOCKS
    attn_one, attn_three, attn_kept = row_chunks(
        attn_pairs, (1, 3, 0), spot, extra=attn_passed, ties=(text_kept,), riders=(riders,), micros=ATTN_MICROS
    )
    pieces = 3 * hidden_cols // (TILES * WIDE)
    tile = pieces * PAIR * block_rows + 2 * inner // TILES
    stage = tiled_call(
        both_second_kernel,
        (spot,),
        [by_slots(part) for part in to_neighbours(ffn_kept, ffn_one, ffn_three)]
        + to_neighbours(text_kept, text_one, text_three),
        [((TILES * tile, WIDE), b16)] * RING,
        "both_second",
        0,
        TILES,
        (attn_kept,),
        axes=[-1] * 3 + [0] * 3,
    )
    kept, sent = tiled_call(
        functools.partial(both_third_kernel, block_rows, pieces),
        (spot,),
        exchange(stage, "second"),
        [((TILES * tile // PAIR, WIDE), b16)] * 2,
        "both_third",
        0,
        TILES,
    )
    gate_sum_out, up_sum_out, down_sum_out, textkey_sum, textvalue_sum = whole_call(
        functools.partial(both_last_kernel, pieces),
        (),
        exchange([kept, sent], "z"),
        [((block_rows, hidden_cols), f32)] * 2
        + [((hidden_cols, block_rows), f32)]
        + [((text_rows, inner), f32)] * 2,
        "both_last",
    )
    stage = tiled_call(
        functools.partial(attn_second_kernel, block_rows),
        (spot,),
        [riders] + to_neighbours(attn_kept, attn_one, attn_three),
        [((PAIR * block_rows + rider_rows(4 * PAIR), width), b16)] * RING,
        "attn_second",
        -1,
        4,
        (kept,),
    )
    got = exchange(stage, "second")
    kept, sent = tiled_call(
        attn_third_kernel, (spot,), got, [((block_rows, width), b16)] * 2, "attn_third",
        -1,
        2
    )
    ada_grad, norm_grads, head_grads, crossgate = tiled_call(
        functools.partial(ada_kernel, 4 * PAIR, heads),
        (lax.axis_index("dp").reshape(1),),
        got,
        [((condition.shape[1] // BLOCKS, width), f32), ((4, width), f32), ((3, HEAD), f32)]
        + [((1, LANES), f32)],
        "ada",
        0,
        1,
        (kept,),
    )
    crossgate_grad = crossgate[0, :HEADS]
    query_sum, key_sum, value_sum, outw_sum = whole_call(
        attn_last_kernel,
        (),
        exchange([kept, sent], "z"),
        [((block_rows, inner), f32)] * 3 + [((inner, block_rows), f32)],
        "attn_last",
    )
    return (
        block_out,
        in_grad,
        ada_grad,
        norm_grads,
        query_sum,
        key_sum,
        value_sum,
        head_grads,
        textkey_sum,
        textvalue_sum,
        crossgate_grad,
        outw_sum,
        gate_sum_out,
        up_sum_out,
        down_sum_out,
    )


def solution(mesh):
    return jax.shard_map(
        shards,
        mesh=mesh,
        in_specs=(
            P(("dp", "tensor"), None),
            P(("dp", "tensor"), None),
            P("dp", None),
            P("dp", None, None),
            P("dp"),
            P("dp"),
            P(None, "tensor"),
            P(),
            P(None, "tensor"),
            P(None, "tensor"),
            P(None, "tensor"),
            P(),
            P(None, "tensor"),
            P(None, "tensor"),
            P("tensor"),
            P("tensor", None),
            P(None, "tensor"),
            P(None, "tensor"),
            P("tensor", None),
        ),
        out_specs=(
            P(("dp", "tensor"), None),
            P(("dp", "tensor"), None),
            P("dp", "tensor"),
            P(),
            P("dp", "tensor"),
            P("dp", "tensor"),
            P("dp", "tensor"),
            P(),
            P("dp", "tensor"),
            P("dp", "tensor"),
            P(),
            P("tensor", "dp"),
            P("dp", "tensor"),
            P("dp", "tensor"),
            P("tensor", "dp"),
        ),
        check_vma=False,
    )
```

```python
import functools
import math

import jax
import jax.numpy as jnp
from jax import lax
from jax.experimental import pallas as pl
from jax.experimental.pallas import tpu as pltpu
from jax.sharding import PartitionSpec as P

HEAD = 64
HEADS = 24
TXT = 256
SEGS = 3
EPS = 1e-06
LANES = 2 * HEAD
SHUT = 256.0
ROOT = HEAD ** (-0.5)
VMEM_LIMIT = 50 * 2**20
NO_COST = pl.CostEstimate(flops=0, bytes_accessed=0, transcendentals=0)


def cost_of(micros):
    return pl.CostEstimate(flops=int(micros * 1e9), bytes_accessed=0, transcendentals=0)


SUM_ROWS = 6
CROSS_MICROS = 10
BLOCK_IN_MICROS = 0
FFN_MICROS = 3
FFN_NEXT_MICROS = 8
MIDDLE_MICROS = 10
SELF_MICROS = 0
ATTN_MICROS = 7
ATTN_FIRST_MICROS = 0

RING = 4
PAIR = 2
BLOCKS = RING * PAIR * RING
SLOTS = BLOCKS // RING
SEND_ORDER = (2, 1, 3, 0)
CORE_SWAP = [(0, 1), (1, 0), (2, 3), (3, 2)]
CHIP_SWAP = [(0, 2), (2, 0), (1, 3), (3, 1)]
ROW_ORDER = (0, 2, 1, 3)

def dp_index(x, z, y):
    return (x * PAIR + z) * RING + y


def dp_perm(axis, step):
    pairs = []
    for x in range(RING):
        for z in range(PAIR):
            for y in range(RING):
                for tensor in range(2 * PAIR):
                    way = axis
                    if axis in ("first", "second"):
                        way = "x" if (tensor % 2 == 0) == (axis == "first") else "y"
                    target = {
                        "x": ((x + step) % RING, z, y),
                        "y": (x, z, (y + step) % RING),
                        "z": (x, (z + step) % PAIR, y),
                    }[way]
                    pairs.append(
                        (
                            dp_index(x, z, y) * 2 * PAIR + tensor,
                            dp_index(*target) * 2 * PAIR + tensor,
                        )
                    )
    return pairs


def dp_permute(values, axis, step):
    return lax.ppermute(values, ("dp", "tensor"), dp_perm(axis, step))


def dp_spot(position):
    index = lax.axis_index("dp")
    x, z, y = index // (RING * PAIR), index // RING % PAIR, index % RING
    core = position % 2
    return jnp.stack([jnp.where(core == 0, x, y), z, jnp.where(core == 0, y, x), core])


def swap_core(values):
    return lax.ppermute(values, "tensor", CORE_SWAP)


def swap_chip(values):
    return lax.ppermute(values, "tensor", CHIP_SWAP)


def times_transpose(left, right):
    return lax.dot_general(
        left, right, (((1,), (1,)), ((), ())), preferred_element_type=jnp.float32
    )


def gather_tensor(block):
    far = swap_chip(block)
    near = swap_core(block)
    return [block, far, near, swap_core(far)]


def scatter_tensor(upper, lower):
    near = swap_core(lower)
    rows = upper.shape[0] // 2
    far = (upper[rows:].astype(jnp.float32) + near[rows:].astype(jnp.float32)).astype(near.dtype)
    return [upper, near, swap_chip(far)], far


def turn_kernel(source, target):
    target[...] = source[...].T


def turned(values, ties=()):
    tile = 512 if values.shape[1] % 512 == 0 else values.shape[1]
    return pl.pallas_call(
        lambda source, *rest: turn_kernel(source, rest[-1]),
        grid=(values.shape[1] // tile,),
        in_specs=[pl.BlockSpec((values.shape[0], tile), lambda step: (0, step))]
        + [pl.BlockSpec(memory_space=pl.ANY)] * len(ties),
        out_specs=pl.BlockSpec((tile, values.shape[0]), lambda step: (step, 0)),
        out_shape=jax.ShapeDtypeStruct(values.shape[::-1], values.dtype),
        compiler_params=pltpu.CompilerParams(vmem_limit_bytes=VMEM_LIMIT),
        cost_estimate=NO_COST,
    )(values, *ties)


def chunk_block(offset, slot, spot):
    first = (spot[0] + offset) % RING
    z, second = slot // RING, slot % RING
    x = jnp.where(spot[3] == 0, first, second)
    y = jnp.where(spot[3] == 0, second, first)
    return dp_index(x, z, y)


def offset_of_step(offsets, step):
    offset = offsets[-1]
    for place in range(len(offsets) - 1):
        offset = jnp.where(step == place, offsets[place], offset)
    return offset


def chunk_kernel(make, offsets, halves, extra, outs, held, sems):
    step = pl.program_id(0)
    first, second = halves

    def copies(place):
        slot = held.at[place % 2]
        if offsets[place] != 2:
            return [pltpu.make_async_copy(slot, outs[place], sems.at[place % 2, 0])]
        return [
            pltpu.make_async_copy(slot.at[half], out, sems.at[place % 2, way])
            for way, (half, out) in enumerate(zip((first, second), outs[place]))
        ]

    for place, offset in enumerate(offsets):

        @pl.when(step == place)
        def _(place=place, offset=offset):
            if place >= 2:
                for copy in copies(place - 2):
                    copy.wait()
            added = {1: (first, extra[0]), 3: (second, extra[1])}.get(offset) if extra else None
            make(held.at[place % 2], added, offset)
            for copy in copies(place):
                copy.start()
            if place == len(offsets) - 1:
                for last in range(max(place - 1, 0), place + 1):
                    for copy in copies(last):
                        copy.wait()


def chunk_call(make, operands, specs, offsets, halves, shape, spot, extra, ties, name, micros):
    count = len(operands)
    pieces = []
    for offset in offsets:
        if offset == 2:
            pieces += [tuple(len(range(*s.indices(d))) for s, d in zip(h, shape)) for h in halves]
        else:
            pieces.append(shape)

    def kernel(spot_ref, *refs):
        inputs, extras = refs[:count], refs[count : count + len(extra)]
        outs = list(refs[-len(pieces) - 2 : -2])
        grouped = []
        for offset in offsets:
            grouped.append((outs.pop(0), outs.pop(0)) if offset == 2 else outs.pop(0))
        chunk_kernel(
            functools.partial(make, inputs), offsets, halves, extras, grouped, refs[-2], refs[-1]
        )

    found = pl.pallas_call(
        kernel,
        grid_spec=pltpu.PrefetchScalarGridSpec(
            num_scalar_prefetch=1,
            grid=(len(offsets),),
            in_specs=list(specs)
            + [pl.BlockSpec(part.shape, lambda step, spot: (0, 0)) for part in extra]
            + [pl.BlockSpec(memory_space=pl.ANY)] * len(ties),
            out_specs=[pl.BlockSpec(memory_space=pl.ANY)] * len(pieces),
            scratch_shapes=[
                pltpu.VMEM((2,) + shape, jnp.bfloat16),
                pltpu.SemaphoreType.DMA((2, 2)),
            ],
        ),
        out_shape=[jax.ShapeDtypeStruct(piece, jnp.bfloat16) for piece in pieces],
        compiler_params=pltpu.CompilerParams(vmem_limit_bytes=VMEM_LIMIT),
        cost_estimate=cost_of(micros),
        name=name,
    )(spot, *operands, *extra, *ties)
    found = list(found)
    return [
        (found.pop(0), found.pop(0)) if offset == 2 else found.pop(0) for offset in offsets
    ]


def make_rows(groups, inputs, slot, added, offset):
    lefts, rights = inputs[: SLOTS * len(groups)], inputs[SLOTS * len(groups) :]
    size = SLOTS * lefts[0].shape[1]
    if len(rights) > sum(groups):
        riders = rights[-1][...]
        count, half = riders.shape[0], riders.shape[1] // 2
        first, second = slice(size, size + count), slice(size + count, size + 2 * count)
        if offset == 2:
            for side in (slice(0, half), slice(half, 2 * half)):
                slot[first, side] = riders[:, :half]
                slot[second, side] = riders[:, half:]
        else:
            slot[first, :] = riders
            if offset == 1:
                slot[second, :half] = added[1][first, :]
                slot[second, half:] = added[1][second, :]
            else:
                slot[second, :] = riders
    column = place = 0
    for group, count in enumerate(groups):
        rows = jnp.concatenate(
            [left[0] for left in lefts[SLOTS * group : SLOTS * (group + 1)]], axis=0
        )
        for right in rights[place : place + count]:
            wide = right.shape[1]
            product = dot(rows, right[...])
            low, high = column, column
            if added is not None:
                low = min(max(column, added[0][1].start), column + wide)
                high = min(max(column, added[0][1].stop), column + wide)
            for start, stop in ((column, low), (low, high), (high, column + wide)):
                if start < stop:
                    part = product[:, start - column : stop - column]
                    if (start, stop) == (low, high):
                        base = added[0][1].start
                        part = part + added[1][:size, start - base : stop - base].astype(jnp.float32)
                    slot[:size, start:stop] = part.astype(jnp.bfloat16)
            column += wide
        place += count


def row_chunks(pairs, offsets, spot, extra=(), ties=(), micros=0, riders=()):
    lefts = [left.reshape(BLOCKS, left.shape[0] // BLOCKS, left.shape[1]) for left, _ in pairs]
    rights = [right for _, group in pairs for right in group]
    total = sum(right.shape[1] for right in rights)
    specs, operands = [], []
    for left in lefts:
        for slot in range(SLOTS):
            specs.append(
                pl.BlockSpec(
                    (1,) + left.shape[1:],
                    lambda step, spot, slot=slot: (
                        chunk_block(offset_of_step(offsets, step), slot, spot),
                        0,
                        0,
                    ),
                )
            )
            operands.append(left)
    specs += [pl.BlockSpec(right.shape, lambda step, spot: (0, 0)) for right in rights]
    specs += [pl.BlockSpec(part.shape, lambda step, spot: (0, 0)) for part in riders]
    rows = SLOTS * lefts[0].shape[1] + sum(2 * part.shape[0] for part in riders)
    halves = [(slice(0, rows), slice(0, total // 2)), (slice(0, rows), slice(total // 2, total))]
    return chunk_call(
        functools.partial(make_rows, [len(group) for _, group in pairs]),
        operands + rights + list(riders),
        specs,
        offsets,
        halves,
        (rows, total),
        spot,
        extra,
        ties,
        "row_chunks",
        micros,
    )


def make_columns(lefts, inputs, slot, added, offset):
    whole = jnp.concatenate([right[...] for right in inputs[lefts:]], axis=1)
    row = 0
    for left in inputs[:lefts]:
        product = dot(left[...], whole)
        if added is not None and added[0][0].start == row:
            product = product + added[1][...].astype(jnp.float32)
        slot[row : row + left.shape[0], :] = product.astype(jnp.bfloat16)
        row += left.shape[0]


def column_chunks(lefts, right, offsets, spot, extra=(), ties=(), micros=0):
    rows = lefts[0].shape[0]
    depth, columns = right.shape
    specs = [pl.BlockSpec(left.shape, lambda step, spot: (0, 0)) for left in lefts]
    for slot in range(SLOTS):
        specs.append(
            pl.BlockSpec(
                (depth, columns // BLOCKS),
                lambda step, spot, slot=slot: (
                    0,
                    chunk_block(offset_of_step(offsets, step), slot, spot),
                ),
            )
        )
    lanes = columns // RING
    halves = [(slice(0, rows), slice(0, lanes)), (slice(rows, 2 * rows), slice(0, lanes))]
    return chunk_call(
        functools.partial(make_columns, len(lefts)),
        list(lefts) + [right] * SLOTS,
        specs,
        offsets,
        halves,
        (2 * rows, lanes),
        spot,
        extra,
        ties,
        "column_chunks",
        micros,
    )


def add_up(refs, index):
    total = refs[0][index].astype(jnp.float32)
    for ref in refs[1:]:
        total = total + ref[index].astype(jnp.float32)
    return total


def lane_slice(start, size):
    return (slice(None), pl.ds(pl.multiple_of(start * size, size), size))


def ffn_second_kernel(spot, *refs):
    parts, outs = refs[:-RING], refs[-RING:]
    for offset in range(RING):
        for z in range(PAIR):
            slot = z * RING + (spot[2] + offset) % RING
            outs[offset][z] = add_up(parts, slot).astype(jnp.bfloat16)


def ffn_third_kernel(spot, *refs):
    for out, z in ((refs[-2], spot[1]), (refs[-1], (spot[1] + 1) % PAIR)):
        out[...] = add_up(refs[:RING], z).astype(jnp.bfloat16)


def ffn_last_kernel(kept, got, gate_out, up_out, down_out):
    total = kept[...].astype(jnp.float32) + got[...].astype(jnp.float32)
    hidden = gate_out.shape[1]
    gate_out[...] = total[:, :hidden]
    up_out[...] = total[:, hidden : 2 * hidden]
    down_out[...] = total[:, 2 * hidden :].T


def text_second_kernel(spot, *refs):
    parts, outs = refs[:-RING], refs[-RING:]
    lanes = parts[0].shape[1] // SLOTS
    for offset in range(RING):
        for z in range(PAIR):
            slot = z * RING + (spot[2] + offset) % RING
            outs[offset][:, z * lanes : (z + 1) * lanes] = add_up(
                parts, lane_slice(slot, lanes)
            ).astype(jnp.bfloat16)


def text_third_kernel(spot, *refs):
    lanes = refs[-1].shape[1]
    for out, z in ((refs[-2], spot[1]), (refs[-1], (spot[1] + 1) % PAIR)):
        out[...] = add_up(refs[:RING], lane_slice(z, lanes)).astype(jnp.bfloat16)


def text_last_kernel(kept, got, textkey, textvalue):
    total = kept[...].astype(jnp.float32) + got[...].astype(jnp.float32)
    columns = textkey.shape[1]
    textkey[...] = total[:columns].T
    textvalue[...] = total[columns:].T


def attn_second_kernel(rows, spot, riders, *refs):
    parts, outs = refs[:-RING], refs[-RING:]
    size, count = SLOTS * rows, riders.shape[0]
    for offset in range(RING):
        for z in range(PAIR):
            slot = z * RING + (spot[2] + offset) % RING
            index = (pl.ds(pl.multiple_of(slot * rows, 16), rows), slice(None))
            outs[offset][z * rows : (z + 1) * rows, :] = add_up(parts, index).astype(jnp.bfloat16)
    ahead, behind = parts[1], parts[2]
    pairs = (
        (riders[...], ahead[size : size + count, :]),
        (behind[size : size + count, :], ahead[size + count : size + 2 * count, :]),
    )
    joined = [merge_rows(PAIR, first, second, rider_rows(2 * PAIR)) for first, second in pairs]
    joined = merge_rows(2 * PAIR, joined[0], joined[1], rider_rows(4 * PAIR))
    for out in outs:
        out[PAIR * rows :, :] = joined


def attn_third_kernel(spot, *refs):
    rows = refs[-1].shape[0]
    for out, z in ((refs[-2], spot[1]), (refs[-1], (spot[1] + 1) % PAIR)):
        index = (pl.ds(pl.multiple_of(z * rows, 16), rows), slice(None))
        out[...] = add_up(refs[:RING], index).astype(jnp.bfloat16)


def attn_last_kernel(kept, got, query, key, value, outw):
    total = kept[...].astype(jnp.float32) + got[...].astype(jnp.float32)
    columns = query.shape[1]
    for place, out in enumerate((query, key, value)):
        out[...] = total[:, place * columns : (place + 1) * columns]
    outw[...] = total[:, 3 * columns :].T


def whole_call(kernel, scalars, operands, outs, name, ties=(), scratch=(), micros=0):
    whole = pl.BlockSpec(memory_space=pltpu.VMEM)
    count = len(scalars) + len(operands)
    return pl.pallas_call(
        lambda *refs: kernel(*refs[:count], *refs[count + len(ties) :]),
        in_specs=[pl.BlockSpec(memory_space=pltpu.SMEM)] * len(scalars)
        + [whole] * len(operands)
        + [pl.BlockSpec(memory_space=pl.ANY)] * len(ties),
        out_specs=[whole] * len(outs),
        out_shape=[jax.ShapeDtypeStruct(shape, kind) for shape, kind in outs],
        scratch_shapes=list(scratch),
        compiler_params=pltpu.CompilerParams(vmem_limit_bytes=VMEM_LIMIT),
        cost_estimate=cost_of(micros),
        name=name,
    )(*scalars, *operands, *ties)


def tiled_call(kernel, scalars, operands, outs, name, axis, tiles, ties=(), micros=0, axes=None):
    def spec(shape, axis):
        block = list(shape)
        block[axis] //= tiles
        if axis == 0:
            return pl.BlockSpec(tuple(block), lambda step: (step,) + (0,) * (len(shape) - 1))
        return pl.BlockSpec(tuple(block), lambda step: (0,) * (len(shape) - 1) + (step,))

    count = len(scalars) + len(operands)
    return pl.pallas_call(
        lambda *refs: kernel(*refs[:count], *refs[count + len(ties) :]),
        grid=(tiles,),
        in_specs=[pl.BlockSpec(memory_space=pltpu.SMEM)] * len(scalars)
        + [spec(part.shape, way) for part, way in zip(operands, axes or [axis] * len(operands))]
        + [pl.BlockSpec(memory_space=pl.ANY)] * len(ties),
        out_specs=[spec(shape, axis) for shape, _ in outs],
        out_shape=[jax.ShapeDtypeStruct(shape, kind) for shape, kind in outs],
        compiler_params=pltpu.CompilerParams(vmem_limit_bytes=VMEM_LIMIT),
        cost_estimate=cost_of(micros),
        name=name,
    )(*scalars, *operands, *ties)


def exchange(chunks, axis):
    return [chunks[0]] + [
        dp_permute(chunks[step], axis, step) for step in range(1, len(chunks))
    ]


def one_on(halves):
    return dp_permute(halves[0], "first", 1), dp_permute(halves[1], "first", RING - 1)


def to_neighbours(own, ahead, behind):
    return [own, dp_permute(ahead, "first", 1), dp_permute(behind, "first", RING - 1)]


def by_slots(chunk):
    return chunk.reshape(SLOTS, chunk.shape[0] // SLOTS, chunk.shape[1])


def lane_index(shape):
    return lax.broadcasted_iota(jnp.int32, shape, 1)


def head_lanes(shape, head):
    lane = lane_index(shape)
    return (lane < HEAD) if head == 0 else (lane >= HEAD)


def per_head(values, reduce):
    first = head_lanes(values.shape, 0)
    left = jnp.sum(jnp.where(first, values, 0.0), axis=1, keepdims=True)
    right = jnp.sum(jnp.where(first, 0.0, values), axis=1, keepdims=True)
    return jnp.where(first, left, right)


def head_units(raw):
    inverse = lax.rsqrt(per_head(raw * raw, None) * (1.0 / HEAD) + EPS)
    return raw * inverse, inverse


def partner(values):
    lane = lane_index(values.shape)
    return jnp.where(
        lane % HEAD < HEAD // 2,
        pltpu.roll(values, LANES - HEAD // 2, 1),
        pltpu.roll(values, HEAD // 2, 1),
    )


def dot(left, right):
    return jnp.dot(left, right, preferred_element_type=jnp.float32)


def dot_t(left, right):
    return lax.dot_general(left, right, (((1,), (1,)), ((), ())), preferred_element_type=jnp.float32)


def attend_kernel(
    raw_q, raw_k, value, raw_t, text_value, cosine, sine, gains, gate, gate_swapped, mark_q, mark_k, mark_t,
    query_out, key_out, text_out, mixed_out, self_out, cross_out, self_log, cross_log,
):
    cos, sin = cosine[...], sine[...]
    unit = head_units(raw_q[...])[0] * gains[0:1, :]
    query = ((unit * cos + partner(unit) * sin).astype(jnp.bfloat16) * ROOT).astype(jnp.bfloat16)
    unit = head_units(raw_k[...])[0] * gains[1:2, :]
    key = (unit * cos + partner(unit) * sin).astype(jnp.bfloat16)
    text = (head_units(raw_t[...])[0] * gains[2:3, :]).astype(jnp.bfloat16)
    query_out[...] = query
    key_out[...] = key
    text_out[...] = text

    def attention(keys, marks, values):
        outs, sums = [], []
        for head in range(2):
            own = head_lanes(query.shape, head)
            own_keys = head_lanes(keys.shape, head)
            probe = jnp.where(own, query, mark_q[...])
            scores = dot_t(probe, jnp.where(own_keys, keys, marks))
            weights = jnp.exp(scores).astype(jnp.bfloat16)
            both = dot(weights, jnp.where(own_keys, values, jnp.ones_like(values)))
            outs.append(both)
        first = head_lanes(outs[0].shape, 0)
        product = jnp.where(first, outs[0], outs[1])
        total = jnp.where(first, outs[1], outs[0])
        return product / pltpu.roll(total, HEAD, 1), jnp.log(total)

    out, log = attention(key, mark_k[...], value[...])
    self_out[...] = out
    self_log[...] = log
    cross, log = attention(text, mark_t[...], text_value[...])
    cross_out[...] = cross
    cross_log[...] = log - jnp.log(gate_swapped[...])
    mixed_out[...] = (out + gate[...] * cross).astype(jnp.bfloat16)


def attention_grads(query, keys, marks, values, grad, out, log, mark_q):
    rows = grad.astype(jnp.float32)
    delta = per_head(rows * out, None)
    delta = pltpu.roll(delta, HEAD, 1)
    lane = lane_index(query.shape) % HEAD
    log_high = log.astype(jnp.bfloat16)
    log_low = (log - log_high.astype(jnp.float32)).astype(jnp.bfloat16)
    delta_high = delta.astype(jnp.bfloat16)
    delta_low = (delta - delta_high.astype(jnp.float32)).astype(jnp.bfloat16)
    zero = jnp.zeros_like(query)
    code = jnp.where(lane == 4, -log_high, jnp.where(lane == 5, -log_low, mark_q))
    shift = jnp.where(lane == 4, -delta_high, jnp.where(lane == 5, -delta_low, zero))
    key_grads, value_grads, query_grads = [], [], []
    for head in range(2):
        own = head_lanes(query.shape, head)
        own_keys = head_lanes(keys.shape, head)
        probe = jnp.where(own, query, code)
        probs = jnp.exp(dot_t(jnp.where(own_keys, keys, marks), probe))
        slope = dot_t(jnp.where(own_keys, values, marks), jnp.where(own, grad, shift))
        score_grad = (probs * slope).astype(jnp.bfloat16)
        value_grads.append(dot(probs.astype(jnp.bfloat16), grad))
        key_grads.append(dot(score_grad, query))
        turned = keys[:, head * HEAD : (head + 1) * HEAD].T
        query_grads.append(dot(turned, score_grad))
    first = head_lanes(keys.shape, 0)
    return (
        jnp.concatenate(query_grads, axis=0),
        jnp.where(first, key_grads[0], key_grads[1]),
        jnp.where(first, value_grads[0], value_grads[1]),
    )


def norm_back(weighted, unit, inverse):
    return inverse * (weighted - unit * (per_head(weighted * unit, None) * (1.0 / HEAD)))


def cross_back_kernel(
    query, text, text_value, raw_t, grad, out, log, gains, mark_q, mark_t,
    query_grad, raw_grad, value_grad, gain_sum, gate_sum,
):
    grad_q, grad_t, grad_v = attention_grads(
        query[...], text[...], mark_t[...], text_value[...], grad[...], out[...], log[...], mark_q[...]
    )
    query_grad[...] = grad_q.T
    value_grad[...] = grad_v.astype(jnp.bfloat16).T
    grad_t = grad_t.astype(jnp.bfloat16).astype(jnp.float32)
    unit, inverse = head_units(raw_t[...])
    gain_sum[...] = jnp.sum(grad_t * unit, axis=0, keepdims=True)
    raw_grad[...] = norm_back(grad_t * gains[2:3, :], unit, inverse).astype(jnp.bfloat16).T
    gate_sum[...] = jnp.sum(grad[...].astype(jnp.float32) * out[...], axis=0, keepdims=True)


def self_back_kernel(
    query, key, value, raw_q, raw_k, grad, out, log, cross_grad, cosine, sine, gains, mark_q, mark_k,
    query_grad, key_grad, value_grad, gain_sum,
):
    grad_q, grad_k, grad_v = attention_grads(
        query[...], key[...], mark_k[...], value[...], grad[...], out[...], log[...], mark_q[...]
    )
    value_grad[...] = grad_v.astype(jnp.bfloat16)
    cos, sin = cosine[...], sine[...]
    grad_q = (grad_q.T + cross_grad[...]) * ROOT
    for turn, raw, row, target in ((grad_q, raw_q, 0, query_grad), (grad_k, raw_k, 1, key_grad)):
        turn = turn.astype(jnp.bfloat16).astype(jnp.float32)
        turn = turn * cos - partner(turn) * sin
        unit, inverse = head_units(raw[...])
        gain_sum[row : row + 1, :] = jnp.sum(turn * unit, axis=0, keepdims=True)
        target[...] = norm_back(turn * gains[row : row + 1, :], unit, inverse).astype(jnp.bfloat16)


def pair_call(kernel, operands, outs, name, ties=(), micros=0):
    def spec(shape, cut):
        if cut is None:
            return pl.BlockSpec(shape, lambda pair: (0, 0))
        if cut == 1:
            return pl.BlockSpec((shape[0], LANES), lambda pair: (0, pair))
        return pl.BlockSpec((LANES, shape[1]), lambda pair: (pair, 0))

    width = outs[0][0][0] if outs[0][2] == 0 else outs[0][0][1]
    return pl.pallas_call(
        lambda *refs: kernel(*refs[: len(operands)], *refs[len(operands) + len(ties) :]),
        grid=(width // LANES,),
        in_specs=[spec(part.shape, cut) for part, cut in operands]
        + [pl.BlockSpec(memory_space=pl.ANY)] * len(ties),
        out_specs=[spec(shape, cut) for shape, _, cut in outs],
        out_shape=[jax.ShapeDtypeStruct(shape, kind) for shape, kind, _ in outs],
        compiler_params=pltpu.CompilerParams(vmem_limit_bytes=VMEM_LIMIT),
        cost_estimate=cost_of(micros),
        name=name,
    )(*[part for part, _ in operands], *ties)
def inverse_rms(values):
    return lax.rsqrt(jnp.mean(values * values, axis=-1, keepdims=True) + EPS)


def row_norm_back(weighted, unit, inverse):
    return inverse * (weighted - unit * jnp.mean(weighted * unit, axis=-1, keepdims=True))


def per_row(table, segment):
    return jnp.where(segment == 0.0, table[0:1], jnp.where(segment == 1.0, table[1:2], table[2:3]))


def total_of(parts):
    upper, near, far = parts
    rows = far.shape[0]
    return (
        upper[:rows].astype(jnp.float32) + near[:rows].astype(jnp.float32) + far[...].astype(jnp.float32)
    )


def segment_sums(member, values):
    high = values.astype(jnp.bfloat16)
    low = (values - high.astype(jnp.float32)).astype(jnp.bfloat16)
    return dot(member, high) + dot(member, low)


def tables_kernel(here, lens, gate, segments, head_gains, cosine, sine, mark_q, mark_k, mark_t,
                  segment, member, gate_lanes, gate_swapped, gains):
    heads = gains.shape[1] // HEAD
    lane = lane_index(gate_lanes.shape) // HEAD
    line = jnp.zeros(gate_lanes.shape, jnp.float32)
    swapped = line
    for head in range(heads):
        line = jnp.where(lane == head, gate[head], line)
        swapped = jnp.where(lane == head ^ 1, gate[head], swapped)
    gate_lanes[...] = jnp.tanh(line)
    gate_swapped[...] = jnp.tanh(swapped)
    gains[...] = jnp.concatenate([head_gains[...]] * heads, axis=1)
    rows = segments.shape[1]
    ids = segments[...]
    first = jnp.sum((ids < 1).astype(jnp.float32))
    second = jnp.sum((ids < 2).astype(jnp.float32))
    lane = lane_index((rows, LANES))
    half = HEAD // 2
    rate = jnp.exp((lane % half).astype(jnp.float32) * (-2.0 * math.log(10000.0) / HEAD))
    within = lane % HEAD
    for block, code in enumerate(ROW_ORDER):
        source = here[0] ^ code
        line = segments[pl.ds(source, 1), :].astype(jnp.float32)
        label = jnp.broadcast_to(line, (rows, rows)).T
        start = jnp.where(label == 0.0, 0.0, jnp.where(label == 1.0, first, second))
        token = (lax.broadcasted_iota(jnp.int32, (rows, LANES), 0) + source * rows).astype(jnp.float32)
        angle = (token - start) * rate
        index = slice(block * rows, (block + 1) * rows)
        cosine[index, :] = jnp.cos(angle)
        sine[index, :] = jnp.where(within < half, -1.0, 1.0) * jnp.sin(angle)
        same = ((label == within.astype(jnp.float32)) & (within < SEGS)).astype(jnp.float32)
        shut = (within == SEGS).astype(jnp.float32)
        ones = ((within >= SEGS) & (within < SEGS + 3)).astype(jnp.float32)
        mark_q[index, :] = (SHUT * same - SHUT * shut).astype(jnp.bfloat16)
        mark_k[index, :] = (same + ones).astype(jnp.bfloat16)
        if block == 0:
            segment[...] = label
            member[...] = (
                lax.broadcasted_iota(jnp.int32, (8, rows), 0).astype(jnp.float32) == line
            ).astype(jnp.bfloat16)
    for group in range(SEGS):
        lane = lane_index((TXT, LANES)) % HEAD
        row = lax.broadcasted_iota(jnp.int32, (TXT, LANES), 0)
        inside = ((lane == group) & (row < lens[group])).astype(jnp.float32)
        ones = ((lane >= SEGS) & (lane < SEGS + 3)).astype(jnp.float32)
        mark_t[group * TXT : (group + 1) * TXT, :] = (inside + ones).astype(jnp.bfloat16)


def text_kernel(captions, key_weight, value_weight, raw_out, value_out, raw_sum, value_sum):
    step = pl.program_id(0)

    @pl.when(step == 0)
    def _():
        raw_sum[...] = dot(captions[...], key_weight[...])
        value_sum[...] = dot(captions[...], value_weight[...])

    @pl.when(step > 0)
    def _():
        raw_sum[...] += dot(captions[...], key_weight[...])
        value_sum[...] += dot(captions[...], value_weight[...])

    @pl.when(step == pl.num_programs(0) - 1)
    def _():
        raw_out[...] = raw_sum[...]
        value_out[...] = value_sum[...].astype(jnp.bfloat16)


def text_call(captions, key_weight, value_weight):
    rows, depth = captions.shape
    columns = key_weight.shape[1]
    tile = depth // 4
    return pl.pallas_call(
        text_kernel,
        grid=(depth // tile,),
        in_specs=[
            pl.BlockSpec((rows, tile), lambda step: (0, step)),
            pl.BlockSpec((tile, columns), lambda step: (step, 0)),
            pl.BlockSpec((tile, columns), lambda step: (step, 0)),
        ],
        out_specs=[pl.BlockSpec((rows, columns), lambda step: (0, 0))] * 2,
        out_shape=[
            jax.ShapeDtypeStruct((rows, columns), jnp.float32),
            jax.ShapeDtypeStruct((rows, columns), jnp.bfloat16),
        ],
        scratch_shapes=[pltpu.VMEM((rows, columns), jnp.float32)] * 2,
        compiler_params=pltpu.CompilerParams(vmem_limit_bytes=VMEM_LIMIT),
        cost_estimate=cost_of(9),
        name="text",
    )(captions, key_weight, value_weight)


def project_kernel(here, own, far, near, last, mods, gains, segment_q, query_w, key_w, value_w,
                   rows_out, raw_q, raw_k, value):
    table = mods[here[0]]
    rows = own.shape[0]
    for block, part in enumerate((own, far, near, last)):
        index = slice(block * rows, (block + 1) * rows)
        values = part[...].astype(jnp.float32)
        marks = segment_q[index, :].astype(jnp.float32)
        scale = jnp.where(
            marks[:, 0:1] > 0.0, table[0:1], jnp.where(marks[:, 1:2] > 0.0, table[1:2], table[2:3])
        )
        rows_out[index, :] = (
            values * inverse_rms(values) * gains[0:1] * (1.0 + scale)
        ).astype(jnp.bfloat16)
    raw_q[...] = dot(rows_out[...], query_w[...])
    raw_k[...] = dot(rows_out[...], key_w[...])
    value[...] = dot(rows_out[...], value_w[...]).astype(jnp.bfloat16)


def middle_kernel(here, block, upper, near, far, mods, gains, segment, attn_out, middle_out, rows_out):
    attn_sum = total_of((upper, near, far))
    label = segment[:, 0:1]
    factor = jnp.tanh(per_row(mods[here[0] ^ 1], label)) * gains[1:2]
    middle = block[...].astype(jnp.float32) + factor * (attn_sum * inverse_rms(attn_sum))
    attn_out[...] = attn_sum
    middle_out[...] = middle
    scale = per_row(mods[here[0] ^ 2], label)
    rows_out[...] = (middle * inverse_rms(middle) * gains[2:3] * (1.0 + scale)).astype(jnp.bfloat16)


def block_out_kernel(here, middle, upper, near, far, grad, mods, gains, segment, member,
                     block_out, grad_out, sums):
    ffn_sum = total_of((upper, near, far))
    inverse = inverse_rms(ffn_sum)
    unit = ffn_sum * inverse
    factor = jnp.tanh(per_row(mods[here[0] ^ 3], segment[:, 0:1])) * gains[3:4]
    block_out[...] = (middle[...] + factor * unit).astype(jnp.bfloat16)
    incoming = grad[...].astype(jnp.float32)
    grad_out[...] = row_norm_back(incoming * factor, unit, inverse).astype(jnp.bfloat16)
    sums[...] = segment_sums(member[...], incoming * unit)


def middle_back_kernel(here, middle, attn, upper, near, far, grad, mods, gains, segment, member,
                       middle_grad, attn_grad, ffn_sums, attn_sums):
    grad_in = total_of((upper, near, far))
    label = segment[:, 0:1]
    inverse = inverse_rms(middle[...])
    unit = middle[...] * inverse
    factor = gains[2:3] * (1.0 + per_row(mods[here[0] ^ 2], label))
    ffn_sums[...] = segment_sums(member[...], grad_in * unit)
    grad_middle = grad[...].astype(jnp.float32) + row_norm_back(grad_in * factor, unit, inverse)
    middle_grad[...] = grad_middle
    inverse = inverse_rms(attn[...])
    unit = attn[...] * inverse
    factor = jnp.tanh(per_row(mods[here[0] ^ 1], label)) * gains[1:2]
    attn_grad[...] = row_norm_back(grad_middle * factor, unit, inverse).astype(jnp.bfloat16)
    attn_sums[...] = segment_sums(member[...], grad_middle * unit)


def block_in_kernel(here, block, middle_grad, upper, near, far, mods, gains, segment, member,
                    in_grad, sums):
    grad_in = total_of((upper, near, far))
    values = block[...].astype(jnp.float32)
    inverse = inverse_rms(values)
    unit = values * inverse
    factor = gains[0:1] * (1.0 + per_row(mods[here[0]], segment[:, 0:1]))
    in_grad[...] = (
        middle_grad[...] + row_norm_back(grad_in * factor, unit, inverse)
    ).astype(jnp.bfloat16)
    sums[...] = segment_sums(member[...], grad_in * unit)


def stack_sums_kernel(here, first, second, third, fourth, head_gain, text_gain, gate_sum, gate, out):
    width = out.shape[1]
    heads = jnp.concatenate([head_gain[0:1], head_gain[1:2], text_gain[...]], axis=1)
    inner = heads.shape[1] // 3
    gates = gate_sum[...] * (1.0 - gate[...] * gate[...])
    gates = jnp.concatenate([gates, jnp.zeros((1, width - inner), jnp.float32)], axis=1)
    lane = lane_index(gates.shape)
    moved = jnp.zeros_like(gates)
    for position in range(4):
        turn = pltpu.roll(gates, position * inner, 1) if position else gates
        moved = jnp.where((lane // inner == position) & (here[0] == position), turn, moved)
    out[...] = jnp.concatenate(
        [part[0:SEGS] for part in (first, second, third, fourth)]
        + [
            jnp.concatenate([heads, jnp.zeros((1, width - 3 * inner), jnp.float32)], axis=1),
            moved,
            jnp.zeros((2, width), jnp.float32),
        ],
        axis=0,
    )


def pack_kernel(here, own, far, near, last, mods, gains, cond, packed):
    total = own[...] + far[...] + near[...] + last[...]
    grad = jnp.zeros((SEGS, total.shape[1]), jnp.float32)
    rows = []
    for name in range(4):
        part = total[name * SEGS : (name + 1) * SEGS]
        mod = mods[here[0] ^ name]
        gain = gains[name : name + 1]
        if name % 2 == 1:
            factor = jnp.tanh(mod)
            slope = 1.0 - factor * factor
        else:
            factor = 1.0 + mod
            slope = jnp.ones_like(mod)
        rows.append(jnp.sum(part * factor, axis=0, keepdims=True))
        mine = (jnp.zeros(part.shape, jnp.int32) + here[0]) == name
        grad = jnp.where(mine, part * slope * gain, grad)
    rows.append(total[4 * SEGS : 4 * SEGS + 2])
    rows = jnp.concatenate(rows, axis=0)
    high = rows.astype(jnp.bfloat16).astype(jnp.float32)
    pad = jnp.zeros((packed.shape[0] - 2 * SEGS - 2 * SUM_ROWS, total.shape[1]), jnp.float32)
    packed[...] = jnp.concatenate(
        [grad, cond[...].astype(jnp.float32), high, rows - high, pad], axis=0
    ).astype(jnp.bfloat16)


def rider_rows(count):
    return -(-(2 * SEGS * count + 2 * SUM_ROWS) // 16) * 16


def merge_rows(count, first, second, size):
    first, second = first.astype(jnp.float32), second.astype(jnp.float32)
    wide = SEGS * count
    start = 2 * wide
    sums = (
        first[start : start + SUM_ROWS]
        + first[start + SUM_ROWS : start + 2 * SUM_ROWS]
        + second[start : start + SUM_ROWS]
        + second[start + SUM_ROWS : start + 2 * SUM_ROWS]
    )
    high = sums.astype(jnp.bfloat16).astype(jnp.float32)
    pieces = [first[:wide], second[:wide], first[wide:start], second[wide:start], high, sums - high]
    rest = size - 4 * wide - 2 * SUM_ROWS
    if rest:
        pieces.append(jnp.zeros((rest, first.shape[1]), jnp.float32))
    return jnp.concatenate(pieces, axis=0).astype(jnp.bfloat16)


def merge_kernel(ours, theirs, out):
    out[...] = merge_rows(1, ours[...], theirs[...], out.shape[0])


def ada_kernel(count, heads, dp, own, *refs):
    parts = (own,) + refs[:3]
    ada_out, norm_out, head_out, gate_out = refs[3:]
    wide = SEGS * count
    base = own.shape[0] - rider_rows(count)
    columns = ada_out.shape[0]
    share = LANES // columns
    start = pl.multiple_of(dp[0] // share * LANES, LANES)
    grads, conds = [], []
    sums = jnp.zeros((SUM_ROWS, own.shape[1]), jnp.float32)
    for part in parts:
        rows = part[base:, :].astype(jnp.float32)
        grads.append(rows[:wide])
        conds.append(part[base:, pl.ds(start, LANES)].astype(jnp.float32)[wide : 2 * wide])
        for half in range(2):
            place = 2 * wide + half * SUM_ROWS
            sums = sums + rows[place : place + SUM_ROWS]
    conds = jnp.concatenate(conds, axis=0)
    conds = pltpu.roll(conds, (LANES - dp[0] % share * columns) % LANES, 1)
    acts = conds / (1.0 + jnp.exp(-conds))
    ada_out[...] = dot(
        acts.astype(jnp.bfloat16).astype(jnp.float32).T.astype(jnp.bfloat16),
        jnp.concatenate(grads, axis=0).astype(jnp.bfloat16),
    )[:columns]
    norm_out[...] = sums[:4]
    inner = heads * HEAD
    for row in range(3):
        line = jnp.zeros((1, HEAD), jnp.float32)
        for head in range(heads):
            place = row * inner + head * HEAD
            line = line + sums[4:5, place : place + HEAD]
        head_out[row : row + 1, :] = line
    lane = lane_index((1, LANES))
    line = jnp.zeros((1, LANES), jnp.float32)
    for head in range(HEADS):
        value = jnp.sum(sums[5:6, head * HEAD : (head + 1) * HEAD], axis=1, keepdims=True)
        line = jnp.where(lane == head, value, line)
    gate_out[...] = line


def back_kernel(count, *refs):
    grads, weights, upper, lower = refs[:count], refs[count : 2 * count], refs[-2], refs[-1]
    total = dot_t(grads[0][...], weights[0][...])
    for grad, weight in zip(grads[1:], weights[1:]):
        total = total + dot_t(grad[...], weight[...])
    half = upper.shape[0]
    upper[...] = total[:half].astype(jnp.bfloat16)
    lower[...] = total[half:].astype(jnp.bfloat16)


def back_call(grads, weights, name, ties=(), micros=0):
    rows, inner = grads[0].shape
    columns = weights[0].shape[0]
    tile = columns // 3
    return pl.pallas_call(
        lambda *refs: back_kernel(len(grads), *refs[: 2 * len(grads)], *refs[-2:]),
        grid=(columns // tile,),
        in_specs=[pl.BlockSpec((rows, inner), lambda step: (0, 0))] * len(grads)
        + [pl.BlockSpec((tile, inner), lambda step: (step, 0))] * len(grads)
        + [pl.BlockSpec(memory_space=pl.ANY)] * len(ties),
        out_specs=[pl.BlockSpec((rows // 2, tile), lambda step: (0, step))] * 2,
        out_shape=[jax.ShapeDtypeStruct((rows // 2, columns), jnp.bfloat16)] * 2,
        compiler_params=pltpu.CompilerParams(vmem_limit_bytes=VMEM_LIMIT),
        cost_estimate=cost_of(micros),
        name=name,
    )(*grads, *weights, *ties)


def shards(
    block_in,
    out_grad,
    condition,
    captions,
    caption_len,
    segment_ids,
    ada_weight,
    norm_gains,
    query_weight,
    key_weight,
    value_weight,
    head_gains,
    textkey_weight,
    textvalue_weight,
    cross_gate,
    out_weight,
    gate_weight,
    up_weight,
    down_weight,
):
    rows, width = block_in.shape
    length = segment_ids.shape[0]
    heads = cross_gate.shape[0]
    inner = heads * HEAD
    half_rows = length // 2
    position = lax.axis_index("tensor")
    spot = dp_spot(position)
    here = position.reshape(1)
    b16, f32 = jnp.bfloat16, jnp.float32

    blocks = gather_tensor(block_in)
    cond_rows = jnp.pad(condition, ((0, 0), (0, width - condition.shape[1])))
    own_act = jax.nn.silu(condition.astype(f32)).astype(b16)
    own_part = jnp.dot(own_act, ada_weight, preferred_element_type=f32)
    parts = gather_tensor(own_part)
    mods = jnp.stack([parts[ROW_ORDER.index(code)] for code in range(4)])

    cosine, sine, mark_q, mark_k, mark_t, segment, member, gate_lanes, gate_swapped, gains = whole_call(
        tables_kernel,
        (here, caption_len, cross_gate),
        [segment_ids.reshape(length // rows, rows), head_gains],
        [((length, LANES), f32)] * 2
        + [((length, LANES), b16)] * 2
        + [((SEGS * TXT, LANES), b16), ((rows, LANES), f32), ((8, rows), b16)]
        + [((1, inner), f32)] * 2
        + [((3, inner), f32)],
        "tables",
        micros=2,
    )
    caption_flat = captions.reshape(-1, captions.shape[-1])
    texts = caption_flat.shape[0]
    raw_t, text_value = text_call(caption_flat, textkey_weight, textvalue_weight)
    attn_rows, raw_q, raw_k, value = whole_call(
        project_kernel,
        (here,),
        blocks + [mods, norm_gains, mark_q, query_weight, key_weight, value_weight],
        [((length, width), b16), ((length, inner), f32), ((length, inner), f32), ((length, inner), b16)],
        "project",
        micros=6,
    )
    query, key, text, mixed, self_out, cross_out, self_log, cross_log = pair_call(
        attend_kernel,
        [(raw_q, 1), (raw_k, 1), (value, 1), (raw_t, 1), (text_value, 1), (cosine, None), (sine, None)]
        + [(gains, 1), (gate_lanes, 1), (gate_swapped, 1), (mark_q, None), (mark_k, None), (mark_t, None)],
        [((length, inner), b16, 1)] * 2
        + [((texts, inner), b16, 1), ((length, inner), b16, 1)]
        + [((length, inner), f32, 1)] * 4,
        "attend",
        micros=11,
    )

    def halves(product):
        return product(slice(0, half_rows)).astype(b16), product(slice(half_rows, None)).astype(b16)

    def all_of(block):
        return jnp.concatenate(gather_tensor(block), axis=0)

    upper, lower = halves(lambda part: jnp.dot(mixed[part], out_weight, preferred_element_type=f32))
    sums, sent = scatter_tensor(upper, lower)
    attn_rows_t = turned(attn_rows, (sent,))
    wide = ((rows, width), f32)
    narrow = ((rows, width), b16)
    totals = ((8, width), f32)
    attn_sum, middle, ffn_own = whole_call(
        middle_kernel,
        (here,),
        [block_in] + sums + [mods, norm_gains, segment],
        [wide, wide, narrow],
        "middle",
    )
    ffn_rows = all_of(ffn_own)
    gate_pre = jnp.dot(ffn_rows, gate_weight, preferred_element_type=f32)
    up_pre = jnp.dot(ffn_rows, up_weight, preferred_element_type=f32)
    sigmoid_gate = jax.nn.sigmoid(gate_pre)
    silu_gate = gate_pre * sigmoid_gate
    hidden = (silu_gate * up_pre).astype(b16)
    upper, lower = halves(lambda part: jnp.dot(hidden[part], down_weight, preferred_element_type=f32))
    sums, sent = scatter_tensor(upper, lower)
    ffn_rows_t = turned(ffn_rows, (sent,))
    block_out, grad_own, sum_gate_ffn = whole_call(
        block_out_kernel,
        (here,),
        [middle] + sums + [out_grad, mods, norm_gains, segment, member],
        [narrow, narrow, totals],
        "block_out",
    )

    grad_ffn = all_of(grad_own)
    grad_hidden = times_transpose(grad_ffn, down_weight)
    grad_gate = (
        grad_hidden * up_pre * sigmoid_gate * (1.0 + gate_pre * (1.0 - sigmoid_gate))
    ).astype(b16)
    grad_up = (grad_hidden * silu_gate).astype(b16)
    upper, lower = halves(
        lambda part: times_transpose(grad_gate[part], gate_weight)
        + times_transpose(grad_up[part], up_weight)
    )
    sums, sent = scatter_tensor(upper, lower)
    grad_ffn_t = turned(grad_ffn, (sent,))
    ffn_pairs = [(ffn_rows_t, [grad_gate, grad_up]), (grad_ffn_t, [hidden])]
    (halves_two,) = row_chunks(ffn_pairs, (2,), spot, ties=(sent,), micros=FFN_MICROS)
    ffn_passed = one_on(halves_two)
    grad_middle, grad_own, sum_scale_ffn, sum_gate_attn = whole_call(
        middle_back_kernel,
        (here,),
        [middle, attn_sum] + sums + [out_grad, mods, norm_gains, segment, member],
        [wide, narrow, totals, totals],
        "middle_back",
        micros=MIDDLE_MICROS,
    )

    grad_attn = all_of(grad_own)
    grad_mixed = times_transpose(grad_attn, out_weight).astype(b16)
    cross_grad, text_grad, text_value_grad, text_gain, gate_sum = pair_call(
        cross_back_kernel,
        [(query, 1), (text, 1), (text_value, 1), (raw_t, 1), (grad_mixed, 1), (cross_out, 1)]
        + [(cross_log, 1), (gains, 1), (mark_q, None), (mark_t, None)],
        [((length, inner), f32, 1), ((inner, texts), b16, 0), ((inner, texts), b16, 0)]
        + [((1, inner), f32, 1)] * 2,
        "cross_back",
        micros=CROSS_MICROS,
    )
    ffn_one, ffn_three, ffn_kept = row_chunks(
        ffn_pairs, (1, 3, 0), spot, extra=ffn_passed, ties=(text_grad,), micros=FFN_NEXT_MICROS
    )
    text_lefts = [text_grad, text_value_grad]
    (halves_two,) = column_chunks(text_lefts, caption_flat, (2,), spot, ties=(ffn_kept,))
    text_passed = one_on(halves_two)
    query_grad, key_grad, value_grad, head_gain = pair_call(
        self_back_kernel,
        [(query, 1), (key, 1), (value, 1), (raw_q, 1), (raw_k, 1), (grad_mixed, 1), (self_out, 1)]
        + [(self_log, 1), (cross_grad, 1), (cosine, None), (sine, None), (gains, 1)]
        + [(mark_q, None), (mark_k, None)],
        [((length, inner), b16, 1)] * 3 + [((2, inner), f32, 1)],
        "self_back",
        (halves_two[0],),
        micros=SELF_MICROS,
    )

    hidden_cols = hidden.shape[1]
    block_rows = width // BLOCKS
    got = [by_slots(part) for part in to_neighbours(ffn_kept, ffn_one, ffn_three)]
    shape = (PAIR, block_rows, 3 * hidden_cols)
    ffn_stage = tiled_call(
        ffn_second_kernel, (spot,), got, [(shape, b16)] * RING, "ffn_second",
        -1,
        4, (query_grad,)
    )
    upper, lower = back_call(
        [query_grad, key_grad, value_grad], [query_weight, key_weight, value_weight], "attn_back"
    )
    sums, sent = scatter_tensor(upper, lower)
    in_grad, sum_scale_attn = whole_call(
        block_in_kernel,
        (here,),
        [block_in, grad_middle] + sums + [mods, norm_gains, segment, member],
        [narrow, totals],
        "block_in",
        (ffn_stage[0],),
        micros=BLOCK_IN_MICROS,
    )
    (stacked,) = whole_call(
        stack_sums_kernel,
        (here,),
        [sum_scale_attn, sum_gate_attn, sum_scale_ffn, sum_gate_ffn]
        + [head_gain, text_gain, gate_sum, gate_lanes],
        [((16, width), f32)],
        "stack_sums",
    )
    stacked = gather_tensor(stacked)
    (riders,) = whole_call(
        pack_kernel,
        (here,),
        stacked + [mods, norm_gains, cond_rows],
        [((rider_rows(1), width), b16)],
        "pack",
    )
    theirs = dp_permute(riders, "z", 1)
    (riders,) = whole_call(
        merge_kernel, (), [riders, theirs], [((rider_rows(PAIR), width), b16)], "merge"
    )
    attn_pairs = [
        (attn_rows_t, [query_grad, key_grad, value_grad]),
        (turned(grad_attn, (halves_two[0],)), [mixed]),
    ]
    (halves_two,) = row_chunks(attn_pairs, (2,), spot, riders=(riders,), micros=ATTN_FIRST_MICROS)
    attn_passed = one_on(halves_two)
    text_one, text_three, text_kept = column_chunks(
        text_lefts, caption_flat, (1, 3, 0), spot, extra=text_passed, ties=(halves_two[0],), micros=8
    )
    kept, sent = tiled_call(
        ffn_third_kernel,
        (spot,),
        exchange(ffn_stage, "second"),
        [(shape[1:], b16)] * 2,
        "ffn_third",
        -1,
        2,
        (text_kept,),
    )
    gate_sum_out, up_sum_out, down_sum_out = whole_call(
        ffn_last_kernel,
        (),
        exchange([kept, sent], "z"),
        [((block_rows, hidden_cols), f32)] * 2 + [((hidden_cols, block_rows), f32)],
        "ffn_last",
    )
    text_rows = caption_flat.shape[1] // BLOCKS
    attn_one, attn_three, attn_kept = row_chunks(
        attn_pairs, (1, 3, 0), spot, extra=attn_passed, ties=(kept,), riders=(riders,), micros=ATTN_MICROS
    )
    stage = tiled_call(
        text_second_kernel,
        (spot,),
        to_neighbours(text_kept, text_one, text_three),
        [((2 * inner, PAIR * text_rows), b16)] * RING,
        "text_second",
        0,
        4,
        (attn_kept,),
    )
    kept, sent = tiled_call(
        text_third_kernel,
        (spot,),
        exchange(stage, "second"),
        [((2 * inner, text_rows), b16)] * 2,
        "text_third",
        0,
        2,
        (gate_sum_out,),
    )
    textkey_sum, textvalue_sum = whole_call(
        text_last_kernel,
        (),
        exchange([kept, sent], "z"),
        [((text_rows, inner), f32)] * 2,
        "text_last",
    )
    stage = tiled_call(
        functools.partial(attn_second_kernel, block_rows),
        (spot,),
        [riders] + to_neighbours(attn_kept, attn_one, attn_three),
        [((PAIR * block_rows + rider_rows(4 * PAIR), width), b16)] * RING,
        "attn_second",
        -1,
        4,
        (kept,),
    )
    got = exchange(stage, "second")
    kept, sent = tiled_call(
        attn_third_kernel, (spot,), got, [((block_rows, width), b16)] * 2, "attn_third",
        -1,
        2
    )
    ada_grad, norm_grads, head_grads, crossgate = tiled_call(
        functools.partial(ada_kernel, 4 * PAIR, heads),
        (lax.axis_index("dp").reshape(1),),
        got,
        [((condition.shape[1] // BLOCKS, width), f32), ((4, width), f32), ((3, HEAD), f32)]
        + [((1, LANES), f32)],
        "ada",
        0,
        1,
        (kept,),
    )
    crossgate_grad = crossgate[0, :HEADS]
    query_sum, key_sum, value_sum, outw_sum = whole_call(
        attn_last_kernel,
        (),
        exchange([kept, sent], "z"),
        [((block_rows, inner), f32)] * 3 + [((inner, block_rows), f32)],
        "attn_last",
    )
    return (
        block_out,
        in_grad,
        ada_grad,
        norm_grads,
        query_sum,
        key_sum,
        value_sum,
        head_grads,
        textkey_sum,
        textvalue_sum,
        crossgate_grad,
        outw_sum,
        gate_sum_out,
        up_sum_out,
        down_sum_out,
    )


def solution(mesh):
    return jax.shard_map(
        shards,
        mesh=mesh,
        in_specs=(
            P(("dp", "tensor"), None),
            P(("dp", "tensor"), None),
            P("dp", None),
            P("dp", None, None),
            P("dp"),
            P("dp"),
            P(None, "tensor"),
            P(),
            P(None, "tensor"),
            P(None, "tensor"),
            P(None, "tensor"),
            P(),
            P(None, "tensor"),
            P(None, "tensor"),
            P("tensor"),
            P("tensor", None),
            P(None, "tensor"),
            P(None, "tensor"),
            P("tensor", None),
        ),
        out_specs=(
            P(("dp", "tensor"), None),
            P(("dp", "tensor"), None),
            P("dp", "tensor"),
            P(),
            P("dp", "tensor"),
            P("dp", "tensor"),
            P("dp", "tensor"),
            P(),
            P("dp", "tensor"),
            P("dp", "tensor"),
            P(),
            P("tensor", "dp"),
            P("dp", "tensor"),
            P("dp", "tensor"),
            P("tensor", "dp"),
        ),
        check_vma=False,
    )
```

```python
import functools
import math

import jax
import jax.numpy as jnp
from jax import lax
from jax.experimental import pallas as pl
from jax.experimental.pallas import tpu as pltpu
from jax.sharding import PartitionSpec as P

HEAD = 64
HEADS = 24
TXT = 256
SEGS = 3
EPS = 1e-06
LANES = 2 * HEAD
SHUT = 256.0
ROOT = HEAD ** (-0.5)
VMEM_LIMIT = 24 * 2**20
NO_COST = pl.CostEstimate(flops=0, bytes_accessed=0, transcendentals=0)


def cost_of(micros):
    return pl.CostEstimate(flops=int(micros * 1e9), bytes_accessed=0, transcendentals=0)


SUM_ROWS = 6
CROSS_MICROS = 10
BLOCK_IN_MICROS = 0
FFN_MICROS = 3
FFN_NEXT_MICROS = 8
MIDDLE_MICROS = 10
SELF_MICROS = 0
ATTN_MICROS = 7
TEXT_MICROS = 8
ATTN_FIRST_MICROS = 0

RING = 4
PAIR = 2
BLOCKS = RING * PAIR * RING
SLOTS = BLOCKS // RING
SEND_ORDER = (2, 1, 3, 0)
CORE_SWAP = [(0, 1), (1, 0), (2, 3), (3, 2)]
CHIP_SWAP = [(0, 2), (2, 0), (1, 3), (3, 1)]
ROW_ORDER = (0, 2, 1, 3)

def dp_index(x, z, y):
    return (x * PAIR + z) * RING + y


def dp_perm(axis, step):
    pairs = []
    for x in range(RING):
        for z in range(PAIR):
            for y in range(RING):
                for tensor in range(2 * PAIR):
                    way = axis
                    if axis in ("first", "second"):
                        way = "x" if (tensor % 2 == 0) == (axis == "first") else "y"
                    target = {
                        "x": ((x + step) % RING, z, y),
                        "y": (x, z, (y + step) % RING),
                        "z": (x, (z + step) % PAIR, y),
                    }[way]
                    pairs.append(
                        (
                            dp_index(x, z, y) * 2 * PAIR + tensor,
                            dp_index(*target) * 2 * PAIR + tensor,
                        )
                    )
    return pairs


def dp_permute(values, axis, step):
    return lax.ppermute(values, ("dp", "tensor"), dp_perm(axis, step))


def dp_spot(position):
    index = lax.axis_index("dp")
    x, z, y = index // (RING * PAIR), index // RING % PAIR, index % RING
    core = position % 2
    return jnp.stack([jnp.where(core == 0, x, y), z, jnp.where(core == 0, y, x), core])


def swap_core(values):
    return lax.ppermute(values, "tensor", CORE_SWAP)


def swap_chip(values):
    return lax.ppermute(values, "tensor", CHIP_SWAP)


def times_transpose(left, right):
    return lax.dot_general(
        left, right, (((1,), (1,)), ((), ())), preferred_element_type=jnp.float32
    )


def gather_tensor(block):
    far = swap_chip(block)
    near = swap_core(block)
    return [block, far, near, swap_core(far)]


def scatter_tensor(upper, lower):
    near = swap_core(lower)
    rows = upper.shape[0] // 2
    far = (upper[rows:].astype(jnp.float32) + near[rows:].astype(jnp.float32)).astype(near.dtype)
    return [upper, near, swap_chip(far)], far


def turn_kernel(source, target):
    target[...] = source[...].T


def turned(values, ties=()):
    tile = 512 if values.shape[1] % 512 == 0 else values.shape[1]
    return pl.pallas_call(
        lambda source, *rest: turn_kernel(source, rest[-1]),
        grid=(values.shape[1] // tile,),
        in_specs=[pl.BlockSpec((values.shape[0], tile), lambda step: (0, step))]
        + [pl.BlockSpec(memory_space=pl.ANY)] * len(ties),
        out_specs=pl.BlockSpec((tile, values.shape[0]), lambda step: (step, 0)),
        out_shape=jax.ShapeDtypeStruct(values.shape[::-1], values.dtype),
        compiler_params=pltpu.CompilerParams(vmem_limit_bytes=VMEM_LIMIT),
        cost_estimate=NO_COST,
    )(values, *ties)


def chunk_block(offset, slot, spot):
    first = (spot[0] + offset) % RING
    z, second = slot // RING, slot % RING
    x = jnp.where(spot[3] == 0, first, second)
    y = jnp.where(spot[3] == 0, second, first)
    return dp_index(x, z, y)


def offset_of_step(offsets, step):
    offset = offsets[-1]
    for place in range(len(offsets) - 1):
        offset = jnp.where(step == place, offsets[place], offset)
    return offset


def chunk_kernel(make, offsets, halves, extra, outs, held, sems):
    step = pl.program_id(0)
    first, second = halves

    def copies(place):
        slot = held.at[place % 2]
        if offsets[place] != 2:
            return [pltpu.make_async_copy(slot, outs[place], sems.at[place % 2, 0])]
        return [
            pltpu.make_async_copy(slot.at[half], out, sems.at[place % 2, way])
            for way, (half, out) in enumerate(zip((first, second), outs[place]))
        ]

    for place, offset in enumerate(offsets):

        @pl.when(step == place)
        def _(place=place, offset=offset):
            if place >= 2:
                for copy in copies(place - 2):
                    copy.wait()
            added = {1: (first, extra[0]), 3: (second, extra[1])}.get(offset) if extra else None
            make(held.at[place % 2], added, offset)
            for copy in copies(place):
                copy.start()
            if place == len(offsets) - 1:
                for last in range(max(place - 1, 0), place + 1):
                    for copy in copies(last):
                        copy.wait()


def chunk_call(make, operands, specs, offsets, halves, shape, spot, extra, ties, name, micros):
    count = len(operands)
    pieces = []
    for offset in offsets:
        if offset == 2:
            pieces += [tuple(len(range(*s.indices(d))) for s, d in zip(h, shape)) for h in halves]
        else:
            pieces.append(shape)

    def kernel(spot_ref, *refs):
        inputs, extras = refs[:count], refs[count : count + len(extra)]
        outs = list(refs[-len(pieces) - 2 : -2])
        grouped = []
        for offset in offsets:
            grouped.append((outs.pop(0), outs.pop(0)) if offset == 2 else outs.pop(0))
        chunk_kernel(
            functools.partial(make, inputs), offsets, halves, extras, grouped, refs[-2], refs[-1]
        )

    found = pl.pallas_call(
        kernel,
        grid_spec=pltpu.PrefetchScalarGridSpec(
            num_scalar_prefetch=1,
            grid=(len(offsets),),
            in_specs=list(specs)
            + [pl.BlockSpec(part.shape, lambda step, spot: (0, 0)) for part in extra]
            + [pl.BlockSpec(memory_space=pl.ANY)] * len(ties),
            out_specs=[pl.BlockSpec(memory_space=pl.ANY)] * len(pieces),
            scratch_shapes=[
                pltpu.VMEM((2,) + shape, jnp.bfloat16),
                pltpu.SemaphoreType.DMA((2, 2)),
            ],
        ),
        out_shape=[jax.ShapeDtypeStruct(piece, jnp.bfloat16) for piece in pieces],
        compiler_params=pltpu.CompilerParams(vmem_limit_bytes=VMEM_LIMIT),
        cost_estimate=cost_of(micros),
        name=name,
    )(spot, *operands, *extra, *ties)
    found = list(found)
    return [
        (found.pop(0), found.pop(0)) if offset == 2 else found.pop(0) for offset in offsets
    ]


def make_rows(groups, inputs, slot, added, offset):
    lefts, rights = inputs[: SLOTS * len(groups)], inputs[SLOTS * len(groups) :]
    size = SLOTS * lefts[0].shape[1]
    if len(rights) > sum(groups):
        riders = rights[-1][...]
        count, half = riders.shape[0], riders.shape[1] // 2
        first, second = slice(size, size + count), slice(size + count, size + 2 * count)
        if offset == 2:
            for side in (slice(0, half), slice(half, 2 * half)):
                slot[first, side] = riders[:, :half]
                slot[second, side] = riders[:, half:]
        else:
            slot[first, :] = riders
            if offset == 1:
                slot[second, :half] = added[1][first, :]
                slot[second, half:] = added[1][second, :]
            else:
                slot[second, :] = riders
    column = place = 0
    for group, count in enumerate(groups):
        rows = jnp.concatenate(
            [left[0] for left in lefts[SLOTS * group : SLOTS * (group + 1)]], axis=0
        )
        for right in rights[place : place + count]:
            wide = right.shape[1]
            product = dot(rows, right[...])
            low, high = column, column
            if added is not None:
                low = min(max(column, added[0][1].start), column + wide)
                high = min(max(column, added[0][1].stop), column + wide)
            for start, stop in ((column, low), (low, high), (high, column + wide)):
                if start < stop:
                    part = product[:, start - column : stop - column]
                    if (start, stop) == (low, high):
                        base = added[0][1].start
                        part = part + added[1][:size, start - base : stop - base].astype(jnp.float32)
                    slot[:size, start:stop] = part.astype(jnp.bfloat16)
            column += wide
        place += count


def row_chunks(pairs, offsets, spot, extra=(), ties=(), micros=0, riders=()):
    lefts = [left.reshape(BLOCKS, left.shape[0] // BLOCKS, left.shape[1]) for left, _ in pairs]
    rights = [right for _, group in pairs for right in group]
    total = sum(right.shape[1] for right in rights)
    specs, operands = [], []
    for left in lefts:
        for slot in range(SLOTS):
            specs.append(
                pl.BlockSpec(
                    (1,) + left.shape[1:],
                    lambda step, spot, slot=slot: (
                        chunk_block(offset_of_step(offsets, step), slot, spot),
                        0,
                        0,
                    ),
                )
            )
            operands.append(left)
    specs += [pl.BlockSpec(right.shape, lambda step, spot: (0, 0)) for right in rights]
    specs += [pl.BlockSpec(part.shape, lambda step, spot: (0, 0)) for part in riders]
    rows = SLOTS * lefts[0].shape[1] + sum(2 * part.shape[0] for part in riders)
    halves = [(slice(0, rows), slice(0, total // 2)), (slice(0, rows), slice(total // 2, total))]
    return chunk_call(
        functools.partial(make_rows, [len(group) for _, group in pairs]),
        operands + rights + list(riders),
        specs,
        offsets,
        halves,
        (rows, total),
        spot,
        extra,
        ties,
        "row_chunks",
        micros,
    )


def make_columns(lefts, inputs, slot, added, offset):
    whole = jnp.concatenate([right[...] for right in inputs[lefts:]], axis=1)
    row = 0
    for left in inputs[:lefts]:
        product = dot(left[...], whole)
        if added is not None and added[0][0].start == row:
            product = product + added[1][...].astype(jnp.float32)
        slot[row : row + left.shape[0], :] = product.astype(jnp.bfloat16)
        row += left.shape[0]


def column_chunks(lefts, right, offsets, spot, extra=(), ties=(), micros=0):
    rows = lefts[0].shape[0]
    depth, columns = right.shape
    specs = [pl.BlockSpec(left.shape, lambda step, spot: (0, 0)) for left in lefts]
    for slot in range(SLOTS):
        specs.append(
            pl.BlockSpec(
                (depth, columns // BLOCKS),
                lambda step, spot, slot=slot: (
                    0,
                    chunk_block(offset_of_step(offsets, step), slot, spot),
                ),
            )
        )
    lanes = columns // RING
    halves = [(slice(0, rows), slice(0, lanes)), (slice(rows, 2 * rows), slice(0, lanes))]
    return chunk_call(
        functools.partial(make_columns, len(lefts)),
        list(lefts) + [right] * SLOTS,
        specs,
        offsets,
        halves,
        (2 * rows, lanes),
        spot,
        extra,
        ties,
        "column_chunks",
        micros,
    )


def add_up(refs, index):
    total = refs[0][index].astype(jnp.float32)
    for ref in refs[1:]:
        total = total + ref[index].astype(jnp.float32)
    return total


def lane_slice(start, size):
    return (slice(None), pl.ds(pl.multiple_of(start * size, size), size))


def ffn_second_kernel(spot, *refs):
    parts, outs = refs[:-RING], refs[-RING:]
    for offset in range(RING):
        for z in range(PAIR):
            slot = z * RING + (spot[2] + offset) % RING
            outs[offset][z] = add_up(parts, slot).astype(jnp.bfloat16)


def ffn_third_kernel(spot, *refs):
    for out, z in ((refs[-2], spot[1]), (refs[-1], (spot[1] + 1) % PAIR)):
        out[...] = add_up(refs[:RING], z).astype(jnp.bfloat16)


def ffn_last_kernel(kept, got, gate_out, up_out, down_out):
    total = kept[...].astype(jnp.float32) + got[...].astype(jnp.float32)
    hidden = gate_out.shape[1]
    gate_out[...] = total[:, :hidden]
    up_out[...] = total[:, hidden : 2 * hidden]
    down_out[...] = total[:, 2 * hidden :].T


def text_second_kernel(spot, *refs):
    parts, outs = refs[:-RING], refs[-RING:]
    lanes = parts[0].shape[1] // SLOTS
    for offset in range(RING):
        for z in range(PAIR):
            slot = z * RING + (spot[2] + offset) % RING
            outs[offset][:, z * lanes : (z + 1) * lanes] = add_up(
                parts, lane_slice(slot, lanes)
            ).astype(jnp.bfloat16)


def text_third_kernel(spot, *refs):
    lanes = refs[-1].shape[1]
    for out, z in ((refs[-2], spot[1]), (refs[-1], (spot[1] + 1) % PAIR)):
        out[...] = add_up(refs[:RING], lane_slice(z, lanes)).astype(jnp.bfloat16)


def text_last_kernel(kept, got, textkey, textvalue):
    total = kept[...].astype(jnp.float32) + got[...].astype(jnp.float32)
    columns = textkey.shape[1]
    textkey[...] = total[:columns].T
    textvalue[...] = total[columns:].T


def attn_second_kernel(rows, spot, riders, *refs):
    parts, outs = refs[:-RING], refs[-RING:]
    size, count = SLOTS * rows, riders.shape[0]
    for offset in range(RING):
        for z in range(PAIR):
            slot = z * RING + (spot[2] + offset) % RING
            index = (pl.ds(pl.multiple_of(slot * rows, 16), rows), slice(None))
            outs[offset][z * rows : (z + 1) * rows, :] = add_up(parts, index).astype(jnp.bfloat16)
    ahead, behind = parts[1], parts[2]
    pairs = (
        (riders[...], ahead[size : size + count, :]),
        (behind[size : size + count, :], ahead[size + count : size + 2 * count, :]),
    )
    joined = [merge_rows(PAIR, first, second, rider_rows(2 * PAIR)) for first, second in pairs]
    joined = merge_rows(2 * PAIR, joined[0], joined[1], rider_rows(4 * PAIR))
    for out in outs:
        out[PAIR * rows :, :] = joined


def attn_third_kernel(spot, *refs):
    rows = refs[-1].shape[0]
    for out, z in ((refs[-2], spot[1]), (refs[-1], (spot[1] + 1) % PAIR)):
        index = (pl.ds(pl.multiple_of(z * rows, 16), rows), slice(None))
        out[...] = add_up(refs[:RING], index).astype(jnp.bfloat16)


def attn_last_kernel(kept, got, query, key, value, outw):
    total = kept[...].astype(jnp.float32) + got[...].astype(jnp.float32)
    columns = query.shape[1]
    for place, out in enumerate((query, key, value)):
        out[...] = total[:, place * columns : (place + 1) * columns]
    outw[...] = total[:, 3 * columns :].T


def whole_call(kernel, scalars, operands, outs, name, ties=(), scratch=(), micros=0):
    whole = pl.BlockSpec(memory_space=pltpu.VMEM)
    count = len(scalars) + len(operands)
    return pl.pallas_call(
        lambda *refs: kernel(*refs[:count], *refs[count + len(ties) :]),
        in_specs=[pl.BlockSpec(memory_space=pltpu.SMEM)] * len(scalars)
        + [whole] * len(operands)
        + [pl.BlockSpec(memory_space=pl.ANY)] * len(ties),
        out_specs=[whole] * len(outs),
        out_shape=[jax.ShapeDtypeStruct(shape, kind) for shape, kind in outs],
        scratch_shapes=list(scratch),
        compiler_params=pltpu.CompilerParams(vmem_limit_bytes=VMEM_LIMIT),
        cost_estimate=cost_of(micros),
        name=name,
    )(*scalars, *operands, *ties)


def tiled_call(kernel, scalars, operands, outs, name, axis, tiles, ties=(), micros=0, axes=None):
    def spec(shape, axis):
        block = list(shape)
        block[axis] //= tiles
        if axis == 0:
            return pl.BlockSpec(tuple(block), lambda step: (step,) + (0,) * (len(shape) - 1))
        return pl.BlockSpec(tuple(block), lambda step: (0,) * (len(shape) - 1) + (step,))

    count = len(scalars) + len(operands)
    return pl.pallas_call(
        lambda *refs: kernel(*refs[:count], *refs[count + len(ties) :]),
        grid=(tiles,),
        in_specs=[pl.BlockSpec(memory_space=pltpu.SMEM)] * len(scalars)
        + [spec(part.shape, way) for part, way in zip(operands, axes or [axis] * len(operands))]
        + [pl.BlockSpec(memory_space=pl.ANY)] * len(ties),
        out_specs=[spec(shape, axis) for shape, _ in outs],
        out_shape=[jax.ShapeDtypeStruct(shape, kind) for shape, kind in outs],
        compiler_params=pltpu.CompilerParams(vmem_limit_bytes=VMEM_LIMIT),
        cost_estimate=cost_of(micros),
        name=name,
    )(*scalars, *[pltpu.with_memory_space_constraint(part, pltpu.HBM) for part in operands], *ties)


def exchange(chunks, axis):
    return [chunks[0]] + [
        dp_permute(chunks[step], axis, step) for step in range(1, len(chunks))
    ]


def one_on(halves):
    return dp_permute(halves[0], "first", 1), dp_permute(halves[1], "first", RING - 1)


def to_neighbours(own, ahead, behind):
    return [own, dp_permute(ahead, "first", 1), dp_permute(behind, "first", RING - 1)]


def by_slots(chunk):
    return chunk.reshape(SLOTS, chunk.shape[0] // SLOTS, chunk.shape[1])


def lane_index(shape):
    return lax.broadcasted_iota(jnp.int32, shape, 1)


def head_lanes(shape, head):
    lane = lane_index(shape)
    return (lane < HEAD) if head == 0 else (lane >= HEAD)


def per_head(values, reduce):
    first = head_lanes(values.shape, 0)
    left = jnp.sum(jnp.where(first, values, 0.0), axis=1, keepdims=True)
    right = jnp.sum(jnp.where(first, 0.0, values), axis=1, keepdims=True)
    return jnp.where(first, left, right)


def head_units(raw):
    inverse = lax.rsqrt(per_head(raw * raw, None) * (1.0 / HEAD) + EPS)
    return raw * inverse, inverse


def partner(values):
    lane = lane_index(values.shape)
    return jnp.where(
        lane % HEAD < HEAD // 2,
        pltpu.roll(values, LANES - HEAD // 2, 1),
        pltpu.roll(values, HEAD // 2, 1),
    )


def dot(left, right):
    return jnp.dot(left, right, preferred_element_type=jnp.float32)


def dot_t(left, right):
    return lax.dot_general(left, right, (((1,), (1,)), ((), ())), preferred_element_type=jnp.float32)


def attend_kernel(
    raw_q, raw_k, value, raw_t, text_value, cosine, sine, gains, gate, gate_swapped, mark_q, mark_k, mark_t,
    query_out, key_out, text_out, mixed_out, self_out, cross_out, self_log, cross_log,
):
    cos, sin = cosine[...], sine[...]
    unit = head_units(raw_q[...])[0] * gains[0:1, :]
    query = ((unit * cos + partner(unit) * sin).astype(jnp.bfloat16) * ROOT).astype(jnp.bfloat16)
    unit = head_units(raw_k[...])[0] * gains[1:2, :]
    key = (unit * cos + partner(unit) * sin).astype(jnp.bfloat16)
    text = (head_units(raw_t[...])[0] * gains[2:3, :]).astype(jnp.bfloat16)
    query_out[...] = query
    key_out[...] = key
    text_out[...] = text

    def attention(keys, marks, values):
        outs, sums = [], []
        for head in range(2):
            own = head_lanes(query.shape, head)
            own_keys = head_lanes(keys.shape, head)
            probe = jnp.where(own, query, mark_q[...])
            scores = dot_t(probe, jnp.where(own_keys, keys, marks))
            weights = jnp.exp(scores).astype(jnp.bfloat16)
            both = dot(weights, jnp.where(own_keys, values, jnp.ones_like(values)))
            outs.append(both)
        first = head_lanes(outs[0].shape, 0)
        product = jnp.where(first, outs[0], outs[1])
        total = jnp.where(first, outs[1], outs[0])
        return product / pltpu.roll(total, HEAD, 1), jnp.log(total)

    out, log = attention(key, mark_k[...], value[...])
    self_out[...] = out
    self_log[...] = log
    cross, log = attention(text, mark_t[...], text_value[...])
    cross_out[...] = cross
    cross_log[...] = log - jnp.log(gate_swapped[...])
    mixed_out[...] = (out + gate[...] * cross).astype(jnp.bfloat16)


def attention_grads(query, keys, marks, values, grad, out, log, mark_q):
    rows = grad.astype(jnp.float32)
    delta = per_head(rows * out, None)
    delta = pltpu.roll(delta, HEAD, 1)
    lane = lane_index(query.shape) % HEAD
    log_high = log.astype(jnp.bfloat16)
    log_low = (log - log_high.astype(jnp.float32)).astype(jnp.bfloat16)
    delta_high = delta.astype(jnp.bfloat16)
    delta_low = (delta - delta_high.astype(jnp.float32)).astype(jnp.bfloat16)
    zero = jnp.zeros_like(query)
    code = jnp.where(lane == 4, -log_high, jnp.where(lane == 5, -log_low, mark_q))
    shift = jnp.where(lane == 4, -delta_high, jnp.where(lane == 5, -delta_low, zero))
    key_grads, value_grads, query_grads = [], [], []
    for head in range(2):
        own = head_lanes(query.shape, head)
        own_keys = head_lanes(keys.shape, head)
        probe = jnp.where(own, query, code)
        probs = jnp.exp(dot_t(jnp.where(own_keys, keys, marks), probe))
        slope = dot_t(jnp.where(own_keys, values, marks), jnp.where(own, grad, shift))
        score_grad = (probs * slope).astype(jnp.bfloat16)
        value_grads.append(dot(probs.astype(jnp.bfloat16), grad))
        key_grads.append(dot(score_grad, query))
        turned = keys[:, head * HEAD : (head + 1) * HEAD].T
        query_grads.append(dot(turned, score_grad))
    first = head_lanes(keys.shape, 0)
    return (
        jnp.concatenate(query_grads, axis=0),
        jnp.where(first, key_grads[0], key_grads[1]),
        jnp.where(first, value_grads[0], value_grads[1]),
    )


def norm_back(weighted, unit, inverse):
    return inverse * (weighted - unit * (per_head(weighted * unit, None) * (1.0 / HEAD)))


def cross_back_kernel(
    query, text, text_value, raw_t, grad, out, log, gains, mark_q, mark_t,
    query_grad, raw_grad, value_grad, gain_sum, gate_sum,
):
    grad_q, grad_t, grad_v = attention_grads(
        query[...], text[...], mark_t[...], text_value[...], grad[...], out[...], log[...], mark_q[...]
    )
    query_grad[...] = grad_q.T
    value_grad[...] = grad_v.astype(jnp.bfloat16).T
    grad_t = grad_t.astype(jnp.bfloat16).astype(jnp.float32)
    unit, inverse = head_units(raw_t[...])
    gain_sum[...] = jnp.sum(grad_t * unit, axis=0, keepdims=True)
    raw_grad[...] = norm_back(grad_t * gains[2:3, :], unit, inverse).astype(jnp.bfloat16).T
    gate_sum[...] = jnp.sum(grad[...].astype(jnp.float32) * out[...], axis=0, keepdims=True)


def self_back_kernel(
    query, key, value, raw_q, raw_k, grad, out, log, cross_grad, cosine, sine, gains, mark_q, mark_k,
    query_grad, key_grad, value_grad, gain_sum,
):
    grad_q, grad_k, grad_v = attention_grads(
        query[...], key[...], mark_k[...], value[...], grad[...], out[...], log[...], mark_q[...]
    )
    value_grad[...] = grad_v.astype(jnp.bfloat16)
    cos, sin = cosine[...], sine[...]
    grad_q = (grad_q.T + cross_grad[...]) * ROOT
    for turn, raw, row, target in ((grad_q, raw_q, 0, query_grad), (grad_k, raw_k, 1, key_grad)):
        turn = turn.astype(jnp.bfloat16).astype(jnp.float32)
        turn = turn * cos - partner(turn) * sin
        unit, inverse = head_units(raw[...])
        gain_sum[row : row + 1, :] = jnp.sum(turn * unit, axis=0, keepdims=True)
        target[...] = norm_back(turn * gains[row : row + 1, :], unit, inverse).astype(jnp.bfloat16)


def pair_call(kernel, operands, outs, name, ties=(), micros=0):
    def spec(shape, cut):
        if cut is None:
            return pl.BlockSpec(shape, lambda pair: (0, 0))
        if cut == 1:
            return pl.BlockSpec((shape[0], LANES), lambda pair: (0, pair))
        return pl.BlockSpec((LANES, shape[1]), lambda pair: (pair, 0))

    width = outs[0][0][0] if outs[0][2] == 0 else outs[0][0][1]
    return pl.pallas_call(
        lambda *refs: kernel(*refs[: len(operands)], *refs[len(operands) + len(ties) :]),
        grid=(width // LANES,),
        in_specs=[spec(part.shape, cut) for part, cut in operands]
        + [pl.BlockSpec(memory_space=pl.ANY)] * len(ties),
        out_specs=[spec(shape, cut) for shape, _, cut in outs],
        out_shape=[jax.ShapeDtypeStruct(shape, kind) for shape, kind, _ in outs],
        compiler_params=pltpu.CompilerParams(vmem_limit_bytes=VMEM_LIMIT),
        cost_estimate=cost_of(micros),
        name=name,
    )(*[part for part, _ in operands], *ties)
def inverse_rms(values):
    return lax.rsqrt(jnp.mean(values * values, axis=-1, keepdims=True) + EPS)


def row_norm_back(weighted, unit, inverse):
    return inverse * (weighted - unit * jnp.mean(weighted * unit, axis=-1, keepdims=True))


def per_row(table, segment):
    return jnp.where(segment == 0.0, table[0:1], jnp.where(segment == 1.0, table[1:2], table[2:3]))


def total_of(parts):
    upper, near, far = parts
    rows = far.shape[0]
    return (
        upper[:rows].astype(jnp.float32) + near[:rows].astype(jnp.float32) + far[...].astype(jnp.float32)
    )


def segment_sums(member, values):
    high = values.astype(jnp.bfloat16)
    low = (values - high.astype(jnp.float32)).astype(jnp.bfloat16)
    return dot(member, high) + dot(member, low)


def tables_kernel(here, lens, gate, segments, head_gains, cosine, sine, mark_q, mark_k, mark_t,
                  segment, member, gate_lanes, gate_swapped, gains):
    heads = gains.shape[1] // HEAD
    lane = lane_index(gate_lanes.shape) // HEAD
    line = jnp.zeros(gate_lanes.shape, jnp.float32)
    swapped = line
    for head in range(heads):
        line = jnp.where(lane == head, gate[head], line)
        swapped = jnp.where(lane == head ^ 1, gate[head], swapped)
    gate_lanes[...] = jnp.tanh(line)
    gate_swapped[...] = jnp.tanh(swapped)
    gains[...] = jnp.concatenate([head_gains[...]] * heads, axis=1)
    rows = segments.shape[1]
    ids = segments[...]
    first = jnp.sum((ids < 1).astype(jnp.float32))
    second = jnp.sum((ids < 2).astype(jnp.float32))
    lane = lane_index((rows, LANES))
    half = HEAD // 2
    rate = jnp.exp((lane % half).astype(jnp.float32) * (-2.0 * math.log(10000.0) / HEAD))
    within = lane % HEAD
    for block, code in enumerate(ROW_ORDER):
        source = here[0] ^ code
        line = segments[pl.ds(source, 1), :].astype(jnp.float32)
        label = jnp.broadcast_to(line, (rows, rows)).T
        start = jnp.where(label == 0.0, 0.0, jnp.where(label == 1.0, first, second))
        token = (lax.broadcasted_iota(jnp.int32, (rows, LANES), 0) + source * rows).astype(jnp.float32)
        angle = (token - start) * rate
        index = slice(block * rows, (block + 1) * rows)
        cosine[index, :] = jnp.cos(angle)
        sine[index, :] = jnp.where(within < half, -1.0, 1.0) * jnp.sin(angle)
        same = ((label == within.astype(jnp.float32)) & (within < SEGS)).astype(jnp.float32)
        shut = (within == SEGS).astype(jnp.float32)
        ones = ((within >= SEGS) & (within < SEGS + 3)).astype(jnp.float32)
        mark_q[index, :] = (SHUT * same - SHUT * shut).astype(jnp.bfloat16)
        mark_k[index, :] = (same + ones).astype(jnp.bfloat16)
        if block == 0:
            segment[...] = label
            member[...] = (
                lax.broadcasted_iota(jnp.int32, (8, rows), 0).astype(jnp.float32) == line
            ).astype(jnp.bfloat16)
    for group in range(SEGS):
        lane = lane_index((TXT, LANES)) % HEAD
        row = lax.broadcasted_iota(jnp.int32, (TXT, LANES), 0)
        inside = ((lane == group) & (row < lens[group])).astype(jnp.float32)
        ones = ((lane >= SEGS) & (lane < SEGS + 3)).astype(jnp.float32)
        mark_t[group * TXT : (group + 1) * TXT, :] = (inside + ones).astype(jnp.bfloat16)


def text_kernel(captions, key_weight, value_weight, raw_out, value_out, raw_sum, value_sum):
    step = pl.program_id(0)

    @pl.when(step == 0)
    def _():
        raw_sum[...] = dot(captions[...], key_weight[...])
        value_sum[...] = dot(captions[...], value_weight[...])

    @pl.when(step > 0)
    def _():
        raw_sum[...] += dot(captions[...], key_weight[...])
        value_sum[...] += dot(captions[...], value_weight[...])

    @pl.when(step == pl.num_programs(0) - 1)
    def _():
        raw_out[...] = raw_sum[...]
        value_out[...] = value_sum[...].astype(jnp.bfloat16)


def text_call(captions, key_weight, value_weight):
    rows, depth = captions.shape
    columns = key_weight.shape[1]
    tile = depth // 4
    return pl.pallas_call(
        text_kernel,
        grid=(depth // tile,),
        in_specs=[
            pl.BlockSpec((rows, tile), lambda step: (0, step)),
            pl.BlockSpec((tile, columns), lambda step: (step, 0)),
            pl.BlockSpec((tile, columns), lambda step: (step, 0)),
        ],
        out_specs=[pl.BlockSpec((rows, columns), lambda step: (0, 0))] * 2,
        out_shape=[
            jax.ShapeDtypeStruct((rows, columns), jnp.float32),
            jax.ShapeDtypeStruct((rows, columns), jnp.bfloat16),
        ],
        scratch_shapes=[pltpu.VMEM((rows, columns), jnp.float32)] * 2,
        compiler_params=pltpu.CompilerParams(vmem_limit_bytes=VMEM_LIMIT),
        cost_estimate=cost_of(9),
        name="text",
    )(captions, key_weight, value_weight)


def project_kernel(here, own, far, near, last, mods, gains, segment_q, query_w, key_w, value_w,
                   rows_out, raw_q, raw_k, value):
    table = mods[here[0]]
    rows = own.shape[0]
    for block, part in enumerate((own, far, near, last)):
        index = slice(block * rows, (block + 1) * rows)
        values = part[...].astype(jnp.float32)
        marks = segment_q[index, :].astype(jnp.float32)
        scale = jnp.where(
            marks[:, 0:1] > 0.0, table[0:1], jnp.where(marks[:, 1:2] > 0.0, table[1:2], table[2:3])
        )
        rows_out[index, :] = (
            values * inverse_rms(values) * gains[0:1] * (1.0 + scale)
        ).astype(jnp.bfloat16)
    raw_q[...] = dot(rows_out[...], query_w[...])
    raw_k[...] = dot(rows_out[...], key_w[...])
    value[...] = dot(rows_out[...], value_w[...]).astype(jnp.bfloat16)


def middle_kernel(here, block, upper, near, far, mods, gains, segment, attn_out, middle_out, rows_out):
    attn_sum = total_of((upper, near, far))
    label = segment[:, 0:1]
    factor = jnp.tanh(per_row(mods[here[0] ^ 1], label)) * gains[1:2]
    middle = block[...].astype(jnp.float32) + factor * (attn_sum * inverse_rms(attn_sum))
    attn_out[...] = attn_sum
    middle_out[...] = middle
    scale = per_row(mods[here[0] ^ 2], label)
    rows_out[...] = (middle * inverse_rms(middle) * gains[2:3] * (1.0 + scale)).astype(jnp.bfloat16)


def block_out_kernel(here, middle, upper, near, far, grad, mods, gains, segment, member,
                     block_out, grad_out, sums):
    ffn_sum = total_of((upper, near, far))
    inverse = inverse_rms(ffn_sum)
    unit = ffn_sum * inverse
    factor = jnp.tanh(per_row(mods[here[0] ^ 3], segment[:, 0:1])) * gains[3:4]
    block_out[...] = (middle[...] + factor * unit).astype(jnp.bfloat16)
    incoming = grad[...].astype(jnp.float32)
    grad_out[...] = row_norm_back(incoming * factor, unit, inverse).astype(jnp.bfloat16)
    sums[...] = segment_sums(member[...], incoming * unit)


def middle_back_kernel(here, middle, attn, upper, near, far, grad, mods, gains, segment, member,
                       middle_grad, attn_grad, ffn_sums, attn_sums):
    grad_in = total_of((upper, near, far))
    label = segment[:, 0:1]
    inverse = inverse_rms(middle[...])
    unit = middle[...] * inverse
    factor = gains[2:3] * (1.0 + per_row(mods[here[0] ^ 2], label))
    ffn_sums[...] = segment_sums(member[...], grad_in * unit)
    grad_middle = grad[...].astype(jnp.float32) + row_norm_back(grad_in * factor, unit, inverse)
    middle_grad[...] = grad_middle
    inverse = inverse_rms(attn[...])
    unit = attn[...] * inverse
    factor = jnp.tanh(per_row(mods[here[0] ^ 1], label)) * gains[1:2]
    attn_grad[...] = row_norm_back(grad_middle * factor, unit, inverse).astype(jnp.bfloat16)
    attn_sums[...] = segment_sums(member[...], grad_middle * unit)


def block_in_kernel(here, block, middle_grad, upper, near, far, mods, gains, segment, member,
                    in_grad, sums):
    grad_in = total_of((upper, near, far))
    values = block[...].astype(jnp.float32)
    inverse = inverse_rms(values)
    unit = values * inverse
    factor = gains[0:1] * (1.0 + per_row(mods[here[0]], segment[:, 0:1]))
    in_grad[...] = (
        middle_grad[...] + row_norm_back(grad_in * factor, unit, inverse)
    ).astype(jnp.bfloat16)
    sums[...] = segment_sums(member[...], grad_in * unit)


def stack_sums_kernel(here, first, second, third, fourth, head_gain, text_gain, gate_sum, gate, out):
    width = out.shape[1]
    heads = jnp.concatenate([head_gain[0:1], head_gain[1:2], text_gain[...]], axis=1)
    inner = heads.shape[1] // 3
    gates = gate_sum[...] * (1.0 - gate[...] * gate[...])
    gates = jnp.concatenate([gates, jnp.zeros((1, width - inner), jnp.float32)], axis=1)
    lane = lane_index(gates.shape)
    moved = jnp.zeros_like(gates)
    for position in range(4):
        turn = pltpu.roll(gates, position * inner, 1) if position else gates
        moved = jnp.where((lane // inner == position) & (here[0] == position), turn, moved)
    out[...] = jnp.concatenate(
        [part[0:SEGS] for part in (first, second, third, fourth)]
        + [
            jnp.concatenate([heads, jnp.zeros((1, width - 3 * inner), jnp.float32)], axis=1),
            moved,
            jnp.zeros((2, width), jnp.float32),
        ],
        axis=0,
    )


def pack_kernel(here, own, far, near, last, mods, gains, cond, packed):
    total = own[...] + far[...] + near[...] + last[...]
    grad = jnp.zeros((SEGS, total.shape[1]), jnp.float32)
    rows = []
    for name in range(4):
        part = total[name * SEGS : (name + 1) * SEGS]
        mod = mods[here[0] ^ name]
        gain = gains[name : name + 1]
        if name % 2 == 1:
            factor = jnp.tanh(mod)
            slope = 1.0 - factor * factor
        else:
            factor = 1.0 + mod
            slope = jnp.ones_like(mod)
        rows.append(jnp.sum(part * factor, axis=0, keepdims=True))
        mine = (jnp.zeros(part.shape, jnp.int32) + here[0]) == name
        grad = jnp.where(mine, part * slope * gain, grad)
    rows.append(total[4 * SEGS : 4 * SEGS + 2])
    rows = jnp.concatenate(rows, axis=0)
    high = rows.astype(jnp.bfloat16).astype(jnp.float32)
    pad = jnp.zeros((packed.shape[0] - 2 * SEGS - 2 * SUM_ROWS, total.shape[1]), jnp.float32)
    packed[...] = jnp.concatenate(
        [grad, cond[...].astype(jnp.float32), high, rows - high, pad], axis=0
    ).astype(jnp.bfloat16)


def rider_rows(count):
    return -(-(2 * SEGS * count + 2 * SUM_ROWS) // 16) * 16


def merge_rows(count, first, second, size):
    first, second = first.astype(jnp.float32), second.astype(jnp.float32)
    wide = SEGS * count
    start = 2 * wide
    sums = (
        first[start : start + SUM_ROWS]
        + first[start + SUM_ROWS : start + 2 * SUM_ROWS]
        + second[start : start + SUM_ROWS]
        + second[start + SUM_ROWS : start + 2 * SUM_ROWS]
    )
    high = sums.astype(jnp.bfloat16).astype(jnp.float32)
    pieces = [first[:wide], second[:wide], first[wide:start], second[wide:start], high, sums - high]
    rest = size - 4 * wide - 2 * SUM_ROWS
    if rest:
        pieces.append(jnp.zeros((rest, first.shape[1]), jnp.float32))
    return jnp.concatenate(pieces, axis=0).astype(jnp.bfloat16)


def merge_kernel(ours, theirs, out):
    out[...] = merge_rows(1, ours[...], theirs[...], out.shape[0])


def ada_kernel(count, heads, dp, own, *refs):
    parts = (own,) + refs[:3]
    ada_out, norm_out, head_out, gate_out = refs[3:]
    wide = SEGS * count
    base = own.shape[0] - rider_rows(count)
    columns = ada_out.shape[0]
    share = LANES // columns
    start = pl.multiple_of(dp[0] // share * LANES, LANES)
    grads, conds = [], []
    sums = jnp.zeros((SUM_ROWS, own.shape[1]), jnp.float32)
    for part in parts:
        rows = part[base:, :].astype(jnp.float32)
        grads.append(rows[:wide])
        conds.append(part[base:, pl.ds(start, LANES)].astype(jnp.float32)[wide : 2 * wide])
        for half in range(2):
            place = 2 * wide + half * SUM_ROWS
            sums = sums + rows[place : place + SUM_ROWS]
    conds = jnp.concatenate(conds, axis=0)
    conds = pltpu.roll(conds, (LANES - dp[0] % share * columns) % LANES, 1)
    acts = conds / (1.0 + jnp.exp(-conds))
    ada_out[...] = dot(
        acts.astype(jnp.bfloat16).astype(jnp.float32).T.astype(jnp.bfloat16),
        jnp.concatenate(grads, axis=0).astype(jnp.bfloat16),
    )[:columns]
    norm_out[...] = sums[:4]
    inner = heads * HEAD
    for row in range(3):
        line = jnp.zeros((1, HEAD), jnp.float32)
        for head in range(heads):
            place = row * inner + head * HEAD
            line = line + sums[4:5, place : place + HEAD]
        head_out[row : row + 1, :] = line
    lane = lane_index((1, LANES))
    line = jnp.zeros((1, LANES), jnp.float32)
    for head in range(HEADS):
        value = jnp.sum(sums[5:6, head * HEAD : (head + 1) * HEAD], axis=1, keepdims=True)
        line = jnp.where(lane == head, value, line)
    gate_out[...] = line


def back_kernel(count, *refs):
    grads, weights, upper, lower = refs[:count], refs[count : 2 * count], refs[-2], refs[-1]
    total = dot_t(grads[0][...], weights[0][...])
    for grad, weight in zip(grads[1:], weights[1:]):
        total = total + dot_t(grad[...], weight[...])
    half = upper.shape[0]
    upper[...] = total[:half].astype(jnp.bfloat16)
    lower[...] = total[half:].astype(jnp.bfloat16)


def back_call(grads, weights, name, ties=(), micros=0):
    rows, inner = grads[0].shape
    columns = weights[0].shape[0]
    tile = columns // 3
    return pl.pallas_call(
        lambda *refs: back_kernel(len(grads), *refs[: 2 * len(grads)], *refs[-2:]),
        grid=(columns // tile,),
        in_specs=[pl.BlockSpec((rows, inner), lambda step: (0, 0))] * len(grads)
        + [pl.BlockSpec((tile, inner), lambda step: (step, 0))] * len(grads)
        + [pl.BlockSpec(memory_space=pl.ANY)] * len(ties),
        out_specs=[pl.BlockSpec((rows // 2, tile), lambda step: (0, step))] * 2,
        out_shape=[jax.ShapeDtypeStruct((rows // 2, columns), jnp.bfloat16)] * 2,
        compiler_params=pltpu.CompilerParams(vmem_limit_bytes=VMEM_LIMIT),
        cost_estimate=cost_of(micros),
        name=name,
    )(*grads, *weights, *ties)


def shards(
    block_in,
    out_grad,
    condition,
    captions,
    caption_len,
    segment_ids,
    ada_weight,
    norm_gains,
    query_weight,
    key_weight,
    value_weight,
    head_gains,
    textkey_weight,
    textvalue_weight,
    cross_gate,
    out_weight,
    gate_weight,
    up_weight,
    down_weight,
):
    rows, width = block_in.shape
    length = segment_ids.shape[0]
    heads = cross_gate.shape[0]
    inner = heads * HEAD
    half_rows = length // 2
    position = lax.axis_index("tensor")
    spot = dp_spot(position)
    here = position.reshape(1)
    b16, f32 = jnp.bfloat16, jnp.float32

    blocks = gather_tensor(block_in)
    cond_rows = jnp.pad(condition, ((0, 0), (0, width - condition.shape[1])))
    own_act = jax.nn.silu(condition.astype(f32)).astype(b16)
    own_part = jnp.dot(own_act, ada_weight, preferred_element_type=f32)
    parts = gather_tensor(own_part)
    mods = jnp.stack([parts[ROW_ORDER.index(code)] for code in range(4)])

    cosine, sine, mark_q, mark_k, mark_t, segment, member, gate_lanes, gate_swapped, gains = whole_call(
        tables_kernel,
        (here, caption_len, cross_gate),
        [segment_ids.reshape(length // rows, rows), head_gains],
        [((length, LANES), f32)] * 2
        + [((length, LANES), b16)] * 2
        + [((SEGS * TXT, LANES), b16), ((rows, LANES), f32), ((8, rows), b16)]
        + [((1, inner), f32)] * 2
        + [((3, inner), f32)],
        "tables",
        micros=2,
    )
    caption_flat = captions.reshape(-1, captions.shape[-1])
    texts = caption_flat.shape[0]
    raw_t, text_value = text_call(caption_flat, textkey_weight, textvalue_weight)
    attn_rows, raw_q, raw_k, value = whole_call(
        project_kernel,
        (here,),
        blocks + [mods, norm_gains, mark_q, query_weight, key_weight, value_weight],
        [((length, width), b16), ((length, inner), f32), ((length, inner), f32), ((length, inner), b16)],
        "project",
        micros=6,
    )
    query, key, text, mixed, self_out, cross_out, self_log, cross_log = pair_call(
        attend_kernel,
        [(raw_q, 1), (raw_k, 1), (value, 1), (raw_t, 1), (text_value, 1), (cosine, None), (sine, None)]
        + [(gains, 1), (gate_lanes, 1), (gate_swapped, 1), (mark_q, None), (mark_k, None), (mark_t, None)],
        [((length, inner), b16, 1)] * 2
        + [((texts, inner), b16, 1), ((length, inner), b16, 1)]
        + [((length, inner), f32, 1)] * 4,
        "attend",
        micros=11,
    )

    def halves(product):
        return product(slice(0, half_rows)).astype(b16), product(slice(half_rows, None)).astype(b16)

    def all_of(block):
        return jnp.concatenate(gather_tensor(block), axis=0)

    upper, lower = halves(lambda part: jnp.dot(mixed[part], out_weight, preferred_element_type=f32))
    sums, sent = scatter_tensor(upper, lower)
    attn_rows_t = turned(attn_rows, (sent,))
    wide = ((rows, width), f32)
    narrow = ((rows, width), b16)
    totals = ((8, width), f32)
    attn_sum, middle, ffn_own = whole_call(
        middle_kernel,
        (here,),
        [block_in] + sums + [mods, norm_gains, segment],
        [wide, wide, narrow],
        "middle",
    )
    ffn_rows = all_of(ffn_own)
    gate_pre = jnp.dot(ffn_rows, gate_weight, preferred_element_type=f32)
    up_pre = jnp.dot(ffn_rows, up_weight, preferred_element_type=f32)
    sigmoid_gate = jax.nn.sigmoid(gate_pre)
    silu_gate = gate_pre * sigmoid_gate
    hidden = (silu_gate * up_pre).astype(b16)
    upper, lower = halves(lambda part: jnp.dot(hidden[part], down_weight, preferred_element_type=f32))
    sums, sent = scatter_tensor(upper, lower)
    ffn_rows_t = turned(ffn_rows, (sent,))
    block_out, grad_own, sum_gate_ffn = whole_call(
        block_out_kernel,
        (here,),
        [middle] + sums + [out_grad, mods, norm_gains, segment, member],
        [narrow, narrow, totals],
        "block_out",
    )

    grad_ffn = all_of(grad_own)
    grad_hidden = times_transpose(grad_ffn, down_weight)
    grad_gate = (
        grad_hidden * up_pre * sigmoid_gate * (1.0 + gate_pre * (1.0 - sigmoid_gate))
    ).astype(b16)
    grad_up = (grad_hidden * silu_gate).astype(b16)
    upper, lower = halves(
        lambda part: times_transpose(grad_gate[part], gate_weight)
        + times_transpose(grad_up[part], up_weight)
    )
    sums, sent = scatter_tensor(upper, lower)
    grad_ffn_t = turned(grad_ffn, (sent,))
    ffn_pairs = [(ffn_rows_t, [grad_gate, grad_up]), (grad_ffn_t, [hidden])]
    (halves_two,) = row_chunks(ffn_pairs, (2,), spot, ties=(sent,), micros=FFN_MICROS)
    ffn_passed = one_on(halves_two)
    grad_middle, grad_own, sum_scale_ffn, sum_gate_attn = whole_call(
        middle_back_kernel,
        (here,),
        [middle, attn_sum] + sums + [out_grad, mods, norm_gains, segment, member],
        [wide, narrow, totals, totals],
        "middle_back",
        micros=MIDDLE_MICROS,
    )

    grad_attn = all_of(grad_own)
    grad_mixed = times_transpose(grad_attn, out_weight).astype(b16)
    cross_grad, text_grad, text_value_grad, text_gain, gate_sum = pair_call(
        cross_back_kernel,
        [(query, 1), (text, 1), (text_value, 1), (raw_t, 1), (grad_mixed, 1), (cross_out, 1)]
        + [(cross_log, 1), (gains, 1), (mark_q, None), (mark_t, None)],
        [((length, inner), f32, 1), ((inner, texts), b16, 0), ((inner, texts), b16, 0)]
        + [((1, inner), f32, 1)] * 2,
        "cross_back",
        micros=CROSS_MICROS,
    )
    ffn_one, ffn_three, ffn_kept = row_chunks(
        ffn_pairs, (1, 3, 0), spot, extra=ffn_passed, ties=(text_grad,), micros=FFN_NEXT_MICROS
    )
    text_lefts = [text_grad, text_value_grad]
    (halves_two,) = column_chunks(text_lefts, caption_flat, (2,), spot, ties=(ffn_kept,))
    text_passed = one_on(halves_two)
    query_grad, key_grad, value_grad, head_gain = pair_call(
        self_back_kernel,
        [(query, 1), (key, 1), (value, 1), (raw_q, 1), (raw_k, 1), (grad_mixed, 1), (self_out, 1)]
        + [(self_log, 1), (cross_grad, 1), (cosine, None), (sine, None), (gains, 1)]
        + [(mark_q, None), (mark_k, None)],
        [((length, inner), b16, 1)] * 3 + [((2, inner), f32, 1)],
        "self_back",
        (halves_two[0],),
        micros=SELF_MICROS,
    )

    hidden_cols = hidden.shape[1]
    block_rows = width // BLOCKS
    got = [by_slots(part) for part in to_neighbours(ffn_kept, ffn_one, ffn_three)]
    shape = (PAIR, block_rows, 3 * hidden_cols)
    ffn_stage = tiled_call(
        ffn_second_kernel, (spot,), got, [(shape, b16)] * RING, "ffn_second",
        -1,
        4, (query_grad,)
    )
    upper, lower = back_call(
        [query_grad, key_grad, value_grad], [query_weight, key_weight, value_weight], "attn_back"
    )
    sums, sent = scatter_tensor(upper, lower)
    in_grad, sum_scale_attn = whole_call(
        block_in_kernel,
        (here,),
        [block_in, grad_middle] + sums + [mods, norm_gains, segment, member],
        [narrow, totals],
        "block_in",
        (ffn_stage[0],),
        micros=BLOCK_IN_MICROS,
    )
    (stacked,) = whole_call(
        stack_sums_kernel,
        (here,),
        [sum_scale_attn, sum_gate_attn, sum_scale_ffn, sum_gate_ffn]
        + [head_gain, text_gain, gate_sum, gate_lanes],
        [((16, width), f32)],
        "stack_sums",
    )
    sums_stacked = stacked
    text_one, text_three, text_kept = column_chunks(
        text_lefts, caption_flat, (1, 3, 0), spot, extra=text_passed, ties=(sums_stacked,), micros=TEXT_MICROS
    )
    stacked = gather_tensor(stacked)
    kept, sent = tiled_call(
        ffn_third_kernel,
        (spot,),
        exchange(ffn_stage, "second"),
        [(shape[1:], b16)] * 2,
        "ffn_third",
        -1,
        2,
        (text_kept,),
    )
    (riders,) = whole_call(
        pack_kernel,
        (here,),
        stacked + [mods, norm_gains, cond_rows],
        [((rider_rows(1), width), b16)],
        "pack",
        (kept,),
    )
    theirs = dp_permute(riders, "z", 1)
    (riders,) = whole_call(
        merge_kernel, (), [riders, theirs], [((rider_rows(PAIR), width), b16)], "merge"
    )
    attn_pairs = [
        (attn_rows_t, [query_grad, key_grad, value_grad]),
        (turned(grad_attn, (halves_two[0],)), [mixed]),
    ]
    (halves_two,) = row_chunks(attn_pairs, (2,), spot, riders=(riders,), micros=ATTN_FIRST_MICROS)
    attn_passed = one_on(halves_two)
    gate_sum_out, up_sum_out, down_sum_out = whole_call(
        ffn_last_kernel,
        (),
        exchange([kept, sent], "z"),
        [((block_rows, hidden_cols), f32)] * 2 + [((hidden_cols, block_rows), f32)],
        "ffn_last",
    )
    text_rows = caption_flat.shape[1] // BLOCKS
    attn_one, attn_three, attn_kept = row_chunks(
        attn_pairs, (1, 3, 0), spot, extra=attn_passed, ties=(kept,), riders=(riders,), micros=ATTN_MICROS
    )
    stage = tiled_call(
        text_second_kernel,
        (spot,),
        to_neighbours(text_kept, text_one, text_three),
        [((2 * inner, PAIR * text_rows), b16)] * RING,
        "text_second",
        0,
        4,
        (attn_kept,),
    )
    kept, sent = tiled_call(
        text_third_kernel,
        (spot,),
        exchange(stage, "second"),
        [((2 * inner, text_rows), b16)] * 2,
        "text_third",
        0,
        2,
        (gate_sum_out,),
    )
    textkey_sum, textvalue_sum = whole_call(
        text_last_kernel,
        (),
        exchange([kept, sent], "z"),
        [((text_rows, inner), f32)] * 2,
        "text_last",
    )
    stage = tiled_call(
        functools.partial(attn_second_kernel, block_rows),
        (spot,),
        [riders] + to_neighbours(attn_kept, attn_one, attn_three),
        [((PAIR * block_rows + rider_rows(4 * PAIR), width), b16)] * RING,
        "attn_second",
        -1,
        4,
        (kept,),
    )
    got = exchange(stage, "second")
    kept, sent = tiled_call(
        attn_third_kernel, (spot,), got, [((block_rows, width), b16)] * 2, "attn_third",
        -1,
        2
    )
    ada_grad, norm_grads, head_grads, crossgate = tiled_call(
        functools.partial(ada_kernel, 4 * PAIR, heads),
        (lax.axis_index("dp").reshape(1),),
        got,
        [((condition.shape[1] // BLOCKS, width), f32), ((4, width), f32), ((3, HEAD), f32)]
        + [((1, LANES), f32)],
        "ada",
        0,
        1,
        (kept,),
    )
    crossgate_grad = crossgate[0, :HEADS]
    query_sum, key_sum, value_sum, outw_sum = whole_call(
        attn_last_kernel,
        (),
        exchange([kept, sent], "z"),
        [((block_rows, inner), f32)] * 3 + [((inner, block_rows), f32)],
        "attn_last",
    )
    return (
        block_out,
        in_grad,
        ada_grad,
        norm_grads,
        query_sum,
        key_sum,
        value_sum,
        head_grads,
        textkey_sum,
        textvalue_sum,
        crossgate_grad,
        outw_sum,
        gate_sum_out,
        up_sum_out,
        down_sum_out,
    )


def solution(mesh):
    return jax.shard_map(
        shards,
        mesh=mesh,
        in_specs=(
            P(("dp", "tensor"), None),
            P(("dp", "tensor"), None),
            P("dp", None),
            P("dp", None, None),
            P("dp"),
            P("dp"),
            P(None, "tensor"),
            P(),
            P(None, "tensor"),
            P(None, "tensor"),
            P(None, "tensor"),
            P(),
            P(None, "tensor"),
            P(None, "tensor"),
            P("tensor"),
            P("tensor", None),
            P(None, "tensor"),
            P(None, "tensor"),
            P("tensor", None),
        ),
        out_specs=(
            P(("dp", "tensor"), None),
            P(("dp", "tensor"), None),
            P("dp", "tensor"),
            P(),
            P("dp", "tensor"),
            P("dp", "tensor"),
            P("dp", "tensor"),
            P(),
            P("dp", "tensor"),
            P("dp", "tensor"),
            P(),
            P("tensor", "dp"),
            P("dp", "tensor"),
            P("dp", "tensor"),
            P("tensor", "dp"),
        ),
        check_vma=False,
    )
```

```python
import functools
import math

import jax
import jax.numpy as jnp
from jax import lax
from jax.experimental import pallas as pl
from jax.experimental.pallas import tpu as pltpu
from jax.sharding import PartitionSpec as P

HEAD = 64
HEADS = 24
TXT = 256
SEGS = 3
EPS = 1e-06
LANES = 2 * HEAD
SHUT = 256.0
ROOT = HEAD ** (-0.5)
VMEM_LIMIT = 24 * 2**20
NO_COST = pl.CostEstimate(flops=0, bytes_accessed=0, transcendentals=0)


def cost_of(micros):
    return pl.CostEstimate(flops=int(micros * 1e9), bytes_accessed=0, transcendentals=0)


SUM_ROWS = 6
CROSS_MICROS = 10
BLOCK_IN_MICROS = 0
FFN_MICROS = 3
FFN_NEXT_MICROS = 8
MIDDLE_MICROS = 10
SELF_MICROS = 0
ATTN_MICROS = 3
TEXT_MICROS = 8
ATTN_FIRST_MICROS = 0

RING = 4
PAIR = 2
BLOCKS = RING * PAIR * RING
SLOTS = BLOCKS // RING
SEND_ORDER = (2, 1, 3, 0)
CORE_SWAP = [(0, 1), (1, 0), (2, 3), (3, 2)]
CHIP_SWAP = [(0, 2), (2, 0), (1, 3), (3, 1)]
ROW_ORDER = (0, 2, 1, 3)

def dp_index(x, z, y):
    return (x * PAIR + z) * RING + y


def dp_perm(axis, step):
    pairs = []

    def moved(place, size):
        if step == "flip":
            return place ^ 1
        if step == "mirror":
            return size - 1 - place
        return (place + step) % size

    for x in range(RING):
        for z in range(PAIR):
            for y in range(RING):
                for tensor in range(2 * PAIR):
                    way = axis
                    if axis in ("first", "second"):
                        way = "x" if (tensor % 2 == 0) == (axis == "first") else "y"
                    target = {
                        "x": (moved(x, RING), z, y),
                        "y": (x, z, moved(y, RING)),
                        "z": (x, moved(z, PAIR), y),
                    }[way]
                    pairs.append(
                        (
                            dp_index(x, z, y) * 2 * PAIR + tensor,
                            dp_index(*target) * 2 * PAIR + tensor,
                        )
                    )
    return pairs


def dp_permute(values, axis, step):
    return lax.ppermute(values, ("dp", "tensor"), dp_perm(axis, step))


def dp_spot(position):
    index = lax.axis_index("dp")
    x, z, y = index // (RING * PAIR), index // RING % PAIR, index % RING
    core = position % 2
    return jnp.stack([jnp.where(core == 0, x, y), z, jnp.where(core == 0, y, x), core])


def swap_core(values):
    return lax.ppermute(values, "tensor", CORE_SWAP)


def swap_chip(values):
    return lax.ppermute(values, "tensor", CHIP_SWAP)


def times_transpose(left, right):
    return lax.dot_general(
        left, right, (((1,), (1,)), ((), ())), preferred_element_type=jnp.float32
    )


def gather_tensor(block):
    far = swap_chip(block)
    near = swap_core(block)
    return [block, far, near, swap_core(far)]


def scatter_tensor(upper, lower):
    near = swap_core(lower)
    rows = upper.shape[0] // 2
    far = (upper[rows:].astype(jnp.float32) + near[rows:].astype(jnp.float32)).astype(near.dtype)
    return [upper, near, swap_chip(far)], far


def turn_kernel(source, target):
    target[...] = source[...].T


def turned(values, ties=()):
    tile = 512 if values.shape[1] % 512 == 0 else values.shape[1]
    return pl.pallas_call(
        lambda source, *rest: turn_kernel(source, rest[-1]),
        grid=(values.shape[1] // tile,),
        in_specs=[pl.BlockSpec((values.shape[0], tile), lambda step: (0, step))]
        + [pl.BlockSpec(memory_space=pl.ANY)] * len(ties),
        out_specs=pl.BlockSpec((tile, values.shape[0]), lambda step: (step, 0)),
        out_shape=jax.ShapeDtypeStruct(values.shape[::-1], values.dtype),
        compiler_params=pltpu.CompilerParams(vmem_limit_bytes=VMEM_LIMIT),
        cost_estimate=NO_COST,
    )(values, *ties)


def chunk_block(offset, slot, spot):
    first = (spot[0] + offset) % RING
    z, second = slot // RING, slot % RING
    x = jnp.where(spot[3] == 0, first, second)
    y = jnp.where(spot[3] == 0, second, first)
    return dp_index(x, z, y)


def offset_of_step(offsets, step):
    offset = offsets[-1]
    for place in range(len(offsets) - 1):
        offset = jnp.where(step == place, offsets[place], offset)
    return offset


def chunk_kernel(make, offsets, halves, extra, outs, held, sems):
    step = pl.program_id(0)
    first, second = halves

    def copies(place):
        slot = held.at[place % 2]
        if offsets[place] != 2:
            return [pltpu.make_async_copy(slot, outs[place], sems.at[place % 2, 0])]
        return [
            pltpu.make_async_copy(slot.at[half], out, sems.at[place % 2, way])
            for way, (half, out) in enumerate(zip((first, second), outs[place]))
        ]

    for place, offset in enumerate(offsets):

        @pl.when(step == place)
        def _(place=place, offset=offset):
            if place >= 2:
                for copy in copies(place - 2):
                    copy.wait()
            added = {1: (first, extra[0]), 3: (second, extra[1])}.get(offset) if extra else None
            make(held.at[place % 2], added, offset)
            for copy in copies(place):
                copy.start()
            if place == len(offsets) - 1:
                for last in range(max(place - 1, 0), place + 1):
                    for copy in copies(last):
                        copy.wait()


def chunk_call(make, operands, specs, offsets, halves, shape, spot, extra, ties, name, micros):
    count = len(operands)
    pieces = []
    for offset in offsets:
        if offset == 2:
            pieces += [tuple(len(range(*s.indices(d))) for s, d in zip(h, shape)) for h in halves]
        else:
            pieces.append(shape)

    def kernel(spot_ref, *refs):
        inputs, extras = refs[:count], refs[count : count + len(extra)]
        outs = list(refs[-len(pieces) - 2 : -2])
        grouped = []
        for offset in offsets:
            grouped.append((outs.pop(0), outs.pop(0)) if offset == 2 else outs.pop(0))
        chunk_kernel(
            functools.partial(make, inputs), offsets, halves, extras, grouped, refs[-2], refs[-1]
        )

    found = pl.pallas_call(
        kernel,
        grid_spec=pltpu.PrefetchScalarGridSpec(
            num_scalar_prefetch=1,
            grid=(len(offsets),),
            in_specs=list(specs)
            + [pl.BlockSpec(part.shape, lambda step, spot: (0, 0)) for part in extra]
            + [pl.BlockSpec(memory_space=pl.ANY)] * len(ties),
            out_specs=[pl.BlockSpec(memory_space=pl.ANY)] * len(pieces),
            scratch_shapes=[
                pltpu.VMEM((2,) + shape, jnp.bfloat16),
                pltpu.SemaphoreType.DMA((2, 2)),
            ],
        ),
        out_shape=[jax.ShapeDtypeStruct(piece, jnp.bfloat16) for piece in pieces],
        compiler_params=pltpu.CompilerParams(vmem_limit_bytes=VMEM_LIMIT),
        cost_estimate=cost_of(micros),
        name=name,
    )(spot, *operands, *extra, *ties)
    found = list(found)
    return [
        (found.pop(0), found.pop(0)) if offset == 2 else found.pop(0) for offset in offsets
    ]


def make_rows(groups, inputs, slot, added, offset):
    lefts, rights = inputs[: SLOTS * len(groups)], inputs[SLOTS * len(groups) :]
    size = SLOTS * lefts[0].shape[1]
    if len(rights) > sum(groups):
        riders = rights[-1][...]
        count, half = riders.shape[0], riders.shape[1] // 2
        first, second = slice(size, size + count), slice(size + count, size + 2 * count)
        if offset == 2:
            for side in (slice(0, half), slice(half, 2 * half)):
                slot[first, side] = riders[:, :half]
                slot[second, side] = riders[:, half:]
        else:
            slot[first, :] = riders
            if offset == 1:
                slot[second, :half] = added[1][first, :]
                slot[second, half:] = added[1][second, :]
            else:
                slot[second, :] = riders
    column = place = 0
    for group, count in enumerate(groups):
        rows = jnp.concatenate(
            [left[0] for left in lefts[SLOTS * group : SLOTS * (group + 1)]], axis=0
        )
        for right in rights[place : place + count]:
            wide = right.shape[1]
            product = dot(rows, right[...])
            low, high = column, column
            if added is not None:
                low = min(max(column, added[0][1].start), column + wide)
                high = min(max(column, added[0][1].stop), column + wide)
            for start, stop in ((column, low), (low, high), (high, column + wide)):
                if start < stop:
                    part = product[:, start - column : stop - column]
                    if (start, stop) == (low, high):
                        base = added[0][1].start
                        part = part + added[1][:size, start - base : stop - base].astype(jnp.float32)
                    slot[:size, start:stop] = part.astype(jnp.bfloat16)
            column += wide
        place += count


def row_chunks(pairs, offsets, spot, extra=(), ties=(), micros=0, riders=()):
    lefts = [left.reshape(BLOCKS, left.shape[0] // BLOCKS, left.shape[1]) for left, _ in pairs]
    rights = [right for _, group in pairs for right in group]
    total = sum(right.shape[1] for right in rights)
    specs, operands = [], []
    for left in lefts:
        for slot in range(SLOTS):
            specs.append(
                pl.BlockSpec(
                    (1,) + left.shape[1:],
                    lambda step, spot, slot=slot: (
                        chunk_block(offset_of_step(offsets, step), slot, spot),
                        0,
                        0,
                    ),
                )
            )
            operands.append(left)
    specs += [pl.BlockSpec(right.shape, lambda step, spot: (0, 0)) for right in rights]
    specs += [pl.BlockSpec(part.shape, lambda step, spot: (0, 0)) for part in riders]
    rows = SLOTS * lefts[0].shape[1] + sum(2 * part.shape[0] for part in riders)
    halves = [(slice(0, rows), slice(0, total // 2)), (slice(0, rows), slice(total // 2, total))]
    return chunk_call(
        functools.partial(make_rows, [len(group) for _, group in pairs]),
        operands + rights + list(riders),
        specs,
        offsets,
        halves,
        (rows, total),
        spot,
        extra,
        ties,
        "row_chunks",
        micros,
    )


def make_columns(lefts, inputs, slot, added, offset):
    whole = jnp.concatenate([right[...] for right in inputs[lefts:]], axis=1)
    row = 0
    for left in inputs[:lefts]:
        product = dot(left[...], whole)
        if added is not None and added[0][0].start == row:
            product = product + added[1][...].astype(jnp.float32)
        slot[row : row + left.shape[0], :] = product.astype(jnp.bfloat16)
        row += left.shape[0]


def column_chunks(lefts, right, offsets, spot, extra=(), ties=(), micros=0):
    rows = lefts[0].shape[0]
    depth, columns = right.shape
    specs = [pl.BlockSpec(left.shape, lambda step, spot: (0, 0)) for left in lefts]
    for slot in range(SLOTS):
        specs.append(
            pl.BlockSpec(
                (depth, columns // BLOCKS),
                lambda step, spot, slot=slot: (
                    0,
                    chunk_block(offset_of_step(offsets, step), slot, spot),
                ),
            )
        )
    lanes = columns // RING
    halves = [(slice(0, rows), slice(0, lanes)), (slice(rows, 2 * rows), slice(0, lanes))]
    return chunk_call(
        functools.partial(make_columns, len(lefts)),
        list(lefts) + [right] * SLOTS,
        specs,
        offsets,
        halves,
        (2 * rows, lanes),
        spot,
        extra,
        ties,
        "column_chunks",
        micros,
    )


def add_up(refs, index):
    total = refs[0][index].astype(jnp.float32)
    for ref in refs[1:]:
        total = total + ref[index].astype(jnp.float32)
    return total


def lane_slice(start, size):
    return (slice(None), pl.ds(pl.multiple_of(start * size, size), size))


def halving_places(spot):
    own = spot[2]
    other = own ^ 1
    return (own, RING - 1 - own), (other, RING - 1 - other)


def ffn_second_kernel(spot, *refs):
    parts = refs[:-2]
    for out, places in zip(refs[-2:], halving_places(spot)):
        for index, place in enumerate(places):
            for z in range(PAIR):
                out[index * PAIR + z] = add_up(parts, z * RING + place).astype(jnp.bfloat16)


def ffn_middle_kernel(kept, got, own, sent):
    for out, start in ((own, 0), (sent, PAIR)):
        for z in range(PAIR):
            out[z] = add_up((kept, got), start + z).astype(jnp.bfloat16)


def ffn_third_kernel(spot, *refs):
    for out, z in ((refs[-2], spot[1]), (refs[-1], (spot[1] + 1) % PAIR)):
        out[...] = add_up(refs[:-2], z).astype(jnp.bfloat16)


def ffn_last_kernel(kept, got, gate_out, up_out, down_out):
    total = kept[...].astype(jnp.float32) + got[...].astype(jnp.float32)
    hidden = gate_out.shape[1]
    gate_out[...] = total[:, :hidden]
    up_out[...] = total[:, hidden : 2 * hidden]
    down_out[...] = total[:, 2 * hidden :].T


def text_second_kernel(spot, *refs):
    parts = refs[:-2]
    lanes = parts[0].shape[1] // SLOTS
    for out, places in zip(refs[-2:], halving_places(spot)):
        for index, place in enumerate(places):
            for z in range(PAIR):
                start = (index * PAIR + z) * lanes
                out[:, start : start + lanes] = add_up(
                    parts, lane_slice(z * RING + place, lanes)
                ).astype(jnp.bfloat16)


def text_middle_kernel(kept, got, own, sent):
    wide = own.shape[1]
    for out, start in ((own, 0), (sent, wide)):
        index = (slice(None), slice(start, start + wide))
        out[...] = add_up((kept, got), index).astype(jnp.bfloat16)


def text_third_kernel(spot, *refs):
    lanes = refs[-1].shape[1]
    for out, z in ((refs[-2], spot[1]), (refs[-1], (spot[1] + 1) % PAIR)):
        out[...] = add_up(refs[:-2], lane_slice(z, lanes)).astype(jnp.bfloat16)


def text_last_kernel(kept, got, textkey, textvalue):
    total = kept[...].astype(jnp.float32) + got[...].astype(jnp.float32)
    columns = textkey.shape[1]
    textkey[...] = total[:columns].T
    textvalue[...] = total[columns:].T


def attn_second_kernel(rows, spot, riders, *refs):
    parts, outs = refs[:-RING], refs[-RING:]
    size, count = SLOTS * rows, riders.shape[0]
    for offset in range(RING):
        for z in range(PAIR):
            slot = z * RING + (spot[2] + offset) % RING
            index = (pl.ds(pl.multiple_of(slot * rows, 16), rows), slice(None))
            outs[offset][z * rows : (z + 1) * rows, :] = add_up(parts, index).astype(jnp.bfloat16)
    ahead, behind = parts[1], parts[2]
    pairs = (
        (riders[...], ahead[size : size + count, :]),
        (behind[size : size + count, :], ahead[size + count : size + 2 * count, :]),
    )
    joined = [merge_rows(PAIR, first, second, rider_rows(2 * PAIR)) for first, second in pairs]
    joined = merge_rows(2 * PAIR, joined[0], joined[1], rider_rows(4 * PAIR))
    for out in outs:
        out[PAIR * rows :, :] = joined


def attn_third_kernel(spot, *refs):
    rows = refs[-1].shape[0]
    for out, z in ((refs[-2], spot[1]), (refs[-1], (spot[1] + 1) % PAIR)):
        index = (pl.ds(pl.multiple_of(z * rows, 16), rows), slice(None))
        out[...] = add_up(refs[:RING], index).astype(jnp.bfloat16)


def attn_last_kernel(kept, got, query, key, value, outw):
    total = kept[...].astype(jnp.float32) + got[...].astype(jnp.float32)
    columns = query.shape[1]
    for place, out in enumerate((query, key, value)):
        out[...] = total[:, place * columns : (place + 1) * columns]
    outw[...] = total[:, 3 * columns :].T


def whole_call(kernel, scalars, operands, outs, name, ties=(), scratch=(), micros=0):
    whole = pl.BlockSpec(memory_space=pltpu.VMEM)
    count = len(scalars) + len(operands)
    return pl.pallas_call(
        lambda *refs: kernel(*refs[:count], *refs[count + len(ties) :]),
        in_specs=[pl.BlockSpec(memory_space=pltpu.SMEM)] * len(scalars)
        + [whole] * len(operands)
        + [pl.BlockSpec(memory_space=pl.ANY)] * len(ties),
        out_specs=[whole] * len(outs),
        out_shape=[jax.ShapeDtypeStruct(shape, kind) for shape, kind in outs],
        scratch_shapes=list(scratch),
        compiler_params=pltpu.CompilerParams(vmem_limit_bytes=VMEM_LIMIT),
        cost_estimate=cost_of(micros),
        name=name,
    )(*scalars, *operands, *ties)


def tiled_call(kernel, scalars, operands, outs, name, axis, tiles, ties=(), micros=0, axes=None):
    def spec(shape, axis):
        block = list(shape)
        block[axis] //= tiles
        if axis == 0:
            return pl.BlockSpec(tuple(block), lambda step: (step,) + (0,) * (len(shape) - 1))
        return pl.BlockSpec(tuple(block), lambda step: (0,) * (len(shape) - 1) + (step,))

    count = len(scalars) + len(operands)
    return pl.pallas_call(
        lambda *refs: kernel(*refs[:count], *refs[count + len(ties) :]),
        grid=(tiles,),
        in_specs=[pl.BlockSpec(memory_space=pltpu.SMEM)] * len(scalars)
        + [spec(part.shape, way) for part, way in zip(operands, axes or [axis] * len(operands))]
        + [pl.BlockSpec(memory_space=pl.ANY)] * len(ties),
        out_specs=[spec(shape, axis) for shape, _ in outs],
        out_shape=[jax.ShapeDtypeStruct(shape, kind) for shape, kind in outs],
        compiler_params=pltpu.CompilerParams(vmem_limit_bytes=VMEM_LIMIT),
        cost_estimate=cost_of(micros),
        name=name,
    )(*scalars, *[pltpu.with_memory_space_constraint(part, pltpu.HBM) for part in operands], *ties)


def exchange(chunks, axis):
    return [chunks[0]] + [
        dp_permute(chunks[step], axis, step) for step in range(1, len(chunks))
    ]


def one_on(halves):
    return dp_permute(halves[0], "first", 1), dp_permute(halves[1], "first", RING - 1)


def to_neighbours(own, ahead, behind):
    return [own, dp_permute(ahead, "first", 1), dp_permute(behind, "first", RING - 1)]


def by_slots(chunk):
    return chunk.reshape(SLOTS, chunk.shape[0] // SLOTS, chunk.shape[1])


def lane_index(shape):
    return lax.broadcasted_iota(jnp.int32, shape, 1)


def head_lanes(shape, head):
    lane = lane_index(shape)
    return (lane < HEAD) if head == 0 else (lane >= HEAD)


def per_head(values, reduce):
    first = head_lanes(values.shape, 0)
    left = jnp.sum(jnp.where(first, values, 0.0), axis=1, keepdims=True)
    right = jnp.sum(jnp.where(first, 0.0, values), axis=1, keepdims=True)
    return jnp.where(first, left, right)


def head_units(raw):
    inverse = lax.rsqrt(per_head(raw * raw, None) * (1.0 / HEAD) + EPS)
    return raw * inverse, inverse


def partner(values):
    lane = lane_index(values.shape)
    return jnp.where(
        lane % HEAD < HEAD // 2,
        pltpu.roll(values, LANES - HEAD // 2, 1),
        pltpu.roll(values, HEAD // 2, 1),
    )


def dot(left, right):
    return jnp.dot(left, right, preferred_element_type=jnp.float32)


def dot_t(left, right):
    return lax.dot_general(left, right, (((1,), (1,)), ((), ())), preferred_element_type=jnp.float32)


def attend_kernel(
    raw_q, raw_k, value, raw_t, text_value, cosine, sine, gains, gate, gate_swapped, mark_q, mark_k, mark_t,
    query_out, key_out, text_out, mixed_out, self_out, cross_out, self_log, cross_log,
):
    cos, sin = cosine[...], sine[...]
    unit = head_units(raw_q[...])[0] * gains[0:1, :]
    query = ((unit * cos + partner(unit) * sin).astype(jnp.bfloat16) * ROOT).astype(jnp.bfloat16)
    unit = head_units(raw_k[...])[0] * gains[1:2, :]
    key = (unit * cos + partner(unit) * sin).astype(jnp.bfloat16)
    text = (head_units(raw_t[...])[0] * gains[2:3, :]).astype(jnp.bfloat16)
    query_out[...] = query
    key_out[...] = key
    text_out[...] = text

    def attention(keys, marks, values):
        outs, sums = [], []
        for head in range(2):
            own = head_lanes(query.shape, head)
            own_keys = head_lanes(keys.shape, head)
            probe = jnp.where(own, query, mark_q[...])
            scores = dot_t(probe, jnp.where(own_keys, keys, marks))
            weights = jnp.exp(scores).astype(jnp.bfloat16)
            both = dot(weights, jnp.where(own_keys, values, jnp.ones_like(values)))
            outs.append(both)
        first = head_lanes(outs[0].shape, 0)
        product = jnp.where(first, outs[0], outs[1])
        total = jnp.where(first, outs[1], outs[0])
        return product / pltpu.roll(total, HEAD, 1), jnp.log(total)

    out, log = attention(key, mark_k[...], value[...])
    self_out[...] = out
    self_log[...] = log
    cross, log = attention(text, mark_t[...], text_value[...])
    cross_out[...] = cross
    cross_log[...] = log - jnp.log(gate_swapped[...])
    mixed_out[...] = (out + gate[...] * cross).astype(jnp.bfloat16)


def attention_grads(query, keys, marks, values, grad, out, log, mark_q):
    rows = grad.astype(jnp.float32)
    delta = per_head(rows * out, None)
    delta = pltpu.roll(delta, HEAD, 1)
    lane = lane_index(query.shape) % HEAD
    log_high = log.astype(jnp.bfloat16)
    log_low = (log - log_high.astype(jnp.float32)).astype(jnp.bfloat16)
    delta_high = delta.astype(jnp.bfloat16)
    delta_low = (delta - delta_high.astype(jnp.float32)).astype(jnp.bfloat16)
    zero = jnp.zeros_like(query)
    code = jnp.where(lane == 4, -log_high, jnp.where(lane == 5, -log_low, mark_q))
    shift = jnp.where(lane == 4, -delta_high, jnp.where(lane == 5, -delta_low, zero))
    key_grads, value_grads, query_grads = [], [], []
    for head in range(2):
        own = head_lanes(query.shape, head)
        own_keys = head_lanes(keys.shape, head)
        probe = jnp.where(own, query, code)
        probs = jnp.exp(dot_t(jnp.where(own_keys, keys, marks), probe))
        slope = dot_t(jnp.where(own_keys, values, marks), jnp.where(own, grad, shift))
        score_grad = (probs * slope).astype(jnp.bfloat16)
        value_grads.append(dot(probs.astype(jnp.bfloat16), grad))
        key_grads.append(dot(score_grad, query))
        turned = keys[:, head * HEAD : (head + 1) * HEAD].T
        query_grads.append(dot(turned, score_grad))
    first = head_lanes(keys.shape, 0)
    return (
        jnp.concatenate(query_grads, axis=0),
        jnp.where(first, key_grads[0], key_grads[1]),
        jnp.where(first, value_grads[0], value_grads[1]),
    )


def norm_back(weighted, unit, inverse):
    return inverse * (weighted - unit * (per_head(weighted * unit, None) * (1.0 / HEAD)))


def cross_back_kernel(
    query, text, text_value, raw_t, grad, out, log, gains, mark_q, mark_t,
    query_grad, raw_grad, value_grad, gain_sum, gate_sum,
):
    grad_q, grad_t, grad_v = attention_grads(
        query[...], text[...], mark_t[...], text_value[...], grad[...], out[...], log[...], mark_q[...]
    )
    query_grad[...] = grad_q.T
    value_grad[...] = grad_v.astype(jnp.bfloat16).T
    grad_t = grad_t.astype(jnp.bfloat16).astype(jnp.float32)
    unit, inverse = head_units(raw_t[...])
    gain_sum[...] = jnp.sum(grad_t * unit, axis=0, keepdims=True)
    raw_grad[...] = norm_back(grad_t * gains[2:3, :], unit, inverse).astype(jnp.bfloat16).T
    gate_sum[...] = jnp.sum(grad[...].astype(jnp.float32) * out[...], axis=0, keepdims=True)


def self_back_kernel(
    query, key, value, raw_q, raw_k, grad, out, log, cross_grad, cosine, sine, gains, mark_q, mark_k,
    query_grad, key_grad, value_grad, gain_sum,
):
    grad_q, grad_k, grad_v = attention_grads(
        query[...], key[...], mark_k[...], value[...], grad[...], out[...], log[...], mark_q[...]
    )
    value_grad[...] = grad_v.astype(jnp.bfloat16)
    cos, sin = cosine[...], sine[...]
    grad_q = (grad_q.T + cross_grad[...]) * ROOT
    for turn, raw, row, target in ((grad_q, raw_q, 0, query_grad), (grad_k, raw_k, 1, key_grad)):
        turn = turn.astype(jnp.bfloat16).astype(jnp.float32)
        turn = turn * cos - partner(turn) * sin
        unit, inverse = head_units(raw[...])
        gain_sum[row : row + 1, :] = jnp.sum(turn * unit, axis=0, keepdims=True)
        target[...] = norm_back(turn * gains[row : row + 1, :], unit, inverse).astype(jnp.bfloat16)


def pair_call(kernel, operands, outs, name, ties=(), micros=0):
    def spec(shape, cut):
        if cut is None:
            return pl.BlockSpec(shape, lambda pair: (0, 0))
        if cut == 1:
            return pl.BlockSpec((shape[0], LANES), lambda pair: (0, pair))
        return pl.BlockSpec((LANES, shape[1]), lambda pair: (pair, 0))

    width = outs[0][0][0] if outs[0][2] == 0 else outs[0][0][1]
    return pl.pallas_call(
        lambda *refs: kernel(*refs[: len(operands)], *refs[len(operands) + len(ties) :]),
        grid=(width // LANES,),
        in_specs=[spec(part.shape, cut) for part, cut in operands]
        + [pl.BlockSpec(memory_space=pl.ANY)] * len(ties),
        out_specs=[spec(shape, cut) for shape, _, cut in outs],
        out_shape=[jax.ShapeDtypeStruct(shape, kind) for shape, kind, _ in outs],
        compiler_params=pltpu.CompilerParams(vmem_limit_bytes=VMEM_LIMIT),
        cost_estimate=cost_of(micros),
        name=name,
    )(*[part for part, _ in operands], *ties)
def inverse_rms(values):
    return lax.rsqrt(jnp.mean(values * values, axis=-1, keepdims=True) + EPS)


def row_norm_back(weighted, unit, inverse):
    return inverse * (weighted - unit * jnp.mean(weighted * unit, axis=-1, keepdims=True))


def per_row(table, segment):
    return jnp.where(segment == 0.0, table[0:1], jnp.where(segment == 1.0, table[1:2], table[2:3]))


def total_of(parts):
    upper, near, far = parts
    rows = far.shape[0]
    return (
        upper[:rows].astype(jnp.float32) + near[:rows].astype(jnp.float32) + far[...].astype(jnp.float32)
    )


def segment_sums(member, values):
    high = values.astype(jnp.bfloat16)
    low = (values - high.astype(jnp.float32)).astype(jnp.bfloat16)
    return dot(member, high) + dot(member, low)


def tables_kernel(here, lens, gate, segments, head_gains, cosine, sine, mark_q, mark_k, mark_t,
                  segment, member, gate_lanes, gate_swapped, gains):
    heads = gains.shape[1] // HEAD
    lane = lane_index(gate_lanes.shape) // HEAD
    line = jnp.zeros(gate_lanes.shape, jnp.float32)
    swapped = line
    for head in range(heads):
        line = jnp.where(lane == head, gate[head], line)
        swapped = jnp.where(lane == head ^ 1, gate[head], swapped)
    gate_lanes[...] = jnp.tanh(line)
    gate_swapped[...] = jnp.tanh(swapped)
    gains[...] = jnp.concatenate([head_gains[...]] * heads, axis=1)
    rows = segments.shape[1]
    ids = segments[...]
    first = jnp.sum((ids < 1).astype(jnp.float32))
    second = jnp.sum((ids < 2).astype(jnp.float32))
    lane = lane_index((rows, LANES))
    half = HEAD // 2
    rate = jnp.exp((lane % half).astype(jnp.float32) * (-2.0 * math.log(10000.0) / HEAD))
    within = lane % HEAD
    for block, code in enumerate(ROW_ORDER):
        source = here[0] ^ code
        line = segments[pl.ds(source, 1), :].astype(jnp.float32)
        label = jnp.broadcast_to(line, (rows, rows)).T
        start = jnp.where(label == 0.0, 0.0, jnp.where(label == 1.0, first, second))
        token = (lax.broadcasted_iota(jnp.int32, (rows, LANES), 0) + source * rows).astype(jnp.float32)
        angle = (token - start) * rate
        index = slice(block * rows, (block + 1) * rows)
        cosine[index, :] = jnp.cos(angle)
        sine[index, :] = jnp.where(within < half, -1.0, 1.0) * jnp.sin(angle)
        same = ((label == within.astype(jnp.float32)) & (within < SEGS)).astype(jnp.float32)
        shut = (within == SEGS).astype(jnp.float32)
        ones = ((within >= SEGS) & (within < SEGS + 3)).astype(jnp.float32)
        mark_q[index, :] = (SHUT * same - SHUT * shut).astype(jnp.bfloat16)
        mark_k[index, :] = (same + ones).astype(jnp.bfloat16)
        if block == 0:
            segment[...] = label
            member[...] = (
                lax.broadcasted_iota(jnp.int32, (8, rows), 0).astype(jnp.float32) == line
            ).astype(jnp.bfloat16)
    for group in range(SEGS):
        lane = lane_index((TXT, LANES)) % HEAD
        row = lax.broadcasted_iota(jnp.int32, (TXT, LANES), 0)
        inside = ((lane == group) & (row < lens[group])).astype(jnp.float32)
        ones = ((lane >= SEGS) & (lane < SEGS + 3)).astype(jnp.float32)
        mark_t[group * TXT : (group + 1) * TXT, :] = (inside + ones).astype(jnp.bfloat16)


def text_kernel(captions, key_weight, value_weight, raw_out, value_out, raw_sum, value_sum):
    step = pl.program_id(0)

    @pl.when(step == 0)
    def _():
        raw_sum[...] = dot(captions[...], key_weight[...])
        value_sum[...] = dot(captions[...], value_weight[...])

    @pl.when(step > 0)
    def _():
        raw_sum[...] += dot(captions[...], key_weight[...])
        value_sum[...] += dot(captions[...], value_weight[...])

    @pl.when(step == pl.num_programs(0) - 1)
    def _():
        raw_out[...] = raw_sum[...]
        value_out[...] = value_sum[...].astype(jnp.bfloat16)


def text_call(captions, key_weight, value_weight):
    rows, depth = captions.shape
    columns = key_weight.shape[1]
    tile = depth // 4
    return pl.pallas_call(
        text_kernel,
        grid=(depth // tile,),
        in_specs=[
            pl.BlockSpec((rows, tile), lambda step: (0, step)),
            pl.BlockSpec((tile, columns), lambda step: (step, 0)),
            pl.BlockSpec((tile, columns), lambda step: (step, 0)),
        ],
        out_specs=[pl.BlockSpec((rows, columns), lambda step: (0, 0))] * 2,
        out_shape=[
            jax.ShapeDtypeStruct((rows, columns), jnp.float32),
            jax.ShapeDtypeStruct((rows, columns), jnp.bfloat16),
        ],
        scratch_shapes=[pltpu.VMEM((rows, columns), jnp.float32)] * 2,
        compiler_params=pltpu.CompilerParams(vmem_limit_bytes=VMEM_LIMIT),
        cost_estimate=cost_of(9),
        name="text",
    )(*[pltpu.with_memory_space_constraint(part, pltpu.HBM) for part in (captions, key_weight, value_weight)])


def project_kernel(here, own, far, near, last, mods, gains, segment_q, query_w, key_w, value_w,
                   rows_out, raw_q, raw_k, value):
    table = mods[here[0]]
    rows = own.shape[0]
    for block, part in enumerate((own, far, near, last)):
        index = slice(block * rows, (block + 1) * rows)
        values = part[...].astype(jnp.float32)
        marks = segment_q[index, :].astype(jnp.float32)
        scale = jnp.where(
            marks[:, 0:1] > 0.0, table[0:1], jnp.where(marks[:, 1:2] > 0.0, table[1:2], table[2:3])
        )
        rows_out[index, :] = (
            values * inverse_rms(values) * gains[0:1] * (1.0 + scale)
        ).astype(jnp.bfloat16)
    raw_q[...] = dot(rows_out[...], query_w[...])
    raw_k[...] = dot(rows_out[...], key_w[...])
    value[...] = dot(rows_out[...], value_w[...]).astype(jnp.bfloat16)


def middle_kernel(here, block, upper, near, far, mods, gains, segment, attn_out, middle_out, rows_out):
    attn_sum = total_of((upper, near, far))
    label = segment[:, 0:1]
    factor = jnp.tanh(per_row(mods[here[0] ^ 1], label)) * gains[1:2]
    middle = block[...].astype(jnp.float32) + factor * (attn_sum * inverse_rms(attn_sum))
    attn_out[...] = attn_sum
    middle_out[...] = middle
    scale = per_row(mods[here[0] ^ 2], label)
    rows_out[...] = (middle * inverse_rms(middle) * gains[2:3] * (1.0 + scale)).astype(jnp.bfloat16)


def block_out_kernel(here, middle, upper, near, far, grad, mods, gains, segment, member,
                     block_out, grad_out, sums):
    ffn_sum = total_of((upper, near, far))
    inverse = inverse_rms(ffn_sum)
    unit = ffn_sum * inverse
    factor = jnp.tanh(per_row(mods[here[0] ^ 3], segment[:, 0:1])) * gains[3:4]
    block_out[...] = (middle[...] + factor * unit).astype(jnp.bfloat16)
    incoming = grad[...].astype(jnp.float32)
    grad_out[...] = row_norm_back(incoming * factor, unit, inverse).astype(jnp.bfloat16)
    sums[...] = segment_sums(member[...], incoming * unit)


def middle_back_kernel(here, middle, attn, upper, near, far, grad, mods, gains, segment, member,
                       middle_grad, attn_grad, ffn_sums, attn_sums):
    grad_in = total_of((upper, near, far))
    label = segment[:, 0:1]
    inverse = inverse_rms(middle[...])
    unit = middle[...] * inverse
    factor = gains[2:3] * (1.0 + per_row(mods[here[0] ^ 2], label))
    ffn_sums[...] = segment_sums(member[...], grad_in * unit)
    grad_middle = grad[...].astype(jnp.float32) + row_norm_back(grad_in * factor, unit, inverse)
    middle_grad[...] = grad_middle
    inverse = inverse_rms(attn[...])
    unit = attn[...] * inverse
    factor = jnp.tanh(per_row(mods[here[0] ^ 1], label)) * gains[1:2]
    attn_grad[...] = row_norm_back(grad_middle * factor, unit, inverse).astype(jnp.bfloat16)
    attn_sums[...] = segment_sums(member[...], grad_middle * unit)


def block_in_kernel(here, block, middle_grad, upper, near, far, mods, gains, segment, member,
                    in_grad, sums):
    grad_in = total_of((upper, near, far))
    values = block[...].astype(jnp.float32)
    inverse = inverse_rms(values)
    unit = values * inverse
    factor = gains[0:1] * (1.0 + per_row(mods[here[0]], segment[:, 0:1]))
    in_grad[...] = (
        middle_grad[...] + row_norm_back(grad_in * factor, unit, inverse)
    ).astype(jnp.bfloat16)
    sums[...] = segment_sums(member[...], grad_in * unit)


def stack_sums_kernel(here, first, second, third, fourth, head_gain, text_gain, gate_sum, gate, out):
    width = out.shape[1]
    heads = jnp.concatenate([head_gain[0:1], head_gain[1:2], text_gain[...]], axis=1)
    inner = heads.shape[1] // 3
    gates = gate_sum[...] * (1.0 - gate[...] * gate[...])
    gates = jnp.concatenate([gates, jnp.zeros((1, width - inner), jnp.float32)], axis=1)
    lane = lane_index(gates.shape)
    moved = jnp.zeros_like(gates)
    for position in range(4):
        turn = pltpu.roll(gates, position * inner, 1) if position else gates
        moved = jnp.where((lane // inner == position) & (here[0] == position), turn, moved)
    out[...] = jnp.concatenate(
        [part[0:SEGS] for part in (first, second, third, fourth)]
        + [
            jnp.concatenate([heads, jnp.zeros((1, width - 3 * inner), jnp.float32)], axis=1),
            moved,
            jnp.zeros((2, width), jnp.float32),
        ],
        axis=0,
    )


def pack_kernel(here, own, far, near, last, mods, gains, cond, packed):
    total = own[...] + far[...] + near[...] + last[...]
    grad = jnp.zeros((SEGS, total.shape[1]), jnp.float32)
    rows = []
    for name in range(4):
        part = total[name * SEGS : (name + 1) * SEGS]
        mod = mods[here[0] ^ name]
        gain = gains[name : name + 1]
        if name % 2 == 1:
            factor = jnp.tanh(mod)
            slope = 1.0 - factor * factor
        else:
            factor = 1.0 + mod
            slope = jnp.ones_like(mod)
        rows.append(jnp.sum(part * factor, axis=0, keepdims=True))
        mine = (jnp.zeros(part.shape, jnp.int32) + here[0]) == name
        grad = jnp.where(mine, part * slope * gain, grad)
    rows.append(total[4 * SEGS : 4 * SEGS + 2])
    rows = jnp.concatenate(rows, axis=0)
    high = rows.astype(jnp.bfloat16).astype(jnp.float32)
    pad = jnp.zeros((packed.shape[0] - 2 * SEGS - 2 * SUM_ROWS, total.shape[1]), jnp.float32)
    packed[...] = jnp.concatenate(
        [grad, cond[...].astype(jnp.float32), high, rows - high, pad], axis=0
    ).astype(jnp.bfloat16)


def rider_rows(count):
    return -(-(2 * SEGS * count + 2 * SUM_ROWS) // 16) * 16


def merge_rows(count, first, second, size):
    first, second = first.astype(jnp.float32), second.astype(jnp.float32)
    wide = SEGS * count
    start = 2 * wide
    sums = (
        first[start : start + SUM_ROWS]
        + first[start + SUM_ROWS : start + 2 * SUM_ROWS]
        + second[start : start + SUM_ROWS]
        + second[start + SUM_ROWS : start + 2 * SUM_ROWS]
    )
    high = sums.astype(jnp.bfloat16).astype(jnp.float32)
    pieces = [first[:wide], second[:wide], first[wide:start], second[wide:start], high, sums - high]
    rest = size - 4 * wide - 2 * SUM_ROWS
    if rest:
        pieces.append(jnp.zeros((rest, first.shape[1]), jnp.float32))
    return jnp.concatenate(pieces, axis=0).astype(jnp.bfloat16)


def merge_kernel(ours, theirs, out):
    out[...] = merge_rows(1, ours[...], theirs[...], out.shape[0])


def ada_kernel(count, heads, dp, own, *refs):
    parts = (own,) + refs[:3]
    ada_out, norm_out, head_out, gate_out = refs[3:]
    wide = SEGS * count
    base = own.shape[0] - rider_rows(count)
    columns = ada_out.shape[0]
    share = LANES // columns
    start = pl.multiple_of(dp[0] // share * LANES, LANES)
    grads, conds = [], []
    sums = jnp.zeros((SUM_ROWS, own.shape[1]), jnp.float32)
    for part in parts:
        rows = part[base:, :].astype(jnp.float32)
        grads.append(rows[:wide])
        conds.append(part[base:, pl.ds(start, LANES)].astype(jnp.float32)[wide : 2 * wide])
        for half in range(2):
            place = 2 * wide + half * SUM_ROWS
            sums = sums + rows[place : place + SUM_ROWS]
    conds = jnp.concatenate(conds, axis=0)
    conds = pltpu.roll(conds, (LANES - dp[0] % share * columns) % LANES, 1)
    acts = conds / (1.0 + jnp.exp(-conds))
    ada_out[...] = dot(
        acts.astype(jnp.bfloat16).astype(jnp.float32).T.astype(jnp.bfloat16),
        jnp.concatenate(grads, axis=0).astype(jnp.bfloat16),
    )[:columns]
    norm_out[...] = sums[:4]
    inner = heads * HEAD
    for row in range(3):
        line = jnp.zeros((1, HEAD), jnp.float32)
        for head in range(heads):
            place = row * inner + head * HEAD
            line = line + sums[4:5, place : place + HEAD]
        head_out[row : row + 1, :] = line
    lane = lane_index((1, LANES))
    line = jnp.zeros((1, LANES), jnp.float32)
    for head in range(HEADS):
        value = jnp.sum(sums[5:6, head * HEAD : (head + 1) * HEAD], axis=1, keepdims=True)
        line = jnp.where(lane == head, value, line)
    gate_out[...] = line


def back_kernel(count, *refs):
    grads, weights, upper, lower = refs[:count], refs[count : 2 * count], refs[-2], refs[-1]
    total = dot_t(grads[0][...], weights[0][...])
    for grad, weight in zip(grads[1:], weights[1:]):
        total = total + dot_t(grad[...], weight[...])
    half = upper.shape[0]
    upper[...] = total[:half].astype(jnp.bfloat16)
    lower[...] = total[half:].astype(jnp.bfloat16)


def back_call(grads, weights, name, ties=(), micros=0):
    rows, inner = grads[0].shape
    columns = weights[0].shape[0]
    tile = columns // 3
    return pl.pallas_call(
        lambda *refs: back_kernel(len(grads), *refs[: 2 * len(grads)], *refs[-2:]),
        grid=(columns // tile,),
        in_specs=[pl.BlockSpec((rows, inner), lambda step: (0, 0))] * len(grads)
        + [pl.BlockSpec((tile, inner), lambda step: (step, 0))] * len(grads)
        + [pl.BlockSpec(memory_space=pl.ANY)] * len(ties),
        out_specs=[pl.BlockSpec((rows // 2, tile), lambda step: (0, step))] * 2,
        out_shape=[jax.ShapeDtypeStruct((rows // 2, columns), jnp.bfloat16)] * 2,
        compiler_params=pltpu.CompilerParams(vmem_limit_bytes=VMEM_LIMIT),
        cost_estimate=cost_of(micros),
        name=name,
    )(*grads, *weights, *ties)


def shards(
    block_in,
    out_grad,
    condition,
    captions,
    caption_len,
    segment_ids,
    ada_weight,
    norm_gains,
    query_weight,
    key_weight,
    value_weight,
    head_gains,
    textkey_weight,
    textvalue_weight,
    cross_gate,
    out_weight,
    gate_weight,
    up_weight,
    down_weight,
):
    rows, width = block_in.shape
    length = segment_ids.shape[0]
    heads = cross_gate.shape[0]
    inner = heads * HEAD
    half_rows = length // 2
    position = lax.axis_index("tensor")
    spot = dp_spot(position)
    here = position.reshape(1)
    b16, f32 = jnp.bfloat16, jnp.float32

    blocks = gather_tensor(block_in)
    cond_rows = jnp.pad(condition, ((0, 0), (0, width - condition.shape[1])))
    own_act = jax.nn.silu(condition.astype(f32)).astype(b16)
    own_part = jnp.dot(own_act, ada_weight, preferred_element_type=f32)
    parts = gather_tensor(own_part)
    mods = jnp.stack([parts[ROW_ORDER.index(code)] for code in range(4)])

    cosine, sine, mark_q, mark_k, mark_t, segment, member, gate_lanes, gate_swapped, gains = whole_call(
        tables_kernel,
        (here, caption_len, cross_gate),
        [segment_ids.reshape(length // rows, rows), head_gains],
        [((length, LANES), f32)] * 2
        + [((length, LANES), b16)] * 2
        + [((SEGS * TXT, LANES), b16), ((rows, LANES), f32), ((8, rows), b16)]
        + [((1, inner), f32)] * 2
        + [((3, inner), f32)],
        "tables",
        micros=2,
    )
    caption_flat = captions.reshape(-1, captions.shape[-1])
    texts = caption_flat.shape[0]
    raw_t, text_value = text_call(caption_flat, textkey_weight, textvalue_weight)
    attn_rows, raw_q, raw_k, value = whole_call(
        project_kernel,
        (here,),
        blocks + [mods, norm_gains, mark_q, query_weight, key_weight, value_weight],
        [((length, width), b16), ((length, inner), f32), ((length, inner), f32), ((length, inner), b16)],
        "project",
        micros=6,
    )
    query, key, text, mixed, self_out, cross_out, self_log, cross_log = pair_call(
        attend_kernel,
        [(raw_q, 1), (raw_k, 1), (value, 1), (raw_t, 1), (text_value, 1), (cosine, None), (sine, None)]
        + [(gains, 1), (gate_lanes, 1), (gate_swapped, 1), (mark_q, None), (mark_k, None), (mark_t, None)],
        [((length, inner), b16, 1)] * 2
        + [((texts, inner), b16, 1), ((length, inner), b16, 1)]
        + [((length, inner), f32, 1)] * 4,
        "attend",
        micros=11,
    )

    def halves(product):
        return product(slice(0, half_rows)).astype(b16), product(slice(half_rows, None)).astype(b16)

    def all_of(block):
        return jnp.concatenate(gather_tensor(block), axis=0)

    upper, lower = halves(lambda part: jnp.dot(mixed[part], out_weight, preferred_element_type=f32))
    sums, sent = scatter_tensor(upper, lower)
    attn_rows_t = turned(attn_rows, (sent,))
    wide = ((rows, width), f32)
    narrow = ((rows, width), b16)
    totals = ((8, width), f32)
    attn_sum, middle, ffn_own = whole_call(
        middle_kernel,
        (here,),
        [block_in] + sums + [mods, norm_gains, segment],
        [wide, wide, narrow],
        "middle",
    )
    ffn_rows = all_of(ffn_own)
    gate_pre = jnp.dot(ffn_rows, gate_weight, preferred_element_type=f32)
    up_pre = jnp.dot(ffn_rows, up_weight, preferred_element_type=f32)
    sigmoid_gate = jax.nn.sigmoid(gate_pre)
    silu_gate = gate_pre * sigmoid_gate
    hidden = (silu_gate * up_pre).astype(b16)
    upper, lower = halves(lambda part: jnp.dot(hidden[part], down_weight, preferred_element_type=f32))
    sums, sent = scatter_tensor(upper, lower)
    ffn_rows_t = turned(ffn_rows, (sent,))
    block_out, grad_own, sum_gate_ffn = whole_call(
        block_out_kernel,
        (here,),
        [middle] + sums + [out_grad, mods, norm_gains, segment, member],
        [narrow, narrow, totals],
        "block_out",
    )

    grad_ffn = all_of(grad_own)
    grad_hidden = times_transpose(grad_ffn, down_weight)
    grad_gate = (
        grad_hidden * up_pre * sigmoid_gate * (1.0 + gate_pre * (1.0 - sigmoid_gate))
    ).astype(b16)
    grad_up = (grad_hidden * silu_gate).astype(b16)
    upper, lower = halves(
        lambda part: times_transpose(grad_gate[part], gate_weight)
        + times_transpose(grad_up[part], up_weight)
    )
    sums, sent = scatter_tensor(upper, lower)
    grad_ffn_t = turned(grad_ffn, (sent,))
    ffn_pairs = [(ffn_rows_t, [grad_gate, grad_up]), (grad_ffn_t, [hidden])]
    (halves_two,) = row_chunks(ffn_pairs, (2,), spot, ties=(sent,), micros=FFN_MICROS)
    ffn_passed = one_on(halves_two)
    grad_middle, grad_own, sum_scale_ffn, sum_gate_attn = whole_call(
        middle_back_kernel,
        (here,),
        [middle, attn_sum] + sums + [out_grad, mods, norm_gains, segment, member],
        [wide, narrow, totals, totals],
        "middle_back",
        micros=MIDDLE_MICROS,
    )

    grad_attn = all_of(grad_own)
    grad_mixed = times_transpose(grad_attn, out_weight).astype(b16)
    cross_grad, text_grad, text_value_grad, text_gain, gate_sum = pair_call(
        cross_back_kernel,
        [(query, 1), (text, 1), (text_value, 1), (raw_t, 1), (grad_mixed, 1), (cross_out, 1)]
        + [(cross_log, 1), (gains, 1), (mark_q, None), (mark_t, None)],
        [((length, inner), f32, 1), ((inner, texts), b16, 0), ((inner, texts), b16, 0)]
        + [((1, inner), f32, 1)] * 2,
        "cross_back",
        micros=CROSS_MICROS,
    )
    ffn_one, ffn_three, ffn_kept = row_chunks(
        ffn_pairs, (1, 3, 0), spot, extra=ffn_passed, ties=(text_grad,), micros=FFN_NEXT_MICROS
    )
    text_lefts = [text_grad, text_value_grad]
    (halves_two,) = column_chunks(text_lefts, caption_flat, (2,), spot, ties=(ffn_kept,))
    text_passed = one_on(halves_two)
    query_grad, key_grad, value_grad, head_gain = pair_call(
        self_back_kernel,
        [(query, 1), (key, 1), (value, 1), (raw_q, 1), (raw_k, 1), (grad_mixed, 1), (self_out, 1)]
        + [(self_log, 1), (cross_grad, 1), (cosine, None), (sine, None), (gains, 1)]
        + [(mark_q, None), (mark_k, None)],
        [((length, inner), b16, 1)] * 3 + [((2, inner), f32, 1)],
        "self_back",
        (halves_two[0],),
        micros=SELF_MICROS,
    )

    hidden_cols = hidden.shape[1]
    block_rows = width // BLOCKS
    got = [by_slots(part) for part in to_neighbours(ffn_kept, ffn_one, ffn_three)]
    shape = (PAIR, block_rows, 3 * hidden_cols)
    ffn_kept, ffn_sent = tiled_call(
        ffn_second_kernel,
        (spot,),
        got,
        [((2 * PAIR,) + shape[1:], b16)] * 2,
        "ffn_second",
        -1,
        4,
        (query_grad,),
    )
    upper, lower = back_call(
        [query_grad, key_grad, value_grad], [query_weight, key_weight, value_weight], "attn_back"
    )
    sums, sent = scatter_tensor(upper, lower)
    in_grad, sum_scale_attn = whole_call(
        block_in_kernel,
        (here,),
        [block_in, grad_middle] + sums + [mods, norm_gains, segment, member],
        [narrow, totals],
        "block_in",
        (ffn_sent,),
        micros=BLOCK_IN_MICROS,
    )
    (stacked,) = whole_call(
        stack_sums_kernel,
        (here,),
        [sum_scale_attn, sum_gate_attn, sum_scale_ffn, sum_gate_ffn]
        + [head_gain, text_gain, gate_sum, gate_lanes],
        [((16, width), f32)],
        "stack_sums",
    )
    sums_stacked = stacked
    text_one, text_three, text_kept = column_chunks(
        text_lefts, caption_flat, (1, 3, 0), spot, extra=text_passed, ties=(sums_stacked,), micros=TEXT_MICROS
    )
    stacked = gather_tensor(stacked)
    ffn_own, ffn_sent = tiled_call(
        ffn_middle_kernel,
        (),
        [ffn_kept, dp_permute(ffn_sent, "second", "flip")],
        [(shape, b16)] * 2,
        "ffn_middle",
        -1,
        2,
        (text_kept,),
    )
    (riders,) = whole_call(
        pack_kernel,
        (here,),
        stacked + [mods, norm_gains, cond_rows],
        [((rider_rows(1), width), b16)],
        "pack",
        (ffn_sent,),
    )
    theirs = dp_permute(riders, "z", 1)
    (riders,) = whole_call(
        merge_kernel, (), [riders, theirs], [((rider_rows(PAIR), width), b16)], "merge"
    )
    attn_pairs = [
        (attn_rows_t, [query_grad, key_grad, value_grad]),
        (turned(grad_attn, (halves_two[0],)), [mixed]),
    ]
    (halves_two,) = row_chunks(attn_pairs, (2,), spot, riders=(riders,), micros=ATTN_FIRST_MICROS)
    attn_passed = one_on(halves_two)
    kept, sent = tiled_call(
        ffn_third_kernel,
        (spot,),
        [ffn_own, dp_permute(ffn_sent, "second", "mirror")],
        [(shape[1:], b16)] * 2,
        "ffn_third",
        -1,
        2,
        (halves_two[0],),
    )
    gate_sum_out, up_sum_out, down_sum_out = whole_call(
        ffn_last_kernel,
        (),
        exchange([kept, sent], "z"),
        [((block_rows, hidden_cols), f32)] * 2 + [((hidden_cols, block_rows), f32)],
        "ffn_last",
    )
    text_rows = caption_flat.shape[1] // BLOCKS
    attn_one, attn_three, attn_kept = row_chunks(
        attn_pairs, (1, 3, 0), spot, extra=attn_passed, ties=(kept,), riders=(riders,), micros=ATTN_MICROS
    )
    text_own, text_sent = tiled_call(
        text_second_kernel,
        (spot,),
        to_neighbours(text_kept, text_one, text_three),
        [((2 * inner, 2 * PAIR * text_rows), b16)] * 2,
        "text_second",
        0,
        4,
        (attn_kept,),
    )
    text_own, text_sent = tiled_call(
        text_middle_kernel,
        (),
        [text_own, dp_permute(text_sent, "second", "flip")],
        [((2 * inner, PAIR * text_rows), b16)] * 2,
        "text_middle",
        0,
        2,
    )
    kept, sent = tiled_call(
        text_third_kernel,
        (spot,),
        [text_own, dp_permute(text_sent, "second", "mirror")],
        [((2 * inner, text_rows), b16)] * 2,
        "text_third",
        0,
        2,
    )
    textkey_sum, textvalue_sum = whole_call(
        text_last_kernel,
        (),
        exchange([kept, sent], "z"),
        [((text_rows, inner), f32)] * 2,
        "text_last",
    )
    stage = tiled_call(
        functools.partial(attn_second_kernel, block_rows),
        (spot,),
        [riders] + to_neighbours(attn_kept, attn_one, attn_three),
        [((PAIR * block_rows + rider_rows(4 * PAIR), width), b16)] * RING,
        "attn_second",
        -1,
        4,
        (text_own,),
    )
    got = exchange(stage, "second")
    kept, sent = tiled_call(
        attn_third_kernel, (spot,), got, [((block_rows, width), b16)] * 2, "attn_third",
        -1,
        2
    )
    ada_grad, norm_grads, head_grads, crossgate = tiled_call(
        functools.partial(ada_kernel, 4 * PAIR, heads),
        (lax.axis_index("dp").reshape(1),),
        got,
        [((condition.shape[1] // BLOCKS, width), f32), ((4, width), f32), ((3, HEAD), f32)]
        + [((1, LANES), f32)],
        "ada",
        0,
        1,
        (kept,),
    )
    crossgate_grad = crossgate[0, :HEADS]
    query_sum, key_sum, value_sum, outw_sum = whole_call(
        attn_last_kernel,
        (),
        exchange([kept, sent], "z"),
        [((block_rows, inner), f32)] * 3 + [((inner, block_rows), f32)],
        "attn_last",
    )
    return (
        block_out,
        in_grad,
        ada_grad,
        norm_grads,
        query_sum,
        key_sum,
        value_sum,
        head_grads,
        textkey_sum,
        textvalue_sum,
        crossgate_grad,
        outw_sum,
        gate_sum_out,
        up_sum_out,
        down_sum_out,
    )


def solution(mesh):
    return jax.shard_map(
        shards,
        mesh=mesh,
        in_specs=(
            P(("dp", "tensor"), None),
            P(("dp", "tensor"), None),
            P("dp", None),
            P("dp", None, None),
            P("dp"),
            P("dp"),
            P(None, "tensor"),
            P(),
            P(None, "tensor"),
            P(None, "tensor"),
            P(None, "tensor"),
            P(),
            P(None, "tensor"),
            P(None, "tensor"),
            P("tensor"),
            P("tensor", None),
            P(None, "tensor"),
            P(None, "tensor"),
            P("tensor", None),
        ),
        out_specs=(
            P(("dp", "tensor"), None),
            P(("dp", "tensor"), None),
            P("dp", "tensor"),
            P(),
            P("dp", "tensor"),
            P("dp", "tensor"),
            P("dp", "tensor"),
            P(),
            P("dp", "tensor"),
            P("dp", "tensor"),
            P(),
            P("tensor", "dp"),
            P("dp", "tensor"),
            P("dp", "tensor"),
            P("tensor", "dp"),
        ),
        check_vma=False,
    )
```

```python
import functools
import math

import jax
import jax.numpy as jnp
from jax import lax
from jax.experimental import pallas as pl
from jax.experimental.pallas import tpu as pltpu
from jax.sharding import PartitionSpec as P

HEAD = 64
HEADS = 24
TXT = 256
SEGS = 3
EPS = 1e-06
LANES = 2 * HEAD
SHUT = 256.0
ROOT = HEAD ** (-0.5)
VMEM_LIMIT = 16 * 2**20
NO_COST = pl.CostEstimate(flops=0, bytes_accessed=0, transcendentals=0)


def cost_of(micros):
    return pl.CostEstimate(flops=int(micros * 1e9), bytes_accessed=0, transcendentals=0)


SUM_ROWS = 6
CROSS_MICROS = 10
BLOCK_IN_MICROS = 0
FFN_MICROS = 3
FFN_NEXT_MICROS = 8
MIDDLE_MICROS = 10
SELF_MICROS = 0
ATTN_MICROS = 1
TEXT_MICROS = 8
ATTN_FIRST_MICROS = 0

RING = 4
PAIR = 2
BLOCKS = RING * PAIR * RING
SLOTS = BLOCKS // RING
SEND_ORDER = (2, 1, 3, 0)
CORE_SWAP = [(0, 1), (1, 0), (2, 3), (3, 2)]
CHIP_SWAP = [(0, 2), (2, 0), (1, 3), (3, 1)]
ROW_ORDER = (0, 2, 1, 3)

def dp_index(x, z, y):
    return (x * PAIR + z) * RING + y


def dp_perm(axis, step):
    pairs = []

    def moved(place, size):
        if step == "flip":
            return place ^ 1
        if step == "mirror":
            return size - 1 - place
        return (place + step) % size

    for x in range(RING):
        for z in range(PAIR):
            for y in range(RING):
                for tensor in range(2 * PAIR):
                    way = axis
                    if axis in ("first", "second"):
                        way = "x" if (tensor % 2 == 0) == (axis == "first") else "y"
                    target = {
                        "x": (moved(x, RING), z, y),
                        "y": (x, z, moved(y, RING)),
                        "z": (x, moved(z, PAIR), y),
                    }[way]
                    pairs.append(
                        (
                            dp_index(x, z, y) * 2 * PAIR + tensor,
                            dp_index(*target) * 2 * PAIR + tensor,
                        )
                    )
    return pairs


def dp_permute(values, axis, step):
    return lax.ppermute(values, ("dp", "tensor"), dp_perm(axis, step))


def dp_spot(position):
    index = lax.axis_index("dp")
    x, z, y = index // (RING * PAIR), index // RING % PAIR, index % RING
    core = position % 2
    return jnp.stack([jnp.where(core == 0, x, y), z, jnp.where(core == 0, y, x), core])


def swap_core(values):
    return lax.ppermute(values, "tensor", CORE_SWAP)


def swap_chip(values):
    return lax.ppermute(values, "tensor", CHIP_SWAP)


def times_transpose(left, right):
    return lax.dot_general(
        left, right, (((1,), (1,)), ((), ())), preferred_element_type=jnp.float32
    )


def gather_tensor(block):
    far = swap_chip(block)
    near = swap_core(block)
    return [block, far, near, swap_core(far)]


def scatter_tensor(upper, lower):
    near = swap_core(lower)
    rows = upper.shape[0] // 2
    far = (upper[rows:].astype(jnp.float32) + near[rows:].astype(jnp.float32)).astype(near.dtype)
    return [upper, near, swap_chip(far)], far


def turn_kernel(source, target):
    target[...] = source[...].T


def turned(values, ties=()):
    tile = 512 if values.shape[1] % 512 == 0 else values.shape[1]
    return pl.pallas_call(
        lambda source, *rest: turn_kernel(source, rest[-1]),
        grid=(values.shape[1] // tile,),
        in_specs=[pl.BlockSpec((values.shape[0], tile), lambda step: (0, step))]
        + [pl.BlockSpec(memory_space=pl.ANY)] * len(ties),
        out_specs=pl.BlockSpec((tile, values.shape[0]), lambda step: (step, 0)),
        out_shape=jax.ShapeDtypeStruct(values.shape[::-1], values.dtype),
        compiler_params=pltpu.CompilerParams(vmem_limit_bytes=VMEM_LIMIT),
        cost_estimate=NO_COST,
    )(values, *ties)


def chunk_block(offset, slot, spot):
    first = (spot[0] + offset) % RING
    z, second = slot // RING, slot % RING
    x = jnp.where(spot[3] == 0, first, second)
    y = jnp.where(spot[3] == 0, second, first)
    return dp_index(x, z, y)


def offset_of_step(offsets, step):
    offset = offsets[-1]
    for place in range(len(offsets) - 1):
        offset = jnp.where(step == place, offsets[place], offset)
    return offset


def chunk_kernel(make, offsets, halves, extra, outs, held, sems):
    step = pl.program_id(0)
    first, second = halves

    def copies(place):
        slot = held.at[place % 2]
        if offsets[place] != 2:
            return [pltpu.make_async_copy(slot, outs[place], sems.at[place % 2, 0])]
        return [
            pltpu.make_async_copy(slot.at[half], out, sems.at[place % 2, way])
            for way, (half, out) in enumerate(zip((first, second), outs[place]))
        ]

    for place, offset in enumerate(offsets):

        @pl.when(step == place)
        def _(place=place, offset=offset):
            if place >= 2:
                for copy in copies(place - 2):
                    copy.wait()
            added = {1: (first, extra[0]), 3: (second, extra[1])}.get(offset) if extra else None
            make(held.at[place % 2], added, offset)
            for copy in copies(place):
                copy.start()
            if place == len(offsets) - 1:
                for last in range(max(place - 1, 0), place + 1):
                    for copy in copies(last):
                        copy.wait()


def chunk_call(make, operands, specs, offsets, halves, shape, spot, extra, ties, name, micros):
    count = len(operands)
    pieces = []
    for offset in offsets:
        if offset == 2:
            pieces += [tuple(len(range(*s.indices(d))) for s, d in zip(h, shape)) for h in halves]
        else:
            pieces.append(shape)

    def kernel(spot_ref, *refs):
        inputs, extras = refs[:count], refs[count : count + len(extra)]
        outs = list(refs[-len(pieces) - 2 : -2])
        grouped = []
        for offset in offsets:
            grouped.append((outs.pop(0), outs.pop(0)) if offset == 2 else outs.pop(0))
        chunk_kernel(
            functools.partial(make, inputs), offsets, halves, extras, grouped, refs[-2], refs[-1]
        )

    found = pl.pallas_call(
        kernel,
        grid_spec=pltpu.PrefetchScalarGridSpec(
            num_scalar_prefetch=1,
            grid=(len(offsets),),
            in_specs=list(specs)
            + [pl.BlockSpec(part.shape, lambda step, spot: (0, 0)) for part in extra]
            + [pl.BlockSpec(memory_space=pl.ANY)] * len(ties),
            out_specs=[pl.BlockSpec(memory_space=pl.ANY)] * len(pieces),
            scratch_shapes=[
                pltpu.VMEM((2,) + shape, jnp.bfloat16),
                pltpu.SemaphoreType.DMA((2, 2)),
            ],
        ),
        out_shape=[jax.ShapeDtypeStruct(piece, jnp.bfloat16) for piece in pieces],
        compiler_params=pltpu.CompilerParams(vmem_limit_bytes=VMEM_LIMIT),
        cost_estimate=cost_of(micros),
        name=name,
    )(spot, *operands, *extra, *ties)
    found = list(found)
    return [
        (found.pop(0), found.pop(0)) if offset == 2 else found.pop(0) for offset in offsets
    ]


def make_rows(groups, inputs, slot, added, offset):
    lefts, rights = inputs[: SLOTS * len(groups)], inputs[SLOTS * len(groups) :]
    size = SLOTS * lefts[0].shape[1]
    if len(rights) > sum(groups):
        riders = rights[-1][...]
        count, half = riders.shape[0], riders.shape[1] // 2
        first, second = slice(size, size + count), slice(size + count, size + 2 * count)
        if offset == 2:
            for side in (slice(0, half), slice(half, 2 * half)):
                slot[first, side] = riders[:, :half]
                slot[second, side] = riders[:, half:]
        else:
            slot[first, :] = riders
            if offset == 1:
                slot[second, :half] = added[1][first, :]
                slot[second, half:] = added[1][second, :]
            else:
                slot[second, :] = riders
    column = place = 0
    for group, count in enumerate(groups):
        rows = jnp.concatenate(
            [left[0] for left in lefts[SLOTS * group : SLOTS * (group + 1)]], axis=0
        )
        for right in rights[place : place + count]:
            wide = right.shape[1]
            product = dot(rows, right[...])
            low, high = column, column
            if added is not None:
                low = min(max(column, added[0][1].start), column + wide)
                high = min(max(column, added[0][1].stop), column + wide)
            for start, stop in ((column, low), (low, high), (high, column + wide)):
                if start < stop:
                    part = product[:, start - column : stop - column]
                    if (start, stop) == (low, high):
                        base = added[0][1].start
                        part = part + added[1][:size, start - base : stop - base].astype(jnp.float32)
                    slot[:size, start:stop] = part.astype(jnp.bfloat16)
            column += wide
        place += count


def row_chunks(pairs, offsets, spot, extra=(), ties=(), micros=0, riders=()):
    lefts = [left.reshape(BLOCKS, left.shape[0] // BLOCKS, left.shape[1]) for left, _ in pairs]
    rights = [right for _, group in pairs for right in group]
    total = sum(right.shape[1] for right in rights)
    specs, operands = [], []
    for left in lefts:
        for slot in range(SLOTS):
            specs.append(
                pl.BlockSpec(
                    (1,) + left.shape[1:],
                    lambda step, spot, slot=slot: (
                        chunk_block(offset_of_step(offsets, step), slot, spot),
                        0,
                        0,
                    ),
                )
            )
            operands.append(left)
    specs += [pl.BlockSpec(right.shape, lambda step, spot: (0, 0)) for right in rights]
    specs += [pl.BlockSpec(part.shape, lambda step, spot: (0, 0)) for part in riders]
    rows = SLOTS * lefts[0].shape[1] + sum(2 * part.shape[0] for part in riders)
    halves = [(slice(0, rows), slice(0, total // 2)), (slice(0, rows), slice(total // 2, total))]
    return chunk_call(
        functools.partial(make_rows, [len(group) for _, group in pairs]),
        operands + rights + list(riders),
        specs,
        offsets,
        halves,
        (rows, total),
        spot,
        extra,
        ties,
        "row_chunks",
        micros,
    )


def make_columns(lefts, inputs, slot, added, offset):
    whole = jnp.concatenate([right[...] for right in inputs[lefts:]], axis=1)
    row = 0
    for left in inputs[:lefts]:
        product = dot(left[...], whole)
        if added is not None and added[0][0].start == row:
            product = product + added[1][...].astype(jnp.float32)
        slot[row : row + left.shape[0], :] = product.astype(jnp.bfloat16)
        row += left.shape[0]


def column_chunks(lefts, right, offsets, spot, extra=(), ties=(), micros=0):
    rows = lefts[0].shape[0]
    depth, columns = right.shape
    specs = [pl.BlockSpec(left.shape, lambda step, spot: (0, 0)) for left in lefts]
    for slot in range(SLOTS):
        specs.append(
            pl.BlockSpec(
                (depth, columns // BLOCKS),
                lambda step, spot, slot=slot: (
                    0,
                    chunk_block(offset_of_step(offsets, step), slot, spot),
                ),
            )
        )
    lanes = columns // RING
    halves = [(slice(0, rows), slice(0, lanes)), (slice(rows, 2 * rows), slice(0, lanes))]
    return chunk_call(
        functools.partial(make_columns, len(lefts)),
        list(lefts) + [right] * SLOTS,
        specs,
        offsets,
        halves,
        (2 * rows, lanes),
        spot,
        extra,
        ties,
        "column_chunks",
        micros,
    )


def add_up(refs, index):
    total = refs[0][index].astype(jnp.float32)
    for ref in refs[1:]:
        total = total + ref[index].astype(jnp.float32)
    return total


def lane_slice(start, size):
    return (slice(None), pl.ds(pl.multiple_of(start * size, size), size))


def halving_places(spot):
    own = spot[2]
    other = own ^ 1
    return (own, RING - 1 - own), (other, RING - 1 - other)


def ffn_second_kernel(spot, *refs):
    parts = refs[:-2]
    for out, places in zip(refs[-2:], halving_places(spot)):
        for index, place in enumerate(places):
            for z in range(PAIR):
                out[index * PAIR + z] = add_up(parts, z * RING + place).astype(jnp.bfloat16)


def ffn_middle_kernel(kept, got, own, sent):
    for out, start in ((own, 0), (sent, PAIR)):
        for z in range(PAIR):
            out[z] = add_up((kept, got), start + z).astype(jnp.bfloat16)


def ffn_third_kernel(spot, *refs):
    for out, z in ((refs[-2], spot[1]), (refs[-1], (spot[1] + 1) % PAIR)):
        out[...] = add_up(refs[:-2], z).astype(jnp.bfloat16)


def ffn_last_kernel(kept, got, gate_out, up_out, down_out):
    total = kept[...].astype(jnp.float32) + got[...].astype(jnp.float32)
    hidden = gate_out.shape[1]
    gate_out[...] = total[:, :hidden]
    up_out[...] = total[:, hidden : 2 * hidden]
    down_out[...] = total[:, 2 * hidden :].T


def text_second_kernel(spot, *refs):
    parts = refs[:-2]
    lanes = parts[0].shape[1] // SLOTS
    for out, places in zip(refs[-2:], halving_places(spot)):
        for index, place in enumerate(places):
            for z in range(PAIR):
                start = (index * PAIR + z) * lanes
                out[:, start : start + lanes] = add_up(
                    parts, lane_slice(z * RING + place, lanes)
                ).astype(jnp.bfloat16)


def text_middle_kernel(kept, got, own, sent):
    wide = own.shape[1]
    for out, start in ((own, 0), (sent, wide)):
        index = (slice(None), slice(start, start + wide))
        out[...] = add_up((kept, got), index).astype(jnp.bfloat16)


def text_third_kernel(spot, *refs):
    lanes = refs[-1].shape[1]
    for out, z in ((refs[-2], spot[1]), (refs[-1], (spot[1] + 1) % PAIR)):
        out[...] = add_up(refs[:-2], lane_slice(z, lanes)).astype(jnp.bfloat16)


def text_last_kernel(kept, got, textkey, textvalue):
    total = kept[...].astype(jnp.float32) + got[...].astype(jnp.float32)
    columns = textkey.shape[1]
    textkey[...] = total[:columns].T
    textvalue[...] = total[columns:].T


def attn_second_kernel(rows, spot, riders, *refs):
    parts, outs = refs[:-RING], refs[-RING:]
    size, count = SLOTS * rows, riders.shape[0]
    for offset in range(RING):
        for z in range(PAIR):
            slot = z * RING + (spot[2] + offset) % RING
            index = (pl.ds(pl.multiple_of(slot * rows, 16), rows), slice(None))
            outs[offset][z * rows : (z + 1) * rows, :] = add_up(parts, index).astype(jnp.bfloat16)
    ahead, behind = parts[1], parts[2]
    pairs = (
        (riders[...], ahead[size : size + count, :]),
        (behind[size : size + count, :], ahead[size + count : size + 2 * count, :]),
    )
    joined = [merge_rows(PAIR, first, second, rider_rows(2 * PAIR)) for first, second in pairs]
    joined = merge_rows(2 * PAIR, joined[0], joined[1], rider_rows(4 * PAIR))
    for out in outs:
        out[PAIR * rows :, :] = joined


def attn_third_kernel(spot, *refs):
    rows = refs[-1].shape[0]
    for out, z in ((refs[-2], spot[1]), (refs[-1], (spot[1] + 1) % PAIR)):
        index = (pl.ds(pl.multiple_of(z * rows, 16), rows), slice(None))
        out[...] = add_up(refs[:RING], index).astype(jnp.bfloat16)


def attn_last_kernel(kept, got, query, key, value, outw):
    total = kept[...].astype(jnp.float32) + got[...].astype(jnp.float32)
    columns = query.shape[1]
    for place, out in enumerate((query, key, value)):
        out[...] = total[:, place * columns : (place + 1) * columns]
    outw[...] = total[:, 3 * columns :].T


def whole_call(kernel, scalars, operands, outs, name, ties=(), scratch=(), micros=0):
    whole = pl.BlockSpec(memory_space=pltpu.VMEM)
    count = len(scalars) + len(operands)
    return pl.pallas_call(
        lambda *refs: kernel(*refs[:count], *refs[count + len(ties) :]),
        in_specs=[pl.BlockSpec(memory_space=pltpu.SMEM)] * len(scalars)
        + [whole] * len(operands)
        + [pl.BlockSpec(memory_space=pl.ANY)] * len(ties),
        out_specs=[whole] * len(outs),
        out_shape=[jax.ShapeDtypeStruct(shape, kind) for shape, kind in outs],
        scratch_shapes=list(scratch),
        compiler_params=pltpu.CompilerParams(vmem_limit_bytes=VMEM_LIMIT),
        cost_estimate=cost_of(micros),
        name=name,
    )(*scalars, *operands, *ties)


def tiled_call(kernel, scalars, operands, outs, name, axis, tiles, ties=(), micros=0, axes=None):
    def spec(shape, axis):
        block = list(shape)
        block[axis] //= tiles
        if axis == 0:
            return pl.BlockSpec(tuple(block), lambda step: (step,) + (0,) * (len(shape) - 1))
        return pl.BlockSpec(tuple(block), lambda step: (0,) * (len(shape) - 1) + (step,))

    count = len(scalars) + len(operands)
    return pl.pallas_call(
        lambda *refs: kernel(*refs[:count], *refs[count + len(ties) :]),
        grid=(tiles,),
        in_specs=[pl.BlockSpec(memory_space=pltpu.SMEM)] * len(scalars)
        + [spec(part.shape, way) for part, way in zip(operands, axes or [axis] * len(operands))]
        + [pl.BlockSpec(memory_space=pl.ANY)] * len(ties),
        out_specs=[spec(shape, axis) for shape, _ in outs],
        out_shape=[jax.ShapeDtypeStruct(shape, kind) for shape, kind in outs],
        compiler_params=pltpu.CompilerParams(vmem_limit_bytes=VMEM_LIMIT),
        cost_estimate=cost_of(micros),
        name=name,
    )(*scalars, *[pltpu.with_memory_space_constraint(part, pltpu.HBM) for part in operands], *ties)


def exchange(chunks, axis):
    return [chunks[0]] + [
        dp_permute(chunks[step], axis, step) for step in range(1, len(chunks))
    ]


def one_on(halves):
    return dp_permute(halves[0], "first", 1), dp_permute(halves[1], "first", RING - 1)


def to_neighbours(own, ahead, behind):
    return [own, dp_permute(ahead, "first", 1), dp_permute(behind, "first", RING - 1)]


def by_slots(chunk):
    return chunk.reshape(SLOTS, chunk.shape[0] // SLOTS, chunk.shape[1])


def lane_index(shape):
    return lax.broadcasted_iota(jnp.int32, shape, 1)


def head_lanes(shape, head):
    lane = lane_index(shape)
    return (lane < HEAD) if head == 0 else (lane >= HEAD)


def per_head(values, reduce):
    first = head_lanes(values.shape, 0)
    left = jnp.sum(jnp.where(first, values, 0.0), axis=1, keepdims=True)
    right = jnp.sum(jnp.where(first, 0.0, values), axis=1, keepdims=True)
    return jnp.where(first, left, right)


def head_units(raw):
    inverse = lax.rsqrt(per_head(raw * raw, None) * (1.0 / HEAD) + EPS)
    return raw * inverse, inverse


def partner(values):
    lane = lane_index(values.shape)
    return jnp.where(
        lane % HEAD < HEAD // 2,
        pltpu.roll(values, LANES - HEAD // 2, 1),
        pltpu.roll(values, HEAD // 2, 1),
    )


def dot(left, right):
    return jnp.dot(left, right, preferred_element_type=jnp.float32)


def dot_t(left, right):
    return lax.dot_general(left, right, (((1,), (1,)), ((), ())), preferred_element_type=jnp.float32)


def attend_kernel(
    raw_q, raw_k, value, raw_t, text_value, cosine, sine, gains, gate, gate_swapped, mark_q, mark_k, mark_t,
    query_out, key_out, text_out, mixed_out, self_out, cross_out, self_log, cross_log,
):
    cos, sin = cosine[...], sine[...]
    unit = head_units(raw_q[...])[0] * gains[0:1, :]
    query = ((unit * cos + partner(unit) * sin).astype(jnp.bfloat16) * ROOT).astype(jnp.bfloat16)
    unit = head_units(raw_k[...])[0] * gains[1:2, :]
    key = (unit * cos + partner(unit) * sin).astype(jnp.bfloat16)
    text = (head_units(raw_t[...])[0] * gains[2:3, :]).astype(jnp.bfloat16)
    query_out[...] = query
    key_out[...] = key
    text_out[...] = text

    def attention(keys, marks, values):
        outs, sums = [], []
        for head in range(2):
            own = head_lanes(query.shape, head)
            own_keys = head_lanes(keys.shape, head)
            probe = jnp.where(own, query, mark_q[...])
            scores = dot_t(probe, jnp.where(own_keys, keys, marks))
            weights = jnp.exp(scores).astype(jnp.bfloat16)
            both = dot(weights, jnp.where(own_keys, values, jnp.ones_like(values)))
            outs.append(both)
        first = head_lanes(outs[0].shape, 0)
        product = jnp.where(first, outs[0], outs[1])
        total = jnp.where(first, outs[1], outs[0])
        return product / pltpu.roll(total, HEAD, 1), jnp.log(total)

    out, log = attention(key, mark_k[...], value[...])
    self_out[...] = out
    self_log[...] = log
    cross, log = attention(text, mark_t[...], text_value[...])
    cross_out[...] = cross
    cross_log[...] = log - jnp.log(gate_swapped[...])
    mixed_out[...] = (out + gate[...] * cross).astype(jnp.bfloat16)


def attention_grads(query, keys, marks, values, grad, out, log, mark_q):
    rows = grad.astype(jnp.float32)
    delta = per_head(rows * out, None)
    delta = pltpu.roll(delta, HEAD, 1)
    lane = lane_index(query.shape) % HEAD
    log_high = log.astype(jnp.bfloat16)
    log_low = (log - log_high.astype(jnp.float32)).astype(jnp.bfloat16)
    delta_high = delta.astype(jnp.bfloat16)
    delta_low = (delta - delta_high.astype(jnp.float32)).astype(jnp.bfloat16)
    zero = jnp.zeros_like(query)
    code = jnp.where(lane == 4, -log_high, jnp.where(lane == 5, -log_low, mark_q))
    shift = jnp.where(lane == 4, -delta_high, jnp.where(lane == 5, -delta_low, zero))
    key_grads, value_grads, query_grads = [], [], []
    for head in range(2):
        own = head_lanes(query.shape, head)
        own_keys = head_lanes(keys.shape, head)
        probe = jnp.where(own, query, code)
        probs = jnp.exp(dot_t(jnp.where(own_keys, keys, marks), probe))
        slope = dot_t(jnp.where(own_keys, values, marks), jnp.where(own, grad, shift))
        score_grad = (probs * slope).astype(jnp.bfloat16)
        value_grads.append(dot(probs.astype(jnp.bfloat16), grad))
        key_grads.append(dot(score_grad, query))
        turned = keys[:, head * HEAD : (head + 1) * HEAD].T
        query_grads.append(dot(turned, score_grad))
    first = head_lanes(keys.shape, 0)
    return (
        jnp.concatenate(query_grads, axis=0),
        jnp.where(first, key_grads[0], key_grads[1]),
        jnp.where(first, value_grads[0], value_grads[1]),
    )


def norm_back(weighted, unit, inverse):
    return inverse * (weighted - unit * (per_head(weighted * unit, None) * (1.0 / HEAD)))


def cross_back_kernel(
    query, text, text_value, raw_t, grad, out, log, gains, mark_q, mark_t,
    query_grad, raw_grad, value_grad, gain_sum, gate_sum,
):
    grad_q, grad_t, grad_v = attention_grads(
        query[...], text[...], mark_t[...], text_value[...], grad[...], out[...], log[...], mark_q[...]
    )
    query_grad[...] = grad_q.T
    value_grad[...] = grad_v.astype(jnp.bfloat16).T
    grad_t = grad_t.astype(jnp.bfloat16).astype(jnp.float32)
    unit, inverse = head_units(raw_t[...])
    gain_sum[...] = jnp.sum(grad_t * unit, axis=0, keepdims=True)
    raw_grad[...] = norm_back(grad_t * gains[2:3, :], unit, inverse).astype(jnp.bfloat16).T
    gate_sum[...] = jnp.sum(grad[...].astype(jnp.float32) * out[...], axis=0, keepdims=True)


def self_back_kernel(
    query, key, value, raw_q, raw_k, grad, out, log, cross_grad, cosine, sine, gains, mark_q, mark_k,
    query_grad, key_grad, value_grad, gain_sum,
):
    grad_q, grad_k, grad_v = attention_grads(
        query[...], key[...], mark_k[...], value[...], grad[...], out[...], log[...], mark_q[...]
    )
    value_grad[...] = grad_v.astype(jnp.bfloat16)
    cos, sin = cosine[...], sine[...]
    grad_q = (grad_q.T + cross_grad[...]) * ROOT
    for turn, raw, row, target in ((grad_q, raw_q, 0, query_grad), (grad_k, raw_k, 1, key_grad)):
        turn = turn.astype(jnp.bfloat16).astype(jnp.float32)
        turn = turn * cos - partner(turn) * sin
        unit, inverse = head_units(raw[...])
        gain_sum[row : row + 1, :] = jnp.sum(turn * unit, axis=0, keepdims=True)
        target[...] = norm_back(turn * gains[row : row + 1, :], unit, inverse).astype(jnp.bfloat16)


def pair_call(kernel, operands, outs, name, ties=(), micros=0):
    def spec(shape, cut):
        if cut is None:
            return pl.BlockSpec(shape, lambda pair: (0, 0))
        if cut == 1:
            return pl.BlockSpec((shape[0], LANES), lambda pair: (0, pair))
        return pl.BlockSpec((LANES, shape[1]), lambda pair: (pair, 0))

    width = outs[0][0][0] if outs[0][2] == 0 else outs[0][0][1]
    return pl.pallas_call(
        lambda *refs: kernel(*refs[: len(operands)], *refs[len(operands) + len(ties) :]),
        grid=(width // LANES,),
        in_specs=[spec(part.shape, cut) for part, cut in operands]
        + [pl.BlockSpec(memory_space=pl.ANY)] * len(ties),
        out_specs=[spec(shape, cut) for shape, _, cut in outs],
        out_shape=[jax.ShapeDtypeStruct(shape, kind) for shape, kind, _ in outs],
        compiler_params=pltpu.CompilerParams(vmem_limit_bytes=VMEM_LIMIT),
        cost_estimate=cost_of(micros),
        name=name,
    )(*[part for part, _ in operands], *ties)
def inverse_rms(values):
    return lax.rsqrt(jnp.mean(values * values, axis=-1, keepdims=True) + EPS)


def row_norm_back(weighted, unit, inverse):
    return inverse * (weighted - unit * jnp.mean(weighted * unit, axis=-1, keepdims=True))


def per_row(table, segment):
    return jnp.where(segment == 0.0, table[0:1], jnp.where(segment == 1.0, table[1:2], table[2:3]))


def total_of(parts):
    upper, near, far = parts
    rows = far.shape[0]
    return (
        upper[:rows].astype(jnp.float32) + near[:rows].astype(jnp.float32) + far[...].astype(jnp.float32)
    )


def segment_sums(member, values):
    high = values.astype(jnp.bfloat16)
    low = (values - high.astype(jnp.float32)).astype(jnp.bfloat16)
    return dot(member, high) + dot(member, low)


def tables_kernel(here, lens, gate, segments, head_gains, cosine, sine, mark_q, mark_k, mark_t,
                  segment, member, gate_lanes, gate_swapped, gains):
    heads = gains.shape[1] // HEAD
    lane = lane_index(gate_lanes.shape) // HEAD
    line = jnp.zeros(gate_lanes.shape, jnp.float32)
    swapped = line
    for head in range(heads):
        line = jnp.where(lane == head, gate[head], line)
        swapped = jnp.where(lane == head ^ 1, gate[head], swapped)
    gate_lanes[...] = jnp.tanh(line)
    gate_swapped[...] = jnp.tanh(swapped)
    gains[...] = jnp.concatenate([head_gains[...]] * heads, axis=1)
    rows = segments.shape[1]
    ids = segments[...]
    first = jnp.sum((ids < 1).astype(jnp.float32))
    second = jnp.sum((ids < 2).astype(jnp.float32))
    lane = lane_index((rows, LANES))
    half = HEAD // 2
    rate = jnp.exp((lane % half).astype(jnp.float32) * (-2.0 * math.log(10000.0) / HEAD))
    within = lane % HEAD
    for block, code in enumerate(ROW_ORDER):
        source = here[0] ^ code
        line = segments[pl.ds(source, 1), :].astype(jnp.float32)
        label = jnp.broadcast_to(line, (rows, rows)).T
        start = jnp.where(label == 0.0, 0.0, jnp.where(label == 1.0, first, second))
        token = (lax.broadcasted_iota(jnp.int32, (rows, LANES), 0) + source * rows).astype(jnp.float32)
        angle = (token - start) * rate
        index = slice(block * rows, (block + 1) * rows)
        cosine[index, :] = jnp.cos(angle)
        sine[index, :] = jnp.where(within < half, -1.0, 1.0) * jnp.sin(angle)
        same = ((label == within.astype(jnp.float32)) & (within < SEGS)).astype(jnp.float32)
        shut = (within == SEGS).astype(jnp.float32)
        ones = ((within >= SEGS) & (within < SEGS + 3)).astype(jnp.float32)
        mark_q[index, :] = (SHUT * same - SHUT * shut).astype(jnp.bfloat16)
        mark_k[index, :] = (same + ones).astype(jnp.bfloat16)
        if block == 0:
            segment[...] = label
            member[...] = (
                lax.broadcasted_iota(jnp.int32, (8, rows), 0).astype(jnp.float32) == line
            ).astype(jnp.bfloat16)
    for group in range(SEGS):
        lane = lane_index((TXT, LANES)) % HEAD
        row = lax.broadcasted_iota(jnp.int32, (TXT, LANES), 0)
        inside = ((lane == group) & (row < lens[group])).astype(jnp.float32)
        ones = ((lane >= SEGS) & (lane < SEGS + 3)).astype(jnp.float32)
        mark_t[group * TXT : (group + 1) * TXT, :] = (inside + ones).astype(jnp.bfloat16)


def text_kernel(captions, key_weight, value_weight, raw_out, value_out, raw_sum, value_sum):
    step = pl.program_id(0)

    @pl.when(step == 0)
    def _():
        raw_sum[...] = dot(captions[...], key_weight[...])
        value_sum[...] = dot(captions[...], value_weight[...])

    @pl.when(step > 0)
    def _():
        raw_sum[...] += dot(captions[...], key_weight[...])
        value_sum[...] += dot(captions[...], value_weight[...])

    @pl.when(step == pl.num_programs(0) - 1)
    def _():
        raw_out[...] = raw_sum[...]
        value_out[...] = value_sum[...].astype(jnp.bfloat16)


def text_call(captions, key_weight, value_weight):
    rows, depth = captions.shape
    columns = key_weight.shape[1]
    tile = depth // 4
    return pl.pallas_call(
        text_kernel,
        grid=(depth // tile,),
        in_specs=[
            pl.BlockSpec((rows, tile), lambda step: (0, step)),
            pl.BlockSpec((tile, columns), lambda step: (step, 0)),
            pl.BlockSpec((tile, columns), lambda step: (step, 0)),
        ],
        out_specs=[pl.BlockSpec((rows, columns), lambda step: (0, 0))] * 2,
        out_shape=[
            jax.ShapeDtypeStruct((rows, columns), jnp.float32),
            jax.ShapeDtypeStruct((rows, columns), jnp.bfloat16),
        ],
        scratch_shapes=[pltpu.VMEM((rows, columns), jnp.float32)] * 2,
        compiler_params=pltpu.CompilerParams(vmem_limit_bytes=VMEM_LIMIT),
        cost_estimate=cost_of(9),
        name="text",
    )(*[pltpu.with_memory_space_constraint(part, pltpu.HBM) for part in (captions, key_weight, value_weight)])


def project_kernel(here, own, far, near, last, mods, gains, segment_q, query_w, key_w, value_w,
                   rows_out, raw_q, raw_k, value):
    table = mods[here[0]]
    rows = own.shape[0]
    for block, part in enumerate((own, far, near, last)):
        index = slice(block * rows, (block + 1) * rows)
        values = part[...].astype(jnp.float32)
        marks = segment_q[index, :].astype(jnp.float32)
        scale = jnp.where(
            marks[:, 0:1] > 0.0, table[0:1], jnp.where(marks[:, 1:2] > 0.0, table[1:2], table[2:3])
        )
        rows_out[index, :] = (
            values * inverse_rms(values) * gains[0:1] * (1.0 + scale)
        ).astype(jnp.bfloat16)
    raw_q[...] = dot(rows_out[...], query_w[...])
    raw_k[...] = dot(rows_out[...], key_w[...])
    value[...] = dot(rows_out[...], value_w[...]).astype(jnp.bfloat16)


def middle_kernel(here, block, upper, near, far, mods, gains, segment, attn_out, middle_out, rows_out):
    attn_sum = total_of((upper, near, far))
    label = segment[:, 0:1]
    factor = jnp.tanh(per_row(mods[here[0] ^ 1], label)) * gains[1:2]
    middle = block[...].astype(jnp.float32) + factor * (attn_sum * inverse_rms(attn_sum))
    attn_out[...] = attn_sum
    middle_out[...] = middle
    scale = per_row(mods[here[0] ^ 2], label)
    rows_out[...] = (middle * inverse_rms(middle) * gains[2:3] * (1.0 + scale)).astype(jnp.bfloat16)


def block_out_kernel(here, middle, upper, near, far, grad, mods, gains, segment, member,
                     block_out, grad_out, sums):
    ffn_sum = total_of((upper, near, far))
    inverse = inverse_rms(ffn_sum)
    unit = ffn_sum * inverse
    factor = jnp.tanh(per_row(mods[here[0] ^ 3], segment[:, 0:1])) * gains[3:4]
    block_out[...] = (middle[...] + factor * unit).astype(jnp.bfloat16)
    incoming = grad[...].astype(jnp.float32)
    grad_out[...] = row_norm_back(incoming * factor, unit, inverse).astype(jnp.bfloat16)
    sums[...] = segment_sums(member[...], incoming * unit)


def middle_back_kernel(here, middle, attn, upper, near, far, grad, mods, gains, segment, member,
                       middle_grad, attn_grad, ffn_sums, attn_sums):
    grad_in = total_of((upper, near, far))
    label = segment[:, 0:1]
    inverse = inverse_rms(middle[...])
    unit = middle[...] * inverse
    factor = gains[2:3] * (1.0 + per_row(mods[here[0] ^ 2], label))
    ffn_sums[...] = segment_sums(member[...], grad_in * unit)
    grad_middle = grad[...].astype(jnp.float32) + row_norm_back(grad_in * factor, unit, inverse)
    middle_grad[...] = grad_middle
    inverse = inverse_rms(attn[...])
    unit = attn[...] * inverse
    factor = jnp.tanh(per_row(mods[here[0] ^ 1], label)) * gains[1:2]
    attn_grad[...] = row_norm_back(grad_middle * factor, unit, inverse).astype(jnp.bfloat16)
    attn_sums[...] = segment_sums(member[...], grad_middle * unit)


def block_in_kernel(here, block, middle_grad, upper, near, far, mods, gains, segment, member,
                    in_grad, sums):
    grad_in = total_of((upper, near, far))
    values = block[...].astype(jnp.float32)
    inverse = inverse_rms(values)
    unit = values * inverse
    factor = gains[0:1] * (1.0 + per_row(mods[here[0]], segment[:, 0:1]))
    in_grad[...] = (
        middle_grad[...] + row_norm_back(grad_in * factor, unit, inverse)
    ).astype(jnp.bfloat16)
    sums[...] = segment_sums(member[...], grad_in * unit)


def stack_sums_kernel(here, first, second, third, fourth, head_gain, text_gain, gate_sum, gate, out):
    width = out.shape[1]
    heads = jnp.concatenate([head_gain[0:1], head_gain[1:2], text_gain[...]], axis=1)
    inner = heads.shape[1] // 3
    gates = gate_sum[...] * (1.0 - gate[...] * gate[...])
    gates = jnp.concatenate([gates, jnp.zeros((1, width - inner), jnp.float32)], axis=1)
    lane = lane_index(gates.shape)
    moved = jnp.zeros_like(gates)
    for position in range(4):
        turn = pltpu.roll(gates, position * inner, 1) if position else gates
        moved = jnp.where((lane // inner == position) & (here[0] == position), turn, moved)
    out[...] = jnp.concatenate(
        [part[0:SEGS] for part in (first, second, third, fourth)]
        + [
            jnp.concatenate([heads, jnp.zeros((1, width - 3 * inner), jnp.float32)], axis=1),
            moved,
            jnp.zeros((2, width), jnp.float32),
        ],
        axis=0,
    )


def pack_kernel(here, own, far, near, last, mods, gains, cond, packed):
    total = own[...] + far[...] + near[...] + last[...]
    grad = jnp.zeros((SEGS, total.shape[1]), jnp.float32)
    rows = []
    for name in range(4):
        part = total[name * SEGS : (name + 1) * SEGS]
        mod = mods[here[0] ^ name]
        gain = gains[name : name + 1]
        if name % 2 == 1:
            factor = jnp.tanh(mod)
            slope = 1.0 - factor * factor
        else:
            factor = 1.0 + mod
            slope = jnp.ones_like(mod)
        rows.append(jnp.sum(part * factor, axis=0, keepdims=True))
        mine = (jnp.zeros(part.shape, jnp.int32) + here[0]) == name
        grad = jnp.where(mine, part * slope * gain, grad)
    rows.append(total[4 * SEGS : 4 * SEGS + 2])
    rows = jnp.concatenate(rows, axis=0)
    high = rows.astype(jnp.bfloat16).astype(jnp.float32)
    pad = jnp.zeros((packed.shape[0] - 2 * SEGS - 2 * SUM_ROWS, total.shape[1]), jnp.float32)
    packed[...] = jnp.concatenate(
        [grad, cond[...].astype(jnp.float32), high, rows - high, pad], axis=0
    ).astype(jnp.bfloat16)


def rider_rows(count):
    return -(-(2 * SEGS * count + 2 * SUM_ROWS) // 16) * 16


def merge_rows(count, first, second, size):
    first, second = first.astype(jnp.float32), second.astype(jnp.float32)
    wide = SEGS * count
    start = 2 * wide
    sums = (
        first[start : start + SUM_ROWS]
        + first[start + SUM_ROWS : start + 2 * SUM_ROWS]
        + second[start : start + SUM_ROWS]
        + second[start + SUM_ROWS : start + 2 * SUM_ROWS]
    )
    high = sums.astype(jnp.bfloat16).astype(jnp.float32)
    pieces = [first[:wide], second[:wide], first[wide:start], second[wide:start], high, sums - high]
    rest = size - 4 * wide - 2 * SUM_ROWS
    if rest:
        pieces.append(jnp.zeros((rest, first.shape[1]), jnp.float32))
    return jnp.concatenate(pieces, axis=0).astype(jnp.bfloat16)


def merge_kernel(ours, theirs, out):
    out[...] = merge_rows(1, ours[...], theirs[...], out.shape[0])


def ada_kernel(count, heads, dp, own, *refs):
    parts = (own,) + refs[:3]
    ada_out, norm_out, head_out, gate_out = refs[3:]
    wide = SEGS * count
    base = own.shape[0] - rider_rows(count)
    columns = ada_out.shape[0]
    share = LANES // columns
    start = pl.multiple_of(dp[0] // share * LANES, LANES)
    grads, conds = [], []
    sums = jnp.zeros((SUM_ROWS, own.shape[1]), jnp.float32)
    for part in parts:
        rows = part[base:, :].astype(jnp.float32)
        grads.append(rows[:wide])
        conds.append(part[base:, pl.ds(start, LANES)].astype(jnp.float32)[wide : 2 * wide])
        for half in range(2):
            place = 2 * wide + half * SUM_ROWS
            sums = sums + rows[place : place + SUM_ROWS]
    conds = jnp.concatenate(conds, axis=0)
    conds = pltpu.roll(conds, (LANES - dp[0] % share * columns) % LANES, 1)
    acts = conds / (1.0 + jnp.exp(-conds))
    ada_out[...] = dot(
        acts.astype(jnp.bfloat16).astype(jnp.float32).T.astype(jnp.bfloat16),
        jnp.concatenate(grads, axis=0).astype(jnp.bfloat16),
    )[:columns]
    norm_out[...] = sums[:4]
    inner = heads * HEAD
    for row in range(3):
        line = jnp.zeros((1, HEAD), jnp.float32)
        for head in range(heads):
            place = row * inner + head * HEAD
            line = line + sums[4:5, place : place + HEAD]
        head_out[row : row + 1, :] = line
    lane = lane_index((1, LANES))
    line = jnp.zeros((1, LANES), jnp.float32)
    for head in range(HEADS):
        value = jnp.sum(sums[5:6, head * HEAD : (head + 1) * HEAD], axis=1, keepdims=True)
        line = jnp.where(lane == head, value, line)
    gate_out[...] = line


def back_kernel(count, *refs):
    grads, weights, upper, lower = refs[:count], refs[count : 2 * count], refs[-2], refs[-1]
    total = dot_t(grads[0][...], weights[0][...])
    for grad, weight in zip(grads[1:], weights[1:]):
        total = total + dot_t(grad[...], weight[...])
    half = upper.shape[0]
    upper[...] = total[:half].astype(jnp.bfloat16)
    lower[...] = total[half:].astype(jnp.bfloat16)


def back_call(grads, weights, name, ties=(), micros=0):
    rows, inner = grads[0].shape
    columns = weights[0].shape[0]
    tile = columns // 3
    return pl.pallas_call(
        lambda *refs: back_kernel(len(grads), *refs[: 2 * len(grads)], *refs[-2:]),
        grid=(columns // tile,),
        in_specs=[pl.BlockSpec((rows, inner), lambda step: (0, 0))] * len(grads)
        + [pl.BlockSpec((tile, inner), lambda step: (step, 0))] * len(grads)
        + [pl.BlockSpec(memory_space=pl.ANY)] * len(ties),
        out_specs=[pl.BlockSpec((rows // 2, tile), lambda step: (0, step))] * 2,
        out_shape=[jax.ShapeDtypeStruct((rows // 2, columns), jnp.bfloat16)] * 2,
        compiler_params=pltpu.CompilerParams(vmem_limit_bytes=VMEM_LIMIT),
        cost_estimate=cost_of(micros),
        name=name,
    )(*grads, *weights, *ties)


def shards(
    block_in,
    out_grad,
    condition,
    captions,
    caption_len,
    segment_ids,
    ada_weight,
    norm_gains,
    query_weight,
    key_weight,
    value_weight,
    head_gains,
    textkey_weight,
    textvalue_weight,
    cross_gate,
    out_weight,
    gate_weight,
    up_weight,
    down_weight,
):
    rows, width = block_in.shape
    length = segment_ids.shape[0]
    heads = cross_gate.shape[0]
    inner = heads * HEAD
    half_rows = length // 2
    position = lax.axis_index("tensor")
    spot = dp_spot(position)
    here = position.reshape(1)
    b16, f32 = jnp.bfloat16, jnp.float32

    blocks = gather_tensor(block_in)
    cond_rows = jnp.pad(condition, ((0, 0), (0, width - condition.shape[1])))
    own_act = jax.nn.silu(condition.astype(f32)).astype(b16)
    own_part = jnp.dot(own_act, ada_weight, preferred_element_type=f32)
    parts = gather_tensor(own_part)
    mods = jnp.stack([parts[ROW_ORDER.index(code)] for code in range(4)])

    cosine, sine, mark_q, mark_k, mark_t, segment, member, gate_lanes, gate_swapped, gains = whole_call(
        tables_kernel,
        (here, caption_len, cross_gate),
        [segment_ids.reshape(length // rows, rows), head_gains],
        [((length, LANES), f32)] * 2
        + [((length, LANES), b16)] * 2
        + [((SEGS * TXT, LANES), b16), ((rows, LANES), f32), ((8, rows), b16)]
        + [((1, inner), f32)] * 2
        + [((3, inner), f32)],
        "tables",
        micros=2,
    )
    caption_flat = captions.reshape(-1, captions.shape[-1])
    texts = caption_flat.shape[0]
    raw_t, text_value = text_call(caption_flat, textkey_weight, textvalue_weight)
    attn_rows, raw_q, raw_k, value = whole_call(
        project_kernel,
        (here,),
        blocks + [mods, norm_gains, mark_q, query_weight, key_weight, value_weight],
        [((length, width), b16), ((length, inner), f32), ((length, inner), f32), ((length, inner), b16)],
        "project",
        micros=6,
    )
    query, key, text, mixed, self_out, cross_out, self_log, cross_log = pair_call(
        attend_kernel,
        [(raw_q, 1), (raw_k, 1), (value, 1), (raw_t, 1), (text_value, 1), (cosine, None), (sine, None)]
        + [(gains, 1), (gate_lanes, 1), (gate_swapped, 1), (mark_q, None), (mark_k, None), (mark_t, None)],
        [((length, inner), b16, 1)] * 2
        + [((texts, inner), b16, 1), ((length, inner), b16, 1)]
        + [((length, inner), f32, 1)] * 4,
        "attend",
        micros=11,
    )

    def halves(product):
        return product(slice(0, half_rows)).astype(b16), product(slice(half_rows, None)).astype(b16)

    def all_of(block):
        return jnp.concatenate(gather_tensor(block), axis=0)

    upper, lower = halves(lambda part: jnp.dot(mixed[part], out_weight, preferred_element_type=f32))
    sums, sent = scatter_tensor(upper, lower)
    attn_rows_t = turned(attn_rows, (sent,))
    wide = ((rows, width), f32)
    narrow = ((rows, width), b16)
    totals = ((8, width), f32)
    attn_sum, middle, ffn_own = whole_call(
        middle_kernel,
        (here,),
        [block_in] + sums + [mods, norm_gains, segment],
        [wide, wide, narrow],
        "middle",
    )
    ffn_rows = all_of(ffn_own)
    gate_pre = jnp.dot(ffn_rows, gate_weight, preferred_element_type=f32)
    up_pre = jnp.dot(ffn_rows, up_weight, preferred_element_type=f32)
    sigmoid_gate = jax.nn.sigmoid(gate_pre)
    silu_gate = gate_pre * sigmoid_gate
    hidden = (silu_gate * up_pre).astype(b16)
    upper, lower = halves(lambda part: jnp.dot(hidden[part], down_weight, preferred_element_type=f32))
    sums, sent = scatter_tensor(upper, lower)
    ffn_rows_t = turned(ffn_rows, (sent,))
    block_out, grad_own, sum_gate_ffn = whole_call(
        block_out_kernel,
        (here,),
        [middle] + sums + [out_grad, mods, norm_gains, segment, member],
        [narrow, narrow, totals],
        "block_out",
    )

    grad_ffn = all_of(grad_own)
    grad_hidden = times_transpose(grad_ffn, down_weight)
    grad_gate = (
        grad_hidden * up_pre * sigmoid_gate * (1.0 + gate_pre * (1.0 - sigmoid_gate))
    ).astype(b16)
    grad_up = (grad_hidden * silu_gate).astype(b16)
    upper, lower = halves(
        lambda part: times_transpose(grad_gate[part], gate_weight)
        + times_transpose(grad_up[part], up_weight)
    )
    sums, sent = scatter_tensor(upper, lower)
    grad_ffn_t = turned(grad_ffn, (sent,))
    ffn_pairs = [(ffn_rows_t, [grad_gate, grad_up]), (grad_ffn_t, [hidden])]
    (halves_two,) = row_chunks(ffn_pairs, (2,), spot, ties=(sent,), micros=FFN_MICROS)
    ffn_passed = one_on(halves_two)
    grad_middle, grad_own, sum_scale_ffn, sum_gate_attn = whole_call(
        middle_back_kernel,
        (here,),
        [middle, attn_sum] + sums + [out_grad, mods, norm_gains, segment, member],
        [wide, narrow, totals, totals],
        "middle_back",
        micros=MIDDLE_MICROS,
    )

    grad_attn = all_of(grad_own)
    grad_mixed = times_transpose(grad_attn, out_weight).astype(b16)
    cross_grad, text_grad, text_value_grad, text_gain, gate_sum = pair_call(
        cross_back_kernel,
        [(query, 1), (text, 1), (text_value, 1), (raw_t, 1), (grad_mixed, 1), (cross_out, 1)]
        + [(cross_log, 1), (gains, 1), (mark_q, None), (mark_t, None)],
        [((length, inner), f32, 1), ((inner, texts), b16, 0), ((inner, texts), b16, 0)]
        + [((1, inner), f32, 1)] * 2,
        "cross_back",
        micros=CROSS_MICROS,
    )
    ffn_one, ffn_three, ffn_kept = row_chunks(
        ffn_pairs, (1, 3, 0), spot, extra=ffn_passed, ties=(text_grad,), micros=FFN_NEXT_MICROS
    )
    text_lefts = [text_grad, text_value_grad]
    (halves_two,) = column_chunks(text_lefts, caption_flat, (2,), spot, ties=(ffn_kept,))
    text_passed = one_on(halves_two)
    query_grad, key_grad, value_grad, head_gain = pair_call(
        self_back_kernel,
        [(query, 1), (key, 1), (value, 1), (raw_q, 1), (raw_k, 1), (grad_mixed, 1), (self_out, 1)]
        + [(self_log, 1), (cross_grad, 1), (cosine, None), (sine, None), (gains, 1)]
        + [(mark_q, None), (mark_k, None)],
        [((length, inner), b16, 1)] * 3 + [((2, inner), f32, 1)],
        "self_back",
        (halves_two[0],),
        micros=SELF_MICROS,
    )

    hidden_cols = hidden.shape[1]
    block_rows = width // BLOCKS
    got = [by_slots(part) for part in to_neighbours(ffn_kept, ffn_one, ffn_three)]
    shape = (PAIR, block_rows, 3 * hidden_cols)
    ffn_kept, ffn_sent = tiled_call(
        ffn_second_kernel,
        (spot,),
        got,
        [((2 * PAIR,) + shape[1:], b16)] * 2,
        "ffn_second",
        -1,
        4,
        (query_grad,),
    )
    upper, lower = back_call(
        [query_grad, key_grad, value_grad], [query_weight, key_weight, value_weight], "attn_back"
    )
    sums, sent = scatter_tensor(upper, lower)
    in_grad, sum_scale_attn = whole_call(
        block_in_kernel,
        (here,),
        [block_in, grad_middle] + sums + [mods, norm_gains, segment, member],
        [narrow, totals],
        "block_in",
        (ffn_sent,),
        micros=BLOCK_IN_MICROS,
    )
    (stacked,) = whole_call(
        stack_sums_kernel,
        (here,),
        [sum_scale_attn, sum_gate_attn, sum_scale_ffn, sum_gate_ffn]
        + [head_gain, text_gain, gate_sum, gate_lanes],
        [((16, width), f32)],
        "stack_sums",
    )
    sums_stacked = stacked
    text_one, text_three, text_kept = column_chunks(
        text_lefts, caption_flat, (1, 3, 0), spot, extra=text_passed, ties=(sums_stacked,), micros=TEXT_MICROS
    )
    stacked = gather_tensor(stacked)
    ffn_own, ffn_sent = tiled_call(
        ffn_middle_kernel,
        (),
        [ffn_kept, dp_permute(ffn_sent, "second", "flip")],
        [(shape, b16)] * 2,
        "ffn_middle",
        -1,
        2,
        (text_kept,),
    )
    (riders,) = whole_call(
        pack_kernel,
        (here,),
        stacked + [mods, norm_gains, cond_rows],
        [((rider_rows(1), width), b16)],
        "pack",
        (ffn_sent,),
    )
    theirs = dp_permute(riders, "z", 1)
    (riders,) = whole_call(
        merge_kernel, (), [riders, theirs], [((rider_rows(PAIR), width), b16)], "merge"
    )
    attn_pairs = [
        (attn_rows_t, [query_grad, key_grad, value_grad]),
        (turned(grad_attn, (halves_two[0],)), [mixed]),
    ]
    (halves_two,) = row_chunks(attn_pairs, (2,), spot, riders=(riders,), micros=ATTN_FIRST_MICROS)
    attn_passed = one_on(halves_two)
    text_rows = caption_flat.shape[1] // BLOCKS
    attn_one, attn_three, attn_kept = row_chunks(
        attn_pairs, (1, 3, 0), spot, extra=attn_passed, riders=(riders,), micros=ATTN_MICROS
    )
    text_own, text_sent = tiled_call(
        text_second_kernel,
        (spot,),
        to_neighbours(text_kept, text_one, text_three),
        [((2 * inner, 2 * PAIR * text_rows), b16)] * 2,
        "text_second",
        0,
        4,
        (attn_kept,),
    )
    stage = tiled_call(
        functools.partial(attn_second_kernel, block_rows),
        (spot,),
        [riders] + to_neighbours(attn_kept, attn_one, attn_three),
        [((PAIR * block_rows + rider_rows(4 * PAIR), width), b16)] * RING,
        "attn_second",
        -1,
        4,
        (text_sent,),
    )
    ffn_own_kept, ffn_own_sent = tiled_call(
        ffn_third_kernel,
        (spot,),
        [ffn_own, dp_permute(ffn_sent, "second", "mirror")],
        [(shape[1:], b16)] * 2,
        "ffn_third",
        -1,
        2,
        (stage[0],),
    )
    text_own, text_sent = tiled_call(
        text_middle_kernel,
        (),
        [text_own, dp_permute(text_sent, "second", "flip")],
        [((2 * inner, PAIR * text_rows), b16)] * 2,
        "text_middle",
        0,
        2,
        (stage[0],),
    )
    got = exchange(stage, "second")
    kept, sent = tiled_call(
        attn_third_kernel, (spot,), got, [((block_rows, width), b16)] * 2, "attn_third",
        -1,
        2
    )
    gate_sum_out, up_sum_out, down_sum_out = whole_call(
        ffn_last_kernel,
        (),
        exchange([ffn_own_kept, ffn_own_sent], "z"),
        [((block_rows, hidden_cols), f32)] * 2 + [((hidden_cols, block_rows), f32)],
        "ffn_last",
        (kept,),
    )
    text_own_kept, text_own_sent = tiled_call(
        text_third_kernel,
        (spot,),
        [text_own, dp_permute(text_sent, "second", "mirror")],
        [((2 * inner, text_rows), b16)] * 2,
        "text_third",
        0,
        2,
        (kept,),
    )
    textkey_sum, textvalue_sum = whole_call(
        text_last_kernel,
        (),
        exchange([text_own_kept, text_own_sent], "z"),
        [((text_rows, inner), f32)] * 2,
        "text_last",
    )
    ada_grad, norm_grads, head_grads, crossgate = tiled_call(
        functools.partial(ada_kernel, 4 * PAIR, heads),
        (lax.axis_index("dp").reshape(1),),
        got,
        [((condition.shape[1] // BLOCKS, width), f32), ((4, width), f32), ((3, HEAD), f32)]
        + [((1, LANES), f32)],
        "ada",
        0,
        1,
        (kept,),
    )
    crossgate_grad = crossgate[0, :HEADS]
    query_sum, key_sum, value_sum, outw_sum = whole_call(
        attn_last_kernel,
        (),
        exchange([kept, sent], "z"),
        [((block_rows, inner), f32)] * 3 + [((inner, block_rows), f32)],
        "attn_last",
    )
    return (
        block_out,
        in_grad,
        ada_grad,
        norm_grads,
        query_sum,
        key_sum,
        value_sum,
        head_grads,
        textkey_sum,
        textvalue_sum,
        crossgate_grad,
        outw_sum,
        gate_sum_out,
        up_sum_out,
        down_sum_out,
    )


def solution(mesh):
    return jax.shard_map(
        shards,
        mesh=mesh,
        in_specs=(
            P(("dp", "tensor"), None),
            P(("dp", "tensor"), None),
            P("dp", None),
            P("dp", None, None),
            P("dp"),
            P("dp"),
            P(None, "tensor"),
            P(),
            P(None, "tensor"),
            P(None, "tensor"),
            P(None, "tensor"),
            P(),
            P(None, "tensor"),
            P(None, "tensor"),
            P("tensor"),
            P("tensor", None),
            P(None, "tensor"),
            P(None, "tensor"),
            P("tensor", None),
        ),
        out_specs=(
            P(("dp", "tensor"), None),
            P(("dp", "tensor"), None),
            P("dp", "tensor"),
            P(),
            P("dp", "tensor"),
            P("dp", "tensor"),
            P("dp", "tensor"),
            P(),
            P("dp", "tensor"),
            P("dp", "tensor"),
            P(),
            P("tensor", "dp"),
            P("dp", "tensor"),
            P("dp", "tensor"),
            P("tensor", "dp"),
        ),
        check_vma=False,
    )
```

```python
import functools
import math

import jax
import jax.numpy as jnp
from jax import lax
from jax.experimental import pallas as pl
from jax.experimental.pallas import tpu as pltpu
from jax.sharding import PartitionSpec as P

HEAD = 64
HEADS = 24
TXT = 256
SEGS = 3
EPS = 1e-06
LANES = 2 * HEAD
SHUT = 256.0
ROOT = HEAD ** (-0.5)
VMEM_LIMIT = 16 * 2**20
NO_COST = pl.CostEstimate(flops=0, bytes_accessed=0, transcendentals=0)


def cost_of(micros):
    return pl.CostEstimate(flops=int(micros * 1e9), bytes_accessed=0, transcendentals=0)


SUM_ROWS = 6
CROSS_MICROS = 10
BLOCK_IN_MICROS = 0
FFN_MICROS = 3
FFN_NEXT_MICROS = 8
MIDDLE_MICROS = 10
SELF_MICROS = 0
ATTN_MICROS = 3
TEXT_MICROS = 8
TEXT_AFTER = 1
PACK_MICROS = 16
ATTN_FIRST_MICROS = 0

RING = 4
PAIR = 2
BLOCKS = RING * PAIR * RING
SLOTS = BLOCKS // RING
SEND_ORDER = (2, 1, 3, 0)
CORE_SWAP = [(0, 1), (1, 0), (2, 3), (3, 2)]
CHIP_SWAP = [(0, 2), (2, 0), (1, 3), (3, 1)]
ROW_ORDER = (0, 2, 1, 3)

def dp_index(x, z, y):
    return (x * PAIR + z) * RING + y


def dp_perm(axis, step):
    pairs = []

    def moved(place, size):
        if step == "flip":
            return place ^ 1
        if step == "mirror":
            return size - 1 - place
        return (place + step) % size

    for x in range(RING):
        for z in range(PAIR):
            for y in range(RING):
                for tensor in range(2 * PAIR):
                    way = axis
                    if axis in ("first", "second"):
                        way = "x" if (tensor % 2 == 0) == (axis == "first") else "y"
                    target = {
                        "x": (moved(x, RING), z, y),
                        "y": (x, z, moved(y, RING)),
                        "z": (x, moved(z, PAIR), y),
                    }[way]
                    pairs.append(
                        (
                            dp_index(x, z, y) * 2 * PAIR + tensor,
                            dp_index(*target) * 2 * PAIR + tensor,
                        )
                    )
    return pairs


def dp_permute(values, axis, step):
    return lax.ppermute(values, ("dp", "tensor"), dp_perm(axis, step))


def dp_spot(position):
    index = lax.axis_index("dp")
    x, z, y = index // (RING * PAIR), index // RING % PAIR, index % RING
    core = position % 2
    return jnp.stack([jnp.where(core == 0, x, y), z, jnp.where(core == 0, y, x), core])


def swap_core(values):
    return lax.ppermute(values, "tensor", CORE_SWAP)


def swap_chip(values):
    return lax.ppermute(values, "tensor", CHIP_SWAP)


def times_transpose(left, right):
    return lax.dot_general(
        left, right, (((1,), (1,)), ((), ())), preferred_element_type=jnp.float32
    )


def gather_tensor(block):
    far = swap_chip(block)
    near = swap_core(block)
    return [block, far, near, swap_core(far)]


def scatter_tensor(upper, lower):
    near = swap_core(lower)
    rows = upper.shape[0] // 2
    far = (upper[rows:].astype(jnp.float32) + near[rows:].astype(jnp.float32)).astype(near.dtype)
    return [upper, near, swap_chip(far)], far


def turn_kernel(source, target):
    target[...] = source[...].T


def turned(values, ties=()):
    tile = 512 if values.shape[1] % 512 == 0 else values.shape[1]
    return pl.pallas_call(
        lambda source, *rest: turn_kernel(source, rest[-1]),
        grid=(values.shape[1] // tile,),
        in_specs=[pl.BlockSpec((values.shape[0], tile), lambda step: (0, step))]
        + [pl.BlockSpec(memory_space=pl.ANY)] * len(ties),
        out_specs=pl.BlockSpec((tile, values.shape[0]), lambda step: (step, 0)),
        out_shape=jax.ShapeDtypeStruct(values.shape[::-1], values.dtype),
        compiler_params=pltpu.CompilerParams(vmem_limit_bytes=VMEM_LIMIT),
        cost_estimate=NO_COST,
    )(values, *ties)


def chunk_block(offset, slot, spot):
    first = (spot[0] + offset) % RING
    z, second = slot // RING, slot % RING
    x = jnp.where(spot[3] == 0, first, second)
    y = jnp.where(spot[3] == 0, second, first)
    return dp_index(x, z, y)


def offset_of_step(offsets, step):
    offset = offsets[-1]
    for place in range(len(offsets) - 1):
        offset = jnp.where(step == place, offsets[place], offset)
    return offset


def chunk_kernel(make, offsets, halves, extra, outs, held, sems):
    step = pl.program_id(0)
    first, second = halves

    def copies(place):
        slot = held.at[place % 2]
        if offsets[place] != 2:
            return [pltpu.make_async_copy(slot, outs[place], sems.at[place % 2, 0])]
        return [
            pltpu.make_async_copy(slot.at[half], out, sems.at[place % 2, way])
            for way, (half, out) in enumerate(zip((first, second), outs[place]))
        ]

    for place, offset in enumerate(offsets):

        @pl.when(step == place)
        def _(place=place, offset=offset):
            if place >= 2:
                for copy in copies(place - 2):
                    copy.wait()
            added = {1: (first, extra[0]), 3: (second, extra[1])}.get(offset) if extra else None
            make(held.at[place % 2], added, offset)
            for copy in copies(place):
                copy.start()
            if place == len(offsets) - 1:
                for last in range(max(place - 1, 0), place + 1):
                    for copy in copies(last):
                        copy.wait()


def chunk_call(make, operands, specs, offsets, halves, shape, spot, extra, ties, name, micros):
    count = len(operands)
    pieces = []
    for offset in offsets:
        if offset == 2:
            pieces += [tuple(len(range(*s.indices(d))) for s, d in zip(h, shape)) for h in halves]
        else:
            pieces.append(shape)

    def kernel(spot_ref, *refs):
        inputs, extras = refs[:count], refs[count : count + len(extra)]
        outs = list(refs[-len(pieces) - 2 : -2])
        grouped = []
        for offset in offsets:
            grouped.append((outs.pop(0), outs.pop(0)) if offset == 2 else outs.pop(0))
        chunk_kernel(
            functools.partial(make, inputs), offsets, halves, extras, grouped, refs[-2], refs[-1]
        )

    found = pl.pallas_call(
        kernel,
        grid_spec=pltpu.PrefetchScalarGridSpec(
            num_scalar_prefetch=1,
            grid=(len(offsets),),
            in_specs=list(specs)
            + [pl.BlockSpec(part.shape, lambda step, spot: (0, 0)) for part in extra]
            + [pl.BlockSpec(memory_space=pl.ANY)] * len(ties),
            out_specs=[pl.BlockSpec(memory_space=pl.ANY)] * len(pieces),
            scratch_shapes=[
                pltpu.VMEM((2,) + shape, jnp.bfloat16),
                pltpu.SemaphoreType.DMA((2, 2)),
            ],
        ),
        out_shape=[jax.ShapeDtypeStruct(piece, jnp.bfloat16) for piece in pieces],
        compiler_params=pltpu.CompilerParams(vmem_limit_bytes=VMEM_LIMIT),
        cost_estimate=cost_of(micros),
        name=name,
    )(spot, *operands, *extra, *ties)
    found = list(found)
    return [
        (found.pop(0), found.pop(0)) if offset == 2 else found.pop(0) for offset in offsets
    ]


def make_rows(groups, inputs, slot, added, offset):
    lefts, rights = inputs[: SLOTS * len(groups)], inputs[SLOTS * len(groups) :]
    size = SLOTS * lefts[0].shape[1]
    if len(rights) > sum(groups):
        riders = rights[-1][...]
        count, half = riders.shape[0], riders.shape[1] // 2
        first, second = slice(size, size + count), slice(size + count, size + 2 * count)
        if offset == 2:
            for side in (slice(0, half), slice(half, 2 * half)):
                slot[first, side] = riders[:, :half]
                slot[second, side] = riders[:, half:]
        else:
            slot[first, :] = riders
            if offset == 1:
                slot[second, :half] = added[1][first, :]
                slot[second, half:] = added[1][second, :]
            else:
                slot[second, :] = riders
    column = place = 0
    for group, count in enumerate(groups):
        rows = jnp.concatenate(
            [left[0] for left in lefts[SLOTS * group : SLOTS * (group + 1)]], axis=0
        )
        for right in rights[place : place + count]:
            wide = right.shape[1]
            product = dot(rows, right[...])
            low, high = column, column
            if added is not None:
                low = min(max(column, added[0][1].start), column + wide)
                high = min(max(column, added[0][1].stop), column + wide)
            for start, stop in ((column, low), (low, high), (high, column + wide)):
                if start < stop:
                    part = product[:, start - column : stop - column]
                    if (start, stop) == (low, high):
                        base = added[0][1].start
                        part = part + added[1][:size, start - base : stop - base].astype(jnp.float32)
                    slot[:size, start:stop] = part.astype(jnp.bfloat16)
            column += wide
        place += count


def row_chunks(pairs, offsets, spot, extra=(), ties=(), micros=0, riders=()):
    lefts = [left.reshape(BLOCKS, left.shape[0] // BLOCKS, left.shape[1]) for left, _ in pairs]
    rights = [right for _, group in pairs for right in group]
    total = sum(right.shape[1] for right in rights)
    specs, operands = [], []
    for left in lefts:
        for slot in range(SLOTS):
            specs.append(
                pl.BlockSpec(
                    (1,) + left.shape[1:],
                    lambda step, spot, slot=slot: (
                        chunk_block(offset_of_step(offsets, step), slot, spot),
                        0,
                        0,
                    ),
                )
            )
            operands.append(left)
    specs += [pl.BlockSpec(right.shape, lambda step, spot: (0, 0)) for right in rights]
    specs += [pl.BlockSpec(part.shape, lambda step, spot: (0, 0)) for part in riders]
    rows = SLOTS * lefts[0].shape[1] + sum(2 * part.shape[0] for part in riders)
    halves = [(slice(0, rows), slice(0, total // 2)), (slice(0, rows), slice(total // 2, total))]
    return chunk_call(
        functools.partial(make_rows, [len(group) for _, group in pairs]),
        operands + rights + list(riders),
        specs,
        offsets,
        halves,
        (rows, total),
        spot,
        extra,
        ties,
        "row_chunks",
        micros,
    )


def make_columns(lefts, inputs, slot, added, offset):
    whole = jnp.concatenate([right[...] for right in inputs[lefts:]], axis=1)
    row = 0
    for left in inputs[:lefts]:
        product = dot(left[...], whole)
        if added is not None and added[0][0].start == row:
            product = product + added[1][...].astype(jnp.float32)
        slot[row : row + left.shape[0], :] = product.astype(jnp.bfloat16)
        row += left.shape[0]


def column_chunks(lefts, right, offsets, spot, extra=(), ties=(), micros=0):
    rows = lefts[0].shape[0]
    depth, columns = right.shape
    specs = [pl.BlockSpec(left.shape, lambda step, spot: (0, 0)) for left in lefts]
    for slot in range(SLOTS):
        specs.append(
            pl.BlockSpec(
                (depth, columns // BLOCKS),
                lambda step, spot, slot=slot: (
                    0,
                    chunk_block(offset_of_step(offsets, step), slot, spot),
                ),
            )
        )
    lanes = columns // RING
    halves = [(slice(0, rows), slice(0, lanes)), (slice(rows, 2 * rows), slice(0, lanes))]
    return chunk_call(
        functools.partial(make_columns, len(lefts)),
        list(lefts) + [right] * SLOTS,
        specs,
        offsets,
        halves,
        (2 * rows, lanes),
        spot,
        extra,
        ties,
        "column_chunks",
        micros,
    )


def add_up(refs, index):
    total = refs[0][index].astype(jnp.float32)
    for ref in refs[1:]:
        total = total + ref[index].astype(jnp.float32)
    return total


def lane_slice(start, size):
    return (slice(None), pl.ds(pl.multiple_of(start * size, size), size))


def halving_places(spot):
    own = spot[2]
    other = own ^ 1
    return (own, RING - 1 - own), (other, RING - 1 - other)


def ffn_second_kernel(spot, *refs):
    parts = refs[:-2]
    for out, places in zip(refs[-2:], halving_places(spot)):
        for index, place in enumerate(places):
            for z in range(PAIR):
                out[index * PAIR + z] = add_up(parts, z * RING + place).astype(jnp.bfloat16)


def ffn_middle_kernel(kept, got, own, sent):
    for out, start in ((own, 0), (sent, PAIR)):
        for z in range(PAIR):
            out[z] = add_up((kept, got), start + z).astype(jnp.bfloat16)


def ffn_third_kernel(spot, *refs):
    for out, z in ((refs[-2], spot[1]), (refs[-1], (spot[1] + 1) % PAIR)):
        out[...] = add_up(refs[:-2], z).astype(jnp.bfloat16)


def ffn_last_kernel(kept, got, gate_out, up_out, down_out):
    total = kept[...].astype(jnp.float32) + got[...].astype(jnp.float32)
    hidden = gate_out.shape[1]
    gate_out[...] = total[:, :hidden]
    up_out[...] = total[:, hidden : 2 * hidden]
    down_out[...] = total[:, 2 * hidden :].T


def text_second_kernel(spot, *refs):
    parts = refs[:-2]
    lanes = parts[0].shape[1] // SLOTS
    for out, places in zip(refs[-2:], halving_places(spot)):
        for index, place in enumerate(places):
            for z in range(PAIR):
                start = (index * PAIR + z) * lanes
                out[:, start : start + lanes] = add_up(
                    parts, lane_slice(z * RING + place, lanes)
                ).astype(jnp.bfloat16)


def text_middle_kernel(kept, got, own, sent):
    wide = own.shape[1]
    for out, start in ((own, 0), (sent, wide)):
        index = (slice(None), slice(start, start + wide))
        out[...] = add_up((kept, got), index).astype(jnp.bfloat16)


def text_third_kernel(spot, *refs):
    lanes = refs[-1].shape[1]
    for out, z in ((refs[-2], spot[1]), (refs[-1], (spot[1] + 1) % PAIR)):
        out[...] = add_up(refs[:-2], lane_slice(z, lanes)).astype(jnp.bfloat16)


def text_last_kernel(kept, got, textkey, textvalue):
    total = kept[...].astype(jnp.float32) + got[...].astype(jnp.float32)
    columns = textkey.shape[1]
    textkey[...] = total[:columns].T
    textvalue[...] = total[columns:].T


def attn_second_kernel(spot, riders, *refs):
    parts, outs = refs[:-RING], refs[-RING:]
    rows = parts[0].shape[1]
    for offset in range(RING):
        for z in range(PAIR):
            slot = z * RING + (spot[2] + offset) % RING
            outs[offset][z * rows : (z + 1) * rows, :] = add_up(parts, slot).astype(jnp.bfloat16)
        outs[offset][PAIR * rows :, :] = riders[...]


def attn_third_kernel(spot, *refs):
    rows = refs[-1].shape[0]
    for out, z in ((refs[-2], spot[1]), (refs[-1], (spot[1] + 1) % PAIR)):
        index = (pl.ds(pl.multiple_of(z * rows, 16), rows), slice(None))
        out[...] = add_up(refs[:RING], index).astype(jnp.bfloat16)


def attn_last_kernel(kept, got, query, key, value, outw):
    total = kept[...].astype(jnp.float32) + got[...].astype(jnp.float32)
    columns = query.shape[1]
    for place, out in enumerate((query, key, value)):
        out[...] = total[:, place * columns : (place + 1) * columns]
    outw[...] = total[:, 3 * columns :].T


def whole_call(kernel, scalars, operands, outs, name, ties=(), scratch=(), micros=0):
    whole = pl.BlockSpec(memory_space=pltpu.VMEM)
    count = len(scalars) + len(operands)
    return pl.pallas_call(
        lambda *refs: kernel(*refs[:count], *refs[count + len(ties) :]),
        in_specs=[pl.BlockSpec(memory_space=pltpu.SMEM)] * len(scalars)
        + [whole] * len(operands)
        + [pl.BlockSpec(memory_space=pl.ANY)] * len(ties),
        out_specs=[whole] * len(outs),
        out_shape=[jax.ShapeDtypeStruct(shape, kind) for shape, kind in outs],
        scratch_shapes=list(scratch),
        compiler_params=pltpu.CompilerParams(vmem_limit_bytes=VMEM_LIMIT),
        cost_estimate=cost_of(micros),
        name=name,
    )(*scalars, *operands, *ties)


def tiled_call(kernel, scalars, operands, outs, name, axis, tiles, ties=(), micros=0, axes=None):
    def spec(shape, axis):
        block = list(shape)
        block[axis] //= tiles
        if axis == 0:
            return pl.BlockSpec(tuple(block), lambda step: (step,) + (0,) * (len(shape) - 1))
        return pl.BlockSpec(tuple(block), lambda step: (0,) * (len(shape) - 1) + (step,))

    count = len(scalars) + len(operands)
    return pl.pallas_call(
        lambda *refs: kernel(*refs[:count], *refs[count + len(ties) :]),
        grid=(tiles,),
        in_specs=[pl.BlockSpec(memory_space=pltpu.SMEM)] * len(scalars)
        + [spec(part.shape, way) for part, way in zip(operands, axes or [axis] * len(operands))]
        + [pl.BlockSpec(memory_space=pl.ANY)] * len(ties),
        out_specs=[spec(shape, axis) for shape, _ in outs],
        out_shape=[jax.ShapeDtypeStruct(shape, kind) for shape, kind in outs],
        compiler_params=pltpu.CompilerParams(vmem_limit_bytes=VMEM_LIMIT),
        cost_estimate=cost_of(micros),
        name=name,
    )(*scalars, *[pltpu.with_memory_space_constraint(part, pltpu.HBM) for part in operands], *ties)


def exchange(chunks, axis):
    return [chunks[0]] + [
        dp_permute(chunks[step], axis, step) for step in range(1, len(chunks))
    ]


def one_on(halves):
    return dp_permute(halves[0], "first", 1), dp_permute(halves[1], "first", RING - 1)


def to_neighbours(own, ahead, behind):
    return [own, dp_permute(ahead, "first", 1), dp_permute(behind, "first", RING - 1)]


def by_slots(chunk):
    return chunk.reshape(SLOTS, chunk.shape[0] // SLOTS, chunk.shape[1])


def lane_index(shape):
    return lax.broadcasted_iota(jnp.int32, shape, 1)


def head_lanes(shape, head):
    lane = lane_index(shape)
    return (lane < HEAD) if head == 0 else (lane >= HEAD)


def per_head(values, reduce):
    first = head_lanes(values.shape, 0)
    left = jnp.sum(jnp.where(first, values, 0.0), axis=1, keepdims=True)
    right = jnp.sum(jnp.where(first, 0.0, values), axis=1, keepdims=True)
    return jnp.where(first, left, right)


def head_units(raw):
    inverse = lax.rsqrt(per_head(raw * raw, None) * (1.0 / HEAD) + EPS)
    return raw * inverse, inverse


def partner(values):
    lane = lane_index(values.shape)
    return jnp.where(
        lane % HEAD < HEAD // 2,
        pltpu.roll(values, LANES - HEAD // 2, 1),
        pltpu.roll(values, HEAD // 2, 1),
    )


def dot(left, right):
    return jnp.dot(left, right, preferred_element_type=jnp.float32)


def dot_t(left, right):
    return lax.dot_general(left, right, (((1,), (1,)), ((), ())), preferred_element_type=jnp.float32)


def attend_kernel(
    raw_q, raw_k, value, raw_t, text_value, cosine, sine, gains, gate, gate_swapped, mark_q, mark_k, mark_t,
    query_out, key_out, text_out, mixed_out, self_out, cross_out, self_log, cross_log,
):
    cos, sin = cosine[...], sine[...]
    unit = head_units(raw_q[...])[0] * gains[0:1, :]
    query = ((unit * cos + partner(unit) * sin).astype(jnp.bfloat16) * ROOT).astype(jnp.bfloat16)
    unit = head_units(raw_k[...])[0] * gains[1:2, :]
    key = (unit * cos + partner(unit) * sin).astype(jnp.bfloat16)
    text = (head_units(raw_t[...])[0] * gains[2:3, :]).astype(jnp.bfloat16)
    query_out[...] = query
    key_out[...] = key
    text_out[...] = text

    def attention(keys, marks, values):
        outs, sums = [], []
        for head in range(2):
            own = head_lanes(query.shape, head)
            own_keys = head_lanes(keys.shape, head)
            probe = jnp.where(own, query, mark_q[...])
            scores = dot_t(probe, jnp.where(own_keys, keys, marks))
            weights = jnp.exp(scores).astype(jnp.bfloat16)
            both = dot(weights, jnp.where(own_keys, values, jnp.ones_like(values)))
            outs.append(both)
        first = head_lanes(outs[0].shape, 0)
        product = jnp.where(first, outs[0], outs[1])
        total = jnp.where(first, outs[1], outs[0])
        return product / pltpu.roll(total, HEAD, 1), jnp.log(total)

    out, log = attention(key, mark_k[...], value[...])
    self_out[...] = out
    self_log[...] = log
    cross, log = attention(text, mark_t[...], text_value[...])
    cross_out[...] = cross
    cross_log[...] = log - jnp.log(gate_swapped[...])
    mixed_out[...] = (out + gate[...] * cross).astype(jnp.bfloat16)


def attention_grads(query, keys, marks, values, grad, out, log, mark_q):
    rows = grad.astype(jnp.float32)
    delta = per_head(rows * out, None)
    delta = pltpu.roll(delta, HEAD, 1)
    lane = lane_index(query.shape) % HEAD
    log_high = log.astype(jnp.bfloat16)
    log_low = (log - log_high.astype(jnp.float32)).astype(jnp.bfloat16)
    delta_high = delta.astype(jnp.bfloat16)
    delta_low = (delta - delta_high.astype(jnp.float32)).astype(jnp.bfloat16)
    zero = jnp.zeros_like(query)
    code = jnp.where(lane == 4, -log_high, jnp.where(lane == 5, -log_low, mark_q))
    shift = jnp.where(lane == 4, -delta_high, jnp.where(lane == 5, -delta_low, zero))
    key_grads, value_grads, query_grads = [], [], []
    for head in range(2):
        own = head_lanes(query.shape, head)
        own_keys = head_lanes(keys.shape, head)
        probe = jnp.where(own, query, code)
        probs = jnp.exp(dot_t(jnp.where(own_keys, keys, marks), probe))
        slope = dot_t(jnp.where(own_keys, values, marks), jnp.where(own, grad, shift))
        score_grad = (probs * slope).astype(jnp.bfloat16)
        value_grads.append(dot(probs.astype(jnp.bfloat16), grad))
        key_grads.append(dot(score_grad, query))
        turned = keys[:, head * HEAD : (head + 1) * HEAD].T
        query_grads.append(dot(turned, score_grad))
    first = head_lanes(keys.shape, 0)
    return (
        jnp.concatenate(query_grads, axis=0),
        jnp.where(first, key_grads[0], key_grads[1]),
        jnp.where(first, value_grads[0], value_grads[1]),
    )


def norm_back(weighted, unit, inverse):
    return inverse * (weighted - unit * (per_head(weighted * unit, None) * (1.0 / HEAD)))


def cross_back_kernel(
    query, text, text_value, raw_t, grad, out, log, gains, mark_q, mark_t,
    query_grad, raw_grad, value_grad, gain_sum, gate_sum,
):
    grad_q, grad_t, grad_v = attention_grads(
        query[...], text[...], mark_t[...], text_value[...], grad[...], out[...], log[...], mark_q[...]
    )
    query_grad[...] = grad_q.T
    value_grad[...] = grad_v.astype(jnp.bfloat16).T
    grad_t = grad_t.astype(jnp.bfloat16).astype(jnp.float32)
    unit, inverse = head_units(raw_t[...])
    gain_sum[...] = jnp.sum(grad_t * unit, axis=0, keepdims=True)
    raw_grad[...] = norm_back(grad_t * gains[2:3, :], unit, inverse).astype(jnp.bfloat16).T
    gate_sum[...] = jnp.sum(grad[...].astype(jnp.float32) * out[...], axis=0, keepdims=True)


def self_back_kernel(
    query, key, value, raw_q, raw_k, grad, out, log, cross_grad, cosine, sine, gains, mark_q, mark_k,
    query_grad, key_grad, value_grad, gain_sum,
):
    grad_q, grad_k, grad_v = attention_grads(
        query[...], key[...], mark_k[...], value[...], grad[...], out[...], log[...], mark_q[...]
    )
    value_grad[...] = grad_v.astype(jnp.bfloat16)
    cos, sin = cosine[...], sine[...]
    grad_q = (grad_q.T + cross_grad[...]) * ROOT
    for turn, raw, row, target in ((grad_q, raw_q, 0, query_grad), (grad_k, raw_k, 1, key_grad)):
        turn = turn.astype(jnp.bfloat16).astype(jnp.float32)
        turn = turn * cos - partner(turn) * sin
        unit, inverse = head_units(raw[...])
        gain_sum[row : row + 1, :] = jnp.sum(turn * unit, axis=0, keepdims=True)
        target[...] = norm_back(turn * gains[row : row + 1, :], unit, inverse).astype(jnp.bfloat16)


def pair_call(kernel, operands, outs, name, ties=(), micros=0):
    def spec(shape, cut):
        if cut is None:
            return pl.BlockSpec(shape, lambda pair: (0, 0))
        if cut == 1:
            return pl.BlockSpec((shape[0], LANES), lambda pair: (0, pair))
        return pl.BlockSpec((LANES, shape[1]), lambda pair: (pair, 0))

    width = outs[0][0][0] if outs[0][2] == 0 else outs[0][0][1]
    return pl.pallas_call(
        lambda *refs: kernel(*refs[: len(operands)], *refs[len(operands) + len(ties) :]),
        grid=(width // LANES,),
        in_specs=[spec(part.shape, cut) for part, cut in operands]
        + [pl.BlockSpec(memory_space=pl.ANY)] * len(ties),
        out_specs=[spec(shape, cut) for shape, _, cut in outs],
        out_shape=[jax.ShapeDtypeStruct(shape, kind) for shape, kind, _ in outs],
        compiler_params=pltpu.CompilerParams(vmem_limit_bytes=VMEM_LIMIT),
        cost_estimate=cost_of(micros),
        name=name,
    )(*[part for part, _ in operands], *ties)
def inverse_rms(values):
    return lax.rsqrt(jnp.mean(values * values, axis=-1, keepdims=True) + EPS)


def row_norm_back(weighted, unit, inverse):
    return inverse * (weighted - unit * jnp.mean(weighted * unit, axis=-1, keepdims=True))


def per_row(table, segment):
    return jnp.where(segment == 0.0, table[0:1], jnp.where(segment == 1.0, table[1:2], table[2:3]))


def total_of(parts):
    upper, near, far = parts
    rows = far.shape[0]
    return (
        upper[:rows].astype(jnp.float32) + near[:rows].astype(jnp.float32) + far[...].astype(jnp.float32)
    )


def segment_sums(member, values):
    high = values.astype(jnp.bfloat16)
    low = (values - high.astype(jnp.float32)).astype(jnp.bfloat16)
    return dot(member, high) + dot(member, low)


def tables_kernel(here, lens, gate, segments, head_gains, cosine, sine, mark_q, mark_k, mark_t,
                  segment, member, gate_lanes, gate_swapped, gains):
    heads = gains.shape[1] // HEAD
    lane = lane_index(gate_lanes.shape) // HEAD
    line = jnp.zeros(gate_lanes.shape, jnp.float32)
    swapped = line
    for head in range(heads):
        line = jnp.where(lane == head, gate[head], line)
        swapped = jnp.where(lane == head ^ 1, gate[head], swapped)
    gate_lanes[...] = jnp.tanh(line)
    gate_swapped[...] = jnp.tanh(swapped)
    gains[...] = jnp.concatenate([head_gains[...]] * heads, axis=1)
    rows = segments.shape[1]
    ids = segments[...]
    first = jnp.sum((ids < 1).astype(jnp.float32))
    second = jnp.sum((ids < 2).astype(jnp.float32))
    lane = lane_index((rows, LANES))
    half = HEAD // 2
    rate = jnp.exp((lane % half).astype(jnp.float32) * (-2.0 * math.log(10000.0) / HEAD))
    within = lane % HEAD
    for block, code in enumerate(ROW_ORDER):
        source = here[0] ^ code
        line = segments[pl.ds(source, 1), :].astype(jnp.float32)
        label = jnp.broadcast_to(line, (rows, rows)).T
        start = jnp.where(label == 0.0, 0.0, jnp.where(label == 1.0, first, second))
        token = (lax.broadcasted_iota(jnp.int32, (rows, LANES), 0) + source * rows).astype(jnp.float32)
        angle = (token - start) * rate
        index = slice(block * rows, (block + 1) * rows)
        cosine[index, :] = jnp.cos(angle)
        sine[index, :] = jnp.where(within < half, -1.0, 1.0) * jnp.sin(angle)
        same = ((label == within.astype(jnp.float32)) & (within < SEGS)).astype(jnp.float32)
        shut = (within == SEGS).astype(jnp.float32)
        ones = ((within >= SEGS) & (within < SEGS + 3)).astype(jnp.float32)
        mark_q[index, :] = (SHUT * same - SHUT * shut).astype(jnp.bfloat16)
        mark_k[index, :] = (same + ones).astype(jnp.bfloat16)
        if block == 0:
            segment[...] = label
            member[...] = (
                lax.broadcasted_iota(jnp.int32, (8, rows), 0).astype(jnp.float32) == line
            ).astype(jnp.bfloat16)
    for group in range(SEGS):
        lane = lane_index((TXT, LANES)) % HEAD
        row = lax.broadcasted_iota(jnp.int32, (TXT, LANES), 0)
        inside = ((lane == group) & (row < lens[group])).astype(jnp.float32)
        ones = ((lane >= SEGS) & (lane < SEGS + 3)).astype(jnp.float32)
        mark_t[group * TXT : (group + 1) * TXT, :] = (inside + ones).astype(jnp.bfloat16)


def text_kernel(captions, key_weight, value_weight, raw_out, value_out, raw_sum, value_sum):
    step = pl.program_id(0)

    @pl.when(step == 0)
    def _():
        raw_sum[...] = dot(captions[...], key_weight[...])
        value_sum[...] = dot(captions[...], value_weight[...])

    @pl.when(step > 0)
    def _():
        raw_sum[...] += dot(captions[...], key_weight[...])
        value_sum[...] += dot(captions[...], value_weight[...])

    @pl.when(step == pl.num_programs(0) - 1)
    def _():
        raw_out[...] = raw_sum[...]
        value_out[...] = value_sum[...].astype(jnp.bfloat16)


def text_call(captions, key_weight, value_weight):
    rows, depth = captions.shape
    columns = key_weight.shape[1]
    tile = depth // 4
    return pl.pallas_call(
        text_kernel,
        grid=(depth // tile,),
        in_specs=[
            pl.BlockSpec((rows, tile), lambda step: (0, step)),
            pl.BlockSpec((tile, columns), lambda step: (step, 0)),
            pl.BlockSpec((tile, columns), lambda step: (step, 0)),
        ],
        out_specs=[pl.BlockSpec((rows, columns), lambda step: (0, 0))] * 2,
        out_shape=[
            jax.ShapeDtypeStruct((rows, columns), jnp.float32),
            jax.ShapeDtypeStruct((rows, columns), jnp.bfloat16),
        ],
        scratch_shapes=[pltpu.VMEM((rows, columns), jnp.float32)] * 2,
        compiler_params=pltpu.CompilerParams(vmem_limit_bytes=VMEM_LIMIT),
        cost_estimate=cost_of(9),
        name="text",
    )(*[pltpu.with_memory_space_constraint(part, pltpu.HBM) for part in (captions, key_weight, value_weight)])


def project_kernel(here, own, far, near, last, mods, gains, segment_q, query_w, key_w, value_w,
                   rows_out, raw_q, raw_k, value):
    table = mods[here[0]]
    rows = own.shape[0]
    for block, part in enumerate((own, far, near, last)):
        index = slice(block * rows, (block + 1) * rows)
        values = part[...].astype(jnp.float32)
        marks = segment_q[index, :].astype(jnp.float32)
        scale = jnp.where(
            marks[:, 0:1] > 0.0, table[0:1], jnp.where(marks[:, 1:2] > 0.0, table[1:2], table[2:3])
        )
        rows_out[index, :] = (
            values * inverse_rms(values) * gains[0:1] * (1.0 + scale)
        ).astype(jnp.bfloat16)
    raw_q[...] = dot(rows_out[...], query_w[...])
    raw_k[...] = dot(rows_out[...], key_w[...])
    value[...] = dot(rows_out[...], value_w[...]).astype(jnp.bfloat16)


def middle_kernel(here, block, upper, near, far, mods, gains, segment, attn_out, middle_out, rows_out):
    attn_sum = total_of((upper, near, far))
    label = segment[:, 0:1]
    factor = jnp.tanh(per_row(mods[here[0] ^ 1], label)) * gains[1:2]
    middle = block[...].astype(jnp.float32) + factor * (attn_sum * inverse_rms(attn_sum))
    attn_out[...] = attn_sum
    middle_out[...] = middle
    scale = per_row(mods[here[0] ^ 2], label)
    rows_out[...] = (middle * inverse_rms(middle) * gains[2:3] * (1.0 + scale)).astype(jnp.bfloat16)


def block_out_kernel(here, middle, upper, near, far, grad, mods, gains, segment, member,
                     block_out, grad_out, sums):
    ffn_sum = total_of((upper, near, far))
    inverse = inverse_rms(ffn_sum)
    unit = ffn_sum * inverse
    factor = jnp.tanh(per_row(mods[here[0] ^ 3], segment[:, 0:1])) * gains[3:4]
    block_out[...] = (middle[...] + factor * unit).astype(jnp.bfloat16)
    incoming = grad[...].astype(jnp.float32)
    grad_out[...] = row_norm_back(incoming * factor, unit, inverse).astype(jnp.bfloat16)
    sums[...] = segment_sums(member[...], incoming * unit)


def middle_back_kernel(here, middle, attn, upper, near, far, grad, mods, gains, segment, member,
                       middle_grad, attn_grad, ffn_sums, attn_sums):
    grad_in = total_of((upper, near, far))
    label = segment[:, 0:1]
    inverse = inverse_rms(middle[...])
    unit = middle[...] * inverse
    factor = gains[2:3] * (1.0 + per_row(mods[here[0] ^ 2], label))
    ffn_sums[...] = segment_sums(member[...], grad_in * unit)
    grad_middle = grad[...].astype(jnp.float32) + row_norm_back(grad_in * factor, unit, inverse)
    middle_grad[...] = grad_middle
    inverse = inverse_rms(attn[...])
    unit = attn[...] * inverse
    factor = jnp.tanh(per_row(mods[here[0] ^ 1], label)) * gains[1:2]
    attn_grad[...] = row_norm_back(grad_middle * factor, unit, inverse).astype(jnp.bfloat16)
    attn_sums[...] = segment_sums(member[...], grad_middle * unit)


def block_in_kernel(here, block, middle_grad, upper, near, far, mods, gains, segment, member,
                    in_grad, sums):
    grad_in = total_of((upper, near, far))
    values = block[...].astype(jnp.float32)
    inverse = inverse_rms(values)
    unit = values * inverse
    factor = gains[0:1] * (1.0 + per_row(mods[here[0]], segment[:, 0:1]))
    in_grad[...] = (
        middle_grad[...] + row_norm_back(grad_in * factor, unit, inverse)
    ).astype(jnp.bfloat16)
    sums[...] = segment_sums(member[...], grad_in * unit)


def stack_sums_kernel(here, first, second, third, fourth, head_gain, text_gain, gate_sum, gate, out):
    width = out.shape[1]
    heads = jnp.concatenate([head_gain[0:1], head_gain[1:2], text_gain[...]], axis=1)
    inner = heads.shape[1] // 3
    gates = gate_sum[...] * (1.0 - gate[...] * gate[...])
    gates = jnp.concatenate([gates, jnp.zeros((1, width - inner), jnp.float32)], axis=1)
    lane = lane_index(gates.shape)
    moved = jnp.zeros_like(gates)
    for position in range(4):
        turn = pltpu.roll(gates, position * inner, 1) if position else gates
        moved = jnp.where((lane // inner == position) & (here[0] == position), turn, moved)
    out[...] = jnp.concatenate(
        [part[0:SEGS] for part in (first, second, third, fourth)]
        + [
            jnp.concatenate([heads, jnp.zeros((1, width - 3 * inner), jnp.float32)], axis=1),
            moved,
            jnp.zeros((2, width), jnp.float32),
        ],
        axis=0,
    )


def pack_kernel(here, own, far, near, last, mods, gains, cond, packed):
    total = own[...] + far[...] + near[...] + last[...]
    grad = jnp.zeros((SEGS, total.shape[1]), jnp.float32)
    rows = []
    for name in range(4):
        part = total[name * SEGS : (name + 1) * SEGS]
        mod = mods[here[0] ^ name]
        gain = gains[name : name + 1]
        if name % 2 == 1:
            factor = jnp.tanh(mod)
            slope = 1.0 - factor * factor
        else:
            factor = 1.0 + mod
            slope = jnp.ones_like(mod)
        rows.append(jnp.sum(part * factor, axis=0, keepdims=True))
        mine = (jnp.zeros(part.shape, jnp.int32) + here[0]) == name
        grad = jnp.where(mine, part * slope * gain, grad)
    rows.append(total[4 * SEGS : 4 * SEGS + 2])
    rows = jnp.concatenate(rows, axis=0)
    high = rows.astype(jnp.bfloat16).astype(jnp.float32)
    pad = jnp.zeros((packed.shape[0] - 2 * SEGS - 2 * SUM_ROWS, total.shape[1]), jnp.float32)
    packed[...] = jnp.concatenate(
        [grad, cond[...].astype(jnp.float32), high, rows - high, pad], axis=0
    ).astype(jnp.bfloat16)


def rider_rows(count):
    return -(-(2 * SEGS * count + 2 * SUM_ROWS) // 16) * 16


def merge_rows(count, first, second, size):
    first, second = first.astype(jnp.float32), second.astype(jnp.float32)
    wide = SEGS * count
    start = 2 * wide
    sums = (
        first[start : start + SUM_ROWS]
        + first[start + SUM_ROWS : start + 2 * SUM_ROWS]
        + second[start : start + SUM_ROWS]
        + second[start + SUM_ROWS : start + 2 * SUM_ROWS]
    )
    high = sums.astype(jnp.bfloat16).astype(jnp.float32)
    pieces = [first[:wide], second[:wide], first[wide:start], second[wide:start], high, sums - high]
    rest = size - 4 * wide - 2 * SUM_ROWS
    if rest:
        pieces.append(jnp.zeros((rest, first.shape[1]), jnp.float32))
    return jnp.concatenate(pieces, axis=0).astype(jnp.bfloat16)


def merge_kernel(count, ours, theirs, out):
    out[...] = merge_rows(count, ours[...], theirs[...], out.shape[0])


def ada_kernel(count, heads, dp, own, *refs):
    parts = (own,) + refs[:3]
    ada_out, norm_out, head_out, gate_out = refs[3:]
    wide = SEGS * count
    base = own.shape[0] - rider_rows(count)
    columns = ada_out.shape[0]
    share = LANES // columns
    start = pl.multiple_of(dp[0] // share * LANES, LANES)
    grads, conds = [], []
    sums = jnp.zeros((SUM_ROWS, own.shape[1]), jnp.float32)
    for part in parts:
        rows = part[base:, :].astype(jnp.float32)
        grads.append(rows[:wide])
        conds.append(part[base:, pl.ds(start, LANES)].astype(jnp.float32)[wide : 2 * wide])
        for half in range(2):
            place = 2 * wide + half * SUM_ROWS
            sums = sums + rows[place : place + SUM_ROWS]
    conds = jnp.concatenate(conds, axis=0)
    conds = pltpu.roll(conds, (LANES - dp[0] % share * columns) % LANES, 1)
    acts = conds / (1.0 + jnp.exp(-conds))
    ada_out[...] = dot(
        acts.astype(jnp.bfloat16).astype(jnp.float32).T.astype(jnp.bfloat16),
        jnp.concatenate(grads, axis=0).astype(jnp.bfloat16),
    )[:columns]
    norm_out[...] = sums[:4]
    inner = heads * HEAD
    for row in range(3):
        line = jnp.zeros((1, HEAD), jnp.float32)
        for head in range(heads):
            place = row * inner + head * HEAD
            line = line + sums[4:5, place : place + HEAD]
        head_out[row : row + 1, :] = line
    lane = lane_index((1, LANES))
    line = jnp.zeros((1, LANES), jnp.float32)
    for head in range(HEADS):
        value = jnp.sum(sums[5:6, head * HEAD : (head + 1) * HEAD], axis=1, keepdims=True)
        line = jnp.where(lane == head, value, line)
    gate_out[...] = line


def back_kernel(count, *refs):
    grads, weights, upper, lower = refs[:count], refs[count : 2 * count], refs[-2], refs[-1]
    total = dot_t(grads[0][...], weights[0][...])
    for grad, weight in zip(grads[1:], weights[1:]):
        total = total + dot_t(grad[...], weight[...])
    half = upper.shape[0]
    upper[...] = total[:half].astype(jnp.bfloat16)
    lower[...] = total[half:].astype(jnp.bfloat16)


def back_call(grads, weights, name, ties=(), micros=0):
    rows, inner = grads[0].shape
    columns = weights[0].shape[0]
    tile = columns // 3
    return pl.pallas_call(
        lambda *refs: back_kernel(len(grads), *refs[: 2 * len(grads)], *refs[-2:]),
        grid=(columns // tile,),
        in_specs=[pl.BlockSpec((rows, inner), lambda step: (0, 0))] * len(grads)
        + [pl.BlockSpec((tile, inner), lambda step: (step, 0))] * len(grads)
        + [pl.BlockSpec(memory_space=pl.ANY)] * len(ties),
        out_specs=[pl.BlockSpec((rows // 2, tile), lambda step: (0, step))] * 2,
        out_shape=[jax.ShapeDtypeStruct((rows // 2, columns), jnp.bfloat16)] * 2,
        compiler_params=pltpu.CompilerParams(vmem_limit_bytes=VMEM_LIMIT),
        cost_estimate=cost_of(micros),
        name=name,
    )(*grads, *weights, *ties)


def shards(
    block_in,
    out_grad,
    condition,
    captions,
    caption_len,
    segment_ids,
    ada_weight,
    norm_gains,
    query_weight,
    key_weight,
    value_weight,
    head_gains,
    textkey_weight,
    textvalue_weight,
    cross_gate,
    out_weight,
    gate_weight,
    up_weight,
    down_weight,
):
    rows, width = block_in.shape
    length = segment_ids.shape[0]
    heads = cross_gate.shape[0]
    inner = heads * HEAD
    half_rows = length // 2
    position = lax.axis_index("tensor")
    spot = dp_spot(position)
    here = position.reshape(1)
    b16, f32 = jnp.bfloat16, jnp.float32

    blocks = gather_tensor(block_in)
    cond_rows = jnp.pad(condition, ((0, 0), (0, width - condition.shape[1])))
    own_act = jax.nn.silu(condition.astype(f32)).astype(b16)
    own_part = jnp.dot(own_act, ada_weight, preferred_element_type=f32)
    parts = gather_tensor(own_part)
    mods = jnp.stack([parts[ROW_ORDER.index(code)] for code in range(4)])

    cosine, sine, mark_q, mark_k, mark_t, segment, member, gate_lanes, gate_swapped, gains = whole_call(
        tables_kernel,
        (here, caption_len, cross_gate),
        [segment_ids.reshape(length // rows, rows), head_gains],
        [((length, LANES), f32)] * 2
        + [((length, LANES), b16)] * 2
        + [((SEGS * TXT, LANES), b16), ((rows, LANES), f32), ((8, rows), b16)]
        + [((1, inner), f32)] * 2
        + [((3, inner), f32)],
        "tables",
        micros=2,
    )
    caption_flat = captions.reshape(-1, captions.shape[-1])
    texts = caption_flat.shape[0]
    raw_t, text_value = text_call(caption_flat, textkey_weight, textvalue_weight)
    attn_rows, raw_q, raw_k, value = whole_call(
        project_kernel,
        (here,),
        blocks + [mods, norm_gains, mark_q, query_weight, key_weight, value_weight],
        [((length, width), b16), ((length, inner), f32), ((length, inner), f32), ((length, inner), b16)],
        "project",
        micros=6,
    )
    query, key, text, mixed, self_out, cross_out, self_log, cross_log = pair_call(
        attend_kernel,
        [(raw_q, 1), (raw_k, 1), (value, 1), (raw_t, 1), (text_value, 1), (cosine, None), (sine, None)]
        + [(gains, 1), (gate_lanes, 1), (gate_swapped, 1), (mark_q, None), (mark_k, None), (mark_t, None)],
        [((length, inner), b16, 1)] * 2
        + [((texts, inner), b16, 1), ((length, inner), b16, 1)]
        + [((length, inner), f32, 1)] * 4,
        "attend",
        micros=11,
    )

    def halves(product):
        return product(slice(0, half_rows)).astype(b16), product(slice(half_rows, None)).astype(b16)

    def all_of(block):
        return jnp.concatenate(gather_tensor(block), axis=0)

    upper, lower = halves(lambda part: jnp.dot(mixed[part], out_weight, preferred_element_type=f32))
    sums, sent = scatter_tensor(upper, lower)
    attn_rows_t = turned(attn_rows, (sent,))
    wide = ((rows, width), f32)
    narrow = ((rows, width), b16)
    totals = ((8, width), f32)
    attn_sum, middle, ffn_own = whole_call(
        middle_kernel,
        (here,),
        [block_in] + sums + [mods, norm_gains, segment],
        [wide, wide, narrow],
        "middle",
    )
    ffn_rows = all_of(ffn_own)
    gate_pre = jnp.dot(ffn_rows, gate_weight, preferred_element_type=f32)
    up_pre = jnp.dot(ffn_rows, up_weight, preferred_element_type=f32)
    sigmoid_gate = jax.nn.sigmoid(gate_pre)
    silu_gate = gate_pre * sigmoid_gate
    hidden = (silu_gate * up_pre).astype(b16)
    upper, lower = halves(lambda part: jnp.dot(hidden[part], down_weight, preferred_element_type=f32))
    sums, sent = scatter_tensor(upper, lower)
    ffn_rows_t = turned(ffn_rows, (sent,))
    block_out, grad_own, sum_gate_ffn = whole_call(
        block_out_kernel,
        (here,),
        [middle] + sums + [out_grad, mods, norm_gains, segment, member],
        [narrow, narrow, totals],
        "block_out",
    )

    grad_ffn = all_of(grad_own)
    grad_hidden = times_transpose(grad_ffn, down_weight)
    grad_gate = (
        grad_hidden * up_pre * sigmoid_gate * (1.0 + gate_pre * (1.0 - sigmoid_gate))
    ).astype(b16)
    grad_up = (grad_hidden * silu_gate).astype(b16)
    upper, lower = halves(
        lambda part: times_transpose(grad_gate[part], gate_weight)
        + times_transpose(grad_up[part], up_weight)
    )
    sums, sent = scatter_tensor(upper, lower)
    grad_ffn_t = turned(grad_ffn, (sent,))
    ffn_pairs = [(ffn_rows_t, [grad_gate, grad_up]), (grad_ffn_t, [hidden])]
    (halves_two,) = row_chunks(ffn_pairs, (2,), spot, ties=(sent,), micros=FFN_MICROS)
    ffn_passed = one_on(halves_two)
    grad_middle, grad_own, sum_scale_ffn, sum_gate_attn = whole_call(
        middle_back_kernel,
        (here,),
        [middle, attn_sum] + sums + [out_grad, mods, norm_gains, segment, member],
        [wide, narrow, totals, totals],
        "middle_back",
        micros=MIDDLE_MICROS,
    )

    grad_attn = all_of(grad_own)
    grad_mixed = times_transpose(grad_attn, out_weight).astype(b16)
    cross_grad, text_grad, text_value_grad, text_gain, gate_sum = pair_call(
        cross_back_kernel,
        [(query, 1), (text, 1), (text_value, 1), (raw_t, 1), (grad_mixed, 1), (cross_out, 1)]
        + [(cross_log, 1), (gains, 1), (mark_q, None), (mark_t, None)],
        [((length, inner), f32, 1), ((inner, texts), b16, 0), ((inner, texts), b16, 0)]
        + [((1, inner), f32, 1)] * 2,
        "cross_back",
        micros=CROSS_MICROS,
    )
    ffn_one, ffn_three, ffn_kept = row_chunks(
        ffn_pairs, (1, 3, 0), spot, extra=ffn_passed, ties=(text_grad,), micros=FFN_NEXT_MICROS
    )
    text_lefts = [text_grad, text_value_grad]
    (halves_two,) = column_chunks(text_lefts, caption_flat, (2,), spot, ties=(ffn_kept,))
    text_passed = one_on(halves_two)
    query_grad, key_grad, value_grad, head_gain = pair_call(
        self_back_kernel,
        [(query, 1), (key, 1), (value, 1), (raw_q, 1), (raw_k, 1), (grad_mixed, 1), (self_out, 1)]
        + [(self_log, 1), (cross_grad, 1), (cosine, None), (sine, None), (gains, 1)]
        + [(mark_q, None), (mark_k, None)],
        [((length, inner), b16, 1)] * 3 + [((2, inner), f32, 1)],
        "self_back",
        (halves_two[0],),
        micros=SELF_MICROS,
    )

    hidden_cols = hidden.shape[1]
    block_rows = width // BLOCKS
    got = [by_slots(part) for part in to_neighbours(ffn_kept, ffn_one, ffn_three)]
    shape = (PAIR, block_rows, 3 * hidden_cols)
    ffn_kept, ffn_sent = tiled_call(
        ffn_second_kernel,
        (spot,),
        got,
        [((2 * PAIR,) + shape[1:], b16)] * 2,
        "ffn_second",
        -1,
        4,
        (query_grad,),
    )
    upper, lower = back_call(
        [query_grad, key_grad, value_grad], [query_weight, key_weight, value_weight], "attn_back"
    )
    sums, sent = scatter_tensor(upper, lower)
    in_grad, sum_scale_attn = whole_call(
        block_in_kernel,
        (here,),
        [block_in, grad_middle] + sums + [mods, norm_gains, segment, member],
        [narrow, totals],
        "block_in",
        (ffn_sent,),
        micros=BLOCK_IN_MICROS,
    )
    (stacked,) = whole_call(
        stack_sums_kernel,
        (here,),
        [sum_scale_attn, sum_gate_attn, sum_scale_ffn, sum_gate_ffn]
        + [head_gain, text_gain, gate_sum, gate_lanes],
        [((16, width), f32)],
        "stack_sums",
    )
    attn_pairs = [
        (attn_rows_t, [query_grad, key_grad, value_grad]),
        (turned(grad_attn, (halves_two[0],)), [mixed]),
    ]
    (halves_two,) = row_chunks(attn_pairs, (2,), spot, ties=(stacked,), micros=ATTN_FIRST_MICROS)
    attn_passed = one_on(halves_two)
    stacked = gather_tensor(stacked)
    text_one, text_three, text_kept = column_chunks(
        text_lefts, caption_flat, (1, 3, 0), spot, extra=text_passed, ties=(halves_two[0],), micros=TEXT_MICROS
    )
    attn_one, attn_three, attn_kept = row_chunks(
        attn_pairs, (1, 3, 0), spot, extra=attn_passed, ties=(text_kept,), micros=ATTN_MICROS
    )
    ffn_own, ffn_sent = tiled_call(
        ffn_middle_kernel,
        (),
        [ffn_kept, dp_permute(ffn_sent, "second", "flip")],
        [(shape, b16)] * 2,
        "ffn_middle",
        -1,
        2,
        (attn_kept,),
    )
    (riders,) = whole_call(
        pack_kernel,
        (here,),
        stacked + [mods, norm_gains, cond_rows],
        [((rider_rows(1), width), b16)],
        "pack",
        (ffn_sent,),
        micros=PACK_MICROS,
    )
    text_rows = caption_flat.shape[1] // BLOCKS
    count = 1
    held = []
    for axis, step in (("z", 1), ("first", 1), ("first", 2)):
        (riders,) = whole_call(
            functools.partial(merge_kernel, count),
            (),
            [riders, dp_permute(riders, axis, step)],
            [((rider_rows(2 * count), width), b16)],
            "merge",
        )
        held.append(riders)
        count *= 2
    text_own, text_sent = tiled_call(
        text_second_kernel,
        (spot,),
        to_neighbours(text_kept, text_one, text_three),
        [((2 * inner, 2 * PAIR * text_rows), b16)] * 2,
        "text_second",
        0,
        4,
        (held[TEXT_AFTER],),
    )
    stage = tiled_call(
        attn_second_kernel,
        (spot,),
        [riders] + [by_slots(part) for part in to_neighbours(attn_kept, attn_one, attn_three)],
        [((PAIR * block_rows + rider_rows(4 * PAIR), width), b16)] * RING,
        "attn_second",
        -1,
        4,
        (text_sent,),
    )
    ffn_own_kept, ffn_own_sent = tiled_call(
        ffn_third_kernel,
        (spot,),
        [ffn_own, dp_permute(ffn_sent, "second", "mirror")],
        [(shape[1:], b16)] * 2,
        "ffn_third",
        -1,
        2,
        (stage[0],),
    )
    text_own, text_sent = tiled_call(
        text_middle_kernel,
        (),
        [text_own, dp_permute(text_sent, "second", "flip")],
        [((2 * inner, PAIR * text_rows), b16)] * 2,
        "text_middle",
        0,
        2,
        (stage[0],),
    )
    got = exchange(stage, "second")
    kept, sent = tiled_call(
        attn_third_kernel, (spot,), got, [((block_rows, width), b16)] * 2, "attn_third",
        -1,
        2
    )
    gate_sum_out, up_sum_out, down_sum_out = whole_call(
        ffn_last_kernel,
        (),
        exchange([ffn_own_kept, ffn_own_sent], "z"),
        [((block_rows, hidden_cols), f32)] * 2 + [((hidden_cols, block_rows), f32)],
        "ffn_last",
        (kept,),
    )
    text_own_kept, text_own_sent = tiled_call(
        text_third_kernel,
        (spot,),
        [text_own, dp_permute(text_sent, "second", "mirror")],
        [((2 * inner, text_rows), b16)] * 2,
        "text_third",
        0,
        2,
        (kept,),
    )
    textkey_sum, textvalue_sum = whole_call(
        text_last_kernel,
        (),
        exchange([text_own_kept, text_own_sent], "z"),
        [((text_rows, inner), f32)] * 2,
        "text_last",
    )
    ada_grad, norm_grads, head_grads, crossgate = tiled_call(
        functools.partial(ada_kernel, 4 * PAIR, heads),
        (lax.axis_index("dp").reshape(1),),
        got,
        [((condition.shape[1] // BLOCKS, width), f32), ((4, width), f32), ((3, HEAD), f32)]
        + [((1, LANES), f32)],
        "ada",
        0,
        1,
        (kept,),
    )
    crossgate_grad = crossgate[0, :HEADS]
    query_sum, key_sum, value_sum, outw_sum = whole_call(
        attn_last_kernel,
        (),
        exchange([kept, sent], "z"),
        [((block_rows, inner), f32)] * 3 + [((inner, block_rows), f32)],
        "attn_last",
    )
    return (
        block_out,
        in_grad,
        ada_grad,
        norm_grads,
        query_sum,
        key_sum,
        value_sum,
        head_grads,
        textkey_sum,
        textvalue_sum,
        crossgate_grad,
        outw_sum,
        gate_sum_out,
        up_sum_out,
        down_sum_out,
    )


def solution(mesh):
    return jax.shard_map(
        shards,
        mesh=mesh,
        in_specs=(
            P(("dp", "tensor"), None),
            P(("dp", "tensor"), None),
            P("dp", None),
            P("dp", None, None),
            P("dp"),
            P("dp"),
            P(None, "tensor"),
            P(),
            P(None, "tensor"),
            P(None, "tensor"),
            P(None, "tensor"),
            P(),
            P(None, "tensor"),
            P(None, "tensor"),
            P("tensor"),
            P("tensor", None),
            P(None, "tensor"),
            P(None, "tensor"),
            P("tensor", None),
        ),
        out_specs=(
            P(("dp", "tensor"), None),
            P(("dp", "tensor"), None),
            P("dp", "tensor"),
            P(),
            P("dp", "tensor"),
            P("dp", "tensor"),
            P("dp", "tensor"),
            P(),
            P("dp", "tensor"),
            P("dp", "tensor"),
            P(),
            P("tensor", "dp"),
            P("dp", "tensor"),
            P("dp", "tensor"),
            P("tensor", "dp"),
        ),
        check_vma=False,
    )
```

```python
import functools
import math

import jax
import jax.numpy as jnp
from jax import lax
from jax.experimental import pallas as pl
from jax.experimental.pallas import tpu as pltpu
from jax.sharding import PartitionSpec as P

HEAD = 64
HEADS = 24
TXT = 256
SEGS = 3
EPS = 1e-06
LANES = 2 * HEAD
SHUT = 256.0
ROOT = HEAD ** (-0.5)
VMEM_LIMIT = 16 * 2**20
NO_COST = pl.CostEstimate(flops=0, bytes_accessed=0, transcendentals=0)


def cost_of(micros):
    return pl.CostEstimate(flops=int(micros * 1e9), bytes_accessed=0, transcendentals=0)


SUM_ROWS = 6
CROSS_MICROS = 10
BLOCK_IN_MICROS = 0
FFN_MICROS = 3
FFN_NEXT_MICROS = 8
MIDDLE_MICROS = 10
SELF_MICROS = 0
ATTN_MICROS = 3
TEXT_MICROS = 8
PACK_MICROS = 16
SECOND_MICROS = 8
ATTN_FIRST_MICROS = 0

RING = 4
PAIR = 2
BLOCKS = RING * PAIR * RING
SLOTS = BLOCKS // RING
SEND_ORDER = (2, 1, 3, 0)
CORE_SWAP = [(0, 1), (1, 0), (2, 3), (3, 2)]
CHIP_SWAP = [(0, 2), (2, 0), (1, 3), (3, 1)]
ROW_ORDER = (0, 2, 1, 3)

def dp_index(x, z, y):
    return (x * PAIR + z) * RING + y


def dp_perm(axis, step):
    pairs = []

    def moved(place, size):
        if step == "flip":
            return place ^ 1
        if step == "mirror":
            return size - 1 - place
        return (place + step) % size

    for x in range(RING):
        for z in range(PAIR):
            for y in range(RING):
                for tensor in range(2 * PAIR):
                    way = axis
                    if axis in ("first", "second"):
                        way = "x" if (tensor % 2 == 0) == (axis == "first") else "y"
                    target = {
                        "x": (moved(x, RING), z, y),
                        "y": (x, z, moved(y, RING)),
                        "z": (x, moved(z, PAIR), y),
                    }[way]
                    pairs.append(
                        (
                            dp_index(x, z, y) * 2 * PAIR + tensor,
                            dp_index(*target) * 2 * PAIR + tensor,
                        )
                    )
    return pairs


def dp_permute(values, axis, step):
    return lax.ppermute(values, ("dp", "tensor"), dp_perm(axis, step))


def dp_spot(position):
    index = lax.axis_index("dp")
    x, z, y = index // (RING * PAIR), index // RING % PAIR, index % RING
    core = position % 2
    return jnp.stack([jnp.where(core == 0, x, y), z, jnp.where(core == 0, y, x), core])


def swap_core(values):
    return lax.ppermute(values, "tensor", CORE_SWAP)


def swap_chip(values):
    return lax.ppermute(values, "tensor", CHIP_SWAP)


def times_transpose(left, right):
    return lax.dot_general(
        left, right, (((1,), (1,)), ((), ())), preferred_element_type=jnp.float32
    )


def gather_tensor(block):
    far = swap_chip(block)
    near = swap_core(block)
    return [block, far, near, swap_core(far)]


def scatter_tensor(upper, lower):
    near = swap_core(lower)
    rows = upper.shape[0] // 2
    far = (upper[rows:].astype(jnp.float32) + near[rows:].astype(jnp.float32)).astype(near.dtype)
    return [upper, near, swap_chip(far)], far


def turn_kernel(source, target):
    target[...] = source[...].T


def turned(values, ties=()):
    tile = 512 if values.shape[1] % 512 == 0 else values.shape[1]
    return pl.pallas_call(
        lambda source, *rest: turn_kernel(source, rest[-1]),
        grid=(values.shape[1] // tile,),
        in_specs=[pl.BlockSpec((values.shape[0], tile), lambda step: (0, step))]
        + [pl.BlockSpec(memory_space=pl.ANY)] * len(ties),
        out_specs=pl.BlockSpec((tile, values.shape[0]), lambda step: (step, 0)),
        out_shape=jax.ShapeDtypeStruct(values.shape[::-1], values.dtype),
        compiler_params=pltpu.CompilerParams(vmem_limit_bytes=VMEM_LIMIT),
        cost_estimate=NO_COST,
    )(values, *ties)


def chunk_block(offset, slot, spot):
    first = (spot[0] + offset) % RING
    z, second = slot // RING, slot % RING
    x = jnp.where(spot[3] == 0, first, second)
    y = jnp.where(spot[3] == 0, second, first)
    return dp_index(x, z, y)


def offset_of_step(offsets, step):
    offset = offsets[-1]
    for place in range(len(offsets) - 1):
        offset = jnp.where(step == place, offsets[place], offset)
    return offset


def chunk_kernel(make, offsets, halves, extra, outs, held, sems):
    step = pl.program_id(0)
    first, second = halves

    def copies(place):
        slot = held.at[place % 2]
        if offsets[place] != 2:
            return [pltpu.make_async_copy(slot, outs[place], sems.at[place % 2, 0])]
        return [
            pltpu.make_async_copy(slot.at[half], out, sems.at[place % 2, way])
            for way, (half, out) in enumerate(zip((first, second), outs[place]))
        ]

    for place, offset in enumerate(offsets):

        @pl.when(step == place)
        def _(place=place, offset=offset):
            if place >= 2:
                for copy in copies(place - 2):
                    copy.wait()
            added = {1: (first, extra[0]), 3: (second, extra[1])}.get(offset) if extra else None
            make(held.at[place % 2], added, offset)
            for copy in copies(place):
                copy.start()
            if place == len(offsets) - 1:
                for last in range(max(place - 1, 0), place + 1):
                    for copy in copies(last):
                        copy.wait()


def chunk_call(make, operands, specs, offsets, halves, shape, spot, extra, ties, name, micros):
    count = len(operands)
    pieces = []
    for offset in offsets:
        if offset == 2:
            pieces += [tuple(len(range(*s.indices(d))) for s, d in zip(h, shape)) for h in halves]
        else:
            pieces.append(shape)

    def kernel(spot_ref, *refs):
        inputs, extras = refs[:count], refs[count : count + len(extra)]
        outs = list(refs[-len(pieces) - 2 : -2])
        grouped = []
        for offset in offsets:
            grouped.append((outs.pop(0), outs.pop(0)) if offset == 2 else outs.pop(0))
        chunk_kernel(
            functools.partial(make, inputs), offsets, halves, extras, grouped, refs[-2], refs[-1]
        )

    found = pl.pallas_call(
        kernel,
        grid_spec=pltpu.PrefetchScalarGridSpec(
            num_scalar_prefetch=1,
            grid=(len(offsets),),
            in_specs=list(specs)
            + [pl.BlockSpec(part.shape, lambda step, spot: (0, 0)) for part in extra]
            + [pl.BlockSpec(memory_space=pl.ANY)] * len(ties),
            out_specs=[pl.BlockSpec(memory_space=pl.ANY)] * len(pieces),
            scratch_shapes=[
                pltpu.VMEM((2,) + shape, jnp.bfloat16),
                pltpu.SemaphoreType.DMA((2, 2)),
            ],
        ),
        out_shape=[jax.ShapeDtypeStruct(piece, jnp.bfloat16) for piece in pieces],
        compiler_params=pltpu.CompilerParams(vmem_limit_bytes=VMEM_LIMIT),
        cost_estimate=cost_of(micros),
        name=name,
    )(spot, *operands, *extra, *ties)
    found = list(found)
    return [
        (found.pop(0), found.pop(0)) if offset == 2 else found.pop(0) for offset in offsets
    ]


def make_rows(groups, inputs, slot, added, offset):
    lefts, rights = inputs[: SLOTS * len(groups)], inputs[SLOTS * len(groups) :]
    size = SLOTS * lefts[0].shape[1]
    if len(rights) > sum(groups):
        slot[size:, :] = rights[-1][...]
    column = place = 0
    for group, count in enumerate(groups):
        rows = jnp.concatenate(
            [left[0] for left in lefts[SLOTS * group : SLOTS * (group + 1)]], axis=0
        )
        for right in rights[place : place + count]:
            wide = right.shape[1]
            product = dot(rows, right[...])
            low, high = column, column
            if added is not None:
                low = min(max(column, added[0][1].start), column + wide)
                high = min(max(column, added[0][1].stop), column + wide)
            for start, stop in ((column, low), (low, high), (high, column + wide)):
                if start < stop:
                    part = product[:, start - column : stop - column]
                    if (start, stop) == (low, high):
                        base = added[0][1].start
                        part = part + added[1][:size, start - base : stop - base].astype(jnp.float32)
                    slot[:size, start:stop] = part.astype(jnp.bfloat16)
            column += wide
        place += count


def row_chunks(pairs, offsets, spot, extra=(), ties=(), micros=0, riders=()):
    lefts = [left.reshape(BLOCKS, left.shape[0] // BLOCKS, left.shape[1]) for left, _ in pairs]
    rights = [right for _, group in pairs for right in group]
    total = sum(right.shape[1] for right in rights)
    specs, operands = [], []
    for left in lefts:
        for slot in range(SLOTS):
            specs.append(
                pl.BlockSpec(
                    (1,) + left.shape[1:],
                    lambda step, spot, slot=slot: (
                        chunk_block(offset_of_step(offsets, step), slot, spot),
                        0,
                        0,
                    ),
                )
            )
            operands.append(left)
    specs += [pl.BlockSpec(right.shape, lambda step, spot: (0, 0)) for right in rights]
    specs += [pl.BlockSpec(part.shape, lambda step, spot: (0, 0)) for part in riders]
    rows = SLOTS * lefts[0].shape[1] + sum(part.shape[0] for part in riders)
    halves = [(slice(0, rows), slice(0, total // 2)), (slice(0, rows), slice(total // 2, total))]
    return chunk_call(
        functools.partial(make_rows, [len(group) for _, group in pairs]),
        operands + rights + list(riders),
        specs,
        offsets,
        halves,
        (rows, total),
        spot,
        extra,
        ties,
        "row_chunks",
        micros,
    )


def make_columns(lefts, inputs, slot, added, offset):
    whole = jnp.concatenate([right[...] for right in inputs[lefts:]], axis=1)
    row = 0
    for left in inputs[:lefts]:
        product = dot(left[...], whole)
        if added is not None and added[0][0].start == row:
            product = product + added[1][...].astype(jnp.float32)
        slot[row : row + left.shape[0], :] = product.astype(jnp.bfloat16)
        row += left.shape[0]


def column_chunks(lefts, right, offsets, spot, extra=(), ties=(), micros=0):
    rows = lefts[0].shape[0]
    depth, columns = right.shape
    specs = [pl.BlockSpec(left.shape, lambda step, spot: (0, 0)) for left in lefts]
    for slot in range(SLOTS):
        specs.append(
            pl.BlockSpec(
                (depth, columns // BLOCKS),
                lambda step, spot, slot=slot: (
                    0,
                    chunk_block(offset_of_step(offsets, step), slot, spot),
                ),
            )
        )
    lanes = columns // RING
    halves = [(slice(0, rows), slice(0, lanes)), (slice(rows, 2 * rows), slice(0, lanes))]
    return chunk_call(
        functools.partial(make_columns, len(lefts)),
        list(lefts) + [right] * SLOTS,
        specs,
        offsets,
        halves,
        (2 * rows, lanes),
        spot,
        extra,
        ties,
        "column_chunks",
        micros,
    )


def add_up(refs, index):
    total = refs[0][index].astype(jnp.float32)
    for ref in refs[1:]:
        total = total + ref[index].astype(jnp.float32)
    return total


def lane_slice(start, size):
    return (slice(None), pl.ds(pl.multiple_of(start * size, size), size))


def halving_places(spot):
    own = spot[2]
    other = own ^ 1
    return (own, RING - 1 - own), (other, RING - 1 - other)


def ffn_second_kernel(spot, *refs):
    parts = refs[:-2]
    for out, places in zip(refs[-2:], halving_places(spot)):
        for index, place in enumerate(places):
            for z in range(PAIR):
                out[index * PAIR + z] = add_up(parts, z * RING + place).astype(jnp.bfloat16)


def ffn_middle_kernel(kept, got, own, sent):
    for out, start in ((own, 0), (sent, PAIR)):
        for z in range(PAIR):
            out[z] = add_up((kept, got), start + z).astype(jnp.bfloat16)


def ffn_third_kernel(spot, *refs):
    for out, z in ((refs[-2], spot[1]), (refs[-1], (spot[1] + 1) % PAIR)):
        out[...] = add_up(refs[:-2], z).astype(jnp.bfloat16)


def ffn_last_kernel(kept, got, gate_out, up_out, down_out):
    total = kept[...].astype(jnp.float32) + got[...].astype(jnp.float32)
    hidden = gate_out.shape[1]
    gate_out[...] = total[:, :hidden]
    up_out[...] = total[:, hidden : 2 * hidden]
    down_out[...] = total[:, 2 * hidden :].T


def text_second_kernel(spot, *refs):
    parts = refs[:-2]
    lanes = parts[0].shape[1] // SLOTS
    for out, places in zip(refs[-2:], halving_places(spot)):
        for index, place in enumerate(places):
            for z in range(PAIR):
                start = (index * PAIR + z) * lanes
                out[:, start : start + lanes] = add_up(
                    parts, lane_slice(z * RING + place, lanes)
                ).astype(jnp.bfloat16)


def text_middle_kernel(kept, got, own, sent):
    wide = own.shape[1]
    for out, start in ((own, 0), (sent, wide)):
        index = (slice(None), slice(start, start + wide))
        out[...] = add_up((kept, got), index).astype(jnp.bfloat16)


def text_third_kernel(spot, *refs):
    lanes = refs[-1].shape[1]
    for out, z in ((refs[-2], spot[1]), (refs[-1], (spot[1] + 1) % PAIR)):
        out[...] = add_up(refs[:-2], lane_slice(z, lanes)).astype(jnp.bfloat16)


def text_last_kernel(kept, got, textkey, textvalue):
    total = kept[...].astype(jnp.float32) + got[...].astype(jnp.float32)
    columns = textkey.shape[1]
    textkey[...] = total[:columns].T
    textvalue[...] = total[columns:].T


def attn_second_kernel(rows, spot, riders, opposite, *refs):
    parts, outs = refs[:-RING], refs[-RING:]
    size = SLOTS * rows
    for offset in range(RING):
        for z in range(PAIR):
            slot = z * RING + (spot[2] + offset) % RING
            index = (pl.ds(pl.multiple_of(slot * rows, 16), rows), slice(None))
            outs[offset][z * rows : (z + 1) * rows, :] = add_up(parts, index).astype(jnp.bfloat16)
    pairs = ((riders[...], parts[1][size:, :]), (opposite[...], parts[2][size:, :]))
    joined = [merge_rows(PAIR, first, second, rider_rows(2 * PAIR)) for first, second in pairs]
    joined = merge_rows(2 * PAIR, joined[0], joined[1], rider_rows(4 * PAIR))
    for out in outs:
        out[PAIR * rows :, :] = joined


def attn_third_kernel(spot, *refs):
    rows = refs[-1].shape[0]
    for out, z in ((refs[-2], spot[1]), (refs[-1], (spot[1] + 1) % PAIR)):
        index = (pl.ds(pl.multiple_of(z * rows, 16), rows), slice(None))
        out[...] = add_up(refs[:RING], index).astype(jnp.bfloat16)


def attn_last_kernel(kept, got, query, key, value, outw):
    total = kept[...].astype(jnp.float32) + got[...].astype(jnp.float32)
    columns = query.shape[1]
    for place, out in enumerate((query, key, value)):
        out[...] = total[:, place * columns : (place + 1) * columns]
    outw[...] = total[:, 3 * columns :].T


def whole_call(kernel, scalars, operands, outs, name, ties=(), scratch=(), micros=0):
    whole = pl.BlockSpec(memory_space=pltpu.VMEM)
    count = len(scalars) + len(operands)
    return pl.pallas_call(
        lambda *refs: kernel(*refs[:count], *refs[count + len(ties) :]),
        in_specs=[pl.BlockSpec(memory_space=pltpu.SMEM)] * len(scalars)
        + [whole] * len(operands)
        + [pl.BlockSpec(memory_space=pl.ANY)] * len(ties),
        out_specs=[whole] * len(outs),
        out_shape=[jax.ShapeDtypeStruct(shape, kind) for shape, kind in outs],
        scratch_shapes=list(scratch),
        compiler_params=pltpu.CompilerParams(vmem_limit_bytes=VMEM_LIMIT),
        cost_estimate=cost_of(micros),
        name=name,
    )(*scalars, *operands, *ties)


def tiled_call(kernel, scalars, operands, outs, name, axis, tiles, ties=(), micros=0, axes=None):
    def spec(shape, axis):
        block = list(shape)
        block[axis] //= tiles
        if axis == 0:
            return pl.BlockSpec(tuple(block), lambda step: (step,) + (0,) * (len(shape) - 1))
        return pl.BlockSpec(tuple(block), lambda step: (0,) * (len(shape) - 1) + (step,))

    count = len(scalars) + len(operands)
    return pl.pallas_call(
        lambda *refs: kernel(*refs[:count], *refs[count + len(ties) :]),
        grid=(tiles,),
        in_specs=[pl.BlockSpec(memory_space=pltpu.SMEM)] * len(scalars)
        + [spec(part.shape, way) for part, way in zip(operands, axes or [axis] * len(operands))]
        + [pl.BlockSpec(memory_space=pl.ANY)] * len(ties),
        out_specs=[spec(shape, axis) for shape, _ in outs],
        out_shape=[jax.ShapeDtypeStruct(shape, kind) for shape, kind in outs],
        compiler_params=pltpu.CompilerParams(vmem_limit_bytes=VMEM_LIMIT),
        cost_estimate=cost_of(micros),
        name=name,
    )(*scalars, *[pltpu.with_memory_space_constraint(part, pltpu.HBM) for part in operands], *ties)


def exchange(chunks, axis):
    return [chunks[0]] + [
        dp_permute(chunks[step], axis, step) for step in range(1, len(chunks))
    ]


def one_on(halves):
    return dp_permute(halves[0], "first", 1), dp_permute(halves[1], "first", RING - 1)


def to_neighbours(own, ahead, behind):
    return [own, dp_permute(ahead, "first", 1), dp_permute(behind, "first", RING - 1)]


def by_slots(chunk):
    return chunk.reshape(SLOTS, chunk.shape[0] // SLOTS, chunk.shape[1])


def lane_index(shape):
    return lax.broadcasted_iota(jnp.int32, shape, 1)


def head_lanes(shape, head):
    lane = lane_index(shape)
    return (lane < HEAD) if head == 0 else (lane >= HEAD)


def per_head(values, reduce):
    first = head_lanes(values.shape, 0)
    left = jnp.sum(jnp.where(first, values, 0.0), axis=1, keepdims=True)
    right = jnp.sum(jnp.where(first, 0.0, values), axis=1, keepdims=True)
    return jnp.where(first, left, right)


def head_units(raw):
    inverse = lax.rsqrt(per_head(raw * raw, None) * (1.0 / HEAD) + EPS)
    return raw * inverse, inverse


def partner(values):
    lane = lane_index(values.shape)
    return jnp.where(
        lane % HEAD < HEAD // 2,
        pltpu.roll(values, LANES - HEAD // 2, 1),
        pltpu.roll(values, HEAD // 2, 1),
    )


def dot(left, right):
    return jnp.dot(left, right, preferred_element_type=jnp.float32)


def dot_t(left, right):
    return lax.dot_general(left, right, (((1,), (1,)), ((), ())), preferred_element_type=jnp.float32)


def attend_kernel(
    raw_q, raw_k, value, raw_t, text_value, cosine, sine, gains, gate, gate_swapped, mark_q, mark_k, mark_t,
    query_out, key_out, text_out, mixed_out, self_out, cross_out, self_log, cross_log,
):
    cos, sin = cosine[...], sine[...]
    unit = head_units(raw_q[...])[0] * gains[0:1, :]
    query = ((unit * cos + partner(unit) * sin).astype(jnp.bfloat16) * ROOT).astype(jnp.bfloat16)
    unit = head_units(raw_k[...])[0] * gains[1:2, :]
    key = (unit * cos + partner(unit) * sin).astype(jnp.bfloat16)
    text = (head_units(raw_t[...])[0] * gains[2:3, :]).astype(jnp.bfloat16)
    query_out[...] = query
    key_out[...] = key
    text_out[...] = text

    def attention(keys, marks, values):
        outs, sums = [], []
        for head in range(2):
            own = head_lanes(query.shape, head)
            own_keys = head_lanes(keys.shape, head)
            probe = jnp.where(own, query, mark_q[...])
            scores = dot_t(probe, jnp.where(own_keys, keys, marks))
            weights = jnp.exp(scores).astype(jnp.bfloat16)
            both = dot(weights, jnp.where(own_keys, values, jnp.ones_like(values)))
            outs.append(both)
        first = head_lanes(outs[0].shape, 0)
        product = jnp.where(first, outs[0], outs[1])
        total = jnp.where(first, outs[1], outs[0])
        return product / pltpu.roll(total, HEAD, 1), jnp.log(total)

    out, log = attention(key, mark_k[...], value[...])
    self_out[...] = out
    self_log[...] = log
    cross, log = attention(text, mark_t[...], text_value[...])
    cross_out[...] = cross
    cross_log[...] = log - jnp.log(gate_swapped[...])
    mixed_out[...] = (out + gate[...] * cross).astype(jnp.bfloat16)


def attention_grads(query, keys, marks, values, grad, out, log, mark_q):
    rows = grad.astype(jnp.float32)
    delta = per_head(rows * out, None)
    delta = pltpu.roll(delta, HEAD, 1)
    lane = lane_index(query.shape) % HEAD
    log_high = log.astype(jnp.bfloat16)
    log_low = (log - log_high.astype(jnp.float32)).astype(jnp.bfloat16)
    delta_high = delta.astype(jnp.bfloat16)
    delta_low = (delta - delta_high.astype(jnp.float32)).astype(jnp.bfloat16)
    zero = jnp.zeros_like(query)
    code = jnp.where(lane == 4, -log_high, jnp.where(lane == 5, -log_low, mark_q))
    shift = jnp.where(lane == 4, -delta_high, jnp.where(lane == 5, -delta_low, zero))
    key_grads, value_grads, query_grads = [], [], []
    for head in range(2):
        own = head_lanes(query.shape, head)
        own_keys = head_lanes(keys.shape, head)
        probe = jnp.where(own, query, code)
        probs = jnp.exp(dot_t(jnp.where(own_keys, keys, marks), probe))
        slope = dot_t(jnp.where(own_keys, values, marks), jnp.where(own, grad, shift))
        score_grad = (probs * slope).astype(jnp.bfloat16)
        value_grads.append(dot(probs.astype(jnp.bfloat16), grad))
        key_grads.append(dot(score_grad, query))
        turned = keys[:, head * HEAD : (head + 1) * HEAD].T
        query_grads.append(dot(turned, score_grad))
    first = head_lanes(keys.shape, 0)
    return (
        jnp.concatenate(query_grads, axis=0),
        jnp.where(first, key_grads[0], key_grads[1]),
        jnp.where(first, value_grads[0], value_grads[1]),
    )


def norm_back(weighted, unit, inverse):
    return inverse * (weighted - unit * (per_head(weighted * unit, None) * (1.0 / HEAD)))


def cross_back_kernel(
    query, text, text_value, raw_t, grad, out, log, gains, mark_q, mark_t,
    query_grad, raw_grad, value_grad, gain_sum, gate_sum,
):
    grad_q, grad_t, grad_v = attention_grads(
        query[...], text[...], mark_t[...], text_value[...], grad[...], out[...], log[...], mark_q[...]
    )
    query_grad[...] = grad_q.T
    value_grad[...] = grad_v.astype(jnp.bfloat16).T
    grad_t = grad_t.astype(jnp.bfloat16).astype(jnp.float32)
    unit, inverse = head_units(raw_t[...])
    gain_sum[...] = jnp.sum(grad_t * unit, axis=0, keepdims=True)
    raw_grad[...] = norm_back(grad_t * gains[2:3, :], unit, inverse).astype(jnp.bfloat16).T
    gate_sum[...] = jnp.sum(grad[...].astype(jnp.float32) * out[...], axis=0, keepdims=True)


def self_back_kernel(
    query, key, value, raw_q, raw_k, grad, out, log, cross_grad, cosine, sine, gains, mark_q, mark_k,
    query_grad, key_grad, value_grad, gain_sum,
):
    grad_q, grad_k, grad_v = attention_grads(
        query[...], key[...], mark_k[...], value[...], grad[...], out[...], log[...], mark_q[...]
    )
    value_grad[...] = grad_v.astype(jnp.bfloat16)
    cos, sin = cosine[...], sine[...]
    grad_q = (grad_q.T + cross_grad[...]) * ROOT
    for turn, raw, row, target in ((grad_q, raw_q, 0, query_grad), (grad_k, raw_k, 1, key_grad)):
        turn = turn.astype(jnp.bfloat16).astype(jnp.float32)
        turn = turn * cos - partner(turn) * sin
        unit, inverse = head_units(raw[...])
        gain_sum[row : row + 1, :] = jnp.sum(turn * unit, axis=0, keepdims=True)
        target[...] = norm_back(turn * gains[row : row + 1, :], unit, inverse).astype(jnp.bfloat16)


def pair_call(kernel, operands, outs, name, ties=(), micros=0):
    def spec(shape, cut):
        if cut is None:
            return pl.BlockSpec(shape, lambda pair: (0, 0))
        if cut == 1:
            return pl.BlockSpec((shape[0], LANES), lambda pair: (0, pair))
        return pl.BlockSpec((LANES, shape[1]), lambda pair: (pair, 0))

    width = outs[0][0][0] if outs[0][2] == 0 else outs[0][0][1]
    return pl.pallas_call(
        lambda *refs: kernel(*refs[: len(operands)], *refs[len(operands) + len(ties) :]),
        grid=(width // LANES,),
        in_specs=[spec(part.shape, cut) for part, cut in operands]
        + [pl.BlockSpec(memory_space=pl.ANY)] * len(ties),
        out_specs=[spec(shape, cut) for shape, _, cut in outs],
        out_shape=[jax.ShapeDtypeStruct(shape, kind) for shape, kind, _ in outs],
        compiler_params=pltpu.CompilerParams(vmem_limit_bytes=VMEM_LIMIT),
        cost_estimate=cost_of(micros),
        name=name,
    )(*[part for part, _ in operands], *ties)
def inverse_rms(values):
    return lax.rsqrt(jnp.mean(values * values, axis=-1, keepdims=True) + EPS)


def row_norm_back(weighted, unit, inverse):
    return inverse * (weighted - unit * jnp.mean(weighted * unit, axis=-1, keepdims=True))


def per_row(table, segment):
    return jnp.where(segment == 0.0, table[0:1], jnp.where(segment == 1.0, table[1:2], table[2:3]))


def total_of(parts):
    upper, near, far = parts
    rows = far.shape[0]
    return (
        upper[:rows].astype(jnp.float32) + near[:rows].astype(jnp.float32) + far[...].astype(jnp.float32)
    )


def segment_sums(member, values):
    high = values.astype(jnp.bfloat16)
    low = (values - high.astype(jnp.float32)).astype(jnp.bfloat16)
    return dot(member, high) + dot(member, low)


def tables_kernel(here, lens, gate, segments, head_gains, cosine, sine, mark_q, mark_k, mark_t,
                  segment, member, gate_lanes, gate_swapped, gains):
    heads = gains.shape[1] // HEAD
    lane = lane_index(gate_lanes.shape) // HEAD
    line = jnp.zeros(gate_lanes.shape, jnp.float32)
    swapped = line
    for head in range(heads):
        line = jnp.where(lane == head, gate[head], line)
        swapped = jnp.where(lane == head ^ 1, gate[head], swapped)
    gate_lanes[...] = jnp.tanh(line)
    gate_swapped[...] = jnp.tanh(swapped)
    gains[...] = jnp.concatenate([head_gains[...]] * heads, axis=1)
    rows = segments.shape[1]
    ids = segments[...]
    first = jnp.sum((ids < 1).astype(jnp.float32))
    second = jnp.sum((ids < 2).astype(jnp.float32))
    lane = lane_index((rows, LANES))
    half = HEAD // 2
    rate = jnp.exp((lane % half).astype(jnp.float32) * (-2.0 * math.log(10000.0) / HEAD))
    within = lane % HEAD
    for block, code in enumerate(ROW_ORDER):
        source = here[0] ^ code
        line = segments[pl.ds(source, 1), :].astype(jnp.float32)
        label = jnp.broadcast_to(line, (rows, rows)).T
        start = jnp.where(label == 0.0, 0.0, jnp.where(label == 1.0, first, second))
        token = (lax.broadcasted_iota(jnp.int32, (rows, LANES), 0) + source * rows).astype(jnp.float32)
        angle = (token - start) * rate
        index = slice(block * rows, (block + 1) * rows)
        cosine[index, :] = jnp.cos(angle)
        sine[index, :] = jnp.where(within < half, -1.0, 1.0) * jnp.sin(angle)
        same = ((label == within.astype(jnp.float32)) & (within < SEGS)).astype(jnp.float32)
        shut = (within == SEGS).astype(jnp.float32)
        ones = ((within >= SEGS) & (within < SEGS + 3)).astype(jnp.float32)
        mark_q[index, :] = (SHUT * same - SHUT * shut).astype(jnp.bfloat16)
        mark_k[index, :] = (same + ones).astype(jnp.bfloat16)
        if block == 0:
            segment[...] = label
            member[...] = (
                lax.broadcasted_iota(jnp.int32, (8, rows), 0).astype(jnp.float32) == line
            ).astype(jnp.bfloat16)
    for group in range(SEGS):
        lane = lane_index((TXT, LANES)) % HEAD
        row = lax.broadcasted_iota(jnp.int32, (TXT, LANES), 0)
        inside = ((lane == group) & (row < lens[group])).astype(jnp.float32)
        ones = ((lane >= SEGS) & (lane < SEGS + 3)).astype(jnp.float32)
        mark_t[group * TXT : (group + 1) * TXT, :] = (inside + ones).astype(jnp.bfloat16)


def text_kernel(captions, key_weight, value_weight, raw_out, value_out, raw_sum, value_sum):
    step = pl.program_id(0)

    @pl.when(step == 0)
    def _():
        raw_sum[...] = dot(captions[...], key_weight[...])
        value_sum[...] = dot(captions[...], value_weight[...])

    @pl.when(step > 0)
    def _():
        raw_sum[...] += dot(captions[...], key_weight[...])
        value_sum[...] += dot(captions[...], value_weight[...])

    @pl.when(step == pl.num_programs(0) - 1)
    def _():
        raw_out[...] = raw_sum[...]
        value_out[...] = value_sum[...].astype(jnp.bfloat16)


def text_call(captions, key_weight, value_weight):
    rows, depth = captions.shape
    columns = key_weight.shape[1]
    tile = depth // 4
    return pl.pallas_call(
        text_kernel,
        grid=(depth // tile,),
        in_specs=[
            pl.BlockSpec((rows, tile), lambda step: (0, step)),
            pl.BlockSpec((tile, columns), lambda step: (step, 0)),
            pl.BlockSpec((tile, columns), lambda step: (step, 0)),
        ],
        out_specs=[pl.BlockSpec((rows, columns), lambda step: (0, 0))] * 2,
        out_shape=[
            jax.ShapeDtypeStruct((rows, columns), jnp.float32),
            jax.ShapeDtypeStruct((rows, columns), jnp.bfloat16),
        ],
        scratch_shapes=[pltpu.VMEM((rows, columns), jnp.float32)] * 2,
        compiler_params=pltpu.CompilerParams(vmem_limit_bytes=VMEM_LIMIT),
        cost_estimate=cost_of(9),
        name="text",
    )(*[pltpu.with_memory_space_constraint(part, pltpu.HBM) for part in (captions, key_weight, value_weight)])


def project_kernel(here, own, far, near, last, mods, gains, segment_q, query_w, key_w, value_w,
                   rows_out, raw_q, raw_k, value):
    table = mods[here[0]]
    rows = own.shape[0]
    for block, part in enumerate((own, far, near, last)):
        index = slice(block * rows, (block + 1) * rows)
        values = part[...].astype(jnp.float32)
        marks = segment_q[index, :].astype(jnp.float32)
        scale = jnp.where(
            marks[:, 0:1] > 0.0, table[0:1], jnp.where(marks[:, 1:2] > 0.0, table[1:2], table[2:3])
        )
        rows_out[index, :] = (
            values * inverse_rms(values) * gains[0:1] * (1.0 + scale)
        ).astype(jnp.bfloat16)
    raw_q[...] = dot(rows_out[...], query_w[...])
    raw_k[...] = dot(rows_out[...], key_w[...])
    value[...] = dot(rows_out[...], value_w[...]).astype(jnp.bfloat16)


def middle_kernel(here, block, upper, near, far, mods, gains, segment, attn_out, middle_out, rows_out):
    attn_sum = total_of((upper, near, far))
    label = segment[:, 0:1]
    factor = jnp.tanh(per_row(mods[here[0] ^ 1], label)) * gains[1:2]
    middle = block[...].astype(jnp.float32) + factor * (attn_sum * inverse_rms(attn_sum))
    attn_out[...] = attn_sum
    middle_out[...] = middle
    scale = per_row(mods[here[0] ^ 2], label)
    rows_out[...] = (middle * inverse_rms(middle) * gains[2:3] * (1.0 + scale)).astype(jnp.bfloat16)


def block_out_kernel(here, middle, upper, near, far, grad, mods, gains, segment, member,
                     block_out, grad_out, sums):
    ffn_sum = total_of((upper, near, far))
    inverse = inverse_rms(ffn_sum)
    unit = ffn_sum * inverse
    factor = jnp.tanh(per_row(mods[here[0] ^ 3], segment[:, 0:1])) * gains[3:4]
    block_out[...] = (middle[...] + factor * unit).astype(jnp.bfloat16)
    incoming = grad[...].astype(jnp.float32)
    grad_out[...] = row_norm_back(incoming * factor, unit, inverse).astype(jnp.bfloat16)
    sums[...] = segment_sums(member[...], incoming * unit)


def middle_back_kernel(here, middle, attn, upper, near, far, grad, mods, gains, segment, member,
                       middle_grad, attn_grad, ffn_sums, attn_sums):
    grad_in = total_of((upper, near, far))
    label = segment[:, 0:1]
    inverse = inverse_rms(middle[...])
    unit = middle[...] * inverse
    factor = gains[2:3] * (1.0 + per_row(mods[here[0] ^ 2], label))
    ffn_sums[...] = segment_sums(member[...], grad_in * unit)
    grad_middle = grad[...].astype(jnp.float32) + row_norm_back(grad_in * factor, unit, inverse)
    middle_grad[...] = grad_middle
    inverse = inverse_rms(attn[...])
    unit = attn[...] * inverse
    factor = jnp.tanh(per_row(mods[here[0] ^ 1], label)) * gains[1:2]
    attn_grad[...] = row_norm_back(grad_middle * factor, unit, inverse).astype(jnp.bfloat16)
    attn_sums[...] = segment_sums(member[...], grad_middle * unit)


def block_in_kernel(here, block, middle_grad, upper, near, far, mods, gains, segment, member,
                    in_grad, sums):
    grad_in = total_of((upper, near, far))
    values = block[...].astype(jnp.float32)
    inverse = inverse_rms(values)
    unit = values * inverse
    factor = gains[0:1] * (1.0 + per_row(mods[here[0]], segment[:, 0:1]))
    in_grad[...] = (
        middle_grad[...] + row_norm_back(grad_in * factor, unit, inverse)
    ).astype(jnp.bfloat16)
    sums[...] = segment_sums(member[...], grad_in * unit)


def stack_sums_kernel(here, first, second, third, fourth, head_gain, text_gain, gate_sum, gate, out):
    width = out.shape[1]
    heads = jnp.concatenate([head_gain[0:1], head_gain[1:2], text_gain[...]], axis=1)
    inner = heads.shape[1] // 3
    gates = gate_sum[...] * (1.0 - gate[...] * gate[...])
    gates = jnp.concatenate([gates, jnp.zeros((1, width - inner), jnp.float32)], axis=1)
    lane = lane_index(gates.shape)
    moved = jnp.zeros_like(gates)
    for position in range(4):
        turn = pltpu.roll(gates, position * inner, 1) if position else gates
        moved = jnp.where((lane // inner == position) & (here[0] == position), turn, moved)
    out[...] = jnp.concatenate(
        [part[0:SEGS] for part in (first, second, third, fourth)]
        + [
            jnp.concatenate([heads, jnp.zeros((1, width - 3 * inner), jnp.float32)], axis=1),
            moved,
            jnp.zeros((2, width), jnp.float32),
        ],
        axis=0,
    )


def pack_kernel(here, own, far, near, last, mods, gains, cond, packed):
    total = own[...] + far[...] + near[...] + last[...]
    grad = jnp.zeros((SEGS, total.shape[1]), jnp.float32)
    rows = []
    for name in range(4):
        part = total[name * SEGS : (name + 1) * SEGS]
        mod = mods[here[0] ^ name]
        gain = gains[name : name + 1]
        if name % 2 == 1:
            factor = jnp.tanh(mod)
            slope = 1.0 - factor * factor
        else:
            factor = 1.0 + mod
            slope = jnp.ones_like(mod)
        rows.append(jnp.sum(part * factor, axis=0, keepdims=True))
        mine = (jnp.zeros(part.shape, jnp.int32) + here[0]) == name
        grad = jnp.where(mine, part * slope * gain, grad)
    rows.append(total[4 * SEGS : 4 * SEGS + 2])
    rows = jnp.concatenate(rows, axis=0)
    high = rows.astype(jnp.bfloat16).astype(jnp.float32)
    pad = jnp.zeros((packed.shape[0] - 2 * SEGS - 2 * SUM_ROWS, total.shape[1]), jnp.float32)
    packed[...] = jnp.concatenate(
        [grad, cond[...].astype(jnp.float32), high, rows - high, pad], axis=0
    ).astype(jnp.bfloat16)


def rider_rows(count):
    return -(-(2 * SEGS * count + 2 * SUM_ROWS) // 16) * 16


def merge_rows(count, first, second, size):
    first, second = first.astype(jnp.float32), second.astype(jnp.float32)
    wide = SEGS * count
    start = 2 * wide
    sums = (
        first[start : start + SUM_ROWS]
        + first[start + SUM_ROWS : start + 2 * SUM_ROWS]
        + second[start : start + SUM_ROWS]
        + second[start + SUM_ROWS : start + 2 * SUM_ROWS]
    )
    high = sums.astype(jnp.bfloat16).astype(jnp.float32)
    pieces = [first[:wide], second[:wide], first[wide:start], second[wide:start], high, sums - high]
    rest = size - 4 * wide - 2 * SUM_ROWS
    if rest:
        pieces.append(jnp.zeros((rest, first.shape[1]), jnp.float32))
    return jnp.concatenate(pieces, axis=0).astype(jnp.bfloat16)


def merge_kernel(count, ours, theirs, out):
    out[...] = merge_rows(count, ours[...], theirs[...], out.shape[0])


def ada_kernel(count, heads, dp, own, *refs):
    parts = (own,) + refs[:3]
    ada_out, norm_out, head_out, gate_out = refs[3:]
    wide = SEGS * count
    base = own.shape[0] - rider_rows(count)
    columns = ada_out.shape[0]
    share = LANES // columns
    start = pl.multiple_of(dp[0] // share * LANES, LANES)
    grads, conds = [], []
    sums = jnp.zeros((SUM_ROWS, own.shape[1]), jnp.float32)
    for part in parts:
        rows = part[base:, :].astype(jnp.float32)
        grads.append(rows[:wide])
        conds.append(part[base:, pl.ds(start, LANES)].astype(jnp.float32)[wide : 2 * wide])
        for half in range(2):
            place = 2 * wide + half * SUM_ROWS
            sums = sums + rows[place : place + SUM_ROWS]
    conds = jnp.concatenate(conds, axis=0)
    conds = pltpu.roll(conds, (LANES - dp[0] % share * columns) % LANES, 1)
    acts = conds / (1.0 + jnp.exp(-conds))
    ada_out[...] = dot(
        acts.astype(jnp.bfloat16).astype(jnp.float32).T.astype(jnp.bfloat16),
        jnp.concatenate(grads, axis=0).astype(jnp.bfloat16),
    )[:columns]
    norm_out[...] = sums[:4]
    inner = heads * HEAD
    for row in range(3):
        line = jnp.zeros((1, HEAD), jnp.float32)
        for head in range(heads):
            place = row * inner + head * HEAD
            line = line + sums[4:5, place : place + HEAD]
        head_out[row : row + 1, :] = line
    lane = lane_index((1, LANES))
    line = jnp.zeros((1, LANES), jnp.float32)
    for head in range(HEADS):
        value = jnp.sum(sums[5:6, head * HEAD : (head + 1) * HEAD], axis=1, keepdims=True)
        line = jnp.where(lane == head, value, line)
    gate_out[...] = line


def back_kernel(count, *refs):
    grads, weights, upper, lower = refs[:count], refs[count : 2 * count], refs[-2], refs[-1]
    total = dot_t(grads[0][...], weights[0][...])
    for grad, weight in zip(grads[1:], weights[1:]):
        total = total + dot_t(grad[...], weight[...])
    half = upper.shape[0]
    upper[...] = total[:half].astype(jnp.bfloat16)
    lower[...] = total[half:].astype(jnp.bfloat16)


def back_call(grads, weights, name, ties=(), micros=0):
    rows, inner = grads[0].shape
    columns = weights[0].shape[0]
    tile = columns // 3
    return pl.pallas_call(
        lambda *refs: back_kernel(len(grads), *refs[: 2 * len(grads)], *refs[-2:]),
        grid=(columns // tile,),
        in_specs=[pl.BlockSpec((rows, inner), lambda step: (0, 0))] * len(grads)
        + [pl.BlockSpec((tile, inner), lambda step: (step, 0))] * len(grads)
        + [pl.BlockSpec(memory_space=pl.ANY)] * len(ties),
        out_specs=[pl.BlockSpec((rows // 2, tile), lambda step: (0, step))] * 2,
        out_shape=[jax.ShapeDtypeStruct((rows // 2, columns), jnp.bfloat16)] * 2,
        compiler_params=pltpu.CompilerParams(vmem_limit_bytes=VMEM_LIMIT),
        cost_estimate=cost_of(micros),
        name=name,
    )(*grads, *weights, *ties)


def shards(
    block_in,
    out_grad,
    condition,
    captions,
    caption_len,
    segment_ids,
    ada_weight,
    norm_gains,
    query_weight,
    key_weight,
    value_weight,
    head_gains,
    textkey_weight,
    textvalue_weight,
    cross_gate,
    out_weight,
    gate_weight,
    up_weight,
    down_weight,
):
    rows, width = block_in.shape
    length = segment_ids.shape[0]
    heads = cross_gate.shape[0]
    inner = heads * HEAD
    half_rows = length // 2
    position = lax.axis_index("tensor")
    spot = dp_spot(position)
    here = position.reshape(1)
    b16, f32 = jnp.bfloat16, jnp.float32

    blocks = gather_tensor(block_in)
    cond_rows = jnp.pad(condition, ((0, 0), (0, width - condition.shape[1])))
    own_act = jax.nn.silu(condition.astype(f32)).astype(b16)
    own_part = jnp.dot(own_act, ada_weight, preferred_element_type=f32)
    parts = gather_tensor(own_part)
    mods = jnp.stack([parts[ROW_ORDER.index(code)] for code in range(4)])

    cosine, sine, mark_q, mark_k, mark_t, segment, member, gate_lanes, gate_swapped, gains = whole_call(
        tables_kernel,
        (here, caption_len, cross_gate),
        [segment_ids.reshape(length // rows, rows), head_gains],
        [((length, LANES), f32)] * 2
        + [((length, LANES), b16)] * 2
        + [((SEGS * TXT, LANES), b16), ((rows, LANES), f32), ((8, rows), b16)]
        + [((1, inner), f32)] * 2
        + [((3, inner), f32)],
        "tables",
        micros=2,
    )
    caption_flat = captions.reshape(-1, captions.shape[-1])
    texts = caption_flat.shape[0]
    raw_t, text_value = text_call(caption_flat, textkey_weight, textvalue_weight)
    attn_rows, raw_q, raw_k, value = whole_call(
        project_kernel,
        (here,),
        blocks + [mods, norm_gains, mark_q, query_weight, key_weight, value_weight],
        [((length, width), b16), ((length, inner), f32), ((length, inner), f32), ((length, inner), b16)],
        "project",
        micros=6,
    )
    query, key, text, mixed, self_out, cross_out, self_log, cross_log = pair_call(
        attend_kernel,
        [(raw_q, 1), (raw_k, 1), (value, 1), (raw_t, 1), (text_value, 1), (cosine, None), (sine, None)]
        + [(gains, 1), (gate_lanes, 1), (gate_swapped, 1), (mark_q, None), (mark_k, None), (mark_t, None)],
        [((length, inner), b16, 1)] * 2
        + [((texts, inner), b16, 1), ((length, inner), b16, 1)]
        + [((length, inner), f32, 1)] * 4,
        "attend",
        micros=11,
    )

    def halves(product):
        return product(slice(0, half_rows)).astype(b16), product(slice(half_rows, None)).astype(b16)

    def all_of(block):
        return jnp.concatenate(gather_tensor(block), axis=0)

    upper, lower = halves(lambda part: jnp.dot(mixed[part], out_weight, preferred_element_type=f32))
    sums, sent = scatter_tensor(upper, lower)
    attn_rows_t = turned(attn_rows, (sent,))
    wide = ((rows, width), f32)
    narrow = ((rows, width), b16)
    totals = ((8, width), f32)
    attn_sum, middle, ffn_own = whole_call(
        middle_kernel,
        (here,),
        [block_in] + sums + [mods, norm_gains, segment],
        [wide, wide, narrow],
        "middle",
    )
    ffn_rows = all_of(ffn_own)
    gate_pre = jnp.dot(ffn_rows, gate_weight, preferred_element_type=f32)
    up_pre = jnp.dot(ffn_rows, up_weight, preferred_element_type=f32)
    sigmoid_gate = jax.nn.sigmoid(gate_pre)
    silu_gate = gate_pre * sigmoid_gate
    hidden = (silu_gate * up_pre).astype(b16)
    upper, lower = halves(lambda part: jnp.dot(hidden[part], down_weight, preferred_element_type=f32))
    sums, sent = scatter_tensor(upper, lower)
    ffn_rows_t = turned(ffn_rows, (sent,))
    block_out, grad_own, sum_gate_ffn = whole_call(
        block_out_kernel,
        (here,),
        [middle] + sums + [out_grad, mods, norm_gains, segment, member],
        [narrow, narrow, totals],
        "block_out",
    )

    grad_ffn = all_of(grad_own)
    grad_hidden = times_transpose(grad_ffn, down_weight)
    grad_gate = (
        grad_hidden * up_pre * sigmoid_gate * (1.0 + gate_pre * (1.0 - sigmoid_gate))
    ).astype(b16)
    grad_up = (grad_hidden * silu_gate).astype(b16)
    upper, lower = halves(
        lambda part: times_transpose(grad_gate[part], gate_weight)
        + times_transpose(grad_up[part], up_weight)
    )
    sums, sent = scatter_tensor(upper, lower)
    grad_ffn_t = turned(grad_ffn, (sent,))
    ffn_pairs = [(ffn_rows_t, [grad_gate, grad_up]), (grad_ffn_t, [hidden])]
    (halves_two,) = row_chunks(ffn_pairs, (2,), spot, ties=(sent,), micros=FFN_MICROS)
    ffn_passed = one_on(halves_two)
    grad_middle, grad_own, sum_scale_ffn, sum_gate_attn = whole_call(
        middle_back_kernel,
        (here,),
        [middle, attn_sum] + sums + [out_grad, mods, norm_gains, segment, member],
        [wide, narrow, totals, totals],
        "middle_back",
        micros=MIDDLE_MICROS,
    )

    grad_attn = all_of(grad_own)
    grad_mixed = times_transpose(grad_attn, out_weight).astype(b16)
    cross_grad, text_grad, text_value_grad, text_gain, gate_sum = pair_call(
        cross_back_kernel,
        [(query, 1), (text, 1), (text_value, 1), (raw_t, 1), (grad_mixed, 1), (cross_out, 1)]
        + [(cross_log, 1), (gains, 1), (mark_q, None), (mark_t, None)],
        [((length, inner), f32, 1), ((inner, texts), b16, 0), ((inner, texts), b16, 0)]
        + [((1, inner), f32, 1)] * 2,
        "cross_back",
        micros=CROSS_MICROS,
    )
    ffn_one, ffn_three, ffn_kept = row_chunks(
        ffn_pairs, (1, 3, 0), spot, extra=ffn_passed, ties=(text_grad,), micros=FFN_NEXT_MICROS
    )
    text_lefts = [text_grad, text_value_grad]
    (halves_two,) = column_chunks(text_lefts, caption_flat, (2,), spot, ties=(ffn_kept,))
    text_passed = one_on(halves_two)
    query_grad, key_grad, value_grad, head_gain = pair_call(
        self_back_kernel,
        [(query, 1), (key, 1), (value, 1), (raw_q, 1), (raw_k, 1), (grad_mixed, 1), (self_out, 1)]
        + [(self_log, 1), (cross_grad, 1), (cosine, None), (sine, None), (gains, 1)]
        + [(mark_q, None), (mark_k, None)],
        [((length, inner), b16, 1)] * 3 + [((2, inner), f32, 1)],
        "self_back",
        (halves_two[0],),
        micros=SELF_MICROS,
    )

    hidden_cols = hidden.shape[1]
    block_rows = width // BLOCKS
    got = [by_slots(part) for part in to_neighbours(ffn_kept, ffn_one, ffn_three)]
    shape = (PAIR, block_rows, 3 * hidden_cols)
    ffn_kept, ffn_sent = tiled_call(
        ffn_second_kernel,
        (spot,),
        got,
        [((2 * PAIR,) + shape[1:], b16)] * 2,
        "ffn_second",
        -1,
        4,
        (query_grad,),
    )
    upper, lower = back_call(
        [query_grad, key_grad, value_grad], [query_weight, key_weight, value_weight], "attn_back"
    )
    sums, sent = scatter_tensor(upper, lower)
    in_grad, sum_scale_attn = whole_call(
        block_in_kernel,
        (here,),
        [block_in, grad_middle] + sums + [mods, norm_gains, segment, member],
        [narrow, totals],
        "block_in",
        (ffn_sent,),
        micros=BLOCK_IN_MICROS,
    )
    (stacked,) = whole_call(
        stack_sums_kernel,
        (here,),
        [sum_scale_attn, sum_gate_attn, sum_scale_ffn, sum_gate_ffn]
        + [head_gain, text_gain, gate_sum, gate_lanes],
        [((16, width), f32)],
        "stack_sums",
    )
    attn_pairs = [
        (attn_rows_t, [query_grad, key_grad, value_grad]),
        (turned(grad_attn, (halves_two[0],)), [mixed]),
    ]
    (halves_two,) = row_chunks(attn_pairs, (2,), spot, ties=(stacked,), micros=ATTN_FIRST_MICROS)
    attn_passed = one_on(halves_two)
    stacked = gather_tensor(stacked)
    text_one, text_three, text_kept = column_chunks(
        text_lefts, caption_flat, (1, 3, 0), spot, extra=text_passed, ties=(halves_two[0],), micros=TEXT_MICROS
    )
    ffn_own, ffn_sent = tiled_call(
        ffn_middle_kernel,
        (),
        [ffn_kept, dp_permute(ffn_sent, "second", "flip")],
        [(shape, b16)] * 2,
        "ffn_middle",
        -1,
        2,
        (text_kept,),
    )
    (riders,) = whole_call(
        pack_kernel,
        (here,),
        stacked + [mods, norm_gains, cond_rows],
        [((rider_rows(1), width), b16)],
        "pack",
        (ffn_sent,),
        micros=PACK_MICROS,
    )
    (riders,) = whole_call(
        functools.partial(merge_kernel, 1),
        (),
        [riders, dp_permute(riders, "z", 1)],
        [((rider_rows(PAIR), width), b16)],
        "merge",
    )
    opposite = dp_permute(riders, "first", 2)
    attn_one, attn_three, attn_kept = row_chunks(
        attn_pairs, (1, 3, 0), spot, extra=attn_passed, riders=(riders,), ties=(text_kept,), micros=ATTN_MICROS
    )
    text_rows = caption_flat.shape[1] // BLOCKS
    text_own, text_sent = tiled_call(
        text_second_kernel,
        (spot,),
        to_neighbours(text_kept, text_one, text_three),
        [((2 * inner, 2 * PAIR * text_rows), b16)] * 2,
        "text_second",
        0,
        4,
        (opposite,),
        micros=SECOND_MICROS,
    )
    stage = tiled_call(
        functools.partial(attn_second_kernel, block_rows),
        (spot,),
        [riders, opposite] + to_neighbours(attn_kept, attn_one, attn_three),
        [((PAIR * block_rows + rider_rows(4 * PAIR), width), b16)] * RING,
        "attn_second",
        -1,
        4,
        (text_sent,),
    )
    ffn_own_kept, ffn_own_sent = tiled_call(
        ffn_third_kernel,
        (spot,),
        [ffn_own, dp_permute(ffn_sent, "second", "mirror")],
        [(shape[1:], b16)] * 2,
        "ffn_third",
        -1,
        2,
        (stage[0],),
    )
    text_own, text_sent = tiled_call(
        text_middle_kernel,
        (),
        [text_own, dp_permute(text_sent, "second", "flip")],
        [((2 * inner, PAIR * text_rows), b16)] * 2,
        "text_middle",
        0,
        2,
        (stage[0],),
    )
    got = exchange(stage, "second")
    kept, sent = tiled_call(
        attn_third_kernel, (spot,), got, [((block_rows, width), b16)] * 2, "attn_third",
        -1,
        2
    )
    gate_sum_out, up_sum_out, down_sum_out = whole_call(
        ffn_last_kernel,
        (),
        exchange([ffn_own_kept, ffn_own_sent], "z"),
        [((block_rows, hidden_cols), f32)] * 2 + [((hidden_cols, block_rows), f32)],
        "ffn_last",
        (kept,),
    )
    text_own_kept, text_own_sent = tiled_call(
        text_third_kernel,
        (spot,),
        [text_own, dp_permute(text_sent, "second", "mirror")],
        [((2 * inner, text_rows), b16)] * 2,
        "text_third",
        0,
        2,
        (kept,),
    )
    textkey_sum, textvalue_sum = whole_call(
        text_last_kernel,
        (),
        exchange([text_own_kept, text_own_sent], "z"),
        [((text_rows, inner), f32)] * 2,
        "text_last",
    )
    ada_grad, norm_grads, head_grads, crossgate = tiled_call(
        functools.partial(ada_kernel, 4 * PAIR, heads),
        (lax.axis_index("dp").reshape(1),),
        got,
        [((condition.shape[1] // BLOCKS, width), f32), ((4, width), f32), ((3, HEAD), f32)]
        + [((1, LANES), f32)],
        "ada",
        0,
        1,
        (kept,),
    )
    crossgate_grad = crossgate[0, :HEADS]
    query_sum, key_sum, value_sum, outw_sum = whole_call(
        attn_last_kernel,
        (),
        exchange([kept, sent], "z"),
        [((block_rows, inner), f32)] * 3 + [((inner, block_rows), f32)],
        "attn_last",
    )
    return (
        block_out,
        in_grad,
        ada_grad,
        norm_grads,
        query_sum,
        key_sum,
        value_sum,
        head_grads,
        textkey_sum,
        textvalue_sum,
        crossgate_grad,
        outw_sum,
        gate_sum_out,
        up_sum_out,
        down_sum_out,
    )


def solution(mesh):
    return jax.shard_map(
        shards,
        mesh=mesh,
        in_specs=(
            P(("dp", "tensor"), None),
            P(("dp", "tensor"), None),
            P("dp", None),
            P("dp", None, None),
            P("dp"),
            P("dp"),
            P(None, "tensor"),
            P(),
            P(None, "tensor"),
            P(None, "tensor"),
            P(None, "tensor"),
            P(),
            P(None, "tensor"),
            P(None, "tensor"),
            P("tensor"),
            P("tensor", None),
            P(None, "tensor"),
            P(None, "tensor"),
            P("tensor", None),
        ),
        out_specs=(
            P(("dp", "tensor"), None),
            P(("dp", "tensor"), None),
            P("dp", "tensor"),
            P(),
            P("dp", "tensor"),
            P("dp", "tensor"),
            P("dp", "tensor"),
            P(),
            P("dp", "tensor"),
            P("dp", "tensor"),
            P(),
            P("tensor", "dp"),
            P("dp", "tensor"),
            P("dp", "tensor"),
            P("tensor", "dp"),
        ),
        check_vma=False,
    )
```

```python
import functools
import math

import jax
import jax.numpy as jnp
from jax import lax
from jax.experimental import pallas as pl
from jax.experimental.pallas import tpu as pltpu
from jax.sharding import PartitionSpec as P

HEAD = 64
HEADS = 24
TXT = 256
SEGS = 3
EPS = 1e-06
LANES = 2 * HEAD
SHUT = 256.0
ROOT = HEAD ** (-0.5)
VMEM_LIMIT = 16 * 2**20
NO_COST = pl.CostEstimate(flops=0, bytes_accessed=0, transcendentals=0)


def cost_of(micros):
    return pl.CostEstimate(flops=int(micros * 1e9), bytes_accessed=0, transcendentals=0)


SUM_ROWS = 6
CROSS_MICROS = 10
BLOCK_IN_MICROS = 0
FFN_MICROS = 3
FFN_NEXT_MICROS = 8
MIDDLE_MICROS = 10
SELF_MICROS = 0
ATTN_MICROS = 3
TEXT_MICROS = 8
PACK_MICROS = 16
SECOND_MICROS = 8
ATTN_FIRST_MICROS = 0

RING = 4
PAIR = 2
BLOCKS = RING * PAIR * RING
SLOTS = BLOCKS // RING
SEND_ORDER = (2, 1, 3, 0)
CORE_SWAP = [(0, 1), (1, 0), (2, 3), (3, 2)]
CHIP_SWAP = [(0, 2), (2, 0), (1, 3), (3, 1)]
ROW_ORDER = (0, 2, 1, 3)

def dp_index(x, z, y):
    return (x * PAIR + z) * RING + y


def dp_perm(axis, step):
    pairs = []

    def moved(place, size):
        if step == "flip":
            return place ^ 1
        if step == "mirror":
            return size - 1 - place
        return (place + step) % size

    for x in range(RING):
        for z in range(PAIR):
            for y in range(RING):
                for tensor in range(2 * PAIR):
                    way = axis
                    if axis in ("first", "second"):
                        way = "x" if (tensor % 2 == 0) == (axis == "first") else "y"
                    target = {
                        "x": (moved(x, RING), z, y),
                        "y": (x, z, moved(y, RING)),
                        "z": (x, moved(z, PAIR), y),
                    }[way]
                    pairs.append(
                        (
                            dp_index(x, z, y) * 2 * PAIR + tensor,
                            dp_index(*target) * 2 * PAIR + tensor,
                        )
                    )
    return pairs


def dp_permute(values, axis, step):
    return lax.ppermute(values, ("dp", "tensor"), dp_perm(axis, step))


def dp_spot(position):
    index = lax.axis_index("dp")
    x, z, y = index // (RING * PAIR), index // RING % PAIR, index % RING
    core = position % 2
    return jnp.stack([jnp.where(core == 0, x, y), z, jnp.where(core == 0, y, x), core])


def swap_core(values):
    return lax.ppermute(values, "tensor", CORE_SWAP)


def swap_chip(values):
    return lax.ppermute(values, "tensor", CHIP_SWAP)


def times_transpose(left, right):
    return lax.dot_general(
        left, right, (((1,), (1,)), ((), ())), preferred_element_type=jnp.float32
    )


def gather_tensor(block):
    far = swap_chip(block)
    near = swap_core(block)
    return [block, far, near, swap_core(far)]


def scatter_tensor(upper, lower):
    near = swap_core(lower)
    rows = upper.shape[0] // 2
    far = (upper[rows:].astype(jnp.float32) + near[rows:].astype(jnp.float32)).astype(near.dtype)
    return [upper, near, swap_chip(far)], far


def turn_kernel(source, target):
    target[...] = source[...].T


def turned(values, ties=()):
    tile = 512 if values.shape[1] % 512 == 0 else values.shape[1]
    return pl.pallas_call(
        lambda source, *rest: turn_kernel(source, rest[-1]),
        grid=(values.shape[1] // tile,),
        in_specs=[pl.BlockSpec((values.shape[0], tile), lambda step: (0, step))]
        + [pl.BlockSpec(memory_space=pl.ANY)] * len(ties),
        out_specs=pl.BlockSpec((tile, values.shape[0]), lambda step: (step, 0)),
        out_shape=jax.ShapeDtypeStruct(values.shape[::-1], values.dtype),
        compiler_params=pltpu.CompilerParams(vmem_limit_bytes=VMEM_LIMIT),
        cost_estimate=NO_COST,
    )(values, *ties)


def chunk_block(offset, slot, spot):
    first = (spot[0] + offset) % RING
    z, second = slot // RING, slot % RING
    x = jnp.where(spot[3] == 0, first, second)
    y = jnp.where(spot[3] == 0, second, first)
    return dp_index(x, z, y)


def offset_of_step(offsets, step):
    offset = offsets[-1]
    for place in range(len(offsets) - 1):
        offset = jnp.where(step == place, offsets[place], offset)
    return offset


def chunk_kernel(make, offsets, halves, extra, outs, held, sems):
    step = pl.program_id(0)
    first, second = halves

    def copies(place):
        slot = held.at[place % 2]
        if offsets[place] != 2:
            return [pltpu.make_async_copy(slot, outs[place], sems.at[place % 2, 0])]
        return [
            pltpu.make_async_copy(slot.at[half], out, sems.at[place % 2, way])
            for way, (half, out) in enumerate(zip((first, second), outs[place]))
        ]

    for place, offset in enumerate(offsets):

        @pl.when(step == place)
        def _(place=place, offset=offset):
            if place >= 2:
                for copy in copies(place - 2):
                    copy.wait()
            added = {1: (first, extra[0]), 3: (second, extra[1])}.get(offset) if extra else None
            make(held.at[place % 2], added, offset)
            for copy in copies(place):
                copy.start()
            if place == len(offsets) - 1:
                for last in range(max(place - 1, 0), place + 1):
                    for copy in copies(last):
                        copy.wait()


def chunk_call(make, operands, specs, offsets, halves, shape, spot, extra, ties, name, micros):
    count = len(operands)
    pieces = []
    for offset in offsets:
        if offset == 2:
            pieces += [tuple(len(range(*s.indices(d))) for s, d in zip(h, shape)) for h in halves]
        else:
            pieces.append(shape)

    def kernel(spot_ref, *refs):
        inputs, extras = refs[:count], refs[count : count + len(extra)]
        outs = list(refs[-len(pieces) - 2 : -2])
        grouped = []
        for offset in offsets:
            grouped.append((outs.pop(0), outs.pop(0)) if offset == 2 else outs.pop(0))
        chunk_kernel(
            functools.partial(make, inputs), offsets, halves, extras, grouped, refs[-2], refs[-1]
        )

    found = pl.pallas_call(
        kernel,
        grid_spec=pltpu.PrefetchScalarGridSpec(
            num_scalar_prefetch=1,
            grid=(len(offsets),),
            in_specs=list(specs)
            + [pl.BlockSpec(part.shape, lambda step, spot: (0, 0)) for part in extra]
            + [pl.BlockSpec(memory_space=pl.ANY)] * len(ties),
            out_specs=[pl.BlockSpec(memory_space=pl.ANY)] * len(pieces),
            scratch_shapes=[
                pltpu.VMEM((2,) + shape, jnp.bfloat16),
                pltpu.SemaphoreType.DMA((2, 2)),
            ],
        ),
        out_shape=[jax.ShapeDtypeStruct(piece, jnp.bfloat16) for piece in pieces],
        compiler_params=pltpu.CompilerParams(vmem_limit_bytes=VMEM_LIMIT),
        cost_estimate=cost_of(micros),
        name=name,
    )(spot, *operands, *extra, *ties)
    found = list(found)
    return [
        (found.pop(0), found.pop(0)) if offset == 2 else found.pop(0) for offset in offsets
    ]


def make_rows(groups, inputs, slot, added, offset):
    lefts, rights = inputs[: SLOTS * len(groups)], inputs[SLOTS * len(groups) :]
    size = SLOTS * lefts[0].shape[1]
    if len(rights) > sum(groups):
        slot[size:, :] = rights[-1][...]
    column = place = 0
    for group, count in enumerate(groups):
        rows = jnp.concatenate(
            [left[0] for left in lefts[SLOTS * group : SLOTS * (group + 1)]], axis=0
        )
        for right in rights[place : place + count]:
            wide = right.shape[1]
            product = dot(rows, right[...])
            low, high = column, column
            if added is not None:
                low = min(max(column, added[0][1].start), column + wide)
                high = min(max(column, added[0][1].stop), column + wide)
            for start, stop in ((column, low), (low, high), (high, column + wide)):
                if start < stop:
                    part = product[:, start - column : stop - column]
                    if (start, stop) == (low, high):
                        base = added[0][1].start
                        part = part + added[1][:size, start - base : stop - base].astype(jnp.float32)
                    slot[:size, start:stop] = part.astype(jnp.bfloat16)
            column += wide
        place += count


def row_chunks(pairs, offsets, spot, extra=(), ties=(), micros=0, riders=()):
    lefts = [left.reshape(BLOCKS, left.shape[0] // BLOCKS, left.shape[1]) for left, _ in pairs]
    rights = [right for _, group in pairs for right in group]
    total = sum(right.shape[1] for right in rights)
    specs, operands = [], []
    for left in lefts:
        for slot in range(SLOTS):
            specs.append(
                pl.BlockSpec(
                    (1,) + left.shape[1:],
                    lambda step, spot, slot=slot: (
                        chunk_block(offset_of_step(offsets, step), slot, spot),
                        0,
                        0,
                    ),
                )
            )
            operands.append(left)
    specs += [pl.BlockSpec(right.shape, lambda step, spot: (0, 0)) for right in rights]
    specs += [pl.BlockSpec(part.shape, lambda step, spot: (0, 0)) for part in riders]
    rows = SLOTS * lefts[0].shape[1] + sum(part.shape[0] for part in riders)
    halves = [(slice(0, rows), slice(0, total // 2)), (slice(0, rows), slice(total // 2, total))]
    return chunk_call(
        functools.partial(make_rows, [len(group) for _, group in pairs]),
        operands + rights + list(riders),
        specs,
        offsets,
        halves,
        (rows, total),
        spot,
        extra,
        ties,
        "row_chunks",
        micros,
    )


def make_columns(lefts, inputs, slot, added, offset):
    whole = jnp.concatenate([right[...] for right in inputs[lefts:]], axis=1)
    row = 0
    for left in inputs[:lefts]:
        product = dot(left[...], whole)
        if added is not None and added[0][0].start == row:
            product = product + added[1][...].astype(jnp.float32)
        slot[row : row + left.shape[0], :] = product.astype(jnp.bfloat16)
        row += left.shape[0]


def column_chunks(lefts, right, offsets, spot, extra=(), ties=(), micros=0):
    rows = lefts[0].shape[0]
    depth, columns = right.shape
    specs = [pl.BlockSpec(left.shape, lambda step, spot: (0, 0)) for left in lefts]
    for slot in range(SLOTS):
        specs.append(
            pl.BlockSpec(
                (depth, columns // BLOCKS),
                lambda step, spot, slot=slot: (
                    0,
                    chunk_block(offset_of_step(offsets, step), slot, spot),
                ),
            )
        )
    lanes = columns // RING
    halves = [(slice(0, rows), slice(0, lanes)), (slice(rows, 2 * rows), slice(0, lanes))]
    return chunk_call(
        functools.partial(make_columns, len(lefts)),
        list(lefts) + [right] * SLOTS,
        specs,
        offsets,
        halves,
        (2 * rows, lanes),
        spot,
        extra,
        ties,
        "column_chunks",
        micros,
    )


def add_up(refs, index):
    total = refs[0][index].astype(jnp.float32)
    for ref in refs[1:]:
        total = total + ref[index].astype(jnp.float32)
    return total


def lane_slice(start, size):
    return (slice(None), pl.ds(pl.multiple_of(start * size, size), size))


def halving_places(spot):
    own = spot[2]
    other = own ^ 1
    return (own, RING - 1 - own), (other, RING - 1 - other)


def ffn_second_kernel(spot, *refs):
    parts = refs[:-2]
    for out, places in zip(refs[-2:], halving_places(spot)):
        for index, place in enumerate(places):
            for z in range(PAIR):
                out[index * PAIR + z] = add_up(parts, z * RING + place).astype(jnp.bfloat16)


def ffn_middle_kernel(kept, got, own, sent):
    for out, start in ((own, 0), (sent, PAIR)):
        for z in range(PAIR):
            out[z] = add_up((kept, got), start + z).astype(jnp.bfloat16)


def ffn_third_kernel(spot, *refs):
    for out, z in ((refs[-2], spot[1]), (refs[-1], (spot[1] + 1) % PAIR)):
        out[...] = add_up(refs[:-2], z).astype(jnp.bfloat16)


def ffn_last_kernel(kept, got, gate_out, up_out, down_out):
    total = kept[...].astype(jnp.float32) + got[...].astype(jnp.float32)
    hidden = gate_out.shape[1]
    gate_out[...] = total[:, :hidden]
    up_out[...] = total[:, hidden : 2 * hidden]
    down_out[...] = total[:, 2 * hidden :].T


def text_second_kernel(spot, *refs):
    parts = refs[:-2]
    lanes = parts[0].shape[1] // SLOTS
    for out, places in zip(refs[-2:], halving_places(spot)):
        for index, place in enumerate(places):
            for z in range(PAIR):
                start = (index * PAIR + z) * lanes
                out[:, start : start + lanes] = add_up(
                    parts, lane_slice(z * RING + place, lanes)
                ).astype(jnp.bfloat16)


def text_middle_kernel(kept, got, own, sent):
    wide = own.shape[1]
    for out, start in ((own, 0), (sent, wide)):
        index = (slice(None), slice(start, start + wide))
        out[...] = add_up((kept, got), index).astype(jnp.bfloat16)


def text_third_kernel(spot, *refs):
    lanes = refs[-1].shape[1]
    for out, z in ((refs[-2], spot[1]), (refs[-1], (spot[1] + 1) % PAIR)):
        out[...] = add_up(refs[:-2], lane_slice(z, lanes)).astype(jnp.bfloat16)


def text_last_kernel(kept, got, textkey, textvalue):
    total = kept[...].astype(jnp.float32) + got[...].astype(jnp.float32)
    columns = textkey.shape[1]
    textkey[...] = total[:columns].T
    textvalue[...] = total[columns:].T


def attn_second_kernel(rows, spot, riders, opposite, *refs):
    parts, outs = refs[:-RING], refs[-RING:]
    size = SLOTS * rows
    for offset in range(RING):
        for z in range(PAIR):
            slot = z * RING + (spot[2] + offset) % RING
            index = (pl.ds(pl.multiple_of(slot * rows, 16), rows), slice(None))
            outs[offset][z * rows : (z + 1) * rows, :] = add_up(parts, index).astype(jnp.bfloat16)
    pairs = ((riders[...], parts[1][size:, :]), (opposite[...], parts[2][size:, :]))
    joined = [merge_rows(PAIR, first, second, rider_rows(2 * PAIR)) for first, second in pairs]
    joined = merge_rows(2 * PAIR, joined[0], joined[1], rider_rows(4 * PAIR))
    for out in outs:
        out[PAIR * rows :, :] = joined


def attn_third_kernel(spot, *refs):
    rows = refs[-1].shape[0]
    for out, z in ((refs[-2], spot[1]), (refs[-1], (spot[1] + 1) % PAIR)):
        index = (pl.ds(pl.multiple_of(z * rows, 16), rows), slice(None))
        out[...] = add_up(refs[:RING], index).astype(jnp.bfloat16)


def attn_last_kernel(kept, got, query, key, value, outw):
    total = kept[...].astype(jnp.float32) + got[...].astype(jnp.float32)
    columns = query.shape[1]
    for place, out in enumerate((query, key, value)):
        out[...] = total[:, place * columns : (place + 1) * columns]
    outw[...] = total[:, 3 * columns :].T


def whole_call(kernel, scalars, operands, outs, name, ties=(), scratch=(), micros=0):
    whole = pl.BlockSpec(memory_space=pltpu.VMEM)
    count = len(scalars) + len(operands)
    return pl.pallas_call(
        lambda *refs: kernel(*refs[:count], *refs[count + len(ties) :]),
        in_specs=[pl.BlockSpec(memory_space=pltpu.SMEM)] * len(scalars)
        + [whole] * len(operands)
        + [pl.BlockSpec(memory_space=pl.ANY)] * len(ties),
        out_specs=[whole] * len(outs),
        out_shape=[jax.ShapeDtypeStruct(shape, kind) for shape, kind in outs],
        scratch_shapes=list(scratch),
        compiler_params=pltpu.CompilerParams(vmem_limit_bytes=VMEM_LIMIT),
        cost_estimate=cost_of(micros),
        name=name,
    )(*scalars, *operands, *ties)


def tiled_call(kernel, scalars, operands, outs, name, axis, tiles, ties=(), micros=0, axes=None):
    def spec(shape, axis):
        block = list(shape)
        block[axis] //= tiles
        if axis == 0:
            return pl.BlockSpec(tuple(block), lambda step: (step,) + (0,) * (len(shape) - 1))
        return pl.BlockSpec(tuple(block), lambda step: (0,) * (len(shape) - 1) + (step,))

    count = len(scalars) + len(operands)
    return pl.pallas_call(
        lambda *refs: kernel(*refs[:count], *refs[count + len(ties) :]),
        grid=(tiles,),
        in_specs=[pl.BlockSpec(memory_space=pltpu.SMEM)] * len(scalars)
        + [spec(part.shape, way) for part, way in zip(operands, axes or [axis] * len(operands))]
        + [pl.BlockSpec(memory_space=pl.ANY)] * len(ties),
        out_specs=[spec(shape, axis) for shape, _ in outs],
        out_shape=[jax.ShapeDtypeStruct(shape, kind) for shape, kind in outs],
        compiler_params=pltpu.CompilerParams(vmem_limit_bytes=VMEM_LIMIT),
        cost_estimate=cost_of(micros),
        name=name,
    )(*scalars, *[pltpu.with_memory_space_constraint(part, pltpu.HBM) for part in operands], *ties)


def exchange(chunks, axis):
    return [chunks[0]] + [
        dp_permute(chunks[step], axis, step) for step in range(1, len(chunks))
    ]


def one_on(halves):
    return dp_permute(halves[0], "first", 1), dp_permute(halves[1], "first", RING - 1)


def to_neighbours(own, ahead, behind):
    return [own, dp_permute(ahead, "first", 1), dp_permute(behind, "first", RING - 1)]


def by_slots(chunk):
    return chunk.reshape(SLOTS, chunk.shape[0] // SLOTS, chunk.shape[1])


def lane_index(shape):
    return lax.broadcasted_iota(jnp.int32, shape, 1)


def head_lanes(shape, head):
    lane = lane_index(shape)
    return (lane < HEAD) if head == 0 else (lane >= HEAD)


def per_head(values, reduce):
    first = head_lanes(values.shape, 0)
    left = jnp.sum(jnp.where(first, values, 0.0), axis=1, keepdims=True)
    right = jnp.sum(jnp.where(first, 0.0, values), axis=1, keepdims=True)
    return jnp.where(first, left, right)


def head_units(raw):
    inverse = lax.rsqrt(per_head(raw * raw, None) * (1.0 / HEAD) + EPS)
    return raw * inverse, inverse


def partner(values):
    lane = lane_index(values.shape)
    return jnp.where(
        lane % HEAD < HEAD // 2,
        pltpu.roll(values, LANES - HEAD // 2, 1),
        pltpu.roll(values, HEAD // 2, 1),
    )


def dot(left, right):
    return jnp.dot(left, right, preferred_element_type=jnp.float32)


def dot_t(left, right):
    return lax.dot_general(left, right, (((1,), (1,)), ((), ())), preferred_element_type=jnp.float32)


def attend_kernel(
    raw_q, raw_k, value, raw_t, text_value, cosine, sine, gains, gate, gate_swapped, mark_q, mark_k, mark_t,
    query_out, key_out, text_out, mixed_out, self_out, cross_out, self_log, cross_log,
):
    cos, sin = cosine[...], sine[...]
    unit = head_units(raw_q[...])[0] * gains[0:1, :]
    query = ((unit * cos + partner(unit) * sin).astype(jnp.bfloat16) * ROOT).astype(jnp.bfloat16)
    unit = head_units(raw_k[...])[0] * gains[1:2, :]
    key = (unit * cos + partner(unit) * sin).astype(jnp.bfloat16)
    text = (head_units(raw_t[...])[0] * gains[2:3, :]).astype(jnp.bfloat16)
    query_out[...] = query
    key_out[...] = key
    text_out[...] = text

    def attention(keys, marks, values):
        outs, sums = [], []
        for head in range(2):
            own = head_lanes(query.shape, head)
            own_keys = head_lanes(keys.shape, head)
            probe = jnp.where(own, query, mark_q[...])
            scores = dot_t(probe, jnp.where(own_keys, keys, marks))
            weights = jnp.exp(scores).astype(jnp.bfloat16)
            both = dot(weights, jnp.where(own_keys, values, jnp.ones_like(values)))
            outs.append(both)
        first = head_lanes(outs[0].shape, 0)
        product = jnp.where(first, outs[0], outs[1])
        total = jnp.where(first, outs[1], outs[0])
        return product / pltpu.roll(total, HEAD, 1), jnp.log(total)

    out, log = attention(key, mark_k[...], value[...])
    self_out[...] = out
    self_log[...] = log
    cross, log = attention(text, mark_t[...], text_value[...])
    cross_out[...] = cross
    cross_log[...] = log - jnp.log(gate_swapped[...])
    mixed_out[...] = (out + gate[...] * cross).astype(jnp.bfloat16)


def attention_grads(query, keys, marks, values, grad, out, log, mark_q):
    rows = grad.astype(jnp.float32)
    delta = per_head(rows * out, None)
    delta = pltpu.roll(delta, HEAD, 1)
    lane = lane_index(query.shape) % HEAD
    log_high = log.astype(jnp.bfloat16)
    log_low = (log - log_high.astype(jnp.float32)).astype(jnp.bfloat16)
    delta_high = delta.astype(jnp.bfloat16)
    delta_low = (delta - delta_high.astype(jnp.float32)).astype(jnp.bfloat16)
    zero = jnp.zeros_like(query)
    code = jnp.where(lane == 4, -log_high, jnp.where(lane == 5, -log_low, mark_q))
    shift = jnp.where(lane == 4, -delta_high, jnp.where(lane == 5, -delta_low, zero))
    key_grads, value_grads, query_grads = [], [], []
    for head in range(2):
        own = head_lanes(query.shape, head)
        own_keys = head_lanes(keys.shape, head)
        probe = jnp.where(own, query, code)
        probs = jnp.exp(dot_t(jnp.where(own_keys, keys, marks), probe))
        slope = dot_t(jnp.where(own_keys, values, marks), jnp.where(own, grad, shift))
        score_grad = (probs * slope).astype(jnp.bfloat16)
        value_grads.append(dot(probs.astype(jnp.bfloat16), grad))
        key_grads.append(dot(score_grad, query))
        turned = keys[:, head * HEAD : (head + 1) * HEAD].T
        query_grads.append(dot(turned, score_grad))
    first = head_lanes(keys.shape, 0)
    return (
        jnp.concatenate(query_grads, axis=0),
        jnp.where(first, key_grads[0], key_grads[1]),
        jnp.where(first, value_grads[0], value_grads[1]),
    )


def norm_back(weighted, unit, inverse):
    return inverse * (weighted - unit * (per_head(weighted * unit, None) * (1.0 / HEAD)))


def cross_back_kernel(
    query, text, text_value, raw_t, grad, out, log, gains, mark_q, mark_t,
    query_grad, raw_grad, value_grad, gain_sum, gate_sum,
):
    grad_q, grad_t, grad_v = attention_grads(
        query[...], text[...], mark_t[...], text_value[...], grad[...], out[...], log[...], mark_q[...]
    )
    query_grad[...] = grad_q.T
    value_grad[...] = grad_v.astype(jnp.bfloat16).T
    grad_t = grad_t.astype(jnp.bfloat16).astype(jnp.float32)
    unit, inverse = head_units(raw_t[...])
    gain_sum[...] = jnp.sum(grad_t * unit, axis=0, keepdims=True)
    raw_grad[...] = norm_back(grad_t * gains[2:3, :], unit, inverse).astype(jnp.bfloat16).T
    gate_sum[...] = jnp.sum(grad[...].astype(jnp.float32) * out[...], axis=0, keepdims=True)


def self_back_kernel(
    query, key, value, raw_q, raw_k, grad, out, log, cross_grad, cosine, sine, gains, mark_q, mark_k,
    query_grad, key_grad, value_grad, gain_sum,
):
    grad_q, grad_k, grad_v = attention_grads(
        query[...], key[...], mark_k[...], value[...], grad[...], out[...], log[...], mark_q[...]
    )
    value_grad[...] = grad_v.astype(jnp.bfloat16)
    cos, sin = cosine[...], sine[...]
    grad_q = (grad_q.T + cross_grad[...]) * ROOT
    for turn, raw, row, target in ((grad_q, raw_q, 0, query_grad), (grad_k, raw_k, 1, key_grad)):
        turn = turn.astype(jnp.bfloat16).astype(jnp.float32)
        turn = turn * cos - partner(turn) * sin
        unit, inverse = head_units(raw[...])
        gain_sum[row : row + 1, :] = jnp.sum(turn * unit, axis=0, keepdims=True)
        target[...] = norm_back(turn * gains[row : row + 1, :], unit, inverse).astype(jnp.bfloat16)


def pair_call(kernel, operands, outs, name, ties=(), micros=0):
    def spec(shape, cut):
        if cut is None:
            return pl.BlockSpec(shape, lambda pair: (0, 0))
        if cut == 1:
            return pl.BlockSpec((shape[0], LANES), lambda pair: (0, pair))
        return pl.BlockSpec((LANES, shape[1]), lambda pair: (pair, 0))

    width = outs[0][0][0] if outs[0][2] == 0 else outs[0][0][1]
    return pl.pallas_call(
        lambda *refs: kernel(*refs[: len(operands)], *refs[len(operands) + len(ties) :]),
        grid=(width // LANES,),
        in_specs=[spec(part.shape, cut) for part, cut in operands]
        + [pl.BlockSpec(memory_space=pl.ANY)] * len(ties),
        out_specs=[spec(shape, cut) for shape, _, cut in outs],
        out_shape=[jax.ShapeDtypeStruct(shape, kind) for shape, kind, _ in outs],
        compiler_params=pltpu.CompilerParams(vmem_limit_bytes=VMEM_LIMIT),
        cost_estimate=cost_of(micros),
        name=name,
    )(*[part for part, _ in operands], *ties)
def inverse_rms(values):
    return lax.rsqrt(jnp.mean(values * values, axis=-1, keepdims=True) + EPS)


def row_norm_back(weighted, unit, inverse):
    return inverse * (weighted - unit * jnp.mean(weighted * unit, axis=-1, keepdims=True))


def per_row(table, segment):
    return jnp.where(segment == 0.0, table[0:1], jnp.where(segment == 1.0, table[1:2], table[2:3]))


def total_of(parts):
    upper, near, far = parts
    rows = far.shape[0]
    return (
        upper[:rows].astype(jnp.float32) + near[:rows].astype(jnp.float32) + far[...].astype(jnp.float32)
    )


def segment_sums(member, values):
    high = values.astype(jnp.bfloat16)
    low = (values - high.astype(jnp.float32)).astype(jnp.bfloat16)
    return dot(member, high) + dot(member, low)


def tables_kernel(here, lens, gate, segments, head_gains, cosine, sine, mark_q, mark_k, mark_t,
                  segment, member, gate_lanes, gate_swapped, gains):
    heads = gains.shape[1] // HEAD
    lane = lane_index(gate_lanes.shape) // HEAD
    line = jnp.zeros(gate_lanes.shape, jnp.float32)
    swapped = line
    for head in range(heads):
        line = jnp.where(lane == head, gate[head], line)
        swapped = jnp.where(lane == head ^ 1, gate[head], swapped)
    gate_lanes[...] = jnp.tanh(line)
    gate_swapped[...] = jnp.tanh(swapped)
    gains[...] = jnp.concatenate([head_gains[...]] * heads, axis=1)
    rows = segments.shape[1]
    ids = segments[...]
    first = jnp.sum((ids < 1).astype(jnp.float32))
    second = jnp.sum((ids < 2).astype(jnp.float32))
    lane = lane_index((rows, LANES))
    half = HEAD // 2
    rate = jnp.exp((lane % half).astype(jnp.float32) * (-2.0 * math.log(10000.0) / HEAD))
    within = lane % HEAD
    for block, code in enumerate(ROW_ORDER):
        source = here[0] ^ code
        line = segments[pl.ds(source, 1), :].astype(jnp.float32)
        label = jnp.broadcast_to(line, (rows, rows)).T
        start = jnp.where(label == 0.0, 0.0, jnp.where(label == 1.0, first, second))
        token = (lax.broadcasted_iota(jnp.int32, (rows, LANES), 0) + source * rows).astype(jnp.float32)
        angle = (token - start) * rate
        index = slice(block * rows, (block + 1) * rows)
        cosine[index, :] = jnp.cos(angle)
        sine[index, :] = jnp.where(within < half, -1.0, 1.0) * jnp.sin(angle)
        same = ((label == within.astype(jnp.float32)) & (within < SEGS)).astype(jnp.float32)
        shut = (within == SEGS).astype(jnp.float32)
        ones = ((within >= SEGS) & (within < SEGS + 3)).astype(jnp.float32)
        mark_q[index, :] = (SHUT * same - SHUT * shut).astype(jnp.bfloat16)
        mark_k[index, :] = (same + ones).astype(jnp.bfloat16)
        if block == 0:
            segment[...] = label
            member[...] = (
                lax.broadcasted_iota(jnp.int32, (8, rows), 0).astype(jnp.float32) == line
            ).astype(jnp.bfloat16)
    for group in range(SEGS):
        lane = lane_index((TXT, LANES)) % HEAD
        row = lax.broadcasted_iota(jnp.int32, (TXT, LANES), 0)
        inside = ((lane == group) & (row < lens[group])).astype(jnp.float32)
        ones = ((lane >= SEGS) & (lane < SEGS + 3)).astype(jnp.float32)
        mark_t[group * TXT : (group + 1) * TXT, :] = (inside + ones).astype(jnp.bfloat16)


def text_kernel(captions, key_weight, value_weight, raw_out, value_out, raw_sum, value_sum):
    step = pl.program_id(0)

    @pl.when(step == 0)
    def _():
        raw_sum[...] = dot(captions[...], key_weight[...])
        value_sum[...] = dot(captions[...], value_weight[...])

    @pl.when(step > 0)
    def _():
        raw_sum[...] += dot(captions[...], key_weight[...])
        value_sum[...] += dot(captions[...], value_weight[...])

    @pl.when(step == pl.num_programs(0) - 1)
    def _():
        raw_out[...] = raw_sum[...]
        value_out[...] = value_sum[...].astype(jnp.bfloat16)


def text_call(captions, key_weight, value_weight):
    rows, depth = captions.shape
    columns = key_weight.shape[1]
    tile = depth // 4
    return pl.pallas_call(
        text_kernel,
        grid=(depth // tile,),
        in_specs=[
            pl.BlockSpec((rows, tile), lambda step: (0, step)),
            pl.BlockSpec((tile, columns), lambda step: (step, 0)),
            pl.BlockSpec((tile, columns), lambda step: (step, 0)),
        ],
        out_specs=[pl.BlockSpec((rows, columns), lambda step: (0, 0))] * 2,
        out_shape=[
            jax.ShapeDtypeStruct((rows, columns), jnp.float32),
            jax.ShapeDtypeStruct((rows, columns), jnp.bfloat16),
        ],
        scratch_shapes=[pltpu.VMEM((rows, columns), jnp.float32)] * 2,
        compiler_params=pltpu.CompilerParams(vmem_limit_bytes=VMEM_LIMIT),
        cost_estimate=cost_of(9),
        name="text",
    )(*[pltpu.with_memory_space_constraint(part, pltpu.HBM) for part in (captions, key_weight, value_weight)])


def project_kernel(here, own, far, near, last, mods, gains, segment_q, query_w, key_w, value_w,
                   rows_out, raw_q, raw_k, value):
    table = mods[here[0]]
    rows = own.shape[0]
    for block, part in enumerate((own, far, near, last)):
        index = slice(block * rows, (block + 1) * rows)
        values = part[...].astype(jnp.float32)
        marks = segment_q[index, :].astype(jnp.float32)
        scale = jnp.where(
            marks[:, 0:1] > 0.0, table[0:1], jnp.where(marks[:, 1:2] > 0.0, table[1:2], table[2:3])
        )
        rows_out[index, :] = (
            values * inverse_rms(values) * gains[0:1] * (1.0 + scale)
        ).astype(jnp.bfloat16)
    raw_q[...] = dot(rows_out[...], query_w[...])
    raw_k[...] = dot(rows_out[...], key_w[...])
    value[...] = dot(rows_out[...], value_w[...]).astype(jnp.bfloat16)


def middle_kernel(here, block, upper, near, far, mods, gains, segment, attn_out, middle_out, rows_out):
    attn_sum = total_of((upper, near, far))
    label = segment[:, 0:1]
    factor = jnp.tanh(per_row(mods[here[0] ^ 1], label)) * gains[1:2]
    middle = block[...].astype(jnp.float32) + factor * (attn_sum * inverse_rms(attn_sum))
    attn_out[...] = attn_sum
    middle_out[...] = middle
    scale = per_row(mods[here[0] ^ 2], label)
    rows_out[...] = (middle * inverse_rms(middle) * gains[2:3] * (1.0 + scale)).astype(jnp.bfloat16)


def block_out_kernel(here, middle, upper, near, far, grad, mods, gains, segment, member,
                     block_out, grad_out, sums):
    ffn_sum = total_of((upper, near, far))
    inverse = inverse_rms(ffn_sum)
    unit = ffn_sum * inverse
    factor = jnp.tanh(per_row(mods[here[0] ^ 3], segment[:, 0:1])) * gains[3:4]
    block_out[...] = (middle[...] + factor * unit).astype(jnp.bfloat16)
    incoming = grad[...].astype(jnp.float32)
    grad_out[...] = row_norm_back(incoming * factor, unit, inverse).astype(jnp.bfloat16)
    sums[...] = segment_sums(member[...], incoming * unit)


def middle_back_kernel(here, middle, attn, upper, near, far, grad, mods, gains, segment, member,
                       middle_grad, attn_grad, ffn_sums, attn_sums):
    grad_in = total_of((upper, near, far))
    label = segment[:, 0:1]
    inverse = inverse_rms(middle[...])
    unit = middle[...] * inverse
    factor = gains[2:3] * (1.0 + per_row(mods[here[0] ^ 2], label))
    ffn_sums[...] = segment_sums(member[...], grad_in * unit)
    grad_middle = grad[...].astype(jnp.float32) + row_norm_back(grad_in * factor, unit, inverse)
    middle_grad[...] = grad_middle
    inverse = inverse_rms(attn[...])
    unit = attn[...] * inverse
    factor = jnp.tanh(per_row(mods[here[0] ^ 1], label)) * gains[1:2]
    attn_grad[...] = row_norm_back(grad_middle * factor, unit, inverse).astype(jnp.bfloat16)
    attn_sums[...] = segment_sums(member[...], grad_middle * unit)


def block_in_kernel(here, block, middle_grad, upper, near, far, mods, gains, segment, member,
                    in_grad, sums):
    grad_in = total_of((upper, near, far))
    values = block[...].astype(jnp.float32)
    inverse = inverse_rms(values)
    unit = values * inverse
    factor = gains[0:1] * (1.0 + per_row(mods[here[0]], segment[:, 0:1]))
    in_grad[...] = (
        middle_grad[...] + row_norm_back(grad_in * factor, unit, inverse)
    ).astype(jnp.bfloat16)
    sums[...] = segment_sums(member[...], grad_in * unit)


def stack_sums_kernel(here, first, second, third, fourth, head_gain, text_gain, gate_sum, gate, out):
    width = out.shape[1]
    heads = jnp.concatenate([head_gain[0:1], head_gain[1:2], text_gain[...]], axis=1)
    inner = heads.shape[1] // 3
    gates = gate_sum[...] * (1.0 - gate[...] * gate[...])
    gates = jnp.concatenate([gates, jnp.zeros((1, width - inner), jnp.float32)], axis=1)
    lane = lane_index(gates.shape)
    moved = jnp.zeros_like(gates)
    for position in range(4):
        turn = pltpu.roll(gates, position * inner, 1) if position else gates
        moved = jnp.where((lane // inner == position) & (here[0] == position), turn, moved)
    out[...] = jnp.concatenate(
        [part[0:SEGS] for part in (first, second, third, fourth)]
        + [
            jnp.concatenate([heads, jnp.zeros((1, width - 3 * inner), jnp.float32)], axis=1),
            moved,
            jnp.zeros((2, width), jnp.float32),
        ],
        axis=0,
    )


def pack_kernel(here, own, far, near, last, mods, gains, cond, packed):
    total = own[...] + far[...] + near[...] + last[...]
    grad = jnp.zeros((SEGS, total.shape[1]), jnp.float32)
    rows = []
    for name in range(4):
        part = total[name * SEGS : (name + 1) * SEGS]
        mod = mods[here[0] ^ name]
        gain = gains[name : name + 1]
        if name % 2 == 1:
            factor = jnp.tanh(mod)
            slope = 1.0 - factor * factor
        else:
            factor = 1.0 + mod
            slope = jnp.ones_like(mod)
        rows.append(jnp.sum(part * factor, axis=0, keepdims=True))
        mine = (jnp.zeros(part.shape, jnp.int32) + here[0]) == name
        grad = jnp.where(mine, part * slope * gain, grad)
    rows.append(total[4 * SEGS : 4 * SEGS + 2])
    rows = jnp.concatenate(rows, axis=0)
    high = rows.astype(jnp.bfloat16).astype(jnp.float32)
    pad = jnp.zeros((packed.shape[0] - 2 * SEGS - 2 * SUM_ROWS, total.shape[1]), jnp.float32)
    packed[...] = jnp.concatenate(
        [grad, cond[...].astype(jnp.float32), high, rows - high, pad], axis=0
    ).astype(jnp.bfloat16)


def rider_rows(count):
    return -(-(2 * SEGS * count + 2 * SUM_ROWS) // 16) * 16


def merge_rows(count, first, second, size):
    first, second = first.astype(jnp.float32), second.astype(jnp.float32)
    wide = SEGS * count
    start = 2 * wide
    sums = (
        first[start : start + SUM_ROWS]
        + first[start + SUM_ROWS : start + 2 * SUM_ROWS]
        + second[start : start + SUM_ROWS]
        + second[start + SUM_ROWS : start + 2 * SUM_ROWS]
    )
    high = sums.astype(jnp.bfloat16).astype(jnp.float32)
    pieces = [first[:wide], second[:wide], first[wide:start], second[wide:start], high, sums - high]
    rest = size - 4 * wide - 2 * SUM_ROWS
    if rest:
        pieces.append(jnp.zeros((rest, first.shape[1]), jnp.float32))
    return jnp.concatenate(pieces, axis=0).astype(jnp.bfloat16)


def merge_kernel(count, ours, theirs, out):
    out[...] = merge_rows(count, ours[...], theirs[...], out.shape[0])


def ada_kernel(count, heads, dp, own, *refs):
    parts = (own,) + refs[:3]
    ada_out, norm_out, head_out, gate_out = refs[3:]
    wide = SEGS * count
    base = own.shape[0] - rider_rows(count)
    columns = ada_out.shape[0]
    share = LANES // columns
    start = pl.multiple_of(dp[0] // share * LANES, LANES)
    grads, conds = [], []
    sums = jnp.zeros((SUM_ROWS, own.shape[1]), jnp.float32)
    for part in parts:
        rows = part[base:, :].astype(jnp.float32)
        grads.append(rows[:wide])
        conds.append(part[base:, pl.ds(start, LANES)].astype(jnp.float32)[wide : 2 * wide])
        for half in range(2):
            place = 2 * wide + half * SUM_ROWS
            sums = sums + rows[place : place + SUM_ROWS]
    conds = jnp.concatenate(conds, axis=0)
    conds = pltpu.roll(conds, (LANES - dp[0] % share * columns) % LANES, 1)
    acts = conds / (1.0 + jnp.exp(-conds))
    ada_out[...] = dot(
        acts.astype(jnp.bfloat16).astype(jnp.float32).T.astype(jnp.bfloat16),
        jnp.concatenate(grads, axis=0).astype(jnp.bfloat16),
    )[:columns]
    norm_out[...] = sums[:4]
    inner = heads * HEAD
    for row in range(3):
        line = jnp.zeros((1, HEAD), jnp.float32)
        for head in range(heads):
            place = row * inner + head * HEAD
            line = line + sums[4:5, place : place + HEAD]
        head_out[row : row + 1, :] = line
    lane = lane_index((1, LANES))
    line = jnp.zeros((1, LANES), jnp.float32)
    for head in range(HEADS):
        value = jnp.sum(sums[5:6, head * HEAD : (head + 1) * HEAD], axis=1, keepdims=True)
        line = jnp.where(lane == head, value, line)
    gate_out[...] = line


def back_kernel(count, *refs):
    grads, weights, upper, lower = refs[:count], refs[count : 2 * count], refs[-2], refs[-1]
    total = dot_t(grads[0][...], weights[0][...])
    for grad, weight in zip(grads[1:], weights[1:]):
        total = total + dot_t(grad[...], weight[...])
    half = upper.shape[0]
    upper[...] = total[:half].astype(jnp.bfloat16)
    lower[...] = total[half:].astype(jnp.bfloat16)


def back_call(grads, weights, name, ties=(), micros=0):
    rows, inner = grads[0].shape
    columns = weights[0].shape[0]
    tile = columns // 3
    return pl.pallas_call(
        lambda *refs: back_kernel(len(grads), *refs[: 2 * len(grads)], *refs[-2:]),
        grid=(columns // tile,),
        in_specs=[pl.BlockSpec((rows, inner), lambda step: (0, 0))] * len(grads)
        + [pl.BlockSpec((tile, inner), lambda step: (step, 0))] * len(grads)
        + [pl.BlockSpec(memory_space=pl.ANY)] * len(ties),
        out_specs=[pl.BlockSpec((rows // 2, tile), lambda step: (0, step))] * 2,
        out_shape=[jax.ShapeDtypeStruct((rows // 2, columns), jnp.bfloat16)] * 2,
        compiler_params=pltpu.CompilerParams(vmem_limit_bytes=VMEM_LIMIT),
        cost_estimate=cost_of(micros),
        name=name,
    )(*grads, *weights, *ties)


def shards(
    block_in,
    out_grad,
    condition,
    captions,
    caption_len,
    segment_ids,
    ada_weight,
    norm_gains,
    query_weight,
    key_weight,
    value_weight,
    head_gains,
    textkey_weight,
    textvalue_weight,
    cross_gate,
    out_weight,
    gate_weight,
    up_weight,
    down_weight,
):
    rows, width = block_in.shape
    length = segment_ids.shape[0]
    heads = cross_gate.shape[0]
    inner = heads * HEAD
    half_rows = length // 2
    position = lax.axis_index("tensor")
    spot = dp_spot(position)
    here = position.reshape(1)
    b16, f32 = jnp.bfloat16, jnp.float32

    blocks = gather_tensor(block_in)
    cond_rows = jnp.pad(condition, ((0, 0), (0, width - condition.shape[1])))
    own_act = jax.nn.silu(condition.astype(f32)).astype(b16)
    own_part = jnp.dot(own_act, ada_weight, preferred_element_type=f32)
    parts = gather_tensor(own_part)
    mods = jnp.stack([parts[ROW_ORDER.index(code)] for code in range(4)])

    cosine, sine, mark_q, mark_k, mark_t, segment, member, gate_lanes, gate_swapped, gains = whole_call(
        tables_kernel,
        (here, caption_len, cross_gate),
        [segment_ids.reshape(length // rows, rows), head_gains],
        [((length, LANES), f32)] * 2
        + [((length, LANES), b16)] * 2
        + [((SEGS * TXT, LANES), b16), ((rows, LANES), f32), ((8, rows), b16)]
        + [((1, inner), f32)] * 2
        + [((3, inner), f32)],
        "tables",
        micros=2,
    )
    caption_flat = captions.reshape(-1, captions.shape[-1])
    texts = caption_flat.shape[0]
    raw_t, text_value = text_call(caption_flat, textkey_weight, textvalue_weight)
    attn_rows, raw_q, raw_k, value = whole_call(
        project_kernel,
        (here,),
        blocks + [mods, norm_gains, mark_q, query_weight, key_weight, value_weight],
        [((length, width), b16), ((length, inner), f32), ((length, inner), f32), ((length, inner), b16)],
        "project",
        micros=6,
    )
    query, key, text, mixed, self_out, cross_out, self_log, cross_log = pair_call(
        attend_kernel,
        [(raw_q, 1), (raw_k, 1), (value, 1), (raw_t, 1), (text_value, 1), (cosine, None), (sine, None)]
        + [(gains, 1), (gate_lanes, 1), (gate_swapped, 1), (mark_q, None), (mark_k, None), (mark_t, None)],
        [((length, inner), b16, 1)] * 2
        + [((texts, inner), b16, 1), ((length, inner), b16, 1)]
        + [((length, inner), f32, 1)] * 4,
        "attend",
        micros=11,
    )

    def halves(product):
        return product(slice(0, half_rows)).astype(b16), product(slice(half_rows, None)).astype(b16)

    def all_of(block):
        return jnp.concatenate(gather_tensor(block), axis=0)

    upper, lower = halves(lambda part: jnp.dot(mixed[part], out_weight, preferred_element_type=f32))
    sums, sent = scatter_tensor(upper, lower)
    attn_rows_t = turned(attn_rows, (sent,))
    wide = ((rows, width), f32)
    narrow = ((rows, width), b16)
    totals = ((8, width), f32)
    attn_sum, middle, ffn_own = whole_call(
        middle_kernel,
        (here,),
        [block_in] + sums + [mods, norm_gains, segment],
        [wide, wide, narrow],
        "middle",
    )
    ffn_rows = all_of(ffn_own)
    gate_pre = jnp.dot(ffn_rows, gate_weight, preferred_element_type=f32)
    up_pre = jnp.dot(ffn_rows, up_weight, preferred_element_type=f32)
    sigmoid_gate = jax.nn.sigmoid(gate_pre)
    silu_gate = gate_pre * sigmoid_gate
    hidden = (silu_gate * up_pre).astype(b16)
    upper, lower = halves(lambda part: jnp.dot(hidden[part], down_weight, preferred_element_type=f32))
    sums, sent = scatter_tensor(upper, lower)
    ffn_rows_t = turned(ffn_rows, (sent,))
    block_out, grad_own, sum_gate_ffn = whole_call(
        block_out_kernel,
        (here,),
        [middle] + sums + [out_grad, mods, norm_gains, segment, member],
        [narrow, narrow, totals],
        "block_out",
    )

    grad_ffn = all_of(grad_own)
    grad_hidden = times_transpose(grad_ffn, down_weight)
    grad_gate = (
        grad_hidden * up_pre * sigmoid_gate * (1.0 + gate_pre * (1.0 - sigmoid_gate))
    ).astype(b16)
    grad_up = (grad_hidden * silu_gate).astype(b16)
    upper, lower = halves(
        lambda part: times_transpose(grad_gate[part], gate_weight)
        + times_transpose(grad_up[part], up_weight)
    )
    sums, sent = scatter_tensor(upper, lower)
    grad_ffn_t = turned(grad_ffn, (sent,))
    ffn_pairs = [(ffn_rows_t, [grad_gate, grad_up]), (grad_ffn_t, [hidden])]
    (halves_two,) = row_chunks(ffn_pairs, (2,), spot, ties=(sent,), micros=FFN_MICROS)
    ffn_passed = one_on(halves_two)
    grad_middle, grad_own, sum_scale_ffn, sum_gate_attn = whole_call(
        middle_back_kernel,
        (here,),
        [middle, attn_sum] + sums + [out_grad, mods, norm_gains, segment, member],
        [wide, narrow, totals, totals],
        "middle_back",
        micros=MIDDLE_MICROS,
    )

    grad_attn = all_of(grad_own)
    grad_mixed = times_transpose(grad_attn, out_weight).astype(b16)
    cross_grad, text_grad, text_value_grad, text_gain, gate_sum = pair_call(
        cross_back_kernel,
        [(query, 1), (text, 1), (text_value, 1), (raw_t, 1), (grad_mixed, 1), (cross_out, 1)]
        + [(cross_log, 1), (gains, 1), (mark_q, None), (mark_t, None)],
        [((length, inner), f32, 1), ((inner, texts), b16, 0), ((inner, texts), b16, 0)]
        + [((1, inner), f32, 1)] * 2,
        "cross_back",
        micros=CROSS_MICROS,
    )
    ffn_one, ffn_three, ffn_kept = row_chunks(
        ffn_pairs, (1, 3, 0), spot, extra=ffn_passed, ties=(text_grad,), micros=FFN_NEXT_MICROS
    )
    text_lefts = [text_grad, text_value_grad]
    (halves_two,) = column_chunks(text_lefts, caption_flat, (2,), spot, ties=(ffn_kept,))
    text_passed = one_on(halves_two)
    query_grad, key_grad, value_grad, head_gain = pair_call(
        self_back_kernel,
        [(query, 1), (key, 1), (value, 1), (raw_q, 1), (raw_k, 1), (grad_mixed, 1), (self_out, 1)]
        + [(self_log, 1), (cross_grad, 1), (cosine, None), (sine, None), (gains, 1)]
        + [(mark_q, None), (mark_k, None)],
        [((length, inner), b16, 1)] * 3 + [((2, inner), f32, 1)],
        "self_back",
        (halves_two[0],),
        micros=SELF_MICROS,
    )

    hidden_cols = hidden.shape[1]
    block_rows = width // BLOCKS
    got = [by_slots(part) for part in to_neighbours(ffn_kept, ffn_one, ffn_three)]
    shape = (PAIR, block_rows, 3 * hidden_cols)
    ffn_kept, ffn_sent = tiled_call(
        ffn_second_kernel,
        (spot,),
        got,
        [((2 * PAIR,) + shape[1:], b16)] * 2,
        "ffn_second",
        -1,
        4,
        (query_grad,),
    )
    upper, lower = back_call(
        [query_grad, key_grad, value_grad], [query_weight, key_weight, value_weight], "attn_back"
    )
    sums, sent = scatter_tensor(upper, lower)
    in_grad, sum_scale_attn = whole_call(
        block_in_kernel,
        (here,),
        [block_in, grad_middle] + sums + [mods, norm_gains, segment, member],
        [narrow, totals],
        "block_in",
        (ffn_sent,),
        micros=BLOCK_IN_MICROS,
    )
    (stacked,) = whole_call(
        stack_sums_kernel,
        (here,),
        [sum_scale_attn, sum_gate_attn, sum_scale_ffn, sum_gate_ffn]
        + [head_gain, text_gain, gate_sum, gate_lanes],
        [((16, width), f32)],
        "stack_sums",
    )
    attn_pairs = [
        (attn_rows_t, [query_grad, key_grad, value_grad]),
        (turned(grad_attn, (halves_two[0],)), [mixed]),
    ]
    (halves_two,) = row_chunks(attn_pairs, (2,), spot, ties=(stacked,), micros=ATTN_FIRST_MICROS)
    attn_passed = one_on(halves_two)
    stacked = gather_tensor(stacked)
    text_one, text_three, text_kept = column_chunks(
        text_lefts, caption_flat, (1, 3, 0), spot, extra=text_passed, ties=(halves_two[0],), micros=TEXT_MICROS
    )
    ffn_own, ffn_sent = tiled_call(
        ffn_middle_kernel,
        (),
        [ffn_kept, dp_permute(ffn_sent, "second", "flip")],
        [(shape, b16)] * 2,
        "ffn_middle",
        -1,
        2,
        (text_kept,) + tuple(attn_passed),
    )
    (riders,) = whole_call(
        pack_kernel,
        (here,),
        stacked + [mods, norm_gains, cond_rows],
        [((rider_rows(1), width), b16)],
        "pack",
        (ffn_sent,),
        micros=PACK_MICROS,
    )
    (riders,) = whole_call(
        functools.partial(merge_kernel, 1),
        (),
        [riders, dp_permute(riders, "z", 1)],
        [((rider_rows(PAIR), width), b16)],
        "merge",
    )
    opposite = dp_permute(riders, "first", 2)
    ffn_own_kept, ffn_own_sent = tiled_call(
        ffn_third_kernel,
        (spot,),
        [ffn_own, dp_permute(ffn_sent, "second", "mirror")],
        [(shape[1:], b16)] * 2,
        "ffn_third",
        -1,
        2,
        (riders,),
    )
    attn_one, attn_three, attn_kept = row_chunks(
        attn_pairs, (1, 3, 0), spot, extra=attn_passed, riders=(riders,), ties=(ffn_own_sent,), micros=ATTN_MICROS
    )
    text_rows = caption_flat.shape[1] // BLOCKS
    text_own, text_sent = tiled_call(
        text_second_kernel,
        (spot,),
        to_neighbours(text_kept, text_one, text_three),
        [((2 * inner, 2 * PAIR * text_rows), b16)] * 2,
        "text_second",
        0,
        4,
        (opposite,),
        micros=SECOND_MICROS,
    )
    stage = tiled_call(
        functools.partial(attn_second_kernel, block_rows),
        (spot,),
        [riders, opposite] + to_neighbours(attn_kept, attn_one, attn_three),
        [((PAIR * block_rows + rider_rows(4 * PAIR), width), b16)] * RING,
        "attn_second",
        -1,
        4,
        (text_sent,),
    )
    text_own, text_sent = tiled_call(
        text_middle_kernel,
        (),
        [text_own, dp_permute(text_sent, "second", "flip")],
        [((2 * inner, PAIR * text_rows), b16)] * 2,
        "text_middle",
        0,
        2,
        (stage[0],),
    )
    got = exchange(stage, "second")
    kept, sent = tiled_call(
        attn_third_kernel, (spot,), got, [((block_rows, width), b16)] * 2, "attn_third",
        -1,
        2
    )
    gate_sum_out, up_sum_out, down_sum_out = whole_call(
        ffn_last_kernel,
        (),
        exchange([ffn_own_kept, ffn_own_sent], "z"),
        [((block_rows, hidden_cols), f32)] * 2 + [((hidden_cols, block_rows), f32)],
        "ffn_last",
        (kept,),
    )
    text_own_kept, text_own_sent = tiled_call(
        text_third_kernel,
        (spot,),
        [text_own, dp_permute(text_sent, "second", "mirror")],
        [((2 * inner, text_rows), b16)] * 2,
        "text_third",
        0,
        2,
        (kept,),
    )
    textkey_sum, textvalue_sum = whole_call(
        text_last_kernel,
        (),
        exchange([text_own_kept, text_own_sent], "z"),
        [((text_rows, inner), f32)] * 2,
        "text_last",
    )
    ada_grad, norm_grads, head_grads, crossgate = tiled_call(
        functools.partial(ada_kernel, 4 * PAIR, heads),
        (lax.axis_index("dp").reshape(1),),
        got,
        [((condition.shape[1] // BLOCKS, width), f32), ((4, width), f32), ((3, HEAD), f32)]
        + [((1, LANES), f32)],
        "ada",
        0,
        1,
        (kept,),
    )
    crossgate_grad = crossgate[0, :HEADS]
    query_sum, key_sum, value_sum, outw_sum = whole_call(
        attn_last_kernel,
        (),
        exchange([kept, sent], "z"),
        [((block_rows, inner), f32)] * 3 + [((inner, block_rows), f32)],
        "attn_last",
    )
    return (
        block_out,
        in_grad,
        ada_grad,
        norm_grads,
        query_sum,
        key_sum,
        value_sum,
        head_grads,
        textkey_sum,
        textvalue_sum,
        crossgate_grad,
        outw_sum,
        gate_sum_out,
        up_sum_out,
        down_sum_out,
    )


def solution(mesh):
    return jax.shard_map(
        shards,
        mesh=mesh,
        in_specs=(
            P(("dp", "tensor"), None),
            P(("dp", "tensor"), None),
            P("dp", None),
            P("dp", None, None),
            P("dp"),
            P("dp"),
            P(None, "tensor"),
            P(),
            P(None, "tensor"),
            P(None, "tensor"),
            P(None, "tensor"),
            P(),
            P(None, "tensor"),
            P(None, "tensor"),
            P("tensor"),
            P("tensor", None),
            P(None, "tensor"),
            P(None, "tensor"),
            P("tensor", None),
        ),
        out_specs=(
            P(("dp", "tensor"), None),
            P(("dp", "tensor"), None),
            P("dp", "tensor"),
            P(),
            P("dp", "tensor"),
            P("dp", "tensor"),
            P("dp", "tensor"),
            P(),
            P("dp", "tensor"),
            P("dp", "tensor"),
            P(),
            P("tensor", "dp"),
            P("dp", "tensor"),
            P("dp", "tensor"),
            P("tensor", "dp"),
        ),
        check_vma=False,
    )
```

```python
import functools
import math

import jax
import jax.numpy as jnp
from jax import lax
from jax.experimental import pallas as pl
from jax.experimental.pallas import tpu as pltpu
from jax.sharding import PartitionSpec as P

HEAD = 64
HEADS = 24
TXT = 256
SEGS = 3
EPS = 1e-06
LANES = 2 * HEAD
SHUT = 256.0
ROOT = HEAD ** (-0.5)
VMEM_LIMIT = 16 * 2**20
NO_COST = pl.CostEstimate(flops=0, bytes_accessed=0, transcendentals=0)


def cost_of(micros):
    return pl.CostEstimate(flops=int(micros * 1e9), bytes_accessed=0, transcendentals=0)


SUM_ROWS = 6
CROSS_MICROS = 10
BLOCK_IN_MICROS = 10
FFN_MICROS = 3
FFN_NEXT_MICROS = 8
MIDDLE_MICROS = 10
SELF_MICROS = 0
ATTN_MICROS = 3
TEXT_MICROS = 8
PACK_MICROS = 0
SECOND_MICROS = 8
ATTN_FIRST_MICROS = 0

RING = 4
PAIR = 2
BLOCKS = RING * PAIR * RING
SLOTS = BLOCKS // RING
SEND_ORDER = (2, 1, 3, 0)
CORE_SWAP = [(0, 1), (1, 0), (2, 3), (3, 2)]
CHIP_SWAP = [(0, 2), (2, 0), (1, 3), (3, 1)]
ROW_ORDER = (0, 2, 1, 3)

def dp_index(x, z, y):
    return (x * PAIR + z) * RING + y


def dp_perm(axis, step):
    pairs = []

    def moved(place, size):
        if step == "flip":
            return place ^ 1
        if step == "mirror":
            return size - 1 - place
        return (place + step) % size

    for x in range(RING):
        for z in range(PAIR):
            for y in range(RING):
                for tensor in range(2 * PAIR):
                    way = axis
                    if axis in ("first", "second"):
                        way = "x" if (tensor % 2 == 0) == (axis == "first") else "y"
                    target = {
                        "x": (moved(x, RING), z, y),
                        "y": (x, z, moved(y, RING)),
                        "z": (x, moved(z, PAIR), y),
                    }[way]
                    pairs.append(
                        (
                            dp_index(x, z, y) * 2 * PAIR + tensor,
                            dp_index(*target) * 2 * PAIR + tensor,
                        )
                    )
    return pairs


def dp_permute(values, axis, step):
    return lax.ppermute(values, ("dp", "tensor"), dp_perm(axis, step))


def dp_spot(position):
    index = lax.axis_index("dp")
    x, z, y = index // (RING * PAIR), index // RING % PAIR, index % RING
    core = position % 2
    return jnp.stack([jnp.where(core == 0, x, y), z, jnp.where(core == 0, y, x), core])


def swap_core(values):
    return lax.ppermute(values, "tensor", CORE_SWAP)


def swap_chip(values):
    return lax.ppermute(values, "tensor", CHIP_SWAP)


def times_transpose(left, right):
    return lax.dot_general(
        left, right, (((1,), (1,)), ((), ())), preferred_element_type=jnp.float32
    )


def gather_tensor(block):
    far = swap_chip(block)
    near = swap_core(block)
    return [block, far, near, swap_core(far)]


def scatter_tensor(upper, lower):
    near = swap_core(lower)
    rows = upper.shape[0] // 2
    far = (upper[rows:].astype(jnp.float32) + near[rows:].astype(jnp.float32)).astype(near.dtype)
    return [upper, near, swap_chip(far)], far


def turn_kernel(source, target):
    target[...] = source[...].T


def turned(values, ties=()):
    tile = 512 if values.shape[1] % 512 == 0 else values.shape[1]
    return pl.pallas_call(
        lambda source, *rest: turn_kernel(source, rest[-1]),
        grid=(values.shape[1] // tile,),
        in_specs=[pl.BlockSpec((values.shape[0], tile), lambda step: (0, step))]
        + [pl.BlockSpec(memory_space=pl.ANY)] * len(ties),
        out_specs=pl.BlockSpec((tile, values.shape[0]), lambda step: (step, 0)),
        out_shape=jax.ShapeDtypeStruct(values.shape[::-1], values.dtype),
        compiler_params=pltpu.CompilerParams(vmem_limit_bytes=VMEM_LIMIT),
        cost_estimate=NO_COST,
    )(values, *ties)


def chunk_block(offset, slot, spot):
    first = (spot[0] + offset) % RING
    z, second = slot // RING, slot % RING
    x = jnp.where(spot[3] == 0, first, second)
    y = jnp.where(spot[3] == 0, second, first)
    return dp_index(x, z, y)


def offset_of_step(offsets, step):
    offset = offsets[-1]
    for place in range(len(offsets) - 1):
        offset = jnp.where(step == place, offsets[place], offset)
    return offset


def chunk_kernel(make, offsets, halves, extra, outs, held, sems):
    step = pl.program_id(0)
    first, second = halves

    def copies(place):
        slot = held.at[place % 2]
        if offsets[place] != 2:
            return [pltpu.make_async_copy(slot, outs[place], sems.at[place % 2, 0])]
        return [
            pltpu.make_async_copy(slot.at[half], out, sems.at[place % 2, way])
            for way, (half, out) in enumerate(zip((first, second), outs[place]))
        ]

    for place, offset in enumerate(offsets):

        @pl.when(step == place)
        def _(place=place, offset=offset):
            if place >= 2:
                for copy in copies(place - 2):
                    copy.wait()
            added = {1: (first, extra[0]), 3: (second, extra[1])}.get(offset) if extra else None
            make(held.at[place % 2], added, offset)
            for copy in copies(place):
                copy.start()
            if place == len(offsets) - 1:
                for last in range(max(place - 1, 0), place + 1):
                    for copy in copies(last):
                        copy.wait()


def chunk_call(make, operands, specs, offsets, halves, shape, spot, extra, ties, name, micros):
    count = len(operands)
    pieces = []
    for offset in offsets:
        if offset == 2:
            pieces += [tuple(len(range(*s.indices(d))) for s, d in zip(h, shape)) for h in halves]
        else:
            pieces.append(shape)

    def kernel(spot_ref, *refs):
        inputs, extras = refs[:count], refs[count : count + len(extra)]
        outs = list(refs[-len(pieces) - 2 : -2])
        grouped = []
        for offset in offsets:
            grouped.append((outs.pop(0), outs.pop(0)) if offset == 2 else outs.pop(0))
        chunk_kernel(
            functools.partial(make, inputs), offsets, halves, extras, grouped, refs[-2], refs[-1]
        )

    found = pl.pallas_call(
        kernel,
        grid_spec=pltpu.PrefetchScalarGridSpec(
            num_scalar_prefetch=1,
            grid=(len(offsets),),
            in_specs=list(specs)
            + [pl.BlockSpec(part.shape, lambda step, spot: (0, 0)) for part in extra]
            + [pl.BlockSpec(memory_space=pl.ANY)] * len(ties),
            out_specs=[pl.BlockSpec(memory_space=pl.ANY)] * len(pieces),
            scratch_shapes=[
                pltpu.VMEM((2,) + shape, jnp.bfloat16),
                pltpu.SemaphoreType.DMA((2, 2)),
            ],
        ),
        out_shape=[jax.ShapeDtypeStruct(piece, jnp.bfloat16) for piece in pieces],
        compiler_params=pltpu.CompilerParams(vmem_limit_bytes=VMEM_LIMIT),
        cost_estimate=cost_of(micros),
        name=name,
    )(spot, *operands, *extra, *ties)
    found = list(found)
    return [
        (found.pop(0), found.pop(0)) if offset == 2 else found.pop(0) for offset in offsets
    ]


def make_rows(groups, inputs, slot, added, offset):
    lefts, rights = inputs[: SLOTS * len(groups)], inputs[SLOTS * len(groups) :]
    size = SLOTS * lefts[0].shape[1]
    if len(rights) > sum(groups):
        slot[size:, :] = rights[-1][...]
    column = place = 0
    for group, count in enumerate(groups):
        rows = jnp.concatenate(
            [left[0] for left in lefts[SLOTS * group : SLOTS * (group + 1)]], axis=0
        )
        for right in rights[place : place + count]:
            wide = right.shape[1]
            product = dot(rows, right[...])
            low, high = column, column
            if added is not None:
                low = min(max(column, added[0][1].start), column + wide)
                high = min(max(column, added[0][1].stop), column + wide)
            for start, stop in ((column, low), (low, high), (high, column + wide)):
                if start < stop:
                    part = product[:, start - column : stop - column]
                    if (start, stop) == (low, high):
                        base = added[0][1].start
                        part = part + added[1][:size, start - base : stop - base].astype(jnp.float32)
                    slot[:size, start:stop] = part.astype(jnp.bfloat16)
            column += wide
        place += count


def row_chunks(pairs, offsets, spot, extra=(), ties=(), micros=0, riders=()):
    lefts = [left.reshape(BLOCKS, left.shape[0] // BLOCKS, left.shape[1]) for left, _ in pairs]
    rights = [right for _, group in pairs for right in group]
    total = sum(right.shape[1] for right in rights)
    specs, operands = [], []
    for left in lefts:
        for slot in range(SLOTS):
            specs.append(
                pl.BlockSpec(
                    (1,) + left.shape[1:],
                    lambda step, spot, slot=slot: (
                        chunk_block(offset_of_step(offsets, step), slot, spot),
                        0,
                        0,
                    ),
                )
            )
            operands.append(left)
    specs += [pl.BlockSpec(right.shape, lambda step, spot: (0, 0)) for right in rights]
    specs += [pl.BlockSpec(part.shape, lambda step, spot: (0, 0)) for part in riders]
    rows = SLOTS * lefts[0].shape[1] + sum(part.shape[0] for part in riders)
    halves = [(slice(0, rows), slice(0, total // 2)), (slice(0, rows), slice(total // 2, total))]
    return chunk_call(
        functools.partial(make_rows, [len(group) for _, group in pairs]),
        operands + rights + list(riders),
        specs,
        offsets,
        halves,
        (rows, total),
        spot,
        extra,
        ties,
        "row_chunks",
        micros,
    )


def make_columns(lefts, inputs, slot, added, offset):
    whole = jnp.concatenate([right[...] for right in inputs[lefts:]], axis=1)
    row = 0
    for left in inputs[:lefts]:
        product = dot(left[...], whole)
        if added is not None and added[0][0].start == row:
            product = product + added[1][...].astype(jnp.float32)
        slot[row : row + left.shape[0], :] = product.astype(jnp.bfloat16)
        row += left.shape[0]


def column_chunks(lefts, right, offsets, spot, extra=(), ties=(), micros=0):
    rows = lefts[0].shape[0]
    depth, columns = right.shape
    specs = [pl.BlockSpec(left.shape, lambda step, spot: (0, 0)) for left in lefts]
    for slot in range(SLOTS):
        specs.append(
            pl.BlockSpec(
                (depth, columns // BLOCKS),
                lambda step, spot, slot=slot: (
                    0,
                    chunk_block(offset_of_step(offsets, step), slot, spot),
                ),
            )
        )
    lanes = columns // RING
    halves = [(slice(0, rows), slice(0, lanes)), (slice(rows, 2 * rows), slice(0, lanes))]
    return chunk_call(
        functools.partial(make_columns, len(lefts)),
        list(lefts) + [right] * SLOTS,
        specs,
        offsets,
        halves,
        (2 * rows, lanes),
        spot,
        extra,
        ties,
        "column_chunks",
        micros,
    )


def add_up(refs, index):
    total = refs[0][index].astype(jnp.float32)
    for ref in refs[1:]:
        total = total + ref[index].astype(jnp.float32)
    return total


def lane_slice(start, size):
    return (slice(None), pl.ds(pl.multiple_of(start * size, size), size))


def halving_places(spot):
    own = spot[2]
    other = own ^ 1
    return (own, RING - 1 - own), (other, RING - 1 - other)


def ffn_second_kernel(spot, *refs):
    parts = refs[:-2]
    for out, places in zip(refs[-2:], halving_places(spot)):
        for index, place in enumerate(places):
            for z in range(PAIR):
                out[index * PAIR + z] = add_up(parts, z * RING + place).astype(jnp.bfloat16)


def ffn_middle_kernel(kept, got, own, sent):
    for out, start in ((own, 0), (sent, PAIR)):
        for z in range(PAIR):
            out[z] = add_up((kept, got), start + z).astype(jnp.bfloat16)


def ffn_third_kernel(spot, *refs):
    for out, z in ((refs[-2], spot[1]), (refs[-1], (spot[1] + 1) % PAIR)):
        out[...] = add_up(refs[:-2], z).astype(jnp.bfloat16)


def ffn_last_kernel(kept, got, gate_out, up_out, down_out):
    total = kept[...].astype(jnp.float32) + got[...].astype(jnp.float32)
    hidden = gate_out.shape[1]
    gate_out[...] = total[:, :hidden]
    up_out[...] = total[:, hidden : 2 * hidden]
    down_out[...] = total[:, 2 * hidden :].T


def text_second_kernel(spot, *refs):
    parts = refs[:-2]
    lanes = parts[0].shape[1] // SLOTS
    for out, places in zip(refs[-2:], halving_places(spot)):
        for index, place in enumerate(places):
            for z in range(PAIR):
                start = (index * PAIR + z) * lanes
                out[:, start : start + lanes] = add_up(
                    parts, lane_slice(z * RING + place, lanes)
                ).astype(jnp.bfloat16)


def text_middle_kernel(kept, got, own, sent):
    wide = own.shape[1]
    for out, start in ((own, 0), (sent, wide)):
        index = (slice(None), slice(start, start + wide))
        out[...] = add_up((kept, got), index).astype(jnp.bfloat16)


def text_third_kernel(spot, *refs):
    lanes = refs[-1].shape[1]
    for out, z in ((refs[-2], spot[1]), (refs[-1], (spot[1] + 1) % PAIR)):
        out[...] = add_up(refs[:-2], lane_slice(z, lanes)).astype(jnp.bfloat16)


def text_last_kernel(kept, got, textkey, textvalue):
    total = kept[...].astype(jnp.float32) + got[...].astype(jnp.float32)
    columns = textkey.shape[1]
    textkey[...] = total[:columns].T
    textvalue[...] = total[columns:].T


def attn_second_kernel(rows, spot, riders, opposite, *refs):
    parts, outs = refs[:-RING], refs[-RING:]
    size = SLOTS * rows
    for offset in range(RING):
        for z in range(PAIR):
            slot = z * RING + (spot[2] + offset) % RING
            index = (pl.ds(pl.multiple_of(slot * rows, 16), rows), slice(None))
            outs[offset][z * rows : (z + 1) * rows, :] = add_up(parts, index).astype(jnp.bfloat16)
    pairs = ((riders[...], parts[1][size:, :]), (opposite[...], parts[2][size:, :]))
    joined = [merge_rows(PAIR, first, second, rider_rows(2 * PAIR)) for first, second in pairs]
    joined = merge_rows(2 * PAIR, joined[0], joined[1], rider_rows(4 * PAIR))
    for out in outs:
        out[PAIR * rows :, :] = joined


def attn_third_kernel(spot, *refs):
    rows = refs[-1].shape[0]
    for out, z in ((refs[-2], spot[1]), (refs[-1], (spot[1] + 1) % PAIR)):
        index = (pl.ds(pl.multiple_of(z * rows, 16), rows), slice(None))
        out[...] = add_up(refs[:RING], index).astype(jnp.bfloat16)


def attn_last_kernel(kept, got, query, key, value, outw):
    total = kept[...].astype(jnp.float32) + got[...].astype(jnp.float32)
    columns = query.shape[1]
    for place, out in enumerate((query, key, value)):
        out[...] = total[:, place * columns : (place + 1) * columns]
    outw[...] = total[:, 3 * columns :].T


def whole_call(kernel, scalars, operands, outs, name, ties=(), scratch=(), micros=0):
    whole = pl.BlockSpec(memory_space=pltpu.VMEM)
    count = len(scalars) + len(operands)
    return pl.pallas_call(
        lambda *refs: kernel(*refs[:count], *refs[count + len(ties) :]),
        in_specs=[pl.BlockSpec(memory_space=pltpu.SMEM)] * len(scalars)
        + [whole] * len(operands)
        + [pl.BlockSpec(memory_space=pl.ANY)] * len(ties),
        out_specs=[whole] * len(outs),
        out_shape=[jax.ShapeDtypeStruct(shape, kind) for shape, kind in outs],
        scratch_shapes=list(scratch),
        compiler_params=pltpu.CompilerParams(vmem_limit_bytes=VMEM_LIMIT),
        cost_estimate=cost_of(micros),
        name=name,
    )(*scalars, *operands, *ties)


def tiled_call(kernel, scalars, operands, outs, name, axis, tiles, ties=(), micros=0, axes=None):
    def spec(shape, axis):
        block = list(shape)
        block[axis] //= tiles
        if axis == 0:
            return pl.BlockSpec(tuple(block), lambda step: (step,) + (0,) * (len(shape) - 1))
        return pl.BlockSpec(tuple(block), lambda step: (0,) * (len(shape) - 1) + (step,))

    count = len(scalars) + len(operands)
    return pl.pallas_call(
        lambda *refs: kernel(*refs[:count], *refs[count + len(ties) :]),
        grid=(tiles,),
        in_specs=[pl.BlockSpec(memory_space=pltpu.SMEM)] * len(scalars)
        + [spec(part.shape, way) for part, way in zip(operands, axes or [axis] * len(operands))]
        + [pl.BlockSpec(memory_space=pl.ANY)] * len(ties),
        out_specs=[spec(shape, axis) for shape, _ in outs],
        out_shape=[jax.ShapeDtypeStruct(shape, kind) for shape, kind in outs],
        compiler_params=pltpu.CompilerParams(vmem_limit_bytes=VMEM_LIMIT),
        cost_estimate=cost_of(micros),
        name=name,
    )(*scalars, *[pltpu.with_memory_space_constraint(part, pltpu.HBM) for part in operands], *ties)


def exchange(chunks, axis):
    return [chunks[0]] + [
        dp_permute(chunks[step], axis, step) for step in range(1, len(chunks))
    ]


def one_on(halves):
    return dp_permute(halves[0], "first", 1), dp_permute(halves[1], "first", RING - 1)


def to_neighbours(own, ahead, behind):
    return [own, dp_permute(ahead, "first", 1), dp_permute(behind, "first", RING - 1)]


def by_slots(chunk):
    return chunk.reshape(SLOTS, chunk.shape[0] // SLOTS, chunk.shape[1])


def lane_index(shape):
    return lax.broadcasted_iota(jnp.int32, shape, 1)


def head_lanes(shape, head):
    lane = lane_index(shape)
    return (lane < HEAD) if head == 0 else (lane >= HEAD)


def per_head(values, reduce):
    first = head_lanes(values.shape, 0)
    left = jnp.sum(jnp.where(first, values, 0.0), axis=1, keepdims=True)
    right = jnp.sum(jnp.where(first, 0.0, values), axis=1, keepdims=True)
    return jnp.where(first, left, right)


def head_units(raw):
    inverse = lax.rsqrt(per_head(raw * raw, None) * (1.0 / HEAD) + EPS)
    return raw * inverse, inverse


def partner(values):
    lane = lane_index(values.shape)
    return jnp.where(
        lane % HEAD < HEAD // 2,
        pltpu.roll(values, LANES - HEAD // 2, 1),
        pltpu.roll(values, HEAD // 2, 1),
    )


def dot(left, right):
    return jnp.dot(left, right, preferred_element_type=jnp.float32)


def dot_t(left, right):
    return lax.dot_general(left, right, (((1,), (1,)), ((), ())), preferred_element_type=jnp.float32)


def attend_kernel(
    raw_q, raw_k, value, raw_t, text_value, cosine, sine, gains, gate, gate_swapped, mark_q, mark_k, mark_t,
    query_out, key_out, text_out, mixed_out, self_out, cross_out, self_log, cross_log,
):
    cos, sin = cosine[...], sine[...]
    unit = head_units(raw_q[...])[0] * gains[0:1, :]
    query = ((unit * cos + partner(unit) * sin).astype(jnp.bfloat16) * ROOT).astype(jnp.bfloat16)
    unit = head_units(raw_k[...])[0] * gains[1:2, :]
    key = (unit * cos + partner(unit) * sin).astype(jnp.bfloat16)
    text = (head_units(raw_t[...])[0] * gains[2:3, :]).astype(jnp.bfloat16)
    query_out[...] = query
    key_out[...] = key
    text_out[...] = text

    def attention(keys, marks, values):
        outs, sums = [], []
        for head in range(2):
            own = head_lanes(query.shape, head)
            own_keys = head_lanes(keys.shape, head)
            probe = jnp.where(own, query, mark_q[...])
            scores = dot_t(probe, jnp.where(own_keys, keys, marks))
            weights = jnp.exp(scores).astype(jnp.bfloat16)
            both = dot(weights, jnp.where(own_keys, values, jnp.ones_like(values)))
            outs.append(both)
        first = head_lanes(outs[0].shape, 0)
        product = jnp.where(first, outs[0], outs[1])
        total = jnp.where(first, outs[1], outs[0])
        return product / pltpu.roll(total, HEAD, 1), jnp.log(total)

    out, log = attention(key, mark_k[...], value[...])
    self_out[...] = out
    self_log[...] = log
    cross, log = attention(text, mark_t[...], text_value[...])
    cross_out[...] = cross
    cross_log[...] = log - jnp.log(gate_swapped[...])
    mixed_out[...] = (out + gate[...] * cross).astype(jnp.bfloat16)


def attention_grads(query, keys, marks, values, grad, out, log, mark_q):
    rows = grad.astype(jnp.float32)
    delta = per_head(rows * out, None)
    delta = pltpu.roll(delta, HEAD, 1)
    lane = lane_index(query.shape) % HEAD
    log_high = log.astype(jnp.bfloat16)
    log_low = (log - log_high.astype(jnp.float32)).astype(jnp.bfloat16)
    delta_high = delta.astype(jnp.bfloat16)
    delta_low = (delta - delta_high.astype(jnp.float32)).astype(jnp.bfloat16)
    zero = jnp.zeros_like(query)
    code = jnp.where(lane == 4, -log_high, jnp.where(lane == 5, -log_low, mark_q))
    shift = jnp.where(lane == 4, -delta_high, jnp.where(lane == 5, -delta_low, zero))
    key_grads, value_grads, query_grads = [], [], []
    for head in range(2):
        own = head_lanes(query.shape, head)
        own_keys = head_lanes(keys.shape, head)
        probe = jnp.where(own, query, code)
        probs = jnp.exp(dot_t(jnp.where(own_keys, keys, marks), probe))
        slope = dot_t(jnp.where(own_keys, values, marks), jnp.where(own, grad, shift))
        score_grad = (probs * slope).astype(jnp.bfloat16)
        value_grads.append(dot(probs.astype(jnp.bfloat16), grad))
        key_grads.append(dot(score_grad, query))
        turned = keys[:, head * HEAD : (head + 1) * HEAD].T
        query_grads.append(dot(turned, score_grad))
    first = head_lanes(keys.shape, 0)
    return (
        jnp.concatenate(query_grads, axis=0),
        jnp.where(first, key_grads[0], key_grads[1]),
        jnp.where(first, value_grads[0], value_grads[1]),
    )


def norm_back(weighted, unit, inverse):
    return inverse * (weighted - unit * (per_head(weighted * unit, None) * (1.0 / HEAD)))


def cross_back_kernel(
    query, text, text_value, raw_t, grad, out, log, gains, mark_q, mark_t,
    query_grad, raw_grad, value_grad, gain_sum, gate_sum,
):
    grad_q, grad_t, grad_v = attention_grads(
        query[...], text[...], mark_t[...], text_value[...], grad[...], out[...], log[...], mark_q[...]
    )
    query_grad[...] = grad_q.T
    value_grad[...] = grad_v.astype(jnp.bfloat16).T
    grad_t = grad_t.astype(jnp.bfloat16).astype(jnp.float32)
    unit, inverse = head_units(raw_t[...])
    gain_sum[...] = jnp.sum(grad_t * unit, axis=0, keepdims=True)
    raw_grad[...] = norm_back(grad_t * gains[2:3, :], unit, inverse).astype(jnp.bfloat16).T
    gate_sum[...] = jnp.sum(grad[...].astype(jnp.float32) * out[...], axis=0, keepdims=True)


def self_back_kernel(
    query, key, value, raw_q, raw_k, grad, out, log, cross_grad, cosine, sine, gains, mark_q, mark_k,
    query_grad, key_grad, value_grad, gain_sum,
):
    grad_q, grad_k, grad_v = attention_grads(
        query[...], key[...], mark_k[...], value[...], grad[...], out[...], log[...], mark_q[...]
    )
    value_grad[...] = grad_v.astype(jnp.bfloat16)
    cos, sin = cosine[...], sine[...]
    grad_q = (grad_q.T + cross_grad[...]) * ROOT
    for turn, raw, row, target in ((grad_q, raw_q, 0, query_grad), (grad_k, raw_k, 1, key_grad)):
        turn = turn.astype(jnp.bfloat16).astype(jnp.float32)
        turn = turn * cos - partner(turn) * sin
        unit, inverse = head_units(raw[...])
        gain_sum[row : row + 1, :] = jnp.sum(turn * unit, axis=0, keepdims=True)
        target[...] = norm_back(turn * gains[row : row + 1, :], unit, inverse).astype(jnp.bfloat16)


def pair_call(kernel, operands, outs, name, ties=(), micros=0):
    def spec(shape, cut):
        if cut is None:
            return pl.BlockSpec(shape, lambda pair: (0, 0))
        if cut == 1:
            return pl.BlockSpec((shape[0], LANES), lambda pair: (0, pair))
        return pl.BlockSpec((LANES, shape[1]), lambda pair: (pair, 0))

    width = outs[0][0][0] if outs[0][2] == 0 else outs[0][0][1]
    return pl.pallas_call(
        lambda *refs: kernel(*refs[: len(operands)], *refs[len(operands) + len(ties) :]),
        grid=(width // LANES,),
        in_specs=[spec(part.shape, cut) for part, cut in operands]
        + [pl.BlockSpec(memory_space=pl.ANY)] * len(ties),
        out_specs=[spec(shape, cut) for shape, _, cut in outs],
        out_shape=[jax.ShapeDtypeStruct(shape, kind) for shape, kind, _ in outs],
        compiler_params=pltpu.CompilerParams(vmem_limit_bytes=VMEM_LIMIT),
        cost_estimate=cost_of(micros),
        name=name,
    )(*[part for part, _ in operands], *ties)
def inverse_rms(values):
    return lax.rsqrt(jnp.mean(values * values, axis=-1, keepdims=True) + EPS)


def row_norm_back(weighted, unit, inverse):
    return inverse * (weighted - unit * jnp.mean(weighted * unit, axis=-1, keepdims=True))


def per_row(table, segment):
    return jnp.where(segment == 0.0, table[0:1], jnp.where(segment == 1.0, table[1:2], table[2:3]))


def total_of(parts):
    upper, near, far = parts
    rows = far.shape[0]
    return (
        upper[:rows].astype(jnp.float32) + near[:rows].astype(jnp.float32) + far[...].astype(jnp.float32)
    )


def segment_sums(member, values):
    high = values.astype(jnp.bfloat16)
    low = (values - high.astype(jnp.float32)).astype(jnp.bfloat16)
    return dot(member, high) + dot(member, low)


def tables_kernel(here, lens, gate, segments, head_gains, cosine, sine, mark_q, mark_k, mark_t,
                  segment, member, gate_lanes, gate_swapped, gains):
    heads = gains.shape[1] // HEAD
    lane = lane_index(gate_lanes.shape) // HEAD
    line = jnp.zeros(gate_lanes.shape, jnp.float32)
    swapped = line
    for head in range(heads):
        line = jnp.where(lane == head, gate[head], line)
        swapped = jnp.where(lane == head ^ 1, gate[head], swapped)
    gate_lanes[...] = jnp.tanh(line)
    gate_swapped[...] = jnp.tanh(swapped)
    gains[...] = jnp.concatenate([head_gains[...]] * heads, axis=1)
    rows = segments.shape[1]
    ids = segments[...]
    first = jnp.sum((ids < 1).astype(jnp.float32))
    second = jnp.sum((ids < 2).astype(jnp.float32))
    lane = lane_index((rows, LANES))
    half = HEAD // 2
    rate = jnp.exp((lane % half).astype(jnp.float32) * (-2.0 * math.log(10000.0) / HEAD))
    within = lane % HEAD
    for block, code in enumerate(ROW_ORDER):
        source = here[0] ^ code
        line = segments[pl.ds(source, 1), :].astype(jnp.float32)
        label = jnp.broadcast_to(line, (rows, rows)).T
        start = jnp.where(label == 0.0, 0.0, jnp.where(label == 1.0, first, second))
        token = (lax.broadcasted_iota(jnp.int32, (rows, LANES), 0) + source * rows).astype(jnp.float32)
        angle = (token - start) * rate
        index = slice(block * rows, (block + 1) * rows)
        cosine[index, :] = jnp.cos(angle)
        sine[index, :] = jnp.where(within < half, -1.0, 1.0) * jnp.sin(angle)
        same = ((label == within.astype(jnp.float32)) & (within < SEGS)).astype(jnp.float32)
        shut = (within == SEGS).astype(jnp.float32)
        ones = ((within >= SEGS) & (within < SEGS + 3)).astype(jnp.float32)
        mark_q[index, :] = (SHUT * same - SHUT * shut).astype(jnp.bfloat16)
        mark_k[index, :] = (same + ones).astype(jnp.bfloat16)
        if block == 0:
            segment[...] = label
            member[...] = (
                lax.broadcasted_iota(jnp.int32, (8, rows), 0).astype(jnp.float32) == line
            ).astype(jnp.bfloat16)
    for group in range(SEGS):
        lane = lane_index((TXT, LANES)) % HEAD
        row = lax.broadcasted_iota(jnp.int32, (TXT, LANES), 0)
        inside = ((lane == group) & (row < lens[group])).astype(jnp.float32)
        ones = ((lane >= SEGS) & (lane < SEGS + 3)).astype(jnp.float32)
        mark_t[group * TXT : (group + 1) * TXT, :] = (inside + ones).astype(jnp.bfloat16)


def text_kernel(captions, key_weight, value_weight, raw_out, value_out, raw_sum, value_sum):
    step = pl.program_id(0)

    @pl.when(step == 0)
    def _():
        raw_sum[...] = dot(captions[...], key_weight[...])
        value_sum[...] = dot(captions[...], value_weight[...])

    @pl.when(step > 0)
    def _():
        raw_sum[...] += dot(captions[...], key_weight[...])
        value_sum[...] += dot(captions[...], value_weight[...])

    @pl.when(step == pl.num_programs(0) - 1)
    def _():
        raw_out[...] = raw_sum[...]
        value_out[...] = value_sum[...].astype(jnp.bfloat16)


def text_call(captions, key_weight, value_weight):
    rows, depth = captions.shape
    columns = key_weight.shape[1]
    tile = depth // 4
    return pl.pallas_call(
        text_kernel,
        grid=(depth // tile,),
        in_specs=[
            pl.BlockSpec((rows, tile), lambda step: (0, step)),
            pl.BlockSpec((tile, columns), lambda step: (step, 0)),
            pl.BlockSpec((tile, columns), lambda step: (step, 0)),
        ],
        out_specs=[pl.BlockSpec((rows, columns), lambda step: (0, 0))] * 2,
        out_shape=[
            jax.ShapeDtypeStruct((rows, columns), jnp.float32),
            jax.ShapeDtypeStruct((rows, columns), jnp.bfloat16),
        ],
        scratch_shapes=[pltpu.VMEM((rows, columns), jnp.float32)] * 2,
        compiler_params=pltpu.CompilerParams(vmem_limit_bytes=VMEM_LIMIT),
        cost_estimate=cost_of(9),
        name="text",
    )(*[pltpu.with_memory_space_constraint(part, pltpu.HBM) for part in (captions, key_weight, value_weight)])


def project_kernel(here, own, far, near, last, mods, gains, segment_q, query_w, key_w, value_w,
                   rows_out, raw_q, raw_k, value):
    table = mods[here[0]]
    rows = own.shape[0]
    for block, part in enumerate((own, far, near, last)):
        index = slice(block * rows, (block + 1) * rows)
        values = part[...].astype(jnp.float32)
        marks = segment_q[index, :].astype(jnp.float32)
        scale = jnp.where(
            marks[:, 0:1] > 0.0, table[0:1], jnp.where(marks[:, 1:2] > 0.0, table[1:2], table[2:3])
        )
        rows_out[index, :] = (
            values * inverse_rms(values) * gains[0:1] * (1.0 + scale)
        ).astype(jnp.bfloat16)
    raw_q[...] = dot(rows_out[...], query_w[...])
    raw_k[...] = dot(rows_out[...], key_w[...])
    value[...] = dot(rows_out[...], value_w[...]).astype(jnp.bfloat16)


def middle_kernel(here, block, upper, near, far, mods, gains, segment, attn_out, middle_out, rows_out):
    attn_sum = total_of((upper, near, far))
    label = segment[:, 0:1]
    factor = jnp.tanh(per_row(mods[here[0] ^ 1], label)) * gains[1:2]
    middle = block[...].astype(jnp.float32) + factor * (attn_sum * inverse_rms(attn_sum))
    attn_out[...] = attn_sum
    middle_out[...] = middle
    scale = per_row(mods[here[0] ^ 2], label)
    rows_out[...] = (middle * inverse_rms(middle) * gains[2:3] * (1.0 + scale)).astype(jnp.bfloat16)


def block_out_kernel(here, middle, upper, near, far, grad, mods, gains, segment, member,
                     block_out, grad_out, sums):
    ffn_sum = total_of((upper, near, far))
    inverse = inverse_rms(ffn_sum)
    unit = ffn_sum * inverse
    factor = jnp.tanh(per_row(mods[here[0] ^ 3], segment[:, 0:1])) * gains[3:4]
    block_out[...] = (middle[...] + factor * unit).astype(jnp.bfloat16)
    incoming = grad[...].astype(jnp.float32)
    grad_out[...] = row_norm_back(incoming * factor, unit, inverse).astype(jnp.bfloat16)
    sums[...] = segment_sums(member[...], incoming * unit)


def middle_back_kernel(here, middle, attn, upper, near, far, grad, mods, gains, segment, member,
                       middle_grad, attn_grad, ffn_sums, attn_sums):
    grad_in = total_of((upper, near, far))
    label = segment[:, 0:1]
    inverse = inverse_rms(middle[...])
    unit = middle[...] * inverse
    factor = gains[2:3] * (1.0 + per_row(mods[here[0] ^ 2], label))
    ffn_sums[...] = segment_sums(member[...], grad_in * unit)
    grad_middle = grad[...].astype(jnp.float32) + row_norm_back(grad_in * factor, unit, inverse)
    middle_grad[...] = grad_middle
    inverse = inverse_rms(attn[...])
    unit = attn[...] * inverse
    factor = jnp.tanh(per_row(mods[here[0] ^ 1], label)) * gains[1:2]
    attn_grad[...] = row_norm_back(grad_middle * factor, unit, inverse).astype(jnp.bfloat16)
    attn_sums[...] = segment_sums(member[...], grad_middle * unit)


def block_in_kernel(here, block, middle_grad, upper, near, far, mods, gains, segment, member,
                    in_grad, sums):
    grad_in = total_of((upper, near, far))
    values = block[...].astype(jnp.float32)
    inverse = inverse_rms(values)
    unit = values * inverse
    factor = gains[0:1] * (1.0 + per_row(mods[here[0]], segment[:, 0:1]))
    in_grad[...] = (
        middle_grad[...] + row_norm_back(grad_in * factor, unit, inverse)
    ).astype(jnp.bfloat16)
    sums[...] = segment_sums(member[...], grad_in * unit)


def stack_sums_kernel(here, first, second, third, fourth, head_gain, text_gain, gate_sum, gate, out):
    width = out.shape[1]
    heads = jnp.concatenate([head_gain[0:1], head_gain[1:2], text_gain[...]], axis=1)
    inner = heads.shape[1] // 3
    gates = gate_sum[...] * (1.0 - gate[...] * gate[...])
    gates = jnp.concatenate([gates, jnp.zeros((1, width - inner), jnp.float32)], axis=1)
    lane = lane_index(gates.shape)
    moved = jnp.zeros_like(gates)
    for position in range(4):
        turn = pltpu.roll(gates, position * inner, 1) if position else gates
        moved = jnp.where((lane // inner == position) & (here[0] == position), turn, moved)
    out[...] = jnp.concatenate(
        [part[0:SEGS] for part in (first, second, third, fourth)]
        + [
            jnp.concatenate([heads, jnp.zeros((1, width - 3 * inner), jnp.float32)], axis=1),
            moved,
            jnp.zeros((2, width), jnp.float32),
        ],
        axis=0,
    )


def pack_kernel(here, own, far, near, last, mods, gains, cond, packed):
    total = own[...] + far[...] + near[...] + last[...]
    grad = jnp.zeros((SEGS, total.shape[1]), jnp.float32)
    rows = []
    for name in range(4):
        part = total[name * SEGS : (name + 1) * SEGS]
        mod = mods[here[0] ^ name]
        gain = gains[name : name + 1]
        if name % 2 == 1:
            factor = jnp.tanh(mod)
            slope = 1.0 - factor * factor
        else:
            factor = 1.0 + mod
            slope = jnp.ones_like(mod)
        rows.append(jnp.sum(part * factor, axis=0, keepdims=True))
        mine = (jnp.zeros(part.shape, jnp.int32) + here[0]) == name
        grad = jnp.where(mine, part * slope * gain, grad)
    rows.append(total[4 * SEGS : 4 * SEGS + 2])
    rows = jnp.concatenate(rows, axis=0)
    high = rows.astype(jnp.bfloat16).astype(jnp.float32)
    pad = jnp.zeros((packed.shape[0] - 2 * SEGS - 2 * SUM_ROWS, total.shape[1]), jnp.float32)
    packed[...] = jnp.concatenate(
        [grad, cond[...].astype(jnp.float32), high, rows - high, pad], axis=0
    ).astype(jnp.bfloat16)


def rider_rows(count):
    return -(-(2 * SEGS * count + 2 * SUM_ROWS) // 16) * 16


def merge_rows(count, first, second, size):
    first, second = first.astype(jnp.float32), second.astype(jnp.float32)
    wide = SEGS * count
    start = 2 * wide
    sums = (
        first[start : start + SUM_ROWS]
        + first[start + SUM_ROWS : start + 2 * SUM_ROWS]
        + second[start : start + SUM_ROWS]
        + second[start + SUM_ROWS : start + 2 * SUM_ROWS]
    )
    high = sums.astype(jnp.bfloat16).astype(jnp.float32)
    pieces = [first[:wide], second[:wide], first[wide:start], second[wide:start], high, sums - high]
    rest = size - 4 * wide - 2 * SUM_ROWS
    if rest:
        pieces.append(jnp.zeros((rest, first.shape[1]), jnp.float32))
    return jnp.concatenate(pieces, axis=0).astype(jnp.bfloat16)


def merge_kernel(count, ours, theirs, out):
    out[...] = merge_rows(count, ours[...], theirs[...], out.shape[0])


def ada_kernel(count, heads, dp, own, *refs):
    parts = (own,) + refs[:3]
    ada_out, norm_out, head_out, gate_out = refs[3:]
    wide = SEGS * count
    base = own.shape[0] - rider_rows(count)
    columns = ada_out.shape[0]
    share = LANES // columns
    start = pl.multiple_of(dp[0] // share * LANES, LANES)
    grads, conds = [], []
    sums = jnp.zeros((SUM_ROWS, own.shape[1]), jnp.float32)
    for part in parts:
        rows = part[base:, :].astype(jnp.float32)
        grads.append(rows[:wide])
        conds.append(part[base:, pl.ds(start, LANES)].astype(jnp.float32)[wide : 2 * wide])
        for half in range(2):
            place = 2 * wide + half * SUM_ROWS
            sums = sums + rows[place : place + SUM_ROWS]
    conds = jnp.concatenate(conds, axis=0)
    conds = pltpu.roll(conds, (LANES - dp[0] % share * columns) % LANES, 1)
    acts = conds / (1.0 + jnp.exp(-conds))
    ada_out[...] = dot(
        acts.astype(jnp.bfloat16).astype(jnp.float32).T.astype(jnp.bfloat16),
        jnp.concatenate(grads, axis=0).astype(jnp.bfloat16),
    )[:columns]
    norm_out[...] = sums[:4]
    inner = heads * HEAD
    for row in range(3):
        line = jnp.zeros((1, HEAD), jnp.float32)
        for head in range(heads):
            place = row * inner + head * HEAD
            line = line + sums[4:5, place : place + HEAD]
        head_out[row : row + 1, :] = line
    lane = lane_index((1, LANES))
    line = jnp.zeros((1, LANES), jnp.float32)
    for head in range(HEADS):
        value = jnp.sum(sums[5:6, head * HEAD : (head + 1) * HEAD], axis=1, keepdims=True)
        line = jnp.where(lane == head, value, line)
    gate_out[...] = line


def back_kernel(count, *refs):
    grads, weights, upper, lower = refs[:count], refs[count : 2 * count], refs[-2], refs[-1]
    total = dot_t(grads[0][...], weights[0][...])
    for grad, weight in zip(grads[1:], weights[1:]):
        total = total + dot_t(grad[...], weight[...])
    half = upper.shape[0]
    upper[...] = total[:half].astype(jnp.bfloat16)
    lower[...] = total[half:].astype(jnp.bfloat16)


def back_call(grads, weights, name, ties=(), micros=0):
    rows, inner = grads[0].shape
    columns = weights[0].shape[0]
    tile = columns // 3
    return pl.pallas_call(
        lambda *refs: back_kernel(len(grads), *refs[: 2 * len(grads)], *refs[-2:]),
        grid=(columns // tile,),
        in_specs=[pl.BlockSpec((rows, inner), lambda step: (0, 0))] * len(grads)
        + [pl.BlockSpec((tile, inner), lambda step: (step, 0))] * len(grads)
        + [pl.BlockSpec(memory_space=pl.ANY)] * len(ties),
        out_specs=[pl.BlockSpec((rows // 2, tile), lambda step: (0, step))] * 2,
        out_shape=[jax.ShapeDtypeStruct((rows // 2, columns), jnp.bfloat16)] * 2,
        compiler_params=pltpu.CompilerParams(vmem_limit_bytes=VMEM_LIMIT),
        cost_estimate=cost_of(micros),
        name=name,
    )(*grads, *weights, *ties)


def shards(
    block_in,
    out_grad,
    condition,
    captions,
    caption_len,
    segment_ids,
    ada_weight,
    norm_gains,
    query_weight,
    key_weight,
    value_weight,
    head_gains,
    textkey_weight,
    textvalue_weight,
    cross_gate,
    out_weight,
    gate_weight,
    up_weight,
    down_weight,
):
    rows, width = block_in.shape
    length = segment_ids.shape[0]
    heads = cross_gate.shape[0]
    inner = heads * HEAD
    half_rows = length // 2
    position = lax.axis_index("tensor")
    spot = dp_spot(position)
    here = position.reshape(1)
    b16, f32 = jnp.bfloat16, jnp.float32

    blocks = gather_tensor(block_in)
    cond_rows = jnp.pad(condition, ((0, 0), (0, width - condition.shape[1])))
    own_act = jax.nn.silu(condition.astype(f32)).astype(b16)
    own_part = jnp.dot(own_act, ada_weight, preferred_element_type=f32)
    parts = gather_tensor(own_part)
    mods = jnp.stack([parts[ROW_ORDER.index(code)] for code in range(4)])

    cosine, sine, mark_q, mark_k, mark_t, segment, member, gate_lanes, gate_swapped, gains = whole_call(
        tables_kernel,
        (here, caption_len, cross_gate),
        [segment_ids.reshape(length // rows, rows), head_gains],
        [((length, LANES), f32)] * 2
        + [((length, LANES), b16)] * 2
        + [((SEGS * TXT, LANES), b16), ((rows, LANES), f32), ((8, rows), b16)]
        + [((1, inner), f32)] * 2
        + [((3, inner), f32)],
        "tables",
        micros=2,
    )
    caption_flat = captions.reshape(-1, captions.shape[-1])
    texts = caption_flat.shape[0]
    raw_t, text_value = text_call(caption_flat, textkey_weight, textvalue_weight)
    attn_rows, raw_q, raw_k, value = whole_call(
        project_kernel,
        (here,),
        blocks + [mods, norm_gains, mark_q, query_weight, key_weight, value_weight],
        [((length, width), b16), ((length, inner), f32), ((length, inner), f32), ((length, inner), b16)],
        "project",
        micros=6,
    )
    query, key, text, mixed, self_out, cross_out, self_log, cross_log = pair_call(
        attend_kernel,
        [(raw_q, 1), (raw_k, 1), (value, 1), (raw_t, 1), (text_value, 1), (cosine, None), (sine, None)]
        + [(gains, 1), (gate_lanes, 1), (gate_swapped, 1), (mark_q, None), (mark_k, None), (mark_t, None)],
        [((length, inner), b16, 1)] * 2
        + [((texts, inner), b16, 1), ((length, inner), b16, 1)]
        + [((length, inner), f32, 1)] * 4,
        "attend",
        micros=11,
    )

    def halves(product):
        return product(slice(0, half_rows)).astype(b16), product(slice(half_rows, None)).astype(b16)

    def all_of(block):
        return jnp.concatenate(gather_tensor(block), axis=0)

    upper, lower = halves(lambda part: jnp.dot(mixed[part], out_weight, preferred_element_type=f32))
    sums, sent = scatter_tensor(upper, lower)
    attn_rows_t = turned(attn_rows, (sent,))
    wide = ((rows, width), f32)
    narrow = ((rows, width), b16)
    totals = ((8, width), f32)
    attn_sum, middle, ffn_own = whole_call(
        middle_kernel,
        (here,),
        [block_in] + sums + [mods, norm_gains, segment],
        [wide, wide, narrow],
        "middle",
    )
    ffn_rows = all_of(ffn_own)
    gate_pre = jnp.dot(ffn_rows, gate_weight, preferred_element_type=f32)
    up_pre = jnp.dot(ffn_rows, up_weight, preferred_element_type=f32)
    sigmoid_gate = jax.nn.sigmoid(gate_pre)
    silu_gate = gate_pre * sigmoid_gate
    hidden = (silu_gate * up_pre).astype(b16)
    upper, lower = halves(lambda part: jnp.dot(hidden[part], down_weight, preferred_element_type=f32))
    sums, sent = scatter_tensor(upper, lower)
    ffn_rows_t = turned(ffn_rows, (sent,))
    block_out, grad_own, sum_gate_ffn = whole_call(
        block_out_kernel,
        (here,),
        [middle] + sums + [out_grad, mods, norm_gains, segment, member],
        [narrow, narrow, totals],
        "block_out",
    )

    grad_ffn = all_of(grad_own)
    grad_hidden = times_transpose(grad_ffn, down_weight)
    grad_gate = (
        grad_hidden * up_pre * sigmoid_gate * (1.0 + gate_pre * (1.0 - sigmoid_gate))
    ).astype(b16)
    grad_up = (grad_hidden * silu_gate).astype(b16)
    upper, lower = halves(
        lambda part: times_transpose(grad_gate[part], gate_weight)
        + times_transpose(grad_up[part], up_weight)
    )
    sums, sent = scatter_tensor(upper, lower)
    grad_ffn_t = turned(grad_ffn, (sent,))
    ffn_pairs = [(ffn_rows_t, [grad_gate, grad_up]), (grad_ffn_t, [hidden])]
    (halves_two,) = row_chunks(ffn_pairs, (2,), spot, ties=(sent,), micros=FFN_MICROS)
    ffn_passed = one_on(halves_two)
    grad_middle, grad_own, sum_scale_ffn, sum_gate_attn = whole_call(
        middle_back_kernel,
        (here,),
        [middle, attn_sum] + sums + [out_grad, mods, norm_gains, segment, member],
        [wide, narrow, totals, totals],
        "middle_back",
        micros=MIDDLE_MICROS,
    )

    grad_attn = all_of(grad_own)
    grad_mixed = times_transpose(grad_attn, out_weight).astype(b16)
    cross_grad, text_grad, text_value_grad, text_gain, gate_sum = pair_call(
        cross_back_kernel,
        [(query, 1), (text, 1), (text_value, 1), (raw_t, 1), (grad_mixed, 1), (cross_out, 1)]
        + [(cross_log, 1), (gains, 1), (mark_q, None), (mark_t, None)],
        [((length, inner), f32, 1), ((inner, texts), b16, 0), ((inner, texts), b16, 0)]
        + [((1, inner), f32, 1)] * 2,
        "cross_back",
        micros=CROSS_MICROS,
    )
    ffn_one, ffn_three, ffn_kept = row_chunks(
        ffn_pairs, (1, 3, 0), spot, extra=ffn_passed, ties=(text_grad,), micros=FFN_NEXT_MICROS
    )
    text_lefts = [text_grad, text_value_grad]
    (halves_two,) = column_chunks(text_lefts, caption_flat, (2,), spot, ties=(ffn_kept,))
    text_passed = one_on(halves_two)
    query_grad, key_grad, value_grad, head_gain = pair_call(
        self_back_kernel,
        [(query, 1), (key, 1), (value, 1), (raw_q, 1), (raw_k, 1), (grad_mixed, 1), (self_out, 1)]
        + [(self_log, 1), (cross_grad, 1), (cosine, None), (sine, None), (gains, 1)]
        + [(mark_q, None), (mark_k, None)],
        [((length, inner), b16, 1)] * 3 + [((2, inner), f32, 1)],
        "self_back",
        (halves_two[0],),
        micros=SELF_MICROS,
    )

    hidden_cols = hidden.shape[1]
    block_rows = width // BLOCKS
    upper, lower = back_call(
        [query_grad, key_grad, value_grad], [query_weight, key_weight, value_weight], "attn_back"
    )
    sums, sent = scatter_tensor(upper, lower)
    text_one, text_three, text_kept = column_chunks(
        text_lefts, caption_flat, (1, 3, 0), spot, extra=text_passed, ties=(sent,), micros=TEXT_MICROS
    )
    got = [by_slots(part) for part in to_neighbours(ffn_kept, ffn_one, ffn_three)]
    shape = (PAIR, block_rows, 3 * hidden_cols)
    ffn_kept, ffn_sent = tiled_call(
        ffn_second_kernel,
        (spot,),
        got,
        [((2 * PAIR,) + shape[1:], b16)] * 2,
        "ffn_second",
        -1,
        4,
        (text_kept,),
    )
    in_grad, sum_scale_attn = whole_call(
        block_in_kernel,
        (here,),
        [block_in, grad_middle] + sums + [mods, norm_gains, segment, member],
        [narrow, totals],
        "block_in",
        (ffn_sent,),
        micros=BLOCK_IN_MICROS,
    )
    (stacked,) = whole_call(
        stack_sums_kernel,
        (here,),
        [sum_scale_attn, sum_gate_attn, sum_scale_ffn, sum_gate_ffn]
        + [head_gain, text_gain, gate_sum, gate_lanes],
        [((16, width), f32)],
        "stack_sums",
    )
    attn_pairs = [
        (attn_rows_t, [query_grad, key_grad, value_grad]),
        (turned(grad_attn, (halves_two[0],)), [mixed]),
    ]
    (halves_two,) = row_chunks(attn_pairs, (2,), spot, ties=(stacked,), micros=ATTN_FIRST_MICROS)
    attn_passed = one_on(halves_two)
    stacked = gather_tensor(stacked)
    ffn_own, ffn_sent = tiled_call(
        ffn_middle_kernel,
        (),
        [ffn_kept, dp_permute(ffn_sent, "second", "flip")],
        [(shape, b16)] * 2,
        "ffn_middle",
        -1,
        2,
        (text_kept,),
    )
    (riders,) = whole_call(
        pack_kernel,
        (here,),
        stacked + [mods, norm_gains, cond_rows],
        [((rider_rows(1), width), b16)],
        "pack",
        (ffn_sent,),
        micros=PACK_MICROS,
    )
    (riders,) = whole_call(
        functools.partial(merge_kernel, 1),
        (),
        [riders, dp_permute(riders, "z", 1)],
        [((rider_rows(PAIR), width), b16)],
        "merge",
    )
    opposite = dp_permute(riders, "first", 2)
    attn_one, attn_three, attn_kept = row_chunks(
        attn_pairs, (1, 3, 0), spot, extra=attn_passed, riders=(riders,), ties=(text_kept,), micros=ATTN_MICROS
    )
    text_rows = caption_flat.shape[1] // BLOCKS
    text_own, text_sent = tiled_call(
        text_second_kernel,
        (spot,),
        to_neighbours(text_kept, text_one, text_three),
        [((2 * inner, 2 * PAIR * text_rows), b16)] * 2,
        "text_second",
        0,
        4,
        (opposite,),
        micros=SECOND_MICROS,
    )
    stage = tiled_call(
        functools.partial(attn_second_kernel, block_rows),
        (spot,),
        [riders, opposite] + to_neighbours(attn_kept, attn_one, attn_three),
        [((PAIR * block_rows + rider_rows(4 * PAIR), width), b16)] * RING,
        "attn_second",
        -1,
        4,
        (text_sent,),
    )
    ffn_own_kept, ffn_own_sent = tiled_call(
        ffn_third_kernel,
        (spot,),
        [ffn_own, dp_permute(ffn_sent, "second", "mirror")],
        [(shape[1:], b16)] * 2,
        "ffn_third",
        -1,
        2,
        (stage[0],),
    )
    text_own, text_sent = tiled_call(
        text_middle_kernel,
        (),
        [text_own, dp_permute(text_sent, "second", "flip")],
        [((2 * inner, PAIR * text_rows), b16)] * 2,
        "text_middle",
        0,
        2,
        (stage[0],),
    )
    got = exchange(stage, "second")
    kept, sent = tiled_call(
        attn_third_kernel, (spot,), got, [((block_rows, width), b16)] * 2, "attn_third",
        -1,
        2
    )
    gate_sum_out, up_sum_out, down_sum_out = whole_call(
        ffn_last_kernel,
        (),
        exchange([ffn_own_kept, ffn_own_sent], "z"),
        [((block_rows, hidden_cols), f32)] * 2 + [((hidden_cols, block_rows), f32)],
        "ffn_last",
        (kept,),
    )
    text_own_kept, text_own_sent = tiled_call(
        text_third_kernel,
        (spot,),
        [text_own, dp_permute(text_sent, "second", "mirror")],
        [((2 * inner, text_rows), b16)] * 2,
        "text_third",
        0,
        2,
        (kept,),
    )
    textkey_sum, textvalue_sum = whole_call(
        text_last_kernel,
        (),
        exchange([text_own_kept, text_own_sent], "z"),
        [((text_rows, inner), f32)] * 2,
        "text_last",
    )
    ada_grad, norm_grads, head_grads, crossgate = tiled_call(
        functools.partial(ada_kernel, 4 * PAIR, heads),
        (lax.axis_index("dp").reshape(1),),
        got,
        [((condition.shape[1] // BLOCKS, width), f32), ((4, width), f32), ((3, HEAD), f32)]
        + [((1, LANES), f32)],
        "ada",
        0,
        1,
        (kept,),
    )
    crossgate_grad = crossgate[0, :HEADS]
    query_sum, key_sum, value_sum, outw_sum = whole_call(
        attn_last_kernel,
        (),
        exchange([kept, sent], "z"),
        [((block_rows, inner), f32)] * 3 + [((inner, block_rows), f32)],
        "attn_last",
    )
    return (
        block_out,
        in_grad,
        ada_grad,
        norm_grads,
        query_sum,
        key_sum,
        value_sum,
        head_grads,
        textkey_sum,
        textvalue_sum,
        crossgate_grad,
        outw_sum,
        gate_sum_out,
        up_sum_out,
        down_sum_out,
    )


def solution(mesh):
    return jax.shard_map(
        shards,
        mesh=mesh,
        in_specs=(
            P(("dp", "tensor"), None),
            P(("dp", "tensor"), None),
            P("dp", None),
            P("dp", None, None),
            P("dp"),
            P("dp"),
            P(None, "tensor"),
            P(),
            P(None, "tensor"),
            P(None, "tensor"),
            P(None, "tensor"),
            P(),
            P(None, "tensor"),
            P(None, "tensor"),
            P("tensor"),
            P("tensor", None),
            P(None, "tensor"),
            P(None, "tensor"),
            P("tensor", None),
        ),
        out_specs=(
            P(("dp", "tensor"), None),
            P(("dp", "tensor"), None),
            P("dp", "tensor"),
            P(),
            P("dp", "tensor"),
            P("dp", "tensor"),
            P("dp", "tensor"),
            P(),
            P("dp", "tensor"),
            P("dp", "tensor"),
            P(),
            P("tensor", "dp"),
            P("dp", "tensor"),
            P("dp", "tensor"),
            P("tensor", "dp"),
        ),
        check_vma=False,
    )
```

```python
import functools
import math

import jax
import jax.numpy as jnp
from jax import lax
from jax.experimental import pallas as pl
from jax.experimental.pallas import tpu as pltpu
from jax.sharding import PartitionSpec as P

HEAD = 64
HEADS = 24
TXT = 256
SEGS = 3
EPS = 1e-06
LANES = 2 * HEAD
SHUT = 256.0
ROOT = HEAD ** (-0.5)
VMEM_LIMIT = 16 * 2**20
NO_COST = pl.CostEstimate(flops=0, bytes_accessed=0, transcendentals=0)


def cost_of(micros):
    return pl.CostEstimate(flops=int(micros * 1e9), bytes_accessed=0, transcendentals=0)


SUM_ROWS = 6
CROSS_MICROS = 10
BLOCK_IN_MICROS = 0
FFN_MICROS = 3
FFN_NEXT_MICROS = 8
MIDDLE_MICROS = 10
SELF_MICROS = 0
ATTN_MICROS = 3
TEXT_MICROS = 8
PACK_MICROS = 16
SECOND_MICROS = 8
STAGE_MICROS = 0
ATTN_FIRST_MICROS = 0

RING = 4
PAIR = 2
BLOCKS = RING * PAIR * RING
SLOTS = BLOCKS // RING
SEND_ORDER = (2, 1, 3, 0)
CORE_SWAP = [(0, 1), (1, 0), (2, 3), (3, 2)]
CHIP_SWAP = [(0, 2), (2, 0), (1, 3), (3, 1)]
ROW_ORDER = (0, 2, 1, 3)

def dp_index(x, z, y):
    return (x * PAIR + z) * RING + y


def dp_perm(axis, step):
    pairs = []

    def moved(place, size):
        if step == "flip":
            return place ^ 1
        if step == "mirror":
            return size - 1 - place
        return (place + step) % size

    for x in range(RING):
        for z in range(PAIR):
            for y in range(RING):
                for tensor in range(2 * PAIR):
                    way = axis
                    if axis in ("first", "second"):
                        way = "x" if (tensor % 2 == 0) == (axis == "first") else "y"
                    target = {
                        "x": (moved(x, RING), z, y),
                        "y": (x, z, moved(y, RING)),
                        "z": (x, moved(z, PAIR), y),
                    }[way]
                    pairs.append(
                        (
                            dp_index(x, z, y) * 2 * PAIR + tensor,
                            dp_index(*target) * 2 * PAIR + tensor,
                        )
                    )
    return pairs


def dp_permute(values, axis, step):
    return lax.ppermute(values, ("dp", "tensor"), dp_perm(axis, step))


def dp_spot(position):
    index = lax.axis_index("dp")
    x, z, y = index // (RING * PAIR), index // RING % PAIR, index % RING
    core = position % 2
    return jnp.stack([jnp.where(core == 0, x, y), z, jnp.where(core == 0, y, x), core])


def swap_core(values):
    return lax.ppermute(values, "tensor", CORE_SWAP)


def swap_chip(values):
    return lax.ppermute(values, "tensor", CHIP_SWAP)


def times_transpose(left, right):
    return lax.dot_general(
        left, right, (((1,), (1,)), ((), ())), preferred_element_type=jnp.float32
    )


def gather_tensor(block):
    far = swap_chip(block)
    near = swap_core(block)
    return [block, far, near, swap_core(far)]


def scatter_tensor(upper, lower):
    near = swap_core(lower)
    rows = upper.shape[0] // 2
    far = (upper[rows:].astype(jnp.float32) + near[rows:].astype(jnp.float32)).astype(near.dtype)
    return [upper, near, swap_chip(far)], far


def turn_kernel(source, target):
    target[...] = source[...].T


def turned(values, ties=()):
    tile = 512 if values.shape[1] % 512 == 0 else values.shape[1]
    return pl.pallas_call(
        lambda source, *rest: turn_kernel(source, rest[-1]),
        grid=(values.shape[1] // tile,),
        in_specs=[pl.BlockSpec((values.shape[0], tile), lambda step: (0, step))]
        + [pl.BlockSpec(memory_space=pl.ANY)] * len(ties),
        out_specs=pl.BlockSpec((tile, values.shape[0]), lambda step: (step, 0)),
        out_shape=jax.ShapeDtypeStruct(values.shape[::-1], values.dtype),
        compiler_params=pltpu.CompilerParams(vmem_limit_bytes=VMEM_LIMIT),
        cost_estimate=NO_COST,
    )(values, *ties)


def chunk_block(offset, slot, spot):
    first = (spot[0] + offset) % RING
    z, second = slot // RING, slot % RING
    x = jnp.where(spot[3] == 0, first, second)
    y = jnp.where(spot[3] == 0, second, first)
    return dp_index(x, z, y)


def offset_of_step(offsets, step):
    offset = offsets[-1]
    for place in range(len(offsets) - 1):
        offset = jnp.where(step == place, offsets[place], offset)
    return offset


def chunk_kernel(make, offsets, halves, extra, outs, held, sems):
    step = pl.program_id(0)
    first, second = halves

    def copies(place):
        slot = held.at[place % 2]
        if offsets[place] != 2:
            return [pltpu.make_async_copy(slot, outs[place], sems.at[place % 2, 0])]
        return [
            pltpu.make_async_copy(slot.at[half], out, sems.at[place % 2, way])
            for way, (half, out) in enumerate(zip((first, second), outs[place]))
        ]

    for place, offset in enumerate(offsets):

        @pl.when(step == place)
        def _(place=place, offset=offset):
            if place >= 2:
                for copy in copies(place - 2):
                    copy.wait()
            added = {1: (first, extra[0]), 3: (second, extra[1])}.get(offset) if extra else None
            make(held.at[place % 2], added, offset)
            for copy in copies(place):
                copy.start()
            if place == len(offsets) - 1:
                for last in range(max(place - 1, 0), place + 1):
                    for copy in copies(last):
                        copy.wait()


def chunk_call(make, operands, specs, offsets, halves, shape, spot, extra, ties, name, micros):
    count = len(operands)
    pieces = []
    for offset in offsets:
        if offset == 2:
            pieces += [tuple(len(range(*s.indices(d))) for s, d in zip(h, shape)) for h in halves]
        else:
            pieces.append(shape)

    def kernel(spot_ref, *refs):
        inputs, extras = refs[:count], refs[count : count + len(extra)]
        outs = list(refs[-len(pieces) - 2 : -2])
        grouped = []
        for offset in offsets:
            grouped.append((outs.pop(0), outs.pop(0)) if offset == 2 else outs.pop(0))
        chunk_kernel(
            functools.partial(make, inputs), offsets, halves, extras, grouped, refs[-2], refs[-1]
        )

    found = pl.pallas_call(
        kernel,
        grid_spec=pltpu.PrefetchScalarGridSpec(
            num_scalar_prefetch=1,
            grid=(len(offsets),),
            in_specs=list(specs)
            + [pl.BlockSpec(part.shape, lambda step, spot: (0, 0)) for part in extra]
            + [pl.BlockSpec(memory_space=pl.ANY)] * len(ties),
            out_specs=[pl.BlockSpec(memory_space=pl.ANY)] * len(pieces),
            scratch_shapes=[
                pltpu.VMEM((2,) + shape, jnp.bfloat16),
                pltpu.SemaphoreType.DMA((2, 2)),
            ],
        ),
        out_shape=[jax.ShapeDtypeStruct(piece, jnp.bfloat16) for piece in pieces],
        compiler_params=pltpu.CompilerParams(vmem_limit_bytes=VMEM_LIMIT),
        cost_estimate=cost_of(micros),
        name=name,
    )(spot, *operands, *extra, *ties)
    found = list(found)
    return [
        (found.pop(0), found.pop(0)) if offset == 2 else found.pop(0) for offset in offsets
    ]


def make_rows(groups, inputs, slot, added, offset):
    lefts, rights = inputs[: SLOTS * len(groups)], inputs[SLOTS * len(groups) :]
    size = SLOTS * lefts[0].shape[1]
    if len(rights) > sum(groups):
        slot[size:, :] = rights[-1][...]
    column = place = 0
    for group, count in enumerate(groups):
        rows = jnp.concatenate(
            [left[0] for left in lefts[SLOTS * group : SLOTS * (group + 1)]], axis=0
        )
        for right in rights[place : place + count]:
            wide = right.shape[1]
            product = dot(rows, right[...])
            low, high = column, column
            if added is not None:
                low = min(max(column, added[0][1].start), column + wide)
                high = min(max(column, added[0][1].stop), column + wide)
            for start, stop in ((column, low), (low, high), (high, column + wide)):
                if start < stop:
                    part = product[:, start - column : stop - column]
                    if (start, stop) == (low, high):
                        base = added[0][1].start
                        part = part + added[1][:size, start - base : stop - base].astype(jnp.float32)
                    slot[:size, start:stop] = part.astype(jnp.bfloat16)
            column += wide
        place += count


def row_chunks(pairs, offsets, spot, extra=(), ties=(), micros=0, riders=()):
    lefts = [left.reshape(BLOCKS, left.shape[0] // BLOCKS, left.shape[1]) for left, _ in pairs]
    rights = [right for _, group in pairs for right in group]
    total = sum(right.shape[1] for right in rights)
    specs, operands = [], []
    for left in lefts:
        for slot in range(SLOTS):
            specs.append(
                pl.BlockSpec(
                    (1,) + left.shape[1:],
                    lambda step, spot, slot=slot: (
                        chunk_block(offset_of_step(offsets, step), slot, spot),
                        0,
                        0,
                    ),
                )
            )
            operands.append(left)
    specs += [pl.BlockSpec(right.shape, lambda step, spot: (0, 0)) for right in rights]
    specs += [pl.BlockSpec(part.shape, lambda step, spot: (0, 0)) for part in riders]
    rows = SLOTS * lefts[0].shape[1] + sum(part.shape[0] for part in riders)
    halves = [(slice(0, rows), slice(0, total // 2)), (slice(0, rows), slice(total // 2, total))]
    return chunk_call(
        functools.partial(make_rows, [len(group) for _, group in pairs]),
        operands + rights + list(riders),
        specs,
        offsets,
        halves,
        (rows, total),
        spot,
        extra,
        ties,
        "row_chunks",
        micros,
    )


def make_columns(lefts, inputs, slot, added, offset):
    whole = jnp.concatenate([right[...] for right in inputs[lefts:]], axis=1)
    row = 0
    for left in inputs[:lefts]:
        product = dot(left[...], whole)
        if added is not None and added[0][0].start == row:
            product = product + added[1][...].astype(jnp.float32)
        slot[row : row + left.shape[0], :] = product.astype(jnp.bfloat16)
        row += left.shape[0]


def column_chunks(lefts, right, offsets, spot, extra=(), ties=(), micros=0):
    rows = lefts[0].shape[0]
    depth, columns = right.shape
    specs = [pl.BlockSpec(left.shape, lambda step, spot: (0, 0)) for left in lefts]
    for slot in range(SLOTS):
        specs.append(
            pl.BlockSpec(
                (depth, columns // BLOCKS),
                lambda step, spot, slot=slot: (
                    0,
                    chunk_block(offset_of_step(offsets, step), slot, spot),
                ),
            )
        )
    lanes = columns // RING
    halves = [(slice(0, rows), slice(0, lanes)), (slice(rows, 2 * rows), slice(0, lanes))]
    return chunk_call(
        functools.partial(make_columns, len(lefts)),
        list(lefts) + [right] * SLOTS,
        specs,
        offsets,
        halves,
        (2 * rows, lanes),
        spot,
        extra,
        ties,
        "column_chunks",
        micros,
    )


def add_up(refs, index):
    total = refs[0][index].astype(jnp.float32)
    for ref in refs[1:]:
        total = total + ref[index].astype(jnp.float32)
    return total


def lane_slice(start, size):
    return (slice(None), pl.ds(pl.multiple_of(start * size, size), size))


def halving_places(spot):
    own = spot[2]
    other = own ^ 1
    return (own, RING - 1 - own), (other, RING - 1 - other)


def ffn_second_kernel(spot, *refs):
    parts = refs[:-2]
    for out, places in zip(refs[-2:], halving_places(spot)):
        for index, place in enumerate(places):
            for z in range(PAIR):
                out[index * PAIR + z] = add_up(parts, z * RING + place).astype(jnp.bfloat16)


def ffn_middle_kernel(kept, got, own, sent):
    for out, start in ((own, 0), (sent, PAIR)):
        for z in range(PAIR):
            out[z] = add_up((kept, got), start + z).astype(jnp.bfloat16)


def ffn_third_kernel(spot, *refs):
    for out, z in ((refs[-2], spot[1]), (refs[-1], (spot[1] + 1) % PAIR)):
        out[...] = add_up(refs[:-2], z).astype(jnp.bfloat16)


def ffn_last_kernel(kept, got, gate_out, up_out, down_out):
    total = kept[...].astype(jnp.float32) + got[...].astype(jnp.float32)
    hidden = gate_out.shape[1]
    gate_out[...] = total[:, :hidden]
    up_out[...] = total[:, hidden : 2 * hidden]
    down_out[...] = total[:, 2 * hidden :].T


def text_second_kernel(spot, *refs):
    parts = refs[:-2]
    lanes = parts[0].shape[1] // SLOTS
    for out, places in zip(refs[-2:], halving_places(spot)):
        for index, place in enumerate(places):
            for z in range(PAIR):
                start = (index * PAIR + z) * lanes
                out[:, start : start + lanes] = add_up(
                    parts, lane_slice(z * RING + place, lanes)
                ).astype(jnp.bfloat16)


def text_middle_kernel(kept, got, own, sent):
    wide = own.shape[1]
    for out, start in ((own, 0), (sent, wide)):
        index = (slice(None), slice(start, start + wide))
        out[...] = add_up((kept, got), index).astype(jnp.bfloat16)


def text_third_kernel(spot, *refs):
    lanes = refs[-1].shape[1]
    for out, z in ((refs[-2], spot[1]), (refs[-1], (spot[1] + 1) % PAIR)):
        out[...] = add_up(refs[:-2], lane_slice(z, lanes)).astype(jnp.bfloat16)


def text_last_kernel(kept, got, textkey, textvalue):
    total = kept[...].astype(jnp.float32) + got[...].astype(jnp.float32)
    columns = textkey.shape[1]
    textkey[...] = total[:columns].T
    textvalue[...] = total[columns:].T


def attn_second_kernel(rows, spot, riders, opposite, *refs):
    parts, outs = refs[:-RING], refs[-RING:]
    size = SLOTS * rows
    for offset in range(RING):
        for z in range(PAIR):
            slot = z * RING + (spot[2] + offset) % RING
            index = (pl.ds(pl.multiple_of(slot * rows, 16), rows), slice(None))
            outs[offset][z * rows : (z + 1) * rows, :] = add_up(parts, index).astype(jnp.bfloat16)
    pairs = ((riders[...], parts[1][size:, :]), (opposite[...], parts[2][size:, :]))
    joined = [merge_rows(PAIR, first, second, rider_rows(2 * PAIR)) for first, second in pairs]
    joined = merge_rows(2 * PAIR, joined[0], joined[1], rider_rows(4 * PAIR))
    for out in outs:
        out[PAIR * rows :, :] = joined


def attn_third_kernel(spot, *refs):
    rows = refs[-1].shape[0]
    for out, z in ((refs[-2], spot[1]), (refs[-1], (spot[1] + 1) % PAIR)):
        index = (pl.ds(pl.multiple_of(z * rows, 16), rows), slice(None))
        out[...] = add_up(refs[:RING], index).astype(jnp.bfloat16)


def attn_last_kernel(kept, got, query, key, value, outw):
    total = kept[...].astype(jnp.float32) + got[...].astype(jnp.float32)
    columns = query.shape[1]
    for place, out in enumerate((query, key, value)):
        out[...] = total[:, place * columns : (place + 1) * columns]
    outw[...] = total[:, 3 * columns :].T


def whole_call(kernel, scalars, operands, outs, name, ties=(), scratch=(), micros=0):
    whole = pl.BlockSpec(memory_space=pltpu.VMEM)
    count = len(scalars) + len(operands)
    return pl.pallas_call(
        lambda *refs: kernel(*refs[:count], *refs[count + len(ties) :]),
        in_specs=[pl.BlockSpec(memory_space=pltpu.SMEM)] * len(scalars)
        + [whole] * len(operands)
        + [pl.BlockSpec(memory_space=pl.ANY)] * len(ties),
        out_specs=[whole] * len(outs),
        out_shape=[jax.ShapeDtypeStruct(shape, kind) for shape, kind in outs],
        scratch_shapes=list(scratch),
        compiler_params=pltpu.CompilerParams(vmem_limit_bytes=VMEM_LIMIT),
        cost_estimate=cost_of(micros),
        name=name,
    )(*scalars, *operands, *ties)


def tiled_call(kernel, scalars, operands, outs, name, axis, tiles, ties=(), micros=0, axes=None):
    def spec(shape, axis):
        block = list(shape)
        block[axis] //= tiles
        if axis == 0:
            return pl.BlockSpec(tuple(block), lambda step: (step,) + (0,) * (len(shape) - 1))
        return pl.BlockSpec(tuple(block), lambda step: (0,) * (len(shape) - 1) + (step,))

    count = len(scalars) + len(operands)
    return pl.pallas_call(
        lambda *refs: kernel(*refs[:count], *refs[count + len(ties) :]),
        grid=(tiles,),
        in_specs=[pl.BlockSpec(memory_space=pltpu.SMEM)] * len(scalars)
        + [spec(part.shape, way) for part, way in zip(operands, axes or [axis] * len(operands))]
        + [pl.BlockSpec(memory_space=pl.ANY)] * len(ties),
        out_specs=[spec(shape, axis) for shape, _ in outs],
        out_shape=[jax.ShapeDtypeStruct(shape, kind) for shape, kind in outs],
        compiler_params=pltpu.CompilerParams(vmem_limit_bytes=VMEM_LIMIT),
        cost_estimate=cost_of(micros),
        name=name,
    )(*scalars, *[pltpu.with_memory_space_constraint(part, pltpu.HBM) for part in operands], *ties)


def exchange(chunks, axis):
    return [chunks[0]] + [
        dp_permute(chunks[step], axis, step) for step in range(1, len(chunks))
    ]


def one_on(halves):
    return dp_permute(halves[0], "first", 1), dp_permute(halves[1], "first", RING - 1)


def to_neighbours(own, ahead, behind):
    return [own, dp_permute(ahead, "first", 1), dp_permute(behind, "first", RING - 1)]


def by_slots(chunk):
    return chunk.reshape(SLOTS, chunk.shape[0] // SLOTS, chunk.shape[1])


def lane_index(shape):
    return lax.broadcasted_iota(jnp.int32, shape, 1)


def head_lanes(shape, head):
    lane = lane_index(shape)
    return (lane < HEAD) if head == 0 else (lane >= HEAD)


def per_head(values, reduce):
    first = head_lanes(values.shape, 0)
    left = jnp.sum(jnp.where(first, values, 0.0), axis=1, keepdims=True)
    right = jnp.sum(jnp.where(first, 0.0, values), axis=1, keepdims=True)
    return jnp.where(first, left, right)


def head_units(raw):
    inverse = lax.rsqrt(per_head(raw * raw, None) * (1.0 / HEAD) + EPS)
    return raw * inverse, inverse


def partner(values):
    lane = lane_index(values.shape)
    return jnp.where(
        lane % HEAD < HEAD // 2,
        pltpu.roll(values, LANES - HEAD // 2, 1),
        pltpu.roll(values, HEAD // 2, 1),
    )


def dot(left, right):
    return jnp.dot(left, right, preferred_element_type=jnp.float32)


def dot_t(left, right):
    return lax.dot_general(left, right, (((1,), (1,)), ((), ())), preferred_element_type=jnp.float32)


def attend_kernel(
    raw_q, raw_k, value, raw_t, text_value, cosine, sine, gains, gate, gate_swapped, mark_q, mark_k, mark_t,
    query_out, key_out, text_out, mixed_out, self_out, cross_out, self_log, cross_log,
):
    cos, sin = cosine[...], sine[...]
    unit = head_units(raw_q[...])[0] * gains[0:1, :]
    query = ((unit * cos + partner(unit) * sin).astype(jnp.bfloat16) * ROOT).astype(jnp.bfloat16)
    unit = head_units(raw_k[...])[0] * gains[1:2, :]
    key = (unit * cos + partner(unit) * sin).astype(jnp.bfloat16)
    text = (head_units(raw_t[...])[0] * gains[2:3, :]).astype(jnp.bfloat16)
    query_out[...] = query
    key_out[...] = key
    text_out[...] = text

    def attention(keys, marks, values):
        outs, sums = [], []
        for head in range(2):
            own = head_lanes(query.shape, head)
            own_keys = head_lanes(keys.shape, head)
            probe = jnp.where(own, query, mark_q[...])
            scores = dot_t(probe, jnp.where(own_keys, keys, marks))
            weights = jnp.exp(scores).astype(jnp.bfloat16)
            both = dot(weights, jnp.where(own_keys, values, jnp.ones_like(values)))
            outs.append(both)
        first = head_lanes(outs[0].shape, 0)
        product = jnp.where(first, outs[0], outs[1])
        total = jnp.where(first, outs[1], outs[0])
        return product / pltpu.roll(total, HEAD, 1), jnp.log(total)

    out, log = attention(key, mark_k[...], value[...])
    self_out[...] = out
    self_log[...] = log
    cross, log = attention(text, mark_t[...], text_value[...])
    cross_out[...] = cross
    cross_log[...] = log - jnp.log(gate_swapped[...])
    mixed_out[...] = (out + gate[...] * cross).astype(jnp.bfloat16)


def attention_grads(query, keys, marks, values, grad, out, log, mark_q):
    rows = grad.astype(jnp.float32)
    delta = per_head(rows * out, None)
    delta = pltpu.roll(delta, HEAD, 1)
    lane = lane_index(query.shape) % HEAD
    log_high = log.astype(jnp.bfloat16)
    log_low = (log - log_high.astype(jnp.float32)).astype(jnp.bfloat16)
    delta_high = delta.astype(jnp.bfloat16)
    delta_low = (delta - delta_high.astype(jnp.float32)).astype(jnp.bfloat16)
    zero = jnp.zeros_like(query)
    code = jnp.where(lane == 4, -log_high, jnp.where(lane == 5, -log_low, mark_q))
    shift = jnp.where(lane == 4, -delta_high, jnp.where(lane == 5, -delta_low, zero))
    key_grads, value_grads, query_grads = [], [], []
    for head in range(2):
        own = head_lanes(query.shape, head)
        own_keys = head_lanes(keys.shape, head)
        probe = jnp.where(own, query, code)
        probs = jnp.exp(dot_t(jnp.where(own_keys, keys, marks), probe))
        slope = dot_t(jnp.where(own_keys, values, marks), jnp.where(own, grad, shift))
        score_grad = (probs * slope).astype(jnp.bfloat16)
        value_grads.append(dot(probs.astype(jnp.bfloat16), grad))
        key_grads.append(dot(score_grad, query))
        turned = keys[:, head * HEAD : (head + 1) * HEAD].T
        query_grads.append(dot(turned, score_grad))
    first = head_lanes(keys.shape, 0)
    return (
        jnp.concatenate(query_grads, axis=0),
        jnp.where(first, key_grads[0], key_grads[1]),
        jnp.where(first, value_grads[0], value_grads[1]),
    )


def norm_back(weighted, unit, inverse):
    return inverse * (weighted - unit * (per_head(weighted * unit, None) * (1.0 / HEAD)))


def cross_back_kernel(
    query, text, text_value, raw_t, grad, out, log, gains, mark_q, mark_t,
    query_grad, raw_grad, value_grad, gain_sum, gate_sum,
):
    grad_q, grad_t, grad_v = attention_grads(
        query[...], text[...], mark_t[...], text_value[...], grad[...], out[...], log[...], mark_q[...]
    )
    query_grad[...] = grad_q.T
    value_grad[...] = grad_v.astype(jnp.bfloat16).T
    grad_t = grad_t.astype(jnp.bfloat16).astype(jnp.float32)
    unit, inverse = head_units(raw_t[...])
    gain_sum[...] = jnp.sum(grad_t * unit, axis=0, keepdims=True)
    raw_grad[...] = norm_back(grad_t * gains[2:3, :], unit, inverse).astype(jnp.bfloat16).T
    gate_sum[...] = jnp.sum(grad[...].astype(jnp.float32) * out[...], axis=0, keepdims=True)


def self_back_kernel(
    query, key, value, raw_q, raw_k, grad, out, log, cross_grad, cosine, sine, gains, mark_q, mark_k,
    query_grad, key_grad, value_grad, gain_sum,
):
    grad_q, grad_k, grad_v = attention_grads(
        query[...], key[...], mark_k[...], value[...], grad[...], out[...], log[...], mark_q[...]
    )
    value_grad[...] = grad_v.astype(jnp.bfloat16)
    cos, sin = cosine[...], sine[...]
    grad_q = (grad_q.T + cross_grad[...]) * ROOT
    for turn, raw, row, target in ((grad_q, raw_q, 0, query_grad), (grad_k, raw_k, 1, key_grad)):
        turn = turn.astype(jnp.bfloat16).astype(jnp.float32)
        turn = turn * cos - partner(turn) * sin
        unit, inverse = head_units(raw[...])
        gain_sum[row : row + 1, :] = jnp.sum(turn * unit, axis=0, keepdims=True)
        target[...] = norm_back(turn * gains[row : row + 1, :], unit, inverse).astype(jnp.bfloat16)


def pair_call(kernel, operands, outs, name, ties=(), micros=0):
    def spec(shape, cut):
        if cut is None:
            return pl.BlockSpec(shape, lambda pair: (0, 0))
        if cut == 1:
            return pl.BlockSpec((shape[0], LANES), lambda pair: (0, pair))
        return pl.BlockSpec((LANES, shape[1]), lambda pair: (pair, 0))

    width = outs[0][0][0] if outs[0][2] == 0 else outs[0][0][1]
    return pl.pallas_call(
        lambda *refs: kernel(*refs[: len(operands)], *refs[len(operands) + len(ties) :]),
        grid=(width // LANES,),
        in_specs=[spec(part.shape, cut) for part, cut in operands]
        + [pl.BlockSpec(memory_space=pl.ANY)] * len(ties),
        out_specs=[spec(shape, cut) for shape, _, cut in outs],
        out_shape=[jax.ShapeDtypeStruct(shape, kind) for shape, kind, _ in outs],
        compiler_params=pltpu.CompilerParams(vmem_limit_bytes=VMEM_LIMIT),
        cost_estimate=cost_of(micros),
        name=name,
    )(*[part for part, _ in operands], *ties)
def inverse_rms(values):
    return lax.rsqrt(jnp.mean(values * values, axis=-1, keepdims=True) + EPS)


def row_norm_back(weighted, unit, inverse):
    return inverse * (weighted - unit * jnp.mean(weighted * unit, axis=-1, keepdims=True))


def per_row(table, segment):
    return jnp.where(segment == 0.0, table[0:1], jnp.where(segment == 1.0, table[1:2], table[2:3]))


def total_of(parts):
    upper, near, far = parts
    rows = far.shape[0]
    return (
        upper[:rows].astype(jnp.float32) + near[:rows].astype(jnp.float32) + far[...].astype(jnp.float32)
    )


def segment_sums(member, values):
    high = values.astype(jnp.bfloat16)
    low = (values - high.astype(jnp.float32)).astype(jnp.bfloat16)
    return dot(member, high) + dot(member, low)


def tables_kernel(here, lens, gate, segments, head_gains, cosine, sine, mark_q, mark_k, mark_t,
                  segment, member, gate_lanes, gate_swapped, gains):
    heads = gains.shape[1] // HEAD
    lane = lane_index(gate_lanes.shape) // HEAD
    line = jnp.zeros(gate_lanes.shape, jnp.float32)
    swapped = line
    for head in range(heads):
        line = jnp.where(lane == head, gate[head], line)
        swapped = jnp.where(lane == head ^ 1, gate[head], swapped)
    gate_lanes[...] = jnp.tanh(line)
    gate_swapped[...] = jnp.tanh(swapped)
    gains[...] = jnp.concatenate([head_gains[...]] * heads, axis=1)
    rows = segments.shape[1]
    ids = segments[...]
    first = jnp.sum((ids < 1).astype(jnp.float32))
    second = jnp.sum((ids < 2).astype(jnp.float32))
    lane = lane_index((rows, LANES))
    half = HEAD // 2
    rate = jnp.exp((lane % half).astype(jnp.float32) * (-2.0 * math.log(10000.0) / HEAD))
    within = lane % HEAD
    for block, code in enumerate(ROW_ORDER):
        source = here[0] ^ code
        line = segments[pl.ds(source, 1), :].astype(jnp.float32)
        label = jnp.broadcast_to(line, (rows, rows)).T
        start = jnp.where(label == 0.0, 0.0, jnp.where(label == 1.0, first, second))
        token = (lax.broadcasted_iota(jnp.int32, (rows, LANES), 0) + source * rows).astype(jnp.float32)
        angle = (token - start) * rate
        index = slice(block * rows, (block + 1) * rows)
        cosine[index, :] = jnp.cos(angle)
        sine[index, :] = jnp.where(within < half, -1.0, 1.0) * jnp.sin(angle)
        same = ((label == within.astype(jnp.float32)) & (within < SEGS)).astype(jnp.float32)
        shut = (within == SEGS).astype(jnp.float32)
        ones = ((within >= SEGS) & (within < SEGS + 3)).astype(jnp.float32)
        mark_q[index, :] = (SHUT * same - SHUT * shut).astype(jnp.bfloat16)
        mark_k[index, :] = (same + ones).astype(jnp.bfloat16)
        if block == 0:
            segment[...] = label
            member[...] = (
                lax.broadcasted_iota(jnp.int32, (8, rows), 0).astype(jnp.float32) == line
            ).astype(jnp.bfloat16)
    for group in range(SEGS):
        lane = lane_index((TXT, LANES)) % HEAD
        row = lax.broadcasted_iota(jnp.int32, (TXT, LANES), 0)
        inside = ((lane == group) & (row < lens[group])).astype(jnp.float32)
        ones = ((lane >= SEGS) & (lane < SEGS + 3)).astype(jnp.float32)
        mark_t[group * TXT : (group + 1) * TXT, :] = (inside + ones).astype(jnp.bfloat16)


def text_kernel(captions, key_weight, value_weight, raw_out, value_out, raw_sum, value_sum):
    step = pl.program_id(0)

    @pl.when(step == 0)
    def _():
        raw_sum[...] = dot(captions[...], key_weight[...])
        value_sum[...] = dot(captions[...], value_weight[...])

    @pl.when(step > 0)
    def _():
        raw_sum[...] += dot(captions[...], key_weight[...])
        value_sum[...] += dot(captions[...], value_weight[...])

    @pl.when(step == pl.num_programs(0) - 1)
    def _():
        raw_out[...] = raw_sum[...]
        value_out[...] = value_sum[...].astype(jnp.bfloat16)


def text_call(captions, key_weight, value_weight):
    rows, depth = captions.shape
    columns = key_weight.shape[1]
    tile = depth // 4
    return pl.pallas_call(
        text_kernel,
        grid=(depth // tile,),
        in_specs=[
            pl.BlockSpec((rows, tile), lambda step: (0, step)),
            pl.BlockSpec((tile, columns), lambda step: (step, 0)),
            pl.BlockSpec((tile, columns), lambda step: (step, 0)),
        ],
        out_specs=[pl.BlockSpec((rows, columns), lambda step: (0, 0))] * 2,
        out_shape=[
            jax.ShapeDtypeStruct((rows, columns), jnp.float32),
            jax.ShapeDtypeStruct((rows, columns), jnp.bfloat16),
        ],
        scratch_shapes=[pltpu.VMEM((rows, columns), jnp.float32)] * 2,
        compiler_params=pltpu.CompilerParams(vmem_limit_bytes=VMEM_LIMIT),
        cost_estimate=cost_of(9),
        name="text",
    )(*[pltpu.with_memory_space_constraint(part, pltpu.HBM) for part in (captions, key_weight, value_weight)])


def project_kernel(here, own, far, near, last, mods, gains, segment_q, query_w, key_w, value_w,
                   rows_out, raw_q, raw_k, value):
    table = mods[here[0]]
    rows = own.shape[0]
    for block, part in enumerate((own, far, near, last)):
        index = slice(block * rows, (block + 1) * rows)
        values = part[...].astype(jnp.float32)
        marks = segment_q[index, :].astype(jnp.float32)
        scale = jnp.where(
            marks[:, 0:1] > 0.0, table[0:1], jnp.where(marks[:, 1:2] > 0.0, table[1:2], table[2:3])
        )
        rows_out[index, :] = (
            values * inverse_rms(values) * gains[0:1] * (1.0 + scale)
        ).astype(jnp.bfloat16)
    raw_q[...] = dot(rows_out[...], query_w[...])
    raw_k[...] = dot(rows_out[...], key_w[...])
    value[...] = dot(rows_out[...], value_w[...]).astype(jnp.bfloat16)


def middle_kernel(here, block, upper, near, far, mods, gains, segment, attn_out, middle_out, rows_out):
    attn_sum = total_of((upper, near, far))
    label = segment[:, 0:1]
    factor = jnp.tanh(per_row(mods[here[0] ^ 1], label)) * gains[1:2]
    middle = block[...].astype(jnp.float32) + factor * (attn_sum * inverse_rms(attn_sum))
    attn_out[...] = attn_sum
    middle_out[...] = middle
    scale = per_row(mods[here[0] ^ 2], label)
    rows_out[...] = (middle * inverse_rms(middle) * gains[2:3] * (1.0 + scale)).astype(jnp.bfloat16)


def block_out_kernel(here, middle, upper, near, far, grad, mods, gains, segment, member,
                     block_out, grad_out, sums):
    ffn_sum = total_of((upper, near, far))
    inverse = inverse_rms(ffn_sum)
    unit = ffn_sum * inverse
    factor = jnp.tanh(per_row(mods[here[0] ^ 3], segment[:, 0:1])) * gains[3:4]
    block_out[...] = (middle[...] + factor * unit).astype(jnp.bfloat16)
    incoming = grad[...].astype(jnp.float32)
    grad_out[...] = row_norm_back(incoming * factor, unit, inverse).astype(jnp.bfloat16)
    sums[...] = segment_sums(member[...], incoming * unit)


def middle_back_kernel(here, middle, attn, upper, near, far, grad, mods, gains, segment, member,
                       middle_grad, attn_grad, ffn_sums, attn_sums):
    grad_in = total_of((upper, near, far))
    label = segment[:, 0:1]
    inverse = inverse_rms(middle[...])
    unit = middle[...] * inverse
    factor = gains[2:3] * (1.0 + per_row(mods[here[0] ^ 2], label))
    ffn_sums[...] = segment_sums(member[...], grad_in * unit)
    grad_middle = grad[...].astype(jnp.float32) + row_norm_back(grad_in * factor, unit, inverse)
    middle_grad[...] = grad_middle
    inverse = inverse_rms(attn[...])
    unit = attn[...] * inverse
    factor = jnp.tanh(per_row(mods[here[0] ^ 1], label)) * gains[1:2]
    attn_grad[...] = row_norm_back(grad_middle * factor, unit, inverse).astype(jnp.bfloat16)
    attn_sums[...] = segment_sums(member[...], grad_middle * unit)


def block_in_kernel(here, block, middle_grad, upper, near, far, mods, gains, segment, member,
                    in_grad, sums):
    grad_in = total_of((upper, near, far))
    values = block[...].astype(jnp.float32)
    inverse = inverse_rms(values)
    unit = values * inverse
    factor = gains[0:1] * (1.0 + per_row(mods[here[0]], segment[:, 0:1]))
    in_grad[...] = (
        middle_grad[...] + row_norm_back(grad_in * factor, unit, inverse)
    ).astype(jnp.bfloat16)
    sums[...] = segment_sums(member[...], grad_in * unit)


def stack_sums_kernel(here, first, second, third, fourth, head_gain, text_gain, gate_sum, gate, out):
    width = out.shape[1]
    heads = jnp.concatenate([head_gain[0:1], head_gain[1:2], text_gain[...]], axis=1)
    inner = heads.shape[1] // 3
    gates = gate_sum[...] * (1.0 - gate[...] * gate[...])
    gates = jnp.concatenate([gates, jnp.zeros((1, width - inner), jnp.float32)], axis=1)
    lane = lane_index(gates.shape)
    moved = jnp.zeros_like(gates)
    for position in range(4):
        turn = pltpu.roll(gates, position * inner, 1) if position else gates
        moved = jnp.where((lane // inner == position) & (here[0] == position), turn, moved)
    out[...] = jnp.concatenate(
        [part[0:SEGS] for part in (first, second, third, fourth)]
        + [
            jnp.concatenate([heads, jnp.zeros((1, width - 3 * inner), jnp.float32)], axis=1),
            moved,
            jnp.zeros((2, width), jnp.float32),
        ],
        axis=0,
    )


def pack_kernel(here, own, far, near, last, mods, gains, cond, packed):
    total = own[...] + far[...] + near[...] + last[...]
    grad = jnp.zeros((SEGS, total.shape[1]), jnp.float32)
    rows = []
    for name in range(4):
        part = total[name * SEGS : (name + 1) * SEGS]
        mod = mods[here[0] ^ name]
        gain = gains[name : name + 1]
        if name % 2 == 1:
            factor = jnp.tanh(mod)
            slope = 1.0 - factor * factor
        else:
            factor = 1.0 + mod
            slope = jnp.ones_like(mod)
        rows.append(jnp.sum(part * factor, axis=0, keepdims=True))
        mine = (jnp.zeros(part.shape, jnp.int32) + here[0]) == name
        grad = jnp.where(mine, part * slope * gain, grad)
    rows.append(total[4 * SEGS : 4 * SEGS + 2])
    rows = jnp.concatenate(rows, axis=0)
    high = rows.astype(jnp.bfloat16).astype(jnp.float32)
    pad = jnp.zeros((packed.shape[0] - 2 * SEGS - 2 * SUM_ROWS, total.shape[1]), jnp.float32)
    packed[...] = jnp.concatenate(
        [grad, cond[...].astype(jnp.float32), high, rows - high, pad], axis=0
    ).astype(jnp.bfloat16)


def rider_rows(count):
    return -(-(2 * SEGS * count + 2 * SUM_ROWS) // 16) * 16


def merge_rows(count, first, second, size):
    first, second = first.astype(jnp.float32), second.astype(jnp.float32)
    wide = SEGS * count
    start = 2 * wide
    sums = (
        first[start : start + SUM_ROWS]
        + first[start + SUM_ROWS : start + 2 * SUM_ROWS]
        + second[start : start + SUM_ROWS]
        + second[start + SUM_ROWS : start + 2 * SUM_ROWS]
    )
    high = sums.astype(jnp.bfloat16).astype(jnp.float32)
    pieces = [first[:wide], second[:wide], first[wide:start], second[wide:start], high, sums - high]
    rest = size - 4 * wide - 2 * SUM_ROWS
    if rest:
        pieces.append(jnp.zeros((rest, first.shape[1]), jnp.float32))
    return jnp.concatenate(pieces, axis=0).astype(jnp.bfloat16)


def merge_kernel(count, ours, theirs, out):
    out[...] = merge_rows(count, ours[...], theirs[...], out.shape[0])


def ada_kernel(count, heads, dp, own, *refs):
    parts = (own,) + refs[:3]
    ada_out, norm_out, head_out, gate_out = refs[3:]
    wide = SEGS * count
    base = own.shape[0] - rider_rows(count)
    columns = ada_out.shape[0]
    share = LANES // columns
    start = pl.multiple_of(dp[0] // share * LANES, LANES)
    grads, conds = [], []
    sums = jnp.zeros((SUM_ROWS, own.shape[1]), jnp.float32)
    for part in parts:
        rows = part[base:, :].astype(jnp.float32)
        grads.append(rows[:wide])
        conds.append(part[base:, pl.ds(start, LANES)].astype(jnp.float32)[wide : 2 * wide])
        for half in range(2):
            place = 2 * wide + half * SUM_ROWS
            sums = sums + rows[place : place + SUM_ROWS]
    conds = jnp.concatenate(conds, axis=0)
    conds = pltpu.roll(conds, (LANES - dp[0] % share * columns) % LANES, 1)
    acts = conds / (1.0 + jnp.exp(-conds))
    ada_out[...] = dot(
        acts.astype(jnp.bfloat16).astype(jnp.float32).T.astype(jnp.bfloat16),
        jnp.concatenate(grads, axis=0).astype(jnp.bfloat16),
    )[:columns]
    norm_out[...] = sums[:4]
    inner = heads * HEAD
    for row in range(3):
        line = jnp.zeros((1, HEAD), jnp.float32)
        for head in range(heads):
            place = row * inner + head * HEAD
            line = line + sums[4:5, place : place + HEAD]
        head_out[row : row + 1, :] = line
    lane = lane_index((1, LANES))
    line = jnp.zeros((1, LANES), jnp.float32)
    for head in range(HEADS):
        value = jnp.sum(sums[5:6, head * HEAD : (head + 1) * HEAD], axis=1, keepdims=True)
        line = jnp.where(lane == head, value, line)
    gate_out[...] = line


def back_kernel(count, *refs):
    grads, weights, upper, lower = refs[:count], refs[count : 2 * count], refs[-2], refs[-1]
    total = dot_t(grads[0][...], weights[0][...])
    for grad, weight in zip(grads[1:], weights[1:]):
        total = total + dot_t(grad[...], weight[...])
    half = upper.shape[0]
    upper[...] = total[:half].astype(jnp.bfloat16)
    lower[...] = total[half:].astype(jnp.bfloat16)


def back_call(grads, weights, name, ties=(), micros=0):
    rows, inner = grads[0].shape
    columns = weights[0].shape[0]
    tile = columns // 3
    return pl.pallas_call(
        lambda *refs: back_kernel(len(grads), *refs[: 2 * len(grads)], *refs[-2:]),
        grid=(columns // tile,),
        in_specs=[pl.BlockSpec((rows, inner), lambda step: (0, 0))] * len(grads)
        + [pl.BlockSpec((tile, inner), lambda step: (step, 0))] * len(grads)
        + [pl.BlockSpec(memory_space=pl.ANY)] * len(ties),
        out_specs=[pl.BlockSpec((rows // 2, tile), lambda step: (0, step))] * 2,
        out_shape=[jax.ShapeDtypeStruct((rows // 2, columns), jnp.bfloat16)] * 2,
        compiler_params=pltpu.CompilerParams(vmem_limit_bytes=VMEM_LIMIT),
        cost_estimate=cost_of(micros),
        name=name,
    )(*grads, *weights, *ties)


def shards(
    block_in,
    out_grad,
    condition,
    captions,
    caption_len,
    segment_ids,
    ada_weight,
    norm_gains,
    query_weight,
    key_weight,
    value_weight,
    head_gains,
    textkey_weight,
    textvalue_weight,
    cross_gate,
    out_weight,
    gate_weight,
    up_weight,
    down_weight,
):
    rows, width = block_in.shape
    length = segment_ids.shape[0]
    heads = cross_gate.shape[0]
    inner = heads * HEAD
    half_rows = length // 2
    position = lax.axis_index("tensor")
    spot = dp_spot(position)
    here = position.reshape(1)
    b16, f32 = jnp.bfloat16, jnp.float32

    blocks = gather_tensor(block_in)
    cond_rows = jnp.pad(condition, ((0, 0), (0, width - condition.shape[1])))
    own_act = jax.nn.silu(condition.astype(f32)).astype(b16)
    own_part = jnp.dot(own_act, ada_weight, preferred_element_type=f32)
    parts = gather_tensor(own_part)
    mods = jnp.stack([parts[ROW_ORDER.index(code)] for code in range(4)])

    cosine, sine, mark_q, mark_k, mark_t, segment, member, gate_lanes, gate_swapped, gains = whole_call(
        tables_kernel,
        (here, caption_len, cross_gate),
        [segment_ids.reshape(length // rows, rows), head_gains],
        [((length, LANES), f32)] * 2
        + [((length, LANES), b16)] * 2
        + [((SEGS * TXT, LANES), b16), ((rows, LANES), f32), ((8, rows), b16)]
        + [((1, inner), f32)] * 2
        + [((3, inner), f32)],
        "tables",
        micros=2,
    )
    caption_flat = captions.reshape(-1, captions.shape[-1])
    texts = caption_flat.shape[0]
    raw_t, text_value = text_call(caption_flat, textkey_weight, textvalue_weight)
    attn_rows, raw_q, raw_k, value = whole_call(
        project_kernel,
        (here,),
        blocks + [mods, norm_gains, mark_q, query_weight, key_weight, value_weight],
        [((length, width), b16), ((length, inner), f32), ((length, inner), f32), ((length, inner), b16)],
        "project",
        micros=6,
    )
    query, key, text, mixed, self_out, cross_out, self_log, cross_log = pair_call(
        attend_kernel,
        [(raw_q, 1), (raw_k, 1), (value, 1), (raw_t, 1), (text_value, 1), (cosine, None), (sine, None)]
        + [(gains, 1), (gate_lanes, 1), (gate_swapped, 1), (mark_q, None), (mark_k, None), (mark_t, None)],
        [((length, inner), b16, 1)] * 2
        + [((texts, inner), b16, 1), ((length, inner), b16, 1)]
        + [((length, inner), f32, 1)] * 4,
        "attend",
        micros=11,
    )

    def halves(product):
        return product(slice(0, half_rows)).astype(b16), product(slice(half_rows, None)).astype(b16)

    def all_of(block):
        return jnp.concatenate(gather_tensor(block), axis=0)

    upper, lower = halves(lambda part: jnp.dot(mixed[part], out_weight, preferred_element_type=f32))
    sums, sent = scatter_tensor(upper, lower)
    attn_rows_t = turned(attn_rows, (sent,))
    wide = ((rows, width), f32)
    narrow = ((rows, width), b16)
    totals = ((8, width), f32)
    attn_sum, middle, ffn_own = whole_call(
        middle_kernel,
        (here,),
        [block_in] + sums + [mods, norm_gains, segment],
        [wide, wide, narrow],
        "middle",
    )
    ffn_rows = all_of(ffn_own)
    gate_pre = jnp.dot(ffn_rows, gate_weight, preferred_element_type=f32)
    up_pre = jnp.dot(ffn_rows, up_weight, preferred_element_type=f32)
    sigmoid_gate = jax.nn.sigmoid(gate_pre)
    silu_gate = gate_pre * sigmoid_gate
    hidden = (silu_gate * up_pre).astype(b16)
    upper, lower = halves(lambda part: jnp.dot(hidden[part], down_weight, preferred_element_type=f32))
    sums, sent = scatter_tensor(upper, lower)
    ffn_rows_t = turned(ffn_rows, (sent,))
    block_out, grad_own, sum_gate_ffn = whole_call(
        block_out_kernel,
        (here,),
        [middle] + sums + [out_grad, mods, norm_gains, segment, member],
        [narrow, narrow, totals],
        "block_out",
    )

    grad_ffn = all_of(grad_own)
    grad_hidden = times_transpose(grad_ffn, down_weight)
    grad_gate = (
        grad_hidden * up_pre * sigmoid_gate * (1.0 + gate_pre * (1.0 - sigmoid_gate))
    ).astype(b16)
    grad_up = (grad_hidden * silu_gate).astype(b16)
    upper, lower = halves(
        lambda part: times_transpose(grad_gate[part], gate_weight)
        + times_transpose(grad_up[part], up_weight)
    )
    sums, sent = scatter_tensor(upper, lower)
    grad_ffn_t = turned(grad_ffn, (sent,))
    ffn_pairs = [(ffn_rows_t, [grad_gate, grad_up]), (grad_ffn_t, [hidden])]
    (halves_two,) = row_chunks(ffn_pairs, (2,), spot, ties=(sent,), micros=FFN_MICROS)
    ffn_passed = one_on(halves_two)
    grad_middle, grad_own, sum_scale_ffn, sum_gate_attn = whole_call(
        middle_back_kernel,
        (here,),
        [middle, attn_sum] + sums + [out_grad, mods, norm_gains, segment, member],
        [wide, narrow, totals, totals],
        "middle_back",
        micros=MIDDLE_MICROS,
    )

    grad_attn = all_of(grad_own)
    grad_mixed = times_transpose(grad_attn, out_weight).astype(b16)
    cross_grad, text_grad, text_value_grad, text_gain, gate_sum = pair_call(
        cross_back_kernel,
        [(query, 1), (text, 1), (text_value, 1), (raw_t, 1), (grad_mixed, 1), (cross_out, 1)]
        + [(cross_log, 1), (gains, 1), (mark_q, None), (mark_t, None)],
        [((length, inner), f32, 1), ((inner, texts), b16, 0), ((inner, texts), b16, 0)]
        + [((1, inner), f32, 1)] * 2,
        "cross_back",
        micros=CROSS_MICROS,
    )
    ffn_one, ffn_three, ffn_kept = row_chunks(
        ffn_pairs, (1, 3, 0), spot, extra=ffn_passed, ties=(text_grad,), micros=FFN_NEXT_MICROS
    )
    text_lefts = [text_grad, text_value_grad]
    (halves_two,) = column_chunks(text_lefts, caption_flat, (2,), spot, ties=(ffn_kept,))
    text_passed = one_on(halves_two)
    query_grad, key_grad, value_grad, head_gain = pair_call(
        self_back_kernel,
        [(query, 1), (key, 1), (value, 1), (raw_q, 1), (raw_k, 1), (grad_mixed, 1), (self_out, 1)]
        + [(self_log, 1), (cross_grad, 1), (cosine, None), (sine, None), (gains, 1)]
        + [(mark_q, None), (mark_k, None)],
        [((length, inner), b16, 1)] * 3 + [((2, inner), f32, 1)],
        "self_back",
        (halves_two[0],),
        micros=SELF_MICROS,
    )

    hidden_cols = hidden.shape[1]
    block_rows = width // BLOCKS
    got = [by_slots(part) for part in to_neighbours(ffn_kept, ffn_one, ffn_three)]
    shape = (PAIR, block_rows, 3 * hidden_cols)
    ffn_kept, ffn_sent = tiled_call(
        ffn_second_kernel,
        (spot,),
        got,
        [((2 * PAIR,) + shape[1:], b16)] * 2,
        "ffn_second",
        -1,
        4,
        (query_grad,),
    )
    upper, lower = back_call(
        [query_grad, key_grad, value_grad], [query_weight, key_weight, value_weight], "attn_back"
    )
    sums, sent = scatter_tensor(upper, lower)
    in_grad, sum_scale_attn = whole_call(
        block_in_kernel,
        (here,),
        [block_in, grad_middle] + sums + [mods, norm_gains, segment, member],
        [narrow, totals],
        "block_in",
        (ffn_sent,),
        micros=BLOCK_IN_MICROS,
    )
    (stacked,) = whole_call(
        stack_sums_kernel,
        (here,),
        [sum_scale_attn, sum_gate_attn, sum_scale_ffn, sum_gate_ffn]
        + [head_gain, text_gain, gate_sum, gate_lanes],
        [((16, width), f32)],
        "stack_sums",
    )
    attn_pairs = [
        (attn_rows_t, [query_grad, key_grad, value_grad]),
        (turned(grad_attn, (halves_two[0],)), [mixed]),
    ]
    (halves_two,) = row_chunks(attn_pairs, (2,), spot, ties=(stacked,), micros=ATTN_FIRST_MICROS)
    attn_passed = one_on(halves_two)
    stacked = gather_tensor(stacked)
    text_one, text_three, text_kept = column_chunks(
        text_lefts, caption_flat, (1, 3, 0), spot, extra=text_passed, ties=(halves_two[0],), micros=TEXT_MICROS
    )
    ffn_own, ffn_sent = tiled_call(
        ffn_middle_kernel,
        (),
        [ffn_kept, dp_permute(ffn_sent, "second", "flip")],
        [(shape, b16)] * 2,
        "ffn_middle",
        -1,
        2,
        (text_kept,),
    )
    (riders,) = whole_call(
        pack_kernel,
        (here,),
        stacked + [mods, norm_gains, cond_rows],
        [((rider_rows(1), width), b16)],
        "pack",
        (ffn_sent,),
        micros=PACK_MICROS,
    )
    (riders,) = whole_call(
        functools.partial(merge_kernel, 1),
        (),
        [riders, dp_permute(riders, "z", 1)],
        [((rider_rows(PAIR), width), b16)],
        "merge",
    )
    opposite = dp_permute(riders, "first", 2)
    attn_one, attn_three, attn_kept = row_chunks(
        attn_pairs, (1, 3, 0), spot, extra=attn_passed, riders=(riders,), ties=(text_kept,), micros=ATTN_MICROS
    )
    text_rows = caption_flat.shape[1] // BLOCKS
    stage = tiled_call(
        functools.partial(attn_second_kernel, block_rows),
        (spot,),
        [riders, opposite] + to_neighbours(attn_kept, attn_one, attn_three),
        [((PAIR * block_rows + rider_rows(4 * PAIR), width), b16)] * RING,
        "attn_second",
        -1,
        4,
        micros=STAGE_MICROS,
    )
    text_own, text_sent = tiled_call(
        text_second_kernel,
        (spot,),
        to_neighbours(text_kept, text_one, text_three),
        [((2 * inner, 2 * PAIR * text_rows), b16)] * 2,
        "text_second",
        0,
        4,
        (stage[0],),
        micros=SECOND_MICROS,
    )
    ffn_own_kept, ffn_own_sent = tiled_call(
        ffn_third_kernel,
        (spot,),
        [ffn_own, dp_permute(ffn_sent, "second", "mirror")],
        [(shape[1:], b16)] * 2,
        "ffn_third",
        -1,
        2,
        (stage[0],),
    )
    text_own, text_sent = tiled_call(
        text_middle_kernel,
        (),
        [text_own, dp_permute(text_sent, "second", "flip")],
        [((2 * inner, PAIR * text_rows), b16)] * 2,
        "text_middle",
        0,
        2,
        (stage[0],),
    )
    got = exchange(stage, "second")
    kept, sent = tiled_call(
        attn_third_kernel, (spot,), got, [((block_rows, width), b16)] * 2, "attn_third",
        -1,
        2
    )
    gate_sum_out, up_sum_out, down_sum_out = whole_call(
        ffn_last_kernel,
        (),
        exchange([ffn_own_kept, ffn_own_sent], "z"),
        [((block_rows, hidden_cols), f32)] * 2 + [((hidden_cols, block_rows), f32)],
        "ffn_last",
        (kept,),
    )
    text_own_kept, text_own_sent = tiled_call(
        text_third_kernel,
        (spot,),
        [text_own, dp_permute(text_sent, "second", "mirror")],
        [((2 * inner, text_rows), b16)] * 2,
        "text_third",
        0,
        2,
        (kept,),
    )
    textkey_sum, textvalue_sum = whole_call(
        text_last_kernel,
        (),
        exchange([text_own_kept, text_own_sent], "z"),
        [((text_rows, inner), f32)] * 2,
        "text_last",
    )
    ada_grad, norm_grads, head_grads, crossgate = tiled_call(
        functools.partial(ada_kernel, 4 * PAIR, heads),
        (lax.axis_index("dp").reshape(1),),
        got,
        [((condition.shape[1] // BLOCKS, width), f32), ((4, width), f32), ((3, HEAD), f32)]
        + [((1, LANES), f32)],
        "ada",
        0,
        1,
        (kept,),
    )
    crossgate_grad = crossgate[0, :HEADS]
    query_sum, key_sum, value_sum, outw_sum = whole_call(
        attn_last_kernel,
        (),
        exchange([kept, sent], "z"),
        [((block_rows, inner), f32)] * 3 + [((inner, block_rows), f32)],
        "attn_last",
    )
    return (
        block_out,
        in_grad,
        ada_grad,
        norm_grads,
        query_sum,
        key_sum,
        value_sum,
        head_grads,
        textkey_sum,
        textvalue_sum,
        crossgate_grad,
        outw_sum,
        gate_sum_out,
        up_sum_out,
        down_sum_out,
    )


def solution(mesh):
    return jax.shard_map(
        shards,
        mesh=mesh,
        in_specs=(
            P(("dp", "tensor"), None),
            P(("dp", "tensor"), None),
            P("dp", None),
            P("dp", None, None),
            P("dp"),
            P("dp"),
            P(None, "tensor"),
            P(),
            P(None, "tensor"),
            P(None, "tensor"),
            P(None, "tensor"),
            P(),
            P(None, "tensor"),
            P(None, "tensor"),
            P("tensor"),
            P("tensor", None),
            P(None, "tensor"),
            P(None, "tensor"),
            P("tensor", None),
        ),
        out_specs=(
            P(("dp", "tensor"), None),
            P(("dp", "tensor"), None),
            P("dp", "tensor"),
            P(),
            P("dp", "tensor"),
            P("dp", "tensor"),
            P("dp", "tensor"),
            P(),
            P("dp", "tensor"),
            P("dp", "tensor"),
            P(),
            P("tensor", "dp"),
            P("dp", "tensor"),
            P("dp", "tensor"),
            P("tensor", "dp"),
        ),
        check_vma=False,
    )
```
